32 devices in a mesh: rep: 8 (over y, x, core), shard: 4 (over z).
Axes of the slice: x: 2, y: 2, z: 4, core: 2. Of those that a mesh axis runs over, the one named last changes fastest.
Arguments:
- tokens: bfloat16 [16384, 1024], P(('rep', 'shard')), may hold values from -6 to 6
- cotangent: bfloat16 [16384, 1024], P(('rep', 'shard')), may hold values from -6 to 6
- seq_lengths: int32 [8, 4], P('rep'), may hold values from 1 to 1536, as said below
- qkv_weight: float32 [1024, 3072], P('shard'), may hold values from -0.1875 to 0.1875
- out_weight: float32 [1024, 1024], P('shard'), may hold values from -0.75 to 0.75
- up_weight: float32 [1024, 4096], P('shard'), may hold values from -0.1875 to 0.1875
- down_weight: float32 [4096, 1024], P('shard'), may hold values from -0.09375 to 0.09375
- vectors: float32 [12288], replicated, may hold values from -0.9 to 2.25
- row_state: float32 [3, 1024], P(None, 'shard'), may hold values from 137.6256 to 12451.84, as said below
- down_rows: float32 [4096], P('shard'), may hold values from 137.6256 to 12451.84, as said below
- col_state: float32 [9216], replicated, may hold values from 137.6256 to 12451.84, as said below
- vector_state: float32 [12288], replicated, may hold values from 1474.56 to 6225.92
Outputs:
- block_out: bfloat16 [16384, 1024], P(('rep', 'shard'))
- tokens_grad: bfloat16 [16384, 1024], P(('rep', 'shard'))
- qkv_grad: float32 [1024, 3072], P('shard')
- out_grad: float32 [1024, 1024], P('shard')
- up_grad: float32 [1024, 4096], P('shard')
- down_grad: float32 [4096, 1024], P('shard')
- vector_grad: float32 [12288], replicated
- qkv_new: float32 [1024, 3072], P('shard')
- out_new: float32 [1024, 1024], P('shard')
- up_new: float32 [1024, 4096], P('shard')
- down_new: float32 [4096, 1024], P('shard')
- vector_new: float32 [12288], replicated
- qkv_copy: bfloat16 [1024, 3072], P('shard')
- out_copy: bfloat16 [1024, 1024], P('shard')
- up_copy: bfloat16 [1024, 4096], P('shard')
- down_copy: bfloat16 [4096, 1024], P('shard')
- row_state_new: float32 [3, 1024], P(None, 'shard')
- down_rows_new: float32 [4096], P('shard')
- col_state_new: float32 [9216], replicated
- vector_state_new: float32 [12288], replicated
- update_rms: float32 [5], replicated
The draws below stay inside these ranges and needn't reach their ends.
Inputs may be any that keep to these rules, and one draw needn't show every extreme that they name: `seq_lengths`: in every group one sequence, never the first or the last, has exactly 1536 tokens; the other 3 have together 512 tokens. `row_state`: every entry is positive. `down_rows`: every entry is positive. `col_state`: every entry is positive.
All inputs are finite; a program needn't handle non-finite values.
Results may differ from the reference program's by a relative error of at most 0.013.
Values may be sent and summed in bfloat16 or wider, within the bound.
No kernel may reach another device: no remote copies, remote signals or barrier semaphores. Data moves between devices by JAX's collectives and lax.ppermute only.
A program may use at most 320 MiB of HBM per device.

```python
import math
import jax
import jax.numpy as jnp
from jax import lax

D = 1024
HEADS = 16
FF = 4096
HEAD_DIM = 64
TOK_DEV = 512
SEQS = 4
STEP = 10
GROUPS = 8
GROUP = 2048
TOKENS = 16384
VEC = 12288


def spread_factor(key, shape):
    return jnp.exp(jax.random.uniform(key, shape, jnp.float32, math.log(0.5), math.log(2.0)))


def state_level():
    decay_rate = 1.0 - STEP ** (-0.8)
    return (1.0 - decay_rate) / decay_rate * TOKENS


def draw_seq_lengths(key, part):
    key = jax.random.fold_in(key, 21)
    key_place, key_cut = jax.random.split(key)
    long_place = jax.random.randint(key_place, (GROUPS, 1), 1, SEQS - 1)
    cut_keys = jax.random.split(key_cut, GROUPS)

    def cut_group(single_key):
        return jax.random.permutation(single_key, TOK_DEV - 1)[:SEQS - 2]
    cut_points = jnp.sort(jax.vmap(cut_group)(cut_keys) + 1, axis=1).astype(jnp.int32)
    boundaries = jnp.concatenate([jnp.zeros((GROUPS, 1), jnp.int32), cut_points, jnp.full((GROUPS, 1), TOK_DEV, jnp.int32)], axis=1)
    others = boundaries[:, 1:] - boundaries[:, :-1]
    slot_index = jnp.arange(SEQS, dtype=jnp.int32)[None, :]
    source = jnp.clip(slot_index - (slot_index > long_place).astype(jnp.int32), 0, SEQS - 2)
    picked = jnp.take_along_axis(others, source, axis=1)
    return jnp.where(slot_index == long_place, GROUP - TOK_DEV, picked).astype(jnp.int32)


def draw_vectors(key, part):
    key = jax.random.fold_in(key, 22)
    key_list = jax.random.split(key, 3)
    rising = 0.6 * 3.0 ** (jnp.arange(D, dtype=jnp.float32) / (D - 1))
    gain_rows = rising[None, :] * jax.random.uniform(key_list[0], (2, D), jnp.float32, 0.8, 1.25)
    shifts = 0.3 * jax.random.truncated_normal(key_list[1], -3.0, 3.0, (5, D), jnp.float32)
    tail_shifts = 0.3 * jax.random.truncated_normal(key_list[2], -3.0, 3.0, (FF + D,), jnp.float32)
    return jnp.concatenate([gain_rows[0], shifts[0], shifts[1], shifts[2], shifts[3], gain_rows[1], shifts[4], tail_shifts])


def draw_row_state(key, part):
    key = jax.random.fold_in(key, 23)
    levels = jnp.array([2.0, 0.36, 0.09], jnp.float32)[:, None]
    return levels * state_level() * spread_factor(key, (3, D))


def draw_down_rows(key, part):
    key = jax.random.fold_in(key, 24)
    return 0.4 * state_level() * spread_factor(key, (FF,))


def draw_col_state(key, part):
    key = jax.random.fold_in(key, 25)
    levels = jnp.concatenate([jnp.full((3 * D,), 2.0, jnp.float32), jnp.full((D,), 0.36, jnp.float32), jnp.full((FF,), 0.09, jnp.float32), jnp.full((D,), 0.4, jnp.float32)])
    return levels * state_level() * spread_factor(key, (5 * D + FF,))


def level_of(key, shape, pieces, low, top_value):
    level, own = 1.0, jax.random.fold_in(key, 6)
    for dim, shards_of in pieces:
        steps = jnp.exp(jax.random.uniform(jax.random.fold_in(own, dim), (shards_of,), jnp.float32, low / len(pieces), top_value / len(pieces)))
        level = level * jnp.repeat(steps, shape[dim] // shards_of).reshape([-1 if axis == dim else 1 for axis in range(len(shape))])
    return level


def scatter_about(stream_key, shape, width, reach, cuts=(), kind=jnp.bfloat16):
    entries = jax.random.normal(stream_key, shape, jnp.float32) * width
    if len(cuts) > 0:
        entries = level_of(stream_key, shape, cuts, -0.22, 0.18) * entries
    return jnp.clip(entries, min=-reach, max=reach).astype(kind)


def setup_inputs(seed: int = 0) -> dict:
    streams_of = jax.random.split(jax.random.key(seed), 13)
    tokens = scatter_about(streams_of[0], (TOKENS, D), 1.0, 6.0, ((0, 32),))
    cotangent = scatter_about(streams_of[1], (TOKENS, D), 1.0, 6.0, ((0, 32),))
    seq_lengths = draw_seq_lengths(jax.random.fold_in(streams_of[12], 71), 0)
    qkv_weight = scatter_about(streams_of[3], (D, 3 * D), D ** -0.5, 0.1875, ((0, 4),), jnp.float32)
    out_weight = scatter_about(streams_of[4], (D, D), HEAD_DIM ** -0.5, 0.75, ((0, 4),), jnp.float32)
    up_weight = scatter_about(streams_of[5], (D, FF), D ** -0.5, 0.1875, ((0, 4),), jnp.float32)
    down_weight = scatter_about(streams_of[6], (FF, D), FF ** -0.5, 0.09375, ((0, 4),), jnp.float32)
    vectors = draw_vectors(jax.random.fold_in(streams_of[12], 71), 0)
    row_state = draw_row_state(jax.random.fold_in(streams_of[12], 71), 0)
    down_rows = draw_down_rows(jax.random.fold_in(streams_of[12], 71), 0)
    col_state = draw_col_state(jax.random.fold_in(streams_of[12], 71), 0)
    vector_state = jnp.clip(jnp.exp(jax.random.uniform(streams_of[11], (VEC,), jnp.float32, math.log(1474.56), math.log(6225.92))), 1474.56, 6225.92)
    return dict(tokens=tokens, cotangent=cotangent, seq_lengths=seq_lengths, qkv_weight=qkv_weight, out_weight=out_weight, up_weight=up_weight, down_weight=down_weight, vectors=vectors, row_state=row_state, down_rows=down_rows, col_state=col_state, vector_state=vector_state)


@jax.custom_vjp
def low(v):
    return lax.optimization_barrier(v.astype(jnp.bfloat16)).astype(jnp.float32)

@jax.custom_vjp
def low_back(v):
    return v

def low_keep(v):
    return (low(v), None)

def low_pass(kept, grad):
    return (grad,)

def back_keep(v):
    return (v, None)

def back_low(kept, grad):
    return (low(grad),)
low.defvjp(low_keep, low_pass)
low_back.defvjp(back_keep, back_low)
eps_norm = 1e-05
eps_second = 1e-30
rate_step = 0.5
clip_level = 1.0
masked = -1e+30
highest = lax.Precision.HIGHEST

def layer_norm(values, gain_vec, shift_vec):
    average = lax.optimization_barrier(jnp.mean(values, axis=-1, keepdims=True))
    centred = values - average
    variance = lax.optimization_barrier(jnp.mean(centred * centred, axis=-1, keepdims=True))
    return centred * lax.rsqrt(variance + eps_norm) * gain_vec + shift_vec

def sequence_ids(positions, lengths):
    seq_ends = jnp.cumsum(lengths)
    return lax.optimization_barrier(jnp.sum((positions[:, None] >= seq_ends[None, :]).astype(jnp.int32), axis=1))

def attend(qkv_rows, seq_ids):
    head_width = D // HEADS
    queries = qkv_rows[:, :D].reshape(GROUP, HEADS, head_width)
    key_heads = qkv_rows[:, D:2 * D].reshape(GROUP, HEADS, head_width)
    value_heads = qkv_rows[:, 2 * D:].reshape(GROUP, HEADS, head_width)
    positions = jnp.arange(GROUP, dtype=jnp.int32)
    slopes = jnp.exp2(-8.0 * (jnp.arange(HEADS, dtype=jnp.float32) + 1.0) / HEADS)
    score_scale = head_width ** (-0.5)

    def one_block(start_row):
        block_queries = lax.dynamic_slice_in_dim(queries, start_row, TOK_DEV, 0)
        block_pos = lax.dynamic_slice_in_dim(positions, start_row, TOK_DEV, 0)
        block_ids = lax.dynamic_slice_in_dim(seq_ids, start_row, TOK_DEV, 0)
        raw_scores = jnp.einsum('qhd,khd->hqk', block_queries, key_heads, precision=highest) * score_scale
        distance = (block_pos[:, None] - positions[None, :]).astype(jnp.float32)
        allowed = (distance >= 0.0) & (block_ids[:, None] == seq_ids[None, :])
        scores = low_back(jnp.where(allowed[None], raw_scores - slopes[:, None, None] * distance[None], masked))
        weights = low(jax.nn.softmax(scores, axis=-1))
        return jnp.einsum('hqk,khd->qhd', weights, value_heads, precision=highest).reshape(TOK_DEV, D)
    starts = jnp.arange(0, GROUP, TOK_DEV, dtype=jnp.int32)
    return lax.map(jax.checkpoint(one_block), starts).reshape(GROUP, D)

def group_forward(values, seq_ids, vectors, qkv_weight, out_weight, up_weight, down_weight):
    gain_one = vectors[0:D]
    shift_one = vectors[D:2 * D]
    bias_query = vectors[2 * D:3 * D]
    bias_value = vectors[3 * D:4 * D]
    bias_out = vectors[4 * D:5 * D]
    gain_two = vectors[5 * D:6 * D]
    shift_two = vectors[6 * D:7 * D]
    bias_up = vectors[7 * D:7 * D + FF]
    bias_down = vectors[7 * D + FF:]
    act_one = low(layer_norm(values, gain_one, shift_one))
    qkv_bias = jnp.concatenate([bias_query, jnp.zeros_like(bias_query), bias_value])
    qkv_rows = low(low_back(jnp.dot(act_one, low(qkv_weight), precision=highest) + qkv_bias))
    attended = low(low_back(attend(qkv_rows, seq_ids)))
    residual = values + low_back(jnp.dot(attended, low(out_weight), precision=highest) + bias_out)
    act_two = low(layer_norm(residual, gain_two, shift_two))
    up_rows = low_back(jnp.dot(act_two, low(up_weight), precision=highest) + bias_up)
    hidden = low(jax.nn.gelu(up_rows, approximate=True))
    return residual + low_back(jnp.dot(hidden, low(down_weight), precision=highest) + bias_down)

def factored_step(gradient, weight, rows_old, cols_old, decay_rate):
    squares = gradient * gradient
    rows_new = decay_rate * rows_old + (1.0 - decay_rate) * (lax.optimization_barrier(jnp.mean(squares, axis=1)) + eps_second)
    cols_new = decay_rate * cols_old + (1.0 - decay_rate) * (lax.optimization_barrier(jnp.mean(squares, axis=0)) + eps_second)
    second = rows_new[:, None] * cols_new[None, :] / jnp.mean(rows_new)
    update = gradient * lax.rsqrt(second)
    rms_update = jnp.sqrt(jnp.mean(update * update))
    rms_weight = jnp.sqrt(jnp.mean(weight * weight))
    new_weight = weight - rate_step * rms_weight * update / jnp.maximum(1.0, rms_update / clip_level)
    return (new_weight, rows_new, cols_new, rms_update)

def reference(tokens, cotangent, seq_lengths, qkv_weight, out_weight, up_weight, down_weight, vectors, row_state, down_rows, col_state, vector_state):
    token_groups = tokens.astype(jnp.float32).reshape(GROUPS, GROUP, D)
    grad_groups = cotangent.astype(jnp.float32).reshape(GROUPS, GROUP, D)
    params = (vectors, qkv_weight, out_weight, up_weight, down_weight)
    positions = jnp.arange(GROUP, dtype=jnp.int32)

    def one_group(totals, group_item):
        inputs, grad_out, lengths = group_item
        seq_ids = sequence_ids(positions, lengths)

        def forward(values, *weight_args):
            return group_forward(values, seq_ids, *weight_args)
        outputs, pull_back = jax.vjp(forward, inputs, *params)
        pulled = pull_back(grad_out)
        totals = tuple((t + g for t, g in zip(totals, pulled[1:])))
        return (totals, (outputs.astype(jnp.bfloat16), pulled[0].astype(jnp.bfloat16)))
    zeros = tuple((jnp.zeros_like(p) for p in params))
    totals, (outputs, grads_in) = lax.scan(one_group, zeros, (token_groups, grad_groups, seq_lengths))
    vector_grad, qkv_grad, out_grad, up_grad, down_grad = totals
    block_out = outputs.reshape(TOKENS, D)
    tokens_grad = grads_in.reshape(TOKENS, D)
    decay_rate = 1.0 - STEP ** (-0.8)
    col_edges = [0, 3 * D, 4 * D, 4 * D + FF, 5 * D + FF]
    matrices = [(qkv_grad, qkv_weight, row_state[0]), (out_grad, out_weight, row_state[1]), (up_grad, up_weight, row_state[2]), (down_grad, down_weight, down_rows)]
    results = [factored_step(gradient, weight, rows_old, col_state[col_edges[n]:col_edges[n + 1]], decay_rate) for n, (gradient, weight, rows_old) in enumerate(matrices)]
    qkv_new, out_new, up_new, down_new = [item_result[0] for item_result in results]
    row_state_new = jnp.stack([results[0][1], results[1][1], results[2][1]])
    down_rows_new = results[3][1]
    col_state_new = jnp.concatenate([item_result[2] for item_result in results])
    vector_state_new = decay_rate * vector_state + (1.0 - decay_rate) * (vector_grad * vector_grad + eps_second)
    vector_step = vector_grad * lax.rsqrt(vector_state_new)
    vector_rms = jnp.sqrt(jnp.mean(vector_step * vector_step))
    vector_new = vectors - rate_step * jnp.sqrt(jnp.mean(vectors * vectors)) * vector_step / jnp.maximum(1.0, vector_rms / clip_level)
    update_rms = jnp.stack([results[0][3], results[1][3], results[2][3], results[3][3], vector_rms])
    return (block_out, tokens_grad, qkv_grad, out_grad, up_grad, down_grad, vector_grad, qkv_new, out_new, up_new, down_new, vector_new, qkv_new.astype(jnp.bfloat16), out_new.astype(jnp.bfloat16), up_new.astype(jnp.bfloat16), down_new.astype(jnp.bfloat16), row_state_new, down_rows_new, col_state_new, vector_state_new, update_rms)
```

```python
import functools

import jax
import jax.numpy as jnp
from jax import lax
from jax.experimental import pallas as pl
from jax.experimental.pallas import tpu as pltpu
from jax.sharding import PartitionSpec as P

HEADS = 16
STEP = 10
BLOCK = 256


eps_norm = 1e-05
eps_second = 1e-30
rate_step = 0.5
clip_level = 1.0
masked = -1e30
gelu_root = (2.0 / 3.141592653589793) ** 0.5
gelu_cubic = 0.044715

f32 = jnp.float32
bf16 = jnp.bfloat16


def norm_parts(values):
    average = jnp.mean(values, axis=-1, keepdims=True)
    centred = values - average
    inv_std = lax.rsqrt(jnp.mean(centred * centred, axis=-1, keepdims=True) + eps_norm)
    return (centred * inv_std, inv_std)


def norm_back(grad_out, normed, inv_std, gain_vec):
    grad_normed = grad_out * gain_vec
    inner_mean = jnp.mean(grad_normed * normed, axis=-1, keepdims=True)
    centred = grad_normed - jnp.mean(grad_normed, axis=-1, keepdims=True)
    return (centred - normed * inner_mean) * inv_std


def gelu_value(pre_act):
    curve = jnp.tanh(gelu_root * (pre_act + gelu_cubic * pre_act * pre_act * pre_act))
    return 0.5 * pre_act * (1.0 + curve)


def gelu_slope(pre_act):
    square = pre_act * pre_act
    curve = jnp.tanh(gelu_root * (pre_act + gelu_cubic * square * pre_act))
    inner = gelu_root * (1.0 + 3.0 * gelu_cubic * square)
    return 0.5 * (1.0 + curve) + 0.5 * pre_act * (1.0 - curve * curve) * inner


def dot(left_side, right_side):
    return jnp.dot(left_side, right_side, preferred_element_type=f32)


def dot_right(left_side, right_side):
    return lax.dot_general(
        left_side, right_side, (((1,), (1,)), ((), ())), preferred_element_type=f32
    )


def dot_rows(left_side, right_side):
    return lax.dot_general(
        left_side, right_side, (((0,), (0,)), ((), ())), preferred_element_type=f32
    )


def pick(stack, index, axis=0):
    return lax.dynamic_index_in_dim(stack, index, axis, keepdims=False)


def place(stack, part, index, axis=0):
    return lax.dynamic_update_index_in_dim(stack, part, index, axis)


def head_rows(number, head_width):
    return slice(number * head_width, (number + 1) * head_width)


def lane_masks(block_rows, width, heads):
    lanes = lax.broadcasted_iota(jnp.int32, (block_rows, width), 1)
    head_width = width // heads
    return [
        (lanes >= number * head_width) & (lanes < (number + 1) * head_width)
        for number in range(heads)
    ]


def allowed_pairs(key_block, query_block, start_row, block):
    key_pos = lax.broadcasted_iota(jnp.int32, (block, block), 0) + key_block * block
    query_pos = lax.broadcasted_iota(jnp.int32, (block, block), 1) + query_block * block
    return (key_pos <= query_pos) & (key_pos >= start_row)


def key_offsets(key_block, query_block, block):
    rows = lax.broadcasted_iota(jnp.int32, (block, 1), 0)
    return (rows + (key_block - query_block) * block).astype(f32)


def turned(values):
    return jnp.transpose(values.astype(f32))


def forward_kernel(heads, block, low_ref, mid_ref, slope_ref, start_ref, qkv_ref, out_ref, log_ref, values_turned):
    tokens = qkv_ref.shape[0]
    width = qkv_ref.shape[1] // 3
    head_width = width // heads
    blocks = tokens // block
    query_block = pl.program_id(0)

    @pl.when(query_block == 0)
    def _():
        for number in range(blocks):
            piece = qkv_ref[number * block : (number + 1) * block, 2 * width :]
            values_turned[number] = turned(piece).astype(bf16)

    first_row = pl.multiple_of(query_block * block, block)
    queries = qkv_ref[pl.ds(first_row, block), :width].astype(f32) * head_width ** (-0.5)
    queries = turned(queries).astype(bf16)
    start_row = start_ref[query_block]
    lanes = lane_masks(block, width, heads)
    zero = jnp.zeros((block, width), bf16)

    def step(key_block, state, with_mask):
        key_row = pl.multiple_of(key_block * block, block)
        keys = qkv_ref[pl.ds(key_row, block), width : 2 * width]
        offsets = key_offsets(key_block, query_block, block)
        allowed = allowed_pairs(key_block, query_block, start_row, block) if with_mask else None
        result = []
        for number in range(heads):
            best, total, gathered = state[3 * number : 3 * number + 3]
            scores = dot(jnp.where(lanes[number], keys, zero), queries)
            scores = scores + slope_ref[number] * offsets
            if with_mask:
                scores = jnp.where(allowed, scores, masked)
            new_best = jnp.maximum(best, jnp.max(scores, axis=0, keepdims=True))
            weights = jnp.exp(scores - new_best)
            fade = jnp.exp(best - new_best)
            value_rows = values_turned[key_block, head_rows(number, head_width), :]
            result += [
                new_best,
                total * fade + jnp.sum(weights, axis=0, keepdims=True),
                gathered * fade + dot(value_rows, weights.astype(bf16)),
            ]
        return tuple(result)

    state = ()
    for number in range(heads):
        state += (
            jnp.full((1, block), masked, f32),
            jnp.zeros((1, block), f32),
            jnp.zeros((head_width, block), f32),
        )
    low, mid = low_ref[query_block], mid_ref[query_block]
    state = lax.fori_loop(low, mid, functools.partial(step, with_mask=True), state)
    state = lax.fori_loop(mid, query_block, functools.partial(step, with_mask=False), state)
    state = step(query_block, state, True)
    columns = []
    for number in range(heads):
        best, total, gathered = state[3 * number : 3 * number + 3]
        columns.append(gathered / total)
        log_ref[0, number : number + 1, :] = best + jnp.log(total)
    out_ref[...] = jnp.transpose(jnp.concatenate(columns, axis=0)).astype(bf16)


def backward_kernel(
    heads,
    block,
    full_ref,
    high_ref,
    slope_ref,
    start_ref,
    log_ref,
    qkv_ref,
    grad_ref,
    out_ref,
    result_ref,
    queries_turned,
    grads_turned,
    keys_turned,
    delta_rows,
    query_grads,
):
    tokens = qkv_ref.shape[0]
    width = qkv_ref.shape[1] // 3
    head_width = width // heads
    scale = head_width ** (-0.5)
    blocks = tokens // block
    key_block = pl.program_id(0)

    @pl.when(key_block == 0)
    def _():
        for number in range(blocks):
            rows = slice(number * block, (number + 1) * block)
            queries_turned[number] = turned(qkv_ref[rows, :width].astype(f32) * scale).astype(bf16)
            keys_turned[number] = turned(qkv_ref[rows, width : 2 * width]).astype(bf16)
            grads = grad_ref[rows, :].astype(f32)
            grads_turned[number] = turned(grads).astype(bf16)
            product = turned(grads * out_ref[rows, :].astype(f32))
            for head in range(heads):
                delta_rows[number, head : head + 1, :] = jnp.sum(
                    product[head_rows(head, head_width)], axis=0, keepdims=True
                )
            query_grads[number] = jnp.zeros((width, block), f32)

    lanes = lane_masks(block, width, heads)
    zero = jnp.zeros((block, width), bf16)
    key_row = pl.multiple_of(key_block * block, block)
    keys = qkv_ref[pl.ds(key_row, block), width : 2 * width]
    values = qkv_ref[pl.ds(key_row, block), 2 * width :]

    def step(query_block, state, with_mask):
        key_total, value_total = state
        query_row = pl.multiple_of(query_block * block, block)
        queries = qkv_ref[pl.ds(query_row, block), :width]
        grads = grad_ref[pl.ds(query_row, block), :]
        offsets = key_offsets(key_block, query_block, block)
        if with_mask:
            allowed = allowed_pairs(key_block, query_block, start_ref[query_block], block)
        for number in range(heads):
            scores = dot(jnp.where(lanes[number], keys, zero), queries_turned[query_block])
            scores = scores + slope_ref[number] * offsets - log_ref[query_block, number : number + 1, :]
            if with_mask:
                scores = jnp.where(allowed, scores, masked)
            probabilities = jnp.exp(scores)
            grad_weights = dot(jnp.where(lanes[number], values, zero), grads_turned[query_block])
            grad_scores = probabilities * (
                grad_weights - delta_rows[query_block, number : number + 1, :]
            )
            weights = probabilities.astype(bf16)
            grad_scores = grad_scores.astype(bf16)
            value_total = value_total + dot(weights, jnp.where(lanes[number], grads, zero))
            key_total = key_total + dot(grad_scores, jnp.where(lanes[number], queries, zero))
            rows = head_rows(number, head_width)
            query_grads[query_block, rows, :] += dot(keys_turned[key_block, rows, :], grad_scores)
        return (key_total, value_total)

    state = (jnp.zeros((block, width), f32), jnp.zeros((block, width), f32))
    state = step(key_block, state, True)
    full, high = full_ref[key_block], high_ref[key_block]
    state = lax.fori_loop(key_block + 1, full, functools.partial(step, with_mask=False), state)
    state = lax.fori_loop(full, high, functools.partial(step, with_mask=True), state)
    result_ref[pl.ds(key_row, block), width : 2 * width] = (state[0] * scale).astype(bf16)
    result_ref[pl.ds(key_row, block), 2 * width :] = state[1].astype(bf16)

    @pl.when(key_block == blocks - 1)
    def _():
        for number in range(blocks):
            rows = slice(number * block, (number + 1) * block)
            result_ref[rows, :width] = jnp.transpose(query_grads[number] * scale).astype(bf16)


def block_plan(lengths, tokens, block):
    ends = jnp.cumsum(lengths)
    positions = jnp.arange(tokens, dtype=jnp.int32)
    passed = positions[:, None] >= ends[None, :]
    starts = jnp.max(jnp.where(passed, ends[None, :], 0), axis=1).astype(jnp.int32)
    finish = jnp.min(jnp.where(passed, tokens, ends[None, :]), axis=1).astype(jnp.int32)
    blocks = tokens // block
    number = jnp.arange(blocks, dtype=jnp.int32)
    first_start = starts[::block]
    last_start = starts[block - 1 :: block]
    low = first_start // block
    mid = jnp.clip((last_start + block - 1) // block, low, number)
    high = (finish[block - 1 :: block] - 1) // block + 1
    full = jnp.clip(finish[::block] // block, number + 1, high)
    return (starts.reshape(blocks, 1, block), low, mid, full, high)


def scalar_spec():
    return pl.BlockSpec(memory_space=pltpu.SMEM)


def whole_spec(shape):
    return pl.BlockSpec(shape, lambda step: (0,) * len(shape))


def attend_forward(qkv, plan, slopes, heads, block):
    tokens, triple = qkv.shape
    width = triple // 3
    blocks = tokens // block
    starts, low, mid, full, high = plan
    return pl.pallas_call(
        functools.partial(forward_kernel, heads, block),
        grid=(blocks,),
        in_specs=[
            scalar_spec(),
            scalar_spec(),
            scalar_spec(),
            whole_spec((blocks, 1, block)),
            whole_spec((tokens, triple)),
        ],
        out_specs=[
            pl.BlockSpec((block, width), lambda step: (step, 0)),
            pl.BlockSpec((1, heads, block), lambda step: (step, 0, 0)),
        ],
        out_shape=[
            jax.ShapeDtypeStruct((tokens, width), bf16),
            jax.ShapeDtypeStruct((blocks, heads, block), f32),
        ],
        scratch_shapes=[pltpu.VMEM((blocks, width, block), bf16)],
        compiler_params=pltpu.CompilerParams(
            dimension_semantics=("arbitrary",), vmem_limit_bytes=32 * 1024 * 1024
        ),
        cost_estimate=pl.CostEstimate(
            flops=3 * tokens * tokens * 256 * heads,
            bytes_accessed=10 * tokens * width,
            transcendentals=tokens * tokens * heads // 2,
        ),
        name="attend_forward",
    )(low, mid, slopes, starts, qkv)


def attend_backward(qkv, grads, outputs, logs, plan, slopes, heads, block):
    tokens, triple = qkv.shape
    width = triple // 3
    blocks = tokens // block
    starts, low, mid, full, high = plan
    return pl.pallas_call(
        functools.partial(backward_kernel, heads, block),
        grid=(blocks,),
        in_specs=[
            scalar_spec(),
            scalar_spec(),
            scalar_spec(),
            whole_spec((blocks, 1, block)),
            whole_spec((blocks, heads, block)),
            whole_spec((tokens, triple)),
            whole_spec((tokens, width)),
            whole_spec((tokens, width)),
        ],
        out_specs=whole_spec((tokens, triple)),
        out_shape=jax.ShapeDtypeStruct((tokens, triple), bf16),
        scratch_shapes=[
            pltpu.VMEM((blocks, width, block), bf16),
            pltpu.VMEM((blocks, width, block), bf16),
            pltpu.VMEM((blocks, width, block), bf16),
            pltpu.VMEM((blocks, heads, block), f32),
            pltpu.VMEM((blocks, width, block), f32),
        ],
        compiler_params=pltpu.CompilerParams(
            dimension_semantics=("arbitrary",), vmem_limit_bytes=40 * 1024 * 1024
        ),
        cost_estimate=pl.CostEstimate(
            flops=8 * tokens * tokens * 256 * heads,
            bytes_accessed=20 * tokens * width,
            transcendentals=tokens * tokens * heads // 2,
        ),
        name="attend_backward",
    )(full, high, slopes, starts, logs, qkv, grads, outputs)


class Moves:
    def __init__(self):
        self.shards = lax.axis_size("shard")
        self.reps = lax.axis_size("rep")
        self.half = self.shards // 2
        self.chips = self.reps // 2
        self.shard = lax.axis_index("shard")
        self.rep = lax.axis_index("rep")
        self.core = self.rep % 2
        self.chip = self.rep // 2
        self.side = self.shard // self.half
        self.member = self.shard % self.half + self.core * self.half

    def core_swap(self, part):
        return lax.ppermute(part, "rep", [(r, r ^ 1) for r in range(self.reps)])

    def chip_swap(self, part, bits):
        return lax.ppermute(part, "rep", [(r, r ^ (2 * bits)) for r in range(self.reps)])

    def shard_swap(self, part, bits):
        return lax.ppermute(part, "shard", [(s, s ^ bits) for s in range(self.shards)])

    def shard_shift(self, part, shift):
        return lax.ppermute(
            part, "shard", [(s, (s + shift) % self.shards) for s in range(self.shards)]
        )

    def home_swap(self, part):
        pairs = []
        for rep in range(self.reps):
            for shard in range(self.shards):
                side, core = shard // self.half, rep % 2
                to_rep, to_shard = rep, shard
                if side != core:
                    to_rep = rep ^ 1
                    to_shard = (shard + self.half) % self.shards
                pairs.append((rep * self.shards + shard, to_rep * self.shards + to_shard))
        return lax.ppermute(part, ("rep", "shard"), pairs)

    def member_swap(self, part, bits):
        pairs = []
        shard_bits, core_bit = bits % self.half, bits // self.half
        for rep in range(self.reps):
            for shard in range(self.shards):
                to_rep, to_shard = rep ^ core_bit, shard ^ shard_bits
                pairs.append((rep * self.shards + shard, to_rep * self.shards + to_shard))
        return lax.ppermute(part, ("rep", "shard"), pairs)

    def members_gather(self, part):
        held = [part]
        bits = 1
        while bits < self.half:
            held = held + [self.shard_swap(piece, bits) for piece in held]
            bits *= 2
        held = held + [self.core_swap(piece) for piece in held]
        stack = jnp.zeros((self.shards,) + part.shape, part.dtype)
        for number, piece in enumerate(held):
            stack = place(stack, piece, self.member ^ number)
        return stack

    def members_exchange(self, stack):
        result = jnp.zeros_like(stack)
        for bits in range(self.shards):
            piece = pick(stack, self.member ^ bits)
            if bits:
                piece = self.member_swap(piece, bits)
            result = place(result, piece, self.member ^ bits)
        return result

    def shards_gather(self, part):
        stack = jnp.zeros((self.shards,) + part.shape, part.dtype)
        stack = place(stack, part, self.shard)
        for step in range(1, self.shards):
            part = self.shard_shift(part, 1)
            stack = place(stack, part, (self.shard - step) % self.shards)
        return stack

    def shards_exchange(self, stack):
        result = jnp.zeros_like(stack)
        for shift in range(self.shards):
            piece = pick(stack, (self.shard + shift) % self.shards)
            if shift:
                piece = self.shard_shift(piece, shift)
            result = place(result, piece, (self.shard - shift) % self.shards)
        return result

    def chips_gather(self, part, axis):
        shape = part.shape[:axis] + (self.chips,) + part.shape[axis:]
        stack = jnp.zeros(shape, part.dtype)
        if self.chips == 4:
            cut = part.shape[0] // 2
            by_x, by_y = self.chip_swap(part, 1), self.chip_swap(part, 2)
            far = jnp.concatenate(
                [self.chip_swap(by_x[:cut], 2), self.chip_swap(by_y[cut:], 1)], axis=0
            )
            held = [part, by_x, by_y, far]
        else:
            held = [part]
            bits = 1
            while bits < self.chips:
                held = held + [self.chip_swap(piece, bits) for piece in held]
                bits *= 2
        for number, piece in enumerate(held):
            stack = place(stack, piece, self.chip ^ number, axis)
        return stack

    def chips_reduce(self, stack, axis):
        if self.chips == 4:
            shape = stack.shape[:axis] + (2, 2) + stack.shape[axis + 1 :]
            stack = stack.reshape(shape)
            bit_x, bit_y = self.chip % 2, self.chip // 2
            cut = shape[0] // 2
            first, second = stack[:cut], stack[cut:]
            got_first = self.chip_swap(pick(first, 1 - bit_x, axis + 1), 1)
            got_second = self.chip_swap(pick(second, 1 - bit_y, axis), 2)
            first = pick(first, bit_x, axis + 1).astype(f32) + got_first.astype(f32)
            second = pick(second, bit_y, axis).astype(f32) + got_second.astype(f32)
            got_first = self.chip_swap(pick(first, 1 - bit_y, axis).astype(bf16), 2)
            got_second = self.chip_swap(pick(second, 1 - bit_x, axis).astype(bf16), 1)
            first = pick(first, bit_y, axis) + got_first.astype(f32)
            second = pick(second, bit_x, axis) + got_second.astype(f32)
            return jnp.concatenate([first, second], axis=0)
        count = self.chips
        stack = stack.astype(f32)
        while count > 1:
            count //= 2
            shape = stack.shape[:axis] + (2, count) + stack.shape[axis + 1 :]
            stack = stack.reshape(shape)
            bit = (self.chip // count) % 2
            got = self.chip_swap(pick(stack, 1 - bit, axis).astype(bf16), count)
            stack = pick(stack, bit, axis) + got.astype(f32)
        return pick(stack, 0, axis)

    def core_pair(self, part):
        other = self.core_swap(part)
        first = jnp.where(self.core == 0, part, other)
        second = jnp.where(self.core == 0, other, part)
        return first, second

    def sum_all(self, vector):
        bits = 1
        while bits < self.reps:
            vector = vector + lax.ppermute(vector, "rep", [(r, r ^ bits) for r in range(self.reps)])
            bits *= 2
        return self.sum_shards(vector)

    def sum_shards(self, vector):
        bits = 1
        while bits < self.shards:
            vector = vector + self.shard_swap(vector, bits)
            bits *= 2
        return vector


def factor_stats(gradient, weight, rows_old, decay_rate):
    square = gradient * gradient
    rows_new = decay_rate * rows_old + (1.0 - decay_rate) * (jnp.mean(square, axis=1) + eps_second)
    col_squares = jnp.sum(square, axis=0)
    col_scaled = jnp.sum(square / rows_new[:, None], axis=0)
    scalars = jnp.stack([jnp.sum(rows_new), jnp.sum(weight * weight)])
    return rows_new, [col_squares, col_scaled, scalars]


def factor_apply(gradient, weight, rows_new, sums, cols_old, height, decay_rate):
    col_squares, col_scaled, scalars = sums
    breadth = gradient.shape[1]
    cols_new = decay_rate * cols_old + (1.0 - decay_rate) * (col_squares / height + eps_second)
    row_mean = scalars[0] / height
    rms_update = jnp.sqrt(row_mean / (height * breadth) * jnp.sum(col_scaled / cols_new))
    rms_weight = jnp.sqrt(scalars[1] / (height * breadth))
    factor = rate_step * rms_weight * jnp.sqrt(row_mean) / jnp.maximum(1.0, rms_update / clip_level)
    new_weight = weight - gradient * (factor * lax.rsqrt(rows_new))[:, None] * lax.rsqrt(cols_new)[None, :]
    return new_weight, cols_new, rms_update


def summed(moves, lists):
    flat = [entry for group in lists for entry in group]
    sizes = [entry.shape[0] for entry in flat]
    total = moves.sum_shards(jnp.concatenate(flat))
    result, offset = [], 0
    for size in sizes:
        result.append(total[offset : offset + size])
        offset += size
    return [result[3 * n : 3 * n + 3] for n in range(len(lists))]


def on_device(
    tokens,
    cotangent,
    seq_lengths,
    qkv_weight,
    out_weight,
    up_weight,
    down_weight,
    vectors,
    row_state,
    down_rows,
    col_state,
    vector_state,
):
    moves = Moves()
    shards, half, chips, core = moves.shards, moves.half, moves.chips, moves.core
    row_count, width = tokens.shape
    hidden_width = up_weight.shape[1]
    group_rows = row_count * shards
    heads = HEADS // shards
    head_width = width // HEADS
    span = heads * head_width
    member = moves.member
    decay_rate = 1.0 - STEP ** (-0.8)
    head_number = (member * heads + jnp.arange(heads, dtype=jnp.int32)).astype(f32)
    slopes = jnp.exp2(-8.0 * (head_number + 1.0) / HEADS)

    gain_one = vectors[0:width]
    shift_one = vectors[width : 2 * width]
    bias_query = vectors[2 * width : 3 * width]
    bias_value = vectors[3 * width : 4 * width]
    bias_out = vectors[4 * width : 5 * width]
    gain_two = vectors[5 * width : 6 * width]
    shift_two = vectors[6 * width : 7 * width]
    bias_up = vectors[7 * width : 7 * width + hidden_width]
    bias_down = vectors[7 * width + hidden_width :]

    other_lengths = moves.core_swap(seq_lengths)
    lengths = jnp.where(moves.side == core, seq_lengths, other_lengths)[0]
    plan = block_plan(lengths, group_rows, BLOCK)
    home_tokens = moves.home_swap(tokens)
    inputs = home_tokens.astype(f32)
    normed_one, inv_std_one = norm_parts(inputs)
    act_one = (normed_one * gain_one + shift_one).astype(bf16)

    rows_z = width // shards
    rows_piece = rows_z // chips
    my_rows = lax.dynamic_slice_in_dim(qkv_weight, moves.chip * rows_piece, rows_piece, 0)
    blocks_of = my_rows.astype(bf16).reshape(rows_piece, 3, shards, span).transpose(2, 0, 1, 3)
    blocks_of = blocks_of.reshape(shards, rows_piece, 3 * span)
    to_shard = jnp.stack(
        [pick(blocks_of, shard % half + core * half) for shard in range(shards)]
    )
    qkv_part = moves.shards_exchange(to_shard)
    qkv_cols = moves.chips_gather(qkv_part, 1).reshape(width, 3 * span)

    act_all = moves.members_gather(act_one).reshape(group_rows, width)
    bias_q_part = lax.dynamic_slice_in_dim(bias_query, member * span, span)
    bias_v_part = lax.dynamic_slice_in_dim(bias_value, member * span, span)
    qkv_bias = jnp.concatenate([bias_q_part, jnp.zeros_like(bias_q_part), bias_v_part])
    qkv_rows = (dot(act_all, qkv_cols) + qkv_bias).astype(bf16)

    half_cols = hidden_width // (2 * shards)
    up_rows_mine = lax.dynamic_slice_in_dim(up_weight, moves.chip * rows_piece, rows_piece, 0)
    up_mine = pick(up_rows_mine.reshape(rows_piece, shards, 2, half_cols), core, 2)
    up_mine = up_mine.reshape(rows_piece, shards * half_cols)
    out_rows_mine = lax.dynamic_slice_in_dim(out_weight, moves.chip * rows_piece, rows_piece, 0)
    out_mine = lax.dynamic_slice_in_dim(out_rows_mine, core * (width // 2), width // 2, 1)
    up_out_mine = jnp.concatenate([up_mine, out_mine], axis=1).astype(bf16)
    up_wide = shards * half_cols
    down_piece = half_cols // chips
    down_mine = lax.dynamic_slice_in_dim(
        down_weight, core * half_cols + moves.chip * down_piece, down_piece, 0
    ).astype(bf16)
    up_out_all = moves.chips_gather(moves.shards_gather(up_out_mine), 1)
    up_out_all = up_out_all.reshape(width, up_wide + width // 2)
    up_half = up_out_all[:, :up_wide]
    out_first, out_second = moves.core_pair(up_out_all[:, up_wide:])
    out_low = jnp.concatenate([out_first, out_second], axis=1)
    down_half = moves.chips_gather(moves.shards_gather(down_mine), 1)
    down_half = down_half.reshape(up_wide, width)

    attended_cols, logs = attend_forward(qkv_rows, plan, slopes, heads, BLOCK)
    attended_parts = moves.members_exchange(attended_cols.reshape(shards, row_count, span))
    attended = jnp.concatenate([attended_parts[k] for k in range(shards)], axis=1)
    residual = inputs + dot(attended, out_low) + bias_out
    normed_two, inv_std_two = norm_parts(residual)
    act_two = (normed_two * gain_two + shift_two).astype(bf16)

    home_cot = moves.home_swap(cotangent)
    cot_pair = jnp.concatenate([home_cot, moves.core_swap(home_cot)], axis=0)
    act_two_pair = jnp.concatenate([act_two, moves.core_swap(act_two)], axis=0)
    bias_up_half = pick(bias_up.reshape(shards, 2, half_cols), core, 1).reshape(up_wide)
    up_pair = dot(act_two_pair, up_half) + bias_up_half
    hidden_pair = gelu_value(up_pair).astype(bf16)
    down_other = moves.core_swap(dot(hidden_pair[row_count:], down_half).astype(bf16))
    block_out = (
        residual + dot(hidden_pair[:row_count], down_half) + down_other.astype(f32) + bias_down
    ).astype(bf16)
    block_out = moves.home_swap(block_out)
    grad_y = home_cot.astype(f32)
    grad_bias_down = jnp.sum(grad_y, axis=0)
    grad_up_pair = (dot_right(cot_pair, down_half) * gelu_slope(up_pair)).astype(bf16)
    grad_bias_up = jnp.sum(grad_up_pair, axis=0, dtype=f32)
    back_other = moves.core_swap(dot_right(grad_up_pair[row_count:], up_half).astype(bf16))
    grad_act_two = dot_right(grad_up_pair[:row_count], up_half) + back_other.astype(f32)
    grad_gain_two = jnp.sum(grad_act_two * normed_two, axis=0)
    grad_shift_two = jnp.sum(grad_act_two, axis=0)
    grad_residual = grad_y + norm_back(grad_act_two, normed_two, inv_std_two, gain_two)
    grad_attn = grad_residual.astype(bf16)
    grad_bias_out = jnp.sum(grad_attn, axis=0, dtype=f32)
    grad_attended = dot_right(grad_attn, out_low).astype(bf16)

    down_terms = dot_rows(hidden_pair, cot_pair).astype(bf16)
    down_terms = down_terms.reshape(shards, chips, down_piece, width)
    attended_pair = jnp.concatenate([attended, moves.core_swap(attended)], axis=0)
    attn_halves = grad_attn.reshape(row_count, 2, width // 2)
    attn_pair = jnp.concatenate(
        [pick(attn_halves, core, 1), moves.core_swap(pick(attn_halves, 1 - core, 1))], axis=0
    )
    up_out_terms = jnp.concatenate(
        [
            dot_rows(act_two_pair, grad_up_pair).astype(bf16),
            dot_rows(attended_pair, attn_pair).astype(bf16),
        ],
        axis=1,
    ).reshape(shards, chips, rows_piece, up_wide + width // 2)

    def owned(terms):
        piece = moves.chips_reduce(terms, 1).astype(bf16)
        return jnp.sum(moves.shards_exchange(piece).astype(f32), axis=0).astype(bf16)

    down_first, down_second = moves.core_pair(
        moves.chips_gather(owned(down_terms), 0).reshape(half_cols, width)
    )
    down_grad = jnp.concatenate([down_first, down_second], axis=0).astype(f32)
    up_out_first, up_out_second = moves.core_pair(
        moves.chips_gather(owned(up_out_terms), 0).reshape(rows_z, up_wide + width // 2)
    )
    out_grad = jnp.concatenate(
        [up_out_first[:, up_wide:], up_out_second[:, up_wide:]], axis=1
    ).astype(f32)
    up_columns = []
    for number in range(shards):
        part = slice(number * half_cols, (number + 1) * half_cols)
        up_columns += [up_out_first[:, part], up_out_second[:, part]]
    up_grad = jnp.concatenate(up_columns, axis=1).astype(f32)

    to_members = jnp.stack([grad_attended[:, k * span : (k + 1) * span] for k in range(shards)])
    grad_heads = moves.members_exchange(to_members).reshape(group_rows, span)
    grad_qkv = attend_backward(
        qkv_rows, grad_heads, attended_cols, logs, plan, slopes, heads, BLOCK
    )
    grad_bias_q_part = jnp.sum(grad_qkv[:, :span], axis=0, dtype=f32)
    grad_bias_v_part = jnp.sum(grad_qkv[:, 2 * span :], axis=0, dtype=f32)

    grad_halves = grad_qkv.reshape(2, half * row_count, 3 * span)
    sent = dot_right(pick(grad_halves, 1 - core), qkv_cols).astype(bf16)
    back = dot_right(pick(grad_halves, core), qkv_cols) + moves.core_swap(sent).astype(f32)
    back = back.reshape(half, row_count, width)
    count = half
    while count > 1:
        count //= 2
        back = back.reshape(2, count, row_count, width)
        bit = (moves.shard // count) % 2
        got = moves.shard_swap(pick(back, 1 - bit).astype(bf16), count)
        back = pick(back, bit) + got.astype(f32)
    grad_act_one = back.reshape(row_count, width)
    grad_gain_one = jnp.sum(grad_act_one * normed_one, axis=0)
    grad_shift_one = jnp.sum(grad_act_one, axis=0)
    grad_inputs = grad_residual + norm_back(grad_act_one, normed_one, inv_std_one, gain_one)
    tokens_grad = moves.home_swap(grad_inputs.astype(bf16))

    qkv_terms = dot_rows(act_all, grad_qkv).astype(bf16)
    qkv_terms = qkv_terms.reshape(shards, chips, rows_piece, 3 * span)
    qkv_piece = moves.shards_exchange(moves.chips_reduce(qkv_terms, 1).astype(bf16))
    qkv_piece = qkv_piece.astype(f32).reshape(2, half, rows_piece, 3 * span)
    qkv_piece = jnp.sum(qkv_piece, axis=0).astype(bf16).reshape(half * rows_piece, 3 * span)
    qkv_owned = moves.chips_gather(qkv_piece.reshape(half, rows_piece, 3 * span), 1)
    qkv_first, qkv_second = moves.core_pair(qkv_owned.reshape(half, rows_z, 3 * span))
    qkv_columns = []
    for kind in range(3):
        for source in (qkv_first, qkv_second):
            for number in range(half):
                qkv_columns.append(source[number][:, kind * span : (kind + 1) * span])
    qkv_grad = jnp.concatenate(qkv_columns, axis=1).astype(f32)

    stats = [
        factor_stats(qkv_grad, qkv_weight, row_state[0], decay_rate),
        factor_stats(out_grad, out_weight, row_state[1], decay_rate),
        factor_stats(up_grad, up_weight, row_state[2], decay_rate),
        factor_stats(down_grad, down_weight, down_rows, decay_rate),
    ]
    sums = summed(moves, [stats[1][1], stats[2][1], stats[3][1]])
    sums = summed(moves, [stats[0][1]]) + sums
    gradients = [qkv_grad, out_grad, up_grad, down_grad]
    weights = [qkv_weight, out_weight, up_weight, down_weight]
    heights = [width, width, width, hidden_width]
    new_weights, new_cols, rms_values = [], [], []
    offset = 0
    for number in range(4):
        end_col = offset + gradients[number].shape[1]
        new_weight, cols_new, rms_update = factor_apply(
            gradients[number],
            weights[number],
            stats[number][0],
            sums[number],
            col_state[offset:end_col],
            heights[number],
            decay_rate,
        )
        new_weights.append(new_weight)
        new_cols.append(cols_new)
        rms_values.append(rms_update)
        offset = end_col

    zero_heads = jnp.zeros((width,), f32)
    zero_up = jnp.zeros((shards, 2, half_cols), f32)
    vector_grad = moves.sum_all(
        jnp.concatenate(
            [
                grad_gain_one,
                grad_shift_one,
                lax.dynamic_update_slice_in_dim(zero_heads, grad_bias_q_part, member * span, 0),
                lax.dynamic_update_slice_in_dim(zero_heads, grad_bias_v_part, member * span, 0),
                grad_bias_out,
                grad_gain_two,
                grad_shift_two,
                place(zero_up, grad_bias_up.reshape(shards, half_cols), core, 1).reshape(-1),
                grad_bias_down,
            ]
        )
    )
    vector_state_new = decay_rate * vector_state + (1.0 - decay_rate) * (
        vector_grad * vector_grad + eps_second
    )
    vector_step = vector_grad * lax.rsqrt(vector_state_new)
    vector_rms = jnp.sqrt(jnp.mean(vector_step * vector_step))
    vector_new = vectors - rate_step * jnp.sqrt(
        jnp.mean(vectors * vectors)
    ) * vector_step / jnp.maximum(1.0, vector_rms / clip_level)
    update_rms = jnp.stack(rms_values + [vector_rms])
    return (
        block_out,
        tokens_grad,
        qkv_grad,
        out_grad,
        up_grad,
        down_grad,
        vector_grad,
        new_weights[0],
        new_weights[1],
        new_weights[2],
        new_weights[3],
        vector_new,
        new_weights[0].astype(bf16),
        new_weights[1].astype(bf16),
        new_weights[2].astype(bf16),
        new_weights[3].astype(bf16),
        jnp.stack([stats[0][0], stats[1][0], stats[2][0]]),
        stats[3][0],
        jnp.concatenate(new_cols),
        vector_state_new,
        update_rms,
    )


def solution(mesh):
    in_specs = (
        P(("rep", "shard"), None),
        P(("rep", "shard"), None),
        P("rep", None),
        P("shard", None),
        P("shard", None),
        P("shard", None),
        P("shard", None),
        P(),
        P(None, "shard"),
        P("shard"),
        P(),
        P(),
    )
    out_specs = (
        P(("rep", "shard"), None),
        P(("rep", "shard"), None),
        P("shard", None),
        P("shard", None),
        P("shard", None),
        P("shard", None),
        P(),
        P("shard", None),
        P("shard", None),
        P("shard", None),
        P("shard", None),
        P(),
        P("shard", None),
        P("shard", None),
        P("shard", None),
        P("shard", None),
        P(None, "shard"),
        P("shard"),
        P(),
        P(),
        P(),
    )
    return jax.shard_map(
        on_device, mesh=mesh, in_specs=in_specs, out_specs=out_specs, check_vma=False
    )
```

```python
import functools

import jax
import jax.numpy as jnp
from jax import lax
from jax.experimental import pallas as pl
from jax.experimental.pallas import tpu as pltpu
from jax.sharding import PartitionSpec as P

HEADS = 16
STEP = 10
BLOCK = 256


eps_norm = 1e-05
eps_second = 1e-30
rate_step = 0.5
clip_level = 1.0
masked = -1e30
gelu_root = (2.0 / 3.141592653589793) ** 0.5
gelu_cubic = 0.044715

f32 = jnp.float32
bf16 = jnp.bfloat16


def norm_parts(values):
    average = jnp.mean(values, axis=-1, keepdims=True)
    centred = values - average
    inv_std = lax.rsqrt(jnp.mean(centred * centred, axis=-1, keepdims=True) + eps_norm)
    return (centred * inv_std, inv_std)


def norm_back(grad_out, normed, inv_std, gain_vec):
    grad_normed = grad_out * gain_vec
    inner_mean = jnp.mean(grad_normed * normed, axis=-1, keepdims=True)
    centred = grad_normed - jnp.mean(grad_normed, axis=-1, keepdims=True)
    return (centred - normed * inner_mean) * inv_std


def gelu_value(pre_act):
    curve = jnp.tanh(gelu_root * (pre_act + gelu_cubic * pre_act * pre_act * pre_act))
    return 0.5 * pre_act * (1.0 + curve)


def gelu_slope(pre_act):
    square = pre_act * pre_act
    curve = jnp.tanh(gelu_root * (pre_act + gelu_cubic * square * pre_act))
    inner = gelu_root * (1.0 + 3.0 * gelu_cubic * square)
    return 0.5 * (1.0 + curve) + 0.5 * pre_act * (1.0 - curve * curve) * inner


def dot(left_side, right_side):
    return jnp.dot(left_side, right_side, preferred_element_type=f32)


def dot_right(left_side, right_side):
    return lax.dot_general(
        left_side, right_side, (((1,), (1,)), ((), ())), preferred_element_type=f32
    )


def dot_rows(left_side, right_side):
    return lax.dot_general(
        left_side, right_side, (((0,), (0,)), ((), ())), preferred_element_type=f32
    )


def pick(stack, index, axis=0):
    return lax.dynamic_index_in_dim(stack, index, axis, keepdims=False)


def place(stack, part, index, axis=0):
    return lax.dynamic_update_index_in_dim(stack, part, index, axis)


def head_rows(number, head_width):
    return slice(number * head_width, (number + 1) * head_width)


def lane_masks(block_rows, width, heads):
    lanes = lax.broadcasted_iota(jnp.int32, (block_rows, width), 1)
    head_width = width // heads
    return [
        (lanes >= number * head_width) & (lanes < (number + 1) * head_width)
        for number in range(heads)
    ]


def allowed_pairs(key_block, query_block, start_row, block):
    key_pos = lax.broadcasted_iota(jnp.int32, (block, block), 0) + key_block * block
    query_pos = lax.broadcasted_iota(jnp.int32, (block, block), 1) + query_block * block
    return (key_pos <= query_pos) & (key_pos >= start_row)


def key_offsets(key_block, query_block, block):
    rows = lax.broadcasted_iota(jnp.int32, (block, 1), 0)
    return (rows + (key_block - query_block) * block).astype(f32)


def turned(values):
    return jnp.transpose(values.astype(f32))


def head_stack(values, lanes):
    zero = jnp.zeros(values.shape, values.dtype)
    return jnp.concatenate([jnp.where(lane, values, zero) for lane in lanes], axis=0)


def eights(values, combine):
    rows, columns = values.shape
    return combine(values.reshape(rows // 8, 8, columns), axis=0)


def forward_kernel(
    heads,
    block,
    low_ref,
    mid_ref,
    slope_ref,
    start_ref,
    qkv_ref,
    out_ref,
    log_ref,
    values_turned,
    key_stack,
    score_ref,
):
    tokens = qkv_ref.shape[0]
    width = qkv_ref.shape[1] // 3
    head_width = width // heads
    blocks = tokens // block
    query_block = pl.program_id(0)

    @pl.when(query_block == 0)
    def _():
        lanes = lane_masks(block, width, heads)
        for number in range(blocks):
            rows = slice(number * block, (number + 1) * block)
            values_turned[number] = turned(qkv_ref[rows, 2 * width :]).astype(bf16)
            key_stack[number] = head_stack(qkv_ref[rows, width : 2 * width], lanes)

    first_row = pl.multiple_of(query_block * block, block)
    queries = qkv_ref[pl.ds(first_row, block), :width].astype(f32) * head_width ** (-0.5)
    queries = turned(queries).astype(bf16)
    start_row = start_ref[query_block]

    def score_step(key_block, bests, with_mask):
        scores = dot(key_stack[key_block], queries)
        offsets = key_offsets(key_block, query_block, block)
        allowed = allowed_pairs(key_block, query_block, start_row, block) if with_mask else None
        result = []
        for number in range(heads):
            rows = head_rows(number, block)
            part = scores[rows] + slope_ref[number] * offsets
            if with_mask:
                part = jnp.where(allowed, part, masked)
            score_ref[key_block, rows, :] = part
            result.append(jnp.maximum(bests[number], eights(part, jnp.max)))
        return tuple(result)

    low, mid = low_ref[query_block], mid_ref[query_block]
    bests = tuple(jnp.full((8, block), masked, f32) for _ in range(heads))
    bests = lax.fori_loop(low, mid, functools.partial(score_step, with_mask=True), bests)
    bests = lax.fori_loop(mid, query_block, functools.partial(score_step, with_mask=False), bests)
    bests = score_step(query_block, bests, True)
    bests = [jnp.max(best, axis=0, keepdims=True) for best in bests]

    def value_step(key_block, state):
        result = []
        for number in range(heads):
            total, gathered = state[2 * number : 2 * number + 2]
            weights = jnp.exp(score_ref[key_block, head_rows(number, block), :] - bests[number])
            value_rows = values_turned[key_block, head_rows(number, head_width), :]
            result += [
                total + eights(weights, jnp.sum),
                gathered + dot(value_rows, weights.astype(bf16)),
            ]
        return tuple(result)

    state = ()
    for number in range(heads):
        state += (jnp.zeros((8, block), f32), jnp.zeros((head_width, block), f32))
    state = lax.fori_loop(low, query_block + 1, value_step, state)
    columns = []
    for number in range(heads):
        total = jnp.sum(state[2 * number], axis=0, keepdims=True)
        columns.append(state[2 * number + 1] / total)
        log_ref[0, number : number + 1, :] = bests[number] + jnp.log(total)
    out_ref[...] = jnp.transpose(jnp.concatenate(columns, axis=0)).astype(bf16)


def backward_kernel(heads, block, first_head, merge, *refs):
    full_ref, high_ref, slope_ref, start_ref, log_ref, qkv_ref, grad_ref, out_ref = refs[:8]
    earlier_ref = refs[8] if merge else None
    result_ref = refs[9 if merge else 8]
    (
        queries_turned,
        grads_turned,
        keys_turned,
        query_stack,
        grad_stack,
        key_stack,
        value_stack,
        delta_rows,
        query_grads,
    ) = refs[10 if merge else 9 :]
    tokens, all_width = grad_ref.shape
    head_width = all_width // log_ref.shape[1]
    width = heads * head_width
    scale = head_width ** (-0.5)
    blocks = tokens // block
    key_block = pl.program_id(0)
    lanes = lane_masks(block, width, heads)

    def columns(kind):
        start = kind * all_width + first_head * head_width
        return slice(start, start + width)

    def target(kind):
        start = (kind * all_width + first_head * head_width) if merge else kind * width
        return slice(start, start + width)

    @pl.when(key_block == 0)
    def _():
        for number in range(blocks):
            rows = slice(number * block, (number + 1) * block)
            queries = qkv_ref[rows, columns(0)]
            queries_turned[number] = turned(queries.astype(f32) * scale).astype(bf16)
            query_stack[number] = head_stack(queries, lanes)
            keys_turned[number] = turned(qkv_ref[rows, columns(1)]).astype(bf16)
            grads = grad_ref[rows, columns(0)]
            grad_stack[number] = head_stack(grads, lanes)
            grads = grads.astype(f32)
            grads_turned[number] = turned(grads).astype(bf16)
            product = turned(grads * out_ref[rows, columns(0)].astype(f32))
            for head in range(heads):
                delta_rows[number, head : head + 1, :] = jnp.sum(
                    product[head_rows(head, head_width)], axis=0, keepdims=True
                )
            query_grads[number] = jnp.zeros((width, block), f32)

    key_row = pl.multiple_of(key_block * block, block)
    key_stack[...] = head_stack(qkv_ref[pl.ds(key_row, block), columns(1)], lanes)
    value_stack[...] = head_stack(qkv_ref[pl.ds(key_row, block), columns(2)], lanes)

    def step(query_block, state, with_mask):
        key_total, value_total = state
        scores = dot(key_stack[...], queries_turned[query_block])
        grad_weights = dot(value_stack[...], grads_turned[query_block])
        offsets = key_offsets(key_block, query_block, block)
        if with_mask:
            allowed = allowed_pairs(key_block, query_block, start_ref[query_block], block)
        weight_list, grad_list = [], []
        for number in range(heads):
            rows = head_rows(number, block)
            head = first_head + number
            part = scores[rows] + slope_ref[head] * offsets
            part = part - log_ref[query_block, head : head + 1, :]
            if with_mask:
                part = jnp.where(allowed, part, masked)
            probabilities = jnp.exp(part)
            delta = delta_rows[query_block, number : number + 1, :]
            grad_scores = (probabilities * (grad_weights[rows] - delta)).astype(bf16)
            weight_list.append(probabilities.astype(bf16))
            grad_list.append(grad_scores)
            rows = head_rows(number, head_width)
            query_grads[query_block, rows, :] += dot(keys_turned[key_block, rows, :], grad_scores)
        weight_row = jnp.concatenate(weight_list, axis=1)
        grad_row = jnp.concatenate(grad_list, axis=1)
        return (
            key_total + dot(grad_row, query_stack[query_block]),
            value_total + dot(weight_row, grad_stack[query_block]),
        )

    state = (jnp.zeros((block, width), f32), jnp.zeros((block, width), f32))
    state = step(key_block, state, True)
    full, high = full_ref[key_block], high_ref[key_block]
    state = lax.fori_loop(key_block + 1, full, functools.partial(step, with_mask=False), state)
    state = lax.fori_loop(full, high, functools.partial(step, with_mask=True), state)
    result_ref[pl.ds(key_row, block), target(1)] = (state[0] * scale).astype(bf16)
    result_ref[pl.ds(key_row, block), target(2)] = state[1].astype(bf16)
    if merge:
        other = first_head * head_width
        for kind in range(3):
            result_ref[pl.ds(key_row, block), kind * all_width : kind * all_width + other] = earlier_ref[
                pl.ds(key_row, block), kind * other : (kind + 1) * other
            ]

    @pl.when(key_block == blocks - 1)
    def _():
        for number in range(blocks):
            rows = slice(number * block, (number + 1) * block)
            result_ref[rows, target(0)] = jnp.transpose(query_grads[number] * scale).astype(bf16)


def block_plan(lengths, tokens, block):
    ends = jnp.cumsum(lengths)
    positions = jnp.arange(tokens, dtype=jnp.int32)
    passed = positions[:, None] >= ends[None, :]
    starts = jnp.max(jnp.where(passed, ends[None, :], 0), axis=1).astype(jnp.int32)
    finish = jnp.min(jnp.where(passed, tokens, ends[None, :]), axis=1).astype(jnp.int32)
    blocks = tokens // block
    number = jnp.arange(blocks, dtype=jnp.int32)
    first_start = starts[::block]
    last_start = starts[block - 1 :: block]
    low = first_start // block
    mid = jnp.clip((last_start + block - 1) // block, low, number)
    high = (finish[block - 1 :: block] - 1) // block + 1
    full = jnp.clip(finish[::block] // block, number + 1, high)
    return (starts.reshape(blocks, 1, block), low, mid, full, high)


def scalar_spec():
    return pl.BlockSpec(memory_space=pltpu.SMEM)


def whole_spec(shape):
    return pl.BlockSpec(shape, lambda step: (0,) * len(shape), pipeline_mode=pl.Buffered(1))


def attend_forward(qkv, plan, slopes, heads, block):
    tokens, triple = qkv.shape
    width = triple // 3
    blocks = tokens // block
    starts, low, mid, full, high = plan
    return pl.pallas_call(
        functools.partial(forward_kernel, heads, block),
        grid=(blocks,),
        in_specs=[
            scalar_spec(),
            scalar_spec(),
            scalar_spec(),
            whole_spec((blocks, 1, block)),
            whole_spec((tokens, triple)),
        ],
        out_specs=[
            pl.BlockSpec((block, width), lambda step: (step, 0)),
            pl.BlockSpec((1, heads, block), lambda step: (step, 0, 0)),
        ],
        out_shape=[
            jax.ShapeDtypeStruct((tokens, width), bf16),
            jax.ShapeDtypeStruct((blocks, heads, block), f32),
        ],
        scratch_shapes=[
            pltpu.VMEM((blocks, width, block), bf16),
            pltpu.VMEM((blocks, heads * block, width), bf16),
            pltpu.VMEM((blocks, heads * block, block), f32),
        ],
        compiler_params=pltpu.CompilerParams(
            dimension_semantics=("arbitrary",), vmem_limit_bytes=40 * 1024 * 1024
        ),
        cost_estimate=pl.CostEstimate(
            flops=3 * tokens * tokens * 256 * heads,
            bytes_accessed=10 * tokens * width,
            transcendentals=tokens * tokens * heads // 2,
        ),
        name="attend_forward",
    )(low, mid, slopes, starts, qkv)


def attend_backward(qkv, grads, outputs, logs, plan, slopes, heads, block, first_head, earlier):
    tokens, triple = qkv.shape
    all_width = triple // 3
    all_heads = logs.shape[1]
    width = all_width // all_heads * heads
    blocks = tokens // block
    starts, low, mid, full, high = plan
    merge = earlier is not None
    result_width = triple if merge else 3 * width
    operands = [full, high, slopes, starts, logs, qkv, grads, outputs]
    specs = [scalar_spec() for _ in range(3)] + [whole_spec(entry.shape) for entry in operands[3:]]
    if merge:
        operands.append(earlier)
        specs.append(whole_spec(earlier.shape))
    return pl.pallas_call(
        functools.partial(backward_kernel, heads, block, first_head, merge),
        grid=(blocks,),
        in_specs=specs,
        out_specs=pl.BlockSpec((tokens, result_width), lambda step: (0, 0)),
        out_shape=jax.ShapeDtypeStruct((tokens, result_width), bf16),
        scratch_shapes=[
            pltpu.VMEM((blocks, width, block), bf16),
            pltpu.VMEM((blocks, width, block), bf16),
            pltpu.VMEM((blocks, width, block), bf16),
            pltpu.VMEM((blocks, heads * block, width), bf16),
            pltpu.VMEM((blocks, heads * block, width), bf16),
            pltpu.VMEM((heads * block, width), bf16),
            pltpu.VMEM((heads * block, width), bf16),
            pltpu.VMEM((blocks, heads, block), f32),
            pltpu.VMEM((blocks, width, block), f32),
        ],
        compiler_params=pltpu.CompilerParams(
            dimension_semantics=("arbitrary",), vmem_limit_bytes=40 * 1024 * 1024
        ),
        cost_estimate=pl.CostEstimate(
            flops=8 * tokens * tokens * 256 * heads,
            bytes_accessed=20 * tokens * width,
            transcendentals=tokens * tokens * heads // 2,
        ),
        name="attend_backward",
    )(*operands)


def together(*values):
    return lax.optimization_barrier(values)


def ordered(own, other, bit, axis=0):
    first = jnp.where(bit == 0, own, other)
    second = jnp.where(bit == 0, other, own)
    return jnp.stack([first, second], axis=axis)


class Moves:
    def __init__(self):
        self.shards = lax.axis_size("shard")
        self.reps = lax.axis_size("rep")
        self.half = self.shards // 2
        self.chips = self.reps // 2
        self.shard = lax.axis_index("shard")
        self.rep = lax.axis_index("rep")
        self.core = self.rep % 2
        self.chip = self.rep // 2
        self.side = self.shard // self.half
        self.member = self.shard % self.half + self.core * self.half

    def core_swap(self, part):
        return lax.ppermute(part, "rep", [(r, r ^ 1) for r in range(self.reps)])

    def chip_swap(self, part, bits):
        return lax.ppermute(part, "rep", [(r, r ^ (2 * bits)) for r in range(self.reps)])

    def shard_swap(self, part, bits):
        return lax.ppermute(part, "shard", [(s, s ^ bits) for s in range(self.shards)])

    def shard_bit(self, bits):
        return (self.shard // bits) % 2

    def low_bits(self):
        bits, result = 1, []
        while bits < self.half:
            result.append(bits)
            bits *= 2
        return result

    def home_swap(self, part):
        pairs = []
        for rep in range(self.reps):
            for shard in range(self.shards):
                side, core = shard // self.half, rep % 2
                to_rep, to_shard = rep, shard
                if side != core:
                    to_rep = rep ^ 1
                    to_shard = (shard + self.half) % self.shards
                pairs.append((rep * self.shards + shard, to_rep * self.shards + to_shard))
        return lax.ppermute(part, ("rep", "shard"), pairs)

    def members_gather(self, part):
        stack = part[None]
        for bits in self.low_bits():
            own = stack
            stack = ordered(own, self.shard_swap(own, bits), self.shard_bit(bits))
            stack = stack.reshape((-1,) + part.shape)
        stack = ordered(stack, self.core_swap(stack), self.core)
        return stack.reshape((-1,) + part.shape)

    def exchange_bit(self, stack, bit, swap):
        sources, targets = stack.shape[:2]
        stack = stack.reshape((sources, 2, targets // 2) + stack.shape[2:])
        own, other = pick(stack, bit, 1), swap(pick(stack, 1 - bit, 1))
        return ordered(own, other, bit, 1).reshape((2 * sources,) + own.shape[1:])

    def half_exchange(self, stack):
        stack = stack[None]
        for bits in reversed(self.low_bits()):
            swap = functools.partial(self.shard_swap, bits=bits)
            stack = self.exchange_bit(stack, self.shard_bit(bits), swap)
        return stack.reshape((self.half,) + stack.shape[2:])

    def members_exchange(self, stack):
        stack = self.exchange_bit(stack[None], self.core, self.core_swap)
        for bits in reversed(self.low_bits()):
            swap = functools.partial(self.shard_swap, bits=bits)
            stack = self.exchange_bit(stack, self.shard_bit(bits), swap)
        return stack.reshape((self.shards,) + stack.shape[2:])

    def reduce_bit(self, stack, bit, swap):
        stack = stack.reshape((2, stack.shape[0] // 2) + stack.shape[1:])
        other = swap(pick(stack, 1 - bit).astype(bf16))
        return pick(stack, bit).astype(f32) + other.astype(f32)

    def chips_spread(self, part):
        if self.chips == 4:
            cut = part.shape[0] // 2
            by_x, by_y = self.chip_swap(part, 1), self.chip_swap(part, 2)
            far = jnp.concatenate(
                [self.chip_swap(by_x[:cut], 2), self.chip_swap(by_y[cut:], 1)], axis=0
            )
            return [(1, by_x), (2, by_y), (3, far)]
        held, bits = [part], 1
        while bits < self.chips:
            held = held + [self.chip_swap(piece, bits) for piece in held]
            bits *= 2
        return list(enumerate(held))[1:]

    def chips_gather(self, part, axis):
        shape = part.shape[:axis] + (self.chips,) + part.shape[axis:]
        stack = place(jnp.zeros(shape, part.dtype), part, self.chip, axis)
        for number, piece in self.chips_spread(part):
            stack = place(stack, piece, self.chip ^ number, axis)
        return stack

    def reduce_open(self, stack, axis):
        if self.chips == 4:
            shape = stack.shape[:axis] + (2, 2) + stack.shape[axis + 1 :]
            stack = stack.reshape(shape)
            bit_x, bit_y = self.chip % 2, self.chip // 2
            cut = shape[0] // 2
            first, second = stack[:cut], stack[cut:]
            got_first = self.chip_swap(pick(first, 1 - bit_x, axis + 1), 1)
            got_second = self.chip_swap(pick(second, 1 - bit_y, axis), 2)
            return (pick(first, bit_x, axis + 1), pick(second, bit_y, axis), got_first, got_second)
        count = self.chips
        stack = stack.astype(f32)
        while count > 1:
            count //= 2
            shape = stack.shape[:axis] + (2, count) + stack.shape[axis + 1 :]
            stack = stack.reshape(shape)
            bit = (self.chip // count) % 2
            got = self.chip_swap(pick(stack, 1 - bit, axis).astype(bf16), count)
            stack = pick(stack, bit, axis) + got.astype(f32)
        return (pick(stack, 0, axis).astype(bf16),)

    def reduce_add(self, state):
        if self.chips != 4:
            return state
        first, second, got_first, got_second = state
        first = (first.astype(f32) + got_first.astype(f32)).astype(bf16)
        second = (second.astype(f32) + got_second.astype(f32)).astype(bf16)
        return (first, second)

    def reduce_close(self, state, axis):
        if self.chips != 4:
            return state[0]
        first, second = state
        bit_x, bit_y = self.chip % 2, self.chip // 2
        got_first = self.chip_swap(pick(first, 1 - bit_y, axis), 2)
        got_second = self.chip_swap(pick(second, 1 - bit_x, axis), 1)
        first = pick(first, bit_y, axis).astype(f32) + got_first.astype(f32)
        second = pick(second, bit_x, axis).astype(f32) + got_second.astype(f32)
        return jnp.concatenate([first, second], axis=0).astype(bf16)

    def chips_reduce(self, stack, axis):
        return self.reduce_close(self.reduce_add(self.reduce_open(stack, axis)), axis)

    def core_pair(self, part):
        other = self.core_swap(part)
        first = jnp.where(self.core == 0, part, other)
        second = jnp.where(self.core == 0, other, part)
        return first, second

    def sum_reps(self, vector):
        bits = 1
        while bits < self.reps:
            vector = vector + lax.ppermute(vector, "rep", [(r, r ^ bits) for r in range(self.reps)])
            bits *= 2
        return vector

    def sum_shards(self, vector):
        bits = 1
        while bits < self.shards:
            vector = vector + self.shard_swap(vector, bits)
            bits *= 2
        return vector


def factor_stats(gradient, weight, rows_old, decay_rate):
    square = gradient * gradient
    rows_new = decay_rate * rows_old + (1.0 - decay_rate) * (jnp.mean(square, axis=1) + eps_second)
    col_squares = jnp.sum(square, axis=0)
    col_scaled = jnp.sum(square / rows_new[:, None], axis=0)
    scalars = jnp.stack([jnp.sum(rows_new), jnp.sum(weight * weight)])
    return rows_new, [col_squares, col_scaled, scalars]


def factor_apply(gradient, weight, rows_new, sums, cols_old, height, decay_rate):
    col_squares, col_scaled, scalars = sums
    breadth = gradient.shape[1]
    cols_new = decay_rate * cols_old + (1.0 - decay_rate) * (col_squares / height + eps_second)
    row_mean = scalars[0] / height
    rms_update = jnp.sqrt(row_mean / (height * breadth) * jnp.sum(col_scaled / cols_new))
    rms_weight = jnp.sqrt(scalars[1] / (height * breadth))
    factor = rate_step * rms_weight * jnp.sqrt(row_mean) / jnp.maximum(1.0, rms_update / clip_level)
    new_weight = weight - gradient * (factor * lax.rsqrt(rows_new))[:, None] * lax.rsqrt(cols_new)[None, :]
    return new_weight, cols_new, rms_update


def summed(moves, entries):
    sizes = [entry.shape[0] for entry in entries]
    total = moves.sum_shards(jnp.concatenate(entries))
    result, offset = [], 0
    for size in sizes:
        result.append(total[offset : offset + size])
        offset += size
    return result


def on_device(
    tokens,
    cotangent,
    seq_lengths,
    qkv_weight,
    out_weight,
    up_weight,
    down_weight,
    vectors,
    row_state,
    down_rows,
    col_state,
    vector_state,
):
    moves = Moves()
    shards, half, chips, core = moves.shards, moves.half, moves.chips, moves.core
    row_count, width = tokens.shape
    hidden_width = up_weight.shape[1]
    group_rows = row_count * shards
    heads = HEADS // shards
    head_width = width // HEADS
    span = heads * head_width
    member = moves.member
    decay_rate = 1.0 - STEP ** (-0.8)
    head_number = (member * heads + jnp.arange(heads, dtype=jnp.int32)).astype(f32)
    slopes = jnp.exp2(-8.0 * (head_number + 1.0) / HEADS)

    gain_one = vectors[0:width]
    shift_one = vectors[width : 2 * width]
    bias_query = vectors[2 * width : 3 * width]
    bias_value = vectors[3 * width : 4 * width]
    bias_out = vectors[4 * width : 5 * width]
    gain_two = vectors[5 * width : 6 * width]
    shift_two = vectors[6 * width : 7 * width]
    bias_up = vectors[7 * width : 7 * width + hidden_width]
    bias_down = vectors[7 * width + hidden_width :]

    home_tokens = moves.home_swap(tokens)
    other_lengths = moves.core_swap(seq_lengths)
    lengths = jnp.where(moves.side == core, seq_lengths, other_lengths)[0]
    plan = block_plan(lengths, group_rows, BLOCK)
    rows_z = width // shards
    rows_piece = rows_z // chips
    first_row = moves.chip * rows_piece
    my_rows = lax.dynamic_slice_in_dim(qkv_weight, first_row, rows_piece, 0).astype(bf16)
    my_blocks = my_rows.reshape(rows_piece, 3, 2, half, span)
    my_blocks = pick(my_blocks, core, 2).transpose(2, 0, 1, 3).reshape(half, rows_piece, 3 * span)
    near_part = moves.half_exchange(my_blocks)
    qkv_part = ordered(near_part, moves.shard_swap(near_part, half), moves.side)
    qkv_part = qkv_part.reshape(shards, rows_piece, 3 * span)
    qkv_cols = moves.chips_gather(qkv_part, 1).reshape(width, 3 * span)

    half_cols = hidden_width // (2 * shards)
    up_wide = shards * half_cols
    out_wide = width // 2
    down_piece = half_cols // chips
    down_fold = down_piece // rows_piece
    all_wide = up_wide + out_wide + down_fold * width
    up_own = pick(up_weight.reshape(rows_z, shards, 2, half_cols), core, 2).astype(bf16)
    up_own = up_own.reshape(chips, rows_piece, up_wide)
    out_own = lax.dynamic_slice_in_dim(out_weight, core * out_wide, out_wide, 1).astype(bf16)
    out_own = out_own.reshape(chips, rows_piece, out_wide)
    down_own = lax.dynamic_slice_in_dim(down_weight, core * half_cols, half_cols, 0).astype(bf16)
    down_own = down_own.reshape(chips, down_fold, rows_piece, width)
    my_down = pick(down_own, moves.chip)
    weight_piece = jnp.concatenate(
        [pick(up_own, moves.chip), pick(out_own, moves.chip)]
        + [my_down[number] for number in range(down_fold)],
        axis=1,
    )
    held = [(0, weight_piece)]
    bits = 1
    while bits < half:
        held = held + [(bits + number, moves.shard_swap(piece, bits)) for number, piece in held]
        bits *= 2
    weight_piece, home_tokens = together(weight_piece, home_tokens)
    far_piece = moves.shard_swap(weight_piece, half)
    far_piece, cotangent = together(far_piece, cotangent)
    held, bits = held + [(half, far_piece)], 1
    while bits < half:
        far = [(bits + number, moves.shard_swap(piece, bits)) for number, piece in held if number >= half]
        held, bits = held + far, bits * 2
    inputs = home_tokens.astype(f32)
    normed_one, inv_std_one = norm_parts(inputs)
    act_one = (normed_one * gain_one + shift_one).astype(bf16)
    act_all = moves.members_gather(act_one).reshape(group_rows, width)

    up_all = place(jnp.zeros((shards, chips, rows_piece, up_wide), bf16), up_own, moves.shard)
    out_all = place(jnp.zeros((shards, chips, rows_piece, out_wide), bf16), out_own, moves.shard)
    down_all = place(
        jnp.zeros((shards, chips, down_fold, rows_piece, width), bf16), down_own, moves.shard
    )
    for number, piece in held[1:]:
        plane = moves.shard ^ number
        for far, spread in [(0, piece)] + moves.chips_spread(piece):
            chip = moves.chip ^ far
            up_all = lax.dynamic_update_slice(up_all, spread[None, None, :, :up_wide], (plane, chip, 0, 0))
            out_all = lax.dynamic_update_slice(
                out_all, spread[None, None, :, up_wide : up_wide + out_wide], (plane, chip, 0, 0)
            )
            folds = [
                spread[:, up_wide + out_wide + k * width : up_wide + out_wide + (k + 1) * width]
                for k in range(down_fold)
            ]
            down_all = lax.dynamic_update_slice(
                down_all, jnp.stack(folds)[None, None], (plane, chip, 0, 0, 0)
            )
    up_half = up_all.reshape(width, up_wide)
    down_half = down_all.reshape(up_wide, width)
    out_first, out_second = moves.core_pair(out_all.reshape(width, out_wide))
    out_low = jnp.concatenate([out_first, out_second], axis=1)

    bias_q_part = lax.dynamic_slice_in_dim(bias_query, member * span, span)
    bias_v_part = lax.dynamic_slice_in_dim(bias_value, member * span, span)
    qkv_bias = jnp.concatenate([bias_q_part, jnp.zeros_like(bias_q_part), bias_v_part])
    qkv_rows = (dot(act_all, qkv_cols) + qkv_bias).astype(bf16)
    attended_cols, logs = attend_forward(qkv_rows, plan, slopes, heads, BLOCK)
    attended_parts = moves.members_exchange(attended_cols.reshape(shards, row_count, span))
    attended = jnp.concatenate([attended_parts[k] for k in range(shards)], axis=1)
    residual = inputs + dot(attended, out_low) + bias_out
    normed_two, inv_std_two = norm_parts(residual)
    act_two = (normed_two * gain_two + shift_two).astype(bf16)

    home_cot = moves.home_swap(cotangent)
    cot_pair = jnp.concatenate([home_cot, moves.core_swap(home_cot)], axis=0)
    act_two_pair = jnp.concatenate([act_two, moves.core_swap(act_two)], axis=0)
    bias_up_half = pick(bias_up.reshape(shards, 2, half_cols), core, 1).reshape(up_wide)
    up_pair = dot(act_two_pair, up_half) + bias_up_half
    hidden_pair = gelu_value(up_pair).astype(bf16)
    down_terms = dot_rows(hidden_pair, cot_pair).astype(bf16)
    down_terms = down_terms.reshape(shards, chips, down_piece, width)
    grad_y = home_cot.astype(f32)
    grad_bias_down = jnp.sum(grad_y, axis=0)
    grad_up_pair = (dot_right(cot_pair, down_half) * gelu_slope(up_pair)).astype(bf16)
    grad_bias_up = jnp.sum(grad_up_pair, axis=0, dtype=f32)
    back_other = moves.core_swap(dot_right(grad_up_pair[row_count:], up_half).astype(bf16))
    grad_act_two = dot_right(grad_up_pair[:row_count], up_half) + back_other.astype(f32)
    grad_gain_two = jnp.sum(grad_act_two * normed_two, axis=0)
    grad_shift_two = jnp.sum(grad_act_two, axis=0)
    grad_residual = grad_y + norm_back(grad_act_two, normed_two, inv_std_two, gain_two)
    grad_attn = grad_residual.astype(bf16)
    grad_bias_out = jnp.sum(grad_attn, axis=0, dtype=f32)
    to_members = jnp.stack(
        [
            dot_right(grad_attn, out_low[k * span : (k + 1) * span]).astype(bf16)
            for k in range(shards)
        ]
    )
    grad_heads = moves.members_exchange(to_members).reshape(group_rows, span)
    down_other = moves.core_swap(dot(hidden_pair[row_count:], down_half).astype(bf16))
    block_out = (
        residual + dot(hidden_pair[:row_count], down_half) + down_other.astype(f32) + bias_down
    ).astype(bf16)

    attended_pair = jnp.concatenate([attended, moves.core_swap(attended)], axis=0)
    attn_halves = [grad_attn[:, :out_wide], grad_attn[:, out_wide:]]
    attn_own = jnp.where(core == 0, attn_halves[0], attn_halves[1])
    attn_other = jnp.where(core == 0, attn_halves[1], attn_halves[0])
    attn_pair = jnp.concatenate([attn_own, moves.core_swap(attn_other)], axis=0)
    up_out_terms = jnp.concatenate(
        [
            dot_rows(act_two_pair, grad_up_pair).astype(bf16),
            dot_rows(attended_pair, attn_pair).astype(bf16),
        ],
        axis=1,
    ).reshape(shards, chips, rows_piece, up_wide + out_wide)

    def shards_sum(piece):
        rows = piece.shape[1]
        return lax.psum_scatter(
            piece.reshape(shards * rows, piece.shape[2]), "shard", scatter_dimension=0, tiled=True
        )

    down_state = moves.reduce_add(moves.reduce_open(down_terms, 1))
    grad_heads, up_out_terms, down_state = together(grad_heads, up_out_terms, down_state)
    block_out = moves.home_swap(block_out)
    up_out_state = moves.reduce_add(moves.reduce_open(up_out_terms, 1))
    down_piece_sum = moves.reduce_close(down_state, 1)
    attend_args = (plan, slopes)
    parts = 2 if heads % 4 == 0 else 1
    part_heads = heads // parts
    grad_qkv = attend_backward(
        qkv_rows, grad_heads, attended_cols, logs, *attend_args, part_heads, BLOCK, 0, None
    )
    grad_qkv, up_out_state, down_piece_sum, block_out = together(
        grad_qkv, up_out_state, down_piece_sum, block_out
    )
    if parts == 2:
        grad_qkv = attend_backward(
            qkv_rows, grad_heads, attended_cols, logs, *attend_args, part_heads, BLOCK, part_heads, grad_qkv
        )
    down_owned = shards_sum(down_piece_sum)
    up_out_piece = moves.reduce_close(up_out_state, 1)
    grad_qkv_late, up_out_piece = together(grad_qkv, up_out_piece)
    up_out_owned = shards_sum(up_out_piece)

    grad_bias_q_part = jnp.sum(grad_qkv[:, :span], axis=0, dtype=f32)
    grad_bias_v_part = jnp.sum(grad_qkv[:, 2 * span :], axis=0, dtype=f32)

    grad_halves = grad_qkv.reshape(2, half * row_count, 3 * span)
    sent = dot_right(pick(grad_halves, 1 - core), qkv_cols).astype(bf16)
    back = dot_right(pick(grad_halves, core), qkv_cols) + moves.core_swap(sent).astype(f32)
    down_owned, back_sum = together(down_owned, back)
    down_first, down_second = moves.core_pair(
        moves.chips_gather(down_owned, 0).reshape(half_cols, width)
    )
    qkv_terms = dot_rows(act_all, grad_qkv_late).astype(bf16)
    qkv_terms = qkv_terms.reshape(shards, chips, rows_piece, 3 * span)
    qkv_state = moves.reduce_add(moves.reduce_open(qkv_terms, 1))
    qkv_state, back_sum = together(qkv_state, back_sum)
    qkv_piece = moves.reduce_close(qkv_state, 1)
    back = back_sum.reshape(half, row_count, width)
    for bits in reversed(moves.low_bits()):
        back = moves.reduce_bit(
            back, moves.shard_bit(bits), functools.partial(moves.shard_swap, bits=bits)
        )
    back, down_first, down_second, up_out_owned = together(
        back, down_first, down_second, up_out_owned
    )
    up_out_first, up_out_second = moves.core_pair(
        moves.chips_gather(up_out_owned, 0).reshape(rows_z, up_wide + out_wide)
    )
    out_grad = jnp.concatenate(
        [up_out_first[:, up_wide:], up_out_second[:, up_wide:]], axis=1
    ).astype(f32)
    up_columns = []
    for number in range(shards):
        part = slice(number * half_cols, (number + 1) * half_cols)
        up_columns += [up_out_first[:, part], up_out_second[:, part]]
    up_grad = jnp.concatenate(up_columns, axis=1).astype(f32)

    down_grad = jnp.concatenate([down_first, down_second], axis=0).astype(f32)
    grad_act_one = back.reshape(row_count, width)
    grad_gain_one = jnp.sum(grad_act_one * normed_one, axis=0)
    grad_shift_one = jnp.sum(grad_act_one, axis=0)
    grad_inputs = grad_residual + norm_back(grad_act_one, normed_one, inv_std_one, gain_one)
    tokens_grad = moves.home_swap(grad_inputs.astype(bf16))
    qkv_piece = moves.reduce_bit(
        qkv_piece, moves.side, functools.partial(moves.shard_swap, bits=half)
    )
    qkv_piece = moves.half_exchange(qkv_piece.astype(bf16))
    qkv_owned = moves.chips_gather(qkv_piece, 1)
    qkv_first, qkv_second = moves.core_pair(qkv_owned.reshape(half, rows_z, 3 * span))
    qkv_columns = []
    for kind in range(3):
        for source in (qkv_first, qkv_second):
            for number in range(half):
                qkv_columns.append(source[number][:, kind * span : (kind + 1) * span])
    qkv_grad = jnp.concatenate(qkv_columns, axis=1).astype(f32)

    stats = [
        factor_stats(qkv_grad, qkv_weight, row_state[0], decay_rate),
        factor_stats(out_grad, out_weight, row_state[1], decay_rate),
        factor_stats(up_grad, up_weight, row_state[2], decay_rate),
        factor_stats(down_grad, down_weight, down_rows, decay_rate),
    ]
    zero_heads = jnp.zeros((width,), f32)
    zero_up = jnp.zeros((shards, 2, half_cols), f32)
    vector_part = moves.sum_reps(
        jnp.concatenate(
            [
                grad_gain_one,
                grad_shift_one,
                lax.dynamic_update_slice_in_dim(zero_heads, grad_bias_q_part, member * span, 0),
                lax.dynamic_update_slice_in_dim(zero_heads, grad_bias_v_part, member * span, 0),
                grad_bias_out,
                grad_gain_two,
                grad_shift_two,
                place(zero_up, grad_bias_up.reshape(shards, half_cols), core, 1).reshape(-1),
                grad_bias_down,
            ]
        )
    )
    down_sums = summed(moves, stats[3][1])
    vector_part, tokens_grad = together(vector_part, tokens_grad)
    late_sums = summed(moves, stats[0][1] + stats[1][1] + stats[2][1] + [vector_part])
    sums = [late_sums[0:3], late_sums[3:6], late_sums[6:9], down_sums]
    vector_grad = late_sums[9]
    gradients = [qkv_grad, out_grad, up_grad, down_grad]
    weights = [qkv_weight, out_weight, up_weight, down_weight]
    heights = [width, width, width, hidden_width]
    new_weights, new_cols, rms_values = [], [], []
    offset = 0
    for number in range(4):
        end_col = offset + gradients[number].shape[1]
        new_weight, cols_new, rms_update = factor_apply(
            gradients[number],
            weights[number],
            stats[number][0],
            sums[number],
            col_state[offset:end_col],
            heights[number],
            decay_rate,
        )
        new_weights.append(new_weight)
        new_cols.append(cols_new)
        rms_values.append(rms_update)
        offset = end_col

    vector_state_new = decay_rate * vector_state + (1.0 - decay_rate) * (
        vector_grad * vector_grad + eps_second
    )
    vector_step = vector_grad * lax.rsqrt(vector_state_new)
    vector_rms = jnp.sqrt(jnp.mean(vector_step * vector_step))
    vector_new = vectors - rate_step * jnp.sqrt(
        jnp.mean(vectors * vectors)
    ) * vector_step / jnp.maximum(1.0, vector_rms / clip_level)
    update_rms = jnp.stack(rms_values + [vector_rms])
    return (
        block_out,
        tokens_grad,
        qkv_grad,
        out_grad,
        up_grad,
        down_grad,
        vector_grad,
        new_weights[0],
        new_weights[1],
        new_weights[2],
        new_weights[3],
        vector_new,
        new_weights[0].astype(bf16),
        new_weights[1].astype(bf16),
        new_weights[2].astype(bf16),
        new_weights[3].astype(bf16),
        jnp.stack([stats[0][0], stats[1][0], stats[2][0]]),
        stats[3][0],
        jnp.concatenate(new_cols),
        vector_state_new,
        update_rms,
    )


def solution(mesh):
    in_specs = (
        P(("rep", "shard"), None),
        P(("rep", "shard"), None),
        P("rep", None),
        P("shard", None),
        P("shard", None),
        P("shard", None),
        P("shard", None),
        P(),
        P(None, "shard"),
        P("shard"),
        P(),
        P(),
    )
    out_specs = (
        P(("rep", "shard"), None),
        P(("rep", "shard"), None),
        P("shard", None),
        P("shard", None),
        P("shard", None),
        P("shard", None),
        P(),
        P("shard", None),
        P("shard", None),
        P("shard", None),
        P("shard", None),
        P(),
        P("shard", None),
        P("shard", None),
        P("shard", None),
        P("shard", None),
        P(None, "shard"),
        P("shard"),
        P(),
        P(),
        P(),
    )
    return jax.shard_map(
        on_device, mesh=mesh, in_specs=in_specs, out_specs=out_specs, check_vma=False
    )
```

```python
import functools

import jax
import jax.numpy as jnp
from jax import lax
from jax.experimental import pallas as pl
from jax.experimental.pallas import tpu as pltpu
from jax.sharding import PartitionSpec as P

HEADS = 16
STEP = 10
BLOCK = 256


eps_norm = 1e-05
eps_second = 1e-30
rate_step = 0.5
clip_level = 1.0
masked = -1e30
gelu_root = (2.0 / 3.141592653589793) ** 0.5
gelu_cubic = 0.044715

f32 = jnp.float32
bf16 = jnp.bfloat16


def norm_parts(values):
    average = jnp.mean(values, axis=-1, keepdims=True)
    centred = values - average
    inv_std = lax.rsqrt(jnp.mean(centred * centred, axis=-1, keepdims=True) + eps_norm)
    return (centred * inv_std, inv_std)


def norm_back(grad_out, normed, inv_std, gain_vec):
    grad_normed = grad_out * gain_vec
    inner_mean = jnp.mean(grad_normed * normed, axis=-1, keepdims=True)
    centred = grad_normed - jnp.mean(grad_normed, axis=-1, keepdims=True)
    return (centred - normed * inner_mean) * inv_std


def gelu_value(pre_act):
    curve = jnp.tanh(gelu_root * (pre_act + gelu_cubic * pre_act * pre_act * pre_act))
    return 0.5 * pre_act * (1.0 + curve)


def gelu_slope(pre_act):
    square = pre_act * pre_act
    curve = jnp.tanh(gelu_root * (pre_act + gelu_cubic * square * pre_act))
    inner = gelu_root * (1.0 + 3.0 * gelu_cubic * square)
    return 0.5 * (1.0 + curve) + 0.5 * pre_act * (1.0 - curve * curve) * inner


def dot(left_side, right_side):
    return jnp.dot(left_side, right_side, preferred_element_type=f32)


def dot_right(left_side, right_side):
    return lax.dot_general(
        left_side, right_side, (((1,), (1,)), ((), ())), preferred_element_type=f32
    )


def dot_rows(left_side, right_side):
    return lax.dot_general(
        left_side, right_side, (((0,), (0,)), ((), ())), preferred_element_type=f32
    )


def pick(stack, index, axis=0):
    return lax.dynamic_index_in_dim(stack, index, axis, keepdims=False)


def place(stack, part, index, axis=0):
    return lax.dynamic_update_index_in_dim(stack, part, index, axis)


def head_rows(number, head_width):
    return slice(number * head_width, (number + 1) * head_width)


def lane_masks(block_rows, width, heads):
    lanes = lax.broadcasted_iota(jnp.int32, (block_rows, width), 1)
    head_width = width // heads
    return [
        (lanes >= number * head_width) & (lanes < (number + 1) * head_width)
        for number in range(heads)
    ]


def allowed_pairs(key_block, query_block, start_row, block):
    key_pos = lax.broadcasted_iota(jnp.int32, (block, block), 0) + key_block * block
    query_pos = lax.broadcasted_iota(jnp.int32, (block, block), 1) + query_block * block
    return (key_pos <= query_pos) & (key_pos >= start_row)


def key_offsets(key_block, query_block, block):
    rows = lax.broadcasted_iota(jnp.int32, (block, 1), 0)
    return (rows + (key_block - query_block) * block).astype(f32)


def turned(values):
    return jnp.transpose(values.astype(f32))


def head_stack(values, lanes):
    zero = jnp.zeros(values.shape, values.dtype)
    return jnp.concatenate([jnp.where(lane, values, zero) for lane in lanes], axis=0)


def eights(values, combine):
    rows, columns = values.shape
    return combine(values.reshape(rows // 8, 8, columns), axis=0)


def forward_kernel(
    heads,
    block,
    low_ref,
    mid_ref,
    slope_ref,
    start_ref,
    qkv_ref,
    out_ref,
    log_ref,
    values_turned,
    key_stack,
    score_ref,
):
    tokens = qkv_ref.shape[0]
    width = qkv_ref.shape[1] // 3
    head_width = width // heads
    blocks = tokens // block
    query_block = pl.program_id(0)

    @pl.when(query_block == 0)
    def _():
        lanes = lane_masks(block, width, heads)
        for number in range(blocks):
            rows = slice(number * block, (number + 1) * block)
            values_turned[number] = turned(qkv_ref[rows, 2 * width :]).astype(bf16)
            key_stack[number] = head_stack(qkv_ref[rows, width : 2 * width], lanes)

    first_row = pl.multiple_of(query_block * block, block)
    queries = qkv_ref[pl.ds(first_row, block), :width].astype(f32) * head_width ** (-0.5)
    queries = turned(queries).astype(bf16)
    start_row = start_ref[query_block]

    def score_step(key_block, bests, with_mask):
        scores = dot(key_stack[key_block], queries)
        offsets = key_offsets(key_block, query_block, block)
        allowed = allowed_pairs(key_block, query_block, start_row, block) if with_mask else None
        result = []
        for number in range(heads):
            rows = head_rows(number, block)
            part = scores[rows] + slope_ref[number] * offsets
            if with_mask:
                part = jnp.where(allowed, part, masked)
            score_ref[key_block, rows, :] = part
            result.append(jnp.maximum(bests[number], eights(part, jnp.max)))
        return tuple(result)

    low, mid = low_ref[query_block], mid_ref[query_block]
    bests = tuple(jnp.full((8, block), masked, f32) for _ in range(heads))
    bests = lax.fori_loop(low, mid, functools.partial(score_step, with_mask=True), bests)
    bests = lax.fori_loop(mid, query_block, functools.partial(score_step, with_mask=False), bests)
    bests = score_step(query_block, bests, True)
    bests = [jnp.max(best, axis=0, keepdims=True) for best in bests]

    def value_step(key_block, state):
        result = []
        for number in range(heads):
            total, gathered = state[2 * number : 2 * number + 2]
            weights = jnp.exp(score_ref[key_block, head_rows(number, block), :] - bests[number])
            value_rows = values_turned[key_block, head_rows(number, head_width), :]
            result += [
                total + eights(weights, jnp.sum),
                gathered + dot(value_rows, weights.astype(bf16)),
            ]
        return tuple(result)

    state = ()
    for number in range(heads):
        state += (jnp.zeros((8, block), f32), jnp.zeros((head_width, block), f32))
    state = lax.fori_loop(low, query_block + 1, value_step, state)
    columns = []
    for number in range(heads):
        total = jnp.sum(state[2 * number], axis=0, keepdims=True)
        columns.append(state[2 * number + 1] / total)
        log_ref[0, number : number + 1, :] = bests[number] + jnp.log(total)
    out_ref[...] = jnp.transpose(jnp.concatenate(columns, axis=0)).astype(bf16)


def backward_kernel(heads, block, first_head, merge, *refs):
    full_ref, high_ref, slope_ref, start_ref, log_ref, qkv_ref, grad_ref, out_ref = refs[:8]
    earlier_ref = refs[8] if merge else None
    result_ref = refs[9 if merge else 8]
    (
        queries_turned,
        grads_turned,
        keys_turned,
        query_stack,
        grad_stack,
        key_stack,
        value_stack,
        delta_rows,
        query_grads,
    ) = refs[10 if merge else 9 :]
    tokens, all_width = grad_ref.shape
    head_width = all_width // log_ref.shape[1]
    width = heads * head_width
    scale = head_width ** (-0.5)
    blocks = tokens // block
    key_block = pl.program_id(0)
    lanes = lane_masks(block, width, heads)

    def columns(kind):
        start = kind * all_width + first_head * head_width
        return slice(start, start + width)

    def target(kind):
        start = (kind * all_width + first_head * head_width) if merge else kind * width
        return slice(start, start + width)

    @pl.when(key_block == 0)
    def _():
        for number in range(blocks):
            rows = slice(number * block, (number + 1) * block)
            queries = qkv_ref[rows, columns(0)]
            queries_turned[number] = turned(queries.astype(f32) * scale).astype(bf16)
            query_stack[number] = head_stack(queries, lanes)
            keys_turned[number] = turned(qkv_ref[rows, columns(1)]).astype(bf16)
            grads = grad_ref[rows, columns(0)]
            grad_stack[number] = head_stack(grads, lanes)
            grads = grads.astype(f32)
            grads_turned[number] = turned(grads).astype(bf16)
            product = turned(grads * out_ref[rows, columns(0)].astype(f32))
            for head in range(heads):
                delta_rows[number, head : head + 1, :] = jnp.sum(
                    product[head_rows(head, head_width)], axis=0, keepdims=True
                )
            query_grads[number] = jnp.zeros((width, block), f32)

    key_row = pl.multiple_of(key_block * block, block)
    key_stack[...] = head_stack(qkv_ref[pl.ds(key_row, block), columns(1)], lanes)
    value_stack[...] = head_stack(qkv_ref[pl.ds(key_row, block), columns(2)], lanes)

    def step(query_block, state, with_mask):
        key_total, value_total = state
        scores = dot(key_stack[...], queries_turned[query_block])
        grad_weights = dot(value_stack[...], grads_turned[query_block])
        offsets = key_offsets(key_block, query_block, block)
        if with_mask:
            allowed = allowed_pairs(key_block, query_block, start_ref[query_block], block)
        weight_list, grad_list = [], []
        for number in range(heads):
            rows = head_rows(number, block)
            head = first_head + number
            part = scores[rows] + slope_ref[head] * offsets
            part = part - log_ref[query_block, head : head + 1, :]
            if with_mask:
                part = jnp.where(allowed, part, masked)
            probabilities = jnp.exp(part)
            delta = delta_rows[query_block, number : number + 1, :]
            grad_scores = (probabilities * (grad_weights[rows] - delta)).astype(bf16)
            weight_list.append(probabilities.astype(bf16))
            grad_list.append(grad_scores)
            rows = head_rows(number, head_width)
            query_grads[query_block, rows, :] += dot(keys_turned[key_block, rows, :], grad_scores)
        weight_row = jnp.concatenate(weight_list, axis=1)
        grad_row = jnp.concatenate(grad_list, axis=1)
        return (
            key_total + dot(grad_row, query_stack[query_block]),
            value_total + dot(weight_row, grad_stack[query_block]),
        )

    state = (jnp.zeros((block, width), f32), jnp.zeros((block, width), f32))
    state = step(key_block, state, True)
    full, high = full_ref[key_block], high_ref[key_block]
    state = lax.fori_loop(key_block + 1, full, functools.partial(step, with_mask=False), state)
    state = lax.fori_loop(full, high, functools.partial(step, with_mask=True), state)
    result_ref[pl.ds(key_row, block), target(1)] = (state[0] * scale).astype(bf16)
    result_ref[pl.ds(key_row, block), target(2)] = state[1].astype(bf16)
    if merge:
        other = first_head * head_width
        for kind in range(3):
            result_ref[pl.ds(key_row, block), kind * all_width : kind * all_width + other] = earlier_ref[
                pl.ds(key_row, block), kind * other : (kind + 1) * other
            ]

    @pl.when(key_block == blocks - 1)
    def _():
        for number in range(blocks):
            rows = slice(number * block, (number + 1) * block)
            result_ref[rows, target(0)] = jnp.transpose(query_grads[number] * scale).astype(bf16)


def block_plan(lengths, tokens, block):
    ends = jnp.cumsum(lengths)
    positions = jnp.arange(tokens, dtype=jnp.int32)
    passed = positions[:, None] >= ends[None, :]
    starts = jnp.max(jnp.where(passed, ends[None, :], 0), axis=1).astype(jnp.int32)
    finish = jnp.min(jnp.where(passed, tokens, ends[None, :]), axis=1).astype(jnp.int32)
    blocks = tokens // block
    number = jnp.arange(blocks, dtype=jnp.int32)
    first_start = starts[::block]
    last_start = starts[block - 1 :: block]
    low = first_start // block
    mid = jnp.clip((last_start + block - 1) // block, low, number)
    high = (finish[block - 1 :: block] - 1) // block + 1
    full = jnp.clip(finish[::block] // block, number + 1, high)
    return (starts.reshape(blocks, 1, block), low, mid, full, high)


def scalar_spec():
    return pl.BlockSpec(memory_space=pltpu.SMEM)


def whole_spec(shape):
    return pl.BlockSpec(shape, lambda step: (0,) * len(shape), pipeline_mode=pl.Buffered(1))


def attend_forward(qkv, plan, slopes, heads, block):
    tokens, triple = qkv.shape
    width = triple // 3
    blocks = tokens // block
    starts, low, mid, full, high = plan
    return pl.pallas_call(
        functools.partial(forward_kernel, heads, block),
        grid=(blocks,),
        in_specs=[
            scalar_spec(),
            scalar_spec(),
            scalar_spec(),
            whole_spec((blocks, 1, block)),
            whole_spec((tokens, triple)),
        ],
        out_specs=[
            pl.BlockSpec((block, width), lambda step: (step, 0)),
            pl.BlockSpec((1, heads, block), lambda step: (step, 0, 0)),
        ],
        out_shape=[
            jax.ShapeDtypeStruct((tokens, width), bf16),
            jax.ShapeDtypeStruct((blocks, heads, block), f32),
        ],
        scratch_shapes=[
            pltpu.VMEM((blocks, width, block), bf16),
            pltpu.VMEM((blocks, heads * block, width), bf16),
            pltpu.VMEM((blocks, heads * block, block), f32),
        ],
        compiler_params=pltpu.CompilerParams(
            dimension_semantics=("arbitrary",), vmem_limit_bytes=40 * 1024 * 1024
        ),
        cost_estimate=pl.CostEstimate(
            flops=3 * tokens * tokens * 256 * heads,
            bytes_accessed=10 * tokens * width,
            transcendentals=tokens * tokens * heads // 2,
        ),
        name="attend_forward",
    )(low, mid, slopes, starts, qkv)


def attend_backward(qkv, grads, outputs, logs, plan, slopes, heads, block, first_head, earlier):
    tokens, triple = qkv.shape
    all_width = triple // 3
    all_heads = logs.shape[1]
    width = all_width // all_heads * heads
    blocks = tokens // block
    starts, low, mid, full, high = plan
    merge = earlier is not None
    result_width = triple if merge else 3 * width
    operands = [full, high, slopes, starts, logs, qkv, grads, outputs]
    specs = [scalar_spec() for _ in range(3)] + [whole_spec(entry.shape) for entry in operands[3:]]
    if merge:
        operands.append(earlier)
        specs.append(whole_spec(earlier.shape))
    return pl.pallas_call(
        functools.partial(backward_kernel, heads, block, first_head, merge),
        grid=(blocks,),
        in_specs=specs,
        out_specs=pl.BlockSpec((tokens, result_width), lambda step: (0, 0)),
        out_shape=jax.ShapeDtypeStruct((tokens, result_width), bf16),
        scratch_shapes=[
            pltpu.VMEM((blocks, width, block), bf16),
            pltpu.VMEM((blocks, width, block), bf16),
            pltpu.VMEM((blocks, width, block), bf16),
            pltpu.VMEM((blocks, heads * block, width), bf16),
            pltpu.VMEM((blocks, heads * block, width), bf16),
            pltpu.VMEM((heads * block, width), bf16),
            pltpu.VMEM((heads * block, width), bf16),
            pltpu.VMEM((blocks, heads, block), f32),
            pltpu.VMEM((blocks, width, block), f32),
        ],
        compiler_params=pltpu.CompilerParams(
            dimension_semantics=("arbitrary",), vmem_limit_bytes=40 * 1024 * 1024
        ),
        cost_estimate=pl.CostEstimate(
            flops=8 * tokens * tokens * 256 * heads,
            bytes_accessed=20 * tokens * width,
            transcendentals=tokens * tokens * heads // 2,
        ),
        name="attend_backward",
    )(*operands)


def together(*values):
    return lax.optimization_barrier(tuple(values))


def ordered(own, other, bit, axis=0):
    first = jnp.where(bit == 0, own, other)
    second = jnp.where(bit == 0, other, own)
    return jnp.stack([first, second], axis=axis)


class Moves:
    def __init__(self):
        self.shards = lax.axis_size("shard")
        self.reps = lax.axis_size("rep")
        self.half = self.shards // 2
        self.chips = self.reps // 2
        self.shard = lax.axis_index("shard")
        self.rep = lax.axis_index("rep")
        self.core = self.rep % 2
        self.chip = self.rep // 2
        self.side = self.shard // self.half
        self.member = self.shard % self.half + self.core * self.half

    def core_swap(self, part):
        return lax.ppermute(part, "rep", [(r, r ^ 1) for r in range(self.reps)])

    def chip_swap(self, part, bits):
        return lax.ppermute(part, "rep", [(r, r ^ (2 * bits)) for r in range(self.reps)])

    def shard_swap(self, part, bits):
        return lax.ppermute(part, "shard", [(s, s ^ bits) for s in range(self.shards)])

    def shard_bit(self, bits):
        return (self.shard // bits) % 2

    def low_bits(self):
        bits, result = 1, []
        while bits < self.half:
            result.append(bits)
            bits *= 2
        return result

    def home_swap(self, part):
        pairs = []
        for rep in range(self.reps):
            for shard in range(self.shards):
                side, core = shard // self.half, rep % 2
                to_rep, to_shard = rep, shard
                if side != core:
                    to_rep = rep ^ 1
                    to_shard = (shard + self.half) % self.shards
                pairs.append((rep * self.shards + shard, to_rep * self.shards + to_shard))
        return lax.ppermute(part, ("rep", "shard"), pairs)

    def half_gather(self, part):
        stack = part[None]
        for bits in self.low_bits():
            own = stack
            stack = ordered(own, self.shard_swap(own, bits), self.shard_bit(bits))
            stack = stack.reshape((-1,) + part.shape)
        return stack

    def cores_gather(self, stack):
        stack = ordered(stack, self.core_swap(stack), self.core)
        return stack.reshape((-1,) + stack.shape[2:])

    def exchange_bit(self, stack, bit, swap):
        sources, targets = stack.shape[:2]
        stack = stack.reshape((sources, 2, targets // 2) + stack.shape[2:])
        own, other = pick(stack, bit, 1), swap(pick(stack, 1 - bit, 1))
        return ordered(own, other, bit, 1).reshape((2 * sources,) + own.shape[1:])

    def half_exchange(self, stack):
        stack = stack[None]
        for bits in reversed(self.low_bits()):
            swap = functools.partial(self.shard_swap, bits=bits)
            stack = self.exchange_bit(stack, self.shard_bit(bits), swap)
        return stack.reshape((self.half,) + stack.shape[2:])

    def cores_exchange(self, stack):
        return self.exchange_bit(stack[None], self.core, self.core_swap)

    def members_exchange(self, stack):
        for bits in reversed(self.low_bits()):
            swap = functools.partial(self.shard_swap, bits=bits)
            stack = self.exchange_bit(stack, self.shard_bit(bits), swap)
        return stack.reshape((self.shards,) + stack.shape[2:])

    def reduce_bit(self, stack, bit, swap):
        stack = stack.reshape((2, stack.shape[0] // 2) + stack.shape[1:])
        other = swap(pick(stack, 1 - bit).astype(bf16))
        return pick(stack, bit).astype(f32) + other.astype(f32)

    def spread_open(self, part):
        if self.chips == 4:
            return (self.chip_swap(part, 1), self.chip_swap(part, 2))
        held, bits = [part], 1
        while bits < self.chips:
            held = held + [self.chip_swap(piece, bits) for piece in held]
            bits *= 2
        return tuple(held[1:])

    def spread_close(self, state):
        if self.chips == 4:
            by_x, by_y = state
            cut = by_x.shape[0] // 2
            far = jnp.concatenate(
                [self.chip_swap(by_x[:cut], 2), self.chip_swap(by_y[cut:], 1)], axis=0
            )
            return (by_x, by_y, far)
        return state

    def chips_gather(self, part, axis, state=None):
        shape = part.shape[:axis] + (self.chips,) + part.shape[axis:]
        stack = place(jnp.zeros(shape, part.dtype), part, self.chip, axis)
        others = self.spread_close(self.spread_open(part) if state is None else state)
        for number, piece in enumerate(others):
            stack = place(stack, piece, self.chip ^ (number + 1), axis)
        return stack

    def reduce_open(self, stack, axis):
        if self.chips == 4:
            shape = stack.shape[:axis] + (2, 2) + stack.shape[axis + 1 :]
            stack = stack.reshape(shape)
            bit_x, bit_y = self.chip % 2, self.chip // 2
            cut = shape[0] // 2
            first, second = stack[:cut], stack[cut:]
            got_first = self.chip_swap(pick(first, 1 - bit_x, axis + 1), 1)
            got_second = self.chip_swap(pick(second, 1 - bit_y, axis), 2)
            return (pick(first, bit_x, axis + 1), pick(second, bit_y, axis), got_first, got_second)
        count = self.chips
        stack = stack.astype(f32)
        while count > 1:
            count //= 2
            shape = stack.shape[:axis] + (2, count) + stack.shape[axis + 1 :]
            stack = stack.reshape(shape)
            bit = (self.chip // count) % 2
            got = self.chip_swap(pick(stack, 1 - bit, axis).astype(bf16), count)
            stack = pick(stack, bit, axis) + got.astype(f32)
        return (pick(stack, 0, axis).astype(bf16),)

    def reduce_add(self, state):
        if self.chips != 4:
            return state
        first, second, got_first, got_second = state
        first = (first.astype(f32) + got_first.astype(f32)).astype(bf16)
        second = (second.astype(f32) + got_second.astype(f32)).astype(bf16)
        return (first, second)

    def reduce_close(self, state, axis):
        if self.chips != 4:
            return state[0]
        first, second = state
        bit_x, bit_y = self.chip % 2, self.chip // 2
        got_first = self.chip_swap(pick(first, 1 - bit_y, axis), 2)
        got_second = self.chip_swap(pick(second, 1 - bit_x, axis), 1)
        first = pick(first, bit_y, axis).astype(f32) + got_first.astype(f32)
        second = pick(second, bit_x, axis).astype(f32) + got_second.astype(f32)
        return jnp.concatenate([first, second], axis=0).astype(bf16)

    def chips_reduce(self, stack, axis):
        return self.reduce_close(self.reduce_add(self.reduce_open(stack, axis)), axis)

    def core_pair(self, part):
        other = self.core_swap(part)
        first = jnp.where(self.core == 0, part, other)
        second = jnp.where(self.core == 0, other, part)
        return first, second

    def sum_reps(self, vector):
        bits = 1
        while bits < self.reps:
            vector = vector + lax.ppermute(vector, "rep", [(r, r ^ bits) for r in range(self.reps)])
            bits *= 2
        return vector

    def sum_shards(self, vector):
        bits = 1
        while bits < self.shards:
            vector = vector + self.shard_swap(vector, bits)
            bits *= 2
        return vector


def factor_stats(gradient, weight, rows_old, decay_rate):
    square = gradient * gradient
    rows_new = decay_rate * rows_old + (1.0 - decay_rate) * (jnp.mean(square, axis=1) + eps_second)
    col_squares = jnp.sum(square, axis=0)
    col_scaled = jnp.sum(square / rows_new[:, None], axis=0)
    scalars = jnp.stack([jnp.sum(rows_new), jnp.sum(weight * weight)])
    return rows_new, [col_squares, col_scaled, scalars]


def factor_apply(gradient, weight, rows_new, sums, cols_old, height, decay_rate):
    col_squares, col_scaled, scalars = sums
    breadth = gradient.shape[1]
    cols_new = decay_rate * cols_old + (1.0 - decay_rate) * (col_squares / height + eps_second)
    row_mean = scalars[0] / height
    rms_update = jnp.sqrt(row_mean / (height * breadth) * jnp.sum(col_scaled / cols_new))
    rms_weight = jnp.sqrt(scalars[1] / (height * breadth))
    factor = rate_step * rms_weight * jnp.sqrt(row_mean) / jnp.maximum(1.0, rms_update / clip_level)
    new_weight = weight - gradient * (factor * lax.rsqrt(rows_new))[:, None] * lax.rsqrt(cols_new)[None, :]
    return new_weight, cols_new, rms_update


def summed(moves, entries):
    sizes = [entry.shape[0] for entry in entries]
    total = moves.sum_shards(jnp.concatenate(entries))
    result, offset = [], 0
    for size in sizes:
        result.append(total[offset : offset + size])
        offset += size
    return result


def on_device(
    tokens,
    cotangent,
    seq_lengths,
    qkv_weight,
    out_weight,
    up_weight,
    down_weight,
    vectors,
    row_state,
    down_rows,
    col_state,
    vector_state,
):
    moves = Moves()
    shards, half, chips, core = moves.shards, moves.half, moves.chips, moves.core
    row_count, width = tokens.shape
    hidden_width = up_weight.shape[1]
    group_rows = row_count * shards
    heads = HEADS // shards
    head_width = width // HEADS
    span = heads * head_width
    member = moves.member
    decay_rate = 1.0 - STEP ** (-0.8)
    head_number = (member * heads + jnp.arange(heads, dtype=jnp.int32)).astype(f32)
    slopes = jnp.exp2(-8.0 * (head_number + 1.0) / HEADS)

    gain_one = vectors[0:width]
    shift_one = vectors[width : 2 * width]
    bias_query = vectors[2 * width : 3 * width]
    bias_value = vectors[3 * width : 4 * width]
    bias_out = vectors[4 * width : 5 * width]
    gain_two = vectors[5 * width : 6 * width]
    shift_two = vectors[6 * width : 7 * width]
    bias_up = vectors[7 * width : 7 * width + hidden_width]
    bias_down = vectors[7 * width + hidden_width :]

    home_tokens = moves.home_swap(tokens)
    other_lengths = moves.core_swap(seq_lengths)
    lengths = jnp.where(moves.side == core, seq_lengths, other_lengths)[0]
    plan = block_plan(lengths, group_rows, BLOCK)
    rows_z = width // shards
    rows_piece = rows_z // chips
    first_row = moves.chip * rows_piece
    my_rows = lax.dynamic_slice_in_dim(qkv_weight, first_row, rows_piece, 0).astype(bf16)
    my_blocks = []
    for number in range(half):
        kinds = []
        for kind in range(3):
            first = kind * width + number * span
            second = first + half * span
            kinds.append(
                jnp.where(
                    core == 0, my_rows[:, first : first + span], my_rows[:, second : second + span]
                )
            )
        my_blocks.append(jnp.concatenate(kinds, axis=1))
    near_part = moves.half_exchange(jnp.stack(my_blocks))
    qkv_part = ordered(near_part, moves.shard_swap(near_part, half), moves.side)
    qkv_part = qkv_part.reshape(shards, rows_piece, 3 * span)
    qkv_state = moves.spread_open(qkv_part)
    *qkv_state, home_tokens = together(*qkv_state, home_tokens)
    qkv_cols = moves.chips_gather(qkv_part, 1, tuple(qkv_state)).reshape(width, 3 * span)

    half_cols = hidden_width // (2 * shards)
    up_wide = shards * half_cols
    out_wide = width // 2
    down_piece = half_cols // chips
    down_fold = down_piece // rows_piece
    all_wide = up_wide + out_wide + down_fold * width

    def core_half(values):
        parts = []
        for number in range(shards):
            start = 2 * number * half_cols
            first = values[..., start : start + half_cols]
            second = values[..., start + half_cols : start + 2 * half_cols]
            parts.append(jnp.where(core == 0, first, second))
        return jnp.concatenate(parts, axis=-1)

    up_own = core_half(up_weight).astype(bf16).reshape(chips, rows_piece, up_wide)
    out_own = jnp.where(core == 0, out_weight[:, :out_wide], out_weight[:, out_wide:]).astype(bf16)
    out_own = out_own.reshape(chips, rows_piece, out_wide)
    down_own = lax.dynamic_slice_in_dim(down_weight, core * half_cols, half_cols, 0).astype(bf16)
    down_own = down_own.reshape(chips, down_fold, rows_piece, width)
    my_down = pick(down_own, moves.chip)
    weight_piece = jnp.concatenate(
        [pick(up_own, moves.chip), pick(out_own, moves.chip)]
        + [my_down[number] for number in range(down_fold)],
        axis=1,
    )
    near_pieces, bits = [weight_piece], 1
    while bits < half:
        near_pieces = near_pieces + [moves.shard_swap(piece, bits) for piece in near_pieces]
        bits *= 2
    near_pieces = near_pieces[1:]
    weight_piece, home_tokens, near_pieces = together(weight_piece, home_tokens, near_pieces)
    far_piece = moves.shard_swap(weight_piece, half)
    inputs = home_tokens.astype(f32)
    normed_one, inv_std_one = norm_parts(inputs)
    act_one = (normed_one * gain_one + shift_one).astype(bf16)
    act_half = moves.half_gather(act_one)

    near_open = [moves.spread_open(piece) for piece in near_pieces]
    act_half, near_open, far_piece, qkv_cols, cotangent = together(
        act_half, near_open, far_piece, qkv_cols, cotangent
    )
    act_all = moves.cores_gather(act_half).reshape(group_rows, width)
    near_spread = [moves.spread_close(state) for state in near_open]

    bias_q_part = lax.dynamic_slice_in_dim(bias_query, member * span, span)
    bias_v_part = lax.dynamic_slice_in_dim(bias_value, member * span, span)
    qkv_bias = jnp.concatenate([bias_q_part, jnp.zeros_like(bias_q_part), bias_v_part])
    qkv_rows = (dot(act_all, qkv_cols) + qkv_bias).astype(bf16)
    qkv_rows, near_spread = together(qkv_rows, near_spread)
    far_open = moves.spread_open(far_piece)
    far_pieces, bits = [far_piece], 1
    while bits < half:
        far_pieces = far_pieces + [moves.shard_swap(piece, bits) for piece in far_pieces]
        bits *= 2
    far_pieces = far_pieces[1:]
    home_cot = moves.home_swap(cotangent)
    attended_cols, logs = attend_forward(qkv_rows, plan, slopes, heads, BLOCK)
    attended_parts = moves.cores_exchange(attended_cols.reshape(shards, row_count, span))
    attended_parts, far_open, far_pieces, home_cot = together(
        attended_parts, far_open, far_pieces, home_cot
    )
    attended_parts = moves.members_exchange(attended_parts)
    attended_parts, home_cot = together(attended_parts, home_cot)
    attended = jnp.concatenate([attended_parts[k] for k in range(shards)], axis=1)

    far_spread = [moves.spread_close(far_open)]
    far_spread += [moves.spread_close(moves.spread_open(piece)) for piece in far_pieces]
    arrived = [(piece,) + tuple(spread) for piece, spread in zip(near_pieces, near_spread)]
    arrived += [
        (piece,) + tuple(spread) for piece, spread in zip([far_piece] + far_pieces, far_spread)
    ]
    up_all = place(jnp.zeros((shards, chips, rows_piece, up_wide), bf16), up_own, moves.shard)
    out_all = place(jnp.zeros((shards, chips, rows_piece, out_wide), bf16), out_own, moves.shard)
    down_all = place(
        jnp.zeros((shards, chips, down_fold, rows_piece, width), bf16), down_own, moves.shard
    )
    for number, pieces in enumerate(arrived):
        plane = moves.shard ^ (number + 1)
        for far, spread in enumerate(pieces):
            chip = moves.chip ^ far
            up_all = lax.dynamic_update_slice(up_all, spread[None, None, :, :up_wide], (plane, chip, 0, 0))
            out_all = lax.dynamic_update_slice(
                out_all, spread[None, None, :, up_wide : up_wide + out_wide], (plane, chip, 0, 0)
            )
            folds = [
                spread[:, up_wide + out_wide + k * width : up_wide + out_wide + (k + 1) * width]
                for k in range(down_fold)
            ]
            down_all = lax.dynamic_update_slice(
                down_all, jnp.stack(folds)[None, None], (plane, chip, 0, 0, 0)
            )
    up_half = up_all.reshape(width, up_wide)
    down_half = down_all.reshape(up_wide, width)
    out_first, out_second = moves.core_pair(out_all.reshape(width, out_wide))
    out_low = jnp.concatenate([out_first, out_second], axis=1)
    residual = inputs + dot(attended, out_low) + bias_out
    normed_two, inv_std_two = norm_parts(residual)
    act_two = (normed_two * gain_two + shift_two).astype(bf16)

    cot_pair = jnp.concatenate([home_cot, moves.core_swap(home_cot)], axis=0)
    act_two_pair = jnp.concatenate([act_two, moves.core_swap(act_two)], axis=0)
    bias_up_half = core_half(bias_up)
    up_pair = dot(act_two_pair, up_half) + bias_up_half
    hidden_pair = gelu_value(up_pair).astype(bf16)
    slope_pair = gelu_slope(up_pair).astype(bf16)
    down_terms = dot_rows(hidden_pair, cot_pair).astype(bf16)
    down_terms = down_terms.reshape(shards, chips, down_piece, width)
    grad_y = home_cot.astype(f32)
    grad_bias_down = jnp.sum(grad_y, axis=0)
    grad_up_pair = (dot_right(cot_pair, down_half) * slope_pair.astype(f32)).astype(bf16)
    grad_bias_up = jnp.sum(grad_up_pair, axis=0, dtype=f32)
    back_other = moves.core_swap(dot_right(grad_up_pair[row_count:], up_half).astype(bf16))
    grad_act_two = dot_right(grad_up_pair[:row_count], up_half) + back_other.astype(f32)
    grad_gain_two = jnp.sum(grad_act_two * normed_two, axis=0)
    grad_shift_two = jnp.sum(grad_act_two, axis=0)
    grad_residual = grad_y + norm_back(grad_act_two, normed_two, inv_std_two, gain_two)
    up_terms = dot_rows(act_two_pair, grad_up_pair).astype(bf16)
    up_terms = up_terms.reshape(shards, chips, rows_piece, up_wide)
    down_state = moves.reduce_open(down_terms, 1)
    grad_residual, up_terms, down_state = together(grad_residual, up_terms, down_state)
    up_state = moves.reduce_open(up_terms, 1)
    down_mid = moves.reduce_close(moves.reduce_add(down_state), 1)
    grad_attn = grad_residual.astype(bf16)
    grad_bias_out = jnp.sum(grad_attn, axis=0, dtype=f32)
    to_members = jnp.stack(
        [
            dot_right(grad_attn, out_low[k * span : (k + 1) * span]).astype(bf16)
            for k in range(shards)
        ]
    )
    grad_heads = moves.members_exchange(moves.cores_exchange(to_members)).reshape(group_rows, span)
    down_other = moves.core_swap(dot(hidden_pair[row_count:], down_half).astype(bf16))
    block_out = (
        residual + dot(hidden_pair[:row_count], down_half) + down_other.astype(f32) + bias_down
    ).astype(bf16)

    attended_pair = jnp.concatenate([attended, moves.core_swap(attended)], axis=0)
    attn_halves = [grad_attn[:, :out_wide], grad_attn[:, out_wide:]]
    attn_own = jnp.where(core == 0, attn_halves[0], attn_halves[1])
    attn_other = jnp.where(core == 0, attn_halves[1], attn_halves[0])
    attn_pair = jnp.concatenate([attn_own, moves.core_swap(attn_other)], axis=0)
    out_terms = dot_rows(attended_pair, attn_pair).astype(bf16)
    out_state = moves.reduce_open(out_terms.reshape(shards, chips, rows_piece, out_wide), 1)

    def shards_sum(piece):
        rows = piece.shape[1]
        return lax.psum_scatter(
            piece.reshape(shards * rows, piece.shape[2]), "shard", scatter_dimension=0, tiled=True
        )

    block_out = moves.home_swap(block_out)
    grad_heads, down_mid, out_terms = together(grad_heads, down_mid, out_terms)
    attend_args = (plan, slopes)
    parts = 2 if heads % 4 == 0 else 1
    part_heads = heads // parts
    grad_qkv = attend_backward(
        qkv_rows, grad_heads, attended_cols, logs, *attend_args, part_heads, BLOCK, 0, None
    )
    grad_qkv, up_state, out_state, block_out = together(grad_qkv, up_state, out_state, block_out)
    up_sums, out_sums = moves.reduce_add(up_state), moves.reduce_add(out_state)
    grad_qkv, up_sums, out_sums = together(grad_qkv, up_sums, out_sums)
    up_out_state = [
        jnp.concatenate([up_part, out_part], axis=-1) for up_part, out_part in zip(up_sums, out_sums)
    ]
    if parts == 2:
        grad_qkv = attend_backward(
            qkv_rows, grad_heads, attended_cols, logs, *attend_args, part_heads, BLOCK, part_heads, grad_qkv
        )
    down_owned = shards_sum(down_mid)
    up_out_piece = moves.reduce_close(up_out_state, 1)
    grad_qkv, up_out_piece = together(grad_qkv, up_out_piece)
    up_out_owned = shards_sum(up_out_piece)

    grad_bias_q_part = jnp.sum(grad_qkv[:, :span], axis=0, dtype=f32)
    grad_bias_v_part = jnp.sum(grad_qkv[:, 2 * span :], axis=0, dtype=f32)

    grad_halves = grad_qkv.reshape(2, half * row_count, 3 * span)
    sent = dot_right(pick(grad_halves, 1 - core), qkv_cols).astype(bf16)
    back = dot_right(pick(grad_halves, core), qkv_cols) + moves.core_swap(sent).astype(f32)
    down_owned, back_sum = together(down_owned, back)
    down_first, down_second = moves.core_pair(
        moves.chips_gather(down_owned, 0).reshape(half_cols, width)
    )
    qkv_terms = dot_rows(act_all, grad_qkv).astype(bf16)
    qkv_terms = qkv_terms.reshape(shards, chips, rows_piece, 3 * span)
    qkv_state = moves.reduce_add(moves.reduce_open(qkv_terms, 1))
    qkv_state, back_sum = together(qkv_state, back_sum)
    qkv_piece = moves.reduce_close(qkv_state, 1)
    back = back_sum.reshape(half, row_count, width)
    for bits in reversed(moves.low_bits()):
        back = moves.reduce_bit(
            back, moves.shard_bit(bits), functools.partial(moves.shard_swap, bits=bits)
        )
    back, down_first, down_second, up_out_owned = together(
        back, down_first, down_second, up_out_owned
    )
    up_out_first, up_out_second = moves.core_pair(
        moves.chips_gather(up_out_owned, 0).reshape(rows_z, up_wide + out_wide)
    )
    out_grad = jnp.concatenate(
        [up_out_first[:, up_wide:], up_out_second[:, up_wide:]], axis=1
    ).astype(f32)
    up_columns = []
    for number in range(shards):
        part = slice(number * half_cols, (number + 1) * half_cols)
        up_columns += [up_out_first[:, part], up_out_second[:, part]]
    up_grad = jnp.concatenate(up_columns, axis=1).astype(f32)

    down_grad = jnp.concatenate([down_first, down_second], axis=0).astype(f32)
    grad_act_one = back.reshape(row_count, width)
    grad_gain_one = jnp.sum(grad_act_one * normed_one, axis=0)
    grad_shift_one = jnp.sum(grad_act_one, axis=0)
    grad_inputs = grad_residual + norm_back(grad_act_one, normed_one, inv_std_one, gain_one)
    tokens_grad = moves.home_swap(grad_inputs.astype(bf16))
    qkv_piece = moves.reduce_bit(
        qkv_piece, moves.side, functools.partial(moves.shard_swap, bits=half)
    )
    qkv_piece = moves.half_exchange(qkv_piece.astype(bf16))
    qkv_owned = moves.chips_gather(qkv_piece, 1)
    qkv_first, qkv_second = moves.core_pair(qkv_owned.reshape(half, rows_z, 3 * span))
    qkv_columns = []
    for kind in range(3):
        for source in (qkv_first, qkv_second):
            for number in range(half):
                qkv_columns.append(source[number][:, kind * span : (kind + 1) * span])
    qkv_grad = jnp.concatenate(qkv_columns, axis=1).astype(f32)

    stats = [
        factor_stats(qkv_grad, qkv_weight, row_state[0], decay_rate),
        factor_stats(out_grad, out_weight, row_state[1], decay_rate),
        factor_stats(up_grad, up_weight, row_state[2], decay_rate),
        factor_stats(down_grad, down_weight, down_rows, decay_rate),
    ]
    def spread_heads(part):
        return [jnp.where(member == number, part, 0.0) for number in range(shards)]

    bias_up_parts = []
    for number in range(shards):
        part = grad_bias_up[number * half_cols : (number + 1) * half_cols]
        bias_up_parts += [jnp.where(core == 0, part, 0.0), jnp.where(core == 1, part, 0.0)]
    vector_part = moves.sum_reps(
        jnp.concatenate(
            [grad_gain_one, grad_shift_one]
            + spread_heads(grad_bias_q_part)
            + spread_heads(grad_bias_v_part)
            + [grad_bias_out, grad_gain_two, grad_shift_two]
            + bias_up_parts
            + [grad_bias_down]
        )
    )
    early_sums = summed(moves, stats[1][1] + stats[2][1] + stats[3][1])
    vector_part, tokens_grad = together(vector_part, tokens_grad)
    late_sums = summed(moves, stats[0][1] + [vector_part])
    sums = [late_sums[0:3], early_sums[0:3], early_sums[3:6], early_sums[6:9]]
    vector_grad = late_sums[3]
    gradients = [qkv_grad, out_grad, up_grad, down_grad]
    weights = [qkv_weight, out_weight, up_weight, down_weight]
    heights = [width, width, width, hidden_width]
    new_weights, new_cols, rms_values = [], [], []
    offset = 0
    for number in range(4):
        end_col = offset + gradients[number].shape[1]
        new_weight, cols_new, rms_update = factor_apply(
            gradients[number],
            weights[number],
            stats[number][0],
            sums[number],
            col_state[offset:end_col],
            heights[number],
            decay_rate,
        )
        new_weights.append(new_weight)
        new_cols.append(cols_new)
        rms_values.append(rms_update)
        offset = end_col

    vector_state_new = decay_rate * vector_state + (1.0 - decay_rate) * (
        vector_grad * vector_grad + eps_second
    )
    vector_step = vector_grad * lax.rsqrt(vector_state_new)
    vector_rms = jnp.sqrt(jnp.mean(vector_step * vector_step))
    vector_new = vectors - rate_step * jnp.sqrt(
        jnp.mean(vectors * vectors)
    ) * vector_step / jnp.maximum(1.0, vector_rms / clip_level)
    update_rms = jnp.stack(rms_values + [vector_rms])
    return (
        block_out,
        tokens_grad,
        qkv_grad,
        out_grad,
        up_grad,
        down_grad,
        vector_grad,
        new_weights[0],
        new_weights[1],
        new_weights[2],
        new_weights[3],
        vector_new,
        new_weights[0].astype(bf16),
        new_weights[1].astype(bf16),
        new_weights[2].astype(bf16),
        new_weights[3].astype(bf16),
        jnp.stack([stats[0][0], stats[1][0], stats[2][0]]),
        stats[3][0],
        jnp.concatenate(new_cols),
        vector_state_new,
        update_rms,
    )


def solution(mesh):
    in_specs = (
        P(("rep", "shard"), None),
        P(("rep", "shard"), None),
        P("rep", None),
        P("shard", None),
        P("shard", None),
        P("shard", None),
        P("shard", None),
        P(),
        P(None, "shard"),
        P("shard"),
        P(),
        P(),
    )
    out_specs = (
        P(("rep", "shard"), None),
        P(("rep", "shard"), None),
        P("shard", None),
        P("shard", None),
        P("shard", None),
        P("shard", None),
        P(),
        P("shard", None),
        P("shard", None),
        P("shard", None),
        P("shard", None),
        P(),
        P("shard", None),
        P("shard", None),
        P("shard", None),
        P("shard", None),
        P(None, "shard"),
        P("shard"),
        P(),
        P(),
        P(),
    )
    return jax.shard_map(
        on_device, mesh=mesh, in_specs=in_specs, out_specs=out_specs, check_vma=False
    )
```

```python
import functools

import jax
import jax.numpy as jnp
from jax import lax
from jax.experimental import pallas as pl
from jax.experimental.pallas import tpu as pltpu
from jax.sharding import PartitionSpec as P

HEADS = 16
STEP = 10
BLOCK = 256


eps_norm = 1e-05
eps_second = 1e-30
rate_step = 0.5
clip_level = 1.0
masked = -1e30
gelu_root = (2.0 / 3.141592653589793) ** 0.5
gelu_cubic = 0.044715

f32 = jnp.float32
bf16 = jnp.bfloat16


def norm_parts(values):
    average = jnp.mean(values, axis=-1, keepdims=True)
    centred = values - average
    inv_std = lax.rsqrt(jnp.mean(centred * centred, axis=-1, keepdims=True) + eps_norm)
    return (centred * inv_std, inv_std)


def norm_back(grad_out, normed, inv_std, gain_vec):
    grad_normed = grad_out * gain_vec
    inner_mean = jnp.mean(grad_normed * normed, axis=-1, keepdims=True)
    centred = grad_normed - jnp.mean(grad_normed, axis=-1, keepdims=True)
    return (centred - normed * inner_mean) * inv_std


def gelu_value(pre_act):
    curve = jnp.tanh(gelu_root * (pre_act + gelu_cubic * pre_act * pre_act * pre_act))
    return 0.5 * pre_act * (1.0 + curve)


def gelu_slope(pre_act):
    square = pre_act * pre_act
    curve = jnp.tanh(gelu_root * (pre_act + gelu_cubic * square * pre_act))
    inner = gelu_root * (1.0 + 3.0 * gelu_cubic * square)
    return 0.5 * (1.0 + curve) + 0.5 * pre_act * (1.0 - curve * curve) * inner


def dot(left_side, right_side):
    return jnp.dot(left_side, right_side, preferred_element_type=f32)


def dot_right(left_side, right_side):
    return lax.dot_general(
        left_side, right_side, (((1,), (1,)), ((), ())), preferred_element_type=f32
    )


def dot_rows(left_side, right_side):
    return lax.dot_general(
        left_side, right_side, (((0,), (0,)), ((), ())), preferred_element_type=f32
    )


def pick(stack, index, axis=0):
    return lax.dynamic_index_in_dim(stack, index, axis, keepdims=False)


def place(stack, part, index, axis=0):
    return lax.dynamic_update_index_in_dim(stack, part, index, axis)


def head_rows(number, head_width):
    return slice(number * head_width, (number + 1) * head_width)


def lane_masks(block_rows, width, heads):
    lanes = lax.broadcasted_iota(jnp.int32, (block_rows, width), 1)
    head_width = width // heads
    return [
        (lanes >= number * head_width) & (lanes < (number + 1) * head_width)
        for number in range(heads)
    ]


def allowed_pairs(key_block, query_block, start_row, block):
    key_pos = lax.broadcasted_iota(jnp.int32, (block, block), 0) + key_block * block
    query_pos = lax.broadcasted_iota(jnp.int32, (block, block), 1) + query_block * block
    return (key_pos <= query_pos) & (key_pos >= start_row)


def key_offsets(key_block, query_block, block):
    rows = lax.broadcasted_iota(jnp.int32, (block, 1), 0)
    return (rows + (key_block - query_block) * block).astype(f32)


def turned(values):
    return jnp.transpose(values.astype(f32))


def head_stack(values, lanes):
    zero = jnp.zeros(values.shape, values.dtype)
    return jnp.concatenate([jnp.where(lane, values, zero) for lane in lanes], axis=0)


def eights(values, combine):
    rows, columns = values.shape
    return combine(values.reshape(rows // 8, 8, columns), axis=0)


def forward_kernel(
    heads,
    block,
    low_ref,
    mid_ref,
    slope_ref,
    start_ref,
    qkv_ref,
    out_ref,
    log_ref,
    values_turned,
    key_stack,
    score_ref,
):
    tokens = qkv_ref.shape[0]
    width = qkv_ref.shape[1] // 3
    head_width = width // heads
    blocks = tokens // block
    query_block = pl.program_id(0)

    @pl.when(query_block == 0)
    def _():
        lanes = lane_masks(block, width, heads)
        for number in range(blocks):
            rows = slice(number * block, (number + 1) * block)
            values_turned[number] = turned(qkv_ref[rows, 2 * width :]).astype(bf16)
            key_stack[number] = head_stack(qkv_ref[rows, width : 2 * width], lanes)

    first_row = pl.multiple_of(query_block * block, block)
    queries = qkv_ref[pl.ds(first_row, block), :width].astype(f32) * head_width ** (-0.5)
    queries = turned(queries).astype(bf16)
    start_row = start_ref[query_block]

    def score_step(key_block, bests, with_mask):
        scores = dot(key_stack[key_block], queries)
        offsets = key_offsets(key_block, query_block, block)
        allowed = allowed_pairs(key_block, query_block, start_row, block) if with_mask else None
        result = []
        for number in range(heads):
            rows = head_rows(number, block)
            part = scores[rows] + slope_ref[number] * offsets
            if with_mask:
                part = jnp.where(allowed, part, masked)
            score_ref[key_block, rows, :] = part
            result.append(jnp.maximum(bests[number], eights(part, jnp.max)))
        return tuple(result)

    low, mid = low_ref[query_block], mid_ref[query_block]
    bests = tuple(jnp.full((8, block), masked, f32) for _ in range(heads))
    bests = lax.fori_loop(low, mid, functools.partial(score_step, with_mask=True), bests)
    bests = lax.fori_loop(mid, query_block, functools.partial(score_step, with_mask=False), bests)
    bests = score_step(query_block, bests, True)
    bests = [jnp.max(best, axis=0, keepdims=True) for best in bests]

    def value_step(key_block, state):
        result = []
        for number in range(heads):
            total, gathered = state[2 * number : 2 * number + 2]
            weights = jnp.exp(score_ref[key_block, head_rows(number, block), :] - bests[number])
            value_rows = values_turned[key_block, head_rows(number, head_width), :]
            result += [
                total + eights(weights, jnp.sum),
                gathered + dot(value_rows, weights.astype(bf16)),
            ]
        return tuple(result)

    state = ()
    for number in range(heads):
        state += (jnp.zeros((8, block), f32), jnp.zeros((head_width, block), f32))
    state = lax.fori_loop(low, query_block + 1, value_step, state)
    columns = []
    for number in range(heads):
        total = jnp.sum(state[2 * number], axis=0, keepdims=True)
        columns.append(state[2 * number + 1] / total)
        log_ref[0, number : number + 1, :] = bests[number] + jnp.log(total)
    out_ref[...] = jnp.transpose(jnp.concatenate(columns, axis=0)).astype(bf16)


def backward_kernel(heads, block, first_head, merge, *refs):
    full_ref, high_ref, slope_ref, start_ref, log_ref, qkv_ref, grad_ref, out_ref = refs[:8]
    earlier_ref = refs[8] if merge else None
    result_ref = refs[9 if merge else 8]
    (
        queries_turned,
        grads_turned,
        keys_turned,
        query_stack,
        grad_stack,
        key_stack,
        value_stack,
        delta_rows,
        query_grads,
    ) = refs[10 if merge else 9 :]
    tokens, all_width = grad_ref.shape
    head_width = all_width // log_ref.shape[1]
    width = heads * head_width
    scale = head_width ** (-0.5)
    blocks = tokens // block
    key_block = pl.program_id(0)
    lanes = lane_masks(block, width, heads)

    def columns(kind):
        start = kind * all_width + first_head * head_width
        return slice(start, start + width)

    def target(kind):
        start = (kind * all_width + first_head * head_width) if merge else kind * width
        return slice(start, start + width)

    @pl.when(key_block == 0)
    def _():
        for number in range(blocks):
            rows = slice(number * block, (number + 1) * block)
            queries = qkv_ref[rows, columns(0)]
            queries_turned[number] = turned(queries.astype(f32) * scale).astype(bf16)
            query_stack[number] = head_stack(queries, lanes)
            keys_turned[number] = turned(qkv_ref[rows, columns(1)]).astype(bf16)
            grads = grad_ref[rows, columns(0)]
            grad_stack[number] = head_stack(grads, lanes)
            grads = grads.astype(f32)
            grads_turned[number] = turned(grads).astype(bf16)
            product = turned(grads * out_ref[rows, columns(0)].astype(f32))
            for head in range(heads):
                delta_rows[number, head : head + 1, :] = jnp.sum(
                    product[head_rows(head, head_width)], axis=0, keepdims=True
                )
            query_grads[number] = jnp.zeros((width, block), f32)

    key_row = pl.multiple_of(key_block * block, block)
    key_stack[...] = head_stack(qkv_ref[pl.ds(key_row, block), columns(1)], lanes)
    value_stack[...] = head_stack(qkv_ref[pl.ds(key_row, block), columns(2)], lanes)

    def step(query_block, state, with_mask):
        key_total, value_total = state
        scores = dot(key_stack[...], queries_turned[query_block])
        grad_weights = dot(value_stack[...], grads_turned[query_block])
        offsets = key_offsets(key_block, query_block, block)
        if with_mask:
            allowed = allowed_pairs(key_block, query_block, start_ref[query_block], block)
        weight_list, grad_list = [], []
        for number in range(heads):
            rows = head_rows(number, block)
            head = first_head + number
            part = scores[rows] + slope_ref[head] * offsets
            part = part - log_ref[query_block, head : head + 1, :]
            if with_mask:
                part = jnp.where(allowed, part, masked)
            probabilities = jnp.exp(part)
            delta = delta_rows[query_block, number : number + 1, :]
            grad_scores = (probabilities * (grad_weights[rows] - delta)).astype(bf16)
            weight_list.append(probabilities.astype(bf16))
            grad_list.append(grad_scores)
            rows = head_rows(number, head_width)
            query_grads[query_block, rows, :] += dot(keys_turned[key_block, rows, :], grad_scores)
        weight_row = jnp.concatenate(weight_list, axis=1)
        grad_row = jnp.concatenate(grad_list, axis=1)
        return (
            key_total + dot(grad_row, query_stack[query_block]),
            value_total + dot(weight_row, grad_stack[query_block]),
        )

    state = (jnp.zeros((block, width), f32), jnp.zeros((block, width), f32))
    state = step(key_block, state, True)
    full, high = full_ref[key_block], high_ref[key_block]
    state = lax.fori_loop(key_block + 1, full, functools.partial(step, with_mask=False), state)
    state = lax.fori_loop(full, high, functools.partial(step, with_mask=True), state)
    result_ref[pl.ds(key_row, block), target(1)] = (state[0] * scale).astype(bf16)
    result_ref[pl.ds(key_row, block), target(2)] = state[1].astype(bf16)
    if merge:
        other = first_head * head_width
        for kind in range(3):
            result_ref[pl.ds(key_row, block), kind * all_width : kind * all_width + other] = earlier_ref[
                pl.ds(key_row, block), kind * other : (kind + 1) * other
            ]

    @pl.when(key_block == blocks - 1)
    def _():
        for number in range(blocks):
            rows = slice(number * block, (number + 1) * block)
            result_ref[rows, target(0)] = jnp.transpose(query_grads[number] * scale).astype(bf16)


def block_plan(lengths, tokens, block):
    ends = jnp.cumsum(lengths)
    positions = jnp.arange(tokens, dtype=jnp.int32)
    passed = positions[:, None] >= ends[None, :]
    starts = jnp.max(jnp.where(passed, ends[None, :], 0), axis=1).astype(jnp.int32)
    finish = jnp.min(jnp.where(passed, tokens, ends[None, :]), axis=1).astype(jnp.int32)
    blocks = tokens // block
    number = jnp.arange(blocks, dtype=jnp.int32)
    first_start = starts[::block]
    last_start = starts[block - 1 :: block]
    low = first_start // block
    mid = jnp.clip((last_start + block - 1) // block, low, number)
    high = (finish[block - 1 :: block] - 1) // block + 1
    full = jnp.clip(finish[::block] // block, number + 1, high)
    return (starts.reshape(blocks, 1, block), low, mid, full, high)


def scalar_spec():
    return pl.BlockSpec(memory_space=pltpu.SMEM)


def whole_spec(shape):
    return pl.BlockSpec(shape, lambda step: (0,) * len(shape), pipeline_mode=pl.Buffered(1))


def attend_forward(qkv, plan, slopes, heads, block):
    tokens, triple = qkv.shape
    width = triple // 3
    blocks = tokens // block
    starts, low, mid, full, high = plan
    return pl.pallas_call(
        functools.partial(forward_kernel, heads, block),
        grid=(blocks,),
        in_specs=[
            scalar_spec(),
            scalar_spec(),
            scalar_spec(),
            whole_spec((blocks, 1, block)),
            whole_spec((tokens, triple)),
        ],
        out_specs=[
            pl.BlockSpec((block, width), lambda step: (step, 0)),
            pl.BlockSpec((1, heads, block), lambda step: (step, 0, 0)),
        ],
        out_shape=[
            jax.ShapeDtypeStruct((tokens, width), bf16),
            jax.ShapeDtypeStruct((blocks, heads, block), f32),
        ],
        scratch_shapes=[
            pltpu.VMEM((blocks, width, block), bf16),
            pltpu.VMEM((blocks, heads * block, width), bf16),
            pltpu.VMEM((blocks, heads * block, block), f32),
        ],
        compiler_params=pltpu.CompilerParams(
            dimension_semantics=("arbitrary",), vmem_limit_bytes=40 * 1024 * 1024
        ),
        cost_estimate=pl.CostEstimate(
            flops=3 * tokens * tokens * 256 * heads,
            bytes_accessed=10 * tokens * width,
            transcendentals=tokens * tokens * heads // 2,
        ),
        name="attend_forward",
    )(low, mid, slopes, starts, qkv)


def attend_backward(qkv, grads, outputs, logs, plan, slopes, heads, block, first_head, earlier):
    tokens, triple = qkv.shape
    all_width = triple // 3
    all_heads = logs.shape[1]
    width = all_width // all_heads * heads
    blocks = tokens // block
    starts, low, mid, full, high = plan
    merge = earlier is not None
    result_width = triple if merge else 3 * width
    operands = [full, high, slopes, starts, logs, qkv, grads, outputs]
    specs = [scalar_spec() for _ in range(3)] + [whole_spec(entry.shape) for entry in operands[3:]]
    if merge:
        operands.append(earlier)
        specs.append(whole_spec(earlier.shape))
    return pl.pallas_call(
        functools.partial(backward_kernel, heads, block, first_head, merge),
        grid=(blocks,),
        in_specs=specs,
        out_specs=pl.BlockSpec((tokens, result_width), lambda step: (0, 0)),
        out_shape=jax.ShapeDtypeStruct((tokens, result_width), bf16),
        scratch_shapes=[
            pltpu.VMEM((blocks, width, block), bf16),
            pltpu.VMEM((blocks, width, block), bf16),
            pltpu.VMEM((blocks, width, block), bf16),
            pltpu.VMEM((blocks, heads * block, width), bf16),
            pltpu.VMEM((blocks, heads * block, width), bf16),
            pltpu.VMEM((heads * block, width), bf16),
            pltpu.VMEM((heads * block, width), bf16),
            pltpu.VMEM((blocks, heads, block), f32),
            pltpu.VMEM((blocks, width, block), f32),
        ],
        compiler_params=pltpu.CompilerParams(
            dimension_semantics=("arbitrary",), vmem_limit_bytes=40 * 1024 * 1024
        ),
        cost_estimate=pl.CostEstimate(
            flops=8 * tokens * tokens * 256 * heads,
            bytes_accessed=20 * tokens * width,
            transcendentals=tokens * tokens * heads // 2,
        ),
        name="attend_backward",
    )(*operands)


def together(*values):
    return lax.optimization_barrier(tuple(values))


def ordered(own, other, bit, axis=0):
    first = jnp.where(bit == 0, own, other)
    second = jnp.where(bit == 0, other, own)
    return jnp.stack([first, second], axis=axis)


class Moves:
    def __init__(self):
        self.shards = lax.axis_size("shard")
        self.reps = lax.axis_size("rep")
        self.half = self.shards // 2
        self.chips = self.reps // 2
        self.shard = lax.axis_index("shard")
        self.rep = lax.axis_index("rep")
        self.core = self.rep % 2
        self.chip = self.rep // 2
        self.side = self.shard // self.half
        self.member = self.shard % self.half + self.core * self.half

    def core_swap(self, part):
        return lax.ppermute(part, "rep", [(r, r ^ 1) for r in range(self.reps)])

    def chip_swap(self, part, bits):
        return lax.ppermute(part, "rep", [(r, r ^ (2 * bits)) for r in range(self.reps)])

    def shard_swap(self, part, bits):
        return lax.ppermute(part, "shard", [(s, s ^ bits) for s in range(self.shards)])

    def shard_bit(self, bits):
        return (self.shard // bits) % 2

    def low_bits(self):
        bits, result = 1, []
        while bits < self.half:
            result.append(bits)
            bits *= 2
        return result

    def home_swap(self, part):
        pairs = []
        for rep in range(self.reps):
            for shard in range(self.shards):
                side, core = shard // self.half, rep % 2
                to_rep, to_shard = rep, shard
                if side != core:
                    to_rep = rep ^ 1
                    to_shard = (shard + self.half) % self.shards
                pairs.append((rep * self.shards + shard, to_rep * self.shards + to_shard))
        return lax.ppermute(part, ("rep", "shard"), pairs)

    def half_gather(self, part):
        stack = part[None]
        for bits in self.low_bits():
            own = stack
            stack = ordered(own, self.shard_swap(own, bits), self.shard_bit(bits))
            stack = stack.reshape((-1,) + part.shape)
        return stack

    def cores_gather(self, stack):
        stack = ordered(stack, self.core_swap(stack), self.core)
        return stack.reshape((-1,) + stack.shape[2:])

    def exchange_bit(self, stack, bit, swap):
        sources, targets = stack.shape[:2]
        stack = stack.reshape((sources, 2, targets // 2) + stack.shape[2:])
        own, other = pick(stack, bit, 1), swap(pick(stack, 1 - bit, 1))
        return ordered(own, other, bit, 1).reshape((2 * sources,) + own.shape[1:])

    def half_exchange(self, stack):
        stack = stack[None]
        for bits in reversed(self.low_bits()):
            swap = functools.partial(self.shard_swap, bits=bits)
            stack = self.exchange_bit(stack, self.shard_bit(bits), swap)
        return stack.reshape((self.half,) + stack.shape[2:])

    def cores_exchange(self, stack):
        return self.exchange_bit(stack[None], self.core, self.core_swap)

    def members_exchange(self, stack):
        for bits in reversed(self.low_bits()):
            swap = functools.partial(self.shard_swap, bits=bits)
            stack = self.exchange_bit(stack, self.shard_bit(bits), swap)
        return stack.reshape((self.shards,) + stack.shape[2:])

    def reduce_bit(self, stack, bit, swap):
        stack = stack.reshape((2, stack.shape[0] // 2) + stack.shape[1:])
        other = swap(pick(stack, 1 - bit).astype(bf16))
        return pick(stack, bit).astype(f32) + other.astype(f32)

    def spread_open(self, part):
        if self.chips == 4:
            return (self.chip_swap(part, 1), self.chip_swap(part, 2))
        held, bits = [part], 1
        while bits < self.chips:
            held = held + [self.chip_swap(piece, bits) for piece in held]
            bits *= 2
        return tuple(held[1:])

    def spread_close(self, state):
        if self.chips == 4:
            by_x, by_y = state
            cut = by_x.shape[0] // 2
            far = jnp.concatenate(
                [self.chip_swap(by_x[:cut], 2), self.chip_swap(by_y[cut:], 1)], axis=0
            )
            return (by_x, by_y, far)
        return state

    def chips_gather(self, part, axis, state=None):
        shape = part.shape[:axis] + (self.chips,) + part.shape[axis:]
        stack = place(jnp.zeros(shape, part.dtype), part, self.chip, axis)
        others = self.spread_close(self.spread_open(part) if state is None else state)
        for number, piece in enumerate(others):
            stack = place(stack, piece, self.chip ^ (number + 1), axis)
        return stack

    def reduce_open(self, stack, axis):
        if self.chips == 4:
            shape = stack.shape[:axis] + (2, 2) + stack.shape[axis + 1 :]
            stack = stack.reshape(shape)
            bit_x, bit_y = self.chip % 2, self.chip // 2
            cut = shape[0] // 2
            first, second = stack[:cut], stack[cut:]
            got_first = self.chip_swap(pick(first, 1 - bit_x, axis + 1), 1)
            got_second = self.chip_swap(pick(second, 1 - bit_y, axis), 2)
            return (pick(first, bit_x, axis + 1), pick(second, bit_y, axis), got_first, got_second)
        count = self.chips
        stack = stack.astype(f32)
        while count > 1:
            count //= 2
            shape = stack.shape[:axis] + (2, count) + stack.shape[axis + 1 :]
            stack = stack.reshape(shape)
            bit = (self.chip // count) % 2
            got = self.chip_swap(pick(stack, 1 - bit, axis).astype(bf16), count)
            stack = pick(stack, bit, axis) + got.astype(f32)
        return (pick(stack, 0, axis).astype(bf16),)

    def reduce_add(self, state):
        if self.chips != 4:
            return state
        first, second, got_first, got_second = state
        first = (first.astype(f32) + got_first.astype(f32)).astype(bf16)
        second = (second.astype(f32) + got_second.astype(f32)).astype(bf16)
        return (first, second)

    def reduce_close(self, state, axis):
        if self.chips != 4:
            return state[0]
        first, second = state
        bit_x, bit_y = self.chip % 2, self.chip // 2
        got_first = self.chip_swap(pick(first, 1 - bit_y, axis), 2)
        got_second = self.chip_swap(pick(second, 1 - bit_x, axis), 1)
        first = pick(first, bit_y, axis).astype(f32) + got_first.astype(f32)
        second = pick(second, bit_x, axis).astype(f32) + got_second.astype(f32)
        return jnp.concatenate([first, second], axis=0).astype(bf16)

    def chips_reduce(self, stack, axis):
        return self.reduce_close(self.reduce_add(self.reduce_open(stack, axis)), axis)

    def core_pair(self, part):
        other = self.core_swap(part)
        first = jnp.where(self.core == 0, part, other)
        second = jnp.where(self.core == 0, other, part)
        return first, second

    def sum_reps(self, vector):
        bits = 1
        while bits < self.reps:
            vector = vector + lax.ppermute(vector, "rep", [(r, r ^ bits) for r in range(self.reps)])
            bits *= 2
        return vector

    def sum_shards(self, vector):
        bits = 1
        while bits < self.shards:
            vector = vector + self.shard_swap(vector, bits)
            bits *= 2
        return vector


def factor_stats(gradient, weight, rows_old, decay_rate):
    square = gradient * gradient
    rows_new = decay_rate * rows_old + (1.0 - decay_rate) * (jnp.mean(square, axis=1) + eps_second)
    col_squares = jnp.sum(square, axis=0, keepdims=True)
    col_scaled = jnp.sum(square / rows_new[:, None], axis=0, keepdims=True)
    scalars = [jnp.sum(rows_new), jnp.sum(weight * weight)]
    scalars = jnp.concatenate([jnp.full((1, 128), scalar, f32) for scalar in scalars], axis=0)
    return rows_new, [jnp.concatenate([col_squares, col_scaled], axis=0), scalars]


def factor_apply(gradient, weight, rows_new, sums, cols_old, height, decay_rate):
    columns, scalars = sums
    breadth = gradient.shape[1]
    row_sum, weight_sum = scalars[0, 0], scalars[1, 0]
    cols_new = decay_rate * cols_old + (1.0 - decay_rate) * (columns[0] / height + eps_second)
    row_mean = row_sum / height
    rms_update = jnp.sqrt(row_mean / (height * breadth) * jnp.sum(columns[1] / cols_new))
    rms_weight = jnp.sqrt(weight_sum / (height * breadth))
    factor = rate_step * rms_weight * jnp.sqrt(row_mean) / jnp.maximum(1.0, rms_update / clip_level)
    new_weight = weight - gradient * (factor * lax.rsqrt(rows_new))[:, None] * lax.rsqrt(cols_new)[None, :]
    return new_weight, cols_new, rms_update


def summed(moves, entries):
    total = moves.sum_shards(jnp.concatenate(entries, axis=1))
    result, offset = [], 0
    for entry in entries:
        result.append(total[:, offset : offset + entry.shape[1]])
        offset += entry.shape[1]
    return result


def on_device(
    tokens,
    cotangent,
    seq_lengths,
    qkv_weight,
    out_weight,
    up_weight,
    down_weight,
    vectors,
    row_state,
    down_rows,
    col_state,
    vector_state,
):
    moves = Moves()
    shards, half, chips, core = moves.shards, moves.half, moves.chips, moves.core
    row_count, width = tokens.shape
    hidden_width = up_weight.shape[1]
    group_rows = row_count * shards
    heads = HEADS // shards
    head_width = width // HEADS
    span = heads * head_width
    member = moves.member
    decay_rate = 1.0 - STEP ** (-0.8)
    head_number = (member * heads + jnp.arange(heads, dtype=jnp.int32)).astype(f32)
    slopes = jnp.exp2(-8.0 * (head_number + 1.0) / HEADS)

    gain_one = vectors[0:width]
    shift_one = vectors[width : 2 * width]
    bias_query = vectors[2 * width : 3 * width]
    bias_value = vectors[3 * width : 4 * width]
    bias_out = vectors[4 * width : 5 * width]
    gain_two = vectors[5 * width : 6 * width]
    shift_two = vectors[6 * width : 7 * width]
    bias_up = vectors[7 * width : 7 * width + hidden_width]
    bias_down = vectors[7 * width + hidden_width :]

    home_tokens = moves.home_swap(tokens)
    other_lengths = moves.core_swap(seq_lengths)
    lengths = jnp.where(moves.side == core, seq_lengths, other_lengths)[0]
    plan = block_plan(lengths, group_rows, BLOCK)
    rows_z = width // shards
    rows_piece = rows_z // chips
    my_rows = qkv_weight.astype(bf16)
    my_blocks = []
    for number in range(half):
        kinds = []
        for kind in range(3):
            first = kind * width + number * span
            second = first + half * span
            kinds.append(
                jnp.where(
                    core == 0, my_rows[:, first : first + span], my_rows[:, second : second + span]
                )
            )
        my_blocks.append(jnp.concatenate(kinds, axis=1))
    near_part = moves.half_exchange(jnp.stack(my_blocks))

    half_cols = hidden_width // (2 * shards)
    up_wide = shards * half_cols
    out_wide = width // 2
    down_piece = half_cols // chips
    down_fold = down_piece // rows_piece
    all_wide = up_wide + out_wide + down_fold * width

    def core_half(values):
        parts = []
        for number in range(shards):
            start = 2 * number * half_cols
            first = values[..., start : start + half_cols]
            second = values[..., start + half_cols : start + 2 * half_cols]
            parts.append(jnp.where(core == 0, first, second))
        return jnp.concatenate(parts, axis=-1)

    up_own = core_half(up_weight).astype(bf16).reshape(chips, rows_piece, up_wide)
    out_own = jnp.where(core == 0, out_weight[:, :out_wide], out_weight[:, out_wide:]).astype(bf16)
    out_own = out_own.reshape(chips, rows_piece, out_wide)
    down_own = lax.dynamic_slice_in_dim(down_weight, core * half_cols, half_cols, 0).astype(bf16)
    down_own = down_own.reshape(chips, down_fold, rows_piece, width)
    my_down = pick(down_own, moves.chip)
    weight_piece = jnp.concatenate(
        [pick(up_own, moves.chip), pick(out_own, moves.chip)]
        + [my_down[number] for number in range(down_fold)],
        axis=1,
    )
    near_pieces, bits = [weight_piece], 1
    while bits < half:
        near_pieces = near_pieces + [moves.shard_swap(piece, bits) for piece in near_pieces]
        bits *= 2
    near_pieces = near_pieces[1:]
    weight_piece, home_tokens, near_pieces, near_part = together(
        weight_piece, home_tokens, near_pieces, near_part
    )
    qkv_cols = ordered(near_part, moves.shard_swap(near_part, half), moves.side)
    qkv_cols = qkv_cols.reshape(width, 3 * span)
    inputs = home_tokens.astype(f32)
    normed_one, inv_std_one = norm_parts(inputs)
    act_one = (normed_one * gain_one + shift_one).astype(bf16)
    act_half = moves.half_gather(act_one)

    near_open = [moves.spread_open(piece) for piece in near_pieces]
    act_half, near_open, qkv_cols, weight_piece = together(
        act_half, near_open, qkv_cols, weight_piece
    )
    far_piece = moves.shard_swap(weight_piece, half)
    act_all = moves.cores_gather(act_half).reshape(group_rows, width)
    near_spread = [moves.spread_close(state) for state in near_open]

    bias_q_part = lax.dynamic_slice_in_dim(bias_query, member * span, span)
    bias_v_part = lax.dynamic_slice_in_dim(bias_value, member * span, span)
    qkv_bias = jnp.concatenate([bias_q_part, jnp.zeros_like(bias_q_part), bias_v_part])
    qkv_rows = (dot(act_all, qkv_cols) + qkv_bias).astype(bf16)
    attended_cols, logs = attend_forward(qkv_rows, plan, slopes, heads, BLOCK)
    attended_parts = moves.cores_exchange(attended_cols.reshape(shards, row_count, span))
    attended_parts, far_piece, near_spread, cotangent = together(
        attended_parts, far_piece, near_spread, cotangent
    )
    attended_parts = moves.members_exchange(attended_parts)
    far_open = moves.spread_open(far_piece)
    far_pieces, bits = [far_piece], 1
    while bits < half:
        far_pieces = far_pieces + [moves.shard_swap(piece, bits) for piece in far_pieces]
        bits *= 2
    far_pieces = far_pieces[1:]
    home_cot = moves.home_swap(cotangent)
    attended_parts, far_open, far_pieces = together(attended_parts, far_open, far_pieces)
    attended = jnp.concatenate([attended_parts[k] for k in range(shards)], axis=1)

    far_spread = [moves.spread_close(far_open)]
    far_spread += [moves.spread_close(moves.spread_open(piece)) for piece in far_pieces]
    arrived = [(piece,) + tuple(spread) for piece, spread in zip(near_pieces, near_spread)]
    arrived += [
        (piece,) + tuple(spread) for piece, spread in zip([far_piece] + far_pieces, far_spread)
    ]
    up_all = place(jnp.zeros((shards, chips, rows_piece, up_wide), bf16), up_own, moves.shard)
    out_all = place(jnp.zeros((shards, chips, rows_piece, out_wide), bf16), out_own, moves.shard)
    down_all = place(
        jnp.zeros((shards, chips, down_fold, rows_piece, width), bf16), down_own, moves.shard
    )
    for number, pieces in enumerate(arrived):
        plane = moves.shard ^ (number + 1)
        for far, spread in enumerate(pieces):
            chip = moves.chip ^ far
            up_all = lax.dynamic_update_slice(up_all, spread[None, None, :, :up_wide], (plane, chip, 0, 0))
            out_all = lax.dynamic_update_slice(
                out_all, spread[None, None, :, up_wide : up_wide + out_wide], (plane, chip, 0, 0)
            )
            folds = [
                spread[:, up_wide + out_wide + k * width : up_wide + out_wide + (k + 1) * width]
                for k in range(down_fold)
            ]
            down_all = lax.dynamic_update_slice(
                down_all, jnp.stack(folds)[None, None], (plane, chip, 0, 0, 0)
            )
    up_half = up_all.reshape(width, up_wide)
    down_half = down_all.reshape(up_wide, width)
    out_first, out_second = moves.core_pair(out_all.reshape(width, out_wide))
    out_low = jnp.concatenate([out_first, out_second], axis=1)
    residual = inputs + dot(attended, out_low) + bias_out
    normed_two, inv_std_two = norm_parts(residual)
    act_two = (normed_two * gain_two + shift_two).astype(bf16)

    act_two_other, attended_other, cot_other = together(
        moves.core_swap(act_two), moves.core_swap(attended), moves.core_swap(home_cot)
    )
    cot_pair = jnp.concatenate([home_cot, cot_other], axis=0)
    act_two_pair = jnp.concatenate([act_two, act_two_other], axis=0)
    attended_pair = jnp.concatenate([attended, attended_other], axis=0)
    bias_up_half = core_half(bias_up)
    up_pair = dot(act_two_pair, up_half) + bias_up_half
    hidden_pair = gelu_value(up_pair).astype(bf16)
    slope_pair = gelu_slope(up_pair).astype(bf16)
    down_terms = dot_rows(hidden_pair, cot_pair).astype(bf16)
    down_terms = down_terms.reshape(shards, chips, down_piece, width)
    grad_y = home_cot.astype(f32)
    grad_bias_down = jnp.sum(grad_y, axis=0)
    grad_up_pair = (dot_right(cot_pair, down_half) * slope_pair.astype(f32)).astype(bf16)
    grad_bias_up = jnp.sum(grad_up_pair, axis=0, dtype=f32)
    back_other = moves.core_swap(dot_right(grad_up_pair[row_count:], up_half).astype(bf16))
    up_terms = dot_rows(act_two_pair, grad_up_pair).astype(bf16)
    up_terms = up_terms.reshape(shards, chips, rows_piece, up_wide)
    down_state = moves.reduce_open(down_terms, 1)
    down_other = moves.core_swap(dot(hidden_pair[row_count:], down_half).astype(bf16))
    back_other, down_other, up_terms, down_state = together(
        back_other, down_other, up_terms, down_state
    )
    up_state = moves.reduce_open(up_terms, 1)
    down_mid = moves.reduce_close(moves.reduce_add(down_state), 1)
    grad_act_two = dot_right(grad_up_pair[:row_count], up_half) + back_other.astype(f32)
    grad_gain_two = jnp.sum(grad_act_two * normed_two, axis=0)
    grad_shift_two = jnp.sum(grad_act_two, axis=0)
    grad_residual = grad_y + norm_back(grad_act_two, normed_two, inv_std_two, gain_two)
    grad_attn = grad_residual.astype(bf16)
    grad_bias_out = jnp.sum(grad_attn, axis=0, dtype=f32)
    to_members = jnp.stack(
        [
            dot_right(grad_attn, out_low[k * span : (k + 1) * span]).astype(bf16)
            for k in range(shards)
        ]
    )
    attn_halves = [grad_attn[:, :out_wide], grad_attn[:, out_wide:]]
    attn_own = jnp.where(core == 0, attn_halves[0], attn_halves[1])
    attn_other = jnp.where(core == 0, attn_halves[1], attn_halves[0])
    grad_heads, attn_other = together(moves.cores_exchange(to_members), moves.core_swap(attn_other))
    attn_pair = jnp.concatenate([attn_own, attn_other], axis=0)
    grad_heads = moves.members_exchange(grad_heads).reshape(group_rows, span)
    block_out = (
        residual + dot(hidden_pair[:row_count], down_half) + down_other.astype(f32) + bias_down
    ).astype(bf16)

    out_terms = dot_rows(attended_pair, attn_pair).astype(bf16)
    def shards_sum(piece):
        rows = piece.shape[1]
        return lax.psum_scatter(
            piece.reshape(shards * rows, piece.shape[2]), "shard", scatter_dimension=0, tiled=True
        )

    grad_heads, down_mid, out_terms, block_out = together(
        grad_heads, down_mid, out_terms, block_out
    )
    block_out = moves.home_swap(block_out)
    down_owned = shards_sum(down_mid)
    out_state = moves.reduce_open(out_terms.reshape(shards, chips, rows_piece, out_wide), 1)
    attend_args = (plan, slopes)
    parts = 2 if heads % 4 == 0 else 1
    part_heads = heads // parts
    grad_qkv = attend_backward(
        qkv_rows, grad_heads, attended_cols, logs, *attend_args, part_heads, BLOCK, 0, None
    )
    grad_qkv, up_state, out_state, block_out = together(grad_qkv, up_state, out_state, block_out)
    up_sums, out_sums = moves.reduce_add(up_state), moves.reduce_add(out_state)
    grad_qkv, up_sums, out_sums = together(grad_qkv, up_sums, out_sums)
    up_out_state = [
        jnp.concatenate([up_part, out_part], axis=-1) for up_part, out_part in zip(up_sums, out_sums)
    ]
    if parts == 2:
        grad_qkv = attend_backward(
            qkv_rows, grad_heads, attended_cols, logs, *attend_args, part_heads, BLOCK, part_heads, grad_qkv
        )
    up_out_piece = moves.reduce_close(up_out_state, 1)
    grad_qkv, up_out_piece = together(grad_qkv, up_out_piece)
    up_out_owned = shards_sum(up_out_piece)

    grad_bias_q_part = jnp.sum(grad_qkv[:, :span], axis=0, dtype=f32)
    grad_bias_v_part = jnp.sum(grad_qkv[:, 2 * span :], axis=0, dtype=f32)

    grad_halves = grad_qkv.reshape(2, half * row_count, 3 * span)
    sent = dot_right(pick(grad_halves, 1 - core), qkv_cols).astype(bf16)
    back = dot_right(pick(grad_halves, core), qkv_cols) + moves.core_swap(sent).astype(f32)
    down_owned, back_sum = together(down_owned, back)
    down_first, down_second = moves.core_pair(
        moves.chips_gather(down_owned, 0).reshape(half_cols, width)
    )
    qkv_terms = dot_rows(act_all, grad_qkv).astype(bf16)
    qkv_terms = qkv_terms.reshape(shards, chips, rows_piece, 3 * span)
    qkv_state = moves.reduce_add(moves.reduce_open(qkv_terms, 1))
    qkv_state, back_sum = together(qkv_state, back_sum)
    qkv_piece = moves.reduce_close(qkv_state, 1)
    back = back_sum.reshape(half, row_count, width)
    for bits in reversed(moves.low_bits()):
        back = moves.reduce_bit(
            back, moves.shard_bit(bits), functools.partial(moves.shard_swap, bits=bits)
        )
    qkv_piece = moves.reduce_bit(
        qkv_piece, moves.side, functools.partial(moves.shard_swap, bits=half)
    )
    qkv_piece = moves.half_exchange(qkv_piece.astype(bf16))
    back, qkv_piece, down_first, down_second, up_out_owned = together(
        back, qkv_piece, down_first, down_second, up_out_owned
    )
    up_out_state = moves.spread_open(up_out_owned)
    down_grad = jnp.concatenate([down_first, down_second], axis=0).astype(f32)
    grad_act_one = back.reshape(row_count, width)
    grad_gain_one = jnp.sum(grad_act_one * normed_one, axis=0)
    grad_shift_one = jnp.sum(grad_act_one, axis=0)
    grad_inputs = grad_residual + norm_back(grad_act_one, normed_one, inv_std_one, gain_one)
    tokens_grad = moves.home_swap(grad_inputs.astype(bf16))
    grad_gain_one, *up_out_state = together(grad_gain_one, *up_out_state)
    up_out_first, up_out_second = moves.core_pair(
        moves.chips_gather(up_out_owned, 0, tuple(up_out_state)).reshape(rows_z, up_wide + out_wide)
    )
    out_grad = jnp.concatenate(
        [up_out_first[:, up_wide:], up_out_second[:, up_wide:]], axis=1
    ).astype(f32)
    up_columns = []
    for number in range(shards):
        part = slice(number * half_cols, (number + 1) * half_cols)
        up_columns += [up_out_first[:, part], up_out_second[:, part]]
    up_grad = jnp.concatenate(up_columns, axis=1).astype(f32)
    qkv_owned = moves.chips_gather(qkv_piece, 1)
    qkv_first, qkv_second = moves.core_pair(qkv_owned.reshape(half, rows_z, 3 * span))
    qkv_columns = []
    for kind in range(3):
        for source in (qkv_first, qkv_second):
            for number in range(half):
                qkv_columns.append(source[number][:, kind * span : (kind + 1) * span])
    qkv_grad = jnp.concatenate(qkv_columns, axis=1).astype(f32)

    stats = [
        factor_stats(qkv_grad, qkv_weight, row_state[0], decay_rate),
        factor_stats(out_grad, out_weight, row_state[1], decay_rate),
        factor_stats(up_grad, up_weight, row_state[2], decay_rate),
        factor_stats(down_grad, down_weight, down_rows, decay_rate),
    ]
    def spread_heads(part):
        return [jnp.where(member == number, part, 0.0) for number in range(shards)]

    bias_up_parts = []
    for number in range(shards):
        part = grad_bias_up[number * half_cols : (number + 1) * half_cols]
        bias_up_parts += [jnp.where(core == 0, part, 0.0), jnp.where(core == 1, part, 0.0)]
    vector_part = moves.sum_reps(
        jnp.concatenate(
            [grad_gain_one, grad_shift_one]
            + spread_heads(grad_bias_q_part)
            + spread_heads(grad_bias_v_part)
            + [grad_bias_out, grad_gain_two, grad_shift_two]
            + bias_up_parts
            + [grad_bias_down]
        )
    )
    early_sums = summed(moves, stats[1][1] + stats[2][1] + stats[3][1])
    vector_rows, tokens_grad = together(vector_part.reshape(2, -1), tokens_grad)
    late_sums = summed(moves, stats[0][1] + [vector_rows])
    sums = [late_sums[0:2], early_sums[0:2], early_sums[2:4], early_sums[4:6]]
    vector_grad = late_sums[2].reshape(-1)
    gradients = [qkv_grad, out_grad, up_grad, down_grad]
    weights = [qkv_weight, out_weight, up_weight, down_weight]
    heights = [width, width, width, hidden_width]
    new_weights, new_cols, rms_values = [], [], []
    offset = 0
    for number in range(4):
        end_col = offset + gradients[number].shape[1]
        new_weight, cols_new, rms_update = factor_apply(
            gradients[number],
            weights[number],
            stats[number][0],
            sums[number],
            col_state[offset:end_col],
            heights[number],
            decay_rate,
        )
        new_weights.append(new_weight)
        new_cols.append(cols_new)
        rms_values.append(rms_update)
        offset = end_col

    vector_state_new = decay_rate * vector_state + (1.0 - decay_rate) * (
        vector_grad * vector_grad + eps_second
    )
    vector_step = vector_grad * lax.rsqrt(vector_state_new)
    vector_rms = jnp.sqrt(jnp.mean(vector_step * vector_step))
    vector_new = vectors - rate_step * jnp.sqrt(
        jnp.mean(vectors * vectors)
    ) * vector_step / jnp.maximum(1.0, vector_rms / clip_level)
    update_rms = jnp.stack(rms_values + [vector_rms])
    return (
        block_out,
        tokens_grad,
        qkv_grad,
        out_grad,
        up_grad,
        down_grad,
        vector_grad,
        new_weights[0],
        new_weights[1],
        new_weights[2],
        new_weights[3],
        vector_new,
        new_weights[0].astype(bf16),
        new_weights[1].astype(bf16),
        new_weights[2].astype(bf16),
        new_weights[3].astype(bf16),
        jnp.stack([stats[0][0], stats[1][0], stats[2][0]]),
        stats[3][0],
        jnp.concatenate(new_cols),
        vector_state_new,
        update_rms,
    )


def solution(mesh):
    in_specs = (
        P(("rep", "shard"), None),
        P(("rep", "shard"), None),
        P("rep", None),
        P("shard", None),
        P("shard", None),
        P("shard", None),
        P("shard", None),
        P(),
        P(None, "shard"),
        P("shard"),
        P(),
        P(),
    )
    out_specs = (
        P(("rep", "shard"), None),
        P(("rep", "shard"), None),
        P("shard", None),
        P("shard", None),
        P("shard", None),
        P("shard", None),
        P(),
        P("shard", None),
        P("shard", None),
        P("shard", None),
        P("shard", None),
        P(),
        P("shard", None),
        P("shard", None),
        P("shard", None),
        P("shard", None),
        P(None, "shard"),
        P("shard"),
        P(),
        P(),
        P(),
    )
    return jax.shard_map(
        on_device, mesh=mesh, in_specs=in_specs, out_specs=out_specs, check_vma=False
    )
```

```python
import functools

import jax
import jax.numpy as jnp
from jax import lax
from jax.experimental import pallas as pl
from jax.experimental.pallas import tpu as pltpu
from jax.sharding import PartitionSpec as P

HEADS = 16
STEP = 10
BLOCK = 256


eps_norm = 1e-05
eps_second = 1e-30
rate_step = 0.5
clip_level = 1.0
masked = -1e30
gelu_root = (2.0 / 3.141592653589793) ** 0.5
gelu_cubic = 0.044715

f32 = jnp.float32
bf16 = jnp.bfloat16


def norm_parts(values):
    average = jnp.mean(values, axis=-1, keepdims=True)
    centred = values - average
    inv_std = lax.rsqrt(jnp.mean(centred * centred, axis=-1, keepdims=True) + eps_norm)
    return (centred * inv_std, inv_std)


def norm_back(grad_out, normed, inv_std, gain_vec):
    grad_normed = grad_out * gain_vec
    inner_mean = jnp.mean(grad_normed * normed, axis=-1, keepdims=True)
    centred = grad_normed - jnp.mean(grad_normed, axis=-1, keepdims=True)
    return (centred - normed * inner_mean) * inv_std


def gelu_value(pre_act):
    curve = jnp.tanh(gelu_root * (pre_act + gelu_cubic * pre_act * pre_act * pre_act))
    return 0.5 * pre_act * (1.0 + curve)


def gelu_slope(pre_act):
    square = pre_act * pre_act
    curve = jnp.tanh(gelu_root * (pre_act + gelu_cubic * square * pre_act))
    inner = gelu_root * (1.0 + 3.0 * gelu_cubic * square)
    return 0.5 * (1.0 + curve) + 0.5 * pre_act * (1.0 - curve * curve) * inner


def dot(left_side, right_side):
    return jnp.dot(left_side, right_side, preferred_element_type=f32)


def dot_right(left_side, right_side):
    return lax.dot_general(
        left_side, right_side, (((1,), (1,)), ((), ())), preferred_element_type=f32
    )


def dot_rows(left_side, right_side):
    return lax.dot_general(
        left_side, right_side, (((0,), (0,)), ((), ())), preferred_element_type=f32
    )


def pick(stack, index, axis=0):
    return lax.dynamic_index_in_dim(stack, index, axis, keepdims=False)


def place(stack, part, index, axis=0):
    return lax.dynamic_update_index_in_dim(stack, part, index, axis)


def head_rows(number, head_width):
    return slice(number * head_width, (number + 1) * head_width)


def lane_masks(block_rows, width, heads):
    lanes = lax.broadcasted_iota(jnp.int32, (block_rows, width), 1)
    head_width = width // heads
    return [
        (lanes >= number * head_width) & (lanes < (number + 1) * head_width)
        for number in range(heads)
    ]


def allowed_pairs(key_block, query_block, start_row, block):
    key_pos = lax.broadcasted_iota(jnp.int32, (block, block), 0) + key_block * block
    query_pos = lax.broadcasted_iota(jnp.int32, (block, block), 1) + query_block * block
    return (key_pos <= query_pos) & (key_pos >= start_row)


def key_offsets(key_block, query_block, block):
    rows = lax.broadcasted_iota(jnp.int32, (block, 1), 0)
    return (rows + (key_block - query_block) * block).astype(f32)


def turned(values):
    return jnp.transpose(values.astype(f32))


def head_stack(values, lanes):
    zero = jnp.zeros(values.shape, values.dtype)
    return jnp.concatenate([jnp.where(lane, values, zero) for lane in lanes], axis=0)


def eights(values, combine):
    rows, columns = values.shape
    return combine(values.reshape(rows // 8, 8, columns), axis=0)


def forward_kernel(
    heads,
    block,
    low_ref,
    mid_ref,
    slope_ref,
    start_ref,
    qkv_ref,
    out_ref,
    log_ref,
    values_turned,
    key_stack,
    score_ref,
):
    tokens = qkv_ref.shape[0]
    width = qkv_ref.shape[1] // 3
    head_width = width // heads
    blocks = tokens // block
    query_block = pl.program_id(0)

    @pl.when(query_block == 0)
    def _():
        lanes = lane_masks(block, width, heads)
        for number in range(blocks):
            rows = slice(number * block, (number + 1) * block)
            values_turned[number] = turned(qkv_ref[rows, 2 * width :]).astype(bf16)
            key_stack[number] = head_stack(qkv_ref[rows, width : 2 * width], lanes)

    first_row = pl.multiple_of(query_block * block, block)
    queries = qkv_ref[pl.ds(first_row, block), :width].astype(f32) * head_width ** (-0.5)
    queries = turned(queries).astype(bf16)
    start_row = start_ref[query_block]

    def score_step(key_block, bests, with_mask):
        scores = dot(key_stack[key_block], queries)
        offsets = key_offsets(key_block, query_block, block)
        allowed = allowed_pairs(key_block, query_block, start_row, block) if with_mask else None
        result = []
        for number in range(heads):
            rows = head_rows(number, block)
            part = scores[rows] + slope_ref[number] * offsets
            if with_mask:
                part = jnp.where(allowed, part, masked)
            score_ref[key_block, rows, :] = part
            result.append(jnp.maximum(bests[number], eights(part, jnp.max)))
        return tuple(result)

    low, mid = low_ref[query_block], mid_ref[query_block]
    bests = tuple(jnp.full((8, block), masked, f32) for _ in range(heads))
    bests = lax.fori_loop(low, mid, functools.partial(score_step, with_mask=True), bests)
    bests = lax.fori_loop(mid, query_block, functools.partial(score_step, with_mask=False), bests)
    bests = score_step(query_block, bests, True)
    bests = [jnp.max(best, axis=0, keepdims=True) for best in bests]

    def value_step(key_block, state):
        result = []
        for number in range(heads):
            total, gathered = state[2 * number : 2 * number + 2]
            weights = jnp.exp(score_ref[key_block, head_rows(number, block), :] - bests[number])
            value_rows = values_turned[key_block, head_rows(number, head_width), :]
            result += [
                total + eights(weights, jnp.sum),
                gathered + dot(value_rows, weights.astype(bf16)),
            ]
        return tuple(result)

    state = ()
    for number in range(heads):
        state += (jnp.zeros((8, block), f32), jnp.zeros((head_width, block), f32))
    state = lax.fori_loop(low, query_block + 1, value_step, state)
    columns = []
    for number in range(heads):
        total = jnp.sum(state[2 * number], axis=0, keepdims=True)
        columns.append(state[2 * number + 1] / total)
        log_ref[0, number : number + 1, :] = bests[number] + jnp.log(total)
    out_ref[...] = jnp.transpose(jnp.concatenate(columns, axis=0)).astype(bf16)


def backward_kernel(heads, block, first_head, merge, *refs):
    full_ref, high_ref, slope_ref, start_ref, log_ref, qkv_ref, grad_ref, out_ref = refs[:8]
    earlier_ref = refs[8] if merge else None
    result_ref = refs[9 if merge else 8]
    (
        queries_turned,
        grads_turned,
        keys_turned,
        query_stack,
        grad_stack,
        key_stack,
        value_stack,
        delta_rows,
        query_grads,
    ) = refs[10 if merge else 9 :]
    tokens, all_width = grad_ref.shape
    head_width = all_width // log_ref.shape[1]
    width = heads * head_width
    scale = head_width ** (-0.5)
    blocks = tokens // block
    key_block = pl.program_id(0)
    lanes = lane_masks(block, width, heads)

    def columns(kind):
        start = kind * all_width + first_head * head_width
        return slice(start, start + width)

    def target(kind):
        start = (kind * all_width + first_head * head_width) if merge else kind * width
        return slice(start, start + width)

    @pl.when(key_block == 0)
    def _():
        for number in range(blocks):
            rows = slice(number * block, (number + 1) * block)
            queries = qkv_ref[rows, columns(0)]
            queries_turned[number] = turned(queries.astype(f32) * scale).astype(bf16)
            query_stack[number] = head_stack(queries, lanes)
            keys_turned[number] = turned(qkv_ref[rows, columns(1)]).astype(bf16)
            grads = grad_ref[rows, columns(0)]
            grad_stack[number] = head_stack(grads, lanes)
            grads = grads.astype(f32)
            grads_turned[number] = turned(grads).astype(bf16)
            product = turned(grads * out_ref[rows, columns(0)].astype(f32))
            for head in range(heads):
                delta_rows[number, head : head + 1, :] = jnp.sum(
                    product[head_rows(head, head_width)], axis=0, keepdims=True
                )
            query_grads[number] = jnp.zeros((width, block), f32)

    key_row = pl.multiple_of(key_block * block, block)
    key_stack[...] = head_stack(qkv_ref[pl.ds(key_row, block), columns(1)], lanes)
    value_stack[...] = head_stack(qkv_ref[pl.ds(key_row, block), columns(2)], lanes)

    def step(query_block, state, with_mask):
        key_total, value_total = state
        scores = dot(key_stack[...], queries_turned[query_block])
        grad_weights = dot(value_stack[...], grads_turned[query_block])
        offsets = key_offsets(key_block, query_block, block)
        if with_mask:
            allowed = allowed_pairs(key_block, query_block, start_ref[query_block], block)
        weight_list, grad_list = [], []
        for number in range(heads):
            rows = head_rows(number, block)
            head = first_head + number
            part = scores[rows] + slope_ref[head] * offsets
            part = part - log_ref[query_block, head : head + 1, :]
            if with_mask:
                part = jnp.where(allowed, part, masked)
            probabilities = jnp.exp(part)
            delta = delta_rows[query_block, number : number + 1, :]
            grad_scores = (probabilities * (grad_weights[rows] - delta)).astype(bf16)
            weight_list.append(probabilities.astype(bf16))
            grad_list.append(grad_scores)
            rows = head_rows(number, head_width)
            query_grads[query_block, rows, :] += dot(keys_turned[key_block, rows, :], grad_scores)
        weight_row = jnp.concatenate(weight_list, axis=1)
        grad_row = jnp.concatenate(grad_list, axis=1)
        return (
            key_total + dot(grad_row, query_stack[query_block]),
            value_total + dot(weight_row, grad_stack[query_block]),
        )

    state = (jnp.zeros((block, width), f32), jnp.zeros((block, width), f32))
    state = step(key_block, state, True)
    full, high = full_ref[key_block], high_ref[key_block]
    state = lax.fori_loop(key_block + 1, full, functools.partial(step, with_mask=False), state)
    state = lax.fori_loop(full, high, functools.partial(step, with_mask=True), state)
    result_ref[pl.ds(key_row, block), target(1)] = (state[0] * scale).astype(bf16)
    result_ref[pl.ds(key_row, block), target(2)] = state[1].astype(bf16)
    if merge:
        other = first_head * head_width
        for kind in range(3):
            result_ref[pl.ds(key_row, block), kind * all_width : kind * all_width + other] = earlier_ref[
                pl.ds(key_row, block), kind * other : (kind + 1) * other
            ]

    @pl.when(key_block == blocks - 1)
    def _():
        for number in range(blocks):
            rows = slice(number * block, (number + 1) * block)
            result_ref[rows, target(0)] = jnp.transpose(query_grads[number] * scale).astype(bf16)


def block_plan(lengths, tokens, block):
    ends = jnp.cumsum(lengths)
    positions = jnp.arange(tokens, dtype=jnp.int32)
    passed = positions[:, None] >= ends[None, :]
    starts = jnp.max(jnp.where(passed, ends[None, :], 0), axis=1).astype(jnp.int32)
    finish = jnp.min(jnp.where(passed, tokens, ends[None, :]), axis=1).astype(jnp.int32)
    blocks = tokens // block
    number = jnp.arange(blocks, dtype=jnp.int32)
    first_start = starts[::block]
    last_start = starts[block - 1 :: block]
    low = first_start // block
    mid = jnp.clip((last_start + block - 1) // block, low, number)
    high = (finish[block - 1 :: block] - 1) // block + 1
    full = jnp.clip(finish[::block] // block, number + 1, high)
    return (starts.reshape(blocks, 1, block), low, mid, full, high)


def scalar_spec():
    return pl.BlockSpec(memory_space=pltpu.SMEM)


def whole_spec(shape):
    return pl.BlockSpec(shape, lambda step: (0,) * len(shape), pipeline_mode=pl.Buffered(1))


def attend_forward(qkv, plan, slopes, heads, block):
    tokens, triple = qkv.shape
    width = triple // 3
    blocks = tokens // block
    starts, low, mid, full, high = plan
    return pl.pallas_call(
        functools.partial(forward_kernel, heads, block),
        grid=(blocks,),
        in_specs=[
            scalar_spec(),
            scalar_spec(),
            scalar_spec(),
            whole_spec((blocks, 1, block)),
            whole_spec((tokens, triple)),
        ],
        out_specs=[
            pl.BlockSpec((block, width), lambda step: (step, 0)),
            pl.BlockSpec((1, heads, block), lambda step: (step, 0, 0)),
        ],
        out_shape=[
            jax.ShapeDtypeStruct((tokens, width), bf16),
            jax.ShapeDtypeStruct((blocks, heads, block), f32),
        ],
        scratch_shapes=[
            pltpu.VMEM((blocks, width, block), bf16),
            pltpu.VMEM((blocks, heads * block, width), bf16),
            pltpu.VMEM((blocks, heads * block, block), f32),
        ],
        compiler_params=pltpu.CompilerParams(
            dimension_semantics=("arbitrary",), vmem_limit_bytes=40 * 1024 * 1024
        ),
        cost_estimate=pl.CostEstimate(
            flops=3 * tokens * tokens * 256 * heads,
            bytes_accessed=10 * tokens * width,
            transcendentals=tokens * tokens * heads // 2,
        ),
        name="attend_forward",
    )(low, mid, slopes, starts, qkv)


def attend_backward(qkv, grads, outputs, logs, plan, slopes, heads, block, first_head, earlier):
    tokens, triple = qkv.shape
    all_width = triple // 3
    all_heads = logs.shape[1]
    width = all_width // all_heads * heads
    blocks = tokens // block
    starts, low, mid, full, high = plan
    merge = earlier is not None
    result_width = triple if merge else 3 * width
    operands = [full, high, slopes, starts, logs, qkv, grads, outputs]
    specs = [scalar_spec() for _ in range(3)] + [whole_spec(entry.shape) for entry in operands[3:]]
    if merge:
        operands.append(earlier)
        specs.append(whole_spec(earlier.shape))
    return pl.pallas_call(
        functools.partial(backward_kernel, heads, block, first_head, merge),
        grid=(blocks,),
        in_specs=specs,
        out_specs=pl.BlockSpec((tokens, result_width), lambda step: (0, 0)),
        out_shape=jax.ShapeDtypeStruct((tokens, result_width), bf16),
        scratch_shapes=[
            pltpu.VMEM((blocks, width, block), bf16),
            pltpu.VMEM((blocks, width, block), bf16),
            pltpu.VMEM((blocks, width, block), bf16),
            pltpu.VMEM((blocks, heads * block, width), bf16),
            pltpu.VMEM((blocks, heads * block, width), bf16),
            pltpu.VMEM((heads * block, width), bf16),
            pltpu.VMEM((heads * block, width), bf16),
            pltpu.VMEM((blocks, heads, block), f32),
            pltpu.VMEM((blocks, width, block), f32),
        ],
        compiler_params=pltpu.CompilerParams(
            dimension_semantics=("arbitrary",), vmem_limit_bytes=40 * 1024 * 1024
        ),
        cost_estimate=pl.CostEstimate(
            flops=8 * tokens * tokens * 256 * heads,
            bytes_accessed=20 * tokens * width,
            transcendentals=tokens * tokens * heads // 2,
        ),
        name="attend_backward",
    )(*operands)


def together(*values):
    return lax.optimization_barrier(tuple(values))


def ordered(own, other, bit, axis=0):
    first = jnp.where(bit == 0, own, other)
    second = jnp.where(bit == 0, other, own)
    return jnp.stack([first, second], axis=axis)


class Moves:
    def __init__(self):
        self.shards = lax.axis_size("shard")
        self.reps = lax.axis_size("rep")
        self.half = self.shards // 2
        self.chips = self.reps // 2
        self.shard = lax.axis_index("shard")
        self.rep = lax.axis_index("rep")
        self.core = self.rep % 2
        self.chip = self.rep // 2
        self.side = self.shard // self.half
        self.member = self.shard % self.half + self.core * self.half

    def core_swap(self, part):
        return lax.ppermute(part, "rep", [(r, r ^ 1) for r in range(self.reps)])

    def chip_swap(self, part, bits):
        return lax.ppermute(part, "rep", [(r, r ^ (2 * bits)) for r in range(self.reps)])

    def shard_swap(self, part, bits):
        return lax.ppermute(part, "shard", [(s, s ^ bits) for s in range(self.shards)])

    def shard_bit(self, bits):
        return (self.shard // bits) % 2

    def low_bits(self):
        bits, result = 1, []
        while bits < self.half:
            result.append(bits)
            bits *= 2
        return result

    def home_swap(self, part):
        pairs = []
        for rep in range(self.reps):
            for shard in range(self.shards):
                side, core = shard // self.half, rep % 2
                to_rep, to_shard = rep, shard
                if side != core:
                    to_rep = rep ^ 1
                    to_shard = (shard + self.half) % self.shards
                pairs.append((rep * self.shards + shard, to_rep * self.shards + to_shard))
        return lax.ppermute(part, ("rep", "shard"), pairs)

    def half_gather(self, part):
        stack = part[None]
        for bits in self.low_bits():
            own = stack
            stack = ordered(own, self.shard_swap(own, bits), self.shard_bit(bits))
            stack = stack.reshape((-1,) + part.shape)
        return stack

    def cores_gather(self, stack):
        stack = ordered(stack, self.core_swap(stack), self.core)
        return stack.reshape((-1,) + stack.shape[2:])

    def exchange_bit(self, stack, bit, swap):
        sources, targets = stack.shape[:2]
        stack = stack.reshape((sources, 2, targets // 2) + stack.shape[2:])
        own, other = pick(stack, bit, 1), swap(pick(stack, 1 - bit, 1))
        return ordered(own, other, bit, 1).reshape((2 * sources,) + own.shape[1:])

    def half_exchange(self, stack):
        stack = stack[None]
        for bits in reversed(self.low_bits()):
            swap = functools.partial(self.shard_swap, bits=bits)
            stack = self.exchange_bit(stack, self.shard_bit(bits), swap)
        return stack.reshape((self.half,) + stack.shape[2:])

    def cores_exchange(self, stack):
        return self.exchange_bit(stack[None], self.core, self.core_swap)

    def members_exchange(self, stack):
        for bits in reversed(self.low_bits()):
            swap = functools.partial(self.shard_swap, bits=bits)
            stack = self.exchange_bit(stack, self.shard_bit(bits), swap)
        return stack.reshape((self.shards,) + stack.shape[2:])

    def reduce_bit(self, stack, bit, swap):
        stack = stack.reshape((2, stack.shape[0] // 2) + stack.shape[1:])
        other = swap(pick(stack, 1 - bit).astype(bf16))
        return pick(stack, bit).astype(f32) + other.astype(f32)

    def spread_open(self, part):
        if self.chips == 4:
            return (self.chip_swap(part, 1), self.chip_swap(part, 2))
        held, bits = [part], 1
        while bits < self.chips:
            held = held + [self.chip_swap(piece, bits) for piece in held]
            bits *= 2
        return tuple(held[1:])

    def spread_close(self, state):
        if self.chips == 4:
            by_x, by_y = state
            cut, axis = by_x.shape[-2] // 2, by_x.ndim - 2
            far = jnp.concatenate(
                [
                    self.chip_swap(by_x[..., :cut, :], 2),
                    self.chip_swap(by_y[..., cut:, :], 1),
                ],
                axis=axis,
            )
            return (by_x, by_y, far)
        return state

    def chips_gather(self, part, axis, state=None):
        shape = part.shape[:axis] + (self.chips,) + part.shape[axis:]
        stack = place(jnp.zeros(shape, part.dtype), part, self.chip, axis)
        others = self.spread_close(self.spread_open(part) if state is None else state)
        for number, piece in enumerate(others):
            stack = place(stack, piece, self.chip ^ (number + 1), axis)
        return stack

    def reduce_open(self, stack, axis):
        if self.chips == 4:
            shape = stack.shape[:axis] + (2, 2) + stack.shape[axis + 1 :]
            stack = stack.reshape(shape)
            bit_x, bit_y = self.chip % 2, self.chip // 2
            cut = shape[0] // 2
            first, second = stack[:cut], stack[cut:]
            got_first = self.chip_swap(pick(first, 1 - bit_x, axis + 1), 1)
            got_second = self.chip_swap(pick(second, 1 - bit_y, axis), 2)
            return (pick(first, bit_x, axis + 1), pick(second, bit_y, axis), got_first, got_second)
        count = self.chips
        stack = stack.astype(f32)
        while count > 1:
            count //= 2
            shape = stack.shape[:axis] + (2, count) + stack.shape[axis + 1 :]
            stack = stack.reshape(shape)
            bit = (self.chip // count) % 2
            got = self.chip_swap(pick(stack, 1 - bit, axis).astype(bf16), count)
            stack = pick(stack, bit, axis) + got.astype(f32)
        return (pick(stack, 0, axis).astype(bf16),)

    def reduce_add(self, state):
        if self.chips != 4:
            return state
        first, second, got_first, got_second = state
        first = (first.astype(f32) + got_first.astype(f32)).astype(bf16)
        second = (second.astype(f32) + got_second.astype(f32)).astype(bf16)
        return (first, second)

    def reduce_send(self, state, axis):
        if self.chips != 4:
            return state
        first, second = state
        bit_x, bit_y = self.chip % 2, self.chip // 2
        got_first = self.chip_swap(pick(first, 1 - bit_y, axis), 2)
        got_second = self.chip_swap(pick(second, 1 - bit_x, axis), 1)
        return (pick(first, bit_y, axis), pick(second, bit_x, axis), got_first, got_second)

    def reduce_final(self, state):
        if self.chips != 4:
            return state[0]
        first, second, got_first, got_second = state
        first = first.astype(f32) + got_first.astype(f32)
        second = second.astype(f32) + got_second.astype(f32)
        return jnp.concatenate([first, second], axis=0).astype(bf16)

    def reduce_close(self, state, axis):
        return self.reduce_final(self.reduce_send(state, axis))

    def core_pair(self, part):
        other = self.core_swap(part)
        first = jnp.where(self.core == 0, part, other)
        second = jnp.where(self.core == 0, other, part)
        return first, second

    def sum_reps(self, vector):
        bits = 1
        while bits < self.reps:
            vector = vector + lax.ppermute(vector, "rep", [(r, r ^ bits) for r in range(self.reps)])
            bits *= 2
        return vector

    def sum_shards(self, vector):
        bits = 1
        while bits < self.shards:
            vector = vector + self.shard_swap(vector, bits)
            bits *= 2
        return vector


def factor_stats(gradient, weight, rows_old, decay_rate):
    square = gradient * gradient
    rows_new = decay_rate * rows_old + (1.0 - decay_rate) * (jnp.mean(square, axis=1) + eps_second)
    col_squares = jnp.sum(square, axis=0, keepdims=True)
    col_scaled = jnp.sum(square / rows_new[:, None], axis=0, keepdims=True)
    scalars = [jnp.sum(rows_new), jnp.sum(weight * weight)]
    scalars = jnp.concatenate([jnp.full((1, 128), scalar, f32) for scalar in scalars], axis=0)
    return rows_new, [jnp.concatenate([col_squares, col_scaled], axis=0), scalars]


def factor_apply(gradient, weight, rows_new, sums, cols_old, height, decay_rate):
    columns, scalars = sums
    breadth = gradient.shape[1]
    row_sum, weight_sum = scalars[0, 0], scalars[1, 0]
    cols_new = decay_rate * cols_old + (1.0 - decay_rate) * (columns[0] / height + eps_second)
    row_mean = row_sum / height
    rms_update = jnp.sqrt(row_mean / (height * breadth) * jnp.sum(columns[1] / cols_new))
    rms_weight = jnp.sqrt(weight_sum / (height * breadth))
    factor = rate_step * rms_weight * jnp.sqrt(row_mean) / jnp.maximum(1.0, rms_update / clip_level)
    new_weight = weight - gradient * (factor * lax.rsqrt(rows_new))[:, None] * lax.rsqrt(cols_new)[None, :]
    return new_weight, cols_new, rms_update


def summed(moves, entries):
    total = moves.sum_shards(jnp.concatenate(entries, axis=1))
    result, offset = [], 0
    for entry in entries:
        result.append(total[:, offset : offset + entry.shape[1]])
        offset += entry.shape[1]
    return result


def on_device(
    tokens,
    cotangent,
    seq_lengths,
    qkv_weight,
    out_weight,
    up_weight,
    down_weight,
    vectors,
    row_state,
    down_rows,
    col_state,
    vector_state,
):
    moves = Moves()
    shards, half, chips, core = moves.shards, moves.half, moves.chips, moves.core
    row_count, width = tokens.shape
    hidden_width = up_weight.shape[1]
    group_rows = row_count * shards
    heads = HEADS // shards
    head_width = width // HEADS
    span = heads * head_width
    member = moves.member
    decay_rate = 1.0 - STEP ** (-0.8)
    head_number = (member * heads + jnp.arange(heads, dtype=jnp.int32)).astype(f32)
    slopes = jnp.exp2(-8.0 * (head_number + 1.0) / HEADS)

    gain_one = vectors[0:width]
    shift_one = vectors[width : 2 * width]
    bias_query = vectors[2 * width : 3 * width]
    bias_value = vectors[3 * width : 4 * width]
    bias_out = vectors[4 * width : 5 * width]
    gain_two = vectors[5 * width : 6 * width]
    shift_two = vectors[6 * width : 7 * width]
    bias_up = vectors[7 * width : 7 * width + hidden_width]
    bias_down = vectors[7 * width + hidden_width :]

    home_tokens = moves.home_swap(tokens)
    other_lengths = moves.core_swap(seq_lengths)
    lengths = jnp.where(moves.side == core, seq_lengths, other_lengths)[0]
    plan = block_plan(lengths, group_rows, BLOCK)
    rows_z = width // shards
    rows_piece = rows_z // chips
    my_rows = lax.dynamic_slice_in_dim(qkv_weight, moves.chip * rows_piece, rows_piece, 0)
    my_rows = my_rows.astype(bf16)
    my_blocks = []
    for number in range(half):
        kinds = []
        for kind in range(3):
            first = kind * width + number * span
            second = first + half * span
            kinds.append(
                jnp.where(
                    core == 0, my_rows[:, first : first + span], my_rows[:, second : second + span]
                )
            )
        my_blocks.append(jnp.concatenate(kinds, axis=1))
    qkv_part = moves.half_exchange(jnp.stack(my_blocks))
    qkv_part = ordered(qkv_part, moves.shard_swap(qkv_part, half), moves.side)
    qkv_part = qkv_part.reshape(shards, rows_piece, 3 * span)

    half_cols = hidden_width // (2 * shards)
    up_wide = shards * half_cols
    out_wide = width // 2
    down_piece = half_cols // chips

    def core_half(values):
        parts = []
        for number in range(shards):
            start = 2 * number * half_cols
            first = values[..., start : start + half_cols]
            second = values[..., start + half_cols : start + 2 * half_cols]
            parts.append(jnp.where(core == 0, first, second))
        return jnp.concatenate(parts, axis=-1)

    up_own = core_half(up_weight).astype(bf16).reshape(chips, rows_piece, up_wide)
    out_own = jnp.where(core == 0, out_weight[:, :out_wide], out_weight[:, out_wide:]).astype(bf16)
    out_own = out_own.reshape(chips, rows_piece, out_wide)
    down_own = lax.dynamic_slice_in_dim(down_weight, core * half_cols, half_cols, 0).astype(bf16)
    down_own = down_own.reshape(chips, down_piece, width)
    up_out_piece = jnp.concatenate([pick(up_own, moves.chip), pick(out_own, moves.chip)], axis=1)
    up_out_planes = lax.all_gather(up_out_piece, "shard")
    down_planes = lax.all_gather(pick(down_own, moves.chip), "shard")

    def foreign(planes):
        return jnp.stack([pick(planes, (moves.shard + k) % shards) for k in range(1, shards)])

    def place_planes(stack, parts, columns):
        for far, part in enumerate(parts):
            chip = moves.chip ^ far
            for k in range(1, shards):
                plane = (moves.shard + k) % shards
                entry = part[k - 1 : k, None, :, columns]
                stack = lax.dynamic_update_slice(stack, entry, (plane, chip, 0, 0))
        return stack

    home_tokens, qkv_part = together(home_tokens, qkv_part)
    qkv_cols = moves.chips_gather(qkv_part, 1).reshape(width, 3 * span)
    inputs = home_tokens.astype(f32)
    normed_one, inv_std_one = norm_parts(inputs)
    act_one = (normed_one * gain_one + shift_one).astype(bf16)
    act_half = moves.half_gather(act_one)

    act_half, qkv_cols, up_out_planes, cotangent = together(
        act_half, qkv_cols, up_out_planes, cotangent
    )
    up_out_foreign = foreign(up_out_planes)
    up_out_open = moves.spread_open(up_out_foreign)
    act_all = moves.cores_gather(act_half).reshape(group_rows, width)
    home_cot = moves.home_swap(cotangent)

    bias_q_part = lax.dynamic_slice_in_dim(bias_query, member * span, span)
    bias_v_part = lax.dynamic_slice_in_dim(bias_value, member * span, span)
    qkv_bias = jnp.concatenate([bias_q_part, jnp.zeros_like(bias_q_part), bias_v_part])
    qkv_rows = (dot(act_all, qkv_cols) + qkv_bias).astype(bf16)
    attended_cols, logs = attend_forward(qkv_rows, plan, slopes, heads, BLOCK)
    attended_parts = moves.cores_exchange(attended_cols.reshape(shards, row_count, span))
    attended_parts, up_out_open, down_planes = together(attended_parts, up_out_open, down_planes)
    attended_parts = moves.members_exchange(attended_parts)
    up_out_spread = moves.spread_close(up_out_open)
    down_foreign = foreign(down_planes)
    down_open = moves.spread_open(down_foreign)
    attended_parts, up_out_spread, home_cot = together(attended_parts, up_out_spread, home_cot)
    attended = jnp.concatenate([attended_parts[k] for k in range(shards)], axis=1)

    up_all = place(jnp.zeros((shards, chips, rows_piece, up_wide), bf16), up_own, moves.shard)
    out_all = place(jnp.zeros((shards, chips, rows_piece, out_wide), bf16), out_own, moves.shard)
    down_all = place(jnp.zeros((shards, chips, down_piece, width), bf16), down_own, moves.shard)
    up_out_parts = (up_out_foreign,) + tuple(up_out_spread)
    out_all = place_planes(out_all, up_out_parts, slice(up_wide, up_wide + out_wide))
    up_all = place_planes(up_all, up_out_parts, slice(0, up_wide))
    down_parts = (down_foreign,) + tuple(moves.spread_close(down_open))
    down_all = place_planes(down_all, down_parts, slice(0, width))
    up_half = up_all.reshape(width, up_wide)
    down_half = down_all.reshape(up_wide, width)
    out_first, out_second = moves.core_pair(out_all.reshape(width, out_wide))
    out_low = jnp.concatenate([out_first, out_second], axis=1)
    residual = inputs + dot(attended, out_low) + bias_out
    normed_two, inv_std_two = norm_parts(residual)
    act_two = (normed_two * gain_two + shift_two).astype(bf16)

    act_two_other, attended_other, cot_other = together(
        moves.core_swap(act_two), moves.core_swap(attended), moves.core_swap(home_cot)
    )
    cot_pair = jnp.concatenate([home_cot, cot_other], axis=0)
    act_two_pair = jnp.concatenate([act_two, act_two_other], axis=0)
    attended_pair = jnp.concatenate([attended, attended_other], axis=0)
    bias_up_half = core_half(bias_up)
    up_pair = dot(act_two_pair, up_half) + bias_up_half
    hidden_pair = gelu_value(up_pair).astype(bf16)
    slope_pair = gelu_slope(up_pair).astype(bf16)
    down_terms = dot_rows(hidden_pair, cot_pair).astype(bf16)
    down_terms = down_terms.reshape(shards, chips, down_piece, width)
    cot_pair, down_terms = together(cot_pair, down_terms)
    grad_y = home_cot.astype(f32)
    grad_bias_down = jnp.sum(grad_y, axis=0)
    grad_up_pair = (dot_right(cot_pair, down_half) * slope_pair.astype(f32)).astype(bf16)
    grad_bias_up = jnp.sum(grad_up_pair, axis=0, dtype=f32)
    back_other = moves.core_swap(dot_right(grad_up_pair[row_count:], up_half).astype(bf16))
    up_terms = dot_rows(act_two_pair, grad_up_pair).astype(bf16)
    up_terms = up_terms.reshape(shards, chips, rows_piece, up_wide)
    down_state = moves.reduce_open(down_terms, 1)
    back_other, hidden_pair, up_terms, down_state = together(
        back_other, hidden_pair, up_terms, down_state
    )
    up_state = moves.reduce_open(up_terms, 1)
    down_mid = moves.reduce_close(moves.reduce_add(down_state), 1)
    grad_act_two = dot_right(grad_up_pair[:row_count], up_half) + back_other.astype(f32)
    grad_gain_two = jnp.sum(grad_act_two * normed_two, axis=0)
    grad_shift_two = jnp.sum(grad_act_two, axis=0)
    grad_residual = grad_y + norm_back(grad_act_two, normed_two, inv_std_two, gain_two)
    grad_attn = grad_residual.astype(bf16)
    grad_bias_out = jnp.sum(grad_attn, axis=0, dtype=f32)
    to_members = jnp.stack(
        [
            dot_right(grad_attn, out_low[k * span : (k + 1) * span]).astype(bf16)
            for k in range(shards)
        ]
    )
    attn_halves = [grad_attn[:, :out_wide], grad_attn[:, out_wide:]]
    attn_own = jnp.where(core == 0, attn_halves[0], attn_halves[1])
    attn_other = jnp.where(core == 0, attn_halves[1], attn_halves[0])
    grad_heads, attn_other = together(moves.cores_exchange(to_members), moves.core_swap(attn_other))
    attn_pair = jnp.concatenate([attn_own, attn_other], axis=0)
    grad_heads, hidden_pair = together(grad_heads, hidden_pair)
    grad_heads = moves.members_exchange(grad_heads).reshape(group_rows, span)
    down_other = moves.core_swap(dot(hidden_pair[row_count:], down_half).astype(bf16))
    block_out = (
        residual + dot(hidden_pair[:row_count], down_half) + down_other.astype(f32) + bias_down
    ).astype(bf16)

    out_terms = dot_rows(attended_pair, attn_pair).astype(bf16)
    def shards_sum(piece):
        rows = piece.shape[1]
        return lax.psum_scatter(
            piece.reshape(shards * rows, piece.shape[2]), "shard", scatter_dimension=0, tiled=True
        )

    grad_heads, down_mid, out_terms, block_out = together(
        grad_heads, down_mid, out_terms, block_out
    )
    block_out = moves.home_swap(block_out)
    down_owned = shards_sum(down_mid)
    out_state = moves.reduce_open(out_terms.reshape(shards, chips, rows_piece, out_wide), 1)
    attend_args = (plan, slopes)
    parts = 2 if heads % 4 == 0 else 1
    part_heads = heads // parts
    grad_qkv = attend_backward(
        qkv_rows, grad_heads, attended_cols, logs, *attend_args, part_heads, BLOCK, 0, None
    )
    grad_qkv, up_state, out_state = together(grad_qkv, up_state, out_state)
    up_sums, out_sums = moves.reduce_add(up_state), moves.reduce_add(out_state)
    grad_qkv, up_sums, out_sums = together(grad_qkv, up_sums, out_sums)
    up_out_state = [
        jnp.concatenate([up_part, out_part], axis=-1) for up_part, out_part in zip(up_sums, out_sums)
    ]
    if parts == 2:
        grad_qkv = attend_backward(
            qkv_rows, grad_heads, attended_cols, logs, *attend_args, part_heads, BLOCK, part_heads, grad_qkv
        )
    grad_qkv, up_out_state, block_out = together(
        grad_qkv, moves.reduce_send(up_out_state, 1), block_out
    )
    up_out_piece = moves.reduce_final(up_out_state)
    up_out_owned = shards_sum(up_out_piece)

    grad_bias_q_part = jnp.sum(grad_qkv[:, :span], axis=0, dtype=f32)
    grad_bias_v_part = jnp.sum(grad_qkv[:, 2 * span :], axis=0, dtype=f32)

    grad_halves = grad_qkv.reshape(2, half * row_count, 3 * span)
    sent = dot_right(pick(grad_halves, 1 - core), qkv_cols).astype(bf16)
    back = dot_right(pick(grad_halves, core), qkv_cols) + moves.core_swap(sent).astype(f32)
    down_owned, back_sum = together(down_owned, back)
    down_first, down_second = moves.core_pair(
        moves.chips_gather(down_owned, 0).reshape(half_cols, width)
    )
    qkv_terms = dot_rows(act_all, grad_qkv).astype(bf16)
    qkv_terms = qkv_terms.reshape(shards, chips, rows_piece, 3 * span)
    qkv_state = moves.reduce_add(moves.reduce_open(qkv_terms, 1))
    qkv_state, back_sum = together(qkv_state, back_sum)
    qkv_piece = moves.reduce_close(qkv_state, 1)
    back = back_sum.reshape(half, row_count, width)
    for bits in reversed(moves.low_bits()):
        back = moves.reduce_bit(
            back, moves.shard_bit(bits), functools.partial(moves.shard_swap, bits=bits)
        )
    qkv_piece = moves.reduce_bit(
        qkv_piece, moves.side, functools.partial(moves.shard_swap, bits=half)
    )
    qkv_piece = moves.half_exchange(qkv_piece.astype(bf16))
    back, qkv_piece, down_first, down_second, up_out_owned = together(
        back, qkv_piece, down_first, down_second, up_out_owned
    )
    up_out_state = moves.spread_open(up_out_owned)
    down_grad = jnp.concatenate([down_first, down_second], axis=0).astype(f32)
    grad_act_one = back.reshape(row_count, width)
    grad_gain_one = jnp.sum(grad_act_one * normed_one, axis=0)
    grad_shift_one = jnp.sum(grad_act_one, axis=0)
    grad_inputs = grad_residual + norm_back(grad_act_one, normed_one, inv_std_one, gain_one)
    tokens_grad = moves.home_swap(grad_inputs.astype(bf16))
    grad_gain_one, *up_out_state = together(grad_gain_one, *up_out_state)
    up_out_first, up_out_second = moves.core_pair(
        moves.chips_gather(up_out_owned, 0, tuple(up_out_state)).reshape(rows_z, up_wide + out_wide)
    )
    out_grad = jnp.concatenate(
        [up_out_first[:, up_wide:], up_out_second[:, up_wide:]], axis=1
    ).astype(f32)
    up_columns = []
    for number in range(shards):
        part = slice(number * half_cols, (number + 1) * half_cols)
        up_columns += [up_out_first[:, part], up_out_second[:, part]]
    up_grad = jnp.concatenate(up_columns, axis=1).astype(f32)
    qkv_owned = moves.chips_gather(qkv_piece, 1)
    qkv_first, qkv_second = moves.core_pair(qkv_owned.reshape(half, rows_z, 3 * span))
    qkv_columns = []
    for kind in range(3):
        for source in (qkv_first, qkv_second):
            for number in range(half):
                qkv_columns.append(source[number][:, kind * span : (kind + 1) * span])
    qkv_grad = jnp.concatenate(qkv_columns, axis=1).astype(f32)

    stats = [
        factor_stats(qkv_grad, qkv_weight, row_state[0], decay_rate),
        factor_stats(out_grad, out_weight, row_state[1], decay_rate),
        factor_stats(up_grad, up_weight, row_state[2], decay_rate),
        factor_stats(down_grad, down_weight, down_rows, decay_rate),
    ]
    def spread_heads(part):
        return [jnp.where(member == number, part, 0.0) for number in range(shards)]

    bias_up_parts = []
    for number in range(shards):
        part = grad_bias_up[number * half_cols : (number + 1) * half_cols]
        bias_up_parts += [jnp.where(core == 0, part, 0.0), jnp.where(core == 1, part, 0.0)]
    vector_part = moves.sum_reps(
        jnp.concatenate(
            [grad_gain_one, grad_shift_one]
            + spread_heads(grad_bias_q_part)
            + spread_heads(grad_bias_v_part)
            + [grad_bias_out, grad_gain_two, grad_shift_two]
            + bias_up_parts
            + [grad_bias_down]
        )
    )
    early_sums = summed(moves, stats[1][1] + stats[2][1] + stats[3][1])
    vector_rows, tokens_grad = together(vector_part.reshape(2, -1), tokens_grad)
    late_sums = summed(moves, stats[0][1] + [vector_rows])
    sums = [late_sums[0:2], early_sums[0:2], early_sums[2:4], early_sums[4:6]]
    vector_grad = late_sums[2].reshape(-1)
    gradients = [qkv_grad, out_grad, up_grad, down_grad]
    weights = [qkv_weight, out_weight, up_weight, down_weight]
    heights = [width, width, width, hidden_width]
    new_weights, new_cols, rms_values = [], [], []
    offset = 0
    for number in range(4):
        end_col = offset + gradients[number].shape[1]
        new_weight, cols_new, rms_update = factor_apply(
            gradients[number],
            weights[number],
            stats[number][0],
            sums[number],
            col_state[offset:end_col],
            heights[number],
            decay_rate,
        )
        new_weights.append(new_weight)
        new_cols.append(cols_new)
        rms_values.append(rms_update)
        offset = end_col

    vector_state_new = decay_rate * vector_state + (1.0 - decay_rate) * (
        vector_grad * vector_grad + eps_second
    )
    vector_step = vector_grad * lax.rsqrt(vector_state_new)
    vector_rms = jnp.sqrt(jnp.mean(vector_step * vector_step))
    vector_new = vectors - rate_step * jnp.sqrt(
        jnp.mean(vectors * vectors)
    ) * vector_step / jnp.maximum(1.0, vector_rms / clip_level)
    update_rms = jnp.stack(rms_values + [vector_rms])
    return (
        block_out,
        tokens_grad,
        qkv_grad,
        out_grad,
        up_grad,
        down_grad,
        vector_grad,
        new_weights[0],
        new_weights[1],
        new_weights[2],
        new_weights[3],
        vector_new,
        new_weights[0].astype(bf16),
        new_weights[1].astype(bf16),
        new_weights[2].astype(bf16),
        new_weights[3].astype(bf16),
        jnp.stack([stats[0][0], stats[1][0], stats[2][0]]),
        stats[3][0],
        jnp.concatenate(new_cols),
        vector_state_new,
        update_rms,
    )


def solution(mesh):
    in_specs = (
        P(("rep", "shard"), None),
        P(("rep", "shard"), None),
        P("rep", None),
        P("shard", None),
        P("shard", None),
        P("shard", None),
        P("shard", None),
        P(),
        P(None, "shard"),
        P("shard"),
        P(),
        P(),
    )
    out_specs = (
        P(("rep", "shard"), None),
        P(("rep", "shard"), None),
        P("shard", None),
        P("shard", None),
        P("shard", None),
        P("shard", None),
        P(),
        P("shard", None),
        P("shard", None),
        P("shard", None),
        P("shard", None),
        P(),
        P("shard", None),
        P("shard", None),
        P("shard", None),
        P("shard", None),
        P(None, "shard"),
        P("shard"),
        P(),
        P(),
        P(),
    )
    return jax.shard_map(
        on_device, mesh=mesh, in_specs=in_specs, out_specs=out_specs, check_vma=False
    )
```

```python
import functools

import jax
import jax.numpy as jnp
from jax import lax
from jax.experimental import pallas as pl
from jax.experimental.pallas import tpu as pltpu
from jax.sharding import PartitionSpec as P

HEADS = 16
STEP = 10
BLOCK = 256


eps_norm = 1e-05
eps_second = 1e-30
rate_step = 0.5
clip_level = 1.0
masked = -1e30
gelu_root = (2.0 / 3.141592653589793) ** 0.5
gelu_cubic = 0.044715

f32 = jnp.float32
bf16 = jnp.bfloat16


def norm_parts(values):
    average = jnp.mean(values, axis=-1, keepdims=True)
    centred = values - average
    inv_std = lax.rsqrt(jnp.mean(centred * centred, axis=-1, keepdims=True) + eps_norm)
    return (centred * inv_std, inv_std)


def norm_back(grad_out, normed, inv_std, gain_vec):
    grad_normed = grad_out * gain_vec
    inner_mean = jnp.mean(grad_normed * normed, axis=-1, keepdims=True)
    centred = grad_normed - jnp.mean(grad_normed, axis=-1, keepdims=True)
    return (centred - normed * inner_mean) * inv_std


def gelu_value(pre_act):
    curve = jnp.tanh(gelu_root * (pre_act + gelu_cubic * pre_act * pre_act * pre_act))
    return 0.5 * pre_act * (1.0 + curve)


def gelu_slope(pre_act):
    square = pre_act * pre_act
    curve = jnp.tanh(gelu_root * (pre_act + gelu_cubic * square * pre_act))
    inner = gelu_root * (1.0 + 3.0 * gelu_cubic * square)
    return 0.5 * (1.0 + curve) + 0.5 * pre_act * (1.0 - curve * curve) * inner


def dot(left_side, right_side):
    return jnp.dot(left_side, right_side, preferred_element_type=f32)


def dot_right(left_side, right_side):
    return lax.dot_general(
        left_side, right_side, (((1,), (1,)), ((), ())), preferred_element_type=f32
    )


def dot_rows(left_side, right_side):
    return lax.dot_general(
        left_side, right_side, (((0,), (0,)), ((), ())), preferred_element_type=f32
    )


def pick(stack, index, axis=0):
    return lax.dynamic_index_in_dim(stack, index, axis, keepdims=False)


def place(stack, part, index, axis=0):
    return lax.dynamic_update_index_in_dim(stack, part, index, axis)


def head_rows(number, head_width):
    return slice(number * head_width, (number + 1) * head_width)


def lane_masks(block_rows, width, heads):
    lanes = lax.broadcasted_iota(jnp.int32, (block_rows, width), 1)
    head_width = width // heads
    return [
        (lanes >= number * head_width) & (lanes < (number + 1) * head_width)
        for number in range(heads)
    ]


def allowed_pairs(key_block, query_block, start_row, block):
    key_pos = lax.broadcasted_iota(jnp.int32, (block, block), 0) + key_block * block
    query_pos = lax.broadcasted_iota(jnp.int32, (block, block), 1) + query_block * block
    return (key_pos <= query_pos) & (key_pos >= start_row)


def key_offsets(key_block, query_block, block):
    rows = lax.broadcasted_iota(jnp.int32, (block, 1), 0)
    return (rows + (key_block - query_block) * block).astype(f32)


def turned(values):
    return jnp.transpose(values.astype(f32))


def head_stack(values, lanes):
    zero = jnp.zeros(values.shape, values.dtype)
    return jnp.concatenate([jnp.where(lane, values, zero) for lane in lanes], axis=0)


def eights(values, combine):
    rows, columns = values.shape
    return combine(values.reshape(rows // 8, 8, columns), axis=0)


def forward_kernel(
    heads,
    block,
    low_ref,
    mid_ref,
    slope_ref,
    start_ref,
    qkv_ref,
    out_ref,
    log_ref,
    values_turned,
    key_stack,
    score_ref,
):
    tokens = qkv_ref.shape[0]
    width = qkv_ref.shape[1] // 3
    head_width = width // heads
    blocks = tokens // block
    query_block = pl.program_id(0)

    @pl.when(query_block == 0)
    def _():
        lanes = lane_masks(block, width, heads)
        for number in range(blocks):
            rows = slice(number * block, (number + 1) * block)
            values_turned[number] = turned(qkv_ref[rows, 2 * width :]).astype(bf16)
            key_stack[number] = head_stack(qkv_ref[rows, width : 2 * width], lanes)

    first_row = pl.multiple_of(query_block * block, block)
    queries = qkv_ref[pl.ds(first_row, block), :width].astype(f32) * head_width ** (-0.5)
    queries = turned(queries).astype(bf16)
    start_row = start_ref[query_block]

    def score_step(key_block, bests, with_mask):
        scores = dot(key_stack[key_block], queries)
        offsets = key_offsets(key_block, query_block, block)
        allowed = allowed_pairs(key_block, query_block, start_row, block) if with_mask else None
        result = []
        for number in range(heads):
            rows = head_rows(number, block)
            part = scores[rows] + slope_ref[number] * offsets
            if with_mask:
                part = jnp.where(allowed, part, masked)
            score_ref[key_block, rows, :] = part
            result.append(jnp.maximum(bests[number], eights(part, jnp.max)))
        return tuple(result)

    low, mid = low_ref[query_block], mid_ref[query_block]
    bests = tuple(jnp.full((8, block), masked, f32) for _ in range(heads))
    bests = lax.fori_loop(low, mid, functools.partial(score_step, with_mask=True), bests)
    bests = lax.fori_loop(mid, query_block, functools.partial(score_step, with_mask=False), bests)
    bests = score_step(query_block, bests, True)
    bests = [jnp.max(best, axis=0, keepdims=True) for best in bests]

    def value_step(key_block, state):
        result = []
        for number in range(heads):
            total, gathered = state[2 * number : 2 * number + 2]
            weights = jnp.exp(score_ref[key_block, head_rows(number, block), :] - bests[number])
            value_rows = values_turned[key_block, head_rows(number, head_width), :]
            result += [
                total + eights(weights, jnp.sum),
                gathered + dot(value_rows, weights.astype(bf16)),
            ]
        return tuple(result)

    state = ()
    for number in range(heads):
        state += (jnp.zeros((8, block), f32), jnp.zeros((head_width, block), f32))
    state = lax.fori_loop(low, query_block + 1, value_step, state)
    columns = []
    for number in range(heads):
        total = jnp.sum(state[2 * number], axis=0, keepdims=True)
        columns.append(state[2 * number + 1] / total)
        log_ref[0, number : number + 1, :] = bests[number] + jnp.log(total)
    out_ref[...] = jnp.transpose(jnp.concatenate(columns, axis=0)).astype(bf16)


def backward_kernel(heads, block, first_head, merge, *refs):
    full_ref, high_ref, slope_ref, start_ref, log_ref, qkv_ref, grad_ref, out_ref = refs[:8]
    earlier_ref = refs[8] if merge else None
    result_ref = refs[9 if merge else 8]
    (
        queries_turned,
        grads_turned,
        keys_turned,
        query_stack,
        grad_stack,
        key_stack,
        value_stack,
        delta_rows,
        query_grads,
    ) = refs[10 if merge else 9 :]
    tokens, all_width = grad_ref.shape
    head_width = all_width // log_ref.shape[1]
    width = heads * head_width
    scale = head_width ** (-0.5)
    blocks = tokens // block
    key_block = pl.program_id(0)
    lanes = lane_masks(block, width, heads)

    def columns(kind):
        start = kind * all_width + first_head * head_width
        return slice(start, start + width)

    def target(kind):
        start = (kind * all_width + first_head * head_width) if merge else kind * width
        return slice(start, start + width)

    @pl.when(key_block == 0)
    def _():
        for number in range(blocks):
            rows = slice(number * block, (number + 1) * block)
            queries = qkv_ref[rows, columns(0)]
            queries_turned[number] = turned(queries.astype(f32) * scale).astype(bf16)
            query_stack[number] = head_stack(queries, lanes)
            keys_turned[number] = turned(qkv_ref[rows, columns(1)]).astype(bf16)
            grads = grad_ref[rows, columns(0)]
            grad_stack[number] = head_stack(grads, lanes)
            grads = grads.astype(f32)
            grads_turned[number] = turned(grads).astype(bf16)
            product = turned(grads * out_ref[rows, columns(0)].astype(f32))
            for head in range(heads):
                delta_rows[number, head : head + 1, :] = jnp.sum(
                    product[head_rows(head, head_width)], axis=0, keepdims=True
                )
            query_grads[number] = jnp.zeros((width, block), f32)

    key_row = pl.multiple_of(key_block * block, block)
    key_stack[...] = head_stack(qkv_ref[pl.ds(key_row, block), columns(1)], lanes)
    value_stack[...] = head_stack(qkv_ref[pl.ds(key_row, block), columns(2)], lanes)

    def step(query_block, state, with_mask):
        key_total, value_total = state
        scores = dot(key_stack[...], queries_turned[query_block])
        grad_weights = dot(value_stack[...], grads_turned[query_block])
        offsets = key_offsets(key_block, query_block, block)
        if with_mask:
            allowed = allowed_pairs(key_block, query_block, start_ref[query_block], block)
        weight_list, grad_list = [], []
        for number in range(heads):
            rows = head_rows(number, block)
            head = first_head + number
            part = scores[rows] + slope_ref[head] * offsets
            part = part - log_ref[query_block, head : head + 1, :]
            if with_mask:
                part = jnp.where(allowed, part, masked)
            probabilities = jnp.exp(part)
            delta = delta_rows[query_block, number : number + 1, :]
            grad_scores = (probabilities * (grad_weights[rows] - delta)).astype(bf16)
            weight_list.append(probabilities.astype(bf16))
            grad_list.append(grad_scores)
            rows = head_rows(number, head_width)
            query_grads[query_block, rows, :] += dot(keys_turned[key_block, rows, :], grad_scores)
        weight_row = jnp.concatenate(weight_list, axis=1)
        grad_row = jnp.concatenate(grad_list, axis=1)
        return (
            key_total + dot(grad_row, query_stack[query_block]),
            value_total + dot(weight_row, grad_stack[query_block]),
        )

    state = (jnp.zeros((block, width), f32), jnp.zeros((block, width), f32))
    state = step(key_block, state, True)
    full, high = full_ref[key_block], high_ref[key_block]
    state = lax.fori_loop(key_block + 1, full, functools.partial(step, with_mask=False), state)
    state = lax.fori_loop(full, high, functools.partial(step, with_mask=True), state)
    result_ref[pl.ds(key_row, block), target(1)] = (state[0] * scale).astype(bf16)
    result_ref[pl.ds(key_row, block), target(2)] = state[1].astype(bf16)
    if merge:
        other = first_head * head_width
        for kind in range(3):
            result_ref[pl.ds(key_row, block), kind * all_width : kind * all_width + other] = earlier_ref[
                pl.ds(key_row, block), kind * other : (kind + 1) * other
            ]

    @pl.when(key_block == blocks - 1)
    def _():
        for number in range(blocks):
            rows = slice(number * block, (number + 1) * block)
            result_ref[rows, target(0)] = jnp.transpose(query_grads[number] * scale).astype(bf16)


def block_plan(lengths, tokens, block):
    ends = jnp.cumsum(lengths)
    positions = jnp.arange(tokens, dtype=jnp.int32)
    passed = positions[:, None] >= ends[None, :]
    starts = jnp.max(jnp.where(passed, ends[None, :], 0), axis=1).astype(jnp.int32)
    finish = jnp.min(jnp.where(passed, tokens, ends[None, :]), axis=1).astype(jnp.int32)
    blocks = tokens // block
    number = jnp.arange(blocks, dtype=jnp.int32)
    first_start = starts[::block]
    last_start = starts[block - 1 :: block]
    low = first_start // block
    mid = jnp.clip((last_start + block - 1) // block, low, number)
    high = (finish[block - 1 :: block] - 1) // block + 1
    full = jnp.clip(finish[::block] // block, number + 1, high)
    return (starts.reshape(blocks, 1, block), low, mid, full, high)


def scalar_spec():
    return pl.BlockSpec(memory_space=pltpu.SMEM)


def whole_spec(shape):
    return pl.BlockSpec(shape, lambda step: (0,) * len(shape), pipeline_mode=pl.Buffered(1))


def attend_forward(qkv, plan, slopes, heads, block):
    tokens, triple = qkv.shape
    width = triple // 3
    blocks = tokens // block
    starts, low, mid, full, high = plan
    return pl.pallas_call(
        functools.partial(forward_kernel, heads, block),
        grid=(blocks,),
        in_specs=[
            scalar_spec(),
            scalar_spec(),
            scalar_spec(),
            whole_spec((blocks, 1, block)),
            whole_spec((tokens, triple)),
        ],
        out_specs=[
            pl.BlockSpec((block, width), lambda step: (step, 0)),
            pl.BlockSpec((1, heads, block), lambda step: (step, 0, 0)),
        ],
        out_shape=[
            jax.ShapeDtypeStruct((tokens, width), bf16),
            jax.ShapeDtypeStruct((blocks, heads, block), f32),
        ],
        scratch_shapes=[
            pltpu.VMEM((blocks, width, block), bf16),
            pltpu.VMEM((blocks, heads * block, width), bf16),
            pltpu.VMEM((blocks, heads * block, block), f32),
        ],
        compiler_params=pltpu.CompilerParams(
            dimension_semantics=("arbitrary",), vmem_limit_bytes=40 * 1024 * 1024
        ),
        cost_estimate=pl.CostEstimate(
            flops=3 * tokens * tokens * 256 * heads,
            bytes_accessed=10 * tokens * width,
            transcendentals=tokens * tokens * heads // 2,
        ),
        name="attend_forward",
    )(low, mid, slopes, starts, qkv)


def attend_backward(qkv, grads, outputs, logs, plan, slopes, heads, block, first_head, earlier):
    tokens, triple = qkv.shape
    all_width = triple // 3
    all_heads = logs.shape[1]
    width = all_width // all_heads * heads
    blocks = tokens // block
    starts, low, mid, full, high = plan
    merge = earlier is not None
    result_width = triple if merge else 3 * width
    operands = [full, high, slopes, starts, logs, qkv, grads, outputs]
    specs = [scalar_spec() for _ in range(3)] + [whole_spec(entry.shape) for entry in operands[3:]]
    if merge:
        operands.append(earlier)
        specs.append(whole_spec(earlier.shape))
    return pl.pallas_call(
        functools.partial(backward_kernel, heads, block, first_head, merge),
        grid=(blocks,),
        in_specs=specs,
        out_specs=pl.BlockSpec((tokens, result_width), lambda step: (0, 0)),
        out_shape=jax.ShapeDtypeStruct((tokens, result_width), bf16),
        scratch_shapes=[
            pltpu.VMEM((blocks, width, block), bf16),
            pltpu.VMEM((blocks, width, block), bf16),
            pltpu.VMEM((blocks, width, block), bf16),
            pltpu.VMEM((blocks, heads * block, width), bf16),
            pltpu.VMEM((blocks, heads * block, width), bf16),
            pltpu.VMEM((heads * block, width), bf16),
            pltpu.VMEM((heads * block, width), bf16),
            pltpu.VMEM((blocks, heads, block), f32),
            pltpu.VMEM((blocks, width, block), f32),
        ],
        compiler_params=pltpu.CompilerParams(
            dimension_semantics=("arbitrary",), vmem_limit_bytes=40 * 1024 * 1024
        ),
        cost_estimate=pl.CostEstimate(
            flops=8 * tokens * tokens * 256 * heads,
            bytes_accessed=20 * tokens * width,
            transcendentals=tokens * tokens * heads // 2,
        ),
        name="attend_backward",
    )(*operands)


def together(*values):
    return lax.optimization_barrier(tuple(values))


def ordered(own, other, bit, axis=0):
    first = jnp.where(bit == 0, own, other)
    second = jnp.where(bit == 0, other, own)
    return jnp.stack([first, second], axis=axis)


class Moves:
    def __init__(self):
        self.shards = lax.axis_size("shard")
        self.reps = lax.axis_size("rep")
        self.half = self.shards // 2
        self.chips = self.reps // 2
        self.shard = lax.axis_index("shard")
        self.rep = lax.axis_index("rep")
        self.core = self.rep % 2
        self.chip = self.rep // 2
        self.side = self.shard // self.half
        self.member = self.shard % self.half + self.core * self.half

    def core_swap(self, part):
        return lax.ppermute(part, "rep", [(r, r ^ 1) for r in range(self.reps)])

    def chip_swap(self, part, bits):
        return lax.ppermute(part, "rep", [(r, r ^ (2 * bits)) for r in range(self.reps)])

    def shard_swap(self, part, bits):
        return lax.ppermute(part, "shard", [(s, s ^ bits) for s in range(self.shards)])

    def shard_bit(self, bits):
        return (self.shard // bits) % 2

    def low_bits(self):
        bits, result = 1, []
        while bits < self.half:
            result.append(bits)
            bits *= 2
        return result

    def home_swap(self, part):
        pairs = []
        for rep in range(self.reps):
            for shard in range(self.shards):
                side, core = shard // self.half, rep % 2
                to_rep, to_shard = rep, shard
                if side != core:
                    to_rep = rep ^ 1
                    to_shard = (shard + self.half) % self.shards
                pairs.append((rep * self.shards + shard, to_rep * self.shards + to_shard))
        return lax.ppermute(part, ("rep", "shard"), pairs)

    def half_gather(self, part):
        stack = part[None]
        for bits in self.low_bits():
            own = stack
            stack = ordered(own, self.shard_swap(own, bits), self.shard_bit(bits))
            stack = stack.reshape((-1,) + part.shape)
        return stack

    def cores_gather(self, stack):
        stack = ordered(stack, self.core_swap(stack), self.core)
        return stack.reshape((-1,) + stack.shape[2:])

    def exchange_bit(self, stack, bit, swap):
        sources, targets = stack.shape[:2]
        stack = stack.reshape((sources, 2, targets // 2) + stack.shape[2:])
        own, other = pick(stack, bit, 1), swap(pick(stack, 1 - bit, 1))
        return ordered(own, other, bit, 1).reshape((2 * sources,) + own.shape[1:])

    def half_exchange(self, stack):
        stack = stack[None]
        for bits in reversed(self.low_bits()):
            swap = functools.partial(self.shard_swap, bits=bits)
            stack = self.exchange_bit(stack, self.shard_bit(bits), swap)
        return stack.reshape((self.half,) + stack.shape[2:])

    def cores_exchange(self, stack):
        return self.exchange_bit(stack[None], self.core, self.core_swap)

    def members_exchange(self, stack):
        for bits in reversed(self.low_bits()):
            swap = functools.partial(self.shard_swap, bits=bits)
            stack = self.exchange_bit(stack, self.shard_bit(bits), swap)
        return stack.reshape((self.shards,) + stack.shape[2:])

    def reduce_bit(self, stack, bit, swap):
        stack = stack.reshape((2, stack.shape[0] // 2) + stack.shape[1:])
        other = swap(pick(stack, 1 - bit).astype(bf16))
        return pick(stack, bit).astype(f32) + other.astype(f32)

    def spread_open(self, part):
        if self.chips == 4:
            return (self.chip_swap(part, 1), self.chip_swap(part, 2))
        held, bits = [part], 1
        while bits < self.chips:
            held = held + [self.chip_swap(piece, bits) for piece in held]
            bits *= 2
        return tuple(held[1:])

    def spread_close(self, state):
        if self.chips == 4:
            by_x, by_y = state
            cut, axis = by_x.shape[-2] // 2, by_x.ndim - 2
            far = [
                self.chip_swap(by_x[..., :cut, :], 2),
                self.chip_swap(by_y[..., cut:, :], 1),
            ]
            return (by_x, by_y, jnp.concatenate(far, axis=axis))
        return state

    def far_open(self, states):
        if self.chips != 4:
            return ()
        cut = states[0][0].shape[0] // 2
        return (
            self.chip_swap(jnp.concatenate([by_x[:cut] for by_x, _ in states], axis=0), 2),
            self.chip_swap(jnp.concatenate([by_y[cut:] for _, by_y in states], axis=0), 1),
        )

    def far_parts(self, states, far):
        if self.chips != 4:
            return [[(k + 1, 0, part) for k, part in enumerate(state)] for state in states]
        cut = states[0][0].shape[0] // 2
        result = []
        for number, (by_x, by_y) in enumerate(states):
            rows = slice(number * cut, (number + 1) * cut)
            result.append([(1, 0, by_x), (2, 0, by_y), (3, 0, far[0][rows]), (3, cut, far[1][rows])])
        return result

    def chips_gather(self, part, axis, state=None):
        shape = part.shape[:axis] + (self.chips,) + part.shape[axis:]
        stack = place(jnp.zeros(shape, part.dtype), part, self.chip, axis)
        others = self.spread_close(self.spread_open(part) if state is None else state)
        for number, piece in enumerate(others):
            stack = place(stack, piece, self.chip ^ (number + 1), axis)
        return stack

    def reduce_open(self, stack, axis):
        if self.chips == 4:
            shape = stack.shape[:axis] + (2, 2) + stack.shape[axis + 1 :]
            stack = stack.reshape(shape)
            bit_x, bit_y = self.chip % 2, self.chip // 2
            cut = shape[0] // 2
            first, second = stack[:cut], stack[cut:]
            got_first = self.chip_swap(pick(first, 1 - bit_x, axis + 1), 1)
            got_second = self.chip_swap(pick(second, 1 - bit_y, axis), 2)
            return (pick(first, bit_x, axis + 1), pick(second, bit_y, axis), got_first, got_second)
        count = self.chips
        stack = stack.astype(f32)
        while count > 1:
            count //= 2
            shape = stack.shape[:axis] + (2, count) + stack.shape[axis + 1 :]
            stack = stack.reshape(shape)
            bit = (self.chip // count) % 2
            got = self.chip_swap(pick(stack, 1 - bit, axis).astype(bf16), count)
            stack = pick(stack, bit, axis) + got.astype(f32)
        return (pick(stack, 0, axis).astype(bf16),)

    def reduce_add(self, state):
        if self.chips != 4:
            return state
        first, second, got_first, got_second = state
        first = (first.astype(f32) + got_first.astype(f32)).astype(bf16)
        second = (second.astype(f32) + got_second.astype(f32)).astype(bf16)
        return (first, second)

    def reduce_send(self, state, axis):
        if self.chips != 4:
            return state
        first, second = state
        bit_x, bit_y = self.chip % 2, self.chip // 2
        got_first = self.chip_swap(pick(first, 1 - bit_y, axis), 2)
        got_second = self.chip_swap(pick(second, 1 - bit_x, axis), 1)
        return (pick(first, bit_y, axis), pick(second, bit_x, axis), got_first, got_second)

    def reduce_final(self, state):
        if self.chips != 4:
            return state[0]
        first, second, got_first, got_second = state
        first = first.astype(f32) + got_first.astype(f32)
        second = second.astype(f32) + got_second.astype(f32)
        return jnp.concatenate([first, second], axis=0).astype(bf16)

    def reduce_close(self, state, axis):
        return self.reduce_final(self.reduce_send(state, axis))

    def core_pair(self, part):
        other = self.core_swap(part)
        first = jnp.where(self.core == 0, part, other)
        second = jnp.where(self.core == 0, other, part)
        return first, second

    def sum_reps(self, vector):
        bits = 1
        while bits < self.reps:
            vector = vector + lax.ppermute(vector, "rep", [(r, r ^ bits) for r in range(self.reps)])
            bits *= 2
        return vector

    def sum_shards(self, vector):
        bits = 1
        while bits < self.shards:
            vector = vector + self.shard_swap(vector, bits)
            bits *= 2
        return vector


def factor_stats(gradient, weight, rows_old, decay_rate):
    square = gradient * gradient
    rows_new = decay_rate * rows_old + (1.0 - decay_rate) * (jnp.mean(square, axis=1) + eps_second)
    col_squares = jnp.sum(square, axis=0, keepdims=True)
    col_scaled = jnp.sum(square / rows_new[:, None], axis=0, keepdims=True)
    scalars = [jnp.sum(rows_new), jnp.sum(weight * weight)]
    scalars = jnp.concatenate([jnp.full((1, 128), scalar, f32) for scalar in scalars], axis=0)
    return rows_new, [jnp.concatenate([col_squares, col_scaled], axis=0), scalars]


def factor_apply(gradient, weight, rows_new, sums, cols_old, height, decay_rate):
    columns, scalars = sums
    breadth = gradient.shape[1]
    row_sum, weight_sum = scalars[0, 0], scalars[1, 0]
    cols_new = decay_rate * cols_old + (1.0 - decay_rate) * (columns[0] / height + eps_second)
    row_mean = row_sum / height
    rms_update = jnp.sqrt(row_mean / (height * breadth) * jnp.sum(columns[1] / cols_new))
    rms_weight = jnp.sqrt(weight_sum / (height * breadth))
    factor = rate_step * rms_weight * jnp.sqrt(row_mean) / jnp.maximum(1.0, rms_update / clip_level)
    new_weight = weight - gradient * (factor * lax.rsqrt(rows_new))[:, None] * lax.rsqrt(cols_new)[None, :]
    return new_weight, cols_new, rms_update


def summed(moves, entries):
    total = moves.sum_shards(jnp.concatenate(entries, axis=1))
    result, offset = [], 0
    for entry in entries:
        result.append(total[:, offset : offset + entry.shape[1]])
        offset += entry.shape[1]
    return result


def on_device(
    tokens,
    cotangent,
    seq_lengths,
    qkv_weight,
    out_weight,
    up_weight,
    down_weight,
    vectors,
    row_state,
    down_rows,
    col_state,
    vector_state,
):
    moves = Moves()
    shards, half, chips, core = moves.shards, moves.half, moves.chips, moves.core
    row_count, width = tokens.shape
    hidden_width = up_weight.shape[1]
    group_rows = row_count * shards
    heads = HEADS // shards
    head_width = width // HEADS
    span = heads * head_width
    member = moves.member
    decay_rate = 1.0 - STEP ** (-0.8)
    head_number = (member * heads + jnp.arange(heads, dtype=jnp.int32)).astype(f32)
    slopes = jnp.exp2(-8.0 * (head_number + 1.0) / HEADS)

    gain_one = vectors[0:width]
    shift_one = vectors[width : 2 * width]
    bias_query = vectors[2 * width : 3 * width]
    bias_value = vectors[3 * width : 4 * width]
    bias_out = vectors[4 * width : 5 * width]
    gain_two = vectors[5 * width : 6 * width]
    shift_two = vectors[6 * width : 7 * width]
    bias_up = vectors[7 * width : 7 * width + hidden_width]
    bias_down = vectors[7 * width + hidden_width :]

    home_tokens = moves.home_swap(tokens)
    other_lengths = moves.core_swap(seq_lengths)
    lengths = jnp.where(moves.side == core, seq_lengths, other_lengths)[0]
    plan = block_plan(lengths, group_rows, BLOCK)
    rows_z = width // shards
    rows_piece = rows_z // chips
    my_rows = lax.dynamic_slice_in_dim(qkv_weight, moves.chip * rows_piece, rows_piece, 0)
    my_rows = my_rows.astype(bf16)
    my_blocks = []
    for number in range(half):
        kinds = []
        for kind in range(3):
            first = kind * width + number * span
            second = first + half * span
            kinds.append(
                jnp.where(
                    core == 0, my_rows[:, first : first + span], my_rows[:, second : second + span]
                )
            )
        my_blocks.append(jnp.concatenate(kinds, axis=1))
    qkv_part = moves.half_exchange(jnp.stack(my_blocks))
    half_cols = hidden_width // (2 * shards)
    up_wide = shards * half_cols
    out_wide = width // 2
    down_piece = half_cols // chips

    def core_half(values):
        parts = []
        for number in range(shards):
            start = 2 * number * half_cols
            first = values[..., start : start + half_cols]
            second = values[..., start + half_cols : start + 2 * half_cols]
            parts.append(jnp.where(core == 0, first, second))
        return jnp.concatenate(parts, axis=-1)

    up_own = core_half(up_weight).astype(bf16).reshape(chips, rows_piece, up_wide)
    out_own = jnp.where(core == 0, out_weight[:, :out_wide], out_weight[:, out_wide:]).astype(bf16)
    out_own = out_own.reshape(chips, rows_piece, out_wide)
    down_own = lax.dynamic_slice_in_dim(down_weight, core * half_cols, half_cols, 0).astype(bf16)
    fold = down_piece // rows_piece
    down_own = down_own.reshape(chips, fold, rows_piece, width)
    my_down = pick(down_own, moves.chip)
    weight_piece = jnp.concatenate(
        [pick(up_own, moves.chip), pick(out_own, moves.chip)] + [my_down[k] for k in range(fold)],
        axis=1,
    )
    near_pieces, bits = [weight_piece], 1
    while bits < half:
        near_pieces = near_pieces + [moves.shard_swap(piece, bits) for piece in near_pieces]
        bits *= 2
    near_pieces = near_pieces[1:]
    home_tokens, qkv_part, near_pieces, weight_piece = together(
        home_tokens, qkv_part, near_pieces, weight_piece
    )
    far_piece = moves.shard_swap(weight_piece, half)
    near_open = [moves.spread_open(piece) for piece in near_pieces]
    qkv_far = moves.shard_swap(qkv_part, half)
    qkv_far, near_open = together(qkv_far, near_open)
    qkv_part = ordered(qkv_part, qkv_far, moves.side).reshape(shards, rows_piece, 3 * span)
    qkv_cols = moves.chips_gather(qkv_part, 1).reshape(width, 3 * span)
    inputs = home_tokens.astype(f32)
    normed_one, inv_std_one = norm_parts(inputs)
    act_one = (normed_one * gain_one + shift_one).astype(bf16)
    act_half = moves.half_gather(act_one)

    act_half, qkv_cols, far_piece = together(act_half, qkv_cols, far_piece)
    act_all = moves.cores_gather(act_half).reshape(group_rows, width)
    far_open = moves.spread_open(far_piece)
    far_pieces, bits = [far_piece], 1
    while bits < half:
        far_pieces = far_pieces + [moves.shard_swap(piece, bits) for piece in far_pieces]
        bits *= 2
    far_pieces = far_pieces[1:]

    bias_q_part = lax.dynamic_slice_in_dim(bias_query, member * span, span)
    bias_v_part = lax.dynamic_slice_in_dim(bias_value, member * span, span)
    qkv_bias = jnp.concatenate([bias_q_part, jnp.zeros_like(bias_q_part), bias_v_part])
    qkv_rows = (dot(act_all, qkv_cols) + qkv_bias).astype(bf16)
    attended_cols, logs = attend_forward(qkv_rows, plan, slopes, heads, BLOCK)
    attended_cols, far_open, far_pieces = together(attended_cols, far_open, far_pieces)
    attended_parts = moves.cores_exchange(attended_cols.reshape(shards, row_count, span))
    attended_parts = moves.members_exchange(attended_parts)
    first_states = near_open + [far_open]
    first_far = moves.far_open(first_states)
    last_states = [moves.spread_open(piece) for piece in far_pieces]
    attended_parts, first_far, last_states, cotangent = together(
        attended_parts, first_far, last_states, cotangent
    )
    last_far = moves.far_open(last_states)
    home_cot = moves.home_swap(cotangent)
    attended = jnp.concatenate([attended_parts[k] for k in range(shards)], axis=1)

    up_all = place(jnp.zeros((shards, chips, rows_piece, up_wide), bf16), up_own, moves.shard)
    out_all = place(jnp.zeros((shards, chips, rows_piece, out_wide), bf16), out_own, moves.shard)
    down_all = place(jnp.zeros((shards, chips, fold, rows_piece, width), bf16), down_own, moves.shard)
    pieces = near_pieces + [far_piece] + far_pieces
    parts_of = moves.far_parts(first_states, first_far) + moves.far_parts(last_states, last_far)
    for number, (piece, parts) in enumerate(zip(pieces, parts_of)):
        plane = moves.shard ^ (number + 1)
        for far, row, rows in [(0, 0, piece)] + parts:
            chip = moves.chip ^ far
            up_all = lax.dynamic_update_slice(
                up_all, rows[None, None, :, :up_wide], (plane, chip, row, 0)
            )
            out_all = lax.dynamic_update_slice(
                out_all, rows[None, None, :, up_wide : up_wide + out_wide], (plane, chip, row, 0)
            )
            start = up_wide + out_wide
            folds = [rows[:, start + k * width : start + (k + 1) * width] for k in range(fold)]
            down_all = lax.dynamic_update_slice(
                down_all, jnp.stack(folds)[None, None], (plane, chip, 0, row, 0)
            )
    up_half = up_all.reshape(width, up_wide)
    down_half = down_all.reshape(up_wide, width)
    out_first, out_second = moves.core_pair(out_all.reshape(width, out_wide))
    out_low = jnp.concatenate([out_first, out_second], axis=1)
    residual = inputs + dot(attended, out_low) + bias_out
    normed_two, inv_std_two = norm_parts(residual)
    act_two = (normed_two * gain_two + shift_two).astype(bf16)

    act_two_other, attended_other, cot_other = together(
        moves.core_swap(act_two), moves.core_swap(attended), moves.core_swap(home_cot)
    )
    cot_pair = jnp.concatenate([home_cot, cot_other], axis=0)
    act_two_pair = jnp.concatenate([act_two, act_two_other], axis=0)
    attended_pair = jnp.concatenate([attended, attended_other], axis=0)
    bias_up_half = core_half(bias_up)
    up_pair = dot(act_two_pair, up_half) + bias_up_half
    hidden_pair = gelu_value(up_pair).astype(bf16)
    slope_pair = gelu_slope(up_pair).astype(bf16)
    down_terms = dot_rows(hidden_pair, cot_pair).astype(bf16)
    down_terms = down_terms.reshape(shards, chips, down_piece, width)
    cot_pair, down_terms = together(cot_pair, down_terms)
    grad_y = home_cot.astype(f32)
    grad_bias_down = jnp.sum(grad_y, axis=0)
    grad_up_pair = (dot_right(cot_pair, down_half) * slope_pair.astype(f32)).astype(bf16)
    grad_bias_up = jnp.sum(grad_up_pair, axis=0, dtype=f32)
    back_other = moves.core_swap(dot_right(grad_up_pair[row_count:], up_half).astype(bf16))
    up_terms = dot_rows(act_two_pair, grad_up_pair).astype(bf16)
    up_terms = up_terms.reshape(shards, chips, rows_piece, up_wide)
    down_state = moves.reduce_open(down_terms, 1)
    back_other, hidden_pair, up_terms, down_state = together(
        back_other, hidden_pair, up_terms, down_state
    )
    up_state = moves.reduce_open(up_terms, 1)
    down_mid = moves.reduce_close(moves.reduce_add(down_state), 1)
    grad_act_two = dot_right(grad_up_pair[:row_count], up_half) + back_other.astype(f32)
    grad_gain_two = jnp.sum(grad_act_two * normed_two, axis=0)
    grad_shift_two = jnp.sum(grad_act_two, axis=0)
    grad_residual = grad_y + norm_back(grad_act_two, normed_two, inv_std_two, gain_two)
    grad_attn = grad_residual.astype(bf16)
    grad_bias_out = jnp.sum(grad_attn, axis=0, dtype=f32)
    to_members = jnp.stack(
        [
            dot_right(grad_attn, out_low[k * span : (k + 1) * span]).astype(bf16)
            for k in range(shards)
        ]
    )
    attn_halves = [grad_attn[:, :out_wide], grad_attn[:, out_wide:]]
    attn_own = jnp.where(core == 0, attn_halves[0], attn_halves[1])
    attn_other = jnp.where(core == 0, attn_halves[1], attn_halves[0])
    grad_heads, attn_other = together(moves.cores_exchange(to_members), moves.core_swap(attn_other))
    attn_pair = jnp.concatenate([attn_own, attn_other], axis=0)
    grad_heads, hidden_pair = together(grad_heads, hidden_pair)
    grad_heads = moves.members_exchange(grad_heads).reshape(group_rows, span)
    down_other = moves.core_swap(dot(hidden_pair[row_count:], down_half).astype(bf16))
    block_out = (
        residual + dot(hidden_pair[:row_count], down_half) + down_other.astype(f32) + bias_down
    ).astype(bf16)

    out_terms = dot_rows(attended_pair, attn_pair).astype(bf16)
    def shards_sum(piece):
        rows = piece.shape[1]
        return lax.psum_scatter(
            piece.reshape(shards * rows, piece.shape[2]), "shard", scatter_dimension=0, tiled=True
        )

    grad_heads, down_mid, out_terms, block_out = together(
        grad_heads, down_mid, out_terms, block_out
    )
    block_out = moves.home_swap(block_out)
    down_owned = shards_sum(down_mid)
    out_state = moves.reduce_open(out_terms.reshape(shards, chips, rows_piece, out_wide), 1)
    attend_args = (plan, slopes)
    parts = 2 if heads % 4 == 0 else 1
    part_heads = heads // parts
    grad_qkv = attend_backward(
        qkv_rows, grad_heads, attended_cols, logs, *attend_args, part_heads, BLOCK, 0, None
    )
    grad_qkv, up_state, out_state = together(grad_qkv, up_state, out_state)
    up_sums, out_sums = moves.reduce_add(up_state), moves.reduce_add(out_state)
    grad_qkv, up_sums, out_sums = together(grad_qkv, up_sums, out_sums)
    up_out_state = [
        jnp.concatenate([up_part, out_part], axis=-1) for up_part, out_part in zip(up_sums, out_sums)
    ]
    if parts == 2:
        grad_qkv = attend_backward(
            qkv_rows, grad_heads, attended_cols, logs, *attend_args, part_heads, BLOCK, part_heads, grad_qkv
        )
    grad_qkv, up_out_state, block_out = together(
        grad_qkv, moves.reduce_send(up_out_state, 1), block_out
    )
    up_out_piece = moves.reduce_final(up_out_state)
    up_out_owned = shards_sum(up_out_piece)

    grad_bias_q_part = jnp.sum(grad_qkv[:, :span], axis=0, dtype=f32)
    grad_bias_v_part = jnp.sum(grad_qkv[:, 2 * span :], axis=0, dtype=f32)

    grad_halves = grad_qkv.reshape(2, half * row_count, 3 * span)
    sent = dot_right(pick(grad_halves, 1 - core), qkv_cols).astype(bf16)
    back = dot_right(pick(grad_halves, core), qkv_cols) + moves.core_swap(sent).astype(f32)
    down_owned, back_sum = together(down_owned, back)
    down_first, down_second = moves.core_pair(
        moves.chips_gather(down_owned, 0).reshape(half_cols, width)
    )
    qkv_terms = dot_rows(act_all, grad_qkv).astype(bf16)
    qkv_terms = qkv_terms.reshape(shards, chips, rows_piece, 3 * span)
    qkv_state = moves.reduce_add(moves.reduce_open(qkv_terms, 1))
    qkv_state, back_sum = together(qkv_state, back_sum)
    qkv_piece = moves.reduce_close(qkv_state, 1)
    back = back_sum.reshape(half, row_count, width)
    for bits in reversed(moves.low_bits()):
        back = moves.reduce_bit(
            back, moves.shard_bit(bits), functools.partial(moves.shard_swap, bits=bits)
        )
    qkv_piece = moves.reduce_bit(
        qkv_piece, moves.side, functools.partial(moves.shard_swap, bits=half)
    )
    qkv_piece = moves.half_exchange(qkv_piece.astype(bf16))
    back, qkv_piece, down_first, down_second, up_out_owned = together(
        back, qkv_piece, down_first, down_second, up_out_owned
    )
    up_out_state = moves.spread_open(up_out_owned)
    down_grad = jnp.concatenate([down_first, down_second], axis=0).astype(f32)
    grad_act_one = back.reshape(row_count, width)
    grad_gain_one = jnp.sum(grad_act_one * normed_one, axis=0)
    grad_shift_one = jnp.sum(grad_act_one, axis=0)
    grad_inputs = grad_residual + norm_back(grad_act_one, normed_one, inv_std_one, gain_one)
    tokens_grad = moves.home_swap(grad_inputs.astype(bf16))
    grad_gain_one, *up_out_state = together(grad_gain_one, *up_out_state)
    up_out_first, up_out_second = moves.core_pair(
        moves.chips_gather(up_out_owned, 0, tuple(up_out_state)).reshape(rows_z, up_wide + out_wide)
    )
    out_grad = jnp.concatenate(
        [up_out_first[:, up_wide:], up_out_second[:, up_wide:]], axis=1
    ).astype(f32)
    up_columns = []
    for number in range(shards):
        part = slice(number * half_cols, (number + 1) * half_cols)
        up_columns += [up_out_first[:, part], up_out_second[:, part]]
    up_grad = jnp.concatenate(up_columns, axis=1).astype(f32)
    qkv_owned = moves.chips_gather(qkv_piece, 1)
    qkv_first, qkv_second = moves.core_pair(qkv_owned.reshape(half, rows_z, 3 * span))
    qkv_columns = []
    for kind in range(3):
        for source in (qkv_first, qkv_second):
            for number in range(half):
                qkv_columns.append(source[number][:, kind * span : (kind + 1) * span])
    qkv_grad = jnp.concatenate(qkv_columns, axis=1).astype(f32)

    stats = [
        factor_stats(qkv_grad, qkv_weight, row_state[0], decay_rate),
        factor_stats(out_grad, out_weight, row_state[1], decay_rate),
        factor_stats(up_grad, up_weight, row_state[2], decay_rate),
        factor_stats(down_grad, down_weight, down_rows, decay_rate),
    ]
    def spread_heads(part):
        return [jnp.where(member == number, part, 0.0) for number in range(shards)]

    bias_up_parts = []
    for number in range(shards):
        part = grad_bias_up[number * half_cols : (number + 1) * half_cols]
        bias_up_parts += [jnp.where(core == 0, part, 0.0), jnp.where(core == 1, part, 0.0)]
    vector_part = moves.sum_reps(
        jnp.concatenate(
            [grad_gain_one, grad_shift_one]
            + spread_heads(grad_bias_q_part)
            + spread_heads(grad_bias_v_part)
            + [grad_bias_out, grad_gain_two, grad_shift_two]
            + bias_up_parts
            + [grad_bias_down]
        )
    )
    early_sums = summed(moves, stats[1][1] + stats[2][1] + stats[3][1])
    vector_rows, tokens_grad = together(vector_part.reshape(2, -1), tokens_grad)
    late_sums = summed(moves, stats[0][1] + [vector_rows])
    sums = [late_sums[0:2], early_sums[0:2], early_sums[2:4], early_sums[4:6]]
    vector_grad = late_sums[2].reshape(-1)
    gradients = [qkv_grad, out_grad, up_grad, down_grad]
    weights = [qkv_weight, out_weight, up_weight, down_weight]
    heights = [width, width, width, hidden_width]
    new_weights, new_cols, rms_values = [], [], []
    offset = 0
    for number in range(4):
        end_col = offset + gradients[number].shape[1]
        new_weight, cols_new, rms_update = factor_apply(
            gradients[number],
            weights[number],
            stats[number][0],
            sums[number],
            col_state[offset:end_col],
            heights[number],
            decay_rate,
        )
        new_weights.append(new_weight)
        new_cols.append(cols_new)
        rms_values.append(rms_update)
        offset = end_col

    vector_state_new = decay_rate * vector_state + (1.0 - decay_rate) * (
        vector_grad * vector_grad + eps_second
    )
    vector_step = vector_grad * lax.rsqrt(vector_state_new)
    vector_rms = jnp.sqrt(jnp.mean(vector_step * vector_step))
    vector_new = vectors - rate_step * jnp.sqrt(
        jnp.mean(vectors * vectors)
    ) * vector_step / jnp.maximum(1.0, vector_rms / clip_level)
    update_rms = jnp.stack(rms_values + [vector_rms])
    return (
        block_out,
        tokens_grad,
        qkv_grad,
        out_grad,
        up_grad,
        down_grad,
        vector_grad,
        new_weights[0],
        new_weights[1],
        new_weights[2],
        new_weights[3],
        vector_new,
        new_weights[0].astype(bf16),
        new_weights[1].astype(bf16),
        new_weights[2].astype(bf16),
        new_weights[3].astype(bf16),
        jnp.stack([stats[0][0], stats[1][0], stats[2][0]]),
        stats[3][0],
        jnp.concatenate(new_cols),
        vector_state_new,
        update_rms,
    )


def solution(mesh):
    in_specs = (
        P(("rep", "shard"), None),
        P(("rep", "shard"), None),
        P("rep", None),
        P("shard", None),
        P("shard", None),
        P("shard", None),
        P("shard", None),
        P(),
        P(None, "shard"),
        P("shard"),
        P(),
        P(),
    )
    out_specs = (
        P(("rep", "shard"), None),
        P(("rep", "shard"), None),
        P("shard", None),
        P("shard", None),
        P("shard", None),
        P("shard", None),
        P(),
        P("shard", None),
        P("shard", None),
        P("shard", None),
        P("shard", None),
        P(),
        P("shard", None),
        P("shard", None),
        P("shard", None),
        P("shard", None),
        P(None, "shard"),
        P("shard"),
        P(),
        P(),
        P(),
    )
    return jax.shard_map(
        on_device, mesh=mesh, in_specs=in_specs, out_specs=out_specs, check_vma=False
    )
```

```python
import functools

import jax
import jax.numpy as jnp
from jax import lax
from jax.experimental import pallas as pl
from jax.experimental.pallas import tpu as pltpu
from jax.sharding import PartitionSpec as P

HEADS = 16
STEP = 10
BLOCK = 256


eps_norm = 1e-05
eps_second = 1e-30
rate_step = 0.5
clip_level = 1.0
masked = -1e30
gelu_root = (2.0 / 3.141592653589793) ** 0.5
gelu_cubic = 0.044715

f32 = jnp.float32
bf16 = jnp.bfloat16


def norm_parts(values):
    average = jnp.mean(values, axis=-1, keepdims=True)
    centred = values - average
    inv_std = lax.rsqrt(jnp.mean(centred * centred, axis=-1, keepdims=True) + eps_norm)
    return (centred * inv_std, inv_std)


def norm_back(grad_out, normed, inv_std, gain_vec):
    grad_normed = grad_out * gain_vec
    inner_mean = jnp.mean(grad_normed * normed, axis=-1, keepdims=True)
    centred = grad_normed - jnp.mean(grad_normed, axis=-1, keepdims=True)
    return (centred - normed * inner_mean) * inv_std


def gelu_value(pre_act):
    curve = jnp.tanh(gelu_root * (pre_act + gelu_cubic * pre_act * pre_act * pre_act))
    return 0.5 * pre_act * (1.0 + curve)


def gelu_slope(pre_act):
    square = pre_act * pre_act
    curve = jnp.tanh(gelu_root * (pre_act + gelu_cubic * square * pre_act))
    inner = gelu_root * (1.0 + 3.0 * gelu_cubic * square)
    return 0.5 * (1.0 + curve) + 0.5 * pre_act * (1.0 - curve * curve) * inner


def dot(left_side, right_side):
    return jnp.dot(left_side, right_side, preferred_element_type=f32)


def dot_right(left_side, right_side):
    return lax.dot_general(
        left_side, right_side, (((1,), (1,)), ((), ())), preferred_element_type=f32
    )


def dot_rows(left_side, right_side):
    return lax.dot_general(
        left_side, right_side, (((0,), (0,)), ((), ())), preferred_element_type=f32
    )


def pick(stack, index, axis=0):
    return lax.dynamic_index_in_dim(stack, index, axis, keepdims=False)


def place(stack, part, index, axis=0):
    return lax.dynamic_update_index_in_dim(stack, part, index, axis)


def head_rows(number, head_width):
    return slice(number * head_width, (number + 1) * head_width)


def lane_masks(block_rows, width, heads):
    lanes = lax.broadcasted_iota(jnp.int32, (block_rows, width), 1)
    head_width = width // heads
    return [
        (lanes >= number * head_width) & (lanes < (number + 1) * head_width)
        for number in range(heads)
    ]


def allowed_pairs(key_block, query_block, start_row, block):
    key_pos = lax.broadcasted_iota(jnp.int32, (block, block), 0) + key_block * block
    query_pos = lax.broadcasted_iota(jnp.int32, (block, block), 1) + query_block * block
    return (key_pos <= query_pos) & (key_pos >= start_row)


def key_offsets(key_block, query_block, block):
    rows = lax.broadcasted_iota(jnp.int32, (block, 1), 0)
    return (rows + (key_block - query_block) * block).astype(f32)


def turned(values):
    return jnp.transpose(values.astype(f32))


def head_stack(values, lanes):
    zero = jnp.zeros(values.shape, values.dtype)
    return jnp.concatenate([jnp.where(lane, values, zero) for lane in lanes], axis=0)


def eights(values, combine):
    rows, columns = values.shape
    return combine(values.reshape(rows // 8, 8, columns), axis=0)


def forward_kernel(
    heads,
    block,
    low_ref,
    mid_ref,
    slope_ref,
    start_ref,
    qkv_ref,
    out_ref,
    log_ref,
    values_turned,
    key_stack,
    score_ref,
):
    tokens = qkv_ref.shape[0]
    width = qkv_ref.shape[1] // 3
    head_width = width // heads
    blocks = tokens // block
    query_block = pl.program_id(0)

    @pl.when(query_block == 0)
    def _():
        lanes = lane_masks(block, width, heads)
        for number in range(blocks):
            rows = slice(number * block, (number + 1) * block)
            values_turned[number] = turned(qkv_ref[rows, 2 * width :]).astype(bf16)
            key_stack[number] = head_stack(qkv_ref[rows, width : 2 * width], lanes)

    first_row = pl.multiple_of(query_block * block, block)
    queries = qkv_ref[pl.ds(first_row, block), :width].astype(f32) * head_width ** (-0.5)
    queries = turned(queries).astype(bf16)
    start_row = start_ref[query_block]

    def score_step(key_block, bests, with_mask):
        scores = dot(key_stack[key_block], queries)
        offsets = key_offsets(key_block, query_block, block)
        allowed = allowed_pairs(key_block, query_block, start_row, block) if with_mask else None
        result = []
        for number in range(heads):
            rows = head_rows(number, block)
            part = scores[rows] + slope_ref[number] * offsets
            if with_mask:
                part = jnp.where(allowed, part, masked)
            score_ref[key_block, rows, :] = part
            result.append(jnp.maximum(bests[number], eights(part, jnp.max)))
        return tuple(result)

    low, mid = low_ref[query_block], mid_ref[query_block]
    bests = tuple(jnp.full((8, block), masked, f32) for _ in range(heads))
    bests = lax.fori_loop(low, mid, functools.partial(score_step, with_mask=True), bests)
    bests = lax.fori_loop(mid, query_block, functools.partial(score_step, with_mask=False), bests)
    bests = score_step(query_block, bests, True)
    bests = [jnp.max(best, axis=0, keepdims=True) for best in bests]

    def value_step(key_block, state):
        result = []
        for number in range(heads):
            total, gathered = state[2 * number : 2 * number + 2]
            weights = jnp.exp(score_ref[key_block, head_rows(number, block), :] - bests[number])
            value_rows = values_turned[key_block, head_rows(number, head_width), :]
            result += [
                total + eights(weights, jnp.sum),
                gathered + dot(value_rows, weights.astype(bf16)),
            ]
        return tuple(result)

    state = ()
    for number in range(heads):
        state += (jnp.zeros((8, block), f32), jnp.zeros((head_width, block), f32))
    state = lax.fori_loop(low, query_block + 1, value_step, state)
    columns = []
    for number in range(heads):
        total = jnp.sum(state[2 * number], axis=0, keepdims=True)
        columns.append(state[2 * number + 1] / total)
        log_ref[0, number : number + 1, :] = bests[number] + jnp.log(total)
    out_ref[...] = jnp.transpose(jnp.concatenate(columns, axis=0)).astype(bf16)


def backward_kernel(heads, block, first_head, merge, *refs):
    full_ref, high_ref, slope_ref, start_ref, log_ref, qkv_ref, grad_ref, out_ref = refs[:8]
    earlier_ref = refs[8] if merge else None
    result_ref = refs[9 if merge else 8]
    (
        queries_turned,
        grads_turned,
        keys_turned,
        query_stack,
        grad_stack,
        key_stack,
        value_stack,
        delta_rows,
        query_grads,
    ) = refs[10 if merge else 9 :]
    tokens, all_width = grad_ref.shape
    head_width = all_width // log_ref.shape[1]
    width = heads * head_width
    scale = head_width ** (-0.5)
    blocks = tokens // block
    key_block = pl.program_id(0)
    lanes = lane_masks(block, width, heads)

    def columns(kind):
        start = kind * all_width + first_head * head_width
        return slice(start, start + width)

    def target(kind):
        start = (kind * all_width + first_head * head_width) if merge else kind * width
        return slice(start, start + width)

    @pl.when(key_block == 0)
    def _():
        for number in range(blocks):
            rows = slice(number * block, (number + 1) * block)
            queries = qkv_ref[rows, columns(0)]
            queries_turned[number] = turned(queries.astype(f32) * scale).astype(bf16)
            query_stack[number] = head_stack(queries, lanes)
            keys_turned[number] = turned(qkv_ref[rows, columns(1)]).astype(bf16)
            grads = grad_ref[rows, columns(0)]
            grad_stack[number] = head_stack(grads, lanes)
            grads = grads.astype(f32)
            grads_turned[number] = turned(grads).astype(bf16)
            product = turned(grads * out_ref[rows, columns(0)].astype(f32))
            for head in range(heads):
                delta_rows[number, head : head + 1, :] = jnp.sum(
                    product[head_rows(head, head_width)], axis=0, keepdims=True
                )
            query_grads[number] = jnp.zeros((width, block), f32)

    key_row = pl.multiple_of(key_block * block, block)
    key_stack[...] = head_stack(qkv_ref[pl.ds(key_row, block), columns(1)], lanes)
    value_stack[...] = head_stack(qkv_ref[pl.ds(key_row, block), columns(2)], lanes)

    def step(query_block, state, with_mask):
        key_total, value_total = state
        scores = dot(key_stack[...], queries_turned[query_block])
        grad_weights = dot(value_stack[...], grads_turned[query_block])
        offsets = key_offsets(key_block, query_block, block)
        if with_mask:
            allowed = allowed_pairs(key_block, query_block, start_ref[query_block], block)
        weight_list, grad_list = [], []
        for number in range(heads):
            rows = head_rows(number, block)
            head = first_head + number
            part = scores[rows] + slope_ref[head] * offsets
            part = part - log_ref[query_block, head : head + 1, :]
            if with_mask:
                part = jnp.where(allowed, part, masked)
            probabilities = jnp.exp(part)
            delta = delta_rows[query_block, number : number + 1, :]
            grad_scores = (probabilities * (grad_weights[rows] - delta)).astype(bf16)
            weight_list.append(probabilities.astype(bf16))
            grad_list.append(grad_scores)
            rows = head_rows(number, head_width)
            query_grads[query_block, rows, :] += dot(keys_turned[key_block, rows, :], grad_scores)
        weight_row = jnp.concatenate(weight_list, axis=1)
        grad_row = jnp.concatenate(grad_list, axis=1)
        return (
            key_total + dot(grad_row, query_stack[query_block]),
            value_total + dot(weight_row, grad_stack[query_block]),
        )

    state = (jnp.zeros((block, width), f32), jnp.zeros((block, width), f32))
    state = step(key_block, state, True)
    full, high = full_ref[key_block], high_ref[key_block]
    state = lax.fori_loop(key_block + 1, full, functools.partial(step, with_mask=False), state)
    state = lax.fori_loop(full, high, functools.partial(step, with_mask=True), state)
    result_ref[pl.ds(key_row, block), target(1)] = (state[0] * scale).astype(bf16)
    result_ref[pl.ds(key_row, block), target(2)] = state[1].astype(bf16)
    if merge:
        other = first_head * head_width
        for kind in range(3):
            result_ref[pl.ds(key_row, block), kind * all_width : kind * all_width + other] = earlier_ref[
                pl.ds(key_row, block), kind * other : (kind + 1) * other
            ]

    @pl.when(key_block == blocks - 1)
    def _():
        for number in range(blocks):
            rows = slice(number * block, (number + 1) * block)
            result_ref[rows, target(0)] = jnp.transpose(query_grads[number] * scale).astype(bf16)


def block_plan(lengths, tokens, block):
    ends = jnp.cumsum(lengths)
    positions = jnp.arange(tokens, dtype=jnp.int32)
    passed = positions[:, None] >= ends[None, :]
    starts = jnp.max(jnp.where(passed, ends[None, :], 0), axis=1).astype(jnp.int32)
    finish = jnp.min(jnp.where(passed, tokens, ends[None, :]), axis=1).astype(jnp.int32)
    blocks = tokens // block
    number = jnp.arange(blocks, dtype=jnp.int32)
    first_start = starts[::block]
    last_start = starts[block - 1 :: block]
    low = first_start // block
    mid = jnp.clip((last_start + block - 1) // block, low, number)
    high = (finish[block - 1 :: block] - 1) // block + 1
    full = jnp.clip(finish[::block] // block, number + 1, high)
    return (starts.reshape(blocks, 1, block), low, mid, full, high)


def scalar_spec():
    return pl.BlockSpec(memory_space=pltpu.SMEM)


def whole_spec(shape):
    return pl.BlockSpec(shape, lambda step: (0,) * len(shape), pipeline_mode=pl.Buffered(1))


def attend_forward(qkv, plan, slopes, heads, block):
    tokens, triple = qkv.shape
    width = triple // 3
    blocks = tokens // block
    starts, low, mid, full, high = plan
    return pl.pallas_call(
        functools.partial(forward_kernel, heads, block),
        grid=(blocks,),
        in_specs=[
            scalar_spec(),
            scalar_spec(),
            scalar_spec(),
            whole_spec((blocks, 1, block)),
            whole_spec((tokens, triple)),
        ],
        out_specs=[
            pl.BlockSpec((block, width), lambda step: (step, 0)),
            pl.BlockSpec((1, heads, block), lambda step: (step, 0, 0)),
        ],
        out_shape=[
            jax.ShapeDtypeStruct((tokens, width), bf16),
            jax.ShapeDtypeStruct((blocks, heads, block), f32),
        ],
        scratch_shapes=[
            pltpu.VMEM((blocks, width, block), bf16),
            pltpu.VMEM((blocks, heads * block, width), bf16),
            pltpu.VMEM((blocks, heads * block, block), f32),
        ],
        compiler_params=pltpu.CompilerParams(
            dimension_semantics=("arbitrary",), vmem_limit_bytes=40 * 1024 * 1024
        ),
        cost_estimate=pl.CostEstimate(
            flops=3 * tokens * tokens * 256 * heads,
            bytes_accessed=10 * tokens * width,
            transcendentals=tokens * tokens * heads // 2,
        ),
        name="attend_forward",
    )(low, mid, slopes, starts, qkv)


def attend_backward(qkv, grads, outputs, logs, plan, slopes, heads, block, first_head, earlier):
    tokens, triple = qkv.shape
    all_width = triple // 3
    all_heads = logs.shape[1]
    width = all_width // all_heads * heads
    blocks = tokens // block
    starts, low, mid, full, high = plan
    merge = earlier is not None
    result_width = triple if merge else 3 * width
    operands = [full, high, slopes, starts, logs, qkv, grads, outputs]
    specs = [scalar_spec() for _ in range(3)] + [whole_spec(entry.shape) for entry in operands[3:]]
    if merge:
        operands.append(earlier)
        specs.append(whole_spec(earlier.shape))
    return pl.pallas_call(
        functools.partial(backward_kernel, heads, block, first_head, merge),
        grid=(blocks,),
        in_specs=specs,
        out_specs=pl.BlockSpec((tokens, result_width), lambda step: (0, 0)),
        out_shape=jax.ShapeDtypeStruct((tokens, result_width), bf16),
        scratch_shapes=[
            pltpu.VMEM((blocks, width, block), bf16),
            pltpu.VMEM((blocks, width, block), bf16),
            pltpu.VMEM((blocks, width, block), bf16),
            pltpu.VMEM((blocks, heads * block, width), bf16),
            pltpu.VMEM((blocks, heads * block, width), bf16),
            pltpu.VMEM((heads * block, width), bf16),
            pltpu.VMEM((heads * block, width), bf16),
            pltpu.VMEM((blocks, heads, block), f32),
            pltpu.VMEM((blocks, width, block), f32),
        ],
        compiler_params=pltpu.CompilerParams(
            dimension_semantics=("arbitrary",), vmem_limit_bytes=40 * 1024 * 1024
        ),
        cost_estimate=pl.CostEstimate(
            flops=8 * tokens * tokens * 256 * heads,
            bytes_accessed=20 * tokens * width,
            transcendentals=tokens * tokens * heads // 2,
        ),
        name="attend_backward",
    )(*operands)


def together(*values):
    return lax.optimization_barrier(tuple(values))


def ordered(own, other, bit, axis=0):
    first = jnp.where(bit == 0, own, other)
    second = jnp.where(bit == 0, other, own)
    return jnp.stack([first, second], axis=axis)


class Moves:
    def __init__(self):
        self.shards = lax.axis_size("shard")
        self.reps = lax.axis_size("rep")
        self.half = self.shards // 2
        self.chips = self.reps // 2
        self.shard = lax.axis_index("shard")
        self.rep = lax.axis_index("rep")
        self.core = self.rep % 2
        self.chip = self.rep // 2
        self.side = self.shard // self.half
        self.member = self.shard % self.half + self.core * self.half

    def core_swap(self, part):
        return lax.ppermute(part, "rep", [(r, r ^ 1) for r in range(self.reps)])

    def chip_swap(self, part, bits):
        return lax.ppermute(part, "rep", [(r, r ^ (2 * bits)) for r in range(self.reps)])

    def shard_swap(self, part, bits):
        return lax.ppermute(part, "shard", [(s, s ^ bits) for s in range(self.shards)])

    def shard_bit(self, bits):
        return (self.shard // bits) % 2

    def low_bits(self):
        bits, result = 1, []
        while bits < self.half:
            result.append(bits)
            bits *= 2
        return result

    def home_swap(self, part):
        pairs = []
        for rep in range(self.reps):
            for shard in range(self.shards):
                side, core = shard // self.half, rep % 2
                to_rep, to_shard = rep, shard
                if side != core:
                    to_rep = rep ^ 1
                    to_shard = (shard + self.half) % self.shards
                pairs.append((rep * self.shards + shard, to_rep * self.shards + to_shard))
        return lax.ppermute(part, ("rep", "shard"), pairs)

    def half_gather(self, part):
        stack = part[None]
        for bits in self.low_bits():
            own = stack
            stack = ordered(own, self.shard_swap(own, bits), self.shard_bit(bits))
            stack = stack.reshape((-1,) + part.shape)
        return stack

    def cores_gather(self, stack):
        stack = ordered(stack, self.core_swap(stack), self.core)
        return stack.reshape((-1,) + stack.shape[2:])

    def exchange_bit(self, stack, bit, swap):
        sources, targets = stack.shape[:2]
        stack = stack.reshape((sources, 2, targets // 2) + stack.shape[2:])
        own, other = pick(stack, bit, 1), swap(pick(stack, 1 - bit, 1))
        return ordered(own, other, bit, 1).reshape((2 * sources,) + own.shape[1:])

    def half_exchange(self, stack):
        stack = stack[None]
        for bits in reversed(self.low_bits()):
            swap = functools.partial(self.shard_swap, bits=bits)
            stack = self.exchange_bit(stack, self.shard_bit(bits), swap)
        return stack.reshape((self.half,) + stack.shape[2:])

    def cores_exchange(self, stack):
        return self.exchange_bit(stack[None], self.core, self.core_swap)

    def members_exchange(self, stack):
        for bits in reversed(self.low_bits()):
            swap = functools.partial(self.shard_swap, bits=bits)
            stack = self.exchange_bit(stack, self.shard_bit(bits), swap)
        return stack.reshape((self.shards,) + stack.shape[2:])

    def reduce_bit(self, stack, bit, swap):
        stack = stack.reshape((2, stack.shape[0] // 2) + stack.shape[1:])
        other = swap(pick(stack, 1 - bit).astype(bf16))
        return pick(stack, bit).astype(f32) + other.astype(f32)

    def spread_open(self, part):
        if self.chips == 4:
            return (self.chip_swap(part, 1), self.chip_swap(part, 2))
        held, bits = [part], 1
        while bits < self.chips:
            held = held + [self.chip_swap(piece, bits) for piece in held]
            bits *= 2
        return tuple(held[1:])

    def spread_close(self, state):
        if self.chips == 4:
            by_x, by_y = state
            cut, axis = by_x.shape[-2] // 2, by_x.ndim - 2
            far = [
                self.chip_swap(by_x[..., :cut, :], 2),
                self.chip_swap(by_y[..., cut:, :], 1),
            ]
            return (by_x, by_y, jnp.concatenate(far, axis=axis))
        return state

    def far_open(self, states):
        if self.chips != 4:
            return ()
        cut = states[0][0].shape[0] // 2
        return (
            self.chip_swap(jnp.concatenate([by_x[:cut] for by_x, _ in states], axis=0), 2),
            self.chip_swap(jnp.concatenate([by_y[cut:] for _, by_y in states], axis=0), 1),
        )

    def far_parts(self, states, far):
        if self.chips != 4:
            return [[(k + 1, 0, part) for k, part in enumerate(state)] for state in states]
        cut = states[0][0].shape[0] // 2
        result = []
        for number, (by_x, by_y) in enumerate(states):
            rows = slice(number * cut, (number + 1) * cut)
            result.append([(1, 0, by_x), (2, 0, by_y), (3, 0, far[0][rows]), (3, cut, far[1][rows])])
        return result

    def chips_gather(self, part, axis, state=None):
        shape = part.shape[:axis] + (self.chips,) + part.shape[axis:]
        stack = place(jnp.zeros(shape, part.dtype), part, self.chip, axis)
        others = self.spread_close(self.spread_open(part) if state is None else state)
        for number, piece in enumerate(others):
            stack = place(stack, piece, self.chip ^ (number + 1), axis)
        return stack

    def reduce_open(self, stack, axis):
        if self.chips == 4:
            shape = stack.shape[:axis] + (2, 2) + stack.shape[axis + 1 :]
            stack = stack.reshape(shape)
            bit_x, bit_y = self.chip % 2, self.chip // 2
            cut = shape[0] // 2
            first, second = stack[:cut], stack[cut:]
            got_first = self.chip_swap(pick(first, 1 - bit_x, axis + 1), 1)
            got_second = self.chip_swap(pick(second, 1 - bit_y, axis), 2)
            return (pick(first, bit_x, axis + 1), pick(second, bit_y, axis), got_first, got_second)
        count = self.chips
        stack = stack.astype(f32)
        while count > 1:
            count //= 2
            shape = stack.shape[:axis] + (2, count) + stack.shape[axis + 1 :]
            stack = stack.reshape(shape)
            bit = (self.chip // count) % 2
            got = self.chip_swap(pick(stack, 1 - bit, axis).astype(bf16), count)
            stack = pick(stack, bit, axis) + got.astype(f32)
        return (pick(stack, 0, axis).astype(bf16),)

    def reduce_add(self, state):
        if self.chips != 4:
            return state
        first, second, got_first, got_second = state
        first = (first.astype(f32) + got_first.astype(f32)).astype(bf16)
        second = (second.astype(f32) + got_second.astype(f32)).astype(bf16)
        return (first, second)

    def reduce_send(self, state, axis):
        if self.chips != 4:
            return state
        first, second = state
        bit_x, bit_y = self.chip % 2, self.chip // 2
        got_first = self.chip_swap(pick(first, 1 - bit_y, axis), 2)
        got_second = self.chip_swap(pick(second, 1 - bit_x, axis), 1)
        return (pick(first, bit_y, axis), pick(second, bit_x, axis), got_first, got_second)

    def reduce_final(self, state):
        if self.chips != 4:
            return state[0]
        first, second, got_first, got_second = state
        first = first.astype(f32) + got_first.astype(f32)
        second = second.astype(f32) + got_second.astype(f32)
        return jnp.concatenate([first, second], axis=0).astype(bf16)

    def reduce_close(self, state, axis):
        return self.reduce_final(self.reduce_send(state, axis))

    def core_pair(self, part):
        other = self.core_swap(part)
        first = jnp.where(self.core == 0, part, other)
        second = jnp.where(self.core == 0, other, part)
        return first, second

    def sum_reps(self, vector):
        bits = 1
        while bits < self.reps:
            vector = vector + lax.ppermute(vector, "rep", [(r, r ^ bits) for r in range(self.reps)])
            bits *= 2
        return vector

    def sum_shards(self, vector):
        bits = 1
        while bits < self.shards:
            vector = vector + self.shard_swap(vector, bits)
            bits *= 2
        return vector


def stats_kernel(decay_rate, gradient_ref, old_ref, rows_ref, lane_rows_ref, sums_ref, total_ref, partial):
    step = pl.program_id(0)
    rows, columns = gradient_ref.shape

    @pl.when(step == 0)
    def _():
        partial[...] = jnp.zeros_like(partial)
        total_ref[...] = jnp.zeros_like(total_ref)

    gradient = gradient_ref[...].astype(f32)
    square = gradient * gradient
    row_mean = jnp.sum(square, axis=1, keepdims=True) / columns
    rows_new = decay_rate * old_ref[...] + (1.0 - decay_rate) * (row_mean + eps_second)
    rows_ref[...] = rows_new
    lane_rows_ref[...] = jnp.transpose(jnp.broadcast_to(rows_new, (rows, 128)))[0:1, :]
    total_ref[...] += jnp.broadcast_to(jnp.sum(rows_new, axis=0, keepdims=True), (1, 128))
    partial[0:8, :] += eights(square, jnp.sum)
    partial[8:16, :] += eights(square * (1.0 / rows_new), jnp.sum)

    @pl.when(step == pl.num_programs(0) - 1)
    def _():
        sums_ref[0:1, :] = jnp.sum(partial[0:8, :], axis=0, keepdims=True)
        sums_ref[1:2, :] = jnp.sum(partial[8:16, :], axis=0, keepdims=True)


def factor_stats(gradient, rows_old, decay_rate):
    height, breadth = gradient.shape
    rows = min(128, height)
    return pl.pallas_call(
        functools.partial(stats_kernel, decay_rate),
        grid=(height // rows,),
        in_specs=[
            pl.BlockSpec((rows, breadth), lambda step: (step, 0)),
            pl.BlockSpec((rows, 1), lambda step: (step, 0)),
        ],
        out_specs=[
            pl.BlockSpec((rows, 1), lambda step: (step, 0)),
            pl.BlockSpec((1, rows), lambda step: (0, step)),
            pl.BlockSpec((2, breadth), lambda step: (0, 0)),
            pl.BlockSpec((1, 128), lambda step: (0, 0)),
        ],
        out_shape=[
            jax.ShapeDtypeStruct((height, 1), f32),
            jax.ShapeDtypeStruct((1, height), f32),
            jax.ShapeDtypeStruct((2, breadth), f32),
            jax.ShapeDtypeStruct((1, 128), f32),
        ],
        scratch_shapes=[pltpu.VMEM((16, breadth), f32)],
        compiler_params=pltpu.CompilerParams(
            dimension_semantics=("arbitrary",), vmem_limit_bytes=32 * 1024 * 1024
        ),
        name="factor_stats",
    )(gradient, rows_old.reshape(height, 1))


def apply_kernel(
    decay_rate,
    height,
    gradient_ref,
    weight_ref,
    rows_ref,
    sums_ref,
    scalar_ref,
    old_ref,
    gradient_out,
    weight_out,
    copy_out,
    cols_out,
    rms_out,
    col_factor,
):
    columns = gradient_ref.shape[1]

    @pl.when(pl.program_id(0) == 0)
    def _():
        cols_new = decay_rate * old_ref[...] + (1.0 - decay_rate) * (
            sums_ref[0:1, :] / height + eps_second
        )
        row_mean = scalar_ref[0:1, 0:1] / height
        weight_mean = scalar_ref[1:2, 0:1] / (height * columns)
        scaled = jnp.sum(sums_ref[1:2, :] / cols_new, axis=1, keepdims=True)
        rms_update = jnp.sqrt(row_mean / (height * columns) * scaled)
        factor = rate_step * jnp.sqrt(weight_mean) * jnp.sqrt(row_mean)
        factor = factor / jnp.maximum(1.0, rms_update / clip_level)
        col_factor[...] = factor * lax.rsqrt(cols_new)
        cols_out[...] = cols_new
        rms_out[...] = jnp.broadcast_to(rms_update, (1, 128))

    gradient = gradient_ref[...].astype(f32)
    new_weight = weight_ref[...] - gradient * lax.rsqrt(rows_ref[...]) * col_factor[...]
    gradient_out[...] = gradient
    weight_out[...] = new_weight
    copy_out[...] = new_weight.astype(bf16)


def factor_apply(gradient, weight, rows_new, sums, scalars, cols_old, height, decay_rate):
    own_height, breadth = gradient.shape
    rows = min(64, own_height)

    def rows_spec():
        return pl.BlockSpec((rows, breadth), lambda step: (step, 0))

    def row_spec(count, wide):
        return pl.BlockSpec((count, wide), lambda step: (0, 0))

    return pl.pallas_call(
        functools.partial(apply_kernel, decay_rate, height),
        grid=(own_height // rows,),
        in_specs=[
            rows_spec(),
            rows_spec(),
            pl.BlockSpec((rows, 1), lambda step: (step, 0)),
            row_spec(2, breadth),
            row_spec(2, 128),
            row_spec(1, breadth),
        ],
        out_specs=[rows_spec(), rows_spec(), rows_spec(), row_spec(1, breadth), row_spec(1, 128)],
        out_shape=[
            jax.ShapeDtypeStruct((own_height, breadth), f32),
            jax.ShapeDtypeStruct((own_height, breadth), f32),
            jax.ShapeDtypeStruct((own_height, breadth), bf16),
            jax.ShapeDtypeStruct((1, breadth), f32),
            jax.ShapeDtypeStruct((1, 128), f32),
        ],
        scratch_shapes=[pltpu.VMEM((1, breadth), f32)],
        compiler_params=pltpu.CompilerParams(
            dimension_semantics=("arbitrary",), vmem_limit_bytes=32 * 1024 * 1024
        ),
        name="factor_apply",
    )(gradient, weight, rows_new, sums, scalars, cols_old)


def summed(moves, entries):
    total = moves.sum_shards(jnp.concatenate(entries, axis=1))
    result, offset = [], 0
    for entry in entries:
        result.append(total[:, offset : offset + entry.shape[1]])
        offset += entry.shape[1]
    return result


def on_device(
    tokens,
    cotangent,
    seq_lengths,
    qkv_weight,
    out_weight,
    up_weight,
    down_weight,
    vectors,
    row_state,
    down_rows,
    col_state,
    vector_state,
):
    moves = Moves()
    shards, half, chips, core = moves.shards, moves.half, moves.chips, moves.core
    row_count, width = tokens.shape
    hidden_width = up_weight.shape[1]
    group_rows = row_count * shards
    heads = HEADS // shards
    head_width = width // HEADS
    span = heads * head_width
    member = moves.member
    decay_rate = 1.0 - STEP ** (-0.8)
    head_number = (member * heads + jnp.arange(heads, dtype=jnp.int32)).astype(f32)
    slopes = jnp.exp2(-8.0 * (head_number + 1.0) / HEADS)

    gain_one = vectors[0:width]
    shift_one = vectors[width : 2 * width]
    bias_query = vectors[2 * width : 3 * width]
    bias_value = vectors[3 * width : 4 * width]
    bias_out = vectors[4 * width : 5 * width]
    gain_two = vectors[5 * width : 6 * width]
    shift_two = vectors[6 * width : 7 * width]
    bias_up = vectors[7 * width : 7 * width + hidden_width]
    bias_down = vectors[7 * width + hidden_width :]

    home_tokens = moves.home_swap(tokens)
    other_lengths = moves.core_swap(seq_lengths)
    lengths = jnp.where(moves.side == core, seq_lengths, other_lengths)[0]
    plan = block_plan(lengths, group_rows, BLOCK)
    rows_z = width // shards
    rows_piece = rows_z // chips
    my_rows = lax.dynamic_slice_in_dim(qkv_weight, moves.chip * rows_piece, rows_piece, 0)
    my_rows = my_rows.astype(bf16)
    my_blocks = []
    for number in range(half):
        kinds = []
        for kind in range(3):
            first = kind * width + number * span
            second = first + half * span
            kinds.append(
                jnp.where(
                    core == 0, my_rows[:, first : first + span], my_rows[:, second : second + span]
                )
            )
        my_blocks.append(jnp.concatenate(kinds, axis=1))
    qkv_part = moves.half_exchange(jnp.stack(my_blocks))
    half_cols = hidden_width // (2 * shards)
    up_wide = shards * half_cols
    out_wide = width // 2
    down_piece = half_cols // chips

    def core_half(values):
        parts = []
        for number in range(shards):
            start = 2 * number * half_cols
            first = values[..., start : start + half_cols]
            second = values[..., start + half_cols : start + 2 * half_cols]
            parts.append(jnp.where(core == 0, first, second))
        return jnp.concatenate(parts, axis=-1)

    up_own = core_half(up_weight).astype(bf16).reshape(chips, rows_piece, up_wide)
    out_piece_rows = rows_z // moves.reps
    out_piece = lax.dynamic_slice_in_dim(out_weight, moves.rep * out_piece_rows, out_piece_rows, 0)
    out_low = lax.all_gather(out_piece.astype(bf16), ("shard", "rep"), axis=0, tiled=True)
    down_own = lax.dynamic_slice_in_dim(down_weight, core * half_cols, half_cols, 0).astype(bf16)
    fold = down_piece // rows_piece
    down_own = down_own.reshape(chips, fold, rows_piece, width)
    my_down = pick(down_own, moves.chip)
    weight_piece = jnp.concatenate(
        [pick(up_own, moves.chip)] + [my_down[k] for k in range(fold)],
        axis=1,
    )
    up_all = place(jnp.zeros((shards, chips, rows_piece, up_wide), bf16), up_own, moves.shard)
    down_all = place(jnp.zeros((shards, chips, fold, rows_piece, width), bf16), down_own, moves.shard)

    def place_parts(up_all, down_all, pieces, parts_of, first_plane):
        for number, parts in enumerate(parts_of):
            plane = moves.shard ^ (number + first_plane)
            entries = [] if pieces is None else [(0, 0, pieces[number])]
            for far, row, rows in entries + list(parts):
                chip = moves.chip ^ far
                up_all = lax.dynamic_update_slice(
                    up_all, rows[None, None, :, :up_wide], (plane, chip, row, 0)
                )
                folds = [
                    rows[:, up_wide + k * width : up_wide + (k + 1) * width] for k in range(fold)
                ]
                down_all = lax.dynamic_update_slice(
                    down_all, jnp.stack(folds)[None, None], (plane, chip, 0, row, 0)
                )
        return up_all, down_all

    near_pieces, bits = [weight_piece], 1
    while bits < half:
        near_pieces = near_pieces + [moves.shard_swap(piece, bits) for piece in near_pieces]
        bits *= 2
    near_pieces = near_pieces[1:]
    home_tokens, qkv_part, near_pieces, weight_piece = together(
        home_tokens, qkv_part, near_pieces, weight_piece
    )
    far_piece = moves.shard_swap(weight_piece, half)
    near_open = [moves.spread_open(piece) for piece in near_pieces]
    qkv_far = moves.shard_swap(qkv_part, half)
    qkv_far, near_open = together(qkv_far, near_open)
    qkv_part = ordered(qkv_part, qkv_far, moves.side).reshape(shards, rows_piece, 3 * span)
    qkv_cols = moves.chips_gather(qkv_part, 1).reshape(width, 3 * span)
    inputs = home_tokens.astype(f32)
    normed_one, inv_std_one = norm_parts(inputs)
    act_one = (normed_one * gain_one + shift_one).astype(bf16)
    act_half = moves.half_gather(act_one)

    act_half, qkv_cols, far_piece, cotangent = together(
        act_half, qkv_cols, far_piece, cotangent
    )
    home_cot = moves.home_swap(cotangent)
    act_all = moves.cores_gather(act_half).reshape(group_rows, width)
    far_open = moves.spread_open(far_piece)
    far_pieces, bits = [far_piece], 1
    while bits < half:
        far_pieces = far_pieces + [moves.shard_swap(piece, bits) for piece in far_pieces]
        bits *= 2
    far_pieces = far_pieces[1:]

    bias_q_part = lax.dynamic_slice_in_dim(bias_query, member * span, span)
    bias_v_part = lax.dynamic_slice_in_dim(bias_value, member * span, span)
    qkv_bias = jnp.concatenate([bias_q_part, jnp.zeros_like(bias_q_part), bias_v_part])
    qkv_rows = (dot(act_all, qkv_cols) + qkv_bias).astype(bf16)
    attended_cols, logs = attend_forward(qkv_rows, plan, slopes, heads, BLOCK)
    attended_cols, far_open, far_pieces, home_cot = together(
        attended_cols, far_open, far_pieces, home_cot
    )
    attended_parts = moves.cores_exchange(attended_cols.reshape(shards, row_count, span))
    attended_parts = moves.members_exchange(attended_parts)
    first_states = near_open + [far_open]
    first_far = moves.far_open(first_states)
    last_states = [moves.spread_open(piece) for piece in far_pieces]
    first_far_parts = moves.far_parts(first_states, first_far)
    up_all, down_all = place_parts(
        up_all, down_all, near_pieces + [far_piece], [[]] * len(first_states), 1
    )
    up_all, down_all = place_parts(up_all, down_all, None, [p[:2] for p in first_far_parts], 1)
    attended_parts, first_far_parts, last_states, up_all, down_all, home_cot = together(
        attended_parts, [p[2:] for p in first_far_parts], last_states, up_all, down_all, home_cot
    )
    last_far = moves.far_open(last_states)
    attended = jnp.concatenate([attended_parts[k] for k in range(shards)], axis=1)

    up_all, down_all = place_parts(up_all, down_all, None, first_far_parts, 1)
    last_parts = moves.far_parts(last_states, last_far)
    up_all, down_all = place_parts(up_all, down_all, far_pieces, last_parts, half + 1)
    up_half = up_all.reshape(width, up_wide)
    down_half = down_all.reshape(up_wide, width)
    residual = inputs + dot(attended, out_low) + bias_out
    normed_two, inv_std_two = norm_parts(residual)
    act_two = (normed_two * gain_two + shift_two).astype(bf16)

    act_two_other, attended_other, cot_other = together(
        moves.core_swap(act_two), moves.core_swap(attended), moves.core_swap(home_cot)
    )
    cot_pair = jnp.concatenate([home_cot, cot_other], axis=0)
    act_two_pair = jnp.concatenate([act_two, act_two_other], axis=0)
    attended_pair = jnp.concatenate([attended, attended_other], axis=0)
    bias_up_half = core_half(bias_up)
    up_pair = dot(act_two_pair, up_half) + bias_up_half
    hidden_pair = gelu_value(up_pair).astype(bf16)
    slope_pair = gelu_slope(up_pair).astype(bf16)
    down_terms = dot_rows(hidden_pair, cot_pair).astype(bf16)
    down_terms = down_terms.reshape(shards, chips, down_piece, width)
    cot_pair, down_terms = together(cot_pair, down_terms)
    grad_y = home_cot.astype(f32)
    grad_bias_down = jnp.sum(grad_y, axis=0)
    grad_up_pair = (dot_right(cot_pair, down_half) * slope_pair.astype(f32)).astype(bf16)
    grad_bias_up = jnp.sum(grad_up_pair, axis=0, dtype=f32)
    back_other = moves.core_swap(dot_right(grad_up_pair[row_count:], up_half).astype(bf16))
    up_terms = dot_rows(act_two_pair, grad_up_pair).astype(bf16)
    up_terms = up_terms.reshape(shards, chips, rows_piece, up_wide)
    down_state = moves.reduce_open(down_terms, 1)
    back_other, hidden_pair, up_terms, down_state = together(
        back_other, hidden_pair, up_terms, down_state
    )
    up_state = moves.reduce_open(up_terms, 1)
    down_mid = moves.reduce_close(moves.reduce_add(down_state), 1)
    grad_act_two = dot_right(grad_up_pair[:row_count], up_half) + back_other.astype(f32)
    grad_gain_two = jnp.sum(grad_act_two * normed_two, axis=0)
    grad_shift_two = jnp.sum(grad_act_two, axis=0)
    grad_residual = grad_y + norm_back(grad_act_two, normed_two, inv_std_two, gain_two)
    grad_attn = grad_residual.astype(bf16)
    grad_bias_out = jnp.sum(grad_attn, axis=0, dtype=f32)
    to_members = jnp.stack(
        [
            dot_right(grad_attn, out_low[k * span : (k + 1) * span]).astype(bf16)
            for k in range(shards)
        ]
    )
    attn_halves = [grad_attn[:, :out_wide], grad_attn[:, out_wide:]]
    attn_own = jnp.where(core == 0, attn_halves[0], attn_halves[1])
    attn_other = jnp.where(core == 0, attn_halves[1], attn_halves[0])
    grad_heads, attn_other = together(moves.cores_exchange(to_members), moves.core_swap(attn_other))
    attn_pair = jnp.concatenate([attn_own, attn_other], axis=0)
    grad_heads, hidden_pair = together(grad_heads, hidden_pair)
    grad_heads = moves.members_exchange(grad_heads).reshape(group_rows, span)
    down_other = moves.core_swap(dot(hidden_pair[row_count:], down_half).astype(bf16))
    block_out = (
        residual + dot(hidden_pair[:row_count], down_half) + down_other.astype(f32) + bias_down
    ).astype(bf16)

    out_terms = dot_rows(attended_pair, attn_pair).astype(bf16)
    def shards_halve(piece, bits):
        piece = piece.reshape((piece.shape[0] // 2, 2) + piece.shape[1:])
        bit = moves.shard_bit(bits)
        return pick(piece, bit, 1), moves.shard_swap(pick(piece, 1 - bit, 1), bits)

    def halved(state):
        own, other = state
        return (own.astype(f32) + other.astype(f32)).astype(bf16)

    def shards_sum(piece):
        rows = piece.shape[1]
        return lax.psum_scatter(
            piece.reshape(shards * rows, piece.shape[2]), "shard", scatter_dimension=0, tiled=True
        )

    grad_heads, down_mid, out_terms, block_out = together(
        grad_heads, down_mid, out_terms, block_out
    )
    block_out = moves.home_swap(block_out)
    down_owned = shards_sum(down_mid)
    out_state = moves.reduce_open(out_terms.reshape(shards, chips, rows_piece, out_wide), 1)
    attend_args = (plan, slopes)
    parts = 2 if heads % 4 == 0 else 1
    part_heads = heads // parts
    grad_qkv = attend_backward(
        qkv_rows, grad_heads, attended_cols, logs, *attend_args, part_heads, BLOCK, 0, None
    )
    grad_qkv, up_state, out_state = together(grad_qkv, up_state, out_state)
    up_sums, out_sums = moves.reduce_add(up_state), moves.reduce_add(out_state)
    grad_qkv, up_sums, out_sums = together(grad_qkv, up_sums, out_sums)
    up_out_state = [
        jnp.concatenate([up_part, out_part], axis=-1) for up_part, out_part in zip(up_sums, out_sums)
    ]
    if parts == 2:
        grad_qkv = attend_backward(
            qkv_rows, grad_heads, attended_cols, logs, *attend_args, part_heads, BLOCK, part_heads, grad_qkv
        )
    grad_qkv, up_out_state, block_out = together(
        grad_qkv, moves.reduce_send(up_out_state, 1), block_out
    )
    up_out_piece = moves.reduce_final(up_out_state)
    up_out_state = shards_halve(up_out_piece, 1)

    grad_bias_q_part = jnp.sum(grad_qkv[:, :span], axis=0, dtype=f32)
    grad_bias_v_part = jnp.sum(grad_qkv[:, 2 * span :], axis=0, dtype=f32)

    grad_halves = grad_qkv.reshape(2, half * row_count, 3 * span)
    sent = dot_right(pick(grad_halves, 1 - core), qkv_cols).astype(bf16)
    sent = moves.core_swap(sent)
    qkv_terms = dot_rows(act_all, grad_qkv).astype(bf16)
    qkv_terms = qkv_terms.reshape(shards, chips, rows_piece, 3 * span)
    qkv_state = moves.reduce_open(qkv_terms, 1)
    back = dot_right(pick(grad_halves, core), qkv_cols) + sent.astype(f32)
    qkv_state, back, up_out_state = together(qkv_state, back, up_out_state)

    back = back.reshape(half, row_count, width)
    low_bits = list(reversed(moves.low_bits()))
    for bits in low_bits[:-1]:
        back = moves.reduce_bit(
            back, moves.shard_bit(bits), functools.partial(moves.shard_swap, bits=bits)
        )
    back = back.reshape((2, -1) + back.shape[1:])
    back_bit = moves.shard_bit(low_bits[-1])
    back_other = moves.shard_swap(pick(back, 1 - back_bit).astype(bf16), low_bits[-1])
    up_out_piece, bits = halved(up_out_state), 2
    while bits < half:
        up_out_piece = halved(shards_halve(up_out_piece, bits))
        bits *= 2
    up_out_state = shards_halve(up_out_piece, half)
    qkv_state = moves.reduce_send(moves.reduce_add(qkv_state), 1)
    qkv_state, up_out_state = together(qkv_state, up_out_state)

    up_out_owned = halved(up_out_state)[0]
    up_out_state = moves.spread_open(up_out_owned)
    qkv_piece = moves.reduce_final(qkv_state)
    qkv_piece = qkv_piece.reshape((2, half) + qkv_piece.shape[1:])
    qkv_own = pick(qkv_piece, moves.side)
    qkv_other = moves.shard_swap(pick(qkv_piece, 1 - moves.side), half)
    back_other, qkv_other, up_out_state = together(back_other, qkv_other, up_out_state)

    qkv_piece = moves.half_exchange(halved((qkv_own, qkv_other)))
    down_state = moves.spread_open(down_owned)
    grad_act_one = pick(back, back_bit) + back_other.astype(f32)
    grad_act_one = grad_act_one.reshape(row_count, width)
    grad_gain_one = jnp.sum(grad_act_one * normed_one, axis=0)
    grad_shift_one = jnp.sum(grad_act_one, axis=0)
    grad_inputs = grad_residual + norm_back(grad_act_one, normed_one, inv_std_one, gain_one)
    grad_inputs, qkv_piece, down_state = together(grad_inputs.astype(bf16), qkv_piece, down_state)
    tokens_grad = moves.home_swap(grad_inputs)
    qkv_owned = moves.chips_gather(qkv_piece, 1)

    up_out_first, up_out_second = moves.core_pair(
        moves.chips_gather(up_out_owned, 0, tuple(up_out_state)).reshape(rows_z, up_wide + out_wide)
    )
    out_grad = jnp.concatenate([up_out_first[:, up_wide:], up_out_second[:, up_wide:]], axis=1)
    up_columns = []
    for number in range(shards):
        part = slice(number * half_cols, (number + 1) * half_cols)
        up_columns += [up_out_first[:, part], up_out_second[:, part]]
    up_grad = jnp.concatenate(up_columns, axis=1)
    down_first, down_second = moves.core_pair(
        moves.chips_gather(down_owned, 0, tuple(down_state)).reshape(half_cols, width)
    )
    down_grad = jnp.concatenate([down_first, down_second], axis=0)
    qkv_first, qkv_second = moves.core_pair(qkv_owned.reshape(half, rows_z, 3 * span))
    qkv_columns = []
    for kind in range(3):
        for source in (qkv_first, qkv_second):
            for number in range(half):
                qkv_columns.append(source[number][:, kind * span : (kind + 1) * span])
    qkv_grad = jnp.concatenate(qkv_columns, axis=1)

    gradients = [qkv_grad, out_grad, up_grad, down_grad]
    weights = [qkv_weight, out_weight, up_weight, down_weight]
    heights = [width, width, width, hidden_width]
    rows_old = [row_state[0], row_state[1], row_state[2], down_rows]
    weight_sums = [jnp.sum(weight * weight) for weight in weights]
    stats = [
        factor_stats(gradient, old, decay_rate) for gradient, old in zip(gradients, rows_old)
    ]

    def to_sum(number):
        weight_sum = jnp.broadcast_to(weight_sums[number], (1, 128))
        return [stats[number][2], jnp.concatenate([stats[number][3], weight_sum], axis=0)]

    def spread_heads(part):
        return [jnp.where(member == number, part, 0.0) for number in range(shards)]

    bias_up_parts = []
    for number in range(shards):
        part = grad_bias_up[number * half_cols : (number + 1) * half_cols]
        bias_up_parts += [jnp.where(core == 0, part, 0.0), jnp.where(core == 1, part, 0.0)]
    vector_part = moves.sum_reps(
        jnp.concatenate(
            [grad_gain_one, grad_shift_one]
            + spread_heads(grad_bias_q_part)
            + spread_heads(grad_bias_v_part)
            + [grad_bias_out, grad_gain_two, grad_shift_two]
            + bias_up_parts
            + [grad_bias_down]
        )
    )
    vector_rows, tokens_grad = together(vector_part.reshape(2, -1), tokens_grad)
    all_sums = summed(moves, to_sum(0) + to_sum(1) + to_sum(2) + to_sum(3) + [vector_rows])
    sums = [all_sums[0:2], all_sums[2:4], all_sums[4:6], all_sums[6:8]]
    vector_grad = all_sums[8].reshape(-1)
    updates = []
    offset = 0
    for number in range(4):
        end_col = offset + gradients[number].shape[1]
        updates.append(
            factor_apply(
                gradients[number],
                weights[number],
                stats[number][0],
                sums[number][0],
                sums[number][1],
                col_state[offset:end_col].reshape(1, -1),
                heights[number],
                decay_rate,
            )
        )
        offset = end_col
    grads_out, new_weights, copies, new_cols, rms_rows = zip(*updates)
    rms_values = [rms[0, 0] for rms in rms_rows]

    vector_state_new = decay_rate * vector_state + (1.0 - decay_rate) * (
        vector_grad * vector_grad + eps_second
    )
    vector_step = vector_grad * lax.rsqrt(vector_state_new)
    vector_rms = jnp.sqrt(jnp.mean(vector_step * vector_step))
    vector_new = vectors - rate_step * jnp.sqrt(
        jnp.mean(vectors * vectors)
    ) * vector_step / jnp.maximum(1.0, vector_rms / clip_level)
    update_rms = jnp.stack(rms_values + [vector_rms])
    return (
        block_out,
        tokens_grad,
        *grads_out,
        vector_grad,
        *new_weights,
        vector_new,
        *copies,
        jnp.concatenate([stats[0][1], stats[1][1], stats[2][1]], axis=0),
        stats[3][1].reshape(-1),
        jnp.concatenate(new_cols, axis=1).reshape(-1),
        vector_state_new,
        update_rms,
    )


def solution(mesh):
    in_specs = (
        P(("rep", "shard"), None),
        P(("rep", "shard"), None),
        P("rep", None),
        P("shard", None),
        P("shard", None),
        P("shard", None),
        P("shard", None),
        P(),
        P(None, "shard"),
        P("shard"),
        P(),
        P(),
    )
    out_specs = (
        P(("rep", "shard"), None),
        P(("rep", "shard"), None),
        P("shard", None),
        P("shard", None),
        P("shard", None),
        P("shard", None),
        P(),
        P("shard", None),
        P("shard", None),
        P("shard", None),
        P("shard", None),
        P(),
        P("shard", None),
        P("shard", None),
        P("shard", None),
        P("shard", None),
        P(None, "shard"),
        P("shard"),
        P(),
        P(),
        P(),
    )
    return jax.shard_map(
        on_device, mesh=mesh, in_specs=in_specs, out_specs=out_specs, check_vma=False
    )
```

```python
import functools

import jax
import jax.numpy as jnp
from jax import lax
from jax.experimental import pallas as pl
from jax.experimental.pallas import tpu as pltpu
from jax.sharding import PartitionSpec as P

HEADS = 16
STEP = 10
BLOCK = 256


eps_norm = 1e-05
eps_second = 1e-30
rate_step = 0.5
clip_level = 1.0
masked = -1e30
gelu_root = (2.0 / 3.141592653589793) ** 0.5
gelu_cubic = 0.044715

f32 = jnp.float32
bf16 = jnp.bfloat16


def norm_parts(values):
    average = jnp.mean(values, axis=-1, keepdims=True)
    centred = values - average
    inv_std = lax.rsqrt(jnp.mean(centred * centred, axis=-1, keepdims=True) + eps_norm)
    return (centred * inv_std, inv_std)


def norm_back(grad_out, normed, inv_std, gain_vec):
    grad_normed = grad_out * gain_vec
    inner_mean = jnp.mean(grad_normed * normed, axis=-1, keepdims=True)
    centred = grad_normed - jnp.mean(grad_normed, axis=-1, keepdims=True)
    return (centred - normed * inner_mean) * inv_std


def gelu_value(pre_act):
    curve = jnp.tanh(gelu_root * (pre_act + gelu_cubic * pre_act * pre_act * pre_act))
    return 0.5 * pre_act * (1.0 + curve)


def gelu_slope(pre_act):
    square = pre_act * pre_act
    curve = jnp.tanh(gelu_root * (pre_act + gelu_cubic * square * pre_act))
    inner = gelu_root * (1.0 + 3.0 * gelu_cubic * square)
    return 0.5 * (1.0 + curve) + 0.5 * pre_act * (1.0 - curve * curve) * inner


def dot(left_side, right_side):
    return jnp.dot(left_side, right_side, preferred_element_type=f32)


def dot_right(left_side, right_side):
    return lax.dot_general(
        left_side, right_side, (((1,), (1,)), ((), ())), preferred_element_type=f32
    )


def dot_rows(left_side, right_side):
    return lax.dot_general(
        left_side, right_side, (((0,), (0,)), ((), ())), preferred_element_type=f32
    )


def pick(stack, index, axis=0):
    return lax.dynamic_index_in_dim(stack, index, axis, keepdims=False)


def place(stack, part, index, axis=0):
    return lax.dynamic_update_index_in_dim(stack, part, index, axis)


def head_rows(number, head_width):
    return slice(number * head_width, (number + 1) * head_width)


def lane_masks(block_rows, width, heads):
    lanes = lax.broadcasted_iota(jnp.int32, (block_rows, width), 1)
    head_width = width // heads
    return [
        (lanes >= number * head_width) & (lanes < (number + 1) * head_width)
        for number in range(heads)
    ]


def allowed_pairs(key_block, query_block, start_row, block):
    key_pos = lax.broadcasted_iota(jnp.int32, (block, block), 0) + key_block * block
    query_pos = lax.broadcasted_iota(jnp.int32, (block, block), 1) + query_block * block
    return (key_pos <= query_pos) & (key_pos >= start_row)


def key_offsets(key_block, query_block, block):
    rows = lax.broadcasted_iota(jnp.int32, (block, 1), 0)
    return (rows + (key_block - query_block) * block).astype(f32)


def turned(values):
    return jnp.transpose(values.astype(f32))


def head_stack(values, lanes):
    zero = jnp.zeros(values.shape, values.dtype)
    return jnp.concatenate([jnp.where(lane, values, zero) for lane in lanes], axis=0)


def eights(values, combine):
    rows, columns = values.shape
    return combine(values.reshape(rows // 8, 8, columns), axis=0)


def forward_kernel(
    heads,
    block,
    low_ref,
    mid_ref,
    slope_ref,
    start_ref,
    qkv_ref,
    out_ref,
    log_ref,
    values_turned,
    key_stack,
    score_ref,
):
    tokens = qkv_ref.shape[0]
    width = qkv_ref.shape[1] // 3
    head_width = width // heads
    blocks = tokens // block
    query_block = pl.program_id(0)

    @pl.when(query_block == 0)
    def _():
        lanes = lane_masks(block, width, heads)
        for number in range(blocks):
            rows = slice(number * block, (number + 1) * block)
            values_turned[number] = turned(qkv_ref[rows, 2 * width :]).astype(bf16)
            key_stack[number] = head_stack(qkv_ref[rows, width : 2 * width], lanes)

    first_row = pl.multiple_of(query_block * block, block)
    queries = qkv_ref[pl.ds(first_row, block), :width].astype(f32) * head_width ** (-0.5)
    queries = turned(queries).astype(bf16)
    start_row = start_ref[query_block]

    def score_step(key_block, bests, with_mask):
        scores = dot(key_stack[key_block], queries)
        offsets = key_offsets(key_block, query_block, block)
        allowed = allowed_pairs(key_block, query_block, start_row, block) if with_mask else None
        result = []
        for number in range(heads):
            rows = head_rows(number, block)
            part = scores[rows] + slope_ref[number] * offsets
            if with_mask:
                part = jnp.where(allowed, part, masked)
            score_ref[key_block, rows, :] = part
            result.append(jnp.maximum(bests[number], eights(part, jnp.max)))
        return tuple(result)

    low, mid = low_ref[query_block], mid_ref[query_block]
    bests = tuple(jnp.full((8, block), masked, f32) for _ in range(heads))
    bests = lax.fori_loop(low, mid, functools.partial(score_step, with_mask=True), bests)
    bests = lax.fori_loop(mid, query_block, functools.partial(score_step, with_mask=False), bests)
    bests = score_step(query_block, bests, True)
    bests = [jnp.max(best, axis=0, keepdims=True) for best in bests]

    def value_step(key_block, state):
        result = []
        for number in range(heads):
            total, gathered = state[2 * number : 2 * number + 2]
            weights = jnp.exp(score_ref[key_block, head_rows(number, block), :] - bests[number])
            value_rows = values_turned[key_block, head_rows(number, head_width), :]
            result += [
                total + eights(weights, jnp.sum),
                gathered + dot(value_rows, weights.astype(bf16)),
            ]
        return tuple(result)

    state = ()
    for number in range(heads):
        state += (jnp.zeros((8, block), f32), jnp.zeros((head_width, block), f32))
    state = lax.fori_loop(low, query_block + 1, value_step, state)
    columns = []
    for number in range(heads):
        total = jnp.sum(state[2 * number], axis=0, keepdims=True)
        columns.append(state[2 * number + 1] / total)
        log_ref[0, number : number + 1, :] = bests[number] + jnp.log(total)
    out_ref[...] = jnp.transpose(jnp.concatenate(columns, axis=0)).astype(bf16)


def backward_kernel(heads, block, first_head, merge, *refs):
    full_ref, high_ref, slope_ref, start_ref, log_ref, qkv_ref, grad_ref, out_ref = refs[:8]
    earlier_ref = refs[8] if merge else None
    result_ref = refs[9 if merge else 8]
    (
        queries_turned,
        grads_turned,
        keys_turned,
        query_stack,
        grad_stack,
        key_stack,
        value_stack,
        delta_rows,
        query_grads,
    ) = refs[10 if merge else 9 :]
    tokens, all_width = grad_ref.shape
    head_width = all_width // log_ref.shape[1]
    width = heads * head_width
    scale = head_width ** (-0.5)
    blocks = tokens // block
    key_block = pl.program_id(0)
    lanes = lane_masks(block, width, heads)

    def columns(kind):
        start = kind * all_width + first_head * head_width
        return slice(start, start + width)

    def target(kind):
        start = (kind * all_width + first_head * head_width) if merge else kind * width
        return slice(start, start + width)

    @pl.when(key_block == 0)
    def _():
        for number in range(blocks):
            rows = slice(number * block, (number + 1) * block)
            queries = qkv_ref[rows, columns(0)]
            queries_turned[number] = turned(queries.astype(f32) * scale).astype(bf16)
            query_stack[number] = head_stack(queries, lanes)
            keys_turned[number] = turned(qkv_ref[rows, columns(1)]).astype(bf16)
            grads = grad_ref[rows, columns(0)]
            grad_stack[number] = head_stack(grads, lanes)
            grads = grads.astype(f32)
            grads_turned[number] = turned(grads).astype(bf16)
            product = turned(grads * out_ref[rows, columns(0)].astype(f32))
            for head in range(heads):
                delta_rows[number, head : head + 1, :] = jnp.sum(
                    product[head_rows(head, head_width)], axis=0, keepdims=True
                )
            query_grads[number] = jnp.zeros((width, block), f32)

    key_row = pl.multiple_of(key_block * block, block)
    key_stack[...] = head_stack(qkv_ref[pl.ds(key_row, block), columns(1)], lanes)
    value_stack[...] = head_stack(qkv_ref[pl.ds(key_row, block), columns(2)], lanes)

    def step(query_block, state, with_mask):
        key_total, value_total = state
        scores = dot(key_stack[...], queries_turned[query_block])
        grad_weights = dot(value_stack[...], grads_turned[query_block])
        offsets = key_offsets(key_block, query_block, block)
        if with_mask:
            allowed = allowed_pairs(key_block, query_block, start_ref[query_block], block)
        weight_list, grad_list = [], []
        for number in range(heads):
            rows = head_rows(number, block)
            head = first_head + number
            part = scores[rows] + slope_ref[head] * offsets
            part = part - log_ref[query_block, head : head + 1, :]
            if with_mask:
                part = jnp.where(allowed, part, masked)
            probabilities = jnp.exp(part)
            delta = delta_rows[query_block, number : number + 1, :]
            grad_scores = (probabilities * (grad_weights[rows] - delta)).astype(bf16)
            weight_list.append(probabilities.astype(bf16))
            grad_list.append(grad_scores)
            rows = head_rows(number, head_width)
            query_grads[query_block, rows, :] += dot(keys_turned[key_block, rows, :], grad_scores)
        weight_row = jnp.concatenate(weight_list, axis=1)
        grad_row = jnp.concatenate(grad_list, axis=1)
        return (
            key_total + dot(grad_row, query_stack[query_block]),
            value_total + dot(weight_row, grad_stack[query_block]),
        )

    state = (jnp.zeros((block, width), f32), jnp.zeros((block, width), f32))
    state = step(key_block, state, True)
    full, high = full_ref[key_block], high_ref[key_block]
    state = lax.fori_loop(key_block + 1, full, functools.partial(step, with_mask=False), state)
    state = lax.fori_loop(full, high, functools.partial(step, with_mask=True), state)
    result_ref[pl.ds(key_row, block), target(1)] = (state[0] * scale).astype(bf16)
    result_ref[pl.ds(key_row, block), target(2)] = state[1].astype(bf16)
    if merge:
        other = first_head * head_width
        for kind in range(3):
            result_ref[pl.ds(key_row, block), kind * all_width : kind * all_width + other] = earlier_ref[
                pl.ds(key_row, block), kind * other : (kind + 1) * other
            ]

    @pl.when(key_block == blocks - 1)
    def _():
        for number in range(blocks):
            rows = slice(number * block, (number + 1) * block)
            result_ref[rows, target(0)] = jnp.transpose(query_grads[number] * scale).astype(bf16)


def block_plan(lengths, tokens, block):
    ends = jnp.cumsum(lengths)
    positions = jnp.arange(tokens, dtype=jnp.int32)
    passed = positions[:, None] >= ends[None, :]
    starts = jnp.max(jnp.where(passed, ends[None, :], 0), axis=1).astype(jnp.int32)
    finish = jnp.min(jnp.where(passed, tokens, ends[None, :]), axis=1).astype(jnp.int32)
    blocks = tokens // block
    number = jnp.arange(blocks, dtype=jnp.int32)
    first_start = starts[::block]
    last_start = starts[block - 1 :: block]
    low = first_start // block
    mid = jnp.clip((last_start + block - 1) // block, low, number)
    high = (finish[block - 1 :: block] - 1) // block + 1
    full = jnp.clip(finish[::block] // block, number + 1, high)
    return (starts.reshape(blocks, 1, block), low, mid, full, high)


def scalar_spec():
    return pl.BlockSpec(memory_space=pltpu.SMEM)


def whole_spec(shape):
    return pl.BlockSpec(shape, lambda step: (0,) * len(shape), pipeline_mode=pl.Buffered(1))


def attend_forward(qkv, plan, slopes, heads, block):
    tokens, triple = qkv.shape
    width = triple // 3
    blocks = tokens // block
    starts, low, mid, full, high = plan
    return pl.pallas_call(
        functools.partial(forward_kernel, heads, block),
        grid=(blocks,),
        in_specs=[
            scalar_spec(),
            scalar_spec(),
            scalar_spec(),
            whole_spec((blocks, 1, block)),
            whole_spec((tokens, triple)),
        ],
        out_specs=[
            pl.BlockSpec((block, width), lambda step: (step, 0)),
            pl.BlockSpec((1, heads, block), lambda step: (step, 0, 0)),
        ],
        out_shape=[
            jax.ShapeDtypeStruct((tokens, width), bf16),
            jax.ShapeDtypeStruct((blocks, heads, block), f32),
        ],
        scratch_shapes=[
            pltpu.VMEM((blocks, width, block), bf16),
            pltpu.VMEM((blocks, heads * block, width), bf16),
            pltpu.VMEM((blocks, heads * block, block), f32),
        ],
        compiler_params=pltpu.CompilerParams(
            dimension_semantics=("arbitrary",), vmem_limit_bytes=40 * 1024 * 1024
        ),
        cost_estimate=pl.CostEstimate(
            flops=3 * tokens * tokens * 256 * heads,
            bytes_accessed=10 * tokens * width,
            transcendentals=tokens * tokens * heads // 2,
        ),
        name="attend_forward",
    )(low, mid, slopes, starts, qkv)


def attend_backward(qkv, grads, outputs, logs, plan, slopes, heads, block, first_head, earlier):
    tokens, triple = qkv.shape
    all_width = triple // 3
    all_heads = logs.shape[1]
    width = all_width // all_heads * heads
    blocks = tokens // block
    starts, low, mid, full, high = plan
    merge = earlier is not None
    result_width = triple if merge else 3 * width
    operands = [full, high, slopes, starts, logs, qkv, grads, outputs]
    specs = [scalar_spec() for _ in range(3)] + [whole_spec(entry.shape) for entry in operands[3:]]
    if merge:
        operands.append(earlier)
        specs.append(whole_spec(earlier.shape))
    return pl.pallas_call(
        functools.partial(backward_kernel, heads, block, first_head, merge),
        grid=(blocks,),
        in_specs=specs,
        out_specs=pl.BlockSpec((tokens, result_width), lambda step: (0, 0)),
        out_shape=jax.ShapeDtypeStruct((tokens, result_width), bf16),
        scratch_shapes=[
            pltpu.VMEM((blocks, width, block), bf16),
            pltpu.VMEM((blocks, width, block), bf16),
            pltpu.VMEM((blocks, width, block), bf16),
            pltpu.VMEM((blocks, heads * block, width), bf16),
            pltpu.VMEM((blocks, heads * block, width), bf16),
            pltpu.VMEM((heads * block, width), bf16),
            pltpu.VMEM((heads * block, width), bf16),
            pltpu.VMEM((blocks, heads, block), f32),
            pltpu.VMEM((blocks, width, block), f32),
        ],
        compiler_params=pltpu.CompilerParams(
            dimension_semantics=("arbitrary",), vmem_limit_bytes=40 * 1024 * 1024
        ),
        cost_estimate=pl.CostEstimate(
            flops=8 * tokens * tokens * 256 * heads,
            bytes_accessed=20 * tokens * width,
            transcendentals=tokens * tokens * heads // 2,
        ),
        name="attend_backward",
    )(*operands)


class Gathered:
    def __init__(self, arrays, sources, place, sizes):
        self.arrays, self.sources, self.place = arrays, sources, place
        self.rows_z, self.rows_piece, self.up_wide, self.width, self.fold, self.half_cols = sizes

    def parts(self, kind):
        result = []
        for source in self.sources:
            place = source[5]
            if kind == "up":
                result.append((source, (0, self.up_wide), self.rows_z, self.rows_piece, place))
            elif kind == "out":
                columns = (self.up_wide, self.width)
                result.append((source, columns, self.rows_z, self.rows_piece, place))
            else:
                for number in range(self.fold):
                    columns = (self.up_wide + (1 + number) * self.width, self.width)
                    chip_rows = self.rows_piece * self.fold
                    start = place + number * self.rows_piece
                    result.append((source, columns, self.half_cols, chip_rows, start))
        return result

    def shape(self, kind):
        planes = self.width // self.rows_z
        if kind == "down":
            return (planes * self.half_cols, self.width)
        return (self.width, self.up_wide if kind == "up" else self.width)

    def call(self, body, kind, own, operands, outputs, grid, scratch=(), name=None):
        parts = self.parts(kind)
        plane_rows = own.shape[0]
        count = len(self.arrays)

        def kernel(place_ref, own_ref, *refs):
            piece_refs = refs[:count]
            operand_refs = refs[count : count + len(operands)]
            rest = refs[count + len(operands) :]
            output_refs, (weight_ref, semaphores, *extra) = rest[: len(outputs)], rest[len(outputs) :]

            @pl.when(pl.program_id(0) == 0)
            def _():
                shard, chip = place_ref[0], place_ref[1]
                first = pl.multiple_of(shard * plane_rows, plane_rows)
                target = weight_ref.at[pl.ds(first, plane_rows), :]
                copies = [pltpu.make_async_copy(own_ref, target, semaphores.at[0])]
                for number, (source, columns, rows_plane, rows_chip, start) in enumerate(parts):
                    array, row, rows, plane, far, _ = source
                    first = (shard ^ plane) * rows_plane + (chip ^ far) * rows_chip + start
                    target = weight_ref.at[pl.ds(pl.multiple_of(first, 16), rows), :]
                    block = piece_refs[array].at[pl.ds(row, rows), pl.ds(*columns)]
                    copies.append(pltpu.make_async_copy(block, target, semaphores.at[number + 1]))
                for copy in copies:
                    copy.start()
                for copy in copies:
                    copy.wait()

            body(operand_refs, output_refs, weight_ref, extra)

        anywhere = pl.BlockSpec(memory_space=pl.ANY)
        return pl.pallas_call(
            kernel,
            grid=grid,
            in_specs=[scalar_spec()] + [anywhere] * (1 + count) + [spec for _, spec in operands],
            out_specs=[spec for _, _, spec in outputs],
            out_shape=[jax.ShapeDtypeStruct(shape, kind_of) for shape, kind_of, _ in outputs],
            scratch_shapes=[
                pltpu.VMEM(self.shape(kind), bf16),
                pltpu.SemaphoreType.DMA((len(parts) + 1,)),
                *scratch,
            ],
            compiler_params=pltpu.CompilerParams(
                dimension_semantics=("arbitrary",), vmem_limit_bytes=40 * 1024 * 1024
            ),
            cost_estimate=pl.CostEstimate(flops=1, bytes_accessed=1, transcendentals=0),
            name=name,
        )(self.place, own, *self.arrays, *[operand for operand, _ in operands])


def block_spec(shape, place):
    return pl.BlockSpec(shape, place)


def out_projection(gathered, own, attended, inputs, bias, gain, shift):
    rows, width = attended.shape
    tile = rows // 2

    def body(operands, outputs, weight, extra):
        attended_ref, inputs_ref, bias_ref, gain_ref, shift_ref = operands
        residual = inputs_ref[...] + dot(attended_ref[...], weight[...]) + bias_ref[...]
        normed, inv_std = norm_parts(residual)
        outputs[0][...] = residual
        outputs[1][...] = normed
        outputs[2][...] = inv_std
        outputs[3][...] = (normed * gain_ref[...] + shift_ref[...]).astype(bf16)

    by_rows = block_spec((tile, width), lambda step: (step, 0))
    return gathered.call(
        body,
        "out",
        own,
        [(attended, by_rows), (inputs, by_rows)]
        + [(vector.reshape(1, width), whole_spec((1, width))) for vector in (bias, gain, shift)],
        [
            ((rows, width), f32, by_rows),
            ((rows, width), f32, by_rows),
            ((rows, 1), f32, block_spec((tile, 1), lambda step: (step, 0))),
            ((rows, width), bf16, by_rows),
        ],
        (2,),
        name="out_projection",
    )


def out_backward(gathered, own, grads, span):
    rows, width = grads.shape
    members = width // span

    def body(operands, outputs, weight, extra):
        first = pl.multiple_of(pl.program_id(0) * span, span)
        block = weight[pl.ds(first, span), :]
        outputs[0][0] = dot_right(operands[0][...], block).astype(bf16)

    return gathered.call(
        body,
        "out",
        own,
        [(grads, whole_spec((rows, width)))],
        [((members, rows, span), bf16, block_spec((1, rows, span), lambda step: (step, 0, 0)))],
        (members,),
        name="out_backward",
    )[0]


def up_projection(gathered, own, act_own, act_other, bias):
    rows, width = act_own.shape
    breadth = own.shape[1]
    tile = min(512, breadth)

    def body(operands, outputs, weight, extra):
        first = pl.multiple_of(pl.program_id(0) * tile, tile)
        block = weight[:, pl.ds(first, tile)]
        for number in range(2):
            pre_act = dot(operands[number][...], block) + operands[2][...]
            square = pre_act * pre_act
            curve = jnp.tanh(pre_act * (gelu_root + gelu_root * gelu_cubic * square))
            inner = pre_act * (gelu_root + 3.0 * gelu_root * gelu_cubic * square)
            share = 0.5 + 0.5 * curve
            outputs[0][number * rows : (number + 1) * rows, :] = (pre_act * share).astype(bf16)
            slope = share + (0.5 * inner) * (1.0 - curve * curve)
            outputs[1][number * rows : (number + 1) * rows, :] = slope.astype(bf16)

    by_columns = block_spec((2 * rows, tile), lambda step: (0, step))
    return gathered.call(
        body,
        "up",
        own,
        [
            (act_own, whole_spec((rows, width))),
            (act_other, whole_spec((rows, width))),
            (bias.reshape(1, breadth), block_spec((1, tile), lambda step: (0, step))),
        ],
        [((2 * rows, breadth), bf16, by_columns), ((2 * rows, breadth), bf16, by_columns)],
        (breadth // tile,),
        name="up_projection",
    )


def hidden_backward(gathered, own, cot_own, cot_other, slopes):
    rows, width = cot_own.shape
    breadth = slopes.shape[1]
    tile = min(512, breadth)

    def body(operands, outputs, weight, extra):
        first = pl.multiple_of(pl.program_id(0) * tile, tile)
        block = weight[pl.ds(first, tile), :]
        total = jnp.zeros((1, tile), f32)
        for number in range(2):
            part = slice(number * rows, (number + 1) * rows)
            grads = dot_right(operands[number][...], block) * operands[2][part, :].astype(f32)
            grads = grads.astype(bf16)
            outputs[0][part, :] = grads
            total = total + jnp.sum(grads.astype(f32), axis=0, keepdims=True)
        outputs[1][...] = total

    by_columns = block_spec((2 * rows, tile), lambda step: (0, step))
    return gathered.call(
        body,
        "down",
        own,
        [
            (cot_own, whole_spec((rows, width))),
            (cot_other, whole_spec((rows, width))),
            (slopes, by_columns),
        ],
        [
            ((2 * rows, breadth), bf16, by_columns),
            ((1, breadth), f32, block_spec((1, tile), lambda step: (0, step))),
        ],
        (breadth // tile,),
        name="hidden_backward",
    )


def up_backward(gathered, own, grads, number, kind_of):
    rows, breadth = grads.shape[0] // 2, grads.shape[1]
    width = gathered.width
    tile = width // 2

    def body(operands, outputs, weight, extra):
        first = pl.multiple_of(pl.program_id(0) * tile, tile)
        block = weight[pl.ds(first, tile), :]
        outputs[0][...] = dot_right(operands[0][...], block).astype(kind_of)

    return gathered.call(
        body,
        "up",
        own,
        [(grads, block_spec((rows, breadth), lambda step: (number, 0)))],
        [((rows, width), kind_of, block_spec((rows, tile), lambda step: (0, step)))],
        (2,),
        name="up_backward",
    )[0]


def down_projection(gathered, own, hidden):
    rows, breadth = hidden.shape
    width = gathered.width
    tile = min(256, rows)

    def body(operands, outputs, weight, extra):
        outputs[0][...] = dot(operands[0][...], weight[...]).astype(bf16)

    return gathered.call(
        body,
        "down",
        own,
        [(hidden, block_spec((tile, breadth), lambda step: (step, 0)))],
        [((rows, width), bf16, block_spec((tile, width), lambda step: (step, 0)))],
        (rows // tile,),
        name="down_projection",
    )[0]


def up_gradient_kernel(own_ref, other_ref, grads_ref, result_ref, act_turned):
    rows, width = own_ref.shape
    step = 256

    @pl.when(pl.program_id(0) == 0)
    def _():
        for number, ref in enumerate((own_ref, other_ref)):
            for row in range(0, rows, step):
                first = number * rows + row
                for column in range(0, width, step):
                    block = ref[row : row + step, column : column + step]
                    act_turned[column : column + step, first : first + step] = turned(block).astype(bf16)

    result_ref[...] = dot(act_turned[...], grads_ref[...]).astype(bf16)


def up_gradient(act_own, act_other, grads):
    rows, width = act_own.shape
    breadth = grads.shape[1]
    tile = min(512, breadth)
    return pl.pallas_call(
        up_gradient_kernel,
        grid=(breadth // tile,),
        in_specs=[
            whole_spec((rows, width)),
            whole_spec((rows, width)),
            pl.BlockSpec((2 * rows, tile), lambda step: (0, step)),
        ],
        out_specs=pl.BlockSpec((width, tile), lambda step: (0, step)),
        out_shape=jax.ShapeDtypeStruct((width, breadth), bf16),
        scratch_shapes=[pltpu.VMEM((width, 2 * rows), bf16)],
        compiler_params=pltpu.CompilerParams(
            dimension_semantics=("arbitrary",), vmem_limit_bytes=40 * 1024 * 1024
        ),
        cost_estimate=pl.CostEstimate(flops=1, bytes_accessed=1, transcendentals=0),
        name="up_gradient",
    )(act_own, act_other, grads)


def together(*values):
    return lax.optimization_barrier(tuple(values))


def ordered(own, other, bit, axis=0):
    first = jnp.where(bit == 0, own, other)
    second = jnp.where(bit == 0, other, own)
    return jnp.stack([first, second], axis=axis)


class Moves:
    def __init__(self):
        self.shards = lax.axis_size("shard")
        self.reps = lax.axis_size("rep")
        self.half = self.shards // 2
        self.chips = self.reps // 2
        self.shard = lax.axis_index("shard")
        self.rep = lax.axis_index("rep")
        self.core = self.rep % 2
        self.chip = self.rep // 2
        self.side = self.shard // self.half
        self.member = self.shard % self.half + self.core * self.half

    def core_swap(self, part):
        return lax.ppermute(part, "rep", [(r, r ^ 1) for r in range(self.reps)])

    def chip_swap(self, part, bits):
        return lax.ppermute(part, "rep", [(r, r ^ (2 * bits)) for r in range(self.reps)])

    def shard_swap(self, part, bits):
        return lax.ppermute(part, "shard", [(s, s ^ bits) for s in range(self.shards)])

    def shard_bit(self, bits):
        return (self.shard // bits) % 2

    def low_bits(self):
        bits, result = 1, []
        while bits < self.half:
            result.append(bits)
            bits *= 2
        return result

    def home_swap(self, part):
        pairs = []
        for rep in range(self.reps):
            for shard in range(self.shards):
                side, core = shard // self.half, rep % 2
                to_rep, to_shard = rep, shard
                if side != core:
                    to_rep = rep ^ 1
                    to_shard = (shard + self.half) % self.shards
                pairs.append((rep * self.shards + shard, to_rep * self.shards + to_shard))
        return lax.ppermute(part, ("rep", "shard"), pairs)

    def half_gather(self, part):
        stack = part[None]
        for bits in self.low_bits():
            own = stack
            stack = ordered(own, self.shard_swap(own, bits), self.shard_bit(bits))
            stack = stack.reshape((-1,) + part.shape)
        return stack

    def cores_gather(self, stack):
        stack = ordered(stack, self.core_swap(stack), self.core)
        return stack.reshape((-1,) + stack.shape[2:])

    def exchange_bit(self, stack, bit, swap):
        sources, targets = stack.shape[:2]
        stack = stack.reshape((sources, 2, targets // 2) + stack.shape[2:])
        own, other = pick(stack, bit, 1), swap(pick(stack, 1 - bit, 1))
        return ordered(own, other, bit, 1).reshape((2 * sources,) + own.shape[1:])

    def half_exchange(self, stack):
        stack = stack[None]
        for bits in reversed(self.low_bits()):
            swap = functools.partial(self.shard_swap, bits=bits)
            stack = self.exchange_bit(stack, self.shard_bit(bits), swap)
        return stack.reshape((self.half,) + stack.shape[2:])

    def cores_exchange(self, stack):
        return self.exchange_bit(stack[None], self.core, self.core_swap)

    def members_exchange(self, stack):
        for bits in reversed(self.low_bits()):
            swap = functools.partial(self.shard_swap, bits=bits)
            stack = self.exchange_bit(stack, self.shard_bit(bits), swap)
        return stack.reshape((self.shards,) + stack.shape[2:])

    def reduce_bit(self, stack, bit, swap):
        stack = stack.reshape((2, stack.shape[0] // 2) + stack.shape[1:])
        other = swap(pick(stack, 1 - bit).astype(bf16))
        return pick(stack, bit).astype(f32) + other.astype(f32)

    def spread_open(self, part):
        if self.chips == 4:
            return (self.chip_swap(part, 1), self.chip_swap(part, 2))
        held, bits = [part], 1
        while bits < self.chips:
            held = held + [self.chip_swap(piece, bits) for piece in held]
            bits *= 2
        return tuple(held[1:])

    def spread_close(self, state):
        if self.chips == 4:
            by_x, by_y = state
            cut, axis = by_x.shape[-2] // 2, by_x.ndim - 2
            far = [
                self.chip_swap(by_x[..., :cut, :], 2),
                self.chip_swap(by_y[..., cut:, :], 1),
            ]
            return (by_x, by_y, jnp.concatenate(far, axis=axis))
        return state

    def far_open(self, states):
        if self.chips != 4:
            return ()
        cut = states[0][0].shape[0] // 2
        return (
            self.chip_swap(jnp.concatenate([by_x[:cut] for by_x, _ in states], axis=0), 2),
            self.chip_swap(jnp.concatenate([by_y[cut:] for _, by_y in states], axis=0), 1),
        )

    def far_parts(self, states, far):
        if self.chips != 4:
            return [[(k + 1, 0, part) for k, part in enumerate(state)] for state in states]
        cut = states[0][0].shape[0] // 2
        result = []
        for number, (by_x, by_y) in enumerate(states):
            rows = slice(number * cut, (number + 1) * cut)
            result.append([(1, 0, by_x), (2, 0, by_y), (3, 0, far[0][rows]), (3, cut, far[1][rows])])
        return result

    def chips_gather(self, part, axis, state=None):
        shape = part.shape[:axis] + (self.chips,) + part.shape[axis:]
        stack = place(jnp.zeros(shape, part.dtype), part, self.chip, axis)
        others = self.spread_close(self.spread_open(part) if state is None else state)
        for number, piece in enumerate(others):
            stack = place(stack, piece, self.chip ^ (number + 1), axis)
        return stack

    def reduce_open(self, stack, axis):
        if self.chips == 4:
            shape = stack.shape[:axis] + (2, 2) + stack.shape[axis + 1 :]
            stack = stack.reshape(shape)
            bit_x, bit_y = self.chip % 2, self.chip // 2
            cut = shape[0] // 2
            first, second = stack[:cut], stack[cut:]
            got_first = self.chip_swap(pick(first, 1 - bit_x, axis + 1), 1)
            got_second = self.chip_swap(pick(second, 1 - bit_y, axis), 2)
            return (pick(first, bit_x, axis + 1), pick(second, bit_y, axis), got_first, got_second)
        count = self.chips
        stack = stack.astype(f32)
        while count > 1:
            count //= 2
            shape = stack.shape[:axis] + (2, count) + stack.shape[axis + 1 :]
            stack = stack.reshape(shape)
            bit = (self.chip // count) % 2
            got = self.chip_swap(pick(stack, 1 - bit, axis).astype(bf16), count)
            stack = pick(stack, bit, axis) + got.astype(f32)
        return (pick(stack, 0, axis).astype(bf16),)

    def reduce_add(self, state):
        if self.chips != 4:
            return state
        first, second, got_first, got_second = state
        first = (first.astype(f32) + got_first.astype(f32)).astype(bf16)
        second = (second.astype(f32) + got_second.astype(f32)).astype(bf16)
        return (first, second)

    def reduce_send(self, state, axis):
        if self.chips != 4:
            return state
        first, second = state
        bit_x, bit_y = self.chip % 2, self.chip // 2
        got_first = self.chip_swap(pick(first, 1 - bit_y, axis), 2)
        got_second = self.chip_swap(pick(second, 1 - bit_x, axis), 1)
        return (pick(first, bit_y, axis), pick(second, bit_x, axis), got_first, got_second)

    def reduce_final(self, state):
        if self.chips != 4:
            return state[0]
        first, second, got_first, got_second = state
        first = first.astype(f32) + got_first.astype(f32)
        second = second.astype(f32) + got_second.astype(f32)
        return jnp.concatenate([first, second], axis=0).astype(bf16)

    def reduce_close(self, state, axis):
        return self.reduce_final(self.reduce_send(state, axis))

    def core_pair(self, part):
        other = self.core_swap(part)
        first = jnp.where(self.core == 0, part, other)
        second = jnp.where(self.core == 0, other, part)
        return first, second

    def sum_reps(self, vector):
        bits = 1
        while bits < self.reps:
            vector = vector + lax.ppermute(vector, "rep", [(r, r ^ bits) for r in range(self.reps)])
            bits *= 2
        return vector

    def sum_shards(self, vector):
        bits = 1
        while bits < self.shards:
            vector = vector + self.shard_swap(vector, bits)
            bits *= 2
        return vector


def stats_kernel(decay_rate, gradient_ref, old_ref, rows_ref, lane_rows_ref, sums_ref, total_ref, partial):
    step = pl.program_id(0)
    rows, columns = gradient_ref.shape

    @pl.when(step == 0)
    def _():
        partial[...] = jnp.zeros_like(partial)
        total_ref[...] = jnp.zeros_like(total_ref)

    gradient = gradient_ref[...].astype(f32)
    square = gradient * gradient
    row_mean = jnp.sum(square, axis=1, keepdims=True) / columns
    rows_new = decay_rate * old_ref[...] + (1.0 - decay_rate) * (row_mean + eps_second)
    rows_ref[...] = rows_new
    lane_rows_ref[...] = jnp.transpose(jnp.broadcast_to(rows_new, (rows, 128)))[0:1, :]
    total_ref[...] += jnp.broadcast_to(jnp.sum(rows_new, axis=0, keepdims=True), (1, 128))
    partial[0:8, :] += eights(square, jnp.sum)
    partial[8:16, :] += eights(square * (1.0 / rows_new), jnp.sum)

    @pl.when(step == pl.num_programs(0) - 1)
    def _():
        sums_ref[0:1, :] = jnp.sum(partial[0:8, :], axis=0, keepdims=True)
        sums_ref[1:2, :] = jnp.sum(partial[8:16, :], axis=0, keepdims=True)


def factor_stats(gradient, rows_old, decay_rate):
    height, breadth = gradient.shape
    rows = min(128, height)
    return pl.pallas_call(
        functools.partial(stats_kernel, decay_rate),
        grid=(height // rows,),
        in_specs=[
            pl.BlockSpec((rows, breadth), lambda step: (step, 0)),
            pl.BlockSpec((rows, 1), lambda step: (step, 0)),
        ],
        out_specs=[
            pl.BlockSpec((rows, 1), lambda step: (step, 0)),
            pl.BlockSpec((1, rows), lambda step: (0, step)),
            pl.BlockSpec((2, breadth), lambda step: (0, 0)),
            pl.BlockSpec((1, 128), lambda step: (0, 0)),
        ],
        out_shape=[
            jax.ShapeDtypeStruct((height, 1), f32),
            jax.ShapeDtypeStruct((1, height), f32),
            jax.ShapeDtypeStruct((2, breadth), f32),
            jax.ShapeDtypeStruct((1, 128), f32),
        ],
        scratch_shapes=[pltpu.VMEM((16, breadth), f32)],
        compiler_params=pltpu.CompilerParams(
            dimension_semantics=("arbitrary",), vmem_limit_bytes=32 * 1024 * 1024
        ),
        name="factor_stats",
    )(gradient, rows_old.reshape(height, 1))


def apply_kernel(
    decay_rate,
    height,
    gradient_ref,
    weight_ref,
    rows_ref,
    sums_ref,
    scalar_ref,
    old_ref,
    gradient_out,
    weight_out,
    copy_out,
    cols_out,
    rms_out,
    col_factor,
):
    columns = gradient_ref.shape[1]

    @pl.when(pl.program_id(0) == 0)
    def _():
        cols_new = decay_rate * old_ref[...] + (1.0 - decay_rate) * (
            sums_ref[0:1, :] / height + eps_second
        )
        row_mean = scalar_ref[0:1, 0:1] / height
        weight_mean = scalar_ref[1:2, 0:1] / (height * columns)
        scaled = jnp.sum(sums_ref[1:2, :] / cols_new, axis=1, keepdims=True)
        rms_update = jnp.sqrt(row_mean / (height * columns) * scaled)
        factor = rate_step * jnp.sqrt(weight_mean) * jnp.sqrt(row_mean)
        factor = factor / jnp.maximum(1.0, rms_update / clip_level)
        col_factor[...] = factor * lax.rsqrt(cols_new)
        cols_out[...] = cols_new
        rms_out[...] = jnp.broadcast_to(rms_update, (1, 128))

    gradient = gradient_ref[...].astype(f32)
    new_weight = weight_ref[...] - gradient * lax.rsqrt(rows_ref[...]) * col_factor[...]
    gradient_out[...] = gradient
    weight_out[...] = new_weight
    copy_out[...] = new_weight.astype(bf16)


def factor_apply(gradient, weight, rows_new, sums, scalars, cols_old, height, decay_rate):
    own_height, breadth = gradient.shape
    rows = min(64, own_height)

    def rows_spec():
        return pl.BlockSpec((rows, breadth), lambda step: (step, 0))

    def row_spec(count, wide):
        return pl.BlockSpec((count, wide), lambda step: (0, 0))

    return pl.pallas_call(
        functools.partial(apply_kernel, decay_rate, height),
        grid=(own_height // rows,),
        in_specs=[
            rows_spec(),
            rows_spec(),
            pl.BlockSpec((rows, 1), lambda step: (step, 0)),
            row_spec(2, breadth),
            row_spec(2, 128),
            row_spec(1, breadth),
        ],
        out_specs=[rows_spec(), rows_spec(), rows_spec(), row_spec(1, breadth), row_spec(1, 128)],
        out_shape=[
            jax.ShapeDtypeStruct((own_height, breadth), f32),
            jax.ShapeDtypeStruct((own_height, breadth), f32),
            jax.ShapeDtypeStruct((own_height, breadth), bf16),
            jax.ShapeDtypeStruct((1, breadth), f32),
            jax.ShapeDtypeStruct((1, 128), f32),
        ],
        scratch_shapes=[pltpu.VMEM((1, breadth), f32)],
        compiler_params=pltpu.CompilerParams(
            dimension_semantics=("arbitrary",), vmem_limit_bytes=32 * 1024 * 1024
        ),
        name="factor_apply",
    )(gradient, weight, rows_new, sums, scalars, cols_old)


def summed(moves, entries):
    total = moves.sum_shards(jnp.concatenate(entries, axis=1))
    result, offset = [], 0
    for entry in entries:
        result.append(total[:, offset : offset + entry.shape[1]])
        offset += entry.shape[1]
    return result


def on_device(
    tokens,
    cotangent,
    seq_lengths,
    qkv_weight,
    out_weight,
    up_weight,
    down_weight,
    vectors,
    row_state,
    down_rows,
    col_state,
    vector_state,
):
    moves = Moves()
    shards, half, chips, core = moves.shards, moves.half, moves.chips, moves.core
    row_count, width = tokens.shape
    hidden_width = up_weight.shape[1]
    group_rows = row_count * shards
    heads = HEADS // shards
    head_width = width // HEADS
    span = heads * head_width
    member = moves.member
    decay_rate = 1.0 - STEP ** (-0.8)
    head_number = (member * heads + jnp.arange(heads, dtype=jnp.int32)).astype(f32)
    slopes = jnp.exp2(-8.0 * (head_number + 1.0) / HEADS)

    gain_one = vectors[0:width]
    shift_one = vectors[width : 2 * width]
    bias_query = vectors[2 * width : 3 * width]
    bias_value = vectors[3 * width : 4 * width]
    bias_out = vectors[4 * width : 5 * width]
    gain_two = vectors[5 * width : 6 * width]
    shift_two = vectors[6 * width : 7 * width]
    bias_up = vectors[7 * width : 7 * width + hidden_width]
    bias_down = vectors[7 * width + hidden_width :]

    home_tokens = moves.home_swap(tokens)
    other_lengths = moves.core_swap(seq_lengths)
    lengths = jnp.where(moves.side == core, seq_lengths, other_lengths)[0]
    plan = block_plan(lengths, group_rows, BLOCK)
    rows_z = width // shards
    rows_piece = rows_z // chips
    my_rows = lax.dynamic_slice_in_dim(qkv_weight, moves.chip * rows_piece, rows_piece, 0)
    my_rows = my_rows.astype(bf16)
    my_blocks = []
    for number in range(half):
        kinds = []
        for kind in range(3):
            first = kind * width + number * span
            second = first + half * span
            kinds.append(
                jnp.where(
                    core == 0, my_rows[:, first : first + span], my_rows[:, second : second + span]
                )
            )
        my_blocks.append(jnp.concatenate(kinds, axis=1))
    qkv_part = moves.half_exchange(jnp.stack(my_blocks))
    half_cols = hidden_width // (2 * shards)
    up_wide = shards * half_cols
    out_wide = width // 2
    down_piece = half_cols // chips

    def core_half(values):
        parts = []
        for number in range(shards):
            start = 2 * number * half_cols
            first = values[..., start : start + half_cols]
            second = values[..., start + half_cols : start + 2 * half_cols]
            parts.append(jnp.where(core == 0, first, second))
        return jnp.concatenate(parts, axis=-1)

    up_own = core_half(up_weight).astype(bf16)
    out_own = out_weight.astype(bf16)
    down_own = lax.dynamic_slice_in_dim(down_weight, core * half_cols, half_cols, 0).astype(bf16)
    fold = down_piece // rows_piece
    my_down = lax.dynamic_slice_in_dim(down_own, moves.chip * down_piece, down_piece, 0)
    weight_piece = jnp.concatenate(
        [
            lax.dynamic_slice_in_dim(own, moves.chip * rows_piece, rows_piece, 0)
            for own in (up_own, out_own)
        ]
        + [my_down[k * rows_piece : (k + 1) * rows_piece] for k in range(fold)],
        axis=1,
    )
    near_pieces, bits = [weight_piece], 1
    while bits < half:
        near_pieces = near_pieces + [moves.shard_swap(piece, bits) for piece in near_pieces]
        bits *= 2
    near_pieces = near_pieces[1:]
    home_tokens, qkv_part, near_pieces, weight_piece = together(
        home_tokens, qkv_part, near_pieces, weight_piece
    )
    far_piece = moves.shard_swap(weight_piece, half)
    near_open = [moves.spread_open(piece) for piece in near_pieces]
    qkv_far = moves.shard_swap(qkv_part, half)
    qkv_far, near_open = together(qkv_far, near_open)
    qkv_part = ordered(qkv_part, qkv_far, moves.side).reshape(shards, rows_piece, 3 * span)
    qkv_cols = moves.chips_gather(qkv_part, 1).reshape(width, 3 * span)
    inputs = home_tokens.astype(f32)
    normed_one, inv_std_one = norm_parts(inputs)
    act_one = (normed_one * gain_one + shift_one).astype(bf16)
    act_half = moves.half_gather(act_one)

    act_half, qkv_cols, far_piece, cotangent = together(
        act_half, qkv_cols, far_piece, cotangent
    )
    home_cot = moves.home_swap(cotangent)
    act_all = moves.cores_gather(act_half).reshape(group_rows, width)
    far_open = moves.spread_open(far_piece)
    far_pieces, bits = [far_piece], 1
    while bits < half:
        far_pieces = far_pieces + [moves.shard_swap(piece, bits) for piece in far_pieces]
        bits *= 2
    far_pieces = far_pieces[1:]

    bias_q_part = lax.dynamic_slice_in_dim(bias_query, member * span, span)
    bias_v_part = lax.dynamic_slice_in_dim(bias_value, member * span, span)
    qkv_bias = jnp.concatenate([bias_q_part, jnp.zeros_like(bias_q_part), bias_v_part])
    qkv_rows = (dot(act_all, qkv_cols) + qkv_bias).astype(bf16)
    attended_cols, logs = attend_forward(qkv_rows, plan, slopes, heads, BLOCK)
    attended_cols, far_open, far_pieces, home_cot = together(
        attended_cols, far_open, far_pieces, home_cot
    )
    attended_parts = moves.cores_exchange(attended_cols.reshape(shards, row_count, span))
    attended_parts = moves.members_exchange(attended_parts)
    first_states = near_open + [far_open]
    first_far = moves.far_open(first_states)
    last_states = [moves.spread_open(piece) for piece in far_pieces]
    attended_parts, first_far, last_states, home_cot = together(
        attended_parts, first_far, last_states, home_cot
    )
    last_far = moves.far_open(last_states)
    attended = jnp.concatenate([attended_parts[k] for k in range(shards)], axis=1)

    pieces = near_pieces + [far_piece] + far_pieces
    arrays = list(pieces)
    sources = [(k, 0, rows_piece, k + 1, 0, 0) for k in range(len(pieces))]
    for first_plane, states, far in ((1, first_states, first_far), (half + 1, last_states, last_far)):
        cut = rows_piece // 2
        for way, array in enumerate(far):
            for k in range(len(states)):
                sources.append((len(arrays), k * cut, cut, first_plane + k, 3, way * cut))
            arrays.append(array)
        for k, state in enumerate(states):
            for way, array in enumerate(state):
                sources.append((len(arrays), 0, rows_piece, first_plane + k, way + 1, 0))
                arrays.append(array)
    place_now = jnp.stack([moves.shard, moves.chip]).astype(jnp.int32)
    sizes = (rows_z, rows_piece, up_wide, width, fold, half_cols)
    gathered = Gathered(arrays, sources, place_now, sizes)
    residual, normed_two, inv_std_two, act_two = out_projection(
        gathered, out_own, attended, inputs, bias_out, gain_two, shift_two
    )

    act_two_other, attended_other, cot_other = together(
        moves.core_swap(act_two), moves.core_swap(attended), moves.core_swap(home_cot)
    )
    cot_pair = jnp.concatenate([home_cot, cot_other], axis=0)
    attended_pair = jnp.concatenate([attended, attended_other], axis=0)
    hidden_pair, slope_pair = up_projection(
        gathered, up_own, act_two, act_two_other, core_half(bias_up)
    )
    down_terms = dot_rows(hidden_pair, cot_pair).astype(bf16)
    slope_pair, down_terms = together(slope_pair, down_terms)
    down_state = moves.reduce_open(down_terms.reshape(shards, chips, down_piece, width), 1)
    grad_y = home_cot.astype(f32)
    grad_bias_down = jnp.sum(grad_y, axis=0)
    grad_up_pair, grad_bias_up = hidden_backward(gathered, down_own, home_cot, cot_other, slope_pair)
    grad_bias_up = grad_bias_up.reshape(-1)
    back_other = moves.core_swap(up_backward(gathered, up_own, grad_up_pair, 1, bf16))
    up_terms = up_gradient(act_two, act_two_other, grad_up_pair)
    back_other, hidden_pair, up_terms, down_state = together(
        back_other, hidden_pair, up_terms, down_state
    )
    up_state = moves.reduce_open(up_terms.reshape(shards, chips, rows_piece, up_wide), 1)
    down_mid = moves.reduce_close(moves.reduce_add(down_state), 1)
    grad_act_two = up_backward(gathered, up_own, grad_up_pair, 0, f32) + back_other.astype(f32)
    grad_gain_two = jnp.sum(grad_act_two * normed_two, axis=0)
    grad_shift_two = jnp.sum(grad_act_two, axis=0)
    grad_residual = grad_y + norm_back(grad_act_two, normed_two, inv_std_two, gain_two)
    grad_attn = grad_residual.astype(bf16)
    grad_bias_out = jnp.sum(grad_attn, axis=0, dtype=f32)
    to_members = out_backward(gathered, out_own, grad_attn, span)
    attn_halves = [grad_attn[:, :out_wide], grad_attn[:, out_wide:]]
    attn_own = jnp.where(core == 0, attn_halves[0], attn_halves[1])
    attn_other = jnp.where(core == 0, attn_halves[1], attn_halves[0])
    grad_heads, attn_other = together(moves.cores_exchange(to_members), moves.core_swap(attn_other))
    attn_pair = jnp.concatenate([attn_own, attn_other], axis=0)
    grad_heads, hidden_pair = together(grad_heads, hidden_pair)
    grad_heads = moves.members_exchange(grad_heads).reshape(group_rows, span)
    down_pair = down_projection(gathered, down_own, hidden_pair)
    down_other = moves.core_swap(down_pair[row_count:])
    block_out = residual + down_pair[:row_count].astype(f32) + down_other.astype(f32) + bias_down
    block_out = block_out.astype(bf16)

    out_terms = dot_rows(attended_pair, attn_pair).astype(bf16)
    def shards_halve(piece, bits):
        piece = piece.reshape((piece.shape[0] // 2, 2) + piece.shape[1:])
        bit = moves.shard_bit(bits)
        return pick(piece, bit, 1), moves.shard_swap(pick(piece, 1 - bit, 1), bits)

    def halved(state):
        own, other = state
        return (own.astype(f32) + other.astype(f32)).astype(bf16)

    def shards_sum(piece):
        rows = piece.shape[1]
        return lax.psum_scatter(
            piece.reshape(shards * rows, piece.shape[2]), "shard", scatter_dimension=0, tiled=True
        )

    grad_heads, down_mid, out_terms, block_out = together(
        grad_heads, down_mid, out_terms, block_out
    )
    block_out = moves.home_swap(block_out)
    down_owned = shards_sum(down_mid)
    out_state = moves.reduce_open(out_terms.reshape(shards, chips, rows_piece, out_wide), 1)
    attend_args = (plan, slopes)
    parts = 2 if heads % 4 == 0 else 1
    part_heads = heads // parts
    grad_qkv = attend_backward(
        qkv_rows, grad_heads, attended_cols, logs, *attend_args, part_heads, BLOCK, 0, None
    )
    grad_qkv, up_state, out_state = together(grad_qkv, up_state, out_state)
    up_sums, out_sums = moves.reduce_add(up_state), moves.reduce_add(out_state)
    grad_qkv, up_sums, out_sums = together(grad_qkv, up_sums, out_sums)
    up_out_state = [
        jnp.concatenate([up_part, out_part], axis=-1) for up_part, out_part in zip(up_sums, out_sums)
    ]
    if parts == 2:
        grad_qkv = attend_backward(
            qkv_rows, grad_heads, attended_cols, logs, *attend_args, part_heads, BLOCK, part_heads, grad_qkv
        )
    grad_qkv, up_out_state, block_out = together(
        grad_qkv, moves.reduce_send(up_out_state, 1), block_out
    )
    up_out_piece = moves.reduce_final(up_out_state)
    up_out_state = shards_halve(up_out_piece, 1)

    grad_bias_q_part = jnp.sum(grad_qkv[:, :span], axis=0, dtype=f32)
    grad_bias_v_part = jnp.sum(grad_qkv[:, 2 * span :], axis=0, dtype=f32)

    grad_halves = grad_qkv.reshape(2, half * row_count, 3 * span)
    sent = dot_right(pick(grad_halves, 1 - core), qkv_cols).astype(bf16)
    sent = moves.core_swap(sent)
    qkv_terms = dot_rows(act_all, grad_qkv).astype(bf16)
    qkv_terms = qkv_terms.reshape(shards, chips, rows_piece, 3 * span)
    qkv_state = moves.reduce_open(qkv_terms, 1)
    back = dot_right(pick(grad_halves, core), qkv_cols) + sent.astype(f32)
    qkv_state, back, up_out_state = together(qkv_state, back, up_out_state)

    back = back.reshape(half, row_count, width)
    low_bits = list(reversed(moves.low_bits()))
    for bits in low_bits[:-1]:
        back = moves.reduce_bit(
            back, moves.shard_bit(bits), functools.partial(moves.shard_swap, bits=bits)
        )
    back = back.reshape((2, -1) + back.shape[1:])
    back_bit = moves.shard_bit(low_bits[-1])
    back_other = moves.shard_swap(pick(back, 1 - back_bit).astype(bf16), low_bits[-1])
    up_out_piece, bits = halved(up_out_state), 2
    while bits < half:
        up_out_piece = halved(shards_halve(up_out_piece, bits))
        bits *= 2
    up_out_state = shards_halve(up_out_piece, half)
    qkv_state = moves.reduce_send(moves.reduce_add(qkv_state), 1)
    qkv_state, up_out_state = together(qkv_state, up_out_state)

    up_out_owned = halved(up_out_state)[0]
    up_out_state = moves.spread_open(up_out_owned)
    qkv_piece = moves.reduce_final(qkv_state)
    qkv_piece = qkv_piece.reshape((2, half) + qkv_piece.shape[1:])
    qkv_own = pick(qkv_piece, moves.side)
    qkv_other = moves.shard_swap(pick(qkv_piece, 1 - moves.side), half)
    back_other, qkv_other, up_out_state = together(back_other, qkv_other, up_out_state)

    qkv_piece = moves.half_exchange(halved((qkv_own, qkv_other)))
    down_state = moves.spread_open(down_owned)
    grad_act_one = pick(back, back_bit) + back_other.astype(f32)
    grad_act_one = grad_act_one.reshape(row_count, width)
    grad_gain_one = jnp.sum(grad_act_one * normed_one, axis=0)
    grad_shift_one = jnp.sum(grad_act_one, axis=0)
    grad_inputs = grad_residual + norm_back(grad_act_one, normed_one, inv_std_one, gain_one)
    grad_inputs, qkv_piece, down_state = together(grad_inputs.astype(bf16), qkv_piece, down_state)
    tokens_grad = moves.home_swap(grad_inputs)
    qkv_owned = moves.chips_gather(qkv_piece, 1)

    up_out_first, up_out_second = moves.core_pair(
        moves.chips_gather(up_out_owned, 0, tuple(up_out_state)).reshape(rows_z, up_wide + out_wide)
    )
    out_grad = jnp.concatenate([up_out_first[:, up_wide:], up_out_second[:, up_wide:]], axis=1)
    up_columns = []
    for number in range(shards):
        part = slice(number * half_cols, (number + 1) * half_cols)
        up_columns += [up_out_first[:, part], up_out_second[:, part]]
    up_grad = jnp.concatenate(up_columns, axis=1)
    down_first, down_second = moves.core_pair(
        moves.chips_gather(down_owned, 0, tuple(down_state)).reshape(half_cols, width)
    )
    down_grad = jnp.concatenate([down_first, down_second], axis=0)
    qkv_first, qkv_second = moves.core_pair(qkv_owned.reshape(half, rows_z, 3 * span))
    qkv_columns = []
    for kind in range(3):
        for source in (qkv_first, qkv_second):
            for number in range(half):
                qkv_columns.append(source[number][:, kind * span : (kind + 1) * span])
    qkv_grad = jnp.concatenate(qkv_columns, axis=1)

    gradients = [qkv_grad, out_grad, up_grad, down_grad]
    weights = [qkv_weight, out_weight, up_weight, down_weight]
    heights = [width, width, width, hidden_width]
    rows_old = [row_state[0], row_state[1], row_state[2], down_rows]
    weight_sums = [jnp.sum(weight * weight) for weight in weights]
    stats = [
        factor_stats(gradient, old, decay_rate) for gradient, old in zip(gradients, rows_old)
    ]

    def to_sum(number):
        weight_sum = jnp.broadcast_to(weight_sums[number], (1, 128))
        return [stats[number][2], jnp.concatenate([stats[number][3], weight_sum], axis=0)]

    def spread_heads(part):
        return [jnp.where(member == number, part, 0.0) for number in range(shards)]

    bias_up_parts = []
    for number in range(shards):
        part = grad_bias_up[number * half_cols : (number + 1) * half_cols]
        bias_up_parts += [jnp.where(core == 0, part, 0.0), jnp.where(core == 1, part, 0.0)]
    vector_part = moves.sum_reps(
        jnp.concatenate(
            [grad_gain_one, grad_shift_one]
            + spread_heads(grad_bias_q_part)
            + spread_heads(grad_bias_v_part)
            + [grad_bias_out, grad_gain_two, grad_shift_two]
            + bias_up_parts
            + [grad_bias_down]
        )
    )
    vector_rows, tokens_grad = together(vector_part.reshape(2, -1), tokens_grad)
    all_sums = summed(moves, to_sum(0) + to_sum(1) + to_sum(2) + to_sum(3) + [vector_rows])
    sums = [all_sums[0:2], all_sums[2:4], all_sums[4:6], all_sums[6:8]]
    vector_grad = all_sums[8].reshape(-1)
    updates = []
    offset = 0
    for number in range(4):
        end_col = offset + gradients[number].shape[1]
        updates.append(
            factor_apply(
                gradients[number],
                weights[number],
                stats[number][0],
                sums[number][0],
                sums[number][1],
                col_state[offset:end_col].reshape(1, -1),
                heights[number],
                decay_rate,
            )
        )
        offset = end_col
    grads_out, new_weights, copies, new_cols, rms_rows = zip(*updates)
    rms_values = [rms[0, 0] for rms in rms_rows]

    vector_state_new = decay_rate * vector_state + (1.0 - decay_rate) * (
        vector_grad * vector_grad + eps_second
    )
    vector_step = vector_grad * lax.rsqrt(vector_state_new)
    vector_rms = jnp.sqrt(jnp.mean(vector_step * vector_step))
    vector_new = vectors - rate_step * jnp.sqrt(
        jnp.mean(vectors * vectors)
    ) * vector_step / jnp.maximum(1.0, vector_rms / clip_level)
    update_rms = jnp.stack(rms_values + [vector_rms])
    return (
        block_out,
        tokens_grad,
        *grads_out,
        vector_grad,
        *new_weights,
        vector_new,
        *copies,
        jnp.concatenate([stats[0][1], stats[1][1], stats[2][1]], axis=0),
        stats[3][1].reshape(-1),
        jnp.concatenate(new_cols, axis=1).reshape(-1),
        vector_state_new,
        update_rms,
    )


def solution(mesh):
    in_specs = (
        P(("rep", "shard"), None),
        P(("rep", "shard"), None),
        P("rep", None),
        P("shard", None),
        P("shard", None),
        P("shard", None),
        P("shard", None),
        P(),
        P(None, "shard"),
        P("shard"),
        P(),
        P(),
    )
    out_specs = (
        P(("rep", "shard"), None),
        P(("rep", "shard"), None),
        P("shard", None),
        P("shard", None),
        P("shard", None),
        P("shard", None),
        P(),
        P("shard", None),
        P("shard", None),
        P("shard", None),
        P("shard", None),
        P(),
        P("shard", None),
        P("shard", None),
        P("shard", None),
        P("shard", None),
        P(None, "shard"),
        P("shard"),
        P(),
        P(),
        P(),
    )
    return jax.shard_map(
        on_device, mesh=mesh, in_specs=in_specs, out_specs=out_specs, check_vma=False
    )
```

```python
import functools

import jax
import jax.numpy as jnp
from jax import lax
from jax.experimental import pallas as pl
from jax.experimental.pallas import tpu as pltpu
from jax.sharding import PartitionSpec as P

HEADS = 16
STEP = 10
BLOCK = 256


eps_norm = 1e-05
eps_second = 1e-30
rate_step = 0.5
clip_level = 1.0
masked = -1e30
gelu_root = (2.0 / 3.141592653589793) ** 0.5
gelu_cubic = 0.044715

f32 = jnp.float32
bf16 = jnp.bfloat16


def norm_parts(values):
    average = jnp.mean(values, axis=-1, keepdims=True)
    centred = values - average
    inv_std = lax.rsqrt(jnp.mean(centred * centred, axis=-1, keepdims=True) + eps_norm)
    return (centred * inv_std, inv_std)


def norm_back(grad_out, normed, inv_std, gain_vec):
    grad_normed = grad_out * gain_vec
    inner_mean = jnp.mean(grad_normed * normed, axis=-1, keepdims=True)
    centred = grad_normed - jnp.mean(grad_normed, axis=-1, keepdims=True)
    return (centred - normed * inner_mean) * inv_std


def gelu_value(pre_act):
    curve = jnp.tanh(gelu_root * (pre_act + gelu_cubic * pre_act * pre_act * pre_act))
    return 0.5 * pre_act * (1.0 + curve)


def gelu_slope(pre_act):
    square = pre_act * pre_act
    curve = jnp.tanh(gelu_root * (pre_act + gelu_cubic * square * pre_act))
    inner = gelu_root * (1.0 + 3.0 * gelu_cubic * square)
    return 0.5 * (1.0 + curve) + 0.5 * pre_act * (1.0 - curve * curve) * inner


def dot(left_side, right_side):
    return jnp.dot(left_side, right_side, preferred_element_type=f32)


def dot_right(left_side, right_side):
    return lax.dot_general(
        left_side, right_side, (((1,), (1,)), ((), ())), preferred_element_type=f32
    )


def dot_rows(left_side, right_side):
    return lax.dot_general(
        left_side, right_side, (((0,), (0,)), ((), ())), preferred_element_type=f32
    )


def pick(stack, index, axis=0):
    return lax.dynamic_index_in_dim(stack, index, axis, keepdims=False)


def place(stack, part, index, axis=0):
    return lax.dynamic_update_index_in_dim(stack, part, index, axis)


def head_rows(number, head_width):
    return slice(number * head_width, (number + 1) * head_width)


def lane_masks(block_rows, width, heads):
    lanes = lax.broadcasted_iota(jnp.int32, (block_rows, width), 1)
    head_width = width // heads
    return [
        (lanes >= number * head_width) & (lanes < (number + 1) * head_width)
        for number in range(heads)
    ]


def allowed_pairs(key_block, query_block, start_row, block):
    key_pos = lax.broadcasted_iota(jnp.int32, (block, block), 0) + key_block * block
    query_pos = lax.broadcasted_iota(jnp.int32, (block, block), 1) + query_block * block
    return (key_pos <= query_pos) & (key_pos >= start_row)


def key_offsets(key_block, query_block, block):
    rows = lax.broadcasted_iota(jnp.int32, (block, 1), 0)
    return (rows + (key_block - query_block) * block).astype(f32)


def turned(values):
    return jnp.transpose(values.astype(f32))


def head_stack(values, lanes):
    zero = jnp.zeros(values.shape, values.dtype)
    return jnp.concatenate([jnp.where(lane, values, zero) for lane in lanes], axis=0)


def eights(values, combine):
    rows, columns = values.shape
    return combine(values.reshape(rows // 8, 8, columns), axis=0)


def forward_kernel(
    heads,
    block,
    low_ref,
    mid_ref,
    slope_ref,
    start_ref,
    qkv_ref,
    out_ref,
    log_ref,
    values_turned,
    key_stack,
    score_ref,
):
    tokens = qkv_ref.shape[0]
    width = qkv_ref.shape[1] // 3
    head_width = width // heads
    blocks = tokens // block
    query_block = pl.program_id(0)

    @pl.when(query_block == 0)
    def _():
        lanes = lane_masks(block, width, heads)
        for number in range(blocks):
            rows = slice(number * block, (number + 1) * block)
            values_turned[number] = turned(qkv_ref[rows, 2 * width :]).astype(bf16)
            key_stack[number] = head_stack(qkv_ref[rows, width : 2 * width], lanes)

    first_row = pl.multiple_of(query_block * block, block)
    queries = qkv_ref[pl.ds(first_row, block), :width].astype(f32) * head_width ** (-0.5)
    queries = turned(queries).astype(bf16)
    start_row = start_ref[query_block]

    def score_step(key_block, bests, with_mask):
        scores = dot(key_stack[key_block], queries)
        offsets = key_offsets(key_block, query_block, block)
        allowed = allowed_pairs(key_block, query_block, start_row, block) if with_mask else None
        result = []
        for number in range(heads):
            rows = head_rows(number, block)
            part = scores[rows] + slope_ref[number] * offsets
            if with_mask:
                part = jnp.where(allowed, part, masked)
            score_ref[key_block, rows, :] = part
            result.append(jnp.maximum(bests[number], eights(part, jnp.max)))
        return tuple(result)

    low, mid = low_ref[query_block], mid_ref[query_block]
    bests = tuple(jnp.full((8, block), masked, f32) for _ in range(heads))
    bests = lax.fori_loop(low, mid, functools.partial(score_step, with_mask=True), bests)
    bests = lax.fori_loop(mid, query_block, functools.partial(score_step, with_mask=False), bests)
    bests = score_step(query_block, bests, True)
    bests = [jnp.max(best, axis=0, keepdims=True) for best in bests]

    def value_step(key_block, state):
        result = []
        for number in range(heads):
            total, gathered = state[2 * number : 2 * number + 2]
            weights = jnp.exp(score_ref[key_block, head_rows(number, block), :] - bests[number])
            value_rows = values_turned[key_block, head_rows(number, head_width), :]
            result += [
                total + eights(weights, jnp.sum),
                gathered + dot(value_rows, weights.astype(bf16)),
            ]
        return tuple(result)

    state = ()
    for number in range(heads):
        state += (jnp.zeros((8, block), f32), jnp.zeros((head_width, block), f32))
    state = lax.fori_loop(low, query_block + 1, value_step, state)
    columns = []
    for number in range(heads):
        total = jnp.sum(state[2 * number], axis=0, keepdims=True)
        columns.append(state[2 * number + 1] / total)
        log_ref[0, number : number + 1, :] = bests[number] + jnp.log(total)
    out_ref[...] = jnp.transpose(jnp.concatenate(columns, axis=0)).astype(bf16)


def backward_kernel(heads, block, first_head, merge, *refs):
    full_ref, high_ref, slope_ref, start_ref, log_ref, qkv_ref, grad_ref, out_ref = refs[:8]
    earlier_ref = refs[8] if merge else None
    result_ref = refs[9 if merge else 8]
    (
        queries_turned,
        grads_turned,
        keys_turned,
        query_stack,
        grad_stack,
        key_stack,
        value_stack,
        delta_rows,
        query_grads,
    ) = refs[10 if merge else 9 :]
    tokens, all_width = grad_ref.shape
    head_width = all_width // log_ref.shape[1]
    width = heads * head_width
    scale = head_width ** (-0.5)
    blocks = tokens // block
    key_block = pl.program_id(0)
    lanes = lane_masks(block, width, heads)

    def columns(kind):
        start = kind * all_width + first_head * head_width
        return slice(start, start + width)

    def target(kind):
        start = (kind * all_width + first_head * head_width) if merge else kind * width
        return slice(start, start + width)

    @pl.when(key_block == 0)
    def _():
        for number in range(blocks):
            rows = slice(number * block, (number + 1) * block)
            queries = qkv_ref[rows, columns(0)]
            queries_turned[number] = turned(queries.astype(f32) * scale).astype(bf16)
            query_stack[number] = head_stack(queries, lanes)
            keys_turned[number] = turned(qkv_ref[rows, columns(1)]).astype(bf16)
            grads = grad_ref[rows, columns(0)]
            grad_stack[number] = head_stack(grads, lanes)
            grads = grads.astype(f32)
            grads_turned[number] = turned(grads).astype(bf16)
            product = turned(grads * out_ref[rows, columns(0)].astype(f32))
            for head in range(heads):
                delta_rows[number, head : head + 1, :] = jnp.sum(
                    product[head_rows(head, head_width)], axis=0, keepdims=True
                )
            query_grads[number] = jnp.zeros((width, block), f32)

    key_row = pl.multiple_of(key_block * block, block)
    key_stack[...] = head_stack(qkv_ref[pl.ds(key_row, block), columns(1)], lanes)
    value_stack[...] = head_stack(qkv_ref[pl.ds(key_row, block), columns(2)], lanes)

    def step(query_block, state, with_mask):
        key_total, value_total = state
        scores = dot(key_stack[...], queries_turned[query_block])
        grad_weights = dot(value_stack[...], grads_turned[query_block])
        offsets = key_offsets(key_block, query_block, block)
        if with_mask:
            allowed = allowed_pairs(key_block, query_block, start_ref[query_block], block)
        weight_list, grad_list = [], []
        for number in range(heads):
            rows = head_rows(number, block)
            head = first_head + number
            part = scores[rows] + slope_ref[head] * offsets
            part = part - log_ref[query_block, head : head + 1, :]
            if with_mask:
                part = jnp.where(allowed, part, masked)
            probabilities = jnp.exp(part)
            delta = delta_rows[query_block, number : number + 1, :]
            grad_scores = (probabilities * (grad_weights[rows] - delta)).astype(bf16)
            weight_list.append(probabilities.astype(bf16))
            grad_list.append(grad_scores)
            rows = head_rows(number, head_width)
            query_grads[query_block, rows, :] += dot(keys_turned[key_block, rows, :], grad_scores)
        weight_row = jnp.concatenate(weight_list, axis=1)
        grad_row = jnp.concatenate(grad_list, axis=1)
        return (
            key_total + dot(grad_row, query_stack[query_block]),
            value_total + dot(weight_row, grad_stack[query_block]),
        )

    state = (jnp.zeros((block, width), f32), jnp.zeros((block, width), f32))
    state = step(key_block, state, True)
    full, high = full_ref[key_block], high_ref[key_block]
    state = lax.fori_loop(key_block + 1, full, functools.partial(step, with_mask=False), state)
    state = lax.fori_loop(full, high, functools.partial(step, with_mask=True), state)
    result_ref[pl.ds(key_row, block), target(1)] = (state[0] * scale).astype(bf16)
    result_ref[pl.ds(key_row, block), target(2)] = state[1].astype(bf16)
    if merge:
        other = first_head * head_width
        for kind in range(3):
            result_ref[pl.ds(key_row, block), kind * all_width : kind * all_width + other] = earlier_ref[
                pl.ds(key_row, block), kind * other : (kind + 1) * other
            ]

    @pl.when(key_block == blocks - 1)
    def _():
        for number in range(blocks):
            rows = slice(number * block, (number + 1) * block)
            result_ref[rows, target(0)] = jnp.transpose(query_grads[number] * scale).astype(bf16)


def block_plan(lengths, tokens, block):
    ends = jnp.cumsum(lengths)
    positions = jnp.arange(tokens, dtype=jnp.int32)
    passed = positions[:, None] >= ends[None, :]
    starts = jnp.max(jnp.where(passed, ends[None, :], 0), axis=1).astype(jnp.int32)
    finish = jnp.min(jnp.where(passed, tokens, ends[None, :]), axis=1).astype(jnp.int32)
    blocks = tokens // block
    number = jnp.arange(blocks, dtype=jnp.int32)
    first_start = starts[::block]
    last_start = starts[block - 1 :: block]
    low = first_start // block
    mid = jnp.clip((last_start + block - 1) // block, low, number)
    high = (finish[block - 1 :: block] - 1) // block + 1
    full = jnp.clip(finish[::block] // block, number + 1, high)
    return (starts.reshape(blocks, 1, block), low, mid, full, high)


def scalar_spec():
    return pl.BlockSpec(memory_space=pltpu.SMEM)


def whole_spec(shape):
    return pl.BlockSpec(shape, lambda step: (0,) * len(shape), pipeline_mode=pl.Buffered(1))


def attend_forward(qkv, plan, slopes, heads, block):
    tokens, triple = qkv.shape
    width = triple // 3
    blocks = tokens // block
    starts, low, mid, full, high = plan
    return pl.pallas_call(
        functools.partial(forward_kernel, heads, block),
        grid=(blocks,),
        in_specs=[
            scalar_spec(),
            scalar_spec(),
            scalar_spec(),
            whole_spec((blocks, 1, block)),
            whole_spec((tokens, triple)),
        ],
        out_specs=[
            pl.BlockSpec((block, width), lambda step: (step, 0)),
            pl.BlockSpec((1, heads, block), lambda step: (step, 0, 0)),
        ],
        out_shape=[
            jax.ShapeDtypeStruct((tokens, width), bf16),
            jax.ShapeDtypeStruct((blocks, heads, block), f32),
        ],
        scratch_shapes=[
            pltpu.VMEM((blocks, width, block), bf16),
            pltpu.VMEM((blocks, heads * block, width), bf16),
            pltpu.VMEM((blocks, heads * block, block), f32),
        ],
        compiler_params=pltpu.CompilerParams(
            dimension_semantics=("arbitrary",), vmem_limit_bytes=40 * 1024 * 1024
        ),
        cost_estimate=pl.CostEstimate(
            flops=3 * tokens * tokens * 256 * heads,
            bytes_accessed=10 * tokens * width,
            transcendentals=tokens * tokens * heads // 2,
        ),
        name="attend_forward",
    )(low, mid, slopes, starts, qkv)


def attend_backward(qkv, grads, outputs, logs, plan, slopes, heads, block, first_head, earlier):
    tokens, triple = qkv.shape
    all_width = triple // 3
    all_heads = logs.shape[1]
    width = all_width // all_heads * heads
    blocks = tokens // block
    starts, low, mid, full, high = plan
    merge = earlier is not None
    result_width = triple if merge else 3 * width
    operands = [full, high, slopes, starts, logs, qkv, grads, outputs]
    specs = [scalar_spec() for _ in range(3)] + [whole_spec(entry.shape) for entry in operands[3:]]
    if merge:
        operands.append(earlier)
        specs.append(whole_spec(earlier.shape))
    return pl.pallas_call(
        functools.partial(backward_kernel, heads, block, first_head, merge),
        grid=(blocks,),
        in_specs=specs,
        out_specs=pl.BlockSpec((tokens, result_width), lambda step: (0, 0)),
        out_shape=jax.ShapeDtypeStruct((tokens, result_width), bf16),
        scratch_shapes=[
            pltpu.VMEM((blocks, width, block), bf16),
            pltpu.VMEM((blocks, width, block), bf16),
            pltpu.VMEM((blocks, width, block), bf16),
            pltpu.VMEM((blocks, heads * block, width), bf16),
            pltpu.VMEM((blocks, heads * block, width), bf16),
            pltpu.VMEM((heads * block, width), bf16),
            pltpu.VMEM((heads * block, width), bf16),
            pltpu.VMEM((blocks, heads, block), f32),
            pltpu.VMEM((blocks, width, block), f32),
        ],
        compiler_params=pltpu.CompilerParams(
            dimension_semantics=("arbitrary",), vmem_limit_bytes=40 * 1024 * 1024
        ),
        cost_estimate=pl.CostEstimate(
            flops=8 * tokens * tokens * 256 * heads,
            bytes_accessed=20 * tokens * width,
            transcendentals=tokens * tokens * heads // 2,
        ),
        name="attend_backward",
    )(*operands)


class Gathered:
    def __init__(self, arrays, sources, place, sizes):
        self.arrays, self.sources, self.place = arrays, sources, place
        self.rows_z, self.rows_piece, self.up_wide, self.width, self.fold, self.half_cols = sizes

    def parts(self, kind):
        result = []
        for source in self.sources:
            place = source[5]
            if kind == "up":
                result.append((source, (0, self.up_wide), self.rows_z, self.rows_piece, place))
            elif kind == "out":
                columns = (self.up_wide, self.width)
                result.append((source, columns, self.rows_z, self.rows_piece, place))
            else:
                for number in range(self.fold):
                    columns = (self.up_wide + (1 + number) * self.width, self.width)
                    chip_rows = self.rows_piece * self.fold
                    start = place + number * self.rows_piece
                    result.append((source, columns, self.half_cols, chip_rows, start))
        return result

    def shape(self, kind):
        planes = self.width // self.rows_z
        if kind == "down":
            return (planes * self.half_cols, self.width)
        return (self.width, self.up_wide if kind == "up" else self.width)

    def call(self, body, kind, own, operands, outputs, grid, scratch=(), name=None):
        parts = self.parts(kind)
        plane_rows = own.shape[0]
        count = len(self.arrays)

        def kernel(place_ref, own_ref, *refs):
            piece_refs = refs[:count]
            operand_refs = refs[count : count + len(operands)]
            rest = refs[count + len(operands) :]
            output_refs, written_ref = rest[: len(outputs)], rest[len(outputs)]
            weight_ref, semaphores, *extra = rest[len(outputs) + 1 :]
            write = pltpu.make_async_copy(weight_ref, written_ref, semaphores.at[len(parts) + 1])

            @pl.when(pl.program_id(0) == 0)
            def _():
                shard, chip = place_ref[0], place_ref[1]
                first = pl.multiple_of(shard * plane_rows, plane_rows)
                target = weight_ref.at[pl.ds(first, plane_rows), :]
                copies = [pltpu.make_async_copy(own_ref, target, semaphores.at[0])]
                for number, (source, columns, rows_plane, rows_chip, start) in enumerate(parts):
                    array, row, rows, plane, far, _ = source
                    first = (shard ^ plane) * rows_plane + (chip ^ far) * rows_chip + start
                    target = weight_ref.at[pl.ds(pl.multiple_of(first, 16), rows), :]
                    block = piece_refs[array].at[pl.ds(row, rows), pl.ds(*columns)]
                    copies.append(pltpu.make_async_copy(block, target, semaphores.at[number + 1]))
                for copy in copies:
                    copy.start()
                for copy in copies:
                    copy.wait()
                write.start()

            body(operand_refs, output_refs, weight_ref, extra)

            @pl.when(pl.program_id(0) == grid[0] - 1)
            def _():
                write.wait()

        anywhere = pl.BlockSpec(memory_space=pl.ANY)
        return pl.pallas_call(
            kernel,
            grid=grid,
            in_specs=[scalar_spec()] + [anywhere] * (1 + count) + [spec for _, spec in operands],
            out_specs=[spec for _, _, spec in outputs] + [anywhere],
            out_shape=[jax.ShapeDtypeStruct(shape, kind_of) for shape, kind_of, _ in outputs]
            + [jax.ShapeDtypeStruct(self.shape(kind), bf16)],
            scratch_shapes=[
                pltpu.VMEM(self.shape(kind), bf16),
                pltpu.SemaphoreType.DMA((len(parts) + 2,)),
                *scratch,
            ],
            compiler_params=pltpu.CompilerParams(
                dimension_semantics=("arbitrary",), vmem_limit_bytes=40 * 1024 * 1024
            ),
            cost_estimate=pl.CostEstimate(flops=1, bytes_accessed=1, transcendentals=0),
            name=name,
        )(self.place, own, *self.arrays, *[operand for operand, _ in operands])


def block_spec(shape, place):
    return pl.BlockSpec(shape, place)


def out_projection(gathered, own, attended, inputs, bias, gain, shift):
    rows, width = attended.shape
    tile = rows // 2

    def body(operands, outputs, weight, extra):
        attended_ref, inputs_ref, bias_ref, gain_ref, shift_ref = operands
        residual = inputs_ref[...] + dot(attended_ref[...], weight[...]) + bias_ref[...]
        normed, inv_std = norm_parts(residual)
        outputs[0][...] = residual
        outputs[1][...] = normed
        outputs[2][...] = inv_std
        outputs[3][...] = (normed * gain_ref[...] + shift_ref[...]).astype(bf16)

    by_rows = block_spec((tile, width), lambda step: (step, 0))
    return gathered.call(
        body,
        "out",
        own,
        [(attended, by_rows), (inputs, by_rows)]
        + [(vector.reshape(1, width), whole_spec((1, width))) for vector in (bias, gain, shift)],
        [
            ((rows, width), f32, by_rows),
            ((rows, width), f32, by_rows),
            ((rows, 1), f32, block_spec((tile, 1), lambda step: (step, 0))),
            ((rows, width), bf16, by_rows),
        ],
        (2,),
        name="out_projection",
    )


def up_projection(gathered, own, act_own, act_other, bias):
    rows, width = act_own.shape
    breadth = own.shape[1]
    tile = min(512, breadth)

    def body(operands, outputs, weight, extra):
        first = pl.multiple_of(pl.program_id(0) * tile, tile)
        block = weight[:, pl.ds(first, tile)]
        part = rows // 2
        for number in range(4):
            act = operands[number // 2][(number % 2) * part : (number % 2 + 1) * part, :]
            pre_act = dot(act, block) + operands[2][...]
            square = pre_act * pre_act
            curve = jnp.tanh(pre_act * (gelu_root + gelu_root * gelu_cubic * square))
            inner = pre_act * (0.5 * gelu_root + 1.5 * gelu_root * gelu_cubic * square)
            share = 0.5 + 0.5 * curve
            place = slice(number * part, (number + 1) * part)
            outputs[0][place, :] = (pre_act * share).astype(bf16)
            outputs[1][place, :] = (share + inner * (1.0 - curve * curve)).astype(bf16)

    by_columns = block_spec((2 * rows, tile), lambda step: (0, step))
    return gathered.call(
        body,
        "up",
        own,
        [
            (act_own, whole_spec((rows, width))),
            (act_other, whole_spec((rows, width))),
            (bias.reshape(1, breadth), block_spec((1, tile), lambda step: (0, step))),
        ],
        [((2 * rows, breadth), bf16, by_columns), ((2 * rows, breadth), bf16, by_columns)],
        (breadth // tile,),
        name="up_projection",
    )


def hidden_backward(gathered, own, cot_own, cot_other, slopes):
    rows, width = cot_own.shape
    breadth = slopes.shape[1]
    tile = min(512, breadth)

    def body(operands, outputs, weight, extra):
        first = pl.multiple_of(pl.program_id(0) * tile, tile)
        block = weight[pl.ds(first, tile), :]
        total = jnp.zeros((1, tile), f32)
        for number in range(2):
            part = slice(number * rows, (number + 1) * rows)
            grads = dot_right(operands[number][...], block) * operands[2][part, :].astype(f32)
            grads = grads.astype(bf16)
            outputs[0][part, :] = grads
            total = total + jnp.sum(grads.astype(f32), axis=0, keepdims=True)
        outputs[1][...] = total

    by_columns = block_spec((2 * rows, tile), lambda step: (0, step))
    return gathered.call(
        body,
        "down",
        own,
        [
            (cot_own, whole_spec((rows, width))),
            (cot_other, whole_spec((rows, width))),
            (slopes, by_columns),
        ],
        [
            ((2 * rows, breadth), bf16, by_columns),
            ((1, breadth), f32, block_spec((1, tile), lambda step: (0, step))),
        ],
        (breadth // tile,),
        name="hidden_backward",
    )


def up_backward_kernel(grads_ref, weight_ref, result_ref):
    result_ref[...] = dot_right(grads_ref[...], weight_ref[...]).astype(result_ref.dtype)


def up_backward(weight, grads, number, kind_of):
    rows, breadth = grads.shape[0] // 2, grads.shape[1]
    width = weight.shape[0]
    tile = width // 4
    return pl.pallas_call(
        up_backward_kernel,
        grid=(4,),
        in_specs=[
            pl.BlockSpec((rows, breadth), lambda step: (number, 0)),
            pl.BlockSpec((tile, breadth), lambda step: (step, 0)),
        ],
        out_specs=pl.BlockSpec((rows, tile), lambda step: (0, step)),
        out_shape=jax.ShapeDtypeStruct((rows, width), kind_of),
        compiler_params=pltpu.CompilerParams(
            dimension_semantics=("arbitrary",), vmem_limit_bytes=40 * 1024 * 1024
        ),
        cost_estimate=pl.CostEstimate(flops=1, bytes_accessed=1, transcendentals=0),
        name="up_backward",
    )(grads, weight)


def up_gradient_kernel(own_ref, other_ref, grads_ref, result_ref, act_turned):
    rows, width = own_ref.shape
    step = 256

    @pl.when(pl.program_id(0) == 0)
    def _():
        for number, ref in enumerate((own_ref, other_ref)):
            for row in range(0, rows, step):
                first = number * rows + row
                for column in range(0, width, step):
                    block = ref[row : row + step, column : column + step]
                    act_turned[column : column + step, first : first + step] = turned(block).astype(bf16)

    result_ref[...] = dot(act_turned[...], grads_ref[...]).astype(bf16)


def up_gradient(act_own, act_other, grads):
    rows, width = act_own.shape
    breadth = grads.shape[1]
    tile = min(512, breadth)
    return pl.pallas_call(
        up_gradient_kernel,
        grid=(breadth // tile,),
        in_specs=[
            whole_spec((rows, width)),
            whole_spec((rows, width)),
            pl.BlockSpec((2 * rows, tile), lambda step: (0, step)),
        ],
        out_specs=pl.BlockSpec((width, tile), lambda step: (0, step)),
        out_shape=jax.ShapeDtypeStruct((width, breadth), bf16),
        scratch_shapes=[pltpu.VMEM((width, 2 * rows), bf16)],
        compiler_params=pltpu.CompilerParams(
            dimension_semantics=("arbitrary",), vmem_limit_bytes=40 * 1024 * 1024
        ),
        cost_estimate=pl.CostEstimate(flops=1, bytes_accessed=1, transcendentals=0),
        name="up_gradient",
    )(act_own, act_other, grads)


def together(*values):
    return lax.optimization_barrier(tuple(values))


def ordered(own, other, bit, axis=0):
    first = jnp.where(bit == 0, own, other)
    second = jnp.where(bit == 0, other, own)
    return jnp.stack([first, second], axis=axis)


class Moves:
    def __init__(self):
        self.shards = lax.axis_size("shard")
        self.reps = lax.axis_size("rep")
        self.half = self.shards // 2
        self.chips = self.reps // 2
        self.shard = lax.axis_index("shard")
        self.rep = lax.axis_index("rep")
        self.core = self.rep % 2
        self.chip = self.rep // 2
        self.side = self.shard // self.half
        self.member = self.shard % self.half + self.core * self.half

    def core_swap(self, part):
        return lax.ppermute(part, "rep", [(r, r ^ 1) for r in range(self.reps)])

    def chip_swap(self, part, bits):
        return lax.ppermute(part, "rep", [(r, r ^ (2 * bits)) for r in range(self.reps)])

    def shard_swap(self, part, bits):
        return lax.ppermute(part, "shard", [(s, s ^ bits) for s in range(self.shards)])

    def shard_bit(self, bits):
        return (self.shard // bits) % 2

    def low_bits(self):
        bits, result = 1, []
        while bits < self.half:
            result.append(bits)
            bits *= 2
        return result

    def home_swap(self, part):
        pairs = []
        for rep in range(self.reps):
            for shard in range(self.shards):
                side, core = shard // self.half, rep % 2
                to_rep, to_shard = rep, shard
                if side != core:
                    to_rep = rep ^ 1
                    to_shard = (shard + self.half) % self.shards
                pairs.append((rep * self.shards + shard, to_rep * self.shards + to_shard))
        return lax.ppermute(part, ("rep", "shard"), pairs)

    def half_gather(self, part):
        stack = part[None]
        for bits in self.low_bits():
            own = stack
            stack = ordered(own, self.shard_swap(own, bits), self.shard_bit(bits))
            stack = stack.reshape((-1,) + part.shape)
        return stack

    def cores_gather(self, stack):
        stack = ordered(stack, self.core_swap(stack), self.core)
        return stack.reshape((-1,) + stack.shape[2:])

    def exchange_bit(self, stack, bit, swap):
        sources, targets = stack.shape[:2]
        stack = stack.reshape((sources, 2, targets // 2) + stack.shape[2:])
        own, other = pick(stack, bit, 1), swap(pick(stack, 1 - bit, 1))
        return ordered(own, other, bit, 1).reshape((2 * sources,) + own.shape[1:])

    def half_exchange(self, stack):
        stack = stack[None]
        for bits in reversed(self.low_bits()):
            swap = functools.partial(self.shard_swap, bits=bits)
            stack = self.exchange_bit(stack, self.shard_bit(bits), swap)
        return stack.reshape((self.half,) + stack.shape[2:])

    def cores_exchange(self, stack):
        return self.exchange_bit(stack[None], self.core, self.core_swap)

    def members_exchange(self, stack):
        for bits in reversed(self.low_bits()):
            swap = functools.partial(self.shard_swap, bits=bits)
            stack = self.exchange_bit(stack, self.shard_bit(bits), swap)
        return stack.reshape((self.shards,) + stack.shape[2:])

    def reduce_bit(self, stack, bit, swap):
        stack = stack.reshape((2, stack.shape[0] // 2) + stack.shape[1:])
        other = swap(pick(stack, 1 - bit).astype(bf16))
        return pick(stack, bit).astype(f32) + other.astype(f32)

    def spread_open(self, part):
        if self.chips == 4:
            return (self.chip_swap(part, 1), self.chip_swap(part, 2))
        held, bits = [part], 1
        while bits < self.chips:
            held = held + [self.chip_swap(piece, bits) for piece in held]
            bits *= 2
        return tuple(held[1:])

    def spread_close(self, state):
        if self.chips == 4:
            by_x, by_y = state
            cut, axis = by_x.shape[-2] // 2, by_x.ndim - 2
            far = [
                self.chip_swap(by_x[..., :cut, :], 2),
                self.chip_swap(by_y[..., cut:, :], 1),
            ]
            return (by_x, by_y, jnp.concatenate(far, axis=axis))
        return state

    def far_open(self, states):
        if self.chips != 4:
            return ()
        cut = states[0][0].shape[0] // 2
        return (
            self.chip_swap(jnp.concatenate([by_x[:cut] for by_x, _ in states], axis=0), 2),
            self.chip_swap(jnp.concatenate([by_y[cut:] for _, by_y in states], axis=0), 1),
        )

    def far_parts(self, states, far):
        if self.chips != 4:
            return [[(k + 1, 0, part) for k, part in enumerate(state)] for state in states]
        cut = states[0][0].shape[0] // 2
        result = []
        for number, (by_x, by_y) in enumerate(states):
            rows = slice(number * cut, (number + 1) * cut)
            result.append([(1, 0, by_x), (2, 0, by_y), (3, 0, far[0][rows]), (3, cut, far[1][rows])])
        return result

    def chips_gather(self, part, axis, state=None):
        shape = part.shape[:axis] + (self.chips,) + part.shape[axis:]
        stack = place(jnp.zeros(shape, part.dtype), part, self.chip, axis)
        others = self.spread_close(self.spread_open(part) if state is None else state)
        for number, piece in enumerate(others):
            stack = place(stack, piece, self.chip ^ (number + 1), axis)
        return stack

    def reduce_open(self, stack, axis):
        return self.reduce_start(self.reduce_cut(stack, axis), axis)

    def reduce_cut(self, stack, axis):
        if self.chips != 4:
            return (stack,)
        shape = stack.shape[:axis] + (2, 2) + stack.shape[axis + 1 :]
        stack = stack.reshape(shape)
        bit_x, bit_y = self.chip % 2, self.chip // 2
        cut = shape[0] // 2
        first, second = stack[:cut], stack[cut:]
        return (
            pick(first, bit_x, axis + 1),
            pick(second, bit_y, axis),
            pick(first, 1 - bit_x, axis + 1),
            pick(second, 1 - bit_y, axis),
        )

    def reduce_start(self, parts, axis):
        if self.chips == 4:
            first, second, send_first, send_second = parts
            return (first, second, self.chip_swap(send_first, 1), self.chip_swap(send_second, 2))
        (stack,) = parts
        count = self.chips
        stack = stack.astype(f32)
        while count > 1:
            count //= 2
            shape = stack.shape[:axis] + (2, count) + stack.shape[axis + 1 :]
            stack = stack.reshape(shape)
            bit = (self.chip // count) % 2
            got = self.chip_swap(pick(stack, 1 - bit, axis).astype(bf16), count)
            stack = pick(stack, bit, axis) + got.astype(f32)
        return (pick(stack, 0, axis).astype(bf16),)

    def reduce_add(self, state):
        if self.chips != 4:
            return state
        first, second, got_first, got_second = state
        first = (first.astype(f32) + got_first.astype(f32)).astype(bf16)
        second = (second.astype(f32) + got_second.astype(f32)).astype(bf16)
        return (first, second)

    def reduce_send(self, state, axis):
        if self.chips != 4:
            return state
        first, second = state
        bit_x, bit_y = self.chip % 2, self.chip // 2
        got_first = self.chip_swap(pick(first, 1 - bit_y, axis), 2)
        got_second = self.chip_swap(pick(second, 1 - bit_x, axis), 1)
        return (pick(first, bit_y, axis), pick(second, bit_x, axis), got_first, got_second)

    def reduce_final(self, state):
        if self.chips != 4:
            return state[0]
        first, second, got_first, got_second = state
        first = first.astype(f32) + got_first.astype(f32)
        second = second.astype(f32) + got_second.astype(f32)
        return jnp.concatenate([first, second], axis=0).astype(bf16)

    def reduce_close(self, state, axis):
        return self.reduce_final(self.reduce_send(state, axis))

    def core_pair(self, part):
        other = self.core_swap(part)
        first = jnp.where(self.core == 0, part, other)
        second = jnp.where(self.core == 0, other, part)
        return first, second

    def sum_reps(self, vector):
        bits = 1
        while bits < self.reps:
            vector = vector + lax.ppermute(vector, "rep", [(r, r ^ bits) for r in range(self.reps)])
            bits *= 2
        return vector

    def sum_shards(self, vector):
        bits = 1
        while bits < self.shards:
            vector = vector + self.shard_swap(vector, bits)
            bits *= 2
        return vector


def stats_kernel(decay_rate, gradient_ref, old_ref, rows_ref, lane_rows_ref, sums_ref, total_ref, partial):
    step = pl.program_id(0)
    rows, columns = gradient_ref.shape

    @pl.when(step == 0)
    def _():
        partial[...] = jnp.zeros_like(partial)
        total_ref[...] = jnp.zeros_like(total_ref)

    gradient = gradient_ref[...].astype(f32)
    square = gradient * gradient
    row_mean = jnp.sum(square, axis=1, keepdims=True) / columns
    old = jnp.transpose(jnp.broadcast_to(old_ref[...], (128, rows)))[:, 0:1]
    rows_new = decay_rate * old + (1.0 - decay_rate) * (row_mean + eps_second)
    rows_ref[...] = rows_new
    lane_rows_ref[...] = jnp.transpose(jnp.broadcast_to(rows_new, (rows, 128)))[0:1, :]
    total_ref[...] += jnp.broadcast_to(jnp.sum(rows_new, axis=0, keepdims=True), (1, 128))
    partial[0:8, :] += eights(square, jnp.sum)
    partial[8:16, :] += eights(square * (1.0 / rows_new), jnp.sum)

    @pl.when(step == pl.num_programs(0) - 1)
    def _():
        sums_ref[0:1, :] = jnp.sum(partial[0:8, :], axis=0, keepdims=True)
        sums_ref[1:2, :] = jnp.sum(partial[8:16, :], axis=0, keepdims=True)


def factor_stats(gradient, rows_old, decay_rate):
    height, breadth = gradient.shape
    rows = min(128, height)
    return pl.pallas_call(
        functools.partial(stats_kernel, decay_rate),
        grid=(height // rows,),
        in_specs=[
            pl.BlockSpec((rows, breadth), lambda step: (step, 0)),
            pl.BlockSpec((1, rows), lambda step: (0, step)),
        ],
        out_specs=[
            pl.BlockSpec((rows, 1), lambda step: (step, 0)),
            pl.BlockSpec((1, rows), lambda step: (0, step)),
            pl.BlockSpec((2, breadth), lambda step: (0, 0)),
            pl.BlockSpec((1, 128), lambda step: (0, 0)),
        ],
        out_shape=[
            jax.ShapeDtypeStruct((height, 1), f32),
            jax.ShapeDtypeStruct((1, height), f32),
            jax.ShapeDtypeStruct((2, breadth), f32),
            jax.ShapeDtypeStruct((1, 128), f32),
        ],
        scratch_shapes=[pltpu.VMEM((16, breadth), f32)],
        compiler_params=pltpu.CompilerParams(
            dimension_semantics=("arbitrary",), vmem_limit_bytes=32 * 1024 * 1024
        ),
        name="factor_stats",
    )(gradient, rows_old)


def apply_kernel(
    decay_rate,
    height,
    gradient_ref,
    weight_ref,
    rows_ref,
    sums_ref,
    scalar_ref,
    old_ref,
    gradient_out,
    weight_out,
    copy_out,
    cols_out,
    rms_out,
    col_factor,
):
    columns = gradient_ref.shape[1]

    @pl.when(pl.program_id(0) == 0)
    def _():
        cols_new = decay_rate * old_ref[...] + (1.0 - decay_rate) * (
            sums_ref[0:1, :] / height + eps_second
        )
        row_mean = scalar_ref[0:1, 0:1] / height
        weight_mean = scalar_ref[1:2, 0:1] / (height * columns)
        scaled = jnp.sum(sums_ref[1:2, :] / cols_new, axis=1, keepdims=True)
        rms_update = jnp.sqrt(row_mean / (height * columns) * scaled)
        factor = rate_step * jnp.sqrt(weight_mean) * jnp.sqrt(row_mean)
        factor = factor / jnp.maximum(1.0, rms_update / clip_level)
        col_factor[...] = factor * lax.rsqrt(cols_new)
        cols_out[...] = cols_new
        rms_out[...] = jnp.broadcast_to(rms_update, (1, 128))

    gradient = gradient_ref[...].astype(f32)
    new_weight = weight_ref[...] - gradient * lax.rsqrt(rows_ref[...]) * col_factor[...]
    gradient_out[...] = gradient
    weight_out[...] = new_weight
    copy_out[...] = new_weight.astype(bf16)


def factor_apply(gradient, weight, rows_new, sums, scalars, cols_old, height, decay_rate):
    own_height, breadth = gradient.shape
    rows = min(64, own_height)

    def rows_spec():
        return pl.BlockSpec((rows, breadth), lambda step: (step, 0))

    def row_spec(count, wide):
        return pl.BlockSpec((count, wide), lambda step: (0, 0))

    return pl.pallas_call(
        functools.partial(apply_kernel, decay_rate, height),
        grid=(own_height // rows,),
        in_specs=[
            rows_spec(),
            rows_spec(),
            pl.BlockSpec((rows, 1), lambda step: (step, 0)),
            row_spec(2, breadth),
            row_spec(2, 128),
            row_spec(1, breadth),
        ],
        out_specs=[rows_spec(), rows_spec(), rows_spec(), row_spec(1, breadth), row_spec(1, 128)],
        out_shape=[
            jax.ShapeDtypeStruct((own_height, breadth), f32),
            jax.ShapeDtypeStruct((own_height, breadth), f32),
            jax.ShapeDtypeStruct((own_height, breadth), bf16),
            jax.ShapeDtypeStruct((1, breadth), f32),
            jax.ShapeDtypeStruct((1, 128), f32),
        ],
        scratch_shapes=[pltpu.VMEM((1, breadth), f32)],
        compiler_params=pltpu.CompilerParams(
            dimension_semantics=("arbitrary",), vmem_limit_bytes=32 * 1024 * 1024
        ),
        name="factor_apply",
    )(gradient, weight, rows_new, sums, scalars, cols_old)


def summed(moves, entries):
    total = moves.sum_shards(jnp.concatenate(entries, axis=1))
    result, offset = [], 0
    for entry in entries:
        result.append(total[:, offset : offset + entry.shape[1]])
        offset += entry.shape[1]
    return result


def on_device(
    tokens,
    cotangent,
    seq_lengths,
    qkv_weight,
    out_weight,
    up_weight,
    down_weight,
    vectors,
    row_state,
    down_rows,
    col_state,
    vector_state,
):
    moves = Moves()
    shards, half, chips, core = moves.shards, moves.half, moves.chips, moves.core
    row_count, width = tokens.shape
    hidden_width = up_weight.shape[1]
    group_rows = row_count * shards
    heads = HEADS // shards
    head_width = width // HEADS
    span = heads * head_width
    member = moves.member
    decay_rate = 1.0 - STEP ** (-0.8)
    head_number = (member * heads + jnp.arange(heads, dtype=jnp.int32)).astype(f32)
    slopes = jnp.exp2(-8.0 * (head_number + 1.0) / HEADS)

    gain_one = vectors[0:width]
    shift_one = vectors[width : 2 * width]
    bias_query = vectors[2 * width : 3 * width]
    bias_value = vectors[3 * width : 4 * width]
    bias_out = vectors[4 * width : 5 * width]
    gain_two = vectors[5 * width : 6 * width]
    shift_two = vectors[6 * width : 7 * width]
    bias_up = vectors[7 * width : 7 * width + hidden_width]
    bias_down = vectors[7 * width + hidden_width :]

    home_tokens = moves.home_swap(tokens)
    other_lengths = moves.core_swap(seq_lengths)
    lengths = jnp.where(moves.side == core, seq_lengths, other_lengths)[0]
    plan = block_plan(lengths, group_rows, BLOCK)
    rows_z = width // shards
    rows_piece = rows_z // chips
    my_rows = lax.dynamic_slice_in_dim(qkv_weight, moves.chip * rows_piece, rows_piece, 0)
    my_rows = my_rows.astype(bf16)
    my_blocks = []
    for number in range(half):
        kinds = []
        for kind in range(3):
            first = kind * width + number * span
            second = first + half * span
            kinds.append(
                jnp.where(
                    core == 0, my_rows[:, first : first + span], my_rows[:, second : second + span]
                )
            )
        my_blocks.append(jnp.concatenate(kinds, axis=1))
    qkv_part = moves.half_exchange(jnp.stack(my_blocks))
    qkv_part, up_weight, out_weight, down_weight = together(
        qkv_part, up_weight, out_weight, down_weight
    )
    qkv_part = ordered(qkv_part, moves.shard_swap(qkv_part, half), moves.side)
    qkv_part = qkv_part.reshape(shards, rows_piece, 3 * span)
    qkv_open = moves.spread_open(qkv_part)
    half_cols = hidden_width // (2 * shards)
    up_wide = shards * half_cols
    out_wide = width // 2
    down_piece = half_cols // chips

    def core_half(values):
        parts = []
        for number in range(shards):
            start = 2 * number * half_cols
            first = values[..., start : start + half_cols]
            second = values[..., start + half_cols : start + 2 * half_cols]
            parts.append(jnp.where(core == 0, first, second))
        return jnp.concatenate(parts, axis=-1)

    up_own = core_half(up_weight).astype(bf16)
    out_own = out_weight.astype(bf16)
    down_own = lax.dynamic_slice_in_dim(down_weight, core * half_cols, half_cols, 0).astype(bf16)
    fold = down_piece // rows_piece
    my_down = lax.dynamic_slice_in_dim(down_own, moves.chip * down_piece, down_piece, 0)
    weight_piece = jnp.concatenate(
        [
            lax.dynamic_slice_in_dim(own, moves.chip * rows_piece, rows_piece, 0)
            for own in (up_own, out_own)
        ]
        + [my_down[k * rows_piece : (k + 1) * rows_piece] for k in range(fold)],
        axis=1,
    )
    near_pieces, bits = [weight_piece], 1
    while bits < half:
        near_pieces = near_pieces + [moves.shard_swap(piece, bits) for piece in near_pieces]
        bits *= 2
    near_pieces = near_pieces[1:]
    weights = [qkv_weight, out_weight, up_weight, down_weight]
    weight_sums = [jnp.sum(weight * weight) for weight in weights]
    rows_old = [row_state[k : k + 1] for k in range(3)] + [down_rows.reshape(1, -1)]
    home_tokens, qkv_open, near_pieces, weight_piece, weight_sums, rows_old, plan = together(
        home_tokens, qkv_open, near_pieces, weight_piece, weight_sums, rows_old, plan
    )
    qkv_cols = moves.chips_gather(qkv_part, 1, qkv_open).reshape(width, 3 * span)
    far_piece = moves.shard_swap(weight_piece, half)
    near_open = [moves.spread_open(piece) for piece in near_pieces]
    inputs = home_tokens.astype(f32)
    normed_one, inv_std_one = norm_parts(inputs)
    act_one = (normed_one * gain_one + shift_one).astype(bf16)
    act_half = moves.half_gather(act_one)

    act_half, qkv_cols, far_piece, near_open, cotangent = together(
        act_half, qkv_cols, far_piece, near_open, cotangent
    )
    home_cot = moves.home_swap(cotangent)
    act_all = moves.cores_gather(act_half).reshape(group_rows, width)
    far_open = moves.spread_open(far_piece)
    far_pieces, bits = [far_piece], 1
    while bits < half:
        far_pieces = far_pieces + [moves.shard_swap(piece, bits) for piece in far_pieces]
        bits *= 2
    far_pieces = far_pieces[1:]

    bias_q_part = lax.dynamic_slice_in_dim(bias_query, member * span, span)
    bias_v_part = lax.dynamic_slice_in_dim(bias_value, member * span, span)
    qkv_bias = jnp.concatenate([bias_q_part, jnp.zeros_like(bias_q_part), bias_v_part])
    qkv_rows = (dot(act_all, qkv_cols) + qkv_bias).astype(bf16)
    attended_cols, logs = attend_forward(qkv_rows, plan, slopes, heads, BLOCK)
    attended_cols, far_open, far_pieces, home_cot = together(
        attended_cols, far_open, far_pieces, home_cot
    )
    attended_parts = moves.cores_exchange(attended_cols.reshape(shards, row_count, span))
    attended_parts = moves.members_exchange(attended_parts)
    first_states = near_open + [far_open]
    first_far = moves.far_open(first_states)
    last_states = [moves.spread_open(piece) for piece in far_pieces]
    attended_parts, first_far, last_states, home_cot = together(
        attended_parts, first_far, last_states, home_cot
    )
    last_far = moves.far_open(last_states)
    attended = jnp.concatenate([attended_parts[k] for k in range(shards)], axis=1)

    pieces = near_pieces + [far_piece] + far_pieces
    arrays = list(pieces)
    sources = [(k, 0, rows_piece, k + 1, 0, 0) for k in range(len(pieces))]
    for first_plane, states, far in ((1, first_states, first_far), (half + 1, last_states, last_far)):
        cut = rows_piece // 2
        for way, array in enumerate(far):
            for k in range(len(states)):
                sources.append((len(arrays), k * cut, cut, first_plane + k, 3, way * cut))
            arrays.append(array)
        for k, state in enumerate(states):
            for way, array in enumerate(state):
                sources.append((len(arrays), 0, rows_piece, first_plane + k, way + 1, 0))
                arrays.append(array)
    place_now = jnp.stack([moves.shard, moves.chip]).astype(jnp.int32)
    sizes = (rows_z, rows_piece, up_wide, width, fold, half_cols)
    gathered = Gathered(arrays, sources, place_now, sizes)
    residual, normed_two, inv_std_two, act_two, out_low = out_projection(
        gathered, out_own, attended, inputs, bias_out, gain_two, shift_two
    )

    act_two_other, attended_other, cot_other = together(
        moves.core_swap(act_two), moves.core_swap(attended), moves.core_swap(home_cot)
    )
    cot_pair = jnp.concatenate([home_cot, cot_other], axis=0)
    attended_pair = jnp.concatenate([attended, attended_other], axis=0)
    hidden_pair, slope_pair, up_half = up_projection(
        gathered, up_own, act_two, act_two_other, core_half(bias_up)
    )
    down_terms = dot_rows(hidden_pair, cot_pair).astype(bf16)
    down_state = moves.reduce_cut(down_terms.reshape(shards, chips, down_piece, width), 1)
    slope_pair, down_state = together(slope_pair, down_state)
    down_state = moves.reduce_start(down_state, 1)
    grad_y = home_cot.astype(f32)
    grad_bias_down = jnp.sum(grad_y, axis=0)
    grad_up_pair, grad_bias_up, down_half = hidden_backward(
        gathered, down_own, home_cot, cot_other, slope_pair
    )
    grad_bias_up = grad_bias_up.reshape(-1)
    back_other = moves.core_swap(up_backward(up_half, grad_up_pair, 1, bf16))
    up_terms = up_gradient(act_two, act_two_other, grad_up_pair)
    back_other, hidden_pair, up_terms, down_state = together(
        back_other, hidden_pair, up_terms, down_state
    )
    up_state = moves.reduce_open(up_terms.reshape(shards, chips, rows_piece, up_wide), 1)
    down_mid = moves.reduce_close(moves.reduce_add(down_state), 1)
    grad_act_two = up_backward(up_half, grad_up_pair, 0, f32) + back_other.astype(f32)
    grad_gain_two = jnp.sum(grad_act_two * normed_two, axis=0)
    grad_shift_two = jnp.sum(grad_act_two, axis=0)
    grad_residual = grad_y + norm_back(grad_act_two, normed_two, inv_std_two, gain_two)
    grad_attn = grad_residual.astype(bf16)
    grad_bias_out = jnp.sum(grad_attn, axis=0, dtype=f32)
    to_members = jnp.stack(
        [
            dot_right(grad_attn, out_low[k * span : (k + 1) * span]).astype(bf16)
            for k in range(shards)
        ]
    )
    attn_halves = [grad_attn[:, :out_wide], grad_attn[:, out_wide:]]
    attn_own = jnp.where(core == 0, attn_halves[0], attn_halves[1])
    attn_other = jnp.where(core == 0, attn_halves[1], attn_halves[0])
    grad_heads, attn_other = together(moves.cores_exchange(to_members), moves.core_swap(attn_other))
    attn_pair = jnp.concatenate([attn_own, attn_other], axis=0)
    grad_heads, hidden_pair = together(grad_heads, hidden_pair)
    grad_heads = moves.members_exchange(grad_heads).reshape(group_rows, span)
    down_other = moves.core_swap(dot(hidden_pair[row_count:], down_half).astype(bf16))
    block_out = (
        residual + dot(hidden_pair[:row_count], down_half) + down_other.astype(f32) + bias_down
    ).astype(bf16)

    out_terms = dot_rows(attended_pair, attn_pair).astype(bf16)
    def shards_halve(piece, bits):
        piece = piece.reshape((piece.shape[0] // 2, 2) + piece.shape[1:])
        bit = moves.shard_bit(bits)
        return pick(piece, bit, 1), moves.shard_swap(pick(piece, 1 - bit, 1), bits)

    def halved(state):
        own, other = state
        return (own.astype(f32) + other.astype(f32)).astype(bf16)

    def shards_sum(piece):
        rows = piece.shape[1]
        return lax.psum_scatter(
            piece.reshape(shards * rows, piece.shape[2]), "shard", scatter_dimension=0, tiled=True
        )

    grad_heads, down_mid, out_terms, block_out = together(
        grad_heads, down_mid, out_terms, block_out
    )
    block_out = moves.home_swap(block_out)
    down_owned = shards_sum(down_mid)
    out_state = moves.reduce_open(out_terms.reshape(shards, chips, rows_piece, out_wide), 1)
    attend_args = (plan, slopes)
    parts = 2 if heads % 4 == 0 else 1
    part_heads = heads // parts
    grad_qkv = attend_backward(
        qkv_rows, grad_heads, attended_cols, logs, *attend_args, part_heads, BLOCK, 0, None
    )
    grad_qkv, up_state, out_state = together(grad_qkv, up_state, out_state)
    up_sums, out_sums = moves.reduce_add(up_state), moves.reduce_add(out_state)
    grad_qkv, up_sums, out_sums = together(grad_qkv, up_sums, out_sums)
    up_out_state = [
        jnp.concatenate([up_part, out_part], axis=-1) for up_part, out_part in zip(up_sums, out_sums)
    ]
    if parts == 2:
        grad_qkv = attend_backward(
            qkv_rows, grad_heads, attended_cols, logs, *attend_args, part_heads, BLOCK, part_heads, grad_qkv
        )
    grad_qkv, up_out_state, block_out = together(
        grad_qkv, moves.reduce_send(up_out_state, 1), block_out
    )
    up_out_piece = moves.reduce_final(up_out_state)
    up_out_state = shards_halve(up_out_piece, 1)

    grad_bias_q_part = jnp.sum(grad_qkv[:, :span], axis=0, dtype=f32)
    grad_bias_v_part = jnp.sum(grad_qkv[:, 2 * span :], axis=0, dtype=f32)

    grad_halves = grad_qkv.reshape(2, half * row_count, 3 * span)
    sent = dot_right(pick(grad_halves, 1 - core), qkv_cols).astype(bf16)
    sent = moves.core_swap(sent)
    qkv_terms = dot_rows(act_all, grad_qkv).astype(bf16)
    qkv_terms = qkv_terms.reshape(shards, chips, rows_piece, 3 * span)
    qkv_state = moves.reduce_open(qkv_terms, 1)
    back = dot_right(pick(grad_halves, core), qkv_cols) + sent.astype(f32)
    qkv_state, back, up_out_state = together(qkv_state, back, up_out_state)

    back = back.reshape(half, row_count, width)
    low_bits = list(reversed(moves.low_bits()))
    for bits in low_bits[:-1]:
        back = moves.reduce_bit(
            back, moves.shard_bit(bits), functools.partial(moves.shard_swap, bits=bits)
        )
    back = back.reshape((2, -1) + back.shape[1:])
    back_bit = moves.shard_bit(low_bits[-1])
    back_other = moves.shard_swap(pick(back, 1 - back_bit).astype(bf16), low_bits[-1])
    up_out_piece, bits = halved(up_out_state), 2
    while bits < half:
        up_out_piece = halved(shards_halve(up_out_piece, bits))
        bits *= 2
    up_out_state = shards_halve(up_out_piece, half)
    qkv_state = moves.reduce_send(moves.reduce_add(qkv_state), 1)
    qkv_state, up_out_state = together(qkv_state, up_out_state)

    up_out_owned = halved(up_out_state)[0]
    up_out_state = moves.spread_open(up_out_owned)
    qkv_piece = moves.reduce_final(qkv_state)
    qkv_piece = qkv_piece.reshape((2, half) + qkv_piece.shape[1:])
    qkv_own = pick(qkv_piece, moves.side)
    qkv_other = moves.shard_swap(pick(qkv_piece, 1 - moves.side), half)
    back_other, qkv_other, up_out_state = together(back_other, qkv_other, up_out_state)

    qkv_piece = moves.half_exchange(halved((qkv_own, qkv_other)))
    down_state = moves.spread_open(down_owned)
    grad_act_one = pick(back, back_bit) + back_other.astype(f32)
    grad_act_one = grad_act_one.reshape(row_count, width)
    grad_gain_one = jnp.sum(grad_act_one * normed_one, axis=0)
    grad_shift_one = jnp.sum(grad_act_one, axis=0)
    grad_inputs = grad_residual + norm_back(grad_act_one, normed_one, inv_std_one, gain_one)
    grad_inputs, qkv_piece, down_state = together(grad_inputs.astype(bf16), qkv_piece, down_state)
    tokens_grad = moves.home_swap(grad_inputs)
    qkv_owned = moves.chips_gather(qkv_piece, 1)

    up_out_first, up_out_second = moves.core_pair(
        moves.chips_gather(up_out_owned, 0, tuple(up_out_state)).reshape(rows_z, up_wide + out_wide)
    )
    out_grad = jnp.concatenate([up_out_first[:, up_wide:], up_out_second[:, up_wide:]], axis=1)
    up_columns = []
    for number in range(shards):
        part = slice(number * half_cols, (number + 1) * half_cols)
        up_columns += [up_out_first[:, part], up_out_second[:, part]]
    up_grad = jnp.concatenate(up_columns, axis=1)
    down_first, down_second = moves.core_pair(
        moves.chips_gather(down_owned, 0, tuple(down_state)).reshape(half_cols, width)
    )
    down_grad = jnp.concatenate([down_first, down_second], axis=0)
    qkv_first, qkv_second = moves.core_pair(qkv_owned.reshape(half, rows_z, 3 * span))
    qkv_columns = []
    for kind in range(3):
        for source in (qkv_first, qkv_second):
            for number in range(half):
                qkv_columns.append(source[number][:, kind * span : (kind + 1) * span])
    qkv_grad = jnp.concatenate(qkv_columns, axis=1)

    gradients = [qkv_grad, out_grad, up_grad, down_grad]
    heights = [width, width, width, hidden_width]
    stats = [
        factor_stats(gradient, old, decay_rate) for gradient, old in zip(gradients, rows_old)
    ]

    def to_sum(number):
        weight_sum = jnp.broadcast_to(weight_sums[number], (1, 128))
        return [stats[number][2], jnp.concatenate([stats[number][3], weight_sum], axis=0)]

    def spread_heads(part):
        return [jnp.where(member == number, part, 0.0) for number in range(shards)]

    bias_up_parts = []
    for number in range(shards):
        part = grad_bias_up[number * half_cols : (number + 1) * half_cols]
        bias_up_parts += [jnp.where(core == 0, part, 0.0), jnp.where(core == 1, part, 0.0)]
    vector_part = moves.sum_reps(
        jnp.concatenate(
            [grad_gain_one, grad_shift_one]
            + spread_heads(grad_bias_q_part)
            + spread_heads(grad_bias_v_part)
            + [grad_bias_out, grad_gain_two, grad_shift_two]
            + bias_up_parts
            + [grad_bias_down]
        )
    )
    vector_rows, tokens_grad = together(vector_part.reshape(2, -1), tokens_grad)
    all_sums = summed(moves, to_sum(0) + to_sum(1) + to_sum(2) + to_sum(3) + [vector_rows])
    sums = [all_sums[0:2], all_sums[2:4], all_sums[4:6], all_sums[6:8]]
    vector_grad = all_sums[8].reshape(-1)
    updates = []
    offset = 0
    for number in range(4):
        end_col = offset + gradients[number].shape[1]
        updates.append(
            factor_apply(
                gradients[number],
                weights[number],
                stats[number][0],
                sums[number][0],
                sums[number][1],
                col_state[offset:end_col].reshape(1, -1),
                heights[number],
                decay_rate,
            )
        )
        offset = end_col
    grads_out, new_weights, copies, new_cols, rms_rows = zip(*updates)
    rms_values = [rms[0, 0] for rms in rms_rows]

    vector_state_new = decay_rate * vector_state + (1.0 - decay_rate) * (
        vector_grad * vector_grad + eps_second
    )
    vector_step = vector_grad * lax.rsqrt(vector_state_new)
    vector_rms = jnp.sqrt(jnp.mean(vector_step * vector_step))
    vector_new = vectors - rate_step * jnp.sqrt(
        jnp.mean(vectors * vectors)
    ) * vector_step / jnp.maximum(1.0, vector_rms / clip_level)
    update_rms = jnp.stack(rms_values + [vector_rms])
    return (
        block_out,
        tokens_grad,
        *grads_out,
        vector_grad,
        *new_weights,
        vector_new,
        *copies,
        jnp.concatenate([stats[0][1], stats[1][1], stats[2][1]], axis=0),
        stats[3][1].reshape(-1),
        jnp.concatenate(new_cols, axis=1).reshape(-1),
        vector_state_new,
        update_rms,
    )


def solution(mesh):
    in_specs = (
        P(("rep", "shard"), None),
        P(("rep", "shard"), None),
        P("rep", None),
        P("shard", None),
        P("shard", None),
        P("shard", None),
        P("shard", None),
        P(),
        P(None, "shard"),
        P("shard"),
        P(),
        P(),
    )
    out_specs = (
        P(("rep", "shard"), None),
        P(("rep", "shard"), None),
        P("shard", None),
        P("shard", None),
        P("shard", None),
        P("shard", None),
        P(),
        P("shard", None),
        P("shard", None),
        P("shard", None),
        P("shard", None),
        P(),
        P("shard", None),
        P("shard", None),
        P("shard", None),
        P("shard", None),
        P(None, "shard"),
        P("shard"),
        P(),
        P(),
        P(),
    )
    return jax.shard_map(
        on_device, mesh=mesh, in_specs=in_specs, out_specs=out_specs, check_vma=False
    )
```

```python
import functools

import jax
import jax.numpy as jnp
from jax import lax
from jax.experimental import pallas as pl
from jax.experimental.pallas import tpu as pltpu
from jax.sharding import PartitionSpec as P

HEADS = 16
STEP = 10
BLOCK = 256


eps_norm = 1e-05
eps_second = 1e-30
rate_step = 0.5
clip_level = 1.0
masked = -1e30
gelu_root = (2.0 / 3.141592653589793) ** 0.5
gelu_cubic = 0.044715

f32 = jnp.float32
bf16 = jnp.bfloat16


def norm_parts(values):
    average = jnp.mean(values, axis=-1, keepdims=True)
    centred = values - average
    inv_std = lax.rsqrt(jnp.mean(centred * centred, axis=-1, keepdims=True) + eps_norm)
    return (centred * inv_std, inv_std)


def norm_back(grad_out, normed, inv_std, gain_vec):
    grad_normed = grad_out * gain_vec
    inner_mean = jnp.mean(grad_normed * normed, axis=-1, keepdims=True)
    centred = grad_normed - jnp.mean(grad_normed, axis=-1, keepdims=True)
    return (centred - normed * inner_mean) * inv_std


def gelu_value(pre_act):
    curve = jnp.tanh(gelu_root * (pre_act + gelu_cubic * pre_act * pre_act * pre_act))
    return 0.5 * pre_act * (1.0 + curve)


def gelu_slope(pre_act):
    square = pre_act * pre_act
    curve = jnp.tanh(gelu_root * (pre_act + gelu_cubic * square * pre_act))
    inner = gelu_root * (1.0 + 3.0 * gelu_cubic * square)
    return 0.5 * (1.0 + curve) + 0.5 * pre_act * (1.0 - curve * curve) * inner


def dot(left_side, right_side):
    return jnp.dot(left_side, right_side, preferred_element_type=f32)


def dot_right(left_side, right_side):
    return lax.dot_general(
        left_side, right_side, (((1,), (1,)), ((), ())), preferred_element_type=f32
    )


def dot_rows(left_side, right_side):
    return lax.dot_general(
        left_side, right_side, (((0,), (0,)), ((), ())), preferred_element_type=f32
    )


def pick(stack, index, axis=0):
    return lax.dynamic_index_in_dim(stack, index, axis, keepdims=False)


def place(stack, part, index, axis=0):
    return lax.dynamic_update_index_in_dim(stack, part, index, axis)


def head_rows(number, head_width):
    return slice(number * head_width, (number + 1) * head_width)


def lane_masks(block_rows, width, heads):
    lanes = lax.broadcasted_iota(jnp.int32, (block_rows, width), 1)
    head_width = width // heads
    return [
        (lanes >= number * head_width) & (lanes < (number + 1) * head_width)
        for number in range(heads)
    ]


def allowed_pairs(key_block, query_block, start_row, block):
    key_pos = lax.broadcasted_iota(jnp.int32, (block, block), 0) + key_block * block
    query_pos = lax.broadcasted_iota(jnp.int32, (block, block), 1) + query_block * block
    return (key_pos <= query_pos) & (key_pos >= start_row)


def key_offsets(key_block, query_block, block):
    rows = lax.broadcasted_iota(jnp.int32, (block, 1), 0)
    return (rows + (key_block - query_block) * block).astype(f32)


def turned(values):
    return jnp.transpose(values.astype(f32))


def head_stack(values, lanes):
    zero = jnp.zeros(values.shape, values.dtype)
    return jnp.concatenate([jnp.where(lane, values, zero) for lane in lanes], axis=0)


def eights(values, combine):
    rows, columns = values.shape
    return combine(values.reshape(rows // 8, 8, columns), axis=0)


def forward_kernel(
    heads,
    block,
    low_ref,
    mid_ref,
    slope_ref,
    start_ref,
    qkv_ref,
    out_ref,
    log_ref,
    values_turned,
    key_stack,
    score_ref,
):
    tokens = qkv_ref.shape[0]
    width = qkv_ref.shape[1] // 3
    head_width = width // heads
    blocks = tokens // block
    query_block = pl.program_id(0)

    @pl.when(query_block == 0)
    def _():
        lanes = lane_masks(block, width, heads)
        for number in range(blocks):
            rows = slice(number * block, (number + 1) * block)
            values_turned[number] = turned(qkv_ref[rows, 2 * width :]).astype(bf16)
            key_stack[number] = head_stack(qkv_ref[rows, width : 2 * width], lanes)

    first_row = pl.multiple_of(query_block * block, block)
    queries = qkv_ref[pl.ds(first_row, block), :width].astype(f32) * head_width ** (-0.5)
    queries = turned(queries).astype(bf16)
    start_row = start_ref[query_block]

    def score_step(key_block, bests, with_mask):
        scores = dot(key_stack[key_block], queries)
        offsets = key_offsets(key_block, query_block, block)
        allowed = allowed_pairs(key_block, query_block, start_row, block) if with_mask else None
        result = []
        for number in range(heads):
            rows = head_rows(number, block)
            part = scores[rows] + slope_ref[number] * offsets
            if with_mask:
                part = jnp.where(allowed, part, masked)
            score_ref[key_block, rows, :] = part
            result.append(jnp.maximum(bests[number], eights(part, jnp.max)))
        return tuple(result)

    low, mid = low_ref[query_block], mid_ref[query_block]
    bests = tuple(jnp.full((8, block), masked, f32) for _ in range(heads))
    bests = lax.fori_loop(low, mid, functools.partial(score_step, with_mask=True), bests)
    bests = lax.fori_loop(mid, query_block, functools.partial(score_step, with_mask=False), bests)
    bests = score_step(query_block, bests, True)
    bests = [jnp.max(best, axis=0, keepdims=True) for best in bests]

    def value_step(key_block, state):
        result = []
        for number in range(heads):
            total, gathered = state[2 * number : 2 * number + 2]
            weights = jnp.exp(score_ref[key_block, head_rows(number, block), :] - bests[number])
            value_rows = values_turned[key_block, head_rows(number, head_width), :]
            result += [
                total + eights(weights, jnp.sum),
                gathered + dot(value_rows, weights.astype(bf16)),
            ]
        return tuple(result)

    state = ()
    for number in range(heads):
        state += (jnp.zeros((8, block), f32), jnp.zeros((head_width, block), f32))
    state = lax.fori_loop(low, query_block + 1, value_step, state)
    columns = []
    for number in range(heads):
        total = jnp.sum(state[2 * number], axis=0, keepdims=True)
        columns.append(state[2 * number + 1] / total)
        log_ref[0, number : number + 1, :] = bests[number] + jnp.log(total)
    out_ref[...] = jnp.transpose(jnp.concatenate(columns, axis=0)).astype(bf16)


def backward_kernel(heads, block, first_head, merge, *refs):
    full_ref, high_ref, slope_ref, start_ref, log_ref, qkv_ref, grad_ref, out_ref = refs[:8]
    earlier_ref = refs[8] if merge else None
    result_ref = refs[9 if merge else 8]
    (
        queries_turned,
        grads_turned,
        keys_turned,
        query_stack,
        grad_stack,
        key_stack,
        value_stack,
        delta_rows,
        query_grads,
    ) = refs[10 if merge else 9 :]
    tokens, all_width = grad_ref.shape
    head_width = all_width // log_ref.shape[1]
    width = heads * head_width
    scale = head_width ** (-0.5)
    blocks = tokens // block
    key_block = pl.program_id(0)
    lanes = lane_masks(block, width, heads)

    def columns(kind):
        start = kind * all_width + first_head * head_width
        return slice(start, start + width)

    def target(kind):
        start = (kind * all_width + first_head * head_width) if merge else kind * width
        return slice(start, start + width)

    @pl.when(key_block == 0)
    def _():
        for number in range(blocks):
            rows = slice(number * block, (number + 1) * block)
            queries = qkv_ref[rows, columns(0)]
            queries_turned[number] = turned(queries.astype(f32) * scale).astype(bf16)
            query_stack[number] = head_stack(queries, lanes)
            keys_turned[number] = turned(qkv_ref[rows, columns(1)]).astype(bf16)
            grads = grad_ref[rows, columns(0)]
            grad_stack[number] = head_stack(grads, lanes)
            grads = grads.astype(f32)
            grads_turned[number] = turned(grads).astype(bf16)
            product = turned(grads * out_ref[rows, columns(0)].astype(f32))
            for head in range(heads):
                delta_rows[number, head : head + 1, :] = jnp.sum(
                    product[head_rows(head, head_width)], axis=0, keepdims=True
                )
            query_grads[number] = jnp.zeros((width, block), f32)

    key_row = pl.multiple_of(key_block * block, block)
    key_stack[...] = head_stack(qkv_ref[pl.ds(key_row, block), columns(1)], lanes)
    value_stack[...] = head_stack(qkv_ref[pl.ds(key_row, block), columns(2)], lanes)

    def step(query_block, state, with_mask):
        key_total, value_total = state
        scores = dot(key_stack[...], queries_turned[query_block])
        grad_weights = dot(value_stack[...], grads_turned[query_block])
        offsets = key_offsets(key_block, query_block, block)
        if with_mask:
            allowed = allowed_pairs(key_block, query_block, start_ref[query_block], block)
        weight_list, grad_list = [], []
        for number in range(heads):
            rows = head_rows(number, block)
            head = first_head + number
            part = scores[rows] + slope_ref[head] * offsets
            part = part - log_ref[query_block, head : head + 1, :]
            if with_mask:
                part = jnp.where(allowed, part, masked)
            probabilities = jnp.exp(part)
            delta = delta_rows[query_block, number : number + 1, :]
            grad_scores = (probabilities * (grad_weights[rows] - delta)).astype(bf16)
            weight_list.append(probabilities.astype(bf16))
            grad_list.append(grad_scores)
            rows = head_rows(number, head_width)
            query_grads[query_block, rows, :] += dot(keys_turned[key_block, rows, :], grad_scores)
        weight_row = jnp.concatenate(weight_list, axis=1)
        grad_row = jnp.concatenate(grad_list, axis=1)
        return (
            key_total + dot(grad_row, query_stack[query_block]),
            value_total + dot(weight_row, grad_stack[query_block]),
        )

    state = (jnp.zeros((block, width), f32), jnp.zeros((block, width), f32))
    state = step(key_block, state, True)
    full, high = full_ref[key_block], high_ref[key_block]
    state = lax.fori_loop(key_block + 1, full, functools.partial(step, with_mask=False), state)
    state = lax.fori_loop(full, high, functools.partial(step, with_mask=True), state)
    result_ref[pl.ds(key_row, block), target(1)] = (state[0] * scale).astype(bf16)
    result_ref[pl.ds(key_row, block), target(2)] = state[1].astype(bf16)
    if merge:
        other = first_head * head_width
        for kind in range(3):
            result_ref[pl.ds(key_row, block), kind * all_width : kind * all_width + other] = earlier_ref[
                pl.ds(key_row, block), kind * other : (kind + 1) * other
            ]

    @pl.when(key_block == blocks - 1)
    def _():
        for number in range(blocks):
            rows = slice(number * block, (number + 1) * block)
            result_ref[rows, target(0)] = jnp.transpose(query_grads[number] * scale).astype(bf16)


def block_plan(lengths, tokens, block):
    ends = jnp.cumsum(lengths)
    positions = jnp.arange(tokens, dtype=jnp.int32)
    passed = positions[:, None] >= ends[None, :]
    starts = jnp.max(jnp.where(passed, ends[None, :], 0), axis=1).astype(jnp.int32)
    finish = jnp.min(jnp.where(passed, tokens, ends[None, :]), axis=1).astype(jnp.int32)
    blocks = tokens // block
    number = jnp.arange(blocks, dtype=jnp.int32)
    first_start = starts[::block]
    last_start = starts[block - 1 :: block]
    low = first_start // block
    mid = jnp.clip((last_start + block - 1) // block, low, number)
    high = (finish[block - 1 :: block] - 1) // block + 1
    full = jnp.clip(finish[::block] // block, number + 1, high)
    return (starts.reshape(blocks, 1, block), low, mid, full, high)


def scalar_spec():
    return pl.BlockSpec(memory_space=pltpu.SMEM)


def whole_spec(shape):
    return pl.BlockSpec(shape, lambda step: (0,) * len(shape), pipeline_mode=pl.Buffered(1))


def attend_forward(qkv, plan, slopes, heads, block):
    tokens, triple = qkv.shape
    width = triple // 3
    blocks = tokens // block
    starts, low, mid, full, high = plan
    return pl.pallas_call(
        functools.partial(forward_kernel, heads, block),
        grid=(blocks,),
        in_specs=[
            scalar_spec(),
            scalar_spec(),
            scalar_spec(),
            whole_spec((blocks, 1, block)),
            whole_spec((tokens, triple)),
        ],
        out_specs=[
            pl.BlockSpec((block, width), lambda step: (step, 0)),
            pl.BlockSpec((1, heads, block), lambda step: (step, 0, 0)),
        ],
        out_shape=[
            jax.ShapeDtypeStruct((tokens, width), bf16),
            jax.ShapeDtypeStruct((blocks, heads, block), f32),
        ],
        scratch_shapes=[
            pltpu.VMEM((blocks, width, block), bf16),
            pltpu.VMEM((blocks, heads * block, width), bf16),
            pltpu.VMEM((blocks, heads * block, block), f32),
        ],
        compiler_params=pltpu.CompilerParams(
            dimension_semantics=("arbitrary",), vmem_limit_bytes=24 * 1024 * 1024
        ),
        cost_estimate=pl.CostEstimate(
            flops=3 * tokens * tokens * 256 * heads,
            bytes_accessed=10 * tokens * width,
            transcendentals=tokens * tokens * heads // 2,
        ),
        name="attend_forward",
    )(low, mid, slopes, starts, qkv)


def attend_backward(qkv, grads, outputs, logs, plan, slopes, heads, block, first_head, earlier):
    tokens, triple = qkv.shape
    all_width = triple // 3
    all_heads = logs.shape[1]
    width = all_width // all_heads * heads
    blocks = tokens // block
    starts, low, mid, full, high = plan
    merge = earlier is not None
    result_width = triple if merge else 3 * width
    operands = [full, high, slopes, starts, logs, qkv, grads, outputs]
    specs = [scalar_spec() for _ in range(3)] + [whole_spec(entry.shape) for entry in operands[3:]]
    if merge:
        operands.append(earlier)
        specs.append(whole_spec(earlier.shape))
    return pl.pallas_call(
        functools.partial(backward_kernel, heads, block, first_head, merge),
        grid=(blocks,),
        in_specs=specs,
        out_specs=pl.BlockSpec((tokens, result_width), lambda step: (0, 0)),
        out_shape=jax.ShapeDtypeStruct((tokens, result_width), bf16),
        scratch_shapes=[
            pltpu.VMEM((blocks, width, block), bf16),
            pltpu.VMEM((blocks, width, block), bf16),
            pltpu.VMEM((blocks, width, block), bf16),
            pltpu.VMEM((blocks, heads * block, width), bf16),
            pltpu.VMEM((blocks, heads * block, width), bf16),
            pltpu.VMEM((heads * block, width), bf16),
            pltpu.VMEM((heads * block, width), bf16),
            pltpu.VMEM((blocks, heads, block), f32),
            pltpu.VMEM((blocks, width, block), f32),
        ],
        compiler_params=pltpu.CompilerParams(
            dimension_semantics=("arbitrary",), vmem_limit_bytes=24 * 1024 * 1024
        ),
        cost_estimate=pl.CostEstimate(
            flops=8 * tokens * tokens * 256 * heads,
            bytes_accessed=20 * tokens * width,
            transcendentals=tokens * tokens * heads // 2,
        ),
        name="attend_backward",
    )(*operands)


class Gathered:
    def __init__(self, arrays, sources, place, sizes):
        self.arrays, self.sources, self.place = arrays, sources, place
        self.rows_z, self.rows_piece, self.up_wide, self.width, self.fold, self.half_cols = sizes

    def parts(self, kind):
        result = []
        for source in self.sources:
            place = source[5]
            if kind == "up":
                result.append((source, (0, self.up_wide), self.rows_z, self.rows_piece, place))
            elif kind == "out":
                columns = (self.up_wide, self.width)
                result.append((source, columns, self.rows_z, self.rows_piece, place))
            else:
                for number in range(self.fold):
                    columns = (self.up_wide + (1 + number) * self.width, self.width)
                    chip_rows = self.rows_piece * self.fold
                    start = place + number * self.rows_piece
                    result.append((source, columns, self.half_cols, chip_rows, start))
        return result

    def shape(self, kind):
        planes = self.width // self.rows_z
        if kind == "down":
            return (planes * self.half_cols, self.width)
        return (self.width, self.up_wide if kind == "up" else self.width)

    def call(self, body, kind, own, operands, outputs, grid, scratch=(), name=None):
        parts = self.parts(kind)
        plane_rows = own.shape[0]
        count = len(self.arrays)

        def kernel(place_ref, own_ref, *refs):
            piece_refs = refs[:count]
            operand_refs = refs[count : count + len(operands)]
            rest = refs[count + len(operands) :]
            output_refs, written_ref = rest[: len(outputs)], rest[len(outputs)]
            weight_ref, semaphores, *extra = rest[len(outputs) + 1 :]
            write = pltpu.make_async_copy(weight_ref, written_ref, semaphores.at[len(parts) + 1])

            @pl.when(pl.program_id(0) == 0)
            def _():
                shard, chip = place_ref[0], place_ref[1]
                first = pl.multiple_of(shard * plane_rows, plane_rows)
                target = weight_ref.at[pl.ds(first, plane_rows), :]
                copies = [pltpu.make_async_copy(own_ref, target, semaphores.at[0])]
                for number, (source, columns, rows_plane, rows_chip, start) in enumerate(parts):
                    array, row, rows, plane, far, _ = source
                    first = (shard ^ plane) * rows_plane + (chip ^ far) * rows_chip + start
                    target = weight_ref.at[pl.ds(pl.multiple_of(first, 16), rows), :]
                    block = piece_refs[array].at[pl.ds(row, rows), pl.ds(*columns)]
                    copies.append(pltpu.make_async_copy(block, target, semaphores.at[number + 1]))
                for copy in copies:
                    copy.start()
                for copy in copies:
                    copy.wait()
                write.start()

            body(operand_refs, output_refs, weight_ref, extra)

            @pl.when(pl.program_id(0) == grid[0] - 1)
            def _():
                write.wait()

        anywhere = pl.BlockSpec(memory_space=pl.ANY)
        return pl.pallas_call(
            kernel,
            grid=grid,
            in_specs=[scalar_spec()] + [anywhere] * (1 + count) + [spec for _, spec in operands],
            out_specs=[spec for _, _, spec in outputs] + [anywhere],
            out_shape=[jax.ShapeDtypeStruct(shape, kind_of) for shape, kind_of, _ in outputs]
            + [jax.ShapeDtypeStruct(self.shape(kind), bf16)],
            scratch_shapes=[
                pltpu.VMEM(self.shape(kind), bf16),
                pltpu.SemaphoreType.DMA((len(parts) + 2,)),
                *scratch,
            ],
            compiler_params=pltpu.CompilerParams(
                dimension_semantics=("arbitrary",), vmem_limit_bytes=24 * 1024 * 1024
            ),
            cost_estimate=pl.CostEstimate(flops=1, bytes_accessed=1, transcendentals=0),
            name=name,
        )(self.place, own, *self.arrays, *[operand for operand, _ in operands])


def block_spec(shape, place):
    return pl.BlockSpec(shape, place)


def out_projection(gathered, own, attended, inputs, bias, gain, shift):
    rows, width = attended.shape
    tile = rows // 2

    def body(operands, outputs, weight, extra):
        attended_ref, inputs_ref, bias_ref, gain_ref, shift_ref = operands
        residual = inputs_ref[...] + dot(attended_ref[...], weight[...]) + bias_ref[...]
        normed, inv_std = norm_parts(residual)
        outputs[0][...] = residual
        outputs[1][...] = normed
        outputs[2][...] = inv_std
        outputs[3][...] = (normed * gain_ref[...] + shift_ref[...]).astype(bf16)

    by_rows = block_spec((tile, width), lambda step: (step, 0))
    return gathered.call(
        body,
        "out",
        own,
        [(attended, by_rows), (inputs, by_rows)]
        + [(vector.reshape(1, width), whole_spec((1, width))) for vector in (bias, gain, shift)],
        [
            ((rows, width), f32, by_rows),
            ((rows, width), f32, by_rows),
            ((rows, 1), f32, block_spec((tile, 1), lambda step: (step, 0))),
            ((rows, width), bf16, by_rows),
        ],
        (2,),
        name="out_projection",
    )


def up_projection(gathered, own, act_own, act_other, bias):
    rows, width = act_own.shape
    breadth = own.shape[1]
    tile = min(512, breadth)

    def body(operands, outputs, weight, extra):
        first = pl.multiple_of(pl.program_id(0) * tile, tile)
        block = weight[:, pl.ds(first, tile)]
        part = rows // 2
        for number in range(4):
            act = operands[number // 2][(number % 2) * part : (number % 2 + 1) * part, :]
            pre_act = dot(act, block) + operands[2][...]
            square = pre_act * pre_act
            curve = jnp.tanh(pre_act * (gelu_root + gelu_root * gelu_cubic * square))
            inner = pre_act * (0.5 * gelu_root + 1.5 * gelu_root * gelu_cubic * square)
            share = 0.5 + 0.5 * curve
            place = slice(number * part, (number + 1) * part)
            outputs[0][place, :] = (pre_act * share).astype(bf16)
            outputs[1][place, :] = (share + inner * (1.0 - curve * curve)).astype(bf16)

    by_columns = block_spec((2 * rows, tile), lambda step: (0, step))
    return gathered.call(
        body,
        "up",
        own,
        [
            (act_own, whole_spec((rows, width))),
            (act_other, whole_spec((rows, width))),
            (bias.reshape(1, breadth), block_spec((1, tile), lambda step: (0, step))),
        ],
        [((2 * rows, breadth), bf16, by_columns), ((2 * rows, breadth), bf16, by_columns)],
        (breadth // tile,),
        name="up_projection",
    )


def hidden_backward(gathered, own, cot_own, cot_other, slopes):
    rows, width = cot_own.shape
    breadth = slopes.shape[1]
    tile = min(512, breadth)

    def body(operands, outputs, weight, extra):
        first = pl.multiple_of(pl.program_id(0) * tile, tile)
        block = weight[pl.ds(first, tile), :]
        total = jnp.zeros((1, tile), f32)
        for number in range(2):
            part = slice(number * rows, (number + 1) * rows)
            grads = dot_right(operands[number][...], block) * operands[2][part, :].astype(f32)
            grads = grads.astype(bf16)
            outputs[0][part, :] = grads
            total = total + jnp.sum(grads.astype(f32), axis=0, keepdims=True)
        outputs[1][...] = total

    by_columns = block_spec((2 * rows, tile), lambda step: (0, step))
    return gathered.call(
        body,
        "down",
        own,
        [
            (cot_own, whole_spec((rows, width))),
            (cot_other, whole_spec((rows, width))),
            (slopes, by_columns),
        ],
        [
            ((2 * rows, breadth), bf16, by_columns),
            ((1, breadth), f32, block_spec((1, tile), lambda step: (0, step))),
        ],
        (breadth // tile,),
        name="hidden_backward",
    )


def up_backward_kernel(grads_ref, weight_ref, result_ref):
    result_ref[...] = dot_right(grads_ref[...], weight_ref[...]).astype(result_ref.dtype)


def up_backward(weight, grads, number, kind_of):
    rows, breadth = grads.shape[0] // 2, grads.shape[1]
    width = weight.shape[0]
    tile = width // 4
    return pl.pallas_call(
        up_backward_kernel,
        grid=(4,),
        in_specs=[
            pl.BlockSpec((rows, breadth), lambda step: (number, 0)),
            pl.BlockSpec((tile, breadth), lambda step: (step, 0)),
        ],
        out_specs=pl.BlockSpec((rows, tile), lambda step: (0, step)),
        out_shape=jax.ShapeDtypeStruct((rows, width), kind_of),
        compiler_params=pltpu.CompilerParams(
            dimension_semantics=("arbitrary",), vmem_limit_bytes=24 * 1024 * 1024
        ),
        cost_estimate=pl.CostEstimate(flops=1, bytes_accessed=1, transcendentals=0),
        name="up_backward",
    )(grads, weight)


def up_gradient_kernel(own_ref, other_ref, grads_ref, result_ref, act_turned):
    rows, width = own_ref.shape
    step = 256

    @pl.when(pl.program_id(0) == 0)
    def _():
        for number, ref in enumerate((own_ref, other_ref)):
            for row in range(0, rows, step):
                first = number * rows + row
                for column in range(0, width, step):
                    block = ref[row : row + step, column : column + step]
                    act_turned[column : column + step, first : first + step] = turned(block).astype(bf16)

    result_ref[...] = dot(act_turned[...], grads_ref[...]).astype(bf16)


def up_gradient(act_own, act_other, grads):
    rows, width = act_own.shape
    breadth = grads.shape[1]
    tile = min(512, breadth)
    return pl.pallas_call(
        up_gradient_kernel,
        grid=(breadth // tile,),
        in_specs=[
            whole_spec((rows, width)),
            whole_spec((rows, width)),
            pl.BlockSpec((2 * rows, tile), lambda step: (0, step)),
        ],
        out_specs=pl.BlockSpec((width, tile), lambda step: (0, step)),
        out_shape=jax.ShapeDtypeStruct((width, breadth), bf16),
        scratch_shapes=[pltpu.VMEM((width, 2 * rows), bf16)],
        compiler_params=pltpu.CompilerParams(
            dimension_semantics=("arbitrary",), vmem_limit_bytes=24 * 1024 * 1024
        ),
        cost_estimate=pl.CostEstimate(flops=1, bytes_accessed=1, transcendentals=0),
        name="up_gradient",
    )(act_own, act_other, grads)


def together(*values):
    return lax.optimization_barrier(tuple(values))


def ordered(own, other, bit, axis=0):
    first = jnp.where(bit == 0, own, other)
    second = jnp.where(bit == 0, other, own)
    return jnp.stack([first, second], axis=axis)


class Moves:
    def __init__(self):
        self.shards = lax.axis_size("shard")
        self.reps = lax.axis_size("rep")
        self.half = self.shards // 2
        self.chips = self.reps // 2
        self.shard = lax.axis_index("shard")
        self.rep = lax.axis_index("rep")
        self.core = self.rep % 2
        self.chip = self.rep // 2
        self.side = self.shard // self.half
        self.member = self.shard % self.half + self.core * self.half

    def core_swap(self, part):
        return lax.ppermute(part, "rep", [(r, r ^ 1) for r in range(self.reps)])

    def chip_swap(self, part, bits):
        return lax.ppermute(part, "rep", [(r, r ^ (2 * bits)) for r in range(self.reps)])

    def shard_swap(self, part, bits):
        return lax.ppermute(part, "shard", [(s, s ^ bits) for s in range(self.shards)])

    def shard_bit(self, bits):
        return (self.shard // bits) % 2

    def low_bits(self):
        bits, result = 1, []
        while bits < self.half:
            result.append(bits)
            bits *= 2
        return result

    def home_swap(self, part):
        pairs = []
        for rep in range(self.reps):
            for shard in range(self.shards):
                side, core = shard // self.half, rep % 2
                to_rep, to_shard = rep, shard
                if side != core:
                    to_rep = rep ^ 1
                    to_shard = (shard + self.half) % self.shards
                pairs.append((rep * self.shards + shard, to_rep * self.shards + to_shard))
        return lax.ppermute(part, ("rep", "shard"), pairs)

    def half_gather(self, part):
        stack = part[None]
        for bits in self.low_bits():
            own = stack
            stack = ordered(own, self.shard_swap(own, bits), self.shard_bit(bits))
            stack = stack.reshape((-1,) + part.shape)
        return stack

    def cores_gather(self, stack):
        stack = ordered(stack, self.core_swap(stack), self.core)
        return stack.reshape((-1,) + stack.shape[2:])

    def exchange_bit(self, stack, bit, swap):
        sources, targets = stack.shape[:2]
        stack = stack.reshape((sources, 2, targets // 2) + stack.shape[2:])
        own, other = pick(stack, bit, 1), swap(pick(stack, 1 - bit, 1))
        return ordered(own, other, bit, 1).reshape((2 * sources,) + own.shape[1:])

    def half_exchange(self, stack):
        stack = stack[None]
        for bits in reversed(self.low_bits()):
            swap = functools.partial(self.shard_swap, bits=bits)
            stack = self.exchange_bit(stack, self.shard_bit(bits), swap)
        return stack.reshape((self.half,) + stack.shape[2:])

    def cores_exchange(self, stack):
        return self.exchange_bit(stack[None], self.core, self.core_swap)

    def members_exchange(self, stack):
        for bits in reversed(self.low_bits()):
            swap = functools.partial(self.shard_swap, bits=bits)
            stack = self.exchange_bit(stack, self.shard_bit(bits), swap)
        return stack.reshape((self.shards,) + stack.shape[2:])

    def reduce_bit(self, stack, bit, swap):
        stack = stack.reshape((2, stack.shape[0] // 2) + stack.shape[1:])
        other = swap(pick(stack, 1 - bit).astype(bf16))
        return pick(stack, bit).astype(f32) + other.astype(f32)

    def spread_open(self, part):
        if self.chips == 4:
            return (self.chip_swap(part, 1), self.chip_swap(part, 2))
        held, bits = [part], 1
        while bits < self.chips:
            held = held + [self.chip_swap(piece, bits) for piece in held]
            bits *= 2
        return tuple(held[1:])

    def spread_close(self, state):
        if self.chips == 4:
            by_x, by_y = state
            cut, axis = by_x.shape[-2] // 2, by_x.ndim - 2
            far = [
                self.chip_swap(by_x[..., :cut, :], 2),
                self.chip_swap(by_y[..., cut:, :], 1),
            ]
            return (by_x, by_y, jnp.concatenate(far, axis=axis))
        return state

    def far_open(self, states):
        if self.chips != 4:
            return ()
        cut = states[0][0].shape[0] // 2
        return (
            self.chip_swap(jnp.concatenate([by_x[:cut] for by_x, _ in states], axis=0), 2),
            self.chip_swap(jnp.concatenate([by_y[cut:] for _, by_y in states], axis=0), 1),
        )

    def far_parts(self, states, far):
        if self.chips != 4:
            return [[(k + 1, 0, part) for k, part in enumerate(state)] for state in states]
        cut = states[0][0].shape[0] // 2
        result = []
        for number, (by_x, by_y) in enumerate(states):
            rows = slice(number * cut, (number + 1) * cut)
            result.append([(1, 0, by_x), (2, 0, by_y), (3, 0, far[0][rows]), (3, cut, far[1][rows])])
        return result

    def chips_gather(self, part, axis, state=None):
        others = self.spread_close(self.spread_open(part) if state is None else state)
        return self.chips_place(part, axis, others)

    def chips_place(self, part, axis, others):
        shape = part.shape[:axis] + (self.chips,) + part.shape[axis:]
        stack = place(jnp.zeros(shape, part.dtype), part, self.chip, axis)
        for number, piece in enumerate(others):
            stack = place(stack, piece, self.chip ^ (number + 1), axis)
        return stack

    def reduce_open(self, stack, axis):
        return self.reduce_start(self.reduce_cut(stack, axis), axis)

    def reduce_cut(self, stack, axis):
        if self.chips != 4:
            return (stack,)
        shape = stack.shape[:axis] + (2, 2) + stack.shape[axis + 1 :]
        stack = stack.reshape(shape)
        bit_x, bit_y = self.chip % 2, self.chip // 2
        cut = shape[0] // 2
        first, second = stack[:cut], stack[cut:]
        return (
            pick(first, bit_x, axis + 1),
            pick(second, bit_y, axis),
            pick(first, 1 - bit_x, axis + 1),
            pick(second, 1 - bit_y, axis),
        )

    def reduce_start(self, parts, axis):
        if self.chips == 4:
            first, second, send_first, send_second = parts
            return (first, second, self.chip_swap(send_first, 1), self.chip_swap(send_second, 2))
        (stack,) = parts
        count = self.chips
        stack = stack.astype(f32)
        while count > 1:
            count //= 2
            shape = stack.shape[:axis] + (2, count) + stack.shape[axis + 1 :]
            stack = stack.reshape(shape)
            bit = (self.chip // count) % 2
            got = self.chip_swap(pick(stack, 1 - bit, axis).astype(bf16), count)
            stack = pick(stack, bit, axis) + got.astype(f32)
        return (pick(stack, 0, axis).astype(bf16),)

    def reduce_add(self, state):
        if self.chips != 4:
            return state
        first, second, got_first, got_second = state
        first = (first.astype(f32) + got_first.astype(f32)).astype(bf16)
        second = (second.astype(f32) + got_second.astype(f32)).astype(bf16)
        return (first, second)

    def reduce_send(self, state, axis):
        if self.chips != 4:
            return state
        first, second = state
        bit_x, bit_y = self.chip % 2, self.chip // 2
        got_first = self.chip_swap(pick(first, 1 - bit_y, axis), 2)
        got_second = self.chip_swap(pick(second, 1 - bit_x, axis), 1)
        return (pick(first, bit_y, axis), pick(second, bit_x, axis), got_first, got_second)

    def reduce_final(self, state):
        if self.chips != 4:
            return state[0]
        first, second, got_first, got_second = state
        first = first.astype(f32) + got_first.astype(f32)
        second = second.astype(f32) + got_second.astype(f32)
        return jnp.concatenate([first, second], axis=0).astype(bf16)

    def reduce_close(self, state, axis):
        return self.reduce_final(self.reduce_send(state, axis))

    def core_pair(self, part):
        other = self.core_swap(part)
        first = jnp.where(self.core == 0, part, other)
        second = jnp.where(self.core == 0, other, part)
        return first, second

    def sum_reps(self, vector):
        bits = 1
        while bits < self.reps:
            vector = vector + lax.ppermute(vector, "rep", [(r, r ^ bits) for r in range(self.reps)])
            bits *= 2
        return vector

    def sum_shards(self, vector):
        bits = 1
        while bits < self.shards:
            vector = vector + self.shard_swap(vector, bits)
            bits *= 2
        return vector


def stats_kernel(decay_rate, gradient_ref, old_ref, rows_ref, lane_rows_ref, sums_ref, total_ref, partial):
    step = pl.program_id(0)
    rows, columns = gradient_ref.shape

    @pl.when(step == 0)
    def _():
        partial[...] = jnp.zeros_like(partial)
        total_ref[...] = jnp.zeros_like(total_ref)

    gradient = gradient_ref[...].astype(f32)
    square = gradient * gradient
    row_mean = jnp.sum(square, axis=1, keepdims=True) / columns
    old = jnp.transpose(jnp.broadcast_to(old_ref[...], (128, rows)))[:, 0:1]
    rows_new = decay_rate * old + (1.0 - decay_rate) * (row_mean + eps_second)
    rows_ref[...] = rows_new
    lane_rows_ref[...] = jnp.transpose(jnp.broadcast_to(rows_new, (rows, 128)))[0:1, :]
    total_ref[...] += jnp.broadcast_to(jnp.sum(rows_new, axis=0, keepdims=True), (1, 128))
    partial[0:8, :] += eights(square, jnp.sum)
    partial[8:16, :] += eights(square * (1.0 / rows_new), jnp.sum)

    @pl.when(step == pl.num_programs(0) - 1)
    def _():
        sums_ref[0:1, :] = jnp.sum(partial[0:8, :], axis=0, keepdims=True)
        sums_ref[1:2, :] = jnp.sum(partial[8:16, :], axis=0, keepdims=True)


def factor_stats(gradient, rows_old, decay_rate):
    height, breadth = gradient.shape
    rows = min(128, height)
    return pl.pallas_call(
        functools.partial(stats_kernel, decay_rate),
        grid=(height // rows,),
        in_specs=[
            pl.BlockSpec((rows, breadth), lambda step: (step, 0)),
            pl.BlockSpec((1, rows), lambda step: (0, step)),
        ],
        out_specs=[
            pl.BlockSpec((rows, 1), lambda step: (step, 0)),
            pl.BlockSpec((1, rows), lambda step: (0, step)),
            pl.BlockSpec((2, breadth), lambda step: (0, 0)),
            pl.BlockSpec((1, 128), lambda step: (0, 0)),
        ],
        out_shape=[
            jax.ShapeDtypeStruct((height, 1), f32),
            jax.ShapeDtypeStruct((1, height), f32),
            jax.ShapeDtypeStruct((2, breadth), f32),
            jax.ShapeDtypeStruct((1, 128), f32),
        ],
        scratch_shapes=[pltpu.VMEM((16, breadth), f32)],
        compiler_params=pltpu.CompilerParams(
            dimension_semantics=("arbitrary",), vmem_limit_bytes=16 * 1024 * 1024
        ),
        name="factor_stats",
    )(gradient, rows_old)


def apply_kernel(
    decay_rate,
    height,
    gradient_ref,
    weight_ref,
    rows_ref,
    sums_ref,
    scalar_ref,
    old_ref,
    gradient_out,
    weight_out,
    copy_out,
    cols_out,
    rms_out,
    col_factor,
):
    columns = gradient_ref.shape[1]

    @pl.when(pl.program_id(0) == 0)
    def _():
        cols_new = decay_rate * old_ref[...] + (1.0 - decay_rate) * (
            sums_ref[0:1, :] / height + eps_second
        )
        row_mean = scalar_ref[0:1, 0:1] / height
        weight_mean = scalar_ref[1:2, 0:1] / (height * columns)
        scaled = jnp.sum(sums_ref[1:2, :] / cols_new, axis=1, keepdims=True)
        rms_update = jnp.sqrt(row_mean / (height * columns) * scaled)
        factor = rate_step * jnp.sqrt(weight_mean) * jnp.sqrt(row_mean)
        factor = factor / jnp.maximum(1.0, rms_update / clip_level)
        col_factor[...] = factor * lax.rsqrt(cols_new)
        cols_out[...] = cols_new
        rms_out[...] = jnp.broadcast_to(rms_update, (1, 128))

    gradient = gradient_ref[...].astype(f32)
    new_weight = weight_ref[...] - gradient * lax.rsqrt(rows_ref[...]) * col_factor[...]
    gradient_out[...] = gradient
    weight_out[...] = new_weight
    copy_out[...] = new_weight.astype(bf16)


def factor_apply(gradient, weight, rows_new, sums, scalars, cols_old, height, decay_rate):
    own_height, breadth = gradient.shape
    rows = min(64, own_height)

    def rows_spec():
        return pl.BlockSpec((rows, breadth), lambda step: (step, 0))

    def row_spec(count, wide):
        return pl.BlockSpec((count, wide), lambda step: (0, 0))

    return pl.pallas_call(
        functools.partial(apply_kernel, decay_rate, height),
        grid=(own_height // rows,),
        in_specs=[
            rows_spec(),
            rows_spec(),
            pl.BlockSpec((rows, 1), lambda step: (step, 0)),
            row_spec(2, breadth),
            row_spec(2, 128),
            row_spec(1, breadth),
        ],
        out_specs=[rows_spec(), rows_spec(), rows_spec(), row_spec(1, breadth), row_spec(1, 128)],
        out_shape=[
            jax.ShapeDtypeStruct((own_height, breadth), f32),
            jax.ShapeDtypeStruct((own_height, breadth), f32),
            jax.ShapeDtypeStruct((own_height, breadth), bf16),
            jax.ShapeDtypeStruct((1, breadth), f32),
            jax.ShapeDtypeStruct((1, 128), f32),
        ],
        scratch_shapes=[pltpu.VMEM((1, breadth), f32)],
        compiler_params=pltpu.CompilerParams(
            dimension_semantics=("arbitrary",), vmem_limit_bytes=16 * 1024 * 1024
        ),
        name="factor_apply",
    )(gradient, weight, rows_new, sums, scalars, cols_old)


def summed(moves, entries):
    total = moves.sum_shards(jnp.concatenate(entries, axis=1))
    result, offset = [], 0
    for entry in entries:
        result.append(total[:, offset : offset + entry.shape[1]])
        offset += entry.shape[1]
    return result


def on_device(
    tokens,
    cotangent,
    seq_lengths,
    qkv_weight,
    out_weight,
    up_weight,
    down_weight,
    vectors,
    row_state,
    down_rows,
    col_state,
    vector_state,
):
    moves = Moves()
    shards, half, chips, core = moves.shards, moves.half, moves.chips, moves.core
    row_count, width = tokens.shape
    hidden_width = up_weight.shape[1]
    group_rows = row_count * shards
    heads = HEADS // shards
    head_width = width // HEADS
    span = heads * head_width
    member = moves.member
    decay_rate = 1.0 - STEP ** (-0.8)
    head_number = (member * heads + jnp.arange(heads, dtype=jnp.int32)).astype(f32)
    slopes = jnp.exp2(-8.0 * (head_number + 1.0) / HEADS)

    gain_one = vectors[0:width]
    shift_one = vectors[width : 2 * width]
    bias_query = vectors[2 * width : 3 * width]
    bias_value = vectors[3 * width : 4 * width]
    bias_out = vectors[4 * width : 5 * width]
    gain_two = vectors[5 * width : 6 * width]
    shift_two = vectors[6 * width : 7 * width]
    bias_up = vectors[7 * width : 7 * width + hidden_width]
    bias_down = vectors[7 * width + hidden_width :]

    home_tokens = moves.home_swap(tokens)
    other_lengths = moves.core_swap(seq_lengths)
    lengths = jnp.where(moves.side == core, seq_lengths, other_lengths)[0]
    plan = block_plan(lengths, group_rows, BLOCK)
    rows_z = width // shards
    rows_piece = rows_z // chips
    my_rows = lax.dynamic_slice_in_dim(qkv_weight, moves.chip * rows_piece, rows_piece, 0)
    my_rows = my_rows.astype(bf16)
    my_blocks = []
    for number in range(half):
        kinds = []
        for kind in range(3):
            first = kind * width + number * span
            second = first + half * span
            kinds.append(
                jnp.where(
                    core == 0, my_rows[:, first : first + span], my_rows[:, second : second + span]
                )
            )
        my_blocks.append(jnp.concatenate(kinds, axis=1))
    qkv_part = moves.half_exchange(jnp.stack(my_blocks))
    half_cols = hidden_width // (2 * shards)
    up_wide = shards * half_cols
    out_wide = width // 2
    down_piece = half_cols // chips

    def core_half(values):
        parts = []
        for number in range(shards):
            start = 2 * number * half_cols
            first = values[..., start : start + half_cols]
            second = values[..., start + half_cols : start + 2 * half_cols]
            parts.append(jnp.where(core == 0, first, second))
        return jnp.concatenate(parts, axis=-1)

    up_own = core_half(up_weight).astype(bf16)
    out_own = out_weight.astype(bf16)
    down_own = lax.dynamic_slice_in_dim(down_weight, core * half_cols, half_cols, 0).astype(bf16)
    fold = down_piece // rows_piece
    my_down = lax.dynamic_slice_in_dim(down_own, moves.chip * down_piece, down_piece, 0)
    weight_piece = jnp.concatenate(
        [
            lax.dynamic_slice_in_dim(own, moves.chip * rows_piece, rows_piece, 0)
            for own in (up_own, out_own)
        ]
        + [my_down[k * rows_piece : (k + 1) * rows_piece] for k in range(fold)],
        axis=1,
    )
    near_pieces, bits = [weight_piece], 1
    while bits < half:
        near_pieces = near_pieces + [moves.shard_swap(piece, bits) for piece in near_pieces]
        bits *= 2
    near_pieces = near_pieces[1:]
    weights = [qkv_weight, out_weight, up_weight, down_weight]
    weight_sums = [jnp.sum(weight * weight) for weight in weights]
    rows_old = [row_state[k : k + 1] for k in range(3)] + [down_rows.reshape(1, -1)]
    home_tokens, qkv_part, near_pieces, weight_piece, weight_sums, rows_old, plan = together(
        home_tokens, qkv_part, near_pieces, weight_piece, weight_sums, rows_old, plan
    )
    far_piece = moves.shard_swap(weight_piece, half)
    near_open = [moves.spread_open(piece) for piece in near_pieces]
    qkv_far = moves.shard_swap(qkv_part, half)
    qkv_far, near_open = together(qkv_far, near_open)
    qkv_part = ordered(qkv_part, qkv_far, moves.side).reshape(shards, rows_piece, 3 * span)
    qkv_open, far_piece = together(moves.spread_open(qkv_part), far_piece)
    qkv_cols = moves.chips_gather(qkv_part, 1, qkv_open).reshape(width, 3 * span)
    inputs = home_tokens.astype(f32)
    normed_one, inv_std_one = norm_parts(inputs)
    act_one = (normed_one * gain_one + shift_one).astype(bf16)
    act_half = moves.half_gather(act_one)

    act_half, qkv_cols, far_piece, cotangent = together(
        act_half, qkv_cols, far_piece, cotangent
    )
    home_cot = moves.home_swap(cotangent)
    act_all = moves.cores_gather(act_half).reshape(group_rows, width)
    far_open = moves.spread_open(far_piece)
    far_pieces, bits = [far_piece], 1
    while bits < half:
        far_pieces = far_pieces + [moves.shard_swap(piece, bits) for piece in far_pieces]
        bits *= 2
    far_pieces = far_pieces[1:]

    bias_q_part = lax.dynamic_slice_in_dim(bias_query, member * span, span)
    bias_v_part = lax.dynamic_slice_in_dim(bias_value, member * span, span)
    qkv_bias = jnp.concatenate([bias_q_part, jnp.zeros_like(bias_q_part), bias_v_part])
    qkv_rows = (dot(act_all, qkv_cols) + qkv_bias).astype(bf16)
    attended_cols, logs = attend_forward(qkv_rows, plan, slopes, heads, BLOCK)
    attended_cols, far_open, far_pieces, home_cot = together(
        attended_cols, far_open, far_pieces, home_cot
    )
    attended_parts = moves.cores_exchange(attended_cols.reshape(shards, row_count, span))
    attended_parts = moves.members_exchange(attended_parts)
    first_states = near_open + [far_open]
    first_far = moves.far_open(first_states)
    last_states = [moves.spread_open(piece) for piece in far_pieces]
    attended_parts, first_far, last_states, home_cot = together(
        attended_parts, first_far, last_states, home_cot
    )
    last_far = moves.far_open(last_states)
    attended = jnp.concatenate([attended_parts[k] for k in range(shards)], axis=1)

    pieces = near_pieces + [far_piece] + far_pieces
    arrays = list(pieces)
    sources = [(k, 0, rows_piece, k + 1, 0, 0) for k in range(len(pieces))]
    for first_plane, states, far in ((1, first_states, first_far), (half + 1, last_states, last_far)):
        cut = rows_piece // 2
        for way, array in enumerate(far):
            for k in range(len(states)):
                sources.append((len(arrays), k * cut, cut, first_plane + k, 3, way * cut))
            arrays.append(array)
        for k, state in enumerate(states):
            for way, array in enumerate(state):
                sources.append((len(arrays), 0, rows_piece, first_plane + k, way + 1, 0))
                arrays.append(array)
    place_now = jnp.stack([moves.shard, moves.chip]).astype(jnp.int32)
    sizes = (rows_z, rows_piece, up_wide, width, fold, half_cols)
    gathered = Gathered(arrays, sources, place_now, sizes)
    residual, normed_two, inv_std_two, act_two, out_low = out_projection(
        gathered, out_own, attended, inputs, bias_out, gain_two, shift_two
    )

    act_two_other, attended_other, cot_other = together(
        moves.core_swap(act_two), moves.core_swap(attended), moves.core_swap(home_cot)
    )
    cot_pair = jnp.concatenate([home_cot, cot_other], axis=0)
    attended_pair = jnp.concatenate([attended, attended_other], axis=0)
    hidden_pair, slope_pair, up_half = up_projection(
        gathered, up_own, act_two, act_two_other, core_half(bias_up)
    )
    down_terms = dot_rows(hidden_pair, cot_pair).astype(bf16)
    down_state = moves.reduce_cut(down_terms.reshape(shards, chips, down_piece, width), 1)
    slope_pair, down_state = together(slope_pair, down_state)
    down_state = moves.reduce_start(down_state, 1)
    grad_y = home_cot.astype(f32)
    grad_bias_down = jnp.sum(grad_y, axis=0)
    grad_up_pair, grad_bias_up, down_half = hidden_backward(
        gathered, down_own, home_cot, cot_other, slope_pair
    )
    grad_bias_up = grad_bias_up.reshape(-1)
    back_other = moves.core_swap(up_backward(up_half, grad_up_pair, 1, bf16))
    up_terms = up_gradient(act_two, act_two_other, grad_up_pair)
    back_other, hidden_pair, up_terms, down_state = together(
        back_other, hidden_pair, up_terms, down_state
    )
    up_state = moves.reduce_open(up_terms.reshape(shards, chips, rows_piece, up_wide), 1)
    down_mid = moves.reduce_close(moves.reduce_add(down_state), 1)
    grad_act_two = up_backward(up_half, grad_up_pair, 0, f32) + back_other.astype(f32)
    grad_gain_two = jnp.sum(grad_act_two * normed_two, axis=0)
    grad_shift_two = jnp.sum(grad_act_two, axis=0)
    grad_residual = grad_y + norm_back(grad_act_two, normed_two, inv_std_two, gain_two)
    grad_attn = grad_residual.astype(bf16)
    grad_bias_out = jnp.sum(grad_attn, axis=0, dtype=f32)
    to_members = jnp.stack(
        [
            dot_right(grad_attn, out_low[k * span : (k + 1) * span]).astype(bf16)
            for k in range(shards)
        ]
    )
    attn_halves = [grad_attn[:, :out_wide], grad_attn[:, out_wide:]]
    attn_own = jnp.where(core == 0, attn_halves[0], attn_halves[1])
    attn_other = jnp.where(core == 0, attn_halves[1], attn_halves[0])
    grad_heads, attn_other = together(moves.cores_exchange(to_members), moves.core_swap(attn_other))
    attn_pair = jnp.concatenate([attn_own, attn_other], axis=0)
    grad_heads, hidden_pair = together(grad_heads, hidden_pair)
    grad_heads = moves.members_exchange(grad_heads).reshape(group_rows, span)
    down_other = moves.core_swap(dot(hidden_pair[row_count:], down_half).astype(bf16))
    block_out = (
        residual + dot(hidden_pair[:row_count], down_half) + down_other.astype(f32) + bias_down
    ).astype(bf16)

    out_terms = dot_rows(attended_pair, attn_pair).astype(bf16)
    def shards_halve(piece, bits):
        piece = piece.reshape((piece.shape[0] // 2, 2) + piece.shape[1:])
        bit = moves.shard_bit(bits)
        return pick(piece, bit, 1), moves.shard_swap(pick(piece, 1 - bit, 1), bits)

    def halved(state):
        own, other = state
        return (own.astype(f32) + other.astype(f32)).astype(bf16)

    def shards_sum(piece):
        rows = piece.shape[1]
        return lax.psum_scatter(
            piece.reshape(shards * rows, piece.shape[2]), "shard", scatter_dimension=0, tiled=True
        )

    grad_heads, down_mid, out_terms, block_out = together(
        grad_heads, down_mid, out_terms, block_out
    )
    block_out = moves.home_swap(block_out)
    down_owned = shards_sum(down_mid)
    out_state = moves.reduce_open(out_terms.reshape(shards, chips, rows_piece, out_wide), 1)
    attend_args = (plan, slopes)
    parts = 2 if heads % 4 == 0 else 1
    part_heads = heads // parts
    grad_qkv = attend_backward(
        qkv_rows, grad_heads, attended_cols, logs, *attend_args, part_heads, BLOCK, 0, None
    )
    grad_qkv, up_state, out_state = together(grad_qkv, up_state, out_state)
    up_sums, out_sums = moves.reduce_add(up_state), moves.reduce_add(out_state)
    grad_qkv, up_sums, out_sums = together(grad_qkv, up_sums, out_sums)
    up_out_state = [
        jnp.concatenate([up_part, out_part], axis=-1) for up_part, out_part in zip(up_sums, out_sums)
    ]
    if parts == 2:
        grad_qkv = attend_backward(
            qkv_rows, grad_heads, attended_cols, logs, *attend_args, part_heads, BLOCK, part_heads, grad_qkv
        )
    grad_qkv, up_out_state, block_out = together(
        grad_qkv, moves.reduce_send(up_out_state, 1), block_out
    )
    up_out_piece = moves.reduce_final(up_out_state)
    up_out_state = shards_halve(up_out_piece, 1)

    grad_bias_q_part = jnp.sum(grad_qkv[:, :span], axis=0, dtype=f32)
    grad_bias_v_part = jnp.sum(grad_qkv[:, 2 * span :], axis=0, dtype=f32)

    grad_halves = grad_qkv.reshape(2, half * row_count, 3 * span)
    sent = dot_right(pick(grad_halves, 1 - core), qkv_cols).astype(bf16)
    sent = moves.core_swap(sent)
    qkv_terms = dot_rows(act_all, grad_qkv).astype(bf16)
    qkv_terms = qkv_terms.reshape(shards, chips, rows_piece, 3 * span)
    qkv_state = moves.reduce_open(qkv_terms, 1)
    back = dot_right(pick(grad_halves, core), qkv_cols) + sent.astype(f32)
    qkv_state, back, up_out_state = together(qkv_state, back, up_out_state)

    back = back.reshape(half, row_count, width)
    low_bits = list(reversed(moves.low_bits()))
    for bits in low_bits[:-1]:
        back = moves.reduce_bit(
            back, moves.shard_bit(bits), functools.partial(moves.shard_swap, bits=bits)
        )
    back = back.reshape((2, -1) + back.shape[1:])
    back_bit = moves.shard_bit(low_bits[-1])
    back_other = moves.shard_swap(pick(back, 1 - back_bit).astype(bf16), low_bits[-1])
    up_out_piece, bits = halved(up_out_state), 2
    while bits < half:
        up_out_piece = halved(shards_halve(up_out_piece, bits))
        bits *= 2
    up_out_state = shards_halve(up_out_piece, half)
    qkv_state = moves.reduce_send(moves.reduce_add(qkv_state), 1)
    qkv_state, up_out_state = together(qkv_state, up_out_state)

    up_out_owned = halved(up_out_state)[0]
    up_out_state = moves.spread_open(up_out_owned)
    qkv_piece = moves.reduce_final(qkv_state)
    qkv_piece = qkv_piece.reshape((2, half) + qkv_piece.shape[1:])
    qkv_own = pick(qkv_piece, moves.side)
    qkv_other = moves.shard_swap(pick(qkv_piece, 1 - moves.side), half)
    back_other, qkv_other, up_out_state = together(back_other, qkv_other, up_out_state)

    qkv_piece = moves.half_exchange(halved((qkv_own, qkv_other)))
    down_state = moves.spread_open(down_owned)
    grad_act_one = pick(back, back_bit) + back_other.astype(f32)
    grad_act_one = grad_act_one.reshape(row_count, width)
    grad_gain_one = jnp.sum(grad_act_one * normed_one, axis=0)
    grad_shift_one = jnp.sum(grad_act_one, axis=0)
    grad_inputs = grad_residual + norm_back(grad_act_one, normed_one, inv_std_one, gain_one)
    grad_inputs, qkv_piece, down_state = together(grad_inputs.astype(bf16), qkv_piece, down_state)
    tokens_grad = moves.home_swap(grad_inputs)
    qkv_owned = moves.chips_gather(qkv_piece, 1)

    up_out_first, up_out_second = moves.core_pair(
        moves.chips_gather(up_out_owned, 0, tuple(up_out_state)).reshape(rows_z, up_wide + out_wide)
    )
    out_grad = jnp.concatenate([up_out_first[:, up_wide:], up_out_second[:, up_wide:]], axis=1)
    up_columns = []
    for number in range(shards):
        part = slice(number * half_cols, (number + 1) * half_cols)
        up_columns += [up_out_first[:, part], up_out_second[:, part]]
    up_grad = jnp.concatenate(up_columns, axis=1)
    down_first, down_second = moves.core_pair(
        moves.chips_gather(down_owned, 0, tuple(down_state)).reshape(half_cols, width)
    )
    down_grad = jnp.concatenate([down_first, down_second], axis=0)
    qkv_first, qkv_second = moves.core_pair(qkv_owned.reshape(half, rows_z, 3 * span))
    qkv_columns = []
    for kind in range(3):
        for source in (qkv_first, qkv_second):
            for number in range(half):
                qkv_columns.append(source[number][:, kind * span : (kind + 1) * span])
    qkv_grad = jnp.concatenate(qkv_columns, axis=1)

    gradients = [qkv_grad, out_grad, up_grad, down_grad]
    heights = [width, width, width, hidden_width]
    stats = [
        factor_stats(gradient, old, decay_rate) for gradient, old in zip(gradients, rows_old)
    ]

    def to_sum(number):
        weight_sum = jnp.broadcast_to(weight_sums[number], (1, 128))
        return [stats[number][2], jnp.concatenate([stats[number][3], weight_sum], axis=0)]

    def spread_heads(part):
        return [jnp.where(member == number, part, 0.0) for number in range(shards)]

    bias_up_parts = []
    for number in range(shards):
        part = grad_bias_up[number * half_cols : (number + 1) * half_cols]
        bias_up_parts += [jnp.where(core == 0, part, 0.0), jnp.where(core == 1, part, 0.0)]
    vector_part = moves.sum_reps(
        jnp.concatenate(
            [grad_gain_one, grad_shift_one]
            + spread_heads(grad_bias_q_part)
            + spread_heads(grad_bias_v_part)
            + [grad_bias_out, grad_gain_two, grad_shift_two]
            + bias_up_parts
            + [grad_bias_down]
        )
    )
    vector_rows, tokens_grad = together(vector_part.reshape(2, -1), tokens_grad)
    all_sums = summed(moves, to_sum(0) + to_sum(1) + to_sum(2) + to_sum(3) + [vector_rows])
    sums = [all_sums[0:2], all_sums[2:4], all_sums[4:6], all_sums[6:8]]
    vector_grad = all_sums[8].reshape(-1)
    updates = []
    offset = 0
    for number in range(4):
        end_col = offset + gradients[number].shape[1]
        updates.append(
            factor_apply(
                gradients[number],
                weights[number],
                stats[number][0],
                sums[number][0],
                sums[number][1],
                col_state[offset:end_col].reshape(1, -1),
                heights[number],
                decay_rate,
            )
        )
        offset = end_col
    grads_out, new_weights, copies, new_cols, rms_rows = zip(*updates)
    rms_values = [rms[0, 0] for rms in rms_rows]

    vector_state_new = decay_rate * vector_state + (1.0 - decay_rate) * (
        vector_grad * vector_grad + eps_second
    )
    vector_step = vector_grad * lax.rsqrt(vector_state_new)
    vector_rms = jnp.sqrt(jnp.mean(vector_step * vector_step))
    vector_new = vectors - rate_step * jnp.sqrt(
        jnp.mean(vectors * vectors)
    ) * vector_step / jnp.maximum(1.0, vector_rms / clip_level)
    update_rms = jnp.stack(rms_values + [vector_rms])
    return (
        block_out,
        tokens_grad,
        *grads_out,
        vector_grad,
        *new_weights,
        vector_new,
        *copies,
        jnp.concatenate([stats[0][1], stats[1][1], stats[2][1]], axis=0),
        stats[3][1].reshape(-1),
        jnp.concatenate(new_cols, axis=1).reshape(-1),
        vector_state_new,
        update_rms,
    )


def solution(mesh):
    in_specs = (
        P(("rep", "shard"), None),
        P(("rep", "shard"), None),
        P("rep", None),
        P("shard", None),
        P("shard", None),
        P("shard", None),
        P("shard", None),
        P(),
        P(None, "shard"),
        P("shard"),
        P(),
        P(),
    )
    out_specs = (
        P(("rep", "shard"), None),
        P(("rep", "shard"), None),
        P("shard", None),
        P("shard", None),
        P("shard", None),
        P("shard", None),
        P(),
        P("shard", None),
        P("shard", None),
        P("shard", None),
        P("shard", None),
        P(),
        P("shard", None),
        P("shard", None),
        P("shard", None),
        P("shard", None),
        P(None, "shard"),
        P("shard"),
        P(),
        P(),
        P(),
    )
    return jax.shard_map(
        on_device, mesh=mesh, in_specs=in_specs, out_specs=out_specs, check_vma=False
    )
```

```python
import functools

import jax
import jax.numpy as jnp
from jax import lax
from jax.experimental import pallas as pl
from jax.experimental.pallas import tpu as pltpu
from jax.sharding import PartitionSpec as P

HEADS = 16
STEP = 10
BLOCK = 256


eps_norm = 1e-05
eps_second = 1e-30
rate_step = 0.5
clip_level = 1.0
masked = -1e30
gelu_root = (2.0 / 3.141592653589793) ** 0.5
gelu_cubic = 0.044715

f32 = jnp.float32
bf16 = jnp.bfloat16


def norm_parts(values):
    average = jnp.mean(values, axis=-1, keepdims=True)
    centred = values - average
    inv_std = lax.rsqrt(jnp.mean(centred * centred, axis=-1, keepdims=True) + eps_norm)
    return (centred * inv_std, inv_std)


def norm_back(grad_out, normed, inv_std, gain_vec):
    grad_normed = grad_out * gain_vec
    inner_mean = jnp.mean(grad_normed * normed, axis=-1, keepdims=True)
    centred = grad_normed - jnp.mean(grad_normed, axis=-1, keepdims=True)
    return (centred - normed * inner_mean) * inv_std


def gelu_value(pre_act):
    curve = jnp.tanh(gelu_root * (pre_act + gelu_cubic * pre_act * pre_act * pre_act))
    return 0.5 * pre_act * (1.0 + curve)


def gelu_slope(pre_act):
    square = pre_act * pre_act
    curve = jnp.tanh(gelu_root * (pre_act + gelu_cubic * square * pre_act))
    inner = gelu_root * (1.0 + 3.0 * gelu_cubic * square)
    return 0.5 * (1.0 + curve) + 0.5 * pre_act * (1.0 - curve * curve) * inner


def dot(left_side, right_side):
    return jnp.dot(left_side, right_side, preferred_element_type=f32)


def dot_right(left_side, right_side):
    return lax.dot_general(
        left_side, right_side, (((1,), (1,)), ((), ())), preferred_element_type=f32
    )


def dot_rows(left_side, right_side):
    return lax.dot_general(
        left_side, right_side, (((0,), (0,)), ((), ())), preferred_element_type=f32
    )


def pick(stack, index, axis=0):
    return lax.dynamic_index_in_dim(stack, index, axis, keepdims=False)


def place(stack, part, index, axis=0):
    return lax.dynamic_update_index_in_dim(stack, part, index, axis)


def head_rows(number, head_width):
    return slice(number * head_width, (number + 1) * head_width)


def lane_masks(block_rows, width, heads):
    lanes = lax.broadcasted_iota(jnp.int32, (block_rows, width), 1)
    head_width = width // heads
    return [
        (lanes >= number * head_width) & (lanes < (number + 1) * head_width)
        for number in range(heads)
    ]


def allowed_pairs(key_block, query_block, start_row, block):
    key_pos = lax.broadcasted_iota(jnp.int32, (block, block), 0) + key_block * block
    query_pos = lax.broadcasted_iota(jnp.int32, (block, block), 1) + query_block * block
    return (key_pos <= query_pos) & (key_pos >= start_row)


def key_offsets(key_block, query_block, block):
    rows = lax.broadcasted_iota(jnp.int32, (block, 1), 0)
    return (rows + (key_block - query_block) * block).astype(f32)


def turned(values):
    return jnp.transpose(values.astype(f32))


def head_stack(values, lanes):
    zero = jnp.zeros(values.shape, values.dtype)
    return jnp.concatenate([jnp.where(lane, values, zero) for lane in lanes], axis=0)


def eights(values, combine):
    rows, columns = values.shape
    return combine(values.reshape(rows // 8, 8, columns), axis=0)


def forward_kernel(
    heads,
    block,
    low_ref,
    mid_ref,
    slope_ref,
    start_ref,
    qkv_ref,
    out_ref,
    log_ref,
    values_turned,
    key_stack,
    score_ref,
):
    tokens = qkv_ref.shape[0]
    width = qkv_ref.shape[1] // 3
    head_width = width // heads
    blocks = tokens // block
    query_block = pl.program_id(0)

    @pl.when(query_block == 0)
    def _():
        lanes = lane_masks(block, width, heads)
        for number in range(blocks):
            rows = slice(number * block, (number + 1) * block)
            values_turned[number] = turned(qkv_ref[rows, 2 * width :]).astype(bf16)
            key_stack[number] = head_stack(qkv_ref[rows, width : 2 * width], lanes)

    first_row = pl.multiple_of(query_block * block, block)
    queries = qkv_ref[pl.ds(first_row, block), :width].astype(f32) * head_width ** (-0.5)
    queries = turned(queries).astype(bf16)
    start_row = start_ref[query_block]

    def score_step(key_block, bests, with_mask):
        scores = dot(key_stack[key_block], queries)
        offsets = key_offsets(key_block, query_block, block)
        allowed = allowed_pairs(key_block, query_block, start_row, block) if with_mask else None
        result = []
        for number in range(heads):
            rows = head_rows(number, block)
            part = scores[rows] + slope_ref[number] * offsets
            if with_mask:
                part = jnp.where(allowed, part, masked)
            score_ref[key_block, rows, :] = part
            result.append(jnp.maximum(bests[number], eights(part, jnp.max)))
        return tuple(result)

    low, mid = low_ref[query_block], mid_ref[query_block]
    bests = tuple(jnp.full((8, block), masked, f32) for _ in range(heads))
    bests = lax.fori_loop(low, mid, functools.partial(score_step, with_mask=True), bests)
    bests = lax.fori_loop(mid, query_block, functools.partial(score_step, with_mask=False), bests)
    bests = score_step(query_block, bests, True)
    bests = [jnp.max(best, axis=0, keepdims=True) for best in bests]

    def value_step(key_block, state):
        result = []
        for number in range(heads):
            total, gathered = state[2 * number : 2 * number + 2]
            weights = jnp.exp(score_ref[key_block, head_rows(number, block), :] - bests[number])
            value_rows = values_turned[key_block, head_rows(number, head_width), :]
            result += [
                total + eights(weights, jnp.sum),
                gathered + dot(value_rows, weights.astype(bf16)),
            ]
        return tuple(result)

    state = ()
    for number in range(heads):
        state += (jnp.zeros((8, block), f32), jnp.zeros((head_width, block), f32))
    state = lax.fori_loop(low, query_block + 1, value_step, state)
    columns = []
    for number in range(heads):
        total = jnp.sum(state[2 * number], axis=0, keepdims=True)
        columns.append(state[2 * number + 1] / total)
        log_ref[0, number : number + 1, :] = bests[number] + jnp.log(total)
    out_ref[...] = jnp.transpose(jnp.concatenate(columns, axis=0)).astype(bf16)


def backward_kernel(heads, block, first_head, merge, *refs):
    full_ref, high_ref, slope_ref, start_ref, log_ref, qkv_ref, grad_ref, out_ref = refs[:8]
    earlier_ref = refs[8] if merge else None
    result_ref = refs[9 if merge else 8]
    (
        queries_turned,
        grads_turned,
        keys_turned,
        query_stack,
        grad_stack,
        key_stack,
        value_stack,
        delta_rows,
        query_grads,
    ) = refs[10 if merge else 9 :]
    tokens, all_width = grad_ref.shape
    head_width = all_width // log_ref.shape[1]
    width = heads * head_width
    scale = head_width ** (-0.5)
    blocks = tokens // block
    key_block = pl.program_id(0)
    lanes = lane_masks(block, width, heads)

    def columns(kind):
        start = kind * all_width + first_head * head_width
        return slice(start, start + width)

    def target(kind):
        start = (kind * all_width + first_head * head_width) if merge else kind * width
        return slice(start, start + width)

    @pl.when(key_block == 0)
    def _():
        for number in range(blocks):
            rows = slice(number * block, (number + 1) * block)
            queries = qkv_ref[rows, columns(0)]
            queries_turned[number] = turned(queries.astype(f32) * scale).astype(bf16)
            query_stack[number] = head_stack(queries, lanes)
            keys_turned[number] = turned(qkv_ref[rows, columns(1)]).astype(bf16)
            grads = grad_ref[rows, columns(0)]
            grad_stack[number] = head_stack(grads, lanes)
            grads = grads.astype(f32)
            grads_turned[number] = turned(grads).astype(bf16)
            product = turned(grads * out_ref[rows, columns(0)].astype(f32))
            for head in range(heads):
                delta_rows[number, head : head + 1, :] = jnp.sum(
                    product[head_rows(head, head_width)], axis=0, keepdims=True
                )
            query_grads[number] = jnp.zeros((width, block), f32)

    key_row = pl.multiple_of(key_block * block, block)
    key_stack[...] = head_stack(qkv_ref[pl.ds(key_row, block), columns(1)], lanes)
    value_stack[...] = head_stack(qkv_ref[pl.ds(key_row, block), columns(2)], lanes)

    def step(query_block, state, with_mask):
        key_total, value_total = state
        scores = dot(key_stack[...], queries_turned[query_block])
        grad_weights = dot(value_stack[...], grads_turned[query_block])
        offsets = key_offsets(key_block, query_block, block)
        if with_mask:
            allowed = allowed_pairs(key_block, query_block, start_ref[query_block], block)
        weight_list, grad_list = [], []
        for number in range(heads):
            rows = head_rows(number, block)
            head = first_head + number
            part = scores[rows] + slope_ref[head] * offsets
            part = part - log_ref[query_block, head : head + 1, :]
            if with_mask:
                part = jnp.where(allowed, part, masked)
            probabilities = jnp.exp(part)
            delta = delta_rows[query_block, number : number + 1, :]
            grad_scores = (probabilities * (grad_weights[rows] - delta)).astype(bf16)
            weight_list.append(probabilities.astype(bf16))
            grad_list.append(grad_scores)
            rows = head_rows(number, head_width)
            query_grads[query_block, rows, :] += dot(keys_turned[key_block, rows, :], grad_scores)
        weight_row = jnp.concatenate(weight_list, axis=1)
        grad_row = jnp.concatenate(grad_list, axis=1)
        return (
            key_total + dot(grad_row, query_stack[query_block]),
            value_total + dot(weight_row, grad_stack[query_block]),
        )

    state = (jnp.zeros((block, width), f32), jnp.zeros((block, width), f32))
    state = step(key_block, state, True)
    full, high = full_ref[key_block], high_ref[key_block]
    state = lax.fori_loop(key_block + 1, full, functools.partial(step, with_mask=False), state)
    state = lax.fori_loop(full, high, functools.partial(step, with_mask=True), state)
    result_ref[pl.ds(key_row, block), target(1)] = (state[0] * scale).astype(bf16)
    result_ref[pl.ds(key_row, block), target(2)] = state[1].astype(bf16)
    if merge:
        other = first_head * head_width
        for kind in range(3):
            result_ref[pl.ds(key_row, block), kind * all_width : kind * all_width + other] = earlier_ref[
                pl.ds(key_row, block), kind * other : (kind + 1) * other
            ]

    @pl.when(key_block == blocks - 1)
    def _():
        for number in range(blocks):
            rows = slice(number * block, (number + 1) * block)
            result_ref[rows, target(0)] = jnp.transpose(query_grads[number] * scale).astype(bf16)


def block_plan(lengths, tokens, block):
    ends = jnp.cumsum(lengths)
    positions = jnp.arange(tokens, dtype=jnp.int32)
    passed = positions[:, None] >= ends[None, :]
    starts = jnp.max(jnp.where(passed, ends[None, :], 0), axis=1).astype(jnp.int32)
    finish = jnp.min(jnp.where(passed, tokens, ends[None, :]), axis=1).astype(jnp.int32)
    blocks = tokens // block
    number = jnp.arange(blocks, dtype=jnp.int32)
    first_start = starts[::block]
    last_start = starts[block - 1 :: block]
    low = first_start // block
    mid = jnp.clip((last_start + block - 1) // block, low, number)
    high = (finish[block - 1 :: block] - 1) // block + 1
    full = jnp.clip(finish[::block] // block, number + 1, high)
    return (starts.reshape(blocks, 1, block), low, mid, full, high)


def scalar_spec():
    return pl.BlockSpec(memory_space=pltpu.SMEM)


def whole_spec(shape):
    return pl.BlockSpec(shape, lambda step: (0,) * len(shape), pipeline_mode=pl.Buffered(1))


def attend_forward(qkv, plan, slopes, heads, block):
    tokens, triple = qkv.shape
    width = triple // 3
    blocks = tokens // block
    starts, low, mid, full, high = plan
    return pl.pallas_call(
        functools.partial(forward_kernel, heads, block),
        grid=(blocks,),
        in_specs=[
            scalar_spec(),
            scalar_spec(),
            scalar_spec(),
            whole_spec((blocks, 1, block)),
            whole_spec((tokens, triple)),
        ],
        out_specs=[
            pl.BlockSpec((block, width), lambda step: (step, 0)),
            pl.BlockSpec((1, heads, block), lambda step: (step, 0, 0)),
        ],
        out_shape=[
            jax.ShapeDtypeStruct((tokens, width), bf16),
            jax.ShapeDtypeStruct((blocks, heads, block), f32),
        ],
        scratch_shapes=[
            pltpu.VMEM((blocks, width, block), bf16),
            pltpu.VMEM((blocks, heads * block, width), bf16),
            pltpu.VMEM((blocks, heads * block, block), f32),
        ],
        compiler_params=pltpu.CompilerParams(
            dimension_semantics=("arbitrary",), vmem_limit_bytes=24 * 1024 * 1024
        ),
        cost_estimate=pl.CostEstimate(
            flops=3 * tokens * tokens * 256 * heads,
            bytes_accessed=10 * tokens * width,
            transcendentals=tokens * tokens * heads // 2,
        ),
        name="attend_forward",
    )(low, mid, slopes, starts, qkv)


def attend_backward(qkv, grads, outputs, logs, plan, slopes, heads, block, first_head, earlier):
    tokens, triple = qkv.shape
    all_width = triple // 3
    all_heads = logs.shape[1]
    width = all_width // all_heads * heads
    blocks = tokens // block
    starts, low, mid, full, high = plan
    merge = earlier is not None
    result_width = triple if merge else 3 * width
    operands = [full, high, slopes, starts, logs, qkv, grads, outputs]
    specs = [scalar_spec() for _ in range(3)] + [whole_spec(entry.shape) for entry in operands[3:]]
    if merge:
        operands.append(earlier)
        specs.append(whole_spec(earlier.shape))
    return pl.pallas_call(
        functools.partial(backward_kernel, heads, block, first_head, merge),
        grid=(blocks,),
        in_specs=specs,
        out_specs=pl.BlockSpec((tokens, result_width), lambda step: (0, 0)),
        out_shape=jax.ShapeDtypeStruct((tokens, result_width), bf16),
        scratch_shapes=[
            pltpu.VMEM((blocks, width, block), bf16),
            pltpu.VMEM((blocks, width, block), bf16),
            pltpu.VMEM((blocks, width, block), bf16),
            pltpu.VMEM((blocks, heads * block, width), bf16),
            pltpu.VMEM((blocks, heads * block, width), bf16),
            pltpu.VMEM((heads * block, width), bf16),
            pltpu.VMEM((heads * block, width), bf16),
            pltpu.VMEM((blocks, heads, block), f32),
            pltpu.VMEM((blocks, width, block), f32),
        ],
        compiler_params=pltpu.CompilerParams(
            dimension_semantics=("arbitrary",), vmem_limit_bytes=24 * 1024 * 1024
        ),
        cost_estimate=pl.CostEstimate(
            flops=8 * tokens * tokens * 256 * heads,
            bytes_accessed=20 * tokens * width,
            transcendentals=tokens * tokens * heads // 2,
        ),
        name="attend_backward",
    )(*operands)


class Gathered:
    def __init__(self, arrays, sources, place, sizes):
        self.arrays, self.sources, self.place = arrays, sources, place
        self.rows_z, self.rows_piece, self.up_wide, self.width, self.fold, self.half_cols = sizes

    def parts(self, kind):
        result = []
        for source in self.sources:
            place = source[5]
            if kind == "up":
                result.append((source, (0, self.up_wide), self.rows_z, self.rows_piece, place))
            elif kind == "out":
                columns = (self.up_wide, self.width)
                result.append((source, columns, self.rows_z, self.rows_piece, place))
            else:
                for number in range(self.fold):
                    columns = (self.up_wide + (1 + number) * self.width, self.width)
                    chip_rows = self.rows_piece * self.fold
                    start = place + number * self.rows_piece
                    result.append((source, columns, self.half_cols, chip_rows, start))
        return result

    def shape(self, kind):
        planes = self.width // self.rows_z
        if kind == "down":
            return (planes * self.half_cols, self.width)
        return (self.width, self.up_wide if kind == "up" else self.width)

    def call(self, body, kind, own, operands, outputs, grid, scratch=(), name=None):
        parts = self.parts(kind)
        plane_rows = own.shape[0]
        count = len(self.arrays)

        def kernel(place_ref, own_ref, *refs):
            piece_refs = refs[:count]
            operand_refs = refs[count : count + len(operands)]
            rest = refs[count + len(operands) :]
            output_refs, written_ref = rest[: len(outputs)], rest[len(outputs)]
            weight_ref, semaphores, *extra = rest[len(outputs) + 1 :]
            write = pltpu.make_async_copy(weight_ref, written_ref, semaphores.at[len(parts) + 1])

            @pl.when(pl.program_id(0) == 0)
            def _():
                shard, chip = place_ref[0], place_ref[1]
                first = pl.multiple_of(shard * plane_rows, plane_rows)
                target = weight_ref.at[pl.ds(first, plane_rows), :]
                copies = [pltpu.make_async_copy(own_ref, target, semaphores.at[0])]
                for number, (source, columns, rows_plane, rows_chip, start) in enumerate(parts):
                    array, row, rows, plane, far, _ = source
                    first = (shard ^ plane) * rows_plane + (chip ^ far) * rows_chip + start
                    target = weight_ref.at[pl.ds(pl.multiple_of(first, 16), rows), :]
                    block = piece_refs[array].at[pl.ds(row, rows), pl.ds(*columns)]
                    copies.append(pltpu.make_async_copy(block, target, semaphores.at[number + 1]))
                for copy in copies:
                    copy.start()
                for copy in copies:
                    copy.wait()
                write.start()

            body(operand_refs, output_refs, weight_ref, extra)

            @pl.when(pl.program_id(0) == grid[0] - 1)
            def _():
                write.wait()

        anywhere = pl.BlockSpec(memory_space=pltpu.HBM)
        return pl.pallas_call(
            kernel,
            grid=grid,
            in_specs=[scalar_spec()] + [anywhere] * (1 + count) + [spec for _, spec in operands],
            out_specs=[spec for _, _, spec in outputs] + [anywhere],
            out_shape=[jax.ShapeDtypeStruct(shape, kind_of) for shape, kind_of, _ in outputs]
            + [jax.ShapeDtypeStruct(self.shape(kind), bf16)],
            scratch_shapes=[
                pltpu.VMEM(self.shape(kind), bf16),
                pltpu.SemaphoreType.DMA((len(parts) + 2,)),
                *scratch,
            ],
            compiler_params=pltpu.CompilerParams(
                dimension_semantics=("arbitrary",), vmem_limit_bytes=24 * 1024 * 1024
            ),
            cost_estimate=pl.CostEstimate(flops=1, bytes_accessed=1, transcendentals=0),
            name=name,
        )(self.place, own, *self.arrays, *[operand for operand, _ in operands])


def block_spec(shape, place):
    return pl.BlockSpec(shape, place)


def out_projection(gathered, own, attended, inputs, bias, gain, shift):
    rows, width = attended.shape
    tile = rows // 2

    def body(operands, outputs, weight, extra):
        attended_ref, inputs_ref, bias_ref, gain_ref, shift_ref = operands
        residual = inputs_ref[...] + dot(attended_ref[...], weight[...]) + bias_ref[...]
        normed, inv_std = norm_parts(residual)
        outputs[0][...] = residual
        outputs[1][...] = normed
        outputs[2][...] = inv_std
        outputs[3][...] = (normed * gain_ref[...] + shift_ref[...]).astype(bf16)

    by_rows = block_spec((tile, width), lambda step: (step, 0))
    return gathered.call(
        body,
        "out",
        own,
        [(attended, by_rows), (inputs, by_rows)]
        + [(vector.reshape(1, width), whole_spec((1, width))) for vector in (bias, gain, shift)],
        [
            ((rows, width), f32, by_rows),
            ((rows, width), f32, by_rows),
            ((rows, 1), f32, block_spec((tile, 1), lambda step: (step, 0))),
            ((rows, width), bf16, by_rows),
        ],
        (2,),
        name="out_projection",
    )


def up_projection(gathered, own, act_own, act_other, bias):
    rows, width = act_own.shape
    breadth = own.shape[1]
    tile = min(512, breadth)

    def body(operands, outputs, weight, extra):
        first = pl.multiple_of(pl.program_id(0) * tile, tile)
        block = weight[:, pl.ds(first, tile)]
        part = rows // 2
        for number in range(4):
            act = operands[number // 2][(number % 2) * part : (number % 2 + 1) * part, :]
            pre_act = dot(act, block) + operands[2][...]
            square = pre_act * pre_act
            curve = jnp.tanh(pre_act * (gelu_root + gelu_root * gelu_cubic * square))
            inner = pre_act * (0.5 * gelu_root + 1.5 * gelu_root * gelu_cubic * square)
            share = 0.5 + 0.5 * curve
            place = slice(number * part, (number + 1) * part)
            outputs[0][place, :] = (pre_act * share).astype(bf16)
            outputs[1][place, :] = (share + inner * (1.0 - curve * curve)).astype(bf16)

    by_columns = block_spec((2 * rows, tile), lambda step: (0, step))
    return gathered.call(
        body,
        "up",
        own,
        [
            (act_own, whole_spec((rows, width))),
            (act_other, whole_spec((rows, width))),
            (bias.reshape(1, breadth), block_spec((1, tile), lambda step: (0, step))),
        ],
        [((2 * rows, breadth), bf16, by_columns), ((2 * rows, breadth), bf16, by_columns)],
        (breadth // tile,),
        name="up_projection",
    )


def hidden_backward(gathered, own, cot_own, cot_other, slopes):
    rows, width = cot_own.shape
    breadth = slopes.shape[1]
    tile = min(512, breadth)

    def body(operands, outputs, weight, extra):
        first = pl.multiple_of(pl.program_id(0) * tile, tile)
        block = weight[pl.ds(first, tile), :]
        total = jnp.zeros((1, tile), f32)
        for number in range(2):
            part = slice(number * rows, (number + 1) * rows)
            grads = dot_right(operands[number][...], block) * operands[2][part, :].astype(f32)
            grads = grads.astype(bf16)
            outputs[0][part, :] = grads
            total = total + jnp.sum(grads.astype(f32), axis=0, keepdims=True)
        outputs[1][...] = total

    by_columns = block_spec((2 * rows, tile), lambda step: (0, step))
    return gathered.call(
        body,
        "down",
        own,
        [
            (cot_own, whole_spec((rows, width))),
            (cot_other, whole_spec((rows, width))),
            (slopes, by_columns),
        ],
        [
            ((2 * rows, breadth), bf16, by_columns),
            ((1, breadth), f32, block_spec((1, tile), lambda step: (0, step))),
        ],
        (breadth // tile,),
        name="hidden_backward",
    )


def up_backward_kernel(grads_ref, weight_ref, result_ref):
    result_ref[...] = dot_right(grads_ref[...], weight_ref[...]).astype(result_ref.dtype)


def up_backward(weight, grads, number, kind_of):
    rows, breadth = grads.shape[0] // 2, grads.shape[1]
    width = weight.shape[0]
    tile = width // 4
    return pl.pallas_call(
        up_backward_kernel,
        grid=(4,),
        in_specs=[
            pl.BlockSpec((rows, breadth), lambda step: (number, 0)),
            pl.BlockSpec((tile, breadth), lambda step: (step, 0)),
        ],
        out_specs=pl.BlockSpec((rows, tile), lambda step: (0, step)),
        out_shape=jax.ShapeDtypeStruct((rows, width), kind_of),
        compiler_params=pltpu.CompilerParams(
            dimension_semantics=("arbitrary",), vmem_limit_bytes=24 * 1024 * 1024
        ),
        cost_estimate=pl.CostEstimate(flops=1, bytes_accessed=1, transcendentals=0),
        name="up_backward",
    )(grads, weight)


def up_gradient_kernel(own_ref, other_ref, grads_ref, result_ref, act_turned):
    rows, width = own_ref.shape
    step = 256

    @pl.when(pl.program_id(0) == 0)
    def _():
        for number, ref in enumerate((own_ref, other_ref)):
            for row in range(0, rows, step):
                first = number * rows + row
                for column in range(0, width, step):
                    block = ref[row : row + step, column : column + step]
                    act_turned[column : column + step, first : first + step] = turned(block).astype(bf16)

    result_ref[...] = dot(act_turned[...], grads_ref[...]).astype(bf16)


def up_gradient(act_own, act_other, grads):
    rows, width = act_own.shape
    breadth = grads.shape[1]
    tile = min(512, breadth)
    return pl.pallas_call(
        up_gradient_kernel,
        grid=(breadth // tile,),
        in_specs=[
            whole_spec((rows, width)),
            whole_spec((rows, width)),
            pl.BlockSpec((2 * rows, tile), lambda step: (0, step)),
        ],
        out_specs=pl.BlockSpec((width, tile), lambda step: (0, step)),
        out_shape=jax.ShapeDtypeStruct((width, breadth), bf16),
        scratch_shapes=[pltpu.VMEM((width, 2 * rows), bf16)],
        compiler_params=pltpu.CompilerParams(
            dimension_semantics=("arbitrary",), vmem_limit_bytes=24 * 1024 * 1024
        ),
        cost_estimate=pl.CostEstimate(flops=1, bytes_accessed=1, transcendentals=0),
        name="up_gradient",
    )(act_own, act_other, grads)


def together(*values):
    return lax.optimization_barrier(tuple(values))


def ordered(own, other, bit, axis=0):
    first = jnp.where(bit == 0, own, other)
    second = jnp.where(bit == 0, other, own)
    return jnp.stack([first, second], axis=axis)


class Moves:
    def __init__(self):
        self.shards = lax.axis_size("shard")
        self.reps = lax.axis_size("rep")
        self.half = self.shards // 2
        self.chips = self.reps // 2
        self.shard = lax.axis_index("shard")
        self.rep = lax.axis_index("rep")
        self.core = self.rep % 2
        self.chip = self.rep // 2
        self.side = self.shard // self.half
        self.member = self.shard % self.half + self.core * self.half

    def core_swap(self, part):
        return lax.ppermute(part, "rep", [(r, r ^ 1) for r in range(self.reps)])

    def chip_swap(self, part, bits):
        return lax.ppermute(part, "rep", [(r, r ^ (2 * bits)) for r in range(self.reps)])

    def shard_swap(self, part, bits):
        return lax.ppermute(part, "shard", [(s, s ^ bits) for s in range(self.shards)])

    def shard_bit(self, bits):
        return (self.shard // bits) % 2

    def low_bits(self):
        bits, result = 1, []
        while bits < self.half:
            result.append(bits)
            bits *= 2
        return result

    def home_swap(self, part):
        pairs = []
        for rep in range(self.reps):
            for shard in range(self.shards):
                if shard // self.half != rep % 2:
                    to_shard = (shard + self.half) % self.shards
                    pairs.append((rep * self.shards + shard, (rep ^ 1) * self.shards + to_shard))
        other = lax.ppermute(part, ("rep", "shard"), pairs)
        return jnp.where(self.side == self.core, part, other)

    def half_gather(self, part):
        stack = part[None]
        for bits in self.low_bits():
            own = stack
            stack = ordered(own, self.shard_swap(own, bits), self.shard_bit(bits))
            stack = stack.reshape((-1,) + part.shape)
        return stack

    def cores_gather(self, stack):
        stack = ordered(stack, self.core_swap(stack), self.core)
        return stack.reshape((-1,) + stack.shape[2:])

    def exchange_bit(self, stack, bit, swap):
        sources, targets = stack.shape[:2]
        stack = stack.reshape((sources, 2, targets // 2) + stack.shape[2:])
        own, other = pick(stack, bit, 1), swap(pick(stack, 1 - bit, 1))
        return ordered(own, other, bit, 1).reshape((2 * sources,) + own.shape[1:])

    def half_exchange(self, stack):
        stack = stack[None]
        for bits in reversed(self.low_bits()):
            swap = functools.partial(self.shard_swap, bits=bits)
            stack = self.exchange_bit(stack, self.shard_bit(bits), swap)
        return stack.reshape((self.half,) + stack.shape[2:])

    def cores_exchange(self, stack):
        return self.exchange_bit(stack[None], self.core, self.core_swap)

    def members_exchange(self, stack):
        for bits in reversed(self.low_bits()):
            swap = functools.partial(self.shard_swap, bits=bits)
            stack = self.exchange_bit(stack, self.shard_bit(bits), swap)
        return stack.reshape((self.shards,) + stack.shape[2:])

    def reduce_bit(self, stack, bit, swap):
        stack = stack.reshape((2, stack.shape[0] // 2) + stack.shape[1:])
        other = swap(pick(stack, 1 - bit).astype(bf16))
        return pick(stack, bit).astype(f32) + other.astype(f32)

    def spread_open(self, part):
        if self.chips == 4:
            return (self.chip_swap(part, 1), self.chip_swap(part, 2))
        held, bits = [part], 1
        while bits < self.chips:
            held = held + [self.chip_swap(piece, bits) for piece in held]
            bits *= 2
        return tuple(held[1:])

    def spread_close(self, state):
        if self.chips == 4:
            by_x, by_y = state
            cut, axis = by_x.shape[-2] // 2, by_x.ndim - 2
            far = [
                self.chip_swap(by_x[..., :cut, :], 2),
                self.chip_swap(by_y[..., cut:, :], 1),
            ]
            return (by_x, by_y, jnp.concatenate(far, axis=axis))
        return state

    def far_send(self, state):
        if self.chips != 4:
            return ()
        by_x, by_y = state
        cut = by_x.shape[-2] // 2
        return (self.chip_swap(by_x[..., :cut, :], 2), self.chip_swap(by_y[..., cut:, :], 1))

    def spread_join(self, state, far):
        if self.chips != 4:
            return state
        return (state[0], state[1], jnp.concatenate(far, axis=far[0].ndim - 2))

    def far_open(self, states):
        if self.chips != 4:
            return ()
        cut = states[0][0].shape[0] // 2
        return (
            self.chip_swap(jnp.concatenate([by_x[:cut] for by_x, _ in states], axis=0), 2),
            self.chip_swap(jnp.concatenate([by_y[cut:] for _, by_y in states], axis=0), 1),
        )

    def far_parts(self, states, far):
        if self.chips != 4:
            return [[(k + 1, 0, part) for k, part in enumerate(state)] for state in states]
        cut = states[0][0].shape[0] // 2
        result = []
        for number, (by_x, by_y) in enumerate(states):
            rows = slice(number * cut, (number + 1) * cut)
            result.append([(1, 0, by_x), (2, 0, by_y), (3, 0, far[0][rows]), (3, cut, far[1][rows])])
        return result

    def chips_gather(self, part, axis, state=None):
        others = self.spread_close(self.spread_open(part) if state is None else state)
        return self.chips_place(part, axis, others)

    def chips_place(self, part, axis, others):
        shape = part.shape[:axis] + (self.chips,) + part.shape[axis:]
        stack = place(jnp.zeros(shape, part.dtype), part, self.chip, axis)
        for number, piece in enumerate(others):
            stack = place(stack, piece, self.chip ^ (number + 1), axis)
        return stack

    def reduce_open(self, stack, axis):
        return self.reduce_start(self.reduce_cut(stack, axis), axis)

    def reduce_cut(self, stack, axis):
        if self.chips != 4:
            return (stack,)
        shape = stack.shape[:axis] + (2, 2) + stack.shape[axis + 1 :]
        stack = stack.reshape(shape)
        bit_x, bit_y = self.chip % 2, self.chip // 2
        cut = shape[0] // 2
        first, second = stack[:cut], stack[cut:]
        return (
            pick(first, bit_x, axis + 1),
            pick(second, bit_y, axis),
            pick(first, 1 - bit_x, axis + 1),
            pick(second, 1 - bit_y, axis),
        )

    def reduce_start(self, parts, axis):
        if self.chips == 4:
            first, second, send_first, send_second = parts
            return (first, second, self.chip_swap(send_first, 1), self.chip_swap(send_second, 2))
        (stack,) = parts
        count = self.chips
        stack = stack.astype(f32)
        while count > 1:
            count //= 2
            shape = stack.shape[:axis] + (2, count) + stack.shape[axis + 1 :]
            stack = stack.reshape(shape)
            bit = (self.chip // count) % 2
            got = self.chip_swap(pick(stack, 1 - bit, axis).astype(bf16), count)
            stack = pick(stack, bit, axis) + got.astype(f32)
        return (pick(stack, 0, axis).astype(bf16),)

    def reduce_add(self, state):
        if self.chips != 4:
            return state
        first, second, got_first, got_second = state
        first = (first.astype(f32) + got_first.astype(f32)).astype(bf16)
        second = (second.astype(f32) + got_second.astype(f32)).astype(bf16)
        return (first, second)

    def reduce_send(self, state, axis):
        if self.chips != 4:
            return state
        first, second = state
        bit_x, bit_y = self.chip % 2, self.chip // 2
        got_first = self.chip_swap(pick(first, 1 - bit_y, axis), 2)
        got_second = self.chip_swap(pick(second, 1 - bit_x, axis), 1)
        return (pick(first, bit_y, axis), pick(second, bit_x, axis), got_first, got_second)

    def reduce_final(self, state):
        if self.chips != 4:
            return state[0]
        first, second, got_first, got_second = state
        first = first.astype(f32) + got_first.astype(f32)
        second = second.astype(f32) + got_second.astype(f32)
        return jnp.concatenate([first, second], axis=0).astype(bf16)

    def reduce_close(self, state, axis):
        return self.reduce_final(self.reduce_send(state, axis))

    def core_pair(self, part):
        other = self.core_swap(part)
        first = jnp.where(self.core == 0, part, other)
        second = jnp.where(self.core == 0, other, part)
        return first, second

    def sum_reps(self, vector):
        bits = 1
        while bits < self.reps:
            vector = vector + lax.ppermute(vector, "rep", [(r, r ^ bits) for r in range(self.reps)])
            bits *= 2
        return vector

    def sum_shards(self, vector):
        bits = 1
        while bits < self.shards:
            vector = vector + self.shard_swap(vector, bits)
            bits *= 2
        return vector


def stats_kernel(decay_rate, gradient_ref, old_ref, rows_ref, lane_rows_ref, sums_ref, total_ref, partial):
    step = pl.program_id(0)
    rows, columns = gradient_ref.shape

    @pl.when(step == 0)
    def _():
        partial[...] = jnp.zeros_like(partial)
        total_ref[...] = jnp.zeros_like(total_ref)

    gradient = gradient_ref[...].astype(f32)
    square = gradient * gradient
    row_mean = jnp.sum(square, axis=1, keepdims=True) / columns
    old = jnp.transpose(jnp.broadcast_to(old_ref[...], (128, rows)))[:, 0:1]
    rows_new = decay_rate * old + (1.0 - decay_rate) * (row_mean + eps_second)
    rows_ref[...] = rows_new
    lane_rows_ref[...] = jnp.transpose(jnp.broadcast_to(rows_new, (rows, 128)))[0:1, :]
    total_ref[...] += jnp.broadcast_to(jnp.sum(rows_new, axis=0, keepdims=True), (1, 128))
    partial[0:8, :] += eights(square, jnp.sum)
    partial[8:16, :] += eights(square * (1.0 / rows_new), jnp.sum)

    @pl.when(step == pl.num_programs(0) - 1)
    def _():
        sums_ref[0:1, :] = jnp.sum(partial[0:8, :], axis=0, keepdims=True)
        sums_ref[1:2, :] = jnp.sum(partial[8:16, :], axis=0, keepdims=True)


def factor_stats(gradient, rows_old, decay_rate):
    height, breadth = gradient.shape
    rows = min(128, height)
    return pl.pallas_call(
        functools.partial(stats_kernel, decay_rate),
        grid=(height // rows,),
        in_specs=[
            pl.BlockSpec((rows, breadth), lambda step: (step, 0)),
            pl.BlockSpec((1, rows), lambda step: (0, step)),
        ],
        out_specs=[
            pl.BlockSpec((rows, 1), lambda step: (step, 0)),
            pl.BlockSpec((1, rows), lambda step: (0, step)),
            pl.BlockSpec((2, breadth), lambda step: (0, 0)),
            pl.BlockSpec((1, 128), lambda step: (0, 0)),
        ],
        out_shape=[
            jax.ShapeDtypeStruct((height, 1), f32),
            jax.ShapeDtypeStruct((1, height), f32),
            jax.ShapeDtypeStruct((2, breadth), f32),
            jax.ShapeDtypeStruct((1, 128), f32),
        ],
        scratch_shapes=[pltpu.VMEM((16, breadth), f32)],
        compiler_params=pltpu.CompilerParams(
            dimension_semantics=("arbitrary",), vmem_limit_bytes=16 * 1024 * 1024
        ),
        name="factor_stats",
    )(gradient, rows_old)


def apply_kernel(
    decay_rate,
    height,
    gradient_ref,
    weight_ref,
    rows_ref,
    sums_ref,
    scalar_ref,
    old_ref,
    gradient_out,
    weight_out,
    copy_out,
    cols_out,
    rms_out,
    col_factor,
):
    columns = gradient_ref.shape[1]

    @pl.when(pl.program_id(0) == 0)
    def _():
        cols_new = decay_rate * old_ref[...] + (1.0 - decay_rate) * (
            sums_ref[0:1, :] / height + eps_second
        )
        row_mean = scalar_ref[0:1, 0:1] / height
        weight_mean = scalar_ref[1:2, 0:1] / (height * columns)
        scaled = jnp.sum(sums_ref[1:2, :] / cols_new, axis=1, keepdims=True)
        rms_update = jnp.sqrt(row_mean / (height * columns) * scaled)
        factor = rate_step * jnp.sqrt(weight_mean) * jnp.sqrt(row_mean)
        factor = factor / jnp.maximum(1.0, rms_update / clip_level)
        col_factor[...] = factor * lax.rsqrt(cols_new)
        cols_out[...] = cols_new
        rms_out[...] = jnp.broadcast_to(rms_update, (1, 128))

    gradient = gradient_ref[...].astype(f32)
    new_weight = weight_ref[...] - gradient * lax.rsqrt(rows_ref[...]) * col_factor[...]
    gradient_out[...] = gradient
    weight_out[...] = new_weight
    copy_out[...] = new_weight.astype(bf16)


def factor_apply(gradient, weight, rows_new, sums, scalars, cols_old, height, decay_rate):
    own_height, breadth = gradient.shape
    rows = min(64, own_height)

    def rows_spec():
        return pl.BlockSpec((rows, breadth), lambda step: (step, 0))

    def row_spec(count, wide):
        return pl.BlockSpec((count, wide), lambda step: (0, 0))

    return pl.pallas_call(
        functools.partial(apply_kernel, decay_rate, height),
        grid=(own_height // rows,),
        in_specs=[
            rows_spec(),
            rows_spec(),
            pl.BlockSpec((rows, 1), lambda step: (step, 0)),
            row_spec(2, breadth),
            row_spec(2, 128),
            row_spec(1, breadth),
        ],
        out_specs=[rows_spec(), rows_spec(), rows_spec(), row_spec(1, breadth), row_spec(1, 128)],
        out_shape=[
            jax.ShapeDtypeStruct((own_height, breadth), f32),
            jax.ShapeDtypeStruct((own_height, breadth), f32),
            jax.ShapeDtypeStruct((own_height, breadth), bf16),
            jax.ShapeDtypeStruct((1, breadth), f32),
            jax.ShapeDtypeStruct((1, 128), f32),
        ],
        scratch_shapes=[pltpu.VMEM((1, breadth), f32)],
        compiler_params=pltpu.CompilerParams(
            dimension_semantics=("arbitrary",), vmem_limit_bytes=16 * 1024 * 1024
        ),
        name="factor_apply",
    )(gradient, weight, rows_new, sums, scalars, cols_old)


def summed(moves, entries):
    total = moves.sum_shards(jnp.concatenate(entries, axis=1))
    result, offset = [], 0
    for entry in entries:
        result.append(total[:, offset : offset + entry.shape[1]])
        offset += entry.shape[1]
    return result


def on_device(
    tokens,
    cotangent,
    seq_lengths,
    qkv_weight,
    out_weight,
    up_weight,
    down_weight,
    vectors,
    row_state,
    down_rows,
    col_state,
    vector_state,
):
    moves = Moves()
    shards, half, chips, core = moves.shards, moves.half, moves.chips, moves.core
    row_count, width = tokens.shape
    hidden_width = up_weight.shape[1]
    group_rows = row_count * shards
    heads = HEADS // shards
    head_width = width // HEADS
    span = heads * head_width
    member = moves.member
    decay_rate = 1.0 - STEP ** (-0.8)
    head_number = (member * heads + jnp.arange(heads, dtype=jnp.int32)).astype(f32)
    slopes = jnp.exp2(-8.0 * (head_number + 1.0) / HEADS)

    gain_one = vectors[0:width]
    shift_one = vectors[width : 2 * width]
    bias_query = vectors[2 * width : 3 * width]
    bias_value = vectors[3 * width : 4 * width]
    bias_out = vectors[4 * width : 5 * width]
    gain_two = vectors[5 * width : 6 * width]
    shift_two = vectors[6 * width : 7 * width]
    bias_up = vectors[7 * width : 7 * width + hidden_width]
    bias_down = vectors[7 * width + hidden_width :]

    home_tokens = moves.home_swap(tokens)
    other_lengths = moves.core_swap(seq_lengths)
    lengths = jnp.where(moves.side == core, seq_lengths, other_lengths)[0]
    plan = block_plan(lengths, group_rows, BLOCK)
    rows_z = width // shards
    rows_piece = rows_z // chips
    my_rows = lax.dynamic_slice_in_dim(qkv_weight, moves.chip * rows_piece, rows_piece, 0)
    my_rows = my_rows.astype(bf16)
    my_blocks = []
    for number in range(half):
        kinds = []
        for kind in range(3):
            first = kind * width + number * span
            second = first + half * span
            kinds.append(
                jnp.where(
                    core == 0, my_rows[:, first : first + span], my_rows[:, second : second + span]
                )
            )
        my_blocks.append(jnp.concatenate(kinds, axis=1))
    qkv_part = moves.half_exchange(jnp.stack(my_blocks))
    half_cols = hidden_width // (2 * shards)
    up_wide = shards * half_cols
    out_wide = width // 2
    down_piece = half_cols // chips

    def core_half(values):
        parts = []
        for number in range(shards):
            start = 2 * number * half_cols
            first = values[..., start : start + half_cols]
            second = values[..., start + half_cols : start + 2 * half_cols]
            parts.append(jnp.where(core == 0, first, second))
        return jnp.concatenate(parts, axis=-1)

    up_own = core_half(up_weight).astype(bf16)
    out_own = out_weight.astype(bf16)
    down_own = lax.dynamic_slice_in_dim(down_weight, core * half_cols, half_cols, 0).astype(bf16)
    fold = down_piece // rows_piece
    my_down = lax.dynamic_slice_in_dim(down_own, moves.chip * down_piece, down_piece, 0)
    weight_piece = jnp.concatenate(
        [
            lax.dynamic_slice_in_dim(own, moves.chip * rows_piece, rows_piece, 0)
            for own in (up_own, out_own)
        ]
        + [my_down[k * rows_piece : (k + 1) * rows_piece] for k in range(fold)],
        axis=1,
    )
    near_pieces, bits = [weight_piece], 1
    while bits < half:
        near_pieces = near_pieces + [moves.shard_swap(piece, bits) for piece in near_pieces]
        bits *= 2
    near_pieces = near_pieces[1:]
    weights = [qkv_weight, out_weight, up_weight, down_weight]
    weight_sums = [jnp.sum(weight * weight) for weight in weights]
    rows_old = [row_state[k : k + 1] for k in range(3)] + [down_rows.reshape(1, -1)]
    home_tokens, qkv_part, near_pieces, weight_piece, weight_sums, rows_old, plan = together(
        home_tokens, qkv_part, near_pieces, weight_piece, weight_sums, rows_old, plan
    )
    far_piece = moves.shard_swap(weight_piece, half)
    near_open = [moves.spread_open(piece) for piece in near_pieces]
    qkv_far = moves.shard_swap(qkv_part, half)
    qkv_far, near_open = together(qkv_far, near_open)
    qkv_part = ordered(qkv_part, qkv_far, moves.side).reshape(shards, rows_piece, 3 * span)
    qkv_open, far_piece = together(moves.spread_open(qkv_part), far_piece)
    qkv_cols = moves.chips_gather(qkv_part, 1, qkv_open).reshape(width, 3 * span)
    inputs = home_tokens.astype(f32)
    normed_one, inv_std_one = norm_parts(inputs)
    act_one = (normed_one * gain_one + shift_one).astype(bf16)
    act_half = moves.half_gather(act_one)

    act_half, qkv_cols, far_piece, cotangent = together(
        act_half, qkv_cols, far_piece, cotangent
    )
    home_cot = moves.home_swap(cotangent)
    act_all = moves.cores_gather(act_half).reshape(group_rows, width)
    far_open = moves.spread_open(far_piece)
    far_pieces, bits = [far_piece], 1
    while bits < half:
        far_pieces = far_pieces + [moves.shard_swap(piece, bits) for piece in far_pieces]
        bits *= 2
    far_pieces = far_pieces[1:]

    bias_q_part = lax.dynamic_slice_in_dim(bias_query, member * span, span)
    bias_v_part = lax.dynamic_slice_in_dim(bias_value, member * span, span)
    qkv_bias = jnp.concatenate([bias_q_part, jnp.zeros_like(bias_q_part), bias_v_part])
    qkv_rows = (dot(act_all, qkv_cols) + qkv_bias).astype(bf16)
    attended_cols, logs = attend_forward(qkv_rows, plan, slopes, heads, BLOCK)
    attended_cols, far_open, far_pieces, home_cot = together(
        attended_cols, far_open, far_pieces, home_cot
    )
    attended_parts = moves.cores_exchange(attended_cols.reshape(shards, row_count, span))
    attended_parts = moves.members_exchange(attended_parts)
    first_states = near_open + [far_open]
    first_far = moves.far_open(first_states)
    last_states = [moves.spread_open(piece) for piece in far_pieces]
    attended_parts, first_far, last_states, home_cot = together(
        attended_parts, first_far, last_states, home_cot
    )
    last_far = moves.far_open(last_states)
    attended = jnp.concatenate([attended_parts[k] for k in range(shards)], axis=1)

    pieces = near_pieces + [far_piece] + far_pieces
    arrays = list(pieces)
    sources = [(k, 0, rows_piece, k + 1, 0, 0) for k in range(len(pieces))]
    for first_plane, states, far in ((1, first_states, first_far), (half + 1, last_states, last_far)):
        cut = rows_piece // 2
        for way, array in enumerate(far):
            for k in range(len(states)):
                sources.append((len(arrays), k * cut, cut, first_plane + k, 3, way * cut))
            arrays.append(array)
        for k, state in enumerate(states):
            for way, array in enumerate(state):
                sources.append((len(arrays), 0, rows_piece, first_plane + k, way + 1, 0))
                arrays.append(array)
    place_now = jnp.stack([moves.shard, moves.chip]).astype(jnp.int32)
    sizes = (rows_z, rows_piece, up_wide, width, fold, half_cols)
    gathered = Gathered(arrays, sources, place_now, sizes)
    residual, normed_two, inv_std_two, act_two, out_low = out_projection(
        gathered, out_own, attended, inputs, bias_out, gain_two, shift_two
    )

    act_two_other, attended_other, cot_other = together(
        moves.core_swap(act_two), moves.core_swap(attended), moves.core_swap(home_cot)
    )
    cot_pair = jnp.concatenate([home_cot, cot_other], axis=0)
    attended_pair = jnp.concatenate([attended, attended_other], axis=0)
    hidden_pair, slope_pair, up_half = up_projection(
        gathered, up_own, act_two, act_two_other, core_half(bias_up)
    )
    down_terms = dot_rows(hidden_pair, cot_pair).astype(bf16)
    down_state = moves.reduce_cut(down_terms.reshape(shards, chips, down_piece, width), 1)
    slope_pair, down_state = together(slope_pair, down_state)
    down_state = moves.reduce_start(down_state, 1)
    grad_y = home_cot.astype(f32)
    grad_bias_down = jnp.sum(grad_y, axis=0)
    grad_up_pair, grad_bias_up, down_half = hidden_backward(
        gathered, down_own, home_cot, cot_other, slope_pair
    )
    grad_bias_up = grad_bias_up.reshape(-1)
    back_other = moves.core_swap(up_backward(up_half, grad_up_pair, 1, bf16))
    up_terms = up_gradient(act_two, act_two_other, grad_up_pair)
    back_other, hidden_pair, up_terms, down_state = together(
        back_other, hidden_pair, up_terms, down_state
    )
    up_state = moves.reduce_open(up_terms.reshape(shards, chips, rows_piece, up_wide), 1)
    down_state = moves.reduce_add(down_state)
    grad_act_two = up_backward(up_half, grad_up_pair, 0, f32) + back_other.astype(f32)
    grad_gain_two = jnp.sum(grad_act_two * normed_two, axis=0)
    grad_shift_two = jnp.sum(grad_act_two, axis=0)
    grad_residual = grad_y + norm_back(grad_act_two, normed_two, inv_std_two, gain_two)
    grad_residual, down_state = together(grad_residual, down_state)
    down_state = moves.reduce_send(down_state, 1)
    grad_attn = grad_residual.astype(bf16)
    grad_bias_out = jnp.sum(grad_attn, axis=0, dtype=f32)
    to_members = jnp.stack(
        [
            dot_right(grad_attn, out_low[k * span : (k + 1) * span]).astype(bf16)
            for k in range(shards)
        ]
    )
    attn_halves = [grad_attn[:, :out_wide], grad_attn[:, out_wide:]]
    attn_own = jnp.where(core == 0, attn_halves[0], attn_halves[1])
    attn_other = jnp.where(core == 0, attn_halves[1], attn_halves[0])
    grad_heads, attn_other = together(moves.cores_exchange(to_members), moves.core_swap(attn_other))
    attn_pair = jnp.concatenate([attn_own, attn_other], axis=0)
    grad_heads, hidden_pair = together(grad_heads, hidden_pair)
    grad_heads = moves.members_exchange(grad_heads).reshape(group_rows, span)
    down_other = moves.core_swap(dot(hidden_pair[row_count:], down_half).astype(bf16))
    block_out = (
        residual + dot(hidden_pair[:row_count], down_half) + down_other.astype(f32) + bias_down
    ).astype(bf16)

    out_terms = dot_rows(attended_pair, attn_pair).astype(bf16)
    def shards_cut(piece, bits):
        piece = piece.reshape((piece.shape[0] // 2, 2) + piece.shape[1:])
        bit = moves.shard_bit(bits)
        return pick(piece, bit, 1), pick(piece, 1 - bit, 1)

    def shards_send(parts, bits):
        return parts[0], moves.shard_swap(parts[1], bits)

    def halved(state):
        own, other = state
        return (own.astype(f32) + other.astype(f32)).astype(bf16)

    def shards_sum(piece):
        rows = piece.shape[1]
        return lax.psum_scatter(
            piece.reshape(shards * rows, piece.shape[2]), "shard", scatter_dimension=0, tiled=True
        )

    out_state = moves.reduce_open(out_terms.reshape(shards, chips, rows_piece, out_wide), 1)
    grad_heads, down_state, up_state, out_state, block_out = together(
        grad_heads, down_state, up_state, out_state, block_out
    )
    block_out = moves.home_swap(block_out)
    down_owned = shards_sum(moves.reduce_final(down_state))
    up_out_state = [
        jnp.concatenate([up_part, out_part], axis=-1)
        for up_part, out_part in zip(moves.reduce_add(up_state), moves.reduce_add(out_state))
    ]
    grad_heads, up_out_state = together(grad_heads, up_out_state)
    up_out_state = moves.reduce_send(up_out_state, 1)
    attend_args = (plan, slopes)
    parts = 2 if heads % 4 == 0 else 1
    part_heads = heads // parts
    grad_qkv = attend_backward(
        qkv_rows, grad_heads, attended_cols, logs, *attend_args, part_heads, BLOCK, 0, None
    )
    grad_qkv, up_out_state = together(grad_qkv, up_out_state)
    up_out_cut = shards_cut(moves.reduce_final(up_out_state), 1)
    grad_qkv, up_out_cut = together(grad_qkv, up_out_cut)
    up_out_state = shards_send(up_out_cut, 1)
    if parts == 2:
        grad_qkv = attend_backward(
            qkv_rows, grad_heads, attended_cols, logs, *attend_args, part_heads, BLOCK, part_heads, grad_qkv
        )
    grad_qkv, up_out_state, block_out = together(grad_qkv, up_out_state, block_out)
    up_out_piece, bits = halved(up_out_state), 2
    while bits < half:
        up_out_piece = halved(shards_send(shards_cut(up_out_piece, bits), bits))
        bits *= 2
    up_out_state = shards_send(shards_cut(up_out_piece, half), half)

    grad_bias_q_part = jnp.sum(grad_qkv[:, :span], axis=0, dtype=f32)
    grad_bias_v_part = jnp.sum(grad_qkv[:, 2 * span :], axis=0, dtype=f32)

    grad_halves = grad_qkv.reshape(2, half * row_count, 3 * span)
    sent = dot_right(pick(grad_halves, 1 - core), qkv_cols).astype(bf16)
    sent = moves.core_swap(sent)
    qkv_terms = dot_rows(act_all, grad_qkv).astype(bf16)
    qkv_terms = qkv_terms.reshape(shards, chips, rows_piece, 3 * span)
    qkv_state = moves.reduce_open(qkv_terms, 1)
    back = dot_right(pick(grad_halves, core), qkv_cols) + sent.astype(f32)
    qkv_state, back, up_out_state = together(qkv_state, back, up_out_state)

    back = back.reshape(half, row_count, width)
    low_bits = list(reversed(moves.low_bits()))
    for bits in low_bits[:-1]:
        back = moves.reduce_bit(
            back, moves.shard_bit(bits), functools.partial(moves.shard_swap, bits=bits)
        )
    back = back.reshape((2, -1) + back.shape[1:])
    back_bit = moves.shard_bit(low_bits[-1])
    back_other = moves.shard_swap(pick(back, 1 - back_bit).astype(bf16), low_bits[-1])
    up_out_owned = halved(up_out_state)[0]
    up_out_open = moves.spread_open(up_out_owned)
    qkv_state = moves.reduce_send(moves.reduce_add(qkv_state), 1)
    qkv_state, up_out_open = together(qkv_state, up_out_open)

    up_out_far = moves.far_send(up_out_open)
    qkv_piece = moves.reduce_final(qkv_state)
    qkv_piece = qkv_piece.reshape((2, half) + qkv_piece.shape[1:])
    qkv_own = pick(qkv_piece, moves.side)
    qkv_other = moves.shard_swap(pick(qkv_piece, 1 - moves.side), half)
    back_other, qkv_other, up_out_far = together(back_other, qkv_other, up_out_far)

    qkv_piece = moves.half_exchange(halved((qkv_own, qkv_other)))
    down_state = moves.spread_open(down_owned)
    grad_act_one = pick(back, back_bit) + back_other.astype(f32)
    grad_act_one = grad_act_one.reshape(row_count, width)
    grad_gain_one = jnp.sum(grad_act_one * normed_one, axis=0)
    grad_shift_one = jnp.sum(grad_act_one, axis=0)
    grad_inputs = grad_residual + norm_back(grad_act_one, normed_one, inv_std_one, gain_one)
    grad_inputs, qkv_piece, down_state = together(grad_inputs.astype(bf16), qkv_piece, down_state)
    tokens_grad = moves.home_swap(grad_inputs)
    qkv_owned = moves.chips_gather(qkv_piece, 1)

    up_out_first, up_out_second = moves.core_pair(
        moves.chips_place(up_out_owned, 0, moves.spread_join(up_out_open, up_out_far)).reshape(
            rows_z, up_wide + out_wide
        )
    )
    out_grad = jnp.concatenate([up_out_first[:, up_wide:], up_out_second[:, up_wide:]], axis=1)
    up_columns = []
    for number in range(shards):
        part = slice(number * half_cols, (number + 1) * half_cols)
        up_columns += [up_out_first[:, part], up_out_second[:, part]]
    up_grad = jnp.concatenate(up_columns, axis=1)
    down_first, down_second = moves.core_pair(
        moves.chips_gather(down_owned, 0, tuple(down_state)).reshape(half_cols, width)
    )
    down_grad = jnp.concatenate([down_first, down_second], axis=0)
    qkv_first, qkv_second = moves.core_pair(qkv_owned.reshape(half, rows_z, 3 * span))
    qkv_columns = []
    for kind in range(3):
        for source in (qkv_first, qkv_second):
            for number in range(half):
                qkv_columns.append(source[number][:, kind * span : (kind + 1) * span])
    qkv_grad = jnp.concatenate(qkv_columns, axis=1)

    gradients = [qkv_grad, out_grad, up_grad, down_grad]
    heights = [width, width, width, hidden_width]
    stats = [
        factor_stats(gradient, old, decay_rate) for gradient, old in zip(gradients, rows_old)
    ]

    def to_sum(number):
        weight_sum = jnp.broadcast_to(weight_sums[number], (1, 128))
        return [stats[number][2], jnp.concatenate([stats[number][3], weight_sum], axis=0)]

    def spread_heads(part):
        return [jnp.where(member == number, part, 0.0) for number in range(shards)]

    bias_up_parts = []
    for number in range(shards):
        part = grad_bias_up[number * half_cols : (number + 1) * half_cols]
        bias_up_parts += [jnp.where(core == 0, part, 0.0), jnp.where(core == 1, part, 0.0)]
    vector_part = moves.sum_reps(
        jnp.concatenate(
            [grad_gain_one, grad_shift_one]
            + spread_heads(grad_bias_q_part)
            + spread_heads(grad_bias_v_part)
            + [grad_bias_out, grad_gain_two, grad_shift_two]
            + bias_up_parts
            + [grad_bias_down]
        )
    )
    vector_rows, tokens_grad = together(vector_part.reshape(2, -1), tokens_grad)
    all_sums = summed(moves, to_sum(0) + to_sum(1) + to_sum(2) + to_sum(3) + [vector_rows])
    sums = [all_sums[0:2], all_sums[2:4], all_sums[4:6], all_sums[6:8]]
    vector_grad = all_sums[8].reshape(-1)
    updates = []
    offset = 0
    for number in range(4):
        end_col = offset + gradients[number].shape[1]
        updates.append(
            factor_apply(
                gradients[number],
                weights[number],
                stats[number][0],
                sums[number][0],
                sums[number][1],
                col_state[offset:end_col].reshape(1, -1),
                heights[number],
                decay_rate,
            )
        )
        offset = end_col
    grads_out, new_weights, copies, new_cols, rms_rows = zip(*updates)
    rms_values = [rms[0, 0] for rms in rms_rows]

    vector_state_new = decay_rate * vector_state + (1.0 - decay_rate) * (
        vector_grad * vector_grad + eps_second
    )
    vector_step = vector_grad * lax.rsqrt(vector_state_new)
    vector_rms = jnp.sqrt(jnp.mean(vector_step * vector_step))
    vector_new = vectors - rate_step * jnp.sqrt(
        jnp.mean(vectors * vectors)
    ) * vector_step / jnp.maximum(1.0, vector_rms / clip_level)
    update_rms = jnp.stack(rms_values + [vector_rms])
    return (
        block_out,
        tokens_grad,
        *grads_out,
        vector_grad,
        *new_weights,
        vector_new,
        *copies,
        jnp.concatenate([stats[0][1], stats[1][1], stats[2][1]], axis=0),
        stats[3][1].reshape(-1),
        jnp.concatenate(new_cols, axis=1).reshape(-1),
        vector_state_new,
        update_rms,
    )


def solution(mesh):
    in_specs = (
        P(("rep", "shard"), None),
        P(("rep", "shard"), None),
        P("rep", None),
        P("shard", None),
        P("shard", None),
        P("shard", None),
        P("shard", None),
        P(),
        P(None, "shard"),
        P("shard"),
        P(),
        P(),
    )
    out_specs = (
        P(("rep", "shard"), None),
        P(("rep", "shard"), None),
        P("shard", None),
        P("shard", None),
        P("shard", None),
        P("shard", None),
        P(),
        P("shard", None),
        P("shard", None),
        P("shard", None),
        P("shard", None),
        P(),
        P("shard", None),
        P("shard", None),
        P("shard", None),
        P("shard", None),
        P(None, "shard"),
        P("shard"),
        P(),
        P(),
        P(),
    )
    return jax.shard_map(
        on_device, mesh=mesh, in_specs=in_specs, out_specs=out_specs, check_vma=False
    )
```

```python
import functools

import jax
import jax.numpy as jnp
from jax import lax
from jax.experimental import pallas as pl
from jax.experimental.pallas import tpu as pltpu
from jax.sharding import PartitionSpec as P

HEADS = 16
STEP = 10
BLOCK = 256


eps_norm = 1e-05
eps_second = 1e-30
rate_step = 0.5
clip_level = 1.0
masked = -1e30
gelu_root = (2.0 / 3.141592653589793) ** 0.5
gelu_cubic = 0.044715

f32 = jnp.float32
bf16 = jnp.bfloat16


def norm_parts(values):
    average = jnp.mean(values, axis=-1, keepdims=True)
    centred = values - average
    inv_std = lax.rsqrt(jnp.mean(centred * centred, axis=-1, keepdims=True) + eps_norm)
    return (centred * inv_std, inv_std)


def norm_back(grad_out, normed, inv_std, gain_vec):
    grad_normed = grad_out * gain_vec
    inner_mean = jnp.mean(grad_normed * normed, axis=-1, keepdims=True)
    centred = grad_normed - jnp.mean(grad_normed, axis=-1, keepdims=True)
    return (centred - normed * inner_mean) * inv_std


def gelu_value(pre_act):
    curve = jnp.tanh(gelu_root * (pre_act + gelu_cubic * pre_act * pre_act * pre_act))
    return 0.5 * pre_act * (1.0 + curve)


def gelu_slope(pre_act):
    square = pre_act * pre_act
    curve = jnp.tanh(gelu_root * (pre_act + gelu_cubic * square * pre_act))
    inner = gelu_root * (1.0 + 3.0 * gelu_cubic * square)
    return 0.5 * (1.0 + curve) + 0.5 * pre_act * (1.0 - curve * curve) * inner


def dot(left_side, right_side):
    return jnp.dot(left_side, right_side, preferred_element_type=f32)


def dot_right(left_side, right_side):
    return lax.dot_general(
        left_side, right_side, (((1,), (1,)), ((), ())), preferred_element_type=f32
    )


def dot_rows(left_side, right_side):
    return lax.dot_general(
        left_side, right_side, (((0,), (0,)), ((), ())), preferred_element_type=f32
    )


def pick(stack, index, axis=0):
    return lax.dynamic_index_in_dim(stack, index, axis, keepdims=False)


def place(stack, part, index, axis=0):
    return lax.dynamic_update_index_in_dim(stack, part, index, axis)


def head_rows(number, head_width):
    return slice(number * head_width, (number + 1) * head_width)


def lane_masks(block_rows, width, heads):
    lanes = lax.broadcasted_iota(jnp.int32, (block_rows, width), 1)
    head_width = width // heads
    return [
        (lanes >= number * head_width) & (lanes < (number + 1) * head_width)
        for number in range(heads)
    ]


def allowed_pairs(key_block, query_block, start_row, block):
    key_pos = lax.broadcasted_iota(jnp.int32, (block, block), 0) + key_block * block
    query_pos = lax.broadcasted_iota(jnp.int32, (block, block), 1) + query_block * block
    return (key_pos <= query_pos) & (key_pos >= start_row)


def key_offsets(key_block, query_block, block):
    rows = lax.broadcasted_iota(jnp.int32, (block, 1), 0)
    return (rows + (key_block - query_block) * block).astype(f32)


def turned(values):
    return jnp.transpose(values.astype(f32))


def head_stack(values, lanes):
    zero = jnp.zeros(values.shape, values.dtype)
    return jnp.concatenate([jnp.where(lane, values, zero) for lane in lanes], axis=0)


def eights(values, combine):
    rows, columns = values.shape
    return combine(values.reshape(rows // 8, 8, columns), axis=0)


def forward_kernel(
    heads,
    block,
    low_ref,
    mid_ref,
    slope_ref,
    start_ref,
    qkv_ref,
    out_ref,
    log_ref,
    values_turned,
    key_stack,
    score_ref,
):
    tokens = qkv_ref.shape[0]
    width = qkv_ref.shape[1] // 3
    head_width = width // heads
    blocks = tokens // block
    query_block = pl.program_id(0)

    @pl.when(query_block == 0)
    def _():
        lanes = lane_masks(block, width, heads)
        for number in range(blocks):
            rows = slice(number * block, (number + 1) * block)
            values_turned[number] = turned(qkv_ref[rows, 2 * width :]).astype(bf16)
            key_stack[number] = head_stack(qkv_ref[rows, width : 2 * width], lanes)

    first_row = pl.multiple_of(query_block * block, block)
    queries = qkv_ref[pl.ds(first_row, block), :width].astype(f32) * head_width ** (-0.5)
    queries = turned(queries).astype(bf16)
    start_row = start_ref[query_block]

    def score_step(key_block, bests, with_mask):
        scores = dot(key_stack[key_block], queries)
        offsets = key_offsets(key_block, query_block, block)
        allowed = allowed_pairs(key_block, query_block, start_row, block) if with_mask else None
        result = []
        for number in range(heads):
            rows = head_rows(number, block)
            part = scores[rows] + slope_ref[number] * offsets
            if with_mask:
                part = jnp.where(allowed, part, masked)
            score_ref[key_block, rows, :] = part
            result.append(jnp.maximum(bests[number], eights(part, jnp.max)))
        return tuple(result)

    low, mid = low_ref[query_block], mid_ref[query_block]
    bests = tuple(jnp.full((8, block), masked, f32) for _ in range(heads))
    bests = lax.fori_loop(low, mid, functools.partial(score_step, with_mask=True), bests)
    bests = lax.fori_loop(mid, query_block, functools.partial(score_step, with_mask=False), bests)
    bests = score_step(query_block, bests, True)
    bests = [jnp.max(best, axis=0, keepdims=True) for best in bests]

    def value_step(key_block, state):
        result = []
        for number in range(heads):
            total, gathered = state[2 * number : 2 * number + 2]
            weights = jnp.exp(score_ref[key_block, head_rows(number, block), :] - bests[number])
            value_rows = values_turned[key_block, head_rows(number, head_width), :]
            result += [
                total + eights(weights, jnp.sum),
                gathered + dot(value_rows, weights.astype(bf16)),
            ]
        return tuple(result)

    state = ()
    for number in range(heads):
        state += (jnp.zeros((8, block), f32), jnp.zeros((head_width, block), f32))
    state = lax.fori_loop(low, query_block + 1, value_step, state)
    columns = []
    for number in range(heads):
        total = jnp.sum(state[2 * number], axis=0, keepdims=True)
        columns.append(state[2 * number + 1] / total)
        log_ref[0, number : number + 1, :] = bests[number] + jnp.log(total)
    out_ref[...] = jnp.transpose(jnp.concatenate(columns, axis=0)).astype(bf16)


def backward_kernel(heads, block, first_head, merge, *refs):
    full_ref, high_ref, slope_ref, start_ref, log_ref, qkv_ref, grad_ref, out_ref = refs[:8]
    earlier_ref = refs[8] if merge else None
    result_ref = refs[9 if merge else 8]
    (
        queries_turned,
        grads_turned,
        keys_turned,
        query_stack,
        grad_stack,
        key_stack,
        value_stack,
        delta_rows,
        query_grads,
    ) = refs[10 if merge else 9 :]
    tokens, all_width = grad_ref.shape
    head_width = all_width // log_ref.shape[1]
    width = heads * head_width
    scale = head_width ** (-0.5)
    blocks = tokens // block
    key_block = pl.program_id(0)
    lanes = lane_masks(block, width, heads)

    def columns(kind):
        start = kind * all_width + first_head * head_width
        return slice(start, start + width)

    def target(kind):
        start = (kind * all_width + first_head * head_width) if merge else kind * width
        return slice(start, start + width)

    @pl.when(key_block == 0)
    def _():
        for number in range(blocks):
            rows = slice(number * block, (number + 1) * block)
            queries = qkv_ref[rows, columns(0)]
            queries_turned[number] = turned(queries.astype(f32) * scale).astype(bf16)
            query_stack[number] = head_stack(queries, lanes)
            keys_turned[number] = turned(qkv_ref[rows, columns(1)]).astype(bf16)
            grads = grad_ref[rows, columns(0)]
            grad_stack[number] = head_stack(grads, lanes)
            grads = grads.astype(f32)
            grads_turned[number] = turned(grads).astype(bf16)
            product = turned(grads * out_ref[rows, columns(0)].astype(f32))
            for head in range(heads):
                delta_rows[number, head : head + 1, :] = jnp.sum(
                    product[head_rows(head, head_width)], axis=0, keepdims=True
                )
            query_grads[number] = jnp.zeros((width, block), f32)

    key_row = pl.multiple_of(key_block * block, block)
    key_stack[...] = head_stack(qkv_ref[pl.ds(key_row, block), columns(1)], lanes)
    value_stack[...] = head_stack(qkv_ref[pl.ds(key_row, block), columns(2)], lanes)

    def step(query_block, state, with_mask):
        key_total, value_total = state
        scores = dot(key_stack[...], queries_turned[query_block])
        grad_weights = dot(value_stack[...], grads_turned[query_block])
        offsets = key_offsets(key_block, query_block, block)
        if with_mask:
            allowed = allowed_pairs(key_block, query_block, start_ref[query_block], block)
        weight_list, grad_list = [], []
        for number in range(heads):
            rows = head_rows(number, block)
            head = first_head + number
            part = scores[rows] + slope_ref[head] * offsets
            part = part - log_ref[query_block, head : head + 1, :]
            if with_mask:
                part = jnp.where(allowed, part, masked)
            probabilities = jnp.exp(part)
            delta = delta_rows[query_block, number : number + 1, :]
            grad_scores = (probabilities * (grad_weights[rows] - delta)).astype(bf16)
            weight_list.append(probabilities.astype(bf16))
            grad_list.append(grad_scores)
            rows = head_rows(number, head_width)
            query_grads[query_block, rows, :] += dot(keys_turned[key_block, rows, :], grad_scores)
        weight_row = jnp.concatenate(weight_list, axis=1)
        grad_row = jnp.concatenate(grad_list, axis=1)
        return (
            key_total + dot(grad_row, query_stack[query_block]),
            value_total + dot(weight_row, grad_stack[query_block]),
        )

    state = (jnp.zeros((block, width), f32), jnp.zeros((block, width), f32))
    state = step(key_block, state, True)
    full, high = full_ref[key_block], high_ref[key_block]
    state = lax.fori_loop(key_block + 1, full, functools.partial(step, with_mask=False), state)
    state = lax.fori_loop(full, high, functools.partial(step, with_mask=True), state)
    result_ref[pl.ds(key_row, block), target(1)] = (state[0] * scale).astype(bf16)
    result_ref[pl.ds(key_row, block), target(2)] = state[1].astype(bf16)
    if merge:
        other = first_head * head_width
        for kind in range(3):
            result_ref[pl.ds(key_row, block), kind * all_width : kind * all_width + other] = earlier_ref[
                pl.ds(key_row, block), kind * other : (kind + 1) * other
            ]

    @pl.when(key_block == blocks - 1)
    def _():
        for number in range(blocks):
            rows = slice(number * block, (number + 1) * block)
            result_ref[rows, target(0)] = jnp.transpose(query_grads[number] * scale).astype(bf16)


def block_plan(lengths, tokens, block):
    ends = jnp.cumsum(lengths)
    positions = jnp.arange(tokens, dtype=jnp.int32)
    passed = positions[:, None] >= ends[None, :]
    starts = jnp.max(jnp.where(passed, ends[None, :], 0), axis=1).astype(jnp.int32)
    finish = jnp.min(jnp.where(passed, tokens, ends[None, :]), axis=1).astype(jnp.int32)
    blocks = tokens // block
    number = jnp.arange(blocks, dtype=jnp.int32)
    first_start = starts[::block]
    last_start = starts[block - 1 :: block]
    low = first_start // block
    mid = jnp.clip((last_start + block - 1) // block, low, number)
    high = (finish[block - 1 :: block] - 1) // block + 1
    full = jnp.clip(finish[::block] // block, number + 1, high)
    return (starts.reshape(blocks, 1, block), low, mid, full, high)


def scalar_spec():
    return pl.BlockSpec(memory_space=pltpu.SMEM)


def whole_spec(shape):
    return pl.BlockSpec(shape, lambda step: (0,) * len(shape), pipeline_mode=pl.Buffered(1))


def attend_forward(qkv, plan, slopes, heads, block):
    tokens, triple = qkv.shape
    width = triple // 3
    blocks = tokens // block
    starts, low, mid, full, high = plan
    return pl.pallas_call(
        functools.partial(forward_kernel, heads, block),
        grid=(blocks,),
        in_specs=[
            scalar_spec(),
            scalar_spec(),
            scalar_spec(),
            whole_spec((blocks, 1, block)),
            whole_spec((tokens, triple)),
        ],
        out_specs=[
            pl.BlockSpec((block, width), lambda step: (step, 0)),
            pl.BlockSpec((1, heads, block), lambda step: (step, 0, 0)),
        ],
        out_shape=[
            jax.ShapeDtypeStruct((tokens, width), bf16),
            jax.ShapeDtypeStruct((blocks, heads, block), f32),
        ],
        scratch_shapes=[
            pltpu.VMEM((blocks, width, block), bf16),
            pltpu.VMEM((blocks, heads * block, width), bf16),
            pltpu.VMEM((blocks, heads * block, block), f32),
        ],
        compiler_params=pltpu.CompilerParams(
            dimension_semantics=("arbitrary",), vmem_limit_bytes=28 * 1024 * 1024
        ),
        cost_estimate=pl.CostEstimate(
            flops=3 * tokens * tokens * 256 * heads,
            bytes_accessed=10 * tokens * width,
            transcendentals=tokens * tokens * heads // 2,
        ),
        name="attend_forward",
    )(low, mid, slopes, starts, qkv)


def attend_backward(qkv, grads, outputs, logs, plan, slopes, heads, block, first_head, earlier):
    tokens, triple = qkv.shape
    all_width = triple // 3
    all_heads = logs.shape[1]
    width = all_width // all_heads * heads
    blocks = tokens // block
    starts, low, mid, full, high = plan
    merge = earlier is not None
    result_width = triple if merge else 3 * width
    operands = [full, high, slopes, starts, logs, qkv, grads, outputs]
    specs = [scalar_spec() for _ in range(3)] + [whole_spec(entry.shape) for entry in operands[3:]]
    if merge:
        operands.append(earlier)
        specs.append(whole_spec(earlier.shape))
    return pl.pallas_call(
        functools.partial(backward_kernel, heads, block, first_head, merge),
        grid=(blocks,),
        in_specs=specs,
        out_specs=pl.BlockSpec((tokens, result_width), lambda step: (0, 0)),
        out_shape=jax.ShapeDtypeStruct((tokens, result_width), bf16),
        scratch_shapes=[
            pltpu.VMEM((blocks, width, block), bf16),
            pltpu.VMEM((blocks, width, block), bf16),
            pltpu.VMEM((blocks, width, block), bf16),
            pltpu.VMEM((blocks, heads * block, width), bf16),
            pltpu.VMEM((blocks, heads * block, width), bf16),
            pltpu.VMEM((heads * block, width), bf16),
            pltpu.VMEM((heads * block, width), bf16),
            pltpu.VMEM((blocks, heads, block), f32),
            pltpu.VMEM((blocks, width, block), f32),
        ],
        compiler_params=pltpu.CompilerParams(
            dimension_semantics=("arbitrary",), vmem_limit_bytes=28 * 1024 * 1024
        ),
        cost_estimate=pl.CostEstimate(
            flops=8 * tokens * tokens * 256 * heads,
            bytes_accessed=20 * tokens * width,
            transcendentals=tokens * tokens * heads // 2,
        ),
        name="attend_backward",
    )(*operands)


def together(*values):
    return lax.optimization_barrier(tuple(values))


def ordered(own, other, bit, axis=0):
    first = jnp.where(bit == 0, own, other)
    second = jnp.where(bit == 0, other, own)
    return jnp.stack([first, second], axis=axis)


class Moves:
    def __init__(self):
        self.shards = lax.axis_size("shard")
        self.reps = lax.axis_size("rep")
        self.half = self.shards // 2
        self.chips = self.reps // 2
        self.shard = lax.axis_index("shard")
        self.rep = lax.axis_index("rep")
        self.core = self.rep % 2
        self.chip = self.rep // 2
        self.side = self.shard // self.half
        self.member = self.shard % self.half + self.core * self.half

    def core_swap(self, part):
        return lax.ppermute(part, "rep", [(r, r ^ 1) for r in range(self.reps)])

    def chip_swap(self, part, bits):
        return lax.ppermute(part, "rep", [(r, r ^ (2 * bits)) for r in range(self.reps)])

    def shard_swap(self, part, bits):
        return lax.ppermute(part, "shard", [(s, s ^ bits) for s in range(self.shards)])

    def shard_bit(self, bits):
        return (self.shard // bits) % 2

    def low_bits(self):
        bits, result = 1, []
        while bits < self.half:
            result.append(bits)
            bits *= 2
        return result

    def home_send(self, part):
        pairs = []
        for rep in range(self.reps):
            for shard in range(self.shards):
                if shard // self.half != rep % 2:
                    to_shard = (shard + self.half) % self.shards
                    pairs.append((rep * self.shards + shard, (rep ^ 1) * self.shards + to_shard))
        return lax.ppermute(part, ("rep", "shard"), pairs)

    def home_join(self, part, other):
        return jnp.where(self.side == self.core, part, other)

    def half_gather(self, part):
        stack = part[None]
        for bits in self.low_bits():
            own = stack
            stack = ordered(own, self.shard_swap(own, bits), self.shard_bit(bits))
            stack = stack.reshape((-1,) + part.shape)
        return stack

    def cores_gather(self, stack):
        stack = ordered(stack, self.core_swap(stack), self.core)
        return stack.reshape((-1,) + stack.shape[2:])

    def exchange_bit(self, stack, bit, swap):
        sources, targets = stack.shape[:2]
        stack = stack.reshape((sources, 2, targets // 2) + stack.shape[2:])
        own, other = pick(stack, bit, 1), swap(pick(stack, 1 - bit, 1))
        return ordered(own, other, bit, 1).reshape((2 * sources,) + own.shape[1:])

    def half_exchange(self, stack):
        stack = stack[None]
        for bits in reversed(self.low_bits()):
            swap = functools.partial(self.shard_swap, bits=bits)
            stack = self.exchange_bit(stack, self.shard_bit(bits), swap)
        return stack.reshape((self.half,) + stack.shape[2:])

    def cores_exchange(self, stack):
        return self.exchange_bit(stack[None], self.core, self.core_swap)

    def members_exchange(self, stack):
        for bits in reversed(self.low_bits()):
            swap = functools.partial(self.shard_swap, bits=bits)
            stack = self.exchange_bit(stack, self.shard_bit(bits), swap)
        return stack.reshape((self.shards,) + stack.shape[2:])

    def reduce_bit(self, stack, bit, swap):
        stack = stack.reshape((2, stack.shape[0] // 2) + stack.shape[1:])
        other = swap(pick(stack, 1 - bit).astype(bf16))
        return pick(stack, bit).astype(f32) + other.astype(f32)

    def spread_open(self, part):
        if self.chips == 4:
            return (self.chip_swap(part, 1), self.chip_swap(part, 2))
        held, bits = [part], 1
        while bits < self.chips:
            held = held + [self.chip_swap(piece, bits) for piece in held]
            bits *= 2
        return tuple(held[1:])

    def spread_close(self, state):
        if self.chips == 4:
            by_x, by_y = state
            cut, axis = by_x.shape[-2] // 2, by_x.ndim - 2
            far = [
                self.chip_swap(by_x[..., :cut, :], 2),
                self.chip_swap(by_y[..., cut:, :], 1),
            ]
            return (by_x, by_y, jnp.concatenate(far, axis=axis))
        return state

    def far_open(self, states):
        if self.chips != 4:
            return ()
        cut = states[0][0].shape[0] // 2
        return (
            self.chip_swap(jnp.concatenate([by_x[:cut] for by_x, _ in states], axis=0), 2),
            self.chip_swap(jnp.concatenate([by_y[cut:] for _, by_y in states], axis=0), 1),
        )

    def far_parts(self, states, far):
        if self.chips != 4:
            return [[(k + 1, 0, part) for k, part in enumerate(state)] for state in states]
        cut = states[0][0].shape[0] // 2
        result = []
        for number, (by_x, by_y) in enumerate(states):
            rows = slice(number * cut, (number + 1) * cut)
            result.append([(1, 0, by_x), (2, 0, by_y), (3, 0, far[0][rows]), (3, cut, far[1][rows])])
        return result

    def chips_gather(self, part, axis, state=None):
        shape = part.shape[:axis] + (self.chips,) + part.shape[axis:]
        stack = place(jnp.zeros(shape, part.dtype), part, self.chip, axis)
        others = self.spread_close(self.spread_open(part) if state is None else state)
        for number, piece in enumerate(others):
            stack = place(stack, piece, self.chip ^ (number + 1), axis)
        return stack

    def reduce_open(self, stack, axis):
        if self.chips == 4:
            shape = stack.shape[:axis] + (2, 2) + stack.shape[axis + 1 :]
            stack = stack.reshape(shape)
            bit_x, bit_y = self.chip % 2, self.chip // 2
            cut = shape[0] // 2
            first, second = stack[:cut], stack[cut:]
            got_first = self.chip_swap(pick(first, 1 - bit_x, axis + 1), 1)
            got_second = self.chip_swap(pick(second, 1 - bit_y, axis), 2)
            return (pick(first, bit_x, axis + 1), pick(second, bit_y, axis), got_first, got_second)
        count = self.chips
        stack = stack.astype(f32)
        while count > 1:
            count //= 2
            shape = stack.shape[:axis] + (2, count) + stack.shape[axis + 1 :]
            stack = stack.reshape(shape)
            bit = (self.chip // count) % 2
            got = self.chip_swap(pick(stack, 1 - bit, axis).astype(bf16), count)
            stack = pick(stack, bit, axis) + got.astype(f32)
        return (pick(stack, 0, axis).astype(bf16),)

    def reduce_add(self, state):
        if self.chips != 4:
            return state
        first, second, got_first, got_second = state
        first = (first.astype(f32) + got_first.astype(f32)).astype(bf16)
        second = (second.astype(f32) + got_second.astype(f32)).astype(bf16)
        return (first, second)

    def reduce_send(self, state, axis):
        if self.chips != 4:
            return state
        first, second = state
        bit_x, bit_y = self.chip % 2, self.chip // 2
        got_first = self.chip_swap(pick(first, 1 - bit_y, axis), 2)
        got_second = self.chip_swap(pick(second, 1 - bit_x, axis), 1)
        return (pick(first, bit_y, axis), pick(second, bit_x, axis), got_first, got_second)

    def reduce_final(self, state):
        if self.chips != 4:
            return state[0]
        first, second, got_first, got_second = state
        first = first.astype(f32) + got_first.astype(f32)
        second = second.astype(f32) + got_second.astype(f32)
        return jnp.concatenate([first, second], axis=0).astype(bf16)

    def reduce_close(self, state, axis):
        return self.reduce_final(self.reduce_send(state, axis))

    def core_pair(self, part):
        other = self.core_swap(part)
        first = jnp.where(self.core == 0, part, other)
        second = jnp.where(self.core == 0, other, part)
        return first, second

    def sum_reps(self, vector):
        bits = 1
        while bits < self.reps:
            vector = vector + lax.ppermute(vector, "rep", [(r, r ^ bits) for r in range(self.reps)])
            bits *= 2
        return vector

    def sum_shards(self, vector):
        bits = 1
        while bits < self.shards:
            vector = vector + self.shard_swap(vector, bits)
            bits *= 2
        return vector


def stats_kernel(decay_rate, gradient_ref, old_ref, rows_ref, lane_rows_ref, sums_ref, total_ref, partial):
    step = pl.program_id(0)
    rows, columns = gradient_ref.shape

    @pl.when(step == 0)
    def _():
        partial[...] = jnp.zeros_like(partial)
        total_ref[...] = jnp.zeros_like(total_ref)

    gradient = gradient_ref[...].astype(f32)
    square = gradient * gradient
    row_mean = jnp.sum(square, axis=1, keepdims=True) / columns
    old = jnp.transpose(jnp.broadcast_to(old_ref[...], (128, rows)))[:, 0:1]
    rows_new = decay_rate * old + (1.0 - decay_rate) * (row_mean + eps_second)
    rows_ref[...] = rows_new
    lane_rows_ref[...] = jnp.transpose(jnp.broadcast_to(rows_new, (rows, 128)))[0:1, :]
    total_ref[...] += jnp.broadcast_to(jnp.sum(rows_new, axis=0, keepdims=True), (1, 128))
    partial[0:8, :] += eights(square, jnp.sum)
    partial[8:16, :] += eights(square * (1.0 / rows_new), jnp.sum)

    @pl.when(step == pl.num_programs(0) - 1)
    def _():
        sums_ref[0:1, :] = jnp.sum(partial[0:8, :], axis=0, keepdims=True)
        sums_ref[1:2, :] = jnp.sum(partial[8:16, :], axis=0, keepdims=True)


def factor_stats(gradient, rows_old, decay_rate):
    height, breadth = gradient.shape
    rows = min(128, height)
    return pl.pallas_call(
        functools.partial(stats_kernel, decay_rate),
        grid=(height // rows,),
        in_specs=[
            pl.BlockSpec((rows, breadth), lambda step: (step, 0)),
            pl.BlockSpec((1, rows), lambda step: (0, step)),
        ],
        out_specs=[
            pl.BlockSpec((rows, 1), lambda step: (step, 0)),
            pl.BlockSpec((1, rows), lambda step: (0, step)),
            pl.BlockSpec((2, breadth), lambda step: (0, 0)),
            pl.BlockSpec((1, 128), lambda step: (0, 0)),
        ],
        out_shape=[
            jax.ShapeDtypeStruct((height, 1), f32),
            jax.ShapeDtypeStruct((1, height), f32),
            jax.ShapeDtypeStruct((2, breadth), f32),
            jax.ShapeDtypeStruct((1, 128), f32),
        ],
        scratch_shapes=[pltpu.VMEM((16, breadth), f32)],
        compiler_params=pltpu.CompilerParams(
            dimension_semantics=("arbitrary",), vmem_limit_bytes=16 * 1024 * 1024
        ),
        name="factor_stats",
    )(gradient, rows_old)


def apply_kernel(
    decay_rate,
    height,
    gradient_ref,
    weight_ref,
    rows_ref,
    sums_ref,
    scalar_ref,
    old_ref,
    gradient_out,
    weight_out,
    copy_out,
    cols_out,
    rms_out,
    col_factor,
):
    columns = gradient_ref.shape[1]

    @pl.when(pl.program_id(0) == 0)
    def _():
        cols_new = decay_rate * old_ref[...] + (1.0 - decay_rate) * (
            sums_ref[0:1, :] / height + eps_second
        )
        row_mean = scalar_ref[0:1, 0:1] / height
        weight_mean = scalar_ref[1:2, 0:1] / (height * columns)
        scaled = jnp.sum(sums_ref[1:2, :] / cols_new, axis=1, keepdims=True)
        rms_update = jnp.sqrt(row_mean / (height * columns) * scaled)
        factor = rate_step * jnp.sqrt(weight_mean) * jnp.sqrt(row_mean)
        factor = factor / jnp.maximum(1.0, rms_update / clip_level)
        col_factor[...] = factor * lax.rsqrt(cols_new)
        cols_out[...] = cols_new
        rms_out[...] = jnp.broadcast_to(rms_update, (1, 128))

    gradient = gradient_ref[...].astype(f32)
    new_weight = weight_ref[...] - gradient * lax.rsqrt(rows_ref[...]) * col_factor[...]
    gradient_out[...] = gradient
    weight_out[...] = new_weight
    copy_out[...] = new_weight.astype(bf16)


def factor_apply(gradient, weight, rows_new, sums, scalars, cols_old, height, decay_rate):
    own_height, breadth = gradient.shape
    rows = min(64, own_height)

    def rows_spec():
        return pl.BlockSpec((rows, breadth), lambda step: (step, 0))

    def row_spec(count, wide):
        return pl.BlockSpec((count, wide), lambda step: (0, 0))

    return pl.pallas_call(
        functools.partial(apply_kernel, decay_rate, height),
        grid=(own_height // rows,),
        in_specs=[
            rows_spec(),
            rows_spec(),
            pl.BlockSpec((rows, 1), lambda step: (step, 0)),
            row_spec(2, breadth),
            row_spec(2, 128),
            row_spec(1, breadth),
        ],
        out_specs=[rows_spec(), rows_spec(), rows_spec(), row_spec(1, breadth), row_spec(1, 128)],
        out_shape=[
            jax.ShapeDtypeStruct((own_height, breadth), f32),
            jax.ShapeDtypeStruct((own_height, breadth), f32),
            jax.ShapeDtypeStruct((own_height, breadth), bf16),
            jax.ShapeDtypeStruct((1, breadth), f32),
            jax.ShapeDtypeStruct((1, 128), f32),
        ],
        scratch_shapes=[pltpu.VMEM((1, breadth), f32)],
        compiler_params=pltpu.CompilerParams(
            dimension_semantics=("arbitrary",), vmem_limit_bytes=16 * 1024 * 1024
        ),
        name="factor_apply",
    )(gradient, weight, rows_new, sums, scalars, cols_old)


def summed(moves, entries):
    total = moves.sum_shards(jnp.concatenate(entries, axis=1))
    result, offset = [], 0
    for entry in entries:
        result.append(total[:, offset : offset + entry.shape[1]])
        offset += entry.shape[1]
    return result


def on_device(
    tokens,
    cotangent,
    seq_lengths,
    qkv_weight,
    out_weight,
    up_weight,
    down_weight,
    vectors,
    row_state,
    down_rows,
    col_state,
    vector_state,
):
    moves = Moves()
    shards, half, chips, core = moves.shards, moves.half, moves.chips, moves.core
    row_count, width = tokens.shape
    hidden_width = up_weight.shape[1]
    group_rows = row_count * shards
    heads = HEADS // shards
    head_width = width // HEADS
    span = heads * head_width
    member = moves.member
    decay_rate = 1.0 - STEP ** (-0.8)
    head_number = (member * heads + jnp.arange(heads, dtype=jnp.int32)).astype(f32)
    slopes = jnp.exp2(-8.0 * (head_number + 1.0) / HEADS)

    gain_one = vectors[0:width]
    shift_one = vectors[width : 2 * width]
    bias_query = vectors[2 * width : 3 * width]
    bias_value = vectors[3 * width : 4 * width]
    bias_out = vectors[4 * width : 5 * width]
    gain_two = vectors[5 * width : 6 * width]
    shift_two = vectors[6 * width : 7 * width]
    bias_up = vectors[7 * width : 7 * width + hidden_width]
    bias_down = vectors[7 * width + hidden_width :]

    other_tokens = moves.home_send(tokens)
    other_lengths = moves.core_swap(seq_lengths)
    lengths = jnp.where(moves.side == core, seq_lengths, other_lengths)[0]
    plan = block_plan(lengths, group_rows, BLOCK)
    rows_z = width // shards
    rows_piece = rows_z // chips
    my_rows = lax.dynamic_slice_in_dim(qkv_weight, moves.chip * rows_piece, rows_piece, 0)
    my_rows = my_rows.astype(bf16)
    my_blocks = []
    for number in range(half):
        kinds = []
        for kind in range(3):
            first = kind * width + number * span
            second = first + half * span
            kinds.append(
                jnp.where(
                    core == 0, my_rows[:, first : first + span], my_rows[:, second : second + span]
                )
            )
        my_blocks.append(jnp.concatenate(kinds, axis=1))
    qkv_part = moves.half_exchange(jnp.stack(my_blocks))
    half_cols = hidden_width // (2 * shards)
    up_wide = shards * half_cols
    out_wide = width // 2
    down_piece = half_cols // chips

    def core_half(values):
        parts = []
        for number in range(shards):
            start = 2 * number * half_cols
            first = values[..., start : start + half_cols]
            second = values[..., start + half_cols : start + 2 * half_cols]
            parts.append(jnp.where(core == 0, first, second))
        return jnp.concatenate(parts, axis=-1)

    up_own = core_half(up_weight).astype(bf16).reshape(chips, rows_piece, up_wide)
    out_own = jnp.where(core == 0, out_weight[:, :out_wide], out_weight[:, out_wide:]).astype(bf16)
    out_own = out_own.reshape(chips, rows_piece, out_wide)
    down_own = lax.dynamic_slice_in_dim(down_weight, core * half_cols, half_cols, 0).astype(bf16)
    fold = down_piece // rows_piece
    down_own = down_own.reshape(chips, fold, rows_piece, width)
    my_down = pick(down_own, moves.chip)
    weight_piece = jnp.concatenate(
        [pick(up_own, moves.chip), pick(out_own, moves.chip)] + [my_down[k] for k in range(fold)],
        axis=1,
    )
    near_pieces, bits = [weight_piece], 1
    while bits < half:
        near_pieces = near_pieces + [moves.shard_swap(piece, bits) for piece in near_pieces]
        bits *= 2
    near_pieces = near_pieces[1:]
    weights = [qkv_weight, out_weight, up_weight, down_weight]
    weight_sums = [jnp.sum(weight * weight) for weight in weights]
    other_tokens, qkv_part, near_pieces, weight_piece, plan, weight_sums = together(
        other_tokens, qkv_part, near_pieces, weight_piece, plan, weight_sums
    )
    home_tokens = moves.home_join(tokens, other_tokens)
    far_piece = moves.shard_swap(weight_piece, half)
    near_open = [moves.spread_open(piece) for piece in near_pieces]
    qkv_far = moves.shard_swap(qkv_part, half)
    qkv_far, near_open = together(qkv_far, near_open)
    qkv_part = ordered(qkv_part, qkv_far, moves.side).reshape(shards, rows_piece, 3 * span)
    qkv_cols = moves.chips_gather(qkv_part, 1).reshape(width, 3 * span)
    inputs = home_tokens.astype(f32)
    normed_one, inv_std_one = norm_parts(inputs)
    act_one = (normed_one * gain_one + shift_one).astype(bf16)
    act_half = moves.half_gather(act_one)

    act_half, qkv_cols, far_piece, cotangent = together(
        act_half, qkv_cols, far_piece, cotangent
    )
    other_cot = moves.home_send(cotangent)
    act_all = moves.cores_gather(act_half).reshape(group_rows, width)
    far_open = moves.spread_open(far_piece)
    far_pieces, bits = [far_piece], 1
    while bits < half:
        far_pieces = far_pieces + [moves.shard_swap(piece, bits) for piece in far_pieces]
        bits *= 2
    far_pieces = far_pieces[1:]

    bias_q_part = lax.dynamic_slice_in_dim(bias_query, member * span, span)
    bias_v_part = lax.dynamic_slice_in_dim(bias_value, member * span, span)
    qkv_bias = jnp.concatenate([bias_q_part, jnp.zeros_like(bias_q_part), bias_v_part])
    qkv_rows = (dot(act_all, qkv_cols) + qkv_bias).astype(bf16)
    attended_cols, logs = attend_forward(qkv_rows, plan, slopes, heads, BLOCK)
    attended_cols, far_open, far_pieces, other_cot = together(
        attended_cols, far_open, far_pieces, other_cot
    )
    attended_parts = moves.cores_exchange(attended_cols.reshape(shards, row_count, span))
    attended_parts = moves.members_exchange(attended_parts)
    first_states = near_open + [far_open]
    first_far = moves.far_open(first_states)
    last_states = [moves.spread_open(piece) for piece in far_pieces]
    attended_parts, first_far, last_states, other_cot = together(
        attended_parts, first_far, last_states, other_cot
    )
    home_cot = moves.home_join(cotangent, other_cot)
    last_far = moves.far_open(last_states)
    attended = jnp.concatenate([attended_parts[k] for k in range(shards)], axis=1)

    up_all = place(jnp.zeros((shards, chips, rows_piece, up_wide), bf16), up_own, moves.shard)
    out_all = place(jnp.zeros((shards, chips, rows_piece, out_wide), bf16), out_own, moves.shard)
    down_all = place(jnp.zeros((shards, chips, fold, rows_piece, width), bf16), down_own, moves.shard)
    pieces = near_pieces + [far_piece] + far_pieces
    parts_of = moves.far_parts(first_states, first_far) + moves.far_parts(last_states, last_far)
    for number, (piece, parts) in enumerate(zip(pieces, parts_of)):
        plane = moves.shard ^ (number + 1)
        for far, row, rows in [(0, 0, piece)] + parts:
            chip = moves.chip ^ far
            up_all = lax.dynamic_update_slice(
                up_all, rows[None, None, :, :up_wide], (plane, chip, row, 0)
            )
            out_all = lax.dynamic_update_slice(
                out_all, rows[None, None, :, up_wide : up_wide + out_wide], (plane, chip, row, 0)
            )
            start = up_wide + out_wide
            folds = [rows[:, start + k * width : start + (k + 1) * width] for k in range(fold)]
            down_all = lax.dynamic_update_slice(
                down_all, jnp.stack(folds)[None, None], (plane, chip, 0, row, 0)
            )
    up_half = up_all.reshape(width, up_wide)
    down_half = down_all.reshape(up_wide, width)
    out_first, out_second = moves.core_pair(out_all.reshape(width, out_wide))
    out_low = jnp.concatenate([out_first, out_second], axis=1)
    residual = inputs + dot(attended, out_low) + bias_out
    normed_two, inv_std_two = norm_parts(residual)
    act_two = (normed_two * gain_two + shift_two).astype(bf16)

    act_two_other, attended_other, cot_other = together(
        moves.core_swap(act_two), moves.core_swap(attended), moves.core_swap(home_cot)
    )
    cot_pair = jnp.concatenate([home_cot, cot_other], axis=0)
    act_two_pair = jnp.concatenate([act_two, act_two_other], axis=0)
    attended_pair = jnp.concatenate([attended, attended_other], axis=0)
    bias_up_half = core_half(bias_up)
    up_pair = dot(act_two_pair, up_half) + bias_up_half
    hidden_pair = gelu_value(up_pair).astype(bf16)
    slope_pair = gelu_slope(up_pair).astype(bf16)
    down_terms = dot_rows(hidden_pair, cot_pair).astype(bf16)
    down_terms = down_terms.reshape(shards, chips, down_piece, width)
    cot_pair, down_terms = together(cot_pair, down_terms)
    grad_y = home_cot.astype(f32)
    grad_bias_down = jnp.sum(grad_y, axis=0)
    grad_up_pair = (dot_right(cot_pair, down_half) * slope_pair.astype(f32)).astype(bf16)
    grad_bias_up = jnp.sum(grad_up_pair, axis=0, dtype=f32)
    back_other = moves.core_swap(dot_right(grad_up_pair[row_count:], up_half).astype(bf16))
    up_terms = dot_rows(act_two_pair, grad_up_pair).astype(bf16)
    up_terms = up_terms.reshape(shards, chips, rows_piece, up_wide)
    down_state = moves.reduce_open(down_terms, 1)
    back_other, hidden_pair, up_terms, down_state = together(
        back_other, hidden_pair, up_terms, down_state
    )
    up_state = moves.reduce_open(up_terms, 1)
    down_mid = moves.reduce_close(moves.reduce_add(down_state), 1)
    grad_act_two = dot_right(grad_up_pair[:row_count], up_half) + back_other.astype(f32)
    grad_gain_two = jnp.sum(grad_act_two * normed_two, axis=0)
    grad_shift_two = jnp.sum(grad_act_two, axis=0)
    grad_residual = grad_y + norm_back(grad_act_two, normed_two, inv_std_two, gain_two)
    grad_attn = grad_residual.astype(bf16)
    grad_bias_out = jnp.sum(grad_attn, axis=0, dtype=f32)
    to_members = jnp.stack(
        [
            dot_right(grad_attn, out_low[k * span : (k + 1) * span]).astype(bf16)
            for k in range(shards)
        ]
    )
    attn_halves = [grad_attn[:, :out_wide], grad_attn[:, out_wide:]]
    attn_own = jnp.where(core == 0, attn_halves[0], attn_halves[1])
    attn_other = jnp.where(core == 0, attn_halves[1], attn_halves[0])
    grad_heads, attn_other = together(moves.cores_exchange(to_members), moves.core_swap(attn_other))
    attn_pair = jnp.concatenate([attn_own, attn_other], axis=0)
    grad_heads, hidden_pair = together(grad_heads, hidden_pair)
    grad_heads = moves.members_exchange(grad_heads).reshape(group_rows, span)
    down_other = moves.core_swap(dot(hidden_pair[row_count:], down_half).astype(bf16))
    block_out = (
        residual + dot(hidden_pair[:row_count], down_half) + down_other.astype(f32) + bias_down
    ).astype(bf16)

    out_terms = dot_rows(attended_pair, attn_pair).astype(bf16)
    def shards_halve(piece, bits):
        piece = piece.reshape((piece.shape[0] // 2, 2) + piece.shape[1:])
        bit = moves.shard_bit(bits)
        return pick(piece, bit, 1), moves.shard_swap(pick(piece, 1 - bit, 1), bits)

    def halved(state):
        own, other = state
        return (own.astype(f32) + other.astype(f32)).astype(bf16)

    def shards_sum(piece):
        rows = piece.shape[1]
        return lax.psum_scatter(
            piece.reshape(shards * rows, piece.shape[2]), "shard", scatter_dimension=0, tiled=True
        )

    grad_heads, down_mid, out_terms, block_out = together(
        grad_heads, down_mid, out_terms, block_out
    )
    block_other = moves.home_send(block_out)
    down_owned = shards_sum(down_mid)
    out_state = moves.reduce_open(out_terms.reshape(shards, chips, rows_piece, out_wide), 1)
    attend_args = (plan, slopes)
    parts = 2 if heads % 4 == 0 else 1
    part_heads = heads // parts
    grad_qkv = attend_backward(
        qkv_rows, grad_heads, attended_cols, logs, *attend_args, part_heads, BLOCK, 0, None
    )
    grad_qkv, up_state, out_state = together(grad_qkv, up_state, out_state)
    up_sums, out_sums = moves.reduce_add(up_state), moves.reduce_add(out_state)
    grad_qkv, up_sums, out_sums = together(grad_qkv, up_sums, out_sums)
    up_out_state = [
        jnp.concatenate([up_part, out_part], axis=-1) for up_part, out_part in zip(up_sums, out_sums)
    ]
    if parts == 2:
        grad_qkv = attend_backward(
            qkv_rows, grad_heads, attended_cols, logs, *attend_args, part_heads, BLOCK, part_heads, grad_qkv
        )
    grad_qkv, up_out_state, block_other = together(
        grad_qkv, moves.reduce_send(up_out_state, 1), block_other
    )
    block_out = moves.home_join(block_out, block_other)
    up_out_piece = moves.reduce_final(up_out_state)
    up_out_state = shards_halve(up_out_piece, 1)

    grad_bias_q_part = jnp.sum(grad_qkv[:, :span], axis=0, dtype=f32)
    grad_bias_v_part = jnp.sum(grad_qkv[:, 2 * span :], axis=0, dtype=f32)

    grad_halves = grad_qkv.reshape(2, half * row_count, 3 * span)
    sent = dot_right(pick(grad_halves, 1 - core), qkv_cols).astype(bf16)
    sent = moves.core_swap(sent)
    qkv_terms = dot_rows(act_all, grad_qkv).astype(bf16)
    qkv_terms = qkv_terms.reshape(shards, chips, rows_piece, 3 * span)
    qkv_state = moves.reduce_open(qkv_terms, 1)
    back = dot_right(pick(grad_halves, core), qkv_cols) + sent.astype(f32)
    qkv_state, back, up_out_state = together(qkv_state, back, up_out_state)

    back = back.reshape(half, row_count, width)
    low_bits = list(reversed(moves.low_bits()))
    for bits in low_bits[:-1]:
        back = moves.reduce_bit(
            back, moves.shard_bit(bits), functools.partial(moves.shard_swap, bits=bits)
        )
    back = back.reshape((2, -1) + back.shape[1:])
    back_bit = moves.shard_bit(low_bits[-1])
    back_other = moves.shard_swap(pick(back, 1 - back_bit).astype(bf16), low_bits[-1])
    up_out_piece, bits = halved(up_out_state), 2
    while bits < half:
        up_out_piece = halved(shards_halve(up_out_piece, bits))
        bits *= 2
    up_out_state = shards_halve(up_out_piece, half)
    qkv_state = moves.reduce_send(moves.reduce_add(qkv_state), 1)
    qkv_state, up_out_state = together(qkv_state, up_out_state)

    up_out_owned = halved(up_out_state)[0]
    up_out_state = moves.spread_open(up_out_owned)
    qkv_piece = moves.reduce_final(qkv_state)
    qkv_piece = qkv_piece.reshape((2, half) + qkv_piece.shape[1:])
    qkv_own = pick(qkv_piece, moves.side)
    qkv_other = moves.shard_swap(pick(qkv_piece, 1 - moves.side), half)
    back_other, qkv_other, up_out_state = together(back_other, qkv_other, up_out_state)

    qkv_piece = moves.half_exchange(halved((qkv_own, qkv_other)))
    down_state = moves.spread_open(down_owned)
    grad_act_one = pick(back, back_bit) + back_other.astype(f32)
    grad_act_one = grad_act_one.reshape(row_count, width)
    grad_gain_one = jnp.sum(grad_act_one * normed_one, axis=0)
    grad_shift_one = jnp.sum(grad_act_one, axis=0)
    grad_inputs = grad_residual + norm_back(grad_act_one, normed_one, inv_std_one, gain_one)
    grad_inputs, qkv_piece, down_state = together(grad_inputs.astype(bf16), qkv_piece, down_state)
    tokens_other = moves.home_send(grad_inputs)
    qkv_owned = moves.chips_gather(qkv_piece, 1)

    up_out_first, up_out_second = moves.core_pair(
        moves.chips_gather(up_out_owned, 0, tuple(up_out_state)).reshape(rows_z, up_wide + out_wide)
    )
    out_grad = jnp.concatenate([up_out_first[:, up_wide:], up_out_second[:, up_wide:]], axis=1)
    up_columns = []
    for number in range(shards):
        part = slice(number * half_cols, (number + 1) * half_cols)
        up_columns += [up_out_first[:, part], up_out_second[:, part]]
    up_grad = jnp.concatenate(up_columns, axis=1)
    down_first, down_second = moves.core_pair(
        moves.chips_gather(down_owned, 0, tuple(down_state)).reshape(half_cols, width)
    )
    down_grad = jnp.concatenate([down_first, down_second], axis=0)
    qkv_first, qkv_second = moves.core_pair(qkv_owned.reshape(half, rows_z, 3 * span))
    qkv_columns = []
    for kind in range(3):
        for source in (qkv_first, qkv_second):
            for number in range(half):
                qkv_columns.append(source[number][:, kind * span : (kind + 1) * span])
    qkv_grad = jnp.concatenate(qkv_columns, axis=1)

    gradients = [qkv_grad, out_grad, up_grad, down_grad]
    heights = [width, width, width, hidden_width]
    rows_old = [row_state[k : k + 1] for k in range(3)] + [down_rows.reshape(1, -1)]
    stats = [
        factor_stats(gradient, old, decay_rate) for gradient, old in zip(gradients, rows_old)
    ]

    def to_sum(number):
        weight_sum = jnp.broadcast_to(weight_sums[number], (1, 128))
        return [stats[number][2], jnp.concatenate([stats[number][3], weight_sum], axis=0)]

    def spread_heads(part):
        return [jnp.where(member == number, part, 0.0) for number in range(shards)]

    bias_up_parts = []
    for number in range(shards):
        part = grad_bias_up[number * half_cols : (number + 1) * half_cols]
        bias_up_parts += [jnp.where(core == 0, part, 0.0), jnp.where(core == 1, part, 0.0)]
    vector_part = moves.sum_reps(
        jnp.concatenate(
            [grad_gain_one, grad_shift_one]
            + spread_heads(grad_bias_q_part)
            + spread_heads(grad_bias_v_part)
            + [grad_bias_out, grad_gain_two, grad_shift_two]
            + bias_up_parts
            + [grad_bias_down]
        )
    )
    vector_rows, tokens_other = together(vector_part.reshape(2, -1), tokens_other)
    tokens_grad = moves.home_join(grad_inputs, tokens_other)
    all_sums = summed(moves, to_sum(0) + to_sum(1) + to_sum(2) + to_sum(3) + [vector_rows])
    sums = [all_sums[0:2], all_sums[2:4], all_sums[4:6], all_sums[6:8]]
    vector_grad = all_sums[8].reshape(-1)
    updates = []
    offset = 0
    for number in range(4):
        end_col = offset + gradients[number].shape[1]
        updates.append(
            factor_apply(
                gradients[number],
                weights[number],
                stats[number][0],
                sums[number][0],
                sums[number][1],
                col_state[offset:end_col].reshape(1, -1),
                heights[number],
                decay_rate,
            )
        )
        offset = end_col
    grads_out, new_weights, copies, new_cols, rms_rows = zip(*updates)
    rms_values = [rms[0, 0] for rms in rms_rows]

    vector_state_new = decay_rate * vector_state + (1.0 - decay_rate) * (
        vector_grad * vector_grad + eps_second
    )
    vector_step = vector_grad * lax.rsqrt(vector_state_new)
    vector_rms = jnp.sqrt(jnp.mean(vector_step * vector_step))
    vector_new = vectors - rate_step * jnp.sqrt(
        jnp.mean(vectors * vectors)
    ) * vector_step / jnp.maximum(1.0, vector_rms / clip_level)
    update_rms = jnp.stack(rms_values + [vector_rms])
    return (
        block_out,
        tokens_grad,
        *grads_out,
        vector_grad,
        *new_weights,
        vector_new,
        *copies,
        jnp.concatenate([stats[0][1], stats[1][1], stats[2][1]], axis=0),
        stats[3][1].reshape(-1),
        jnp.concatenate(new_cols, axis=1).reshape(-1),
        vector_state_new,
        update_rms,
    )


def solution(mesh):
    in_specs = (
        P(("rep", "shard"), None),
        P(("rep", "shard"), None),
        P("rep", None),
        P("shard", None),
        P("shard", None),
        P("shard", None),
        P("shard", None),
        P(),
        P(None, "shard"),
        P("shard"),
        P(),
        P(),
    )
    out_specs = (
        P(("rep", "shard"), None),
        P(("rep", "shard"), None),
        P("shard", None),
        P("shard", None),
        P("shard", None),
        P("shard", None),
        P(),
        P("shard", None),
        P("shard", None),
        P("shard", None),
        P("shard", None),
        P(),
        P("shard", None),
        P("shard", None),
        P("shard", None),
        P("shard", None),
        P(None, "shard"),
        P("shard"),
        P(),
        P(),
        P(),
    )
    return jax.shard_map(
        on_device, mesh=mesh, in_specs=in_specs, out_specs=out_specs, check_vma=False
    )
```

```python
import functools

import jax
import jax.numpy as jnp
from jax import lax
from jax.experimental import pallas as pl
from jax.experimental.pallas import tpu as pltpu
from jax.sharding import PartitionSpec as P

HEADS = 16
STEP = 10
BLOCK = 256


eps_norm = 1e-05
eps_second = 1e-30
rate_step = 0.5
clip_level = 1.0
masked = -1e30
gelu_root = (2.0 / 3.141592653589793) ** 0.5
gelu_cubic = 0.044715

f32 = jnp.float32
bf16 = jnp.bfloat16


def norm_parts(values):
    average = jnp.mean(values, axis=-1, keepdims=True)
    centred = values - average
    inv_std = lax.rsqrt(jnp.mean(centred * centred, axis=-1, keepdims=True) + eps_norm)
    return (centred * inv_std, inv_std)


def norm_back(grad_out, normed, inv_std, gain_vec):
    grad_normed = grad_out * gain_vec
    inner_mean = jnp.mean(grad_normed * normed, axis=-1, keepdims=True)
    centred = grad_normed - jnp.mean(grad_normed, axis=-1, keepdims=True)
    return (centred - normed * inner_mean) * inv_std


def gelu_value(pre_act):
    curve = jnp.tanh(gelu_root * (pre_act + gelu_cubic * pre_act * pre_act * pre_act))
    return 0.5 * pre_act * (1.0 + curve)


def gelu_slope(pre_act):
    square = pre_act * pre_act
    curve = jnp.tanh(gelu_root * (pre_act + gelu_cubic * square * pre_act))
    inner = gelu_root * (1.0 + 3.0 * gelu_cubic * square)
    return 0.5 * (1.0 + curve) + 0.5 * pre_act * (1.0 - curve * curve) * inner


def dot(left_side, right_side):
    return jnp.dot(left_side, right_side, preferred_element_type=f32)


def dot_right(left_side, right_side):
    return lax.dot_general(
        left_side, right_side, (((1,), (1,)), ((), ())), preferred_element_type=f32
    )


def dot_rows(left_side, right_side):
    return lax.dot_general(
        left_side, right_side, (((0,), (0,)), ((), ())), preferred_element_type=f32
    )


def pick(stack, index, axis=0):
    return lax.dynamic_index_in_dim(stack, index, axis, keepdims=False, allow_negative_indices=False)


def cut_rows(values, start, count):
    return lax.dynamic_slice_in_dim(values, start, count, 0, allow_negative_indices=False)


def place(stack, part, index, axis=0):
    return lax.dynamic_update_index_in_dim(stack, part, index, axis, allow_negative_indices=False)


def head_rows(number, head_width):
    return slice(number * head_width, (number + 1) * head_width)


def lane_masks(block_rows, width, heads):
    lanes = lax.broadcasted_iota(jnp.int32, (block_rows, width), 1)
    head_width = width // heads
    return [
        (lanes >= number * head_width) & (lanes < (number + 1) * head_width)
        for number in range(heads)
    ]


def allowed_pairs(key_block, query_block, start_row, block):
    key_pos = lax.broadcasted_iota(jnp.int32, (block, block), 0) + key_block * block
    query_pos = lax.broadcasted_iota(jnp.int32, (block, block), 1) + query_block * block
    return (key_pos <= query_pos) & (key_pos >= start_row)


def key_offsets(key_block, query_block, block):
    rows = lax.broadcasted_iota(jnp.int32, (block, 1), 0)
    return (rows + (key_block - query_block) * block).astype(f32)


def turned(values):
    return jnp.transpose(values.astype(f32))


def head_stack(values, lanes):
    zero = jnp.zeros(values.shape, values.dtype)
    return jnp.concatenate([jnp.where(lane, values, zero) for lane in lanes], axis=0)


def eights(values, combine):
    rows, columns = values.shape
    return combine(values.reshape(rows // 8, 8, columns), axis=0)


def forward_kernel(
    heads,
    block,
    low_ref,
    mid_ref,
    slope_ref,
    start_ref,
    qkv_ref,
    out_ref,
    log_ref,
    values_turned,
    key_stack,
    score_ref,
):
    tokens = qkv_ref.shape[0]
    width = qkv_ref.shape[1] // 3
    head_width = width // heads
    blocks = tokens // block
    query_block = pl.program_id(0)

    @pl.when(query_block == 0)
    def _():
        lanes = lane_masks(block, width, heads)
        for number in range(blocks):
            rows = slice(number * block, (number + 1) * block)
            values_turned[number] = turned(qkv_ref[rows, 2 * width :]).astype(bf16)
            key_stack[number] = head_stack(qkv_ref[rows, width : 2 * width], lanes)

    first_row = pl.multiple_of(query_block * block, block)
    queries = qkv_ref[pl.ds(first_row, block), :width].astype(f32) * head_width ** (-0.5)
    queries = turned(queries).astype(bf16)
    start_row = start_ref[query_block]

    def score_step(key_block, bests, with_mask):
        scores = dot(key_stack[key_block], queries)
        offsets = key_offsets(key_block, query_block, block)
        allowed = allowed_pairs(key_block, query_block, start_row, block) if with_mask else None
        result = []
        for number in range(heads):
            rows = head_rows(number, block)
            part = scores[rows] + slope_ref[number] * offsets
            if with_mask:
                part = jnp.where(allowed, part, masked)
            score_ref[key_block, rows, :] = part
            result.append(jnp.maximum(bests[number], eights(part, jnp.max)))
        return tuple(result)

    low, mid = low_ref[query_block], mid_ref[query_block]
    bests = tuple(jnp.full((8, block), masked, f32) for _ in range(heads))
    bests = lax.fori_loop(low, mid, functools.partial(score_step, with_mask=True), bests)
    bests = lax.fori_loop(mid, query_block, functools.partial(score_step, with_mask=False), bests)
    bests = score_step(query_block, bests, True)
    bests = [jnp.max(best, axis=0, keepdims=True) for best in bests]

    def value_step(key_block, state):
        result = []
        for number in range(heads):
            total, gathered = state[2 * number : 2 * number + 2]
            weights = jnp.exp(score_ref[key_block, head_rows(number, block), :] - bests[number])
            value_rows = values_turned[key_block, head_rows(number, head_width), :]
            result += [
                total + eights(weights, jnp.sum),
                gathered + dot(value_rows, weights.astype(bf16)),
            ]
        return tuple(result)

    state = ()
    for number in range(heads):
        state += (jnp.zeros((8, block), f32), jnp.zeros((head_width, block), f32))
    state = lax.fori_loop(low, query_block + 1, value_step, state)
    columns = []
    for number in range(heads):
        total = jnp.sum(state[2 * number], axis=0, keepdims=True)
        columns.append(state[2 * number + 1] / total)
        log_ref[0, number : number + 1, :] = bests[number] + jnp.log(total)
    out_ref[...] = jnp.transpose(jnp.concatenate(columns, axis=0)).astype(bf16)


def backward_kernel(heads, block, first_head, merge, *refs):
    full_ref, high_ref, slope_ref, start_ref, log_ref, qkv_ref, grad_ref, out_ref = refs[:8]
    earlier_ref = refs[8] if merge else None
    result_ref = refs[9 if merge else 8]
    (
        queries_turned,
        grads_turned,
        keys_turned,
        query_stack,
        grad_stack,
        key_stack,
        value_stack,
        delta_rows,
        query_grads,
    ) = refs[10 if merge else 9 :]
    tokens, all_width = grad_ref.shape
    head_width = all_width // log_ref.shape[1]
    width = heads * head_width
    scale = head_width ** (-0.5)
    blocks = tokens // block
    key_block = pl.program_id(0)
    lanes = lane_masks(block, width, heads)

    def columns(kind):
        start = kind * all_width + first_head * head_width
        return slice(start, start + width)

    def target(kind):
        start = (kind * all_width + first_head * head_width) if merge else kind * width
        return slice(start, start + width)

    @pl.when(key_block == 0)
    def _():
        for number in range(blocks):
            rows = slice(number * block, (number + 1) * block)
            queries = qkv_ref[rows, columns(0)]
            queries_turned[number] = turned(queries.astype(f32) * scale).astype(bf16)
            query_stack[number] = head_stack(queries, lanes)
            keys_turned[number] = turned(qkv_ref[rows, columns(1)]).astype(bf16)
            grads = grad_ref[rows, columns(0)]
            grad_stack[number] = head_stack(grads, lanes)
            grads = grads.astype(f32)
            grads_turned[number] = turned(grads).astype(bf16)
            product = turned(grads * out_ref[rows, columns(0)].astype(f32))
            for head in range(heads):
                delta_rows[number, head : head + 1, :] = jnp.sum(
                    product[head_rows(head, head_width)], axis=0, keepdims=True
                )
            query_grads[number] = jnp.zeros((width, block), f32)

    key_row = pl.multiple_of(key_block * block, block)
    key_stack[...] = head_stack(qkv_ref[pl.ds(key_row, block), columns(1)], lanes)
    value_stack[...] = head_stack(qkv_ref[pl.ds(key_row, block), columns(2)], lanes)

    def step(query_block, state, with_mask):
        key_total, value_total = state
        scores = dot(key_stack[...], queries_turned[query_block])
        grad_weights = dot(value_stack[...], grads_turned[query_block])
        offsets = key_offsets(key_block, query_block, block)
        if with_mask:
            allowed = allowed_pairs(key_block, query_block, start_ref[query_block], block)
        weight_list, grad_list = [], []
        for number in range(heads):
            rows = head_rows(number, block)
            head = first_head + number
            part = scores[rows] + slope_ref[head] * offsets
            part = part - log_ref[query_block, head : head + 1, :]
            if with_mask:
                part = jnp.where(allowed, part, masked)
            probabilities = jnp.exp(part)
            delta = delta_rows[query_block, number : number + 1, :]
            grad_scores = (probabilities * (grad_weights[rows] - delta)).astype(bf16)
            weight_list.append(probabilities.astype(bf16))
            grad_list.append(grad_scores)
            rows = head_rows(number, head_width)
            query_grads[query_block, rows, :] += dot(keys_turned[key_block, rows, :], grad_scores)
        weight_row = jnp.concatenate(weight_list, axis=1)
        grad_row = jnp.concatenate(grad_list, axis=1)
        return (
            key_total + dot(grad_row, query_stack[query_block]),
            value_total + dot(weight_row, grad_stack[query_block]),
        )

    state = (jnp.zeros((block, width), f32), jnp.zeros((block, width), f32))
    state = step(key_block, state, True)
    full, high = full_ref[key_block], high_ref[key_block]
    state = lax.fori_loop(key_block + 1, full, functools.partial(step, with_mask=False), state)
    state = lax.fori_loop(full, high, functools.partial(step, with_mask=True), state)
    result_ref[pl.ds(key_row, block), target(1)] = (state[0] * scale).astype(bf16)
    result_ref[pl.ds(key_row, block), target(2)] = state[1].astype(bf16)
    if merge:
        other = first_head * head_width
        for kind in range(3):
            result_ref[pl.ds(key_row, block), kind * all_width : kind * all_width + other] = earlier_ref[
                pl.ds(key_row, block), kind * other : (kind + 1) * other
            ]

    @pl.when(key_block == blocks - 1)
    def _():
        for number in range(blocks):
            rows = slice(number * block, (number + 1) * block)
            result_ref[rows, target(0)] = jnp.transpose(query_grads[number] * scale).astype(bf16)


def block_plan(lengths, tokens, block):
    ends = jnp.cumsum(lengths)
    positions = jnp.arange(tokens, dtype=jnp.int32)
    passed = positions[:, None] >= ends[None, :]
    starts = jnp.max(jnp.where(passed, ends[None, :], 0), axis=1).astype(jnp.int32)
    finish = jnp.min(jnp.where(passed, tokens, ends[None, :]), axis=1).astype(jnp.int32)
    blocks = tokens // block
    number = jnp.arange(blocks, dtype=jnp.int32)
    first_start = starts[::block]
    last_start = starts[block - 1 :: block]
    low = first_start // block
    mid = jnp.clip((last_start + block - 1) // block, low, number)
    high = (finish[block - 1 :: block] - 1) // block + 1
    full = jnp.clip(finish[::block] // block, number + 1, high)
    return (starts.reshape(blocks, 1, block), low, mid, full, high)


def scalar_spec():
    return pl.BlockSpec(memory_space=pltpu.SMEM)


def whole_spec(shape):
    return pl.BlockSpec(shape, lambda step: (0,) * len(shape), pipeline_mode=pl.Buffered(1))


def attend_forward(qkv, plan, slopes, heads, block):
    tokens, triple = qkv.shape
    width = triple // 3
    blocks = tokens // block
    starts, low, mid, full, high = plan
    return pl.pallas_call(
        functools.partial(forward_kernel, heads, block),
        grid=(blocks,),
        in_specs=[
            scalar_spec(),
            scalar_spec(),
            scalar_spec(),
            whole_spec((blocks, 1, block)),
            whole_spec((tokens, triple)),
        ],
        out_specs=[
            pl.BlockSpec((block, width), lambda step: (step, 0)),
            pl.BlockSpec((1, heads, block), lambda step: (step, 0, 0)),
        ],
        out_shape=[
            jax.ShapeDtypeStruct((tokens, width), bf16),
            jax.ShapeDtypeStruct((blocks, heads, block), f32),
        ],
        scratch_shapes=[
            pltpu.VMEM((blocks, width, block), bf16),
            pltpu.VMEM((blocks, heads * block, width), bf16),
            pltpu.VMEM((blocks, heads * block, block), f32),
        ],
        compiler_params=pltpu.CompilerParams(
            dimension_semantics=("arbitrary",), vmem_limit_bytes=28 * 1024 * 1024
        ),
        cost_estimate=pl.CostEstimate(
            flops=3 * tokens * tokens * 256 * heads,
            bytes_accessed=10 * tokens * width,
            transcendentals=tokens * tokens * heads // 2,
        ),
        name="attend_forward",
    )(low, mid, slopes, starts, qkv)


def attend_backward(qkv, grads, outputs, logs, plan, slopes, heads, block, first_head, earlier):
    tokens, triple = qkv.shape
    all_width = triple // 3
    all_heads = logs.shape[1]
    width = all_width // all_heads * heads
    blocks = tokens // block
    starts, low, mid, full, high = plan
    merge = earlier is not None
    result_width = triple if merge else 3 * width
    operands = [full, high, slopes, starts, logs, qkv, grads, outputs]
    specs = [scalar_spec() for _ in range(3)] + [whole_spec(entry.shape) for entry in operands[3:]]
    if merge:
        operands.append(earlier)
        specs.append(whole_spec(earlier.shape))
    return pl.pallas_call(
        functools.partial(backward_kernel, heads, block, first_head, merge),
        grid=(blocks,),
        in_specs=specs,
        out_specs=pl.BlockSpec((tokens, result_width), lambda step: (0, 0)),
        out_shape=jax.ShapeDtypeStruct((tokens, result_width), bf16),
        scratch_shapes=[
            pltpu.VMEM((blocks, width, block), bf16),
            pltpu.VMEM((blocks, width, block), bf16),
            pltpu.VMEM((blocks, width, block), bf16),
            pltpu.VMEM((blocks, heads * block, width), bf16),
            pltpu.VMEM((blocks, heads * block, width), bf16),
            pltpu.VMEM((heads * block, width), bf16),
            pltpu.VMEM((heads * block, width), bf16),
            pltpu.VMEM((blocks, heads, block), f32),
            pltpu.VMEM((blocks, width, block), f32),
        ],
        compiler_params=pltpu.CompilerParams(
            dimension_semantics=("arbitrary",), vmem_limit_bytes=28 * 1024 * 1024
        ),
        cost_estimate=pl.CostEstimate(
            flops=8 * tokens * tokens * 256 * heads,
            bytes_accessed=20 * tokens * width,
            transcendentals=tokens * tokens * heads // 2,
        ),
        name="attend_backward",
    )(*operands)


def hidden_backward_kernel(own_ref, other_ref, weight_ref, slope_ref, result_ref, total_ref):
    rows = own_ref.shape[0]
    total = jnp.zeros(total_ref.shape, f32)
    for number, ref in enumerate((own_ref, other_ref)):
        part = slice(number * rows, (number + 1) * rows)
        grads = dot_right(ref[...], weight_ref[...]) * slope_ref[part, :].astype(f32)
        grads = grads.astype(bf16)
        result_ref[part, :] = grads
        total = total + jnp.sum(grads.astype(f32), axis=0, keepdims=True)
    total_ref[...] = total


def hidden_backward(weight, cot_own, cot_other, slopes):
    rows, width = cot_own.shape
    breadth = slopes.shape[1]
    tile = min(256, breadth)
    return pl.pallas_call(
        hidden_backward_kernel,
        grid=(breadth // tile,),
        in_specs=[
            whole_spec((rows, width)),
            whole_spec((rows, width)),
            pl.BlockSpec((tile, width), lambda step: (step, 0)),
            pl.BlockSpec((2 * rows, tile), lambda step: (0, step)),
        ],
        out_specs=[
            pl.BlockSpec((2 * rows, tile), lambda step: (0, step)),
            pl.BlockSpec((1, tile), lambda step: (0, step)),
        ],
        out_shape=[
            jax.ShapeDtypeStruct((2 * rows, breadth), bf16),
            jax.ShapeDtypeStruct((1, breadth), f32),
        ],
        compiler_params=pltpu.CompilerParams(
            dimension_semantics=("arbitrary",), vmem_limit_bytes=20 * 1024 * 1024
        ),
        cost_estimate=pl.CostEstimate(flops=1, bytes_accessed=1, transcendentals=0),
        name="hidden_backward",
    )(cot_own, cot_other, weight, slopes)


def up_backward_kernel(grads_ref, weight_ref, result_ref):
    result_ref[...] = dot_right(grads_ref[...], weight_ref[...]).astype(result_ref.dtype)


def up_backward(weight, grads, number, kind_of):
    rows, breadth = grads.shape[0] // 2, grads.shape[1]
    width = weight.shape[0]
    tile = width // 4
    return pl.pallas_call(
        up_backward_kernel,
        grid=(4,),
        in_specs=[
            pl.BlockSpec((rows, breadth), lambda step: (number, 0)),
            pl.BlockSpec((tile, breadth), lambda step: (step, 0)),
        ],
        out_specs=pl.BlockSpec((rows, tile), lambda step: (0, step)),
        out_shape=jax.ShapeDtypeStruct((rows, width), kind_of),
        compiler_params=pltpu.CompilerParams(
            dimension_semantics=("arbitrary",), vmem_limit_bytes=28 * 1024 * 1024
        ),
        cost_estimate=pl.CostEstimate(flops=1, bytes_accessed=1, transcendentals=0),
        name="up_backward",
    )(grads, weight)


def down_projection_kernel(hidden_ref, weight_ref, result_ref):
    result_ref[...] = dot(hidden_ref[...], weight_ref[...]).astype(result_ref.dtype)


def down_projection(hidden, weight):
    rows, breadth = hidden.shape
    width = weight.shape[1]
    tile = min(256, rows)
    return pl.pallas_call(
        down_projection_kernel,
        grid=(rows // tile,),
        in_specs=[
            pl.BlockSpec((tile, breadth), lambda step: (step, 0)),
            whole_spec((breadth, width)),
        ],
        out_specs=pl.BlockSpec((tile, width), lambda step: (step, 0)),
        out_shape=jax.ShapeDtypeStruct((rows, width), bf16),
        compiler_params=pltpu.CompilerParams(
            dimension_semantics=("arbitrary",), vmem_limit_bytes=20 * 1024 * 1024
        ),
        cost_estimate=pl.CostEstimate(flops=1, bytes_accessed=1, transcendentals=0),
        name="down_projection",
    )(hidden, weight)


def up_gradient_kernel(own_ref, other_ref, grads_ref, result_ref, act_turned):
    rows, width = own_ref.shape
    step = 256

    @pl.when(pl.program_id(0) == 0)
    def _():
        for number, ref in enumerate((own_ref, other_ref)):
            for row in range(0, rows, step):
                first = number * rows + row
                for column in range(0, width, step):
                    block = ref[row : row + step, column : column + step]
                    act_turned[column : column + step, first : first + step] = turned(block).astype(bf16)

    result_ref[...] = dot(act_turned[...], grads_ref[...]).astype(bf16)


def up_gradient(act_own, act_other, grads):
    rows, width = act_own.shape
    breadth = grads.shape[1]
    tile = min(512, breadth)
    return pl.pallas_call(
        up_gradient_kernel,
        grid=(breadth // tile,),
        in_specs=[
            whole_spec((rows, width)),
            whole_spec((rows, width)),
            pl.BlockSpec((2 * rows, tile), lambda step: (0, step)),
        ],
        out_specs=pl.BlockSpec((width, tile), lambda step: (0, step)),
        out_shape=jax.ShapeDtypeStruct((width, breadth), bf16),
        scratch_shapes=[pltpu.VMEM((width, 2 * rows), bf16)],
        compiler_params=pltpu.CompilerParams(
            dimension_semantics=("arbitrary",), vmem_limit_bytes=28 * 1024 * 1024
        ),
        cost_estimate=pl.CostEstimate(flops=1, bytes_accessed=1, transcendentals=0),
        name="up_gradient",
    )(act_own, act_other, grads)


def together(*values):
    return lax.optimization_barrier(tuple(values))


def ordered(own, other, bit, axis=0):
    first = jnp.where(bit == 0, own, other)
    second = jnp.where(bit == 0, other, own)
    return jnp.stack([first, second], axis=axis)


class Moves:
    def __init__(self):
        self.shards = lax.axis_size("shard")
        self.reps = lax.axis_size("rep")
        self.half = self.shards // 2
        self.chips = self.reps // 2
        self.shard = lax.axis_index("shard")
        self.rep = lax.axis_index("rep")
        self.core = self.rep & 1
        self.chip = self.rep >> 1
        self.side = lax.div(self.shard, self.half)
        self.member = lax.rem(self.shard, self.half) + self.core * self.half

    def core_swap(self, part):
        return lax.ppermute(part, "rep", [(r, r ^ 1) for r in range(self.reps)])

    def chip_swap(self, part, bits):
        return lax.ppermute(part, "rep", [(r, r ^ (2 * bits)) for r in range(self.reps)])

    def shard_swap(self, part, bits):
        return lax.ppermute(part, "shard", [(s, s ^ bits) for s in range(self.shards)])

    def shard_bit(self, bits):
        return lax.div(self.shard, bits) & 1

    def low_bits(self):
        bits, result = 1, []
        while bits < self.half:
            result.append(bits)
            bits *= 2
        return result

    def home_send(self, part):
        pairs = []
        for rep in range(self.reps):
            for shard in range(self.shards):
                if shard // self.half != rep % 2:
                    to_shard = (shard + self.half) % self.shards
                    pairs.append((rep * self.shards + shard, (rep ^ 1) * self.shards + to_shard))
        return lax.ppermute(part, ("rep", "shard"), pairs)

    def home_join(self, part, other):
        return jnp.where(self.side == self.core, part, other)

    def half_gather(self, part):
        stack = part[None]
        for bits in self.low_bits():
            own = stack
            stack = ordered(own, self.shard_swap(own, bits), self.shard_bit(bits))
            stack = stack.reshape((-1,) + part.shape)
        return stack

    def cores_gather(self, stack):
        stack = ordered(stack, self.core_swap(stack), self.core)
        return stack.reshape((-1,) + stack.shape[2:])

    def exchange_bit(self, stack, bit, swap):
        sources, targets = stack.shape[:2]
        stack = stack.reshape((sources, 2, targets // 2) + stack.shape[2:])
        own, other = pick(stack, bit, 1), swap(pick(stack, 1 - bit, 1))
        return ordered(own, other, bit, 1).reshape((2 * sources,) + own.shape[1:])

    def half_exchange(self, stack):
        stack = stack[None]
        for bits in reversed(self.low_bits()):
            swap = functools.partial(self.shard_swap, bits=bits)
            stack = self.exchange_bit(stack, self.shard_bit(bits), swap)
        return stack.reshape((self.half,) + stack.shape[2:])

    def cores_exchange(self, stack):
        return self.exchange_bit(stack[None], self.core, self.core_swap)

    def members_exchange(self, stack):
        for bits in reversed(self.low_bits()):
            swap = functools.partial(self.shard_swap, bits=bits)
            stack = self.exchange_bit(stack, self.shard_bit(bits), swap)
        return stack.reshape((self.shards,) + stack.shape[2:])

    def reduce_bit(self, stack, bit, swap):
        stack = stack.reshape((2, stack.shape[0] // 2) + stack.shape[1:])
        other = swap(pick(stack, 1 - bit).astype(bf16))
        return pick(stack, bit).astype(f32) + other.astype(f32)

    def spread_open(self, part):
        if self.chips == 4:
            return (self.chip_swap(part, 1), self.chip_swap(part, 2))
        held, bits = [part], 1
        while bits < self.chips:
            held = held + [self.chip_swap(piece, bits) for piece in held]
            bits *= 2
        return tuple(held[1:])

    def spread_close(self, state):
        if self.chips == 4:
            by_x, by_y = state
            cut, axis = by_x.shape[-2] // 2, by_x.ndim - 2
            far = [
                self.chip_swap(by_x[..., :cut, :], 2),
                self.chip_swap(by_y[..., cut:, :], 1),
            ]
            return (by_x, by_y, jnp.concatenate(far, axis=axis))
        return state

    def far_open(self, states):
        if self.chips != 4:
            return ()
        cut = states[0][0].shape[0] // 2
        return (
            self.chip_swap(jnp.concatenate([by_x[:cut] for by_x, _ in states], axis=0), 2),
            self.chip_swap(jnp.concatenate([by_y[cut:] for _, by_y in states], axis=0), 1),
        )

    def far_parts(self, states, far):
        if self.chips != 4:
            return [[(k + 1, 0, part) for k, part in enumerate(state)] for state in states]
        cut = states[0][0].shape[0] // 2
        result = []
        for number, (by_x, by_y) in enumerate(states):
            rows = slice(number * cut, (number + 1) * cut)
            result.append([(1, 0, by_x), (2, 0, by_y), (3, 0, far[0][rows]), (3, cut, far[1][rows])])
        return result

    def chips_gather(self, part, axis, state=None):
        shape = part.shape[:axis] + (self.chips,) + part.shape[axis:]
        stack = place(jnp.zeros(shape, part.dtype), part, self.chip, axis)
        others = self.spread_close(self.spread_open(part) if state is None else state)
        for number, piece in enumerate(others):
            stack = place(stack, piece, self.chip ^ (number + 1), axis)
        return stack

    def reduce_open(self, stack, axis):
        return self.reduce_start(self.reduce_cut(stack, axis), axis)

    def reduce_cut(self, stack, axis):
        if self.chips != 4:
            return (stack,)
        shape = stack.shape[:axis] + (2, 2) + stack.shape[axis + 1 :]
        stack = stack.reshape(shape)
        bit_x, bit_y = self.chip & 1, self.chip >> 1
        cut = shape[0] // 2
        first, second = stack[:cut], stack[cut:]
        return (
            pick(first, bit_x, axis + 1),
            pick(second, bit_y, axis),
            pick(first, 1 - bit_x, axis + 1),
            pick(second, 1 - bit_y, axis),
        )

    def reduce_start(self, parts, axis):
        if self.chips == 4:
            first, second, send_first, send_second = parts
            return (first, second, self.chip_swap(send_first, 1), self.chip_swap(send_second, 2))
        (stack,) = parts
        count = self.chips
        stack = stack.astype(f32)
        while count > 1:
            count //= 2
            shape = stack.shape[:axis] + (2, count) + stack.shape[axis + 1 :]
            stack = stack.reshape(shape)
            bit = lax.div(self.chip, count) & 1
            got = self.chip_swap(pick(stack, 1 - bit, axis).astype(bf16), count)
            stack = pick(stack, bit, axis) + got.astype(f32)
        return (pick(stack, 0, axis).astype(bf16),)

    def reduce_add(self, state):
        if self.chips != 4:
            return state
        first, second, got_first, got_second = state
        first = (first.astype(f32) + got_first.astype(f32)).astype(bf16)
        second = (second.astype(f32) + got_second.astype(f32)).astype(bf16)
        return (first, second)

    def reduce_send(self, state, axis):
        if self.chips != 4:
            return state
        first, second = state
        bit_x, bit_y = self.chip & 1, self.chip >> 1
        got_first = self.chip_swap(pick(first, 1 - bit_y, axis), 2)
        got_second = self.chip_swap(pick(second, 1 - bit_x, axis), 1)
        return (pick(first, bit_y, axis), pick(second, bit_x, axis), got_first, got_second)

    def reduce_final(self, state):
        if self.chips != 4:
            return state[0]
        first, second, got_first, got_second = state
        first = first.astype(f32) + got_first.astype(f32)
        second = second.astype(f32) + got_second.astype(f32)
        return jnp.concatenate([first, second], axis=0).astype(bf16)

    def reduce_close(self, state, axis):
        return self.reduce_final(self.reduce_send(state, axis))

    def core_pair(self, part):
        other = self.core_swap(part)
        first = jnp.where(self.core == 0, part, other)
        second = jnp.where(self.core == 0, other, part)
        return first, second

    def sum_reps(self, vector):
        bits = 1
        while bits < self.reps:
            vector = vector + lax.ppermute(vector, "rep", [(r, r ^ bits) for r in range(self.reps)])
            bits *= 2
        return vector

    def sum_shards(self, vector):
        bits = 1
        while bits < self.shards:
            vector = vector + self.shard_swap(vector, bits)
            bits *= 2
        return vector


def stats_kernel(decay_rate, gradient_ref, old_ref, rows_ref, lane_rows_ref, sums_ref, total_ref, partial):
    step = pl.program_id(0)
    rows, columns = gradient_ref.shape

    @pl.when(step == 0)
    def _():
        partial[...] = jnp.zeros_like(partial)
        total_ref[...] = jnp.zeros_like(total_ref)

    gradient = gradient_ref[...].astype(f32)
    square = gradient * gradient
    row_mean = jnp.sum(square, axis=1, keepdims=True) / columns
    old = jnp.transpose(jnp.broadcast_to(old_ref[...], (128, rows)))[:, 0:1]
    rows_new = decay_rate * old + (1.0 - decay_rate) * (row_mean + eps_second)
    rows_ref[...] = rows_new
    lane_rows_ref[...] = jnp.transpose(jnp.broadcast_to(rows_new, (rows, 128)))[0:1, :]
    total_ref[...] += jnp.broadcast_to(jnp.sum(rows_new, axis=0, keepdims=True), (1, 128))
    partial[0:8, :] += eights(square, jnp.sum)
    partial[8:16, :] += eights(square * (1.0 / rows_new), jnp.sum)

    @pl.when(step == pl.num_programs(0) - 1)
    def _():
        sums_ref[0:1, :] = jnp.sum(partial[0:8, :], axis=0, keepdims=True)
        sums_ref[1:2, :] = jnp.sum(partial[8:16, :], axis=0, keepdims=True)


def factor_stats(gradient, rows_old, decay_rate):
    height, breadth = gradient.shape
    rows = min(128, height)
    return pl.pallas_call(
        functools.partial(stats_kernel, decay_rate),
        grid=(height // rows,),
        in_specs=[
            pl.BlockSpec((rows, breadth), lambda step: (step, 0)),
            pl.BlockSpec((1, rows), lambda step: (0, step)),
        ],
        out_specs=[
            pl.BlockSpec((rows, 1), lambda step: (step, 0)),
            pl.BlockSpec((1, rows), lambda step: (0, step)),
            pl.BlockSpec((2, breadth), lambda step: (0, 0)),
            pl.BlockSpec((1, 128), lambda step: (0, 0)),
        ],
        out_shape=[
            jax.ShapeDtypeStruct((height, 1), f32),
            jax.ShapeDtypeStruct((1, height), f32),
            jax.ShapeDtypeStruct((2, breadth), f32),
            jax.ShapeDtypeStruct((1, 128), f32),
        ],
        scratch_shapes=[pltpu.VMEM((16, breadth), f32)],
        compiler_params=pltpu.CompilerParams(
            dimension_semantics=("arbitrary",), vmem_limit_bytes=16 * 1024 * 1024
        ),
        name="factor_stats",
    )(gradient, rows_old)


def apply_kernel(
    decay_rate,
    height,
    gradient_ref,
    weight_ref,
    rows_ref,
    sums_ref,
    scalar_ref,
    old_ref,
    gradient_out,
    weight_out,
    copy_out,
    cols_out,
    rms_out,
    col_factor,
):
    columns = gradient_ref.shape[1]

    @pl.when(pl.program_id(0) == 0)
    def _():
        cols_new = decay_rate * old_ref[...] + (1.0 - decay_rate) * (
            sums_ref[0:1, :] / height + eps_second
        )
        row_mean = scalar_ref[0:1, 0:1] / height
        weight_mean = scalar_ref[1:2, 0:1] / (height * columns)
        scaled = jnp.sum(sums_ref[1:2, :] / cols_new, axis=1, keepdims=True)
        rms_update = jnp.sqrt(row_mean / (height * columns) * scaled)
        factor = rate_step * jnp.sqrt(weight_mean) * jnp.sqrt(row_mean)
        factor = factor / jnp.maximum(1.0, rms_update / clip_level)
        col_factor[...] = factor * lax.rsqrt(cols_new)
        cols_out[...] = cols_new
        rms_out[...] = jnp.broadcast_to(rms_update, (1, 128))

    gradient = gradient_ref[...].astype(f32)
    new_weight = weight_ref[...] - gradient * lax.rsqrt(rows_ref[...]) * col_factor[...]
    gradient_out[...] = gradient
    weight_out[...] = new_weight
    copy_out[...] = new_weight.astype(bf16)


def factor_apply(gradient, weight, rows_new, sums, scalars, cols_old, height, decay_rate):
    own_height, breadth = gradient.shape
    rows = min(64, own_height)

    def rows_spec():
        return pl.BlockSpec((rows, breadth), lambda step: (step, 0))

    def row_spec(count, wide):
        return pl.BlockSpec((count, wide), lambda step: (0, 0))

    return pl.pallas_call(
        functools.partial(apply_kernel, decay_rate, height),
        grid=(own_height // rows,),
        in_specs=[
            rows_spec(),
            rows_spec(),
            pl.BlockSpec((rows, 1), lambda step: (step, 0)),
            row_spec(2, breadth),
            row_spec(2, 128),
            row_spec(1, breadth),
        ],
        out_specs=[rows_spec(), rows_spec(), rows_spec(), row_spec(1, breadth), row_spec(1, 128)],
        out_shape=[
            jax.ShapeDtypeStruct((own_height, breadth), f32),
            jax.ShapeDtypeStruct((own_height, breadth), f32),
            jax.ShapeDtypeStruct((own_height, breadth), bf16),
            jax.ShapeDtypeStruct((1, breadth), f32),
            jax.ShapeDtypeStruct((1, 128), f32),
        ],
        scratch_shapes=[pltpu.VMEM((1, breadth), f32)],
        compiler_params=pltpu.CompilerParams(
            dimension_semantics=("arbitrary",), vmem_limit_bytes=16 * 1024 * 1024
        ),
        name="factor_apply",
    )(gradient, weight, rows_new, sums, scalars, cols_old)


def summed(moves, entries):
    total = moves.sum_shards(jnp.concatenate(entries, axis=1))
    result, offset = [], 0
    for entry in entries:
        result.append(total[:, offset : offset + entry.shape[1]])
        offset += entry.shape[1]
    return result


def on_device(
    tokens,
    cotangent,
    seq_lengths,
    qkv_weight,
    out_weight,
    up_weight,
    down_weight,
    vectors,
    row_state,
    down_rows,
    col_state,
    vector_state,
):
    moves = Moves()
    shards, half, chips, core = moves.shards, moves.half, moves.chips, moves.core
    row_count, width = tokens.shape
    hidden_width = up_weight.shape[1]
    group_rows = row_count * shards
    heads = HEADS // shards
    head_width = width // HEADS
    span = heads * head_width
    member = moves.member
    decay_rate = 1.0 - STEP ** (-0.8)
    head_number = (member * heads + jnp.arange(heads, dtype=jnp.int32)).astype(f32)
    slopes = jnp.exp2(-8.0 * (head_number + 1.0) / HEADS)

    gain_one = vectors[0:width]
    shift_one = vectors[width : 2 * width]
    bias_query = vectors[2 * width : 3 * width]
    bias_value = vectors[3 * width : 4 * width]
    bias_out = vectors[4 * width : 5 * width]
    gain_two = vectors[5 * width : 6 * width]
    shift_two = vectors[6 * width : 7 * width]
    bias_up = vectors[7 * width : 7 * width + hidden_width]
    bias_down = vectors[7 * width + hidden_width :]

    other_tokens = moves.home_send(tokens)
    other_lengths = moves.core_swap(seq_lengths)
    lengths = jnp.where(moves.side == core, seq_lengths, other_lengths)[0]
    plan = block_plan(lengths, group_rows, BLOCK)
    rows_z = width // shards
    rows_piece = rows_z // chips
    my_rows = cut_rows(qkv_weight, moves.chip * rows_piece, rows_piece)
    my_rows = my_rows.astype(bf16)
    my_blocks = []
    for number in range(half):
        kinds = []
        for kind in range(3):
            first = kind * width + number * span
            second = first + half * span
            kinds.append(
                jnp.where(
                    core == 0, my_rows[:, first : first + span], my_rows[:, second : second + span]
                )
            )
        my_blocks.append(jnp.concatenate(kinds, axis=1))
    qkv_part = moves.half_exchange(jnp.stack(my_blocks))
    half_cols = hidden_width // (2 * shards)
    up_wide = shards * half_cols
    out_wide = width // 2
    down_piece = half_cols // chips

    def core_half(values):
        parts = []
        for number in range(shards):
            start = 2 * number * half_cols
            first = values[..., start : start + half_cols]
            second = values[..., start + half_cols : start + 2 * half_cols]
            parts.append(jnp.where(core == 0, first, second))
        return jnp.concatenate(parts, axis=-1)

    up_own = core_half(up_weight).astype(bf16).reshape(chips, rows_piece, up_wide)
    out_own = jnp.where(core == 0, out_weight[:, :out_wide], out_weight[:, out_wide:]).astype(bf16)
    out_own = out_own.reshape(chips, rows_piece, out_wide)
    down_own = cut_rows(down_weight, core * half_cols, half_cols).astype(bf16)
    fold = down_piece // rows_piece
    down_own = down_own.reshape(chips, fold, rows_piece, width)
    my_down = pick(down_own, moves.chip)
    weight_piece = jnp.concatenate(
        [pick(up_own, moves.chip), pick(out_own, moves.chip)] + [my_down[k] for k in range(fold)],
        axis=1,
    )
    near_pieces, bits = [weight_piece], 1
    while bits < half:
        near_pieces = near_pieces + [moves.shard_swap(piece, bits) for piece in near_pieces]
        bits *= 2
    near_pieces = near_pieces[1:]
    weights = [qkv_weight, out_weight, up_weight, down_weight]
    weight_sums = [jnp.sum(weight * weight) for weight in weights]
    other_tokens, qkv_part, near_pieces, weight_piece, plan, weight_sums = together(
        other_tokens, qkv_part, near_pieces, weight_piece, plan, weight_sums
    )
    home_tokens = moves.home_join(tokens, other_tokens)
    far_piece = moves.shard_swap(weight_piece, half)
    near_open = [moves.spread_open(piece) for piece in near_pieces]
    qkv_far = moves.shard_swap(qkv_part, half)
    qkv_far, near_open = together(qkv_far, near_open)
    qkv_part = ordered(qkv_part, qkv_far, moves.side).reshape(shards, rows_piece, 3 * span)
    qkv_cols = moves.chips_gather(qkv_part, 1).reshape(width, 3 * span)
    inputs = home_tokens.astype(f32)
    normed_one, inv_std_one = norm_parts(inputs)
    act_one = (normed_one * gain_one + shift_one).astype(bf16)
    act_half = moves.half_gather(act_one)

    act_half, qkv_cols, far_piece, cotangent = together(
        act_half, qkv_cols, far_piece, cotangent
    )
    other_cot = moves.home_send(cotangent)
    act_all = moves.cores_gather(act_half).reshape(group_rows, width)
    far_open = moves.spread_open(far_piece)
    far_pieces, bits = [far_piece], 1
    while bits < half:
        far_pieces = far_pieces + [moves.shard_swap(piece, bits) for piece in far_pieces]
        bits *= 2
    far_pieces = far_pieces[1:]

    bias_q_part = cut_rows(bias_query, member * span, span)
    bias_v_part = cut_rows(bias_value, member * span, span)
    qkv_bias = jnp.concatenate([bias_q_part, jnp.zeros_like(bias_q_part), bias_v_part])
    qkv_rows = (dot(act_all, qkv_cols) + qkv_bias).astype(bf16)
    attended_cols, logs = attend_forward(qkv_rows, plan, slopes, heads, BLOCK)
    attended_cols, far_open, far_pieces, other_cot = together(
        attended_cols, far_open, far_pieces, other_cot
    )
    attended_parts = moves.cores_exchange(attended_cols.reshape(shards, row_count, span))
    attended_parts = moves.members_exchange(attended_parts)
    first_states = near_open + [far_open]
    first_far = moves.far_open(first_states)
    last_states = [moves.spread_open(piece) for piece in far_pieces]
    attended_parts, first_far, last_states, other_cot = together(
        attended_parts, first_far, last_states, other_cot
    )
    home_cot = moves.home_join(cotangent, other_cot)
    last_far = moves.far_open(last_states)
    attended = jnp.concatenate([attended_parts[k] for k in range(shards)], axis=1)

    up_all = place(jnp.zeros((shards, chips, rows_piece, up_wide), bf16), up_own, moves.shard)
    out_all = place(jnp.zeros((shards, chips, rows_piece, out_wide), bf16), out_own, moves.shard)
    down_all = place(jnp.zeros((shards, chips, fold, rows_piece, width), bf16), down_own, moves.shard)
    pieces = near_pieces + [far_piece] + far_pieces
    parts_of = moves.far_parts(first_states, first_far) + moves.far_parts(last_states, last_far)
    for number, (piece, parts) in enumerate(zip(pieces, parts_of)):
        plane = moves.shard ^ (number + 1)
        for far, row, rows in [(0, 0, piece)] + parts:
            chip = moves.chip ^ far
            up_all = lax.dynamic_update_slice(
                up_all, rows[None, None, :, :up_wide], (plane, chip, row, 0), allow_negative_indices=False
            )
            out_all = lax.dynamic_update_slice(
                out_all, rows[None, None, :, up_wide : up_wide + out_wide], (plane, chip, row, 0), allow_negative_indices=False
            )
            start = up_wide + out_wide
            folds = [rows[:, start + k * width : start + (k + 1) * width] for k in range(fold)]
            down_all = lax.dynamic_update_slice(
                down_all, jnp.stack(folds)[None, None], (plane, chip, 0, row, 0), allow_negative_indices=False
            )
    up_half = up_all.reshape(width, up_wide)
    down_half = down_all.reshape(up_wide, width)
    out_first, out_second = moves.core_pair(out_all.reshape(width, out_wide))
    out_low = jnp.concatenate([out_first, out_second], axis=1)
    residual = inputs + dot(attended, out_low) + bias_out
    normed_two, inv_std_two = norm_parts(residual)
    act_two = (normed_two * gain_two + shift_two).astype(bf16)

    act_two_other, attended_other, cot_other = together(
        moves.core_swap(act_two), moves.core_swap(attended), moves.core_swap(home_cot)
    )
    cot_pair = jnp.concatenate([home_cot, cot_other], axis=0)
    act_two_pair = jnp.concatenate([act_two, act_two_other], axis=0)
    attended_pair = jnp.concatenate([attended, attended_other], axis=0)
    bias_up_half = core_half(bias_up)
    up_pair = dot(act_two_pair, up_half) + bias_up_half
    hidden_pair = gelu_value(up_pair).astype(bf16)
    slope_pair = gelu_slope(up_pair).astype(bf16)
    down_terms = dot_rows(hidden_pair, cot_pair).astype(bf16)
    down_state = moves.reduce_cut(down_terms.reshape(shards, chips, down_piece, width), 1)
    slope_pair, down_state = together(slope_pair, down_state)
    down_state = moves.reduce_start(down_state, 1)
    grad_y = home_cot.astype(f32)
    grad_bias_down = jnp.sum(grad_y, axis=0)
    grad_up_pair, grad_bias_up = hidden_backward(down_half, home_cot, cot_other, slope_pair)
    grad_bias_up = grad_bias_up.reshape(-1)
    back_other = moves.core_swap(up_backward(up_half, grad_up_pair, 1, bf16))
    up_terms = up_gradient(act_two, act_two_other, grad_up_pair)
    down_pair = down_projection(hidden_pair, down_half)
    back_other, down_pair, up_terms, down_state = together(
        back_other, down_pair, up_terms, down_state
    )
    up_cut = moves.reduce_cut(up_terms.reshape(shards, chips, rows_piece, up_wide), 1)
    down_sums = moves.reduce_add(down_state)
    grad_act_two = up_backward(up_half, grad_up_pair, 0, f32) + back_other.astype(f32)
    grad_gain_two = jnp.sum(grad_act_two * normed_two, axis=0)
    grad_shift_two = jnp.sum(grad_act_two, axis=0)
    grad_residual = grad_y + norm_back(grad_act_two, normed_two, inv_std_two, gain_two)
    grad_attn = grad_residual.astype(bf16)
    grad_bias_out = jnp.sum(grad_attn, axis=0, dtype=f32)
    to_members = jnp.stack(
        [
            dot_right(grad_attn, out_low[k * span : (k + 1) * span]).astype(bf16)
            for k in range(shards)
        ]
    )
    attn_halves = [grad_attn[:, :out_wide], grad_attn[:, out_wide:]]
    attn_own = jnp.where(core == 0, attn_halves[0], attn_halves[1])
    attn_other = jnp.where(core == 0, attn_halves[1], attn_halves[0])
    down_other = moves.core_swap(down_pair[row_count:])
    grad_heads, attn_other, up_cut, down_sums, down_other = together(
        moves.cores_exchange(to_members), moves.core_swap(attn_other), up_cut, down_sums, down_other
    )
    attn_pair = jnp.concatenate([attn_own, attn_other], axis=0)
    grad_heads = moves.members_exchange(grad_heads).reshape(group_rows, span)
    up_state = moves.reduce_start(up_cut, 1)
    down_mid = moves.reduce_close(down_sums, 1)
    block_out = residual + down_pair[:row_count].astype(f32) + down_other.astype(f32) + bias_down
    block_out = block_out.astype(bf16)

    out_terms = dot_rows(attended_pair, attn_pair).astype(bf16)
    def shards_halve(piece, bits):
        piece = piece.reshape((piece.shape[0] // 2, 2) + piece.shape[1:])
        bit = moves.shard_bit(bits)
        return pick(piece, bit, 1), moves.shard_swap(pick(piece, 1 - bit, 1), bits)

    def halved(state):
        own, other = state
        return (own.astype(f32) + other.astype(f32)).astype(bf16)

    def shards_sum(piece):
        rows = piece.shape[1]
        return lax.psum_scatter(
            piece.reshape(shards * rows, piece.shape[2]), "shard", scatter_dimension=0, tiled=True
        )

    grad_heads, down_mid, out_terms, block_out = together(
        grad_heads, down_mid, out_terms, block_out
    )
    block_other = moves.home_send(block_out)
    down_owned = shards_sum(down_mid)
    out_state = moves.reduce_open(out_terms.reshape(shards, chips, rows_piece, out_wide), 1)
    attend_args = (plan, slopes)
    parts = 2 if heads % 4 == 0 else 1
    part_heads = heads // parts
    grad_qkv = attend_backward(
        qkv_rows, grad_heads, attended_cols, logs, *attend_args, part_heads, BLOCK, 0, None
    )
    grad_qkv, up_state, out_state = together(grad_qkv, up_state, out_state)
    up_sums, out_sums = moves.reduce_add(up_state), moves.reduce_add(out_state)
    grad_qkv, up_sums, out_sums = together(grad_qkv, up_sums, out_sums)
    up_out_state = [
        jnp.concatenate([up_part, out_part], axis=-1) for up_part, out_part in zip(up_sums, out_sums)
    ]
    if parts == 2:
        grad_qkv = attend_backward(
            qkv_rows, grad_heads, attended_cols, logs, *attend_args, part_heads, BLOCK, part_heads, grad_qkv
        )
    grad_qkv, up_out_state, block_other = together(
        grad_qkv, moves.reduce_send(up_out_state, 1), block_other
    )
    block_out = moves.home_join(block_out, block_other)
    up_out_piece = moves.reduce_final(up_out_state)
    up_out_state = shards_halve(up_out_piece, 1)

    grad_bias_q_part = jnp.sum(grad_qkv[:, :span], axis=0, dtype=f32)
    grad_bias_v_part = jnp.sum(grad_qkv[:, 2 * span :], axis=0, dtype=f32)

    grad_halves = grad_qkv.reshape(2, half * row_count, 3 * span)
    sent = dot_right(pick(grad_halves, 1 - core), qkv_cols).astype(bf16)
    sent = moves.core_swap(sent)
    qkv_terms = dot_rows(act_all, grad_qkv).astype(bf16)
    qkv_terms = qkv_terms.reshape(shards, chips, rows_piece, 3 * span)
    qkv_state = moves.reduce_open(qkv_terms, 1)
    back = dot_right(pick(grad_halves, core), qkv_cols) + sent.astype(f32)
    qkv_state, back, up_out_state = together(qkv_state, back, up_out_state)

    back = back.reshape(half, row_count, width)
    low_bits = list(reversed(moves.low_bits()))
    for bits in low_bits[:-1]:
        back = moves.reduce_bit(
            back, moves.shard_bit(bits), functools.partial(moves.shard_swap, bits=bits)
        )
    back = back.reshape((2, -1) + back.shape[1:])
    back_bit = moves.shard_bit(low_bits[-1])
    back_other = moves.shard_swap(pick(back, 1 - back_bit).astype(bf16), low_bits[-1])
    up_out_piece, bits = halved(up_out_state), 2
    while bits < half:
        up_out_piece = halved(shards_halve(up_out_piece, bits))
        bits *= 2
    up_out_state = shards_halve(up_out_piece, half)
    qkv_state = moves.reduce_send(moves.reduce_add(qkv_state), 1)
    qkv_state, up_out_state = together(qkv_state, up_out_state)

    up_out_owned = halved(up_out_state)[0]
    up_out_state = moves.spread_open(up_out_owned)
    qkv_piece = moves.reduce_final(qkv_state)
    qkv_piece = qkv_piece.reshape((2, half) + qkv_piece.shape[1:])
    qkv_own = pick(qkv_piece, moves.side)
    qkv_other = moves.shard_swap(pick(qkv_piece, 1 - moves.side), half)
    back_other, qkv_other, up_out_state = together(back_other, qkv_other, up_out_state)

    qkv_piece = moves.half_exchange(halved((qkv_own, qkv_other)))
    down_state = moves.spread_open(down_owned)
    grad_act_one = pick(back, back_bit) + back_other.astype(f32)
    grad_act_one = grad_act_one.reshape(row_count, width)
    grad_gain_one = jnp.sum(grad_act_one * normed_one, axis=0)
    grad_shift_one = jnp.sum(grad_act_one, axis=0)
    grad_inputs = grad_residual + norm_back(grad_act_one, normed_one, inv_std_one, gain_one)
    grad_inputs, qkv_piece, down_state = together(grad_inputs.astype(bf16), qkv_piece, down_state)
    tokens_other = moves.home_send(grad_inputs)
    qkv_owned = moves.chips_gather(qkv_piece, 1)

    up_out_first, up_out_second = moves.core_pair(
        moves.chips_gather(up_out_owned, 0, tuple(up_out_state)).reshape(rows_z, up_wide + out_wide)
    )
    out_grad = jnp.concatenate([up_out_first[:, up_wide:], up_out_second[:, up_wide:]], axis=1)
    up_columns = []
    for number in range(shards):
        part = slice(number * half_cols, (number + 1) * half_cols)
        up_columns += [up_out_first[:, part], up_out_second[:, part]]
    up_grad = jnp.concatenate(up_columns, axis=1)
    down_first, down_second = moves.core_pair(
        moves.chips_gather(down_owned, 0, tuple(down_state)).reshape(half_cols, width)
    )
    down_grad = jnp.concatenate([down_first, down_second], axis=0)
    qkv_owned = qkv_owned.reshape(half, rows_z, 3 * span)
    qkv_other, tokens_other = together(moves.core_swap(qkv_owned), tokens_other)
    tokens_grad = moves.home_join(grad_inputs, tokens_other)
    qkv_first = jnp.where(core == 0, qkv_owned, qkv_other)
    qkv_second = jnp.where(core == 0, qkv_other, qkv_owned)
    qkv_columns = []
    for kind in range(3):
        for source in (qkv_first, qkv_second):
            for number in range(half):
                qkv_columns.append(source[number][:, kind * span : (kind + 1) * span])
    qkv_grad = jnp.concatenate(qkv_columns, axis=1)

    gradients = [qkv_grad, out_grad, up_grad, down_grad]
    heights = [width, width, width, hidden_width]
    rows_old = [row_state[k : k + 1] for k in range(3)] + [down_rows.reshape(1, -1)]
    stats = [
        factor_stats(gradient, old, decay_rate) for gradient, old in zip(gradients, rows_old)
    ]

    def to_sum(number):
        weight_sum = jnp.broadcast_to(weight_sums[number], (1, 128))
        return [stats[number][2], jnp.concatenate([stats[number][3], weight_sum], axis=0)]

    def spread_heads(part):
        return [jnp.where(member == number, part, 0.0) for number in range(shards)]

    bias_up_parts = []
    for number in range(shards):
        part = grad_bias_up[number * half_cols : (number + 1) * half_cols]
        bias_up_parts += [jnp.where(core == 0, part, 0.0), jnp.where(core == 1, part, 0.0)]
    vector_part = moves.sum_reps(
        jnp.concatenate(
            [grad_gain_one, grad_shift_one]
            + spread_heads(grad_bias_q_part)
            + spread_heads(grad_bias_v_part)
            + [grad_bias_out, grad_gain_two, grad_shift_two]
            + bias_up_parts
            + [grad_bias_down]
        )
    )
    vector_rows = vector_part.reshape(2, -1)
    all_sums = summed(moves, to_sum(0) + to_sum(1) + to_sum(2) + to_sum(3) + [vector_rows])
    sums = [all_sums[0:2], all_sums[2:4], all_sums[4:6], all_sums[6:8]]
    vector_grad = all_sums[8].reshape(-1)
    updates = []
    offset = 0
    for number in range(4):
        end_col = offset + gradients[number].shape[1]
        updates.append(
            factor_apply(
                gradients[number],
                weights[number],
                stats[number][0],
                sums[number][0],
                sums[number][1],
                col_state[offset:end_col].reshape(1, -1),
                heights[number],
                decay_rate,
            )
        )
        offset = end_col
    grads_out, new_weights, copies, new_cols, rms_rows = zip(*updates)
    rms_values = [rms[0, 0] for rms in rms_rows]

    vector_state_new = decay_rate * vector_state + (1.0 - decay_rate) * (
        vector_grad * vector_grad + eps_second
    )
    vector_step = vector_grad * lax.rsqrt(vector_state_new)
    vector_rms = jnp.sqrt(jnp.mean(vector_step * vector_step))
    vector_new = vectors - rate_step * jnp.sqrt(
        jnp.mean(vectors * vectors)
    ) * vector_step / jnp.maximum(1.0, vector_rms / clip_level)
    update_rms = jnp.stack(rms_values + [vector_rms])
    return (
        block_out,
        tokens_grad,
        *grads_out,
        vector_grad,
        *new_weights,
        vector_new,
        *copies,
        jnp.concatenate([stats[0][1], stats[1][1], stats[2][1]], axis=0),
        stats[3][1].reshape(-1),
        jnp.concatenate(new_cols, axis=1).reshape(-1),
        vector_state_new,
        update_rms,
    )


def solution(mesh):
    in_specs = (
        P(("rep", "shard"), None),
        P(("rep", "shard"), None),
        P("rep", None),
        P("shard", None),
        P("shard", None),
        P("shard", None),
        P("shard", None),
        P(),
        P(None, "shard"),
        P("shard"),
        P(),
        P(),
    )
    out_specs = (
        P(("rep", "shard"), None),
        P(("rep", "shard"), None),
        P("shard", None),
        P("shard", None),
        P("shard", None),
        P("shard", None),
        P(),
        P("shard", None),
        P("shard", None),
        P("shard", None),
        P("shard", None),
        P(),
        P("shard", None),
        P("shard", None),
        P("shard", None),
        P("shard", None),
        P(None, "shard"),
        P("shard"),
        P(),
        P(),
        P(),
    )
    return jax.shard_map(
        on_device, mesh=mesh, in_specs=in_specs, out_specs=out_specs, check_vma=False
    )
```

```python
import functools

import jax
import jax.numpy as jnp
from jax import lax
from jax.experimental import pallas as pl
from jax.experimental.pallas import tpu as pltpu
from jax.sharding import PartitionSpec as P

HEADS = 16
STEP = 10
BLOCK = 256


eps_norm = 1e-05
eps_second = 1e-30
rate_step = 0.5
clip_level = 1.0
masked = -1e30
gelu_root = (2.0 / 3.141592653589793) ** 0.5
gelu_cubic = 0.044715

f32 = jnp.float32
bf16 = jnp.bfloat16


def norm_parts(values):
    average = jnp.mean(values, axis=-1, keepdims=True)
    centred = values - average
    inv_std = lax.rsqrt(jnp.mean(centred * centred, axis=-1, keepdims=True) + eps_norm)
    return (centred * inv_std, inv_std)


def norm_back(grad_out, normed, inv_std, gain_vec):
    grad_normed = grad_out * gain_vec
    inner_mean = jnp.mean(grad_normed * normed, axis=-1, keepdims=True)
    centred = grad_normed - jnp.mean(grad_normed, axis=-1, keepdims=True)
    return (centred - normed * inner_mean) * inv_std


def gelu_value(pre_act):
    curve = jnp.tanh(gelu_root * (pre_act + gelu_cubic * pre_act * pre_act * pre_act))
    return 0.5 * pre_act * (1.0 + curve)


def gelu_slope(pre_act):
    square = pre_act * pre_act
    curve = jnp.tanh(gelu_root * (pre_act + gelu_cubic * square * pre_act))
    inner = gelu_root * (1.0 + 3.0 * gelu_cubic * square)
    return 0.5 * (1.0 + curve) + 0.5 * pre_act * (1.0 - curve * curve) * inner


def dot(left_side, right_side):
    return jnp.dot(left_side, right_side, preferred_element_type=f32)


def dot_right(left_side, right_side):
    return lax.dot_general(
        left_side, right_side, (((1,), (1,)), ((), ())), preferred_element_type=f32
    )


def dot_rows(left_side, right_side):
    return lax.dot_general(
        left_side, right_side, (((0,), (0,)), ((), ())), preferred_element_type=f32
    )


def pick(stack, index, axis=0):
    return lax.dynamic_index_in_dim(stack, index, axis, keepdims=False, allow_negative_indices=False)


def cut_rows(values, start, count):
    return lax.dynamic_slice_in_dim(values, start, count, 0, allow_negative_indices=False)


def place(stack, part, index, axis=0):
    return lax.dynamic_update_index_in_dim(stack, part, index, axis, allow_negative_indices=False)


def head_rows(number, head_width):
    return slice(number * head_width, (number + 1) * head_width)


def lane_masks(block_rows, width, heads):
    lanes = lax.broadcasted_iota(jnp.int32, (block_rows, width), 1)
    head_width = width // heads
    return [
        (lanes >= number * head_width) & (lanes < (number + 1) * head_width)
        for number in range(heads)
    ]


def allowed_pairs(key_block, query_block, start_row, block):
    key_pos = lax.broadcasted_iota(jnp.int32, (block, block), 0) + key_block * block
    query_pos = lax.broadcasted_iota(jnp.int32, (block, block), 1) + query_block * block
    return (key_pos <= query_pos) & (key_pos >= start_row)


def key_offsets(key_block, query_block, block):
    rows = lax.broadcasted_iota(jnp.int32, (block, 1), 0)
    return (rows + (key_block - query_block) * block).astype(f32)


def turned(values):
    return jnp.transpose(values.astype(f32))


def head_stack(values, lanes):
    zero = jnp.zeros(values.shape, values.dtype)
    return jnp.concatenate([jnp.where(lane, values, zero) for lane in lanes], axis=0)


def eights(values, combine):
    rows, columns = values.shape
    return combine(values.reshape(rows // 8, 8, columns), axis=0)


def forward_kernel(
    heads,
    block,
    low_ref,
    mid_ref,
    slope_ref,
    start_ref,
    qkv_ref,
    out_ref,
    log_ref,
    values_turned,
    key_stack,
    score_ref,
):
    tokens = qkv_ref.shape[0]
    width = qkv_ref.shape[1] // 3
    head_width = width // heads
    blocks = tokens // block
    query_block = pl.program_id(0)

    @pl.when(query_block == 0)
    def _():
        lanes = lane_masks(block, width, heads)
        for number in range(blocks):
            rows = slice(number * block, (number + 1) * block)
            values_turned[number] = turned(qkv_ref[rows, 2 * width :]).astype(bf16)
            key_stack[number] = head_stack(qkv_ref[rows, width : 2 * width], lanes)

    first_row = pl.multiple_of(query_block * block, block)
    queries = qkv_ref[pl.ds(first_row, block), :width].astype(f32) * head_width ** (-0.5)
    queries = turned(queries).astype(bf16)
    start_row = start_ref[query_block]

    def score_step(key_block, bests, with_mask):
        scores = dot(key_stack[key_block], queries)
        offsets = key_offsets(key_block, query_block, block)
        allowed = allowed_pairs(key_block, query_block, start_row, block) if with_mask else None
        result = []
        for number in range(heads):
            rows = head_rows(number, block)
            part = scores[rows] + slope_ref[number] * offsets
            if with_mask:
                part = jnp.where(allowed, part, masked)
            score_ref[key_block, rows, :] = part
            result.append(jnp.maximum(bests[number], eights(part, jnp.max)))
        return tuple(result)

    low, mid = low_ref[query_block], mid_ref[query_block]
    bests = tuple(jnp.full((8, block), masked, f32) for _ in range(heads))
    bests = lax.fori_loop(low, mid, functools.partial(score_step, with_mask=True), bests)
    bests = lax.fori_loop(mid, query_block, functools.partial(score_step, with_mask=False), bests)
    bests = score_step(query_block, bests, True)
    bests = [jnp.max(best, axis=0, keepdims=True) for best in bests]

    def value_step(key_block, state):
        result = []
        for number in range(heads):
            total, gathered = state[2 * number : 2 * number + 2]
            weights = jnp.exp(score_ref[key_block, head_rows(number, block), :] - bests[number])
            value_rows = values_turned[key_block, head_rows(number, head_width), :]
            result += [
                total + eights(weights, jnp.sum),
                gathered + dot(value_rows, weights.astype(bf16)),
            ]
        return tuple(result)

    state = ()
    for number in range(heads):
        state += (jnp.zeros((8, block), f32), jnp.zeros((head_width, block), f32))
    state = lax.fori_loop(low, query_block + 1, value_step, state)
    columns = []
    for number in range(heads):
        total = jnp.sum(state[2 * number], axis=0, keepdims=True)
        columns.append(state[2 * number + 1] / total)
        log_ref[0, number : number + 1, :] = bests[number] + jnp.log(total)
    out_ref[...] = jnp.transpose(jnp.concatenate(columns, axis=0)).astype(bf16)


def backward_kernel(heads, block, first_head, merge, *refs):
    full_ref, high_ref, slope_ref, start_ref, log_ref, qkv_ref, grad_ref, out_ref = refs[:8]
    earlier_ref = refs[8] if merge else None
    result_ref = refs[9 if merge else 8]
    (
        queries_turned,
        grads_turned,
        keys_turned,
        query_stack,
        grad_stack,
        key_stack,
        value_stack,
        delta_rows,
        query_grads,
    ) = refs[10 if merge else 9 :]
    tokens, all_width = grad_ref.shape
    head_width = all_width // log_ref.shape[1]
    width = heads * head_width
    scale = head_width ** (-0.5)
    blocks = tokens // block
    key_block = pl.program_id(0)
    lanes = lane_masks(block, width, heads)

    def columns(kind):
        start = kind * all_width + first_head * head_width
        return slice(start, start + width)

    def target(kind):
        start = (kind * all_width + first_head * head_width) if merge else kind * width
        return slice(start, start + width)

    @pl.when(key_block == 0)
    def _():
        for number in range(blocks):
            rows = slice(number * block, (number + 1) * block)
            queries = qkv_ref[rows, columns(0)]
            queries_turned[number] = turned(queries.astype(f32) * scale).astype(bf16)
            query_stack[number] = head_stack(queries, lanes)
            keys_turned[number] = turned(qkv_ref[rows, columns(1)]).astype(bf16)
            grads = grad_ref[rows, columns(0)]
            grad_stack[number] = head_stack(grads, lanes)
            grads = grads.astype(f32)
            grads_turned[number] = turned(grads).astype(bf16)
            product = turned(grads * out_ref[rows, columns(0)].astype(f32))
            for head in range(heads):
                delta_rows[number, head : head + 1, :] = jnp.sum(
                    product[head_rows(head, head_width)], axis=0, keepdims=True
                )
            query_grads[number] = jnp.zeros((width, block), f32)

    key_row = pl.multiple_of(key_block * block, block)
    key_stack[...] = head_stack(qkv_ref[pl.ds(key_row, block), columns(1)], lanes)
    value_stack[...] = head_stack(qkv_ref[pl.ds(key_row, block), columns(2)], lanes)

    def step(query_block, state, with_mask):
        key_total, value_total = state
        scores = dot(key_stack[...], queries_turned[query_block])
        grad_weights = dot(value_stack[...], grads_turned[query_block])
        offsets = key_offsets(key_block, query_block, block)
        if with_mask:
            allowed = allowed_pairs(key_block, query_block, start_ref[query_block], block)
        weight_list, grad_list = [], []
        for number in range(heads):
            rows = head_rows(number, block)
            head = first_head + number
            part = scores[rows] + slope_ref[head] * offsets
            part = part - log_ref[query_block, head : head + 1, :]
            if with_mask:
                part = jnp.where(allowed, part, masked)
            probabilities = jnp.exp(part)
            delta = delta_rows[query_block, number : number + 1, :]
            grad_scores = (probabilities * (grad_weights[rows] - delta)).astype(bf16)
            weight_list.append(probabilities.astype(bf16))
            grad_list.append(grad_scores)
            rows = head_rows(number, head_width)
            query_grads[query_block, rows, :] += dot(keys_turned[key_block, rows, :], grad_scores)
        weight_row = jnp.concatenate(weight_list, axis=1)
        grad_row = jnp.concatenate(grad_list, axis=1)
        return (
            key_total + dot(grad_row, query_stack[query_block]),
            value_total + dot(weight_row, grad_stack[query_block]),
        )

    state = (jnp.zeros((block, width), f32), jnp.zeros((block, width), f32))
    state = step(key_block, state, True)
    full, high = full_ref[key_block], high_ref[key_block]
    state = lax.fori_loop(key_block + 1, full, functools.partial(step, with_mask=False), state)
    state = lax.fori_loop(full, high, functools.partial(step, with_mask=True), state)
    result_ref[pl.ds(key_row, block), target(1)] = (state[0] * scale).astype(bf16)
    result_ref[pl.ds(key_row, block), target(2)] = state[1].astype(bf16)
    if merge:
        other = first_head * head_width
        for kind in range(3):
            result_ref[pl.ds(key_row, block), kind * all_width : kind * all_width + other] = earlier_ref[
                pl.ds(key_row, block), kind * other : (kind + 1) * other
            ]

    @pl.when(key_block == blocks - 1)
    def _():
        for number in range(blocks):
            rows = slice(number * block, (number + 1) * block)
            result_ref[rows, target(0)] = jnp.transpose(query_grads[number] * scale).astype(bf16)


def block_plan(lengths, tokens, block):
    ends = jnp.cumsum(lengths)
    positions = jnp.arange(tokens, dtype=jnp.int32)
    passed = positions[:, None] >= ends[None, :]
    starts = jnp.max(jnp.where(passed, ends[None, :], 0), axis=1).astype(jnp.int32)
    finish = jnp.min(jnp.where(passed, tokens, ends[None, :]), axis=1).astype(jnp.int32)
    blocks = tokens // block
    number = jnp.arange(blocks, dtype=jnp.int32)
    first_start = starts[::block]
    last_start = starts[block - 1 :: block]
    low = first_start // block
    mid = jnp.clip((last_start + block - 1) // block, low, number)
    high = (finish[block - 1 :: block] - 1) // block + 1
    full = jnp.clip(finish[::block] // block, number + 1, high)
    return (starts.reshape(blocks, 1, block), low, mid, full, high)


def scalar_spec():
    return pl.BlockSpec(memory_space=pltpu.SMEM)


def whole_spec(shape):
    return pl.BlockSpec(shape, lambda step: (0,) * len(shape), pipeline_mode=pl.Buffered(1))


def attend_forward(qkv, plan, slopes, heads, block):
    tokens, triple = qkv.shape
    width = triple // 3
    blocks = tokens // block
    starts, low, mid, full, high = plan
    return pl.pallas_call(
        functools.partial(forward_kernel, heads, block),
        grid=(blocks,),
        in_specs=[
            scalar_spec(),
            scalar_spec(),
            scalar_spec(),
            whole_spec((blocks, 1, block)),
            whole_spec((tokens, triple)),
        ],
        out_specs=[
            pl.BlockSpec((block, width), lambda step: (step, 0)),
            pl.BlockSpec((1, heads, block), lambda step: (step, 0, 0)),
        ],
        out_shape=[
            jax.ShapeDtypeStruct((tokens, width), bf16),
            jax.ShapeDtypeStruct((blocks, heads, block), f32),
        ],
        scratch_shapes=[
            pltpu.VMEM((blocks, width, block), bf16),
            pltpu.VMEM((blocks, heads * block, width), bf16),
            pltpu.VMEM((blocks, heads * block, block), f32),
        ],
        compiler_params=pltpu.CompilerParams(
            dimension_semantics=("arbitrary",), vmem_limit_bytes=28 * 1024 * 1024
        ),
        cost_estimate=pl.CostEstimate(
            flops=3 * tokens * tokens * 256 * heads,
            bytes_accessed=10 * tokens * width,
            transcendentals=tokens * tokens * heads // 2,
        ),
        name="attend_forward",
    )(low, mid, slopes, starts, qkv)


def attend_backward(qkv, grads, outputs, logs, plan, slopes, heads, block, first_head, earlier):
    tokens, triple = qkv.shape
    all_width = triple // 3
    all_heads = logs.shape[1]
    width = all_width // all_heads * heads
    blocks = tokens // block
    starts, low, mid, full, high = plan
    merge = earlier is not None
    result_width = triple if merge else 3 * width
    operands = [full, high, slopes, starts, logs, qkv, grads, outputs]
    specs = [scalar_spec() for _ in range(3)] + [whole_spec(entry.shape) for entry in operands[3:]]
    if merge:
        operands.append(earlier)
        specs.append(whole_spec(earlier.shape))
    return pl.pallas_call(
        functools.partial(backward_kernel, heads, block, first_head, merge),
        grid=(blocks,),
        in_specs=specs,
        out_specs=pl.BlockSpec((tokens, result_width), lambda step: (0, 0)),
        out_shape=jax.ShapeDtypeStruct((tokens, result_width), bf16),
        scratch_shapes=[
            pltpu.VMEM((blocks, width, block), bf16),
            pltpu.VMEM((blocks, width, block), bf16),
            pltpu.VMEM((blocks, width, block), bf16),
            pltpu.VMEM((blocks, heads * block, width), bf16),
            pltpu.VMEM((blocks, heads * block, width), bf16),
            pltpu.VMEM((heads * block, width), bf16),
            pltpu.VMEM((heads * block, width), bf16),
            pltpu.VMEM((blocks, heads, block), f32),
            pltpu.VMEM((blocks, width, block), f32),
        ],
        compiler_params=pltpu.CompilerParams(
            dimension_semantics=("arbitrary",), vmem_limit_bytes=28 * 1024 * 1024
        ),
        cost_estimate=pl.CostEstimate(
            flops=8 * tokens * tokens * 256 * heads,
            bytes_accessed=20 * tokens * width,
            transcendentals=tokens * tokens * heads // 2,
        ),
        name="attend_backward",
    )(*operands)


def hidden_backward_kernel(own_ref, other_ref, weight_ref, slope_ref, result_ref, total_ref):
    rows = own_ref.shape[0]
    total = jnp.zeros(total_ref.shape, f32)
    for number, ref in enumerate((own_ref, other_ref)):
        part = slice(number * rows, (number + 1) * rows)
        grads = dot_right(ref[...], weight_ref[...]) * slope_ref[part, :].astype(f32)
        grads = grads.astype(bf16)
        result_ref[part, :] = grads
        total = total + jnp.sum(grads.astype(f32), axis=0, keepdims=True)
    total_ref[...] = total


def hidden_backward(weight, cot_own, cot_other, slopes):
    rows, width = cot_own.shape
    breadth = slopes.shape[1]
    tile = min(256, breadth)
    return pl.pallas_call(
        hidden_backward_kernel,
        grid=(breadth // tile,),
        in_specs=[
            whole_spec((rows, width)),
            whole_spec((rows, width)),
            pl.BlockSpec((tile, width), lambda step: (step, 0)),
            pl.BlockSpec((2 * rows, tile), lambda step: (0, step)),
        ],
        out_specs=[
            pl.BlockSpec((2 * rows, tile), lambda step: (0, step)),
            pl.BlockSpec((1, tile), lambda step: (0, step)),
        ],
        out_shape=[
            jax.ShapeDtypeStruct((2 * rows, breadth), bf16),
            jax.ShapeDtypeStruct((1, breadth), f32),
        ],
        compiler_params=pltpu.CompilerParams(
            dimension_semantics=("arbitrary",), vmem_limit_bytes=20 * 1024 * 1024
        ),
        cost_estimate=pl.CostEstimate(flops=1, bytes_accessed=1, transcendentals=0),
        name="hidden_backward",
    )(cot_own, cot_other, weight, slopes)


def up_backward_kernel(grads_ref, weight_ref, result_ref):
    result_ref[...] = dot_right(grads_ref[...], weight_ref[...]).astype(result_ref.dtype)


def up_backward(weight, grads, number, kind_of):
    rows, breadth = grads.shape[0] // 2, grads.shape[1]
    width = weight.shape[0]
    tile = width // 4
    return pl.pallas_call(
        up_backward_kernel,
        grid=(4,),
        in_specs=[
            pl.BlockSpec((rows, breadth), lambda step: (number, 0)),
            pl.BlockSpec((tile, breadth), lambda step: (step, 0)),
        ],
        out_specs=pl.BlockSpec((rows, tile), lambda step: (0, step)),
        out_shape=jax.ShapeDtypeStruct((rows, width), kind_of),
        compiler_params=pltpu.CompilerParams(
            dimension_semantics=("arbitrary",), vmem_limit_bytes=28 * 1024 * 1024
        ),
        cost_estimate=pl.CostEstimate(flops=1, bytes_accessed=1, transcendentals=0),
        name="up_backward",
    )(grads, weight)


def down_projection_kernel(hidden_ref, weight_ref, result_ref):
    result_ref[...] = dot(hidden_ref[...], weight_ref[...]).astype(result_ref.dtype)


def down_projection(hidden, weight):
    rows, breadth = hidden.shape
    width = weight.shape[1]
    tile = min(256, rows)
    return pl.pallas_call(
        down_projection_kernel,
        grid=(rows // tile,),
        in_specs=[
            pl.BlockSpec((tile, breadth), lambda step: (step, 0)),
            whole_spec((breadth, width)),
        ],
        out_specs=pl.BlockSpec((tile, width), lambda step: (step, 0)),
        out_shape=jax.ShapeDtypeStruct((rows, width), bf16),
        compiler_params=pltpu.CompilerParams(
            dimension_semantics=("arbitrary",), vmem_limit_bytes=20 * 1024 * 1024
        ),
        cost_estimate=pl.CostEstimate(flops=1, bytes_accessed=1, transcendentals=0),
        name="down_projection",
    )(hidden, weight)


def up_gradient_kernel(own_ref, other_ref, grads_ref, result_ref, act_turned):
    rows, width = own_ref.shape
    step = 256

    @pl.when(pl.program_id(0) == 0)
    def _():
        for number, ref in enumerate((own_ref, other_ref)):
            for row in range(0, rows, step):
                first = number * rows + row
                for column in range(0, width, step):
                    block = ref[row : row + step, column : column + step]
                    act_turned[column : column + step, first : first + step] = turned(block).astype(bf16)

    result_ref[...] = dot(act_turned[...], grads_ref[...]).astype(bf16)


def up_gradient(act_own, act_other, grads):
    rows, width = act_own.shape
    breadth = grads.shape[1]
    tile = min(512, breadth)
    return pl.pallas_call(
        up_gradient_kernel,
        grid=(breadth // tile,),
        in_specs=[
            whole_spec((rows, width)),
            whole_spec((rows, width)),
            pl.BlockSpec((2 * rows, tile), lambda step: (0, step)),
        ],
        out_specs=pl.BlockSpec((width, tile), lambda step: (0, step)),
        out_shape=jax.ShapeDtypeStruct((width, breadth), bf16),
        scratch_shapes=[pltpu.VMEM((width, 2 * rows), bf16)],
        compiler_params=pltpu.CompilerParams(
            dimension_semantics=("arbitrary",), vmem_limit_bytes=28 * 1024 * 1024
        ),
        cost_estimate=pl.CostEstimate(flops=1, bytes_accessed=1, transcendentals=0),
        name="up_gradient",
    )(act_own, act_other, grads)


def together(*values):
    return lax.optimization_barrier(tuple(values))


def ordered(own, other, bit, axis=0):
    first = jnp.where(bit == 0, own, other)
    second = jnp.where(bit == 0, other, own)
    return jnp.stack([first, second], axis=axis)


class Moves:
    def __init__(self):
        self.shards = lax.axis_size("shard")
        self.reps = lax.axis_size("rep")
        self.half = self.shards // 2
        self.chips = self.reps // 2
        self.shard = lax.axis_index("shard")
        self.rep = lax.axis_index("rep")
        self.core = self.rep & 1
        self.chip = self.rep >> 1
        self.side = lax.div(self.shard, self.half)
        self.member = lax.rem(self.shard, self.half) + self.core * self.half

    def core_swap(self, part):
        return lax.ppermute(part, "rep", [(r, r ^ 1) for r in range(self.reps)])

    def chip_swap(self, part, bits):
        return lax.ppermute(part, "rep", [(r, r ^ (2 * bits)) for r in range(self.reps)])

    def shard_swap(self, part, bits):
        return lax.ppermute(part, "shard", [(s, s ^ bits) for s in range(self.shards)])

    def shard_bit(self, bits):
        return lax.div(self.shard, bits) & 1

    def low_bits(self):
        bits, result = 1, []
        while bits < self.half:
            result.append(bits)
            bits *= 2
        return result

    def home_send(self, part):
        pairs = []
        for rep in range(self.reps):
            for shard in range(self.shards):
                if shard // self.half != rep % 2:
                    to_shard = (shard + self.half) % self.shards
                    pairs.append((rep * self.shards + shard, (rep ^ 1) * self.shards + to_shard))
        return lax.ppermute(part, ("rep", "shard"), pairs)

    def home_join(self, part, other):
        return jnp.where(self.side == self.core, part, other)

    def half_gather(self, part):
        stack = part[None]
        for bits in self.low_bits():
            own = stack
            stack = ordered(own, self.shard_swap(own, bits), self.shard_bit(bits))
            stack = stack.reshape((-1,) + part.shape)
        return stack

    def cores_gather(self, stack):
        stack = ordered(stack, self.core_swap(stack), self.core)
        return stack.reshape((-1,) + stack.shape[2:])

    def exchange_bit(self, stack, bit, swap):
        sources, targets = stack.shape[:2]
        stack = stack.reshape((sources, 2, targets // 2) + stack.shape[2:])
        own, other = pick(stack, bit, 1), swap(pick(stack, 1 - bit, 1))
        return ordered(own, other, bit, 1).reshape((2 * sources,) + own.shape[1:])

    def half_exchange(self, stack):
        stack = stack[None]
        for bits in reversed(self.low_bits()):
            swap = functools.partial(self.shard_swap, bits=bits)
            stack = self.exchange_bit(stack, self.shard_bit(bits), swap)
        return stack.reshape((self.half,) + stack.shape[2:])

    def cores_exchange(self, stack):
        return self.exchange_bit(stack[None], self.core, self.core_swap)

    def members_exchange(self, stack):
        for bits in reversed(self.low_bits()):
            swap = functools.partial(self.shard_swap, bits=bits)
            stack = self.exchange_bit(stack, self.shard_bit(bits), swap)
        return stack.reshape((self.shards,) + stack.shape[2:])

    def reduce_bit(self, stack, bit, swap):
        stack = stack.reshape((2, stack.shape[0] // 2) + stack.shape[1:])
        other = swap(pick(stack, 1 - bit).astype(bf16))
        return pick(stack, bit).astype(f32) + other.astype(f32)

    def spread_open(self, part):
        if self.chips == 4:
            return (self.chip_swap(part, 1), self.chip_swap(part, 2))
        held, bits = [part], 1
        while bits < self.chips:
            held = held + [self.chip_swap(piece, bits) for piece in held]
            bits *= 2
        return tuple(held[1:])

    def spread_close(self, state):
        if self.chips == 4:
            by_x, by_y = state
            cut, axis = by_x.shape[-2] // 2, by_x.ndim - 2
            far = [
                self.chip_swap(by_x[..., :cut, :], 2),
                self.chip_swap(by_y[..., cut:, :], 1),
            ]
            return (by_x, by_y, jnp.concatenate(far, axis=axis))
        return state

    def far_open(self, states):
        if self.chips != 4:
            return ()
        cut = states[0][0].shape[0] // 2
        return (
            self.chip_swap(jnp.concatenate([by_x[:cut] for by_x, _ in states], axis=0), 2),
            self.chip_swap(jnp.concatenate([by_y[cut:] for _, by_y in states], axis=0), 1),
        )

    def far_parts(self, states, far):
        if self.chips != 4:
            return [[(k + 1, 0, part) for k, part in enumerate(state)] for state in states]
        cut = states[0][0].shape[0] // 2
        result = []
        for number, (by_x, by_y) in enumerate(states):
            rows = slice(number * cut, (number + 1) * cut)
            result.append([(1, 0, by_x), (2, 0, by_y), (3, 0, far[0][rows]), (3, cut, far[1][rows])])
        return result

    def chips_gather(self, part, axis, state=None):
        shape = part.shape[:axis] + (self.chips,) + part.shape[axis:]
        stack = place(jnp.zeros(shape, part.dtype), part, self.chip, axis)
        others = self.spread_close(self.spread_open(part) if state is None else state)
        for number, piece in enumerate(others):
            stack = place(stack, piece, self.chip ^ (number + 1), axis)
        return stack

    def reduce_open(self, stack, axis):
        return self.reduce_start(self.reduce_cut(stack, axis), axis)

    def reduce_cut(self, stack, axis):
        if self.chips != 4:
            return (stack,)
        shape = stack.shape[:axis] + (2, 2) + stack.shape[axis + 1 :]
        stack = stack.reshape(shape)
        bit_x, bit_y = self.chip & 1, self.chip >> 1
        cut = shape[0] // 2
        first, second = stack[:cut], stack[cut:]
        return (
            pick(first, bit_x, axis + 1),
            pick(second, bit_y, axis),
            pick(first, 1 - bit_x, axis + 1),
            pick(second, 1 - bit_y, axis),
        )

    def reduce_start(self, parts, axis):
        if self.chips == 4:
            first, second, send_first, send_second = parts
            return (first, second, self.chip_swap(send_first, 1), self.chip_swap(send_second, 2))
        (stack,) = parts
        count = self.chips
        stack = stack.astype(f32)
        while count > 1:
            count //= 2
            shape = stack.shape[:axis] + (2, count) + stack.shape[axis + 1 :]
            stack = stack.reshape(shape)
            bit = lax.div(self.chip, count) & 1
            got = self.chip_swap(pick(stack, 1 - bit, axis).astype(bf16), count)
            stack = pick(stack, bit, axis) + got.astype(f32)
        return (pick(stack, 0, axis).astype(bf16),)

    def reduce_add(self, state):
        if self.chips != 4:
            return state
        first, second, got_first, got_second = state
        first = (first.astype(f32) + got_first.astype(f32)).astype(bf16)
        second = (second.astype(f32) + got_second.astype(f32)).astype(bf16)
        return (first, second)

    def reduce_send(self, state, axis):
        if self.chips != 4:
            return state
        first, second = state
        bit_x, bit_y = self.chip & 1, self.chip >> 1
        got_first = self.chip_swap(pick(first, 1 - bit_y, axis), 2)
        got_second = self.chip_swap(pick(second, 1 - bit_x, axis), 1)
        return (pick(first, bit_y, axis), pick(second, bit_x, axis), got_first, got_second)

    def reduce_final(self, state):
        if self.chips != 4:
            return state[0]
        first, second, got_first, got_second = state
        first = first.astype(f32) + got_first.astype(f32)
        second = second.astype(f32) + got_second.astype(f32)
        return jnp.concatenate([first, second], axis=0).astype(bf16)

    def reduce_close(self, state, axis):
        return self.reduce_final(self.reduce_send(state, axis))

    def core_pair(self, part):
        other = self.core_swap(part)
        first = jnp.where(self.core == 0, part, other)
        second = jnp.where(self.core == 0, other, part)
        return first, second

    def sum_reps(self, vector):
        bits = 1
        while bits < self.reps:
            vector = vector + lax.ppermute(vector, "rep", [(r, r ^ bits) for r in range(self.reps)])
            bits *= 2
        return vector

    def sum_shards(self, vector):
        bits = 1
        while bits < self.shards:
            vector = vector + self.shard_swap(vector, bits)
            bits *= 2
        return vector


def stats_kernel(decay_rate, gradient_ref, old_ref, rows_ref, lane_rows_ref, sums_ref, total_ref, partial):
    step = pl.program_id(0)
    rows, columns = gradient_ref.shape

    @pl.when(step == 0)
    def _():
        partial[...] = jnp.zeros_like(partial)
        total_ref[...] = jnp.zeros_like(total_ref)

    gradient = gradient_ref[...].astype(f32)
    square = gradient * gradient
    row_mean = jnp.sum(square, axis=1, keepdims=True) / columns
    old = jnp.transpose(jnp.broadcast_to(old_ref[...], (128, rows)))[:, 0:1]
    rows_new = decay_rate * old + (1.0 - decay_rate) * (row_mean + eps_second)
    rows_ref[...] = rows_new
    lane_rows_ref[...] = jnp.transpose(jnp.broadcast_to(rows_new, (rows, 128)))[0:1, :]
    total_ref[...] += jnp.broadcast_to(jnp.sum(rows_new, axis=0, keepdims=True), (1, 128))
    partial[0:8, :] += eights(square, jnp.sum)
    partial[8:16, :] += eights(square * (1.0 / rows_new), jnp.sum)

    @pl.when(step == pl.num_programs(0) - 1)
    def _():
        sums_ref[0:1, :] = jnp.sum(partial[0:8, :], axis=0, keepdims=True)
        sums_ref[1:2, :] = jnp.sum(partial[8:16, :], axis=0, keepdims=True)


def factor_stats(gradient, rows_old, decay_rate):
    height, breadth = gradient.shape
    rows = min(256 if breadth <= 1024 else 128, height)
    return pl.pallas_call(
        functools.partial(stats_kernel, decay_rate),
        grid=(height // rows,),
        in_specs=[
            pl.BlockSpec((rows, breadth), lambda step: (step, 0)),
            pl.BlockSpec((1, rows), lambda step: (0, step)),
        ],
        out_specs=[
            pl.BlockSpec((rows, 1), lambda step: (step, 0)),
            pl.BlockSpec((1, rows), lambda step: (0, step)),
            pl.BlockSpec((2, breadth), lambda step: (0, 0)),
            pl.BlockSpec((1, 128), lambda step: (0, 0)),
        ],
        out_shape=[
            jax.ShapeDtypeStruct((height, 1), f32),
            jax.ShapeDtypeStruct((1, height), f32),
            jax.ShapeDtypeStruct((2, breadth), f32),
            jax.ShapeDtypeStruct((1, 128), f32),
        ],
        scratch_shapes=[pltpu.VMEM((16, breadth), f32)],
        compiler_params=pltpu.CompilerParams(
            dimension_semantics=("arbitrary",), vmem_limit_bytes=16 * 1024 * 1024
        ),
        name="factor_stats",
    )(gradient, rows_old)


def apply_kernel(
    decay_rate,
    height,
    gradient_ref,
    weight_ref,
    rows_ref,
    sums_ref,
    scalar_ref,
    old_ref,
    gradient_out,
    weight_out,
    copy_out,
    cols_out,
    rms_out,
    col_factor,
):
    columns = gradient_ref.shape[1]

    @pl.when(pl.program_id(0) == 0)
    def _():
        cols_new = decay_rate * old_ref[...] + (1.0 - decay_rate) * (
            sums_ref[0:1, :] / height + eps_second
        )
        row_mean = scalar_ref[0:1, 0:1] / height
        weight_mean = scalar_ref[1:2, 0:1] / (height * columns)
        scaled = jnp.sum(sums_ref[1:2, :] / cols_new, axis=1, keepdims=True)
        rms_update = jnp.sqrt(row_mean / (height * columns) * scaled)
        factor = rate_step * jnp.sqrt(weight_mean) * jnp.sqrt(row_mean)
        factor = factor / jnp.maximum(1.0, rms_update / clip_level)
        col_factor[...] = factor * lax.rsqrt(cols_new)
        cols_out[...] = cols_new
        rms_out[...] = jnp.broadcast_to(rms_update, (1, 128))

    gradient = gradient_ref[...].astype(f32)
    new_weight = weight_ref[...] - gradient * lax.rsqrt(rows_ref[...]) * col_factor[...]
    gradient_out[...] = gradient
    weight_out[...] = new_weight
    copy_out[...] = new_weight.astype(bf16)


def factor_apply(gradient, weight, rows_new, sums, scalars, cols_old, height, decay_rate):
    own_height, breadth = gradient.shape
    rows = min(256 if breadth <= 1024 else 64, own_height)

    def rows_spec():
        return pl.BlockSpec((rows, breadth), lambda step: (step, 0))

    def row_spec(count, wide):
        return pl.BlockSpec((count, wide), lambda step: (0, 0))

    return pl.pallas_call(
        functools.partial(apply_kernel, decay_rate, height),
        grid=(own_height // rows,),
        in_specs=[
            rows_spec(),
            rows_spec(),
            pl.BlockSpec((rows, 1), lambda step: (step, 0)),
            row_spec(2, breadth),
            row_spec(2, 128),
            row_spec(1, breadth),
        ],
        out_specs=[rows_spec(), rows_spec(), rows_spec(), row_spec(1, breadth), row_spec(1, 128)],
        out_shape=[
            jax.ShapeDtypeStruct((own_height, breadth), f32),
            jax.ShapeDtypeStruct((own_height, breadth), f32),
            jax.ShapeDtypeStruct((own_height, breadth), bf16),
            jax.ShapeDtypeStruct((1, breadth), f32),
            jax.ShapeDtypeStruct((1, 128), f32),
        ],
        scratch_shapes=[pltpu.VMEM((1, breadth), f32)],
        compiler_params=pltpu.CompilerParams(
            dimension_semantics=("arbitrary",), vmem_limit_bytes=16 * 1024 * 1024
        ),
        name="factor_apply",
    )(gradient, weight, rows_new, sums, scalars, cols_old)


def summed(moves, entries):
    total = moves.sum_shards(jnp.concatenate(entries, axis=1))
    result, offset = [], 0
    for entry in entries:
        result.append(total[:, offset : offset + entry.shape[1]])
        offset += entry.shape[1]
    return result


def on_device(
    tokens,
    cotangent,
    seq_lengths,
    qkv_weight,
    out_weight,
    up_weight,
    down_weight,
    vectors,
    row_state,
    down_rows,
    col_state,
    vector_state,
):
    moves = Moves()
    shards, half, chips, core = moves.shards, moves.half, moves.chips, moves.core
    row_count, width = tokens.shape
    hidden_width = up_weight.shape[1]
    group_rows = row_count * shards
    heads = HEADS // shards
    head_width = width // HEADS
    span = heads * head_width
    member = moves.member
    decay_rate = 1.0 - STEP ** (-0.8)
    head_number = (member * heads + jnp.arange(heads, dtype=jnp.int32)).astype(f32)
    slopes = jnp.exp2(-8.0 * (head_number + 1.0) / HEADS)

    gain_one = vectors[0:width]
    shift_one = vectors[width : 2 * width]
    bias_query = vectors[2 * width : 3 * width]
    bias_value = vectors[3 * width : 4 * width]
    bias_out = vectors[4 * width : 5 * width]
    gain_two = vectors[5 * width : 6 * width]
    shift_two = vectors[6 * width : 7 * width]
    bias_up = vectors[7 * width : 7 * width + hidden_width]
    bias_down = vectors[7 * width + hidden_width :]

    other_tokens = moves.home_send(tokens)
    other_lengths = moves.core_swap(seq_lengths)
    lengths = jnp.where(moves.side == core, seq_lengths, other_lengths)[0]
    plan = block_plan(lengths, group_rows, BLOCK)
    rows_z = width // shards
    rows_piece = rows_z // chips
    my_rows = cut_rows(qkv_weight, moves.chip * rows_piece, rows_piece)
    my_rows = my_rows.astype(bf16)
    my_blocks = []
    for number in range(half):
        kinds = []
        for kind in range(3):
            first = kind * width + number * span
            second = first + half * span
            kinds.append(
                jnp.where(
                    core == 0, my_rows[:, first : first + span], my_rows[:, second : second + span]
                )
            )
        my_blocks.append(jnp.concatenate(kinds, axis=1))
    qkv_part = moves.half_exchange(jnp.stack(my_blocks))
    half_cols = hidden_width // (2 * shards)
    up_wide = shards * half_cols
    out_wide = width // 2
    down_piece = half_cols // chips

    def core_half(values):
        parts = []
        for number in range(shards):
            start = 2 * number * half_cols
            first = values[..., start : start + half_cols]
            second = values[..., start + half_cols : start + 2 * half_cols]
            parts.append(jnp.where(core == 0, first, second))
        return jnp.concatenate(parts, axis=-1)

    up_own = core_half(up_weight).astype(bf16).reshape(chips, rows_piece, up_wide)
    out_own = jnp.where(core == 0, out_weight[:, :out_wide], out_weight[:, out_wide:]).astype(bf16)
    out_own = out_own.reshape(chips, rows_piece, out_wide)
    down_own = cut_rows(down_weight, core * half_cols, half_cols).astype(bf16)
    fold = down_piece // rows_piece
    down_own = down_own.reshape(chips, fold, rows_piece, width)
    my_down = pick(down_own, moves.chip)
    weight_piece = jnp.concatenate(
        [pick(up_own, moves.chip), pick(out_own, moves.chip)] + [my_down[k] for k in range(fold)],
        axis=1,
    )
    near_pieces, bits = [weight_piece], 1
    while bits < half:
        near_pieces = near_pieces + [moves.shard_swap(piece, bits) for piece in near_pieces]
        bits *= 2
    near_pieces = near_pieces[1:]
    weights = [qkv_weight, out_weight, up_weight, down_weight]
    weight_sums = [jnp.sum(weight * weight) for weight in weights]
    other_tokens, qkv_part, near_pieces, weight_piece, plan, weight_sums = together(
        other_tokens, qkv_part, near_pieces, weight_piece, plan, weight_sums
    )
    home_tokens = moves.home_join(tokens, other_tokens)
    far_piece = moves.shard_swap(weight_piece, half)
    near_open = [moves.spread_open(piece) for piece in near_pieces]
    qkv_far = moves.shard_swap(qkv_part, half)
    qkv_far, near_open = together(qkv_far, near_open)
    qkv_part = ordered(qkv_part, qkv_far, moves.side).reshape(shards, rows_piece, 3 * span)
    qkv_cols = moves.chips_gather(qkv_part, 1).reshape(width, 3 * span)
    inputs = home_tokens.astype(f32)
    normed_one, inv_std_one = norm_parts(inputs)
    act_one = (normed_one * gain_one + shift_one).astype(bf16)
    act_half = moves.half_gather(act_one)

    act_half, qkv_cols, far_piece, cotangent = together(
        act_half, qkv_cols, far_piece, cotangent
    )
    other_cot = moves.home_send(cotangent)
    act_all = moves.cores_gather(act_half).reshape(group_rows, width)
    far_open = moves.spread_open(far_piece)
    far_pieces, bits = [far_piece], 1
    while bits < half:
        far_pieces = far_pieces + [moves.shard_swap(piece, bits) for piece in far_pieces]
        bits *= 2
    far_pieces = far_pieces[1:]

    bias_q_part = cut_rows(bias_query, member * span, span)
    bias_v_part = cut_rows(bias_value, member * span, span)
    qkv_bias = jnp.concatenate([bias_q_part, jnp.zeros_like(bias_q_part), bias_v_part])
    qkv_rows = (dot(act_all, qkv_cols) + qkv_bias).astype(bf16)
    attended_cols, logs = attend_forward(qkv_rows, plan, slopes, heads, BLOCK)
    attended_cols, far_open, far_pieces, other_cot = together(
        attended_cols, far_open, far_pieces, other_cot
    )
    attended_parts = moves.cores_exchange(attended_cols.reshape(shards, row_count, span))
    attended_parts = moves.members_exchange(attended_parts)
    first_states = near_open + [far_open]
    first_far = moves.far_open(first_states)
    last_states = [moves.spread_open(piece) for piece in far_pieces]
    attended_parts, first_far, last_states, other_cot = together(
        attended_parts, first_far, last_states, other_cot
    )
    home_cot = moves.home_join(cotangent, other_cot)
    last_far = moves.far_open(last_states)
    attended = jnp.concatenate([attended_parts[k] for k in range(shards)], axis=1)

    up_all = place(jnp.zeros((shards, chips, rows_piece, up_wide), bf16), up_own, moves.shard)
    out_all = place(jnp.zeros((shards, chips, rows_piece, out_wide), bf16), out_own, moves.shard)
    down_all = place(jnp.zeros((shards, chips, fold, rows_piece, width), bf16), down_own, moves.shard)
    pieces = near_pieces + [far_piece] + far_pieces
    parts_of = moves.far_parts(first_states, first_far) + moves.far_parts(last_states, last_far)
    for number, (piece, parts) in enumerate(zip(pieces, parts_of)):
        plane = moves.shard ^ (number + 1)
        for far, row, rows in [(0, 0, piece)] + parts:
            chip = moves.chip ^ far
            up_all = lax.dynamic_update_slice(
                up_all, rows[None, None, :, :up_wide], (plane, chip, row, 0), allow_negative_indices=False
            )
            out_all = lax.dynamic_update_slice(
                out_all, rows[None, None, :, up_wide : up_wide + out_wide], (plane, chip, row, 0), allow_negative_indices=False
            )
            start = up_wide + out_wide
            folds = [rows[:, start + k * width : start + (k + 1) * width] for k in range(fold)]
            down_all = lax.dynamic_update_slice(
                down_all, jnp.stack(folds)[None, None], (plane, chip, 0, row, 0), allow_negative_indices=False
            )
    up_half = up_all.reshape(width, up_wide)
    down_half = down_all.reshape(up_wide, width)
    out_first, out_second = moves.core_pair(out_all.reshape(width, out_wide))
    out_low = jnp.concatenate([out_first, out_second], axis=1)
    residual = inputs + dot(attended, out_low) + bias_out
    normed_two, inv_std_two = norm_parts(residual)
    act_two = (normed_two * gain_two + shift_two).astype(bf16)

    act_two_other, attended_other, cot_other = together(
        moves.core_swap(act_two), moves.core_swap(attended), moves.core_swap(home_cot)
    )
    cot_pair = jnp.concatenate([home_cot, cot_other], axis=0)
    act_two_pair = jnp.concatenate([act_two, act_two_other], axis=0)
    attended_pair = jnp.concatenate([attended, attended_other], axis=0)
    bias_up_half = core_half(bias_up)
    up_pair = dot(act_two_pair, up_half) + bias_up_half
    hidden_pair = gelu_value(up_pair).astype(bf16)
    slope_pair = gelu_slope(up_pair).astype(bf16)
    down_terms = dot_rows(hidden_pair, cot_pair).astype(bf16)
    down_state = moves.reduce_cut(down_terms.reshape(shards, chips, down_piece, width), 1)
    slope_pair, down_state = together(slope_pair, down_state)
    down_state = moves.reduce_start(down_state, 1)
    grad_y = home_cot.astype(f32)
    grad_bias_down = jnp.sum(grad_y, axis=0)
    grad_up_pair, grad_bias_up = hidden_backward(down_half, home_cot, cot_other, slope_pair)
    grad_bias_up = grad_bias_up.reshape(-1)
    back_other = moves.core_swap(up_backward(up_half, grad_up_pair, 1, bf16))
    up_terms = up_gradient(act_two, act_two_other, grad_up_pair)
    down_pair = down_projection(hidden_pair, down_half)
    back_other, down_pair, up_terms, down_state = together(
        back_other, down_pair, up_terms, down_state
    )
    up_cut = moves.reduce_cut(up_terms.reshape(shards, chips, rows_piece, up_wide), 1)
    down_sums = moves.reduce_add(down_state)
    grad_act_two = up_backward(up_half, grad_up_pair, 0, f32) + back_other.astype(f32)
    grad_gain_two = jnp.sum(grad_act_two * normed_two, axis=0)
    grad_shift_two = jnp.sum(grad_act_two, axis=0)
    grad_residual = grad_y + norm_back(grad_act_two, normed_two, inv_std_two, gain_two)
    grad_attn = grad_residual.astype(bf16)
    grad_bias_out = jnp.sum(grad_attn, axis=0, dtype=f32)
    to_members = jnp.stack(
        [
            dot_right(grad_attn, out_low[k * span : (k + 1) * span]).astype(bf16)
            for k in range(shards)
        ]
    )
    attn_halves = [grad_attn[:, :out_wide], grad_attn[:, out_wide:]]
    attn_own = jnp.where(core == 0, attn_halves[0], attn_halves[1])
    attn_other = jnp.where(core == 0, attn_halves[1], attn_halves[0])
    down_other = moves.core_swap(down_pair[row_count:])
    grad_heads, attn_other, up_cut, down_sums, down_other = together(
        moves.cores_exchange(to_members), moves.core_swap(attn_other), up_cut, down_sums, down_other
    )
    attn_pair = jnp.concatenate([attn_own, attn_other], axis=0)
    grad_heads = moves.members_exchange(grad_heads).reshape(group_rows, span)
    up_state = moves.reduce_start(up_cut, 1)
    down_mid = moves.reduce_close(down_sums, 1)
    block_out = residual + down_pair[:row_count].astype(f32) + down_other.astype(f32) + bias_down
    block_out = block_out.astype(bf16)

    out_terms = dot_rows(attended_pair, attn_pair).astype(bf16)
    def shards_halve(piece, bits):
        piece = piece.reshape((piece.shape[0] // 2, 2) + piece.shape[1:])
        bit = moves.shard_bit(bits)
        return pick(piece, bit, 1), moves.shard_swap(pick(piece, 1 - bit, 1), bits)

    def halved(state):
        own, other = state
        return (own.astype(f32) + other.astype(f32)).astype(bf16)

    def shards_sum(piece):
        rows = piece.shape[1]
        return lax.psum_scatter(
            piece.reshape(shards * rows, piece.shape[2]), "shard", scatter_dimension=0, tiled=True
        )

    grad_heads, down_mid, out_terms, block_out = together(
        grad_heads, down_mid, out_terms, block_out
    )
    block_other = moves.home_send(block_out)
    down_owned = shards_sum(down_mid)
    out_state = moves.reduce_open(out_terms.reshape(shards, chips, rows_piece, out_wide), 1)
    attend_args = (plan, slopes)
    parts = 2 if heads % 4 == 0 else 1
    part_heads = heads // parts
    grad_qkv = attend_backward(
        qkv_rows, grad_heads, attended_cols, logs, *attend_args, part_heads, BLOCK, 0, None
    )
    grad_qkv, up_state, out_state = together(grad_qkv, up_state, out_state)
    up_sums, out_sums = moves.reduce_add(up_state), moves.reduce_add(out_state)
    grad_qkv, up_sums, out_sums = together(grad_qkv, up_sums, out_sums)
    up_out_state = [
        jnp.concatenate([up_part, out_part], axis=-1) for up_part, out_part in zip(up_sums, out_sums)
    ]
    if parts == 2:
        grad_qkv = attend_backward(
            qkv_rows, grad_heads, attended_cols, logs, *attend_args, part_heads, BLOCK, part_heads, grad_qkv
        )
    grad_qkv, up_out_state, block_other = together(
        grad_qkv, moves.reduce_send(up_out_state, 1), block_other
    )
    block_out = moves.home_join(block_out, block_other)
    up_out_piece = moves.reduce_final(up_out_state)
    up_out_state = shards_halve(up_out_piece, 1)

    grad_bias_q_part = jnp.sum(grad_qkv[:, :span], axis=0, dtype=f32)
    grad_bias_v_part = jnp.sum(grad_qkv[:, 2 * span :], axis=0, dtype=f32)

    grad_halves = grad_qkv.reshape(2, half * row_count, 3 * span)
    sent = dot_right(pick(grad_halves, 1 - core), qkv_cols).astype(bf16)
    sent = moves.core_swap(sent)
    qkv_terms = dot_rows(act_all, grad_qkv).astype(bf16)
    qkv_terms = qkv_terms.reshape(shards, chips, rows_piece, 3 * span)
    qkv_state = moves.reduce_open(qkv_terms, 1)
    back = dot_right(pick(grad_halves, core), qkv_cols) + sent.astype(f32)
    qkv_state, back = together(qkv_state, back)

    back = back.reshape(half, row_count, width)
    low_bits = list(reversed(moves.low_bits()))
    for bits in low_bits[:-1]:
        back = moves.reduce_bit(
            back, moves.shard_bit(bits), functools.partial(moves.shard_swap, bits=bits)
        )
    back = back.reshape((2, -1) + back.shape[1:])
    back_bit = moves.shard_bit(low_bits[-1])
    back_other = moves.shard_swap(pick(back, 1 - back_bit).astype(bf16), low_bits[-1])
    qkv_state = moves.reduce_send(moves.reduce_add(qkv_state), 1)
    qkv_state, up_out_state = together(qkv_state, up_out_state)

    up_out_piece, bits = halved(up_out_state), 2
    while bits < half:
        up_out_piece = halved(shards_halve(up_out_piece, bits))
        bits *= 2
    up_out_state = shards_halve(up_out_piece, half)
    qkv_piece = moves.reduce_final(qkv_state)
    qkv_piece = qkv_piece.reshape((2, half) + qkv_piece.shape[1:])
    qkv_own = pick(qkv_piece, moves.side)
    qkv_other = moves.shard_swap(pick(qkv_piece, 1 - moves.side), half)
    back_other, qkv_other, up_out_state, down_owned = together(
        back_other, qkv_other, up_out_state, down_owned
    )

    up_out_owned = halved(up_out_state)[0]
    up_out_state = moves.spread_open(up_out_owned)
    qkv_piece = moves.half_exchange(halved((qkv_own, qkv_other)))
    down_state = moves.spread_open(down_owned)
    grad_act_one = pick(back, back_bit) + back_other.astype(f32)
    grad_act_one = grad_act_one.reshape(row_count, width)
    grad_gain_one = jnp.sum(grad_act_one * normed_one, axis=0)
    grad_shift_one = jnp.sum(grad_act_one, axis=0)
    grad_inputs = grad_residual + norm_back(grad_act_one, normed_one, inv_std_one, gain_one)
    grad_inputs, grad_gain_one, grad_shift_one, qkv_piece, down_state, up_out_state = together(
        grad_inputs.astype(bf16), grad_gain_one, grad_shift_one, qkv_piece, down_state, up_out_state
    )
    tokens_other = moves.home_send(grad_inputs)
    qkv_owned = moves.chips_gather(qkv_piece, 1)

    up_out_first, up_out_second = moves.core_pair(
        moves.chips_gather(up_out_owned, 0, tuple(up_out_state)).reshape(rows_z, up_wide + out_wide)
    )
    out_grad = jnp.concatenate([up_out_first[:, up_wide:], up_out_second[:, up_wide:]], axis=1)
    up_columns = []
    for number in range(shards):
        part = slice(number * half_cols, (number + 1) * half_cols)
        up_columns += [up_out_first[:, part], up_out_second[:, part]]
    up_grad = jnp.concatenate(up_columns, axis=1)
    down_first, down_second = moves.core_pair(
        moves.chips_gather(down_owned, 0, tuple(down_state)).reshape(half_cols, width)
    )
    down_grad = jnp.concatenate([down_first, down_second], axis=0)
    qkv_owned = qkv_owned.reshape(half, rows_z, 3 * span)
    qkv_other, tokens_other = together(moves.core_swap(qkv_owned), tokens_other)
    tokens_grad = moves.home_join(grad_inputs, tokens_other)
    qkv_first = jnp.where(core == 0, qkv_owned, qkv_other)
    qkv_second = jnp.where(core == 0, qkv_other, qkv_owned)
    qkv_columns = []
    for kind in range(3):
        for source in (qkv_first, qkv_second):
            for number in range(half):
                qkv_columns.append(source[number][:, kind * span : (kind + 1) * span])
    qkv_grad = jnp.concatenate(qkv_columns, axis=1)

    gradients = [qkv_grad, out_grad, up_grad, down_grad]
    heights = [width, width, width, hidden_width]
    rows_old = [row_state[k : k + 1] for k in range(3)] + [down_rows.reshape(1, -1)]
    stats = [
        factor_stats(gradient, old, decay_rate) for gradient, old in zip(gradients, rows_old)
    ]

    def to_sum(number):
        weight_sum = jnp.broadcast_to(weight_sums[number], (1, 128))
        return [stats[number][2], jnp.concatenate([stats[number][3], weight_sum], axis=0)]

    def spread_heads(part):
        return [jnp.where(member == number, part, 0.0) for number in range(shards)]

    bias_up_parts = []
    for number in range(shards):
        part = grad_bias_up[number * half_cols : (number + 1) * half_cols]
        bias_up_parts += [jnp.where(core == 0, part, 0.0), jnp.where(core == 1, part, 0.0)]
    vector_part = moves.sum_reps(
        jnp.concatenate(
            [grad_gain_one, grad_shift_one]
            + spread_heads(grad_bias_q_part)
            + spread_heads(grad_bias_v_part)
            + [grad_bias_out, grad_gain_two, grad_shift_two]
            + bias_up_parts
            + [grad_bias_down]
        )
    )
    vector_rows = vector_part.reshape(2, -1)
    all_sums = summed(moves, to_sum(0) + to_sum(1) + to_sum(2) + to_sum(3) + [vector_rows])
    sums = [all_sums[0:2], all_sums[2:4], all_sums[4:6], all_sums[6:8]]
    vector_grad = all_sums[8].reshape(-1)
    updates = []
    offset = 0
    for number in range(4):
        end_col = offset + gradients[number].shape[1]
        updates.append(
            factor_apply(
                gradients[number],
                weights[number],
                stats[number][0],
                sums[number][0],
                sums[number][1],
                col_state[offset:end_col].reshape(1, -1),
                heights[number],
                decay_rate,
            )
        )
        offset = end_col
    grads_out, new_weights, copies, new_cols, rms_rows = zip(*updates)
    rms_values = [rms[0, 0] for rms in rms_rows]

    vector_state_new = decay_rate * vector_state + (1.0 - decay_rate) * (
        vector_grad * vector_grad + eps_second
    )
    vector_step = vector_grad * lax.rsqrt(vector_state_new)
    vector_rms = jnp.sqrt(jnp.mean(vector_step * vector_step))
    vector_new = vectors - rate_step * jnp.sqrt(
        jnp.mean(vectors * vectors)
    ) * vector_step / jnp.maximum(1.0, vector_rms / clip_level)
    update_rms = jnp.stack(rms_values + [vector_rms])
    return (
        block_out,
        tokens_grad,
        *grads_out,
        vector_grad,
        *new_weights,
        vector_new,
        *copies,
        jnp.concatenate([stats[0][1], stats[1][1], stats[2][1]], axis=0),
        stats[3][1].reshape(-1),
        jnp.concatenate(new_cols, axis=1).reshape(-1),
        vector_state_new,
        update_rms,
    )


def solution(mesh):
    in_specs = (
        P(("rep", "shard"), None),
        P(("rep", "shard"), None),
        P("rep", None),
        P("shard", None),
        P("shard", None),
        P("shard", None),
        P("shard", None),
        P(),
        P(None, "shard"),
        P("shard"),
        P(),
        P(),
    )
    out_specs = (
        P(("rep", "shard"), None),
        P(("rep", "shard"), None),
        P("shard", None),
        P("shard", None),
        P("shard", None),
        P("shard", None),
        P(),
        P("shard", None),
        P("shard", None),
        P("shard", None),
        P("shard", None),
        P(),
        P("shard", None),
        P("shard", None),
        P("shard", None),
        P("shard", None),
        P(None, "shard"),
        P("shard"),
        P(),
        P(),
        P(),
    )
    return jax.shard_map(
        on_device, mesh=mesh, in_specs=in_specs, out_specs=out_specs, check_vma=False
    )
```

```python
import functools

import jax
import jax.numpy as jnp
from jax import lax
from jax.experimental import pallas as pl
from jax.experimental.pallas import tpu as pltpu
from jax.sharding import PartitionSpec as P

HEADS = 16
STEP = 10
BLOCK = 256


eps_norm = 1e-05
eps_second = 1e-30
rate_step = 0.5
clip_level = 1.0
masked = -1e30
gelu_root = (2.0 / 3.141592653589793) ** 0.5
gelu_cubic = 0.044715

f32 = jnp.float32
bf16 = jnp.bfloat16


def norm_parts(values):
    average = jnp.mean(values, axis=-1, keepdims=True)
    centred = values - average
    inv_std = lax.rsqrt(jnp.mean(centred * centred, axis=-1, keepdims=True) + eps_norm)
    return (centred * inv_std, inv_std)


def norm_back(grad_out, normed, inv_std, gain_vec):
    grad_normed = grad_out * gain_vec
    inner_mean = jnp.mean(grad_normed * normed, axis=-1, keepdims=True)
    centred = grad_normed - jnp.mean(grad_normed, axis=-1, keepdims=True)
    return (centred - normed * inner_mean) * inv_std


def gelu_value(pre_act):
    curve = jnp.tanh(gelu_root * (pre_act + gelu_cubic * pre_act * pre_act * pre_act))
    return 0.5 * pre_act * (1.0 + curve)


def gelu_slope(pre_act):
    square = pre_act * pre_act
    curve = jnp.tanh(gelu_root * (pre_act + gelu_cubic * square * pre_act))
    inner = gelu_root * (1.0 + 3.0 * gelu_cubic * square)
    return 0.5 * (1.0 + curve) + 0.5 * pre_act * (1.0 - curve * curve) * inner


def dot(left_side, right_side):
    return jnp.dot(left_side, right_side, preferred_element_type=f32)


def dot_right(left_side, right_side):
    return lax.dot_general(
        left_side, right_side, (((1,), (1,)), ((), ())), preferred_element_type=f32
    )


def dot_rows(left_side, right_side):
    return lax.dot_general(
        left_side, right_side, (((0,), (0,)), ((), ())), preferred_element_type=f32
    )


def pick(stack, index, axis=0):
    return lax.dynamic_index_in_dim(stack, index, axis, keepdims=False, allow_negative_indices=False)


def cut_rows(values, start, count):
    return lax.dynamic_slice_in_dim(values, start, count, 0, allow_negative_indices=False)


def place(stack, part, index, axis=0):
    return lax.dynamic_update_index_in_dim(stack, part, index, axis, allow_negative_indices=False)


def head_rows(number, head_width):
    return slice(number * head_width, (number + 1) * head_width)


def lane_masks(block_rows, width, heads):
    lanes = lax.broadcasted_iota(jnp.int32, (block_rows, width), 1)
    head_width = width // heads
    return [
        (lanes >= number * head_width) & (lanes < (number + 1) * head_width)
        for number in range(heads)
    ]


def allowed_pairs(key_block, query_block, start_row, block):
    key_pos = lax.broadcasted_iota(jnp.int32, (block, block), 0) + key_block * block
    query_pos = lax.broadcasted_iota(jnp.int32, (block, block), 1) + query_block * block
    return (key_pos <= query_pos) & (key_pos >= start_row)


def key_offsets(key_block, query_block, block):
    rows = lax.broadcasted_iota(jnp.int32, (block, 1), 0)
    return (rows + (key_block - query_block) * block).astype(f32)


def turned(values):
    return jnp.transpose(values.astype(f32))


def head_stack(values, lanes):
    zero = jnp.zeros(values.shape, values.dtype)
    return jnp.concatenate([jnp.where(lane, values, zero) for lane in lanes], axis=0)


def eights(values, combine):
    rows, columns = values.shape
    return combine(values.reshape(rows // 8, 8, columns), axis=0)


def forward_kernel(
    heads,
    block,
    low_ref,
    mid_ref,
    slope_ref,
    start_ref,
    qkv_ref,
    out_ref,
    log_ref,
    values_turned,
    key_stack,
    score_ref,
):
    tokens = qkv_ref.shape[0]
    width = qkv_ref.shape[1] // 3
    head_width = width // heads
    blocks = tokens // block
    query_block = pl.program_id(0)

    @pl.when(query_block == 0)
    def _():
        lanes = lane_masks(block, width, heads)
        for number in range(blocks):
            rows = slice(number * block, (number + 1) * block)
            values_turned[number] = turned(qkv_ref[rows, 2 * width :]).astype(bf16)
            key_stack[number] = head_stack(qkv_ref[rows, width : 2 * width], lanes)

    first_row = pl.multiple_of(query_block * block, block)
    queries = qkv_ref[pl.ds(first_row, block), :width].astype(f32) * head_width ** (-0.5)
    queries = turned(queries).astype(bf16)
    start_row = start_ref[query_block]

    def score_step(key_block, bests, with_mask):
        scores = dot(key_stack[key_block], queries)
        offsets = key_offsets(key_block, query_block, block)
        allowed = allowed_pairs(key_block, query_block, start_row, block) if with_mask else None
        result = []
        for number in range(heads):
            rows = head_rows(number, block)
            part = scores[rows] + slope_ref[number] * offsets
            if with_mask:
                part = jnp.where(allowed, part, masked)
            score_ref[key_block, rows, :] = part
            result.append(jnp.maximum(bests[number], eights(part, jnp.max)))
        return tuple(result)

    low, mid = low_ref[query_block], mid_ref[query_block]
    bests = tuple(jnp.full((8, block), masked, f32) for _ in range(heads))
    bests = lax.fori_loop(low, mid, functools.partial(score_step, with_mask=True), bests)
    bests = lax.fori_loop(mid, query_block, functools.partial(score_step, with_mask=False), bests)
    bests = score_step(query_block, bests, True)
    bests = [jnp.max(best, axis=0, keepdims=True) for best in bests]

    def value_step(key_block, state):
        result = []
        for number in range(heads):
            total, gathered = state[2 * number : 2 * number + 2]
            weights = jnp.exp(score_ref[key_block, head_rows(number, block), :] - bests[number])
            value_rows = values_turned[key_block, head_rows(number, head_width), :]
            result += [
                total + eights(weights, jnp.sum),
                gathered + dot(value_rows, weights.astype(bf16)),
            ]
        return tuple(result)

    state = ()
    for number in range(heads):
        state += (jnp.zeros((8, block), f32), jnp.zeros((head_width, block), f32))
    state = lax.fori_loop(low, query_block + 1, value_step, state)
    columns = []
    for number in range(heads):
        total = jnp.sum(state[2 * number], axis=0, keepdims=True)
        columns.append(state[2 * number + 1] / total)
        log_ref[0, number : number + 1, :] = bests[number] + jnp.log(total)
    out_ref[...] = jnp.transpose(jnp.concatenate(columns, axis=0)).astype(bf16)


def backward_kernel(heads, block, first_head, merge, *refs):
    full_ref, high_ref, slope_ref, start_ref, log_ref, qkv_ref, grad_ref, out_ref = refs[:8]
    earlier_ref = refs[8] if merge else None
    result_ref = refs[9 if merge else 8]
    (
        queries_turned,
        grads_turned,
        keys_turned,
        query_stack,
        grad_stack,
        key_stack,
        value_stack,
        delta_rows,
        query_grads,
    ) = refs[10 if merge else 9 :]
    tokens, all_width = grad_ref.shape
    head_width = all_width // log_ref.shape[1]
    width = heads * head_width
    scale = head_width ** (-0.5)
    blocks = tokens // block
    key_block = pl.program_id(0)
    lanes = lane_masks(block, width, heads)

    def columns(kind):
        start = kind * all_width + first_head * head_width
        return slice(start, start + width)

    def target(kind):
        start = (kind * all_width + first_head * head_width) if merge else kind * width
        return slice(start, start + width)

    @pl.when(key_block == 0)
    def _():
        for number in range(blocks):
            rows = slice(number * block, (number + 1) * block)
            queries = qkv_ref[rows, columns(0)]
            queries_turned[number] = turned(queries.astype(f32) * scale).astype(bf16)
            query_stack[number] = head_stack(queries, lanes)
            keys_turned[number] = turned(qkv_ref[rows, columns(1)]).astype(bf16)
            grads = grad_ref[rows, columns(0)]
            grad_stack[number] = head_stack(grads, lanes)
            grads = grads.astype(f32)
            grads_turned[number] = turned(grads).astype(bf16)
            product = turned(grads * out_ref[rows, columns(0)].astype(f32))
            for head in range(heads):
                delta_rows[number, head : head + 1, :] = jnp.sum(
                    product[head_rows(head, head_width)], axis=0, keepdims=True
                )
            query_grads[number] = jnp.zeros((width, block), f32)

    key_row = pl.multiple_of(key_block * block, block)
    key_stack[...] = head_stack(qkv_ref[pl.ds(key_row, block), columns(1)], lanes)
    value_stack[...] = head_stack(qkv_ref[pl.ds(key_row, block), columns(2)], lanes)

    def step(query_block, state, with_mask):
        key_total, value_total = state
        scores = dot(key_stack[...], queries_turned[query_block])
        grad_weights = dot(value_stack[...], grads_turned[query_block])
        offsets = key_offsets(key_block, query_block, block)
        if with_mask:
            allowed = allowed_pairs(key_block, query_block, start_ref[query_block], block)
        weight_list, grad_list = [], []
        for number in range(heads):
            rows = head_rows(number, block)
            head = first_head + number
            part = scores[rows] + slope_ref[head] * offsets
            part = part - log_ref[query_block, head : head + 1, :]
            if with_mask:
                part = jnp.where(allowed, part, masked)
            probabilities = jnp.exp(part)
            delta = delta_rows[query_block, number : number + 1, :]
            grad_scores = (probabilities * (grad_weights[rows] - delta)).astype(bf16)
            weight_list.append(probabilities.astype(bf16))
            grad_list.append(grad_scores)
            rows = head_rows(number, head_width)
            query_grads[query_block, rows, :] += dot(keys_turned[key_block, rows, :], grad_scores)
        weight_row = jnp.concatenate(weight_list, axis=1)
        grad_row = jnp.concatenate(grad_list, axis=1)
        return (
            key_total + dot(grad_row, query_stack[query_block]),
            value_total + dot(weight_row, grad_stack[query_block]),
        )

    state = (jnp.zeros((block, width), f32), jnp.zeros((block, width), f32))
    state = step(key_block, state, True)
    full, high = full_ref[key_block], high_ref[key_block]
    state = lax.fori_loop(key_block + 1, full, functools.partial(step, with_mask=False), state)
    state = lax.fori_loop(full, high, functools.partial(step, with_mask=True), state)
    result_ref[pl.ds(key_row, block), target(1)] = (state[0] * scale).astype(bf16)
    result_ref[pl.ds(key_row, block), target(2)] = state[1].astype(bf16)
    if merge:
        other = first_head * head_width
        for kind in range(3):
            result_ref[pl.ds(key_row, block), kind * all_width : kind * all_width + other] = earlier_ref[
                pl.ds(key_row, block), kind * other : (kind + 1) * other
            ]

    @pl.when(key_block == blocks - 1)
    def _():
        for number in range(blocks):
            rows = slice(number * block, (number + 1) * block)
            result_ref[rows, target(0)] = jnp.transpose(query_grads[number] * scale).astype(bf16)


def block_plan(lengths, tokens, block):
    ends = jnp.cumsum(lengths)
    positions = jnp.arange(tokens, dtype=jnp.int32)
    passed = positions[:, None] >= ends[None, :]
    starts = jnp.max(jnp.where(passed, ends[None, :], 0), axis=1).astype(jnp.int32)
    finish = jnp.min(jnp.where(passed, tokens, ends[None, :]), axis=1).astype(jnp.int32)
    blocks = tokens // block
    number = jnp.arange(blocks, dtype=jnp.int32)
    first_start = starts[::block]
    last_start = starts[block - 1 :: block]
    low = first_start // block
    mid = jnp.clip((last_start + block - 1) // block, low, number)
    high = (finish[block - 1 :: block] - 1) // block + 1
    full = jnp.clip(finish[::block] // block, number + 1, high)
    return (starts.reshape(blocks, 1, block), low, mid, full, high)


def scalar_spec():
    return pl.BlockSpec(memory_space=pltpu.SMEM)


def whole_spec(shape):
    return pl.BlockSpec(shape, lambda step: (0,) * len(shape), pipeline_mode=pl.Buffered(1))


def attend_forward(qkv, plan, slopes, heads, block):
    tokens, triple = qkv.shape
    width = triple // 3
    blocks = tokens // block
    starts, low, mid, full, high = plan
    return pl.pallas_call(
        functools.partial(forward_kernel, heads, block),
        grid=(blocks,),
        in_specs=[
            scalar_spec(),
            scalar_spec(),
            scalar_spec(),
            whole_spec((blocks, 1, block)),
            whole_spec((tokens, triple)),
        ],
        out_specs=[
            pl.BlockSpec((block, width), lambda step: (step, 0)),
            pl.BlockSpec((1, heads, block), lambda step: (step, 0, 0)),
        ],
        out_shape=[
            jax.ShapeDtypeStruct((tokens, width), bf16),
            jax.ShapeDtypeStruct((blocks, heads, block), f32),
        ],
        scratch_shapes=[
            pltpu.VMEM((blocks, width, block), bf16),
            pltpu.VMEM((blocks, heads * block, width), bf16),
            pltpu.VMEM((blocks, heads * block, block), f32),
        ],
        compiler_params=pltpu.CompilerParams(
            dimension_semantics=("arbitrary",), vmem_limit_bytes=24 * 1024 * 1024
        ),
        cost_estimate=pl.CostEstimate(
            flops=3 * tokens * tokens * 256 * heads,
            bytes_accessed=10 * tokens * width,
            transcendentals=tokens * tokens * heads // 2,
        ),
        name="attend_forward",
    )(low, mid, slopes, starts, qkv)


def attend_backward(qkv, grads, outputs, logs, plan, slopes, heads, block, first_head, earlier):
    tokens, triple = qkv.shape
    all_width = triple // 3
    all_heads = logs.shape[1]
    width = all_width // all_heads * heads
    blocks = tokens // block
    starts, low, mid, full, high = plan
    merge = earlier is not None
    result_width = triple if merge else 3 * width
    operands = [full, high, slopes, starts, logs, qkv, grads, outputs]
    specs = [scalar_spec() for _ in range(3)] + [whole_spec(entry.shape) for entry in operands[3:]]
    if merge:
        operands.append(earlier)
        specs.append(whole_spec(earlier.shape))
    return pl.pallas_call(
        functools.partial(backward_kernel, heads, block, first_head, merge),
        grid=(blocks,),
        in_specs=specs,
        out_specs=pl.BlockSpec((tokens, result_width), lambda step: (0, 0)),
        out_shape=jax.ShapeDtypeStruct((tokens, result_width), bf16),
        scratch_shapes=[
            pltpu.VMEM((blocks, width, block), bf16),
            pltpu.VMEM((blocks, width, block), bf16),
            pltpu.VMEM((blocks, width, block), bf16),
            pltpu.VMEM((blocks, heads * block, width), bf16),
            pltpu.VMEM((blocks, heads * block, width), bf16),
            pltpu.VMEM((heads * block, width), bf16),
            pltpu.VMEM((heads * block, width), bf16),
            pltpu.VMEM((blocks, heads, block), f32),
            pltpu.VMEM((blocks, width, block), f32),
        ],
        compiler_params=pltpu.CompilerParams(
            dimension_semantics=("arbitrary",), vmem_limit_bytes=24 * 1024 * 1024
        ),
        cost_estimate=pl.CostEstimate(
            flops=8 * tokens * tokens * 256 * heads,
            bytes_accessed=20 * tokens * width,
            transcendentals=tokens * tokens * heads // 2,
        ),
        name="attend_backward",
    )(*operands)


def hidden_backward_kernel(own_ref, other_ref, weight_ref, slope_ref, result_ref, total_ref):
    rows = own_ref.shape[0]
    total = jnp.zeros(total_ref.shape, f32)
    for number, ref in enumerate((own_ref, other_ref)):
        part = slice(number * rows, (number + 1) * rows)
        grads = dot_right(ref[...], weight_ref[...]) * slope_ref[part, :].astype(f32)
        grads = grads.astype(bf16)
        result_ref[part, :] = grads
        total = total + jnp.sum(grads.astype(f32), axis=0, keepdims=True)
    total_ref[...] = total


def hidden_backward(weight, cot_own, cot_other, slopes):
    rows, width = cot_own.shape
    breadth = slopes.shape[1]
    tile = min(256, breadth)
    return pl.pallas_call(
        hidden_backward_kernel,
        grid=(breadth // tile,),
        in_specs=[
            whole_spec((rows, width)),
            whole_spec((rows, width)),
            pl.BlockSpec((tile, width), lambda step: (step, 0)),
            pl.BlockSpec((2 * rows, tile), lambda step: (0, step)),
        ],
        out_specs=[
            pl.BlockSpec((2 * rows, tile), lambda step: (0, step)),
            pl.BlockSpec((1, tile), lambda step: (0, step)),
        ],
        out_shape=[
            jax.ShapeDtypeStruct((2 * rows, breadth), bf16),
            jax.ShapeDtypeStruct((1, breadth), f32),
        ],
        compiler_params=pltpu.CompilerParams(
            dimension_semantics=("arbitrary",), vmem_limit_bytes=12 * 1024 * 1024
        ),
        cost_estimate=pl.CostEstimate(flops=1, bytes_accessed=1, transcendentals=0),
        name="hidden_backward",
    )(cot_own, cot_other, weight, slopes)


def up_backward_kernel(grads_ref, weight_ref, result_ref):
    result_ref[...] = dot_right(grads_ref[...], weight_ref[...]).astype(result_ref.dtype)


def up_backward(weight, grads, number, kind_of):
    rows, breadth = grads.shape[0] // 2, grads.shape[1]
    width = weight.shape[0]
    tile = width // 4
    return pl.pallas_call(
        up_backward_kernel,
        grid=(4,),
        in_specs=[
            pl.BlockSpec((rows, breadth), lambda step: (number, 0)),
            pl.BlockSpec((tile, breadth), lambda step: (step, 0)),
        ],
        out_specs=pl.BlockSpec((rows, tile), lambda step: (0, step)),
        out_shape=jax.ShapeDtypeStruct((rows, width), kind_of),
        compiler_params=pltpu.CompilerParams(
            dimension_semantics=("arbitrary",), vmem_limit_bytes=12 * 1024 * 1024
        ),
        cost_estimate=pl.CostEstimate(flops=1, bytes_accessed=1, transcendentals=0),
        name="up_backward",
    )(grads, weight)


def down_projection_kernel(hidden_ref, weight_ref, result_ref):
    result_ref[...] = dot(hidden_ref[...], weight_ref[...]).astype(result_ref.dtype)


def down_projection(hidden, weight):
    rows, breadth = hidden.shape
    width = weight.shape[1]
    tile = min(256, rows)
    return pl.pallas_call(
        down_projection_kernel,
        grid=(rows // tile,),
        in_specs=[
            pl.BlockSpec((tile, breadth), lambda step: (step, 0)),
            whole_spec((breadth, width)),
        ],
        out_specs=pl.BlockSpec((tile, width), lambda step: (step, 0)),
        out_shape=jax.ShapeDtypeStruct((rows, width), bf16),
        compiler_params=pltpu.CompilerParams(
            dimension_semantics=("arbitrary",), vmem_limit_bytes=14 * 1024 * 1024
        ),
        cost_estimate=pl.CostEstimate(flops=1, bytes_accessed=1, transcendentals=0),
        name="down_projection",
    )(hidden, weight)


def up_gradient_kernel(own_ref, other_ref, grads_ref, result_ref, act_turned):
    rows, width = own_ref.shape
    step = 256

    @pl.when(pl.program_id(0) == 0)
    def _():
        for number, ref in enumerate((own_ref, other_ref)):
            for row in range(0, rows, step):
                first = number * rows + row
                for column in range(0, width, step):
                    block = ref[row : row + step, column : column + step]
                    act_turned[column : column + step, first : first + step] = turned(block).astype(bf16)

    result_ref[...] = dot(act_turned[...], grads_ref[...]).astype(bf16)


def up_gradient(act_own, act_other, grads):
    rows, width = act_own.shape
    breadth = grads.shape[1]
    tile = min(512, breadth)
    return pl.pallas_call(
        up_gradient_kernel,
        grid=(breadth // tile,),
        in_specs=[
            whole_spec((rows, width)),
            whole_spec((rows, width)),
            pl.BlockSpec((2 * rows, tile), lambda step: (0, step)),
        ],
        out_specs=pl.BlockSpec((width, tile), lambda step: (0, step)),
        out_shape=jax.ShapeDtypeStruct((width, breadth), bf16),
        scratch_shapes=[pltpu.VMEM((width, 2 * rows), bf16)],
        compiler_params=pltpu.CompilerParams(
            dimension_semantics=("arbitrary",), vmem_limit_bytes=16 * 1024 * 1024
        ),
        cost_estimate=pl.CostEstimate(flops=1, bytes_accessed=1, transcendentals=0),
        name="up_gradient",
    )(act_own, act_other, grads)


def together(*values):
    return lax.optimization_barrier(tuple(values))


def ordered(own, other, bit, axis=0):
    first = jnp.where(bit == 0, own, other)
    second = jnp.where(bit == 0, other, own)
    return jnp.stack([first, second], axis=axis)


class Moves:
    def __init__(self):
        self.shards = lax.axis_size("shard")
        self.reps = lax.axis_size("rep")
        self.half = self.shards // 2
        self.chips = self.reps // 2
        self.shard = lax.axis_index("shard")
        self.rep = lax.axis_index("rep")
        self.core = self.rep & 1
        self.chip = self.rep >> 1
        self.side = lax.div(self.shard, self.half)
        self.member = lax.rem(self.shard, self.half) + self.core * self.half

    def core_swap(self, part):
        return lax.ppermute(part, "rep", [(r, r ^ 1) for r in range(self.reps)])

    def chip_swap(self, part, bits):
        return lax.ppermute(part, "rep", [(r, r ^ (2 * bits)) for r in range(self.reps)])

    def shard_swap(self, part, bits):
        return lax.ppermute(part, "shard", [(s, s ^ bits) for s in range(self.shards)])

    def shard_bit(self, bits):
        return lax.div(self.shard, bits) & 1

    def low_bits(self):
        bits, result = 1, []
        while bits < self.half:
            result.append(bits)
            bits *= 2
        return result

    def home_send(self, part):
        pairs = []
        for rep in range(self.reps):
            for shard in range(self.shards):
                if shard // self.half != rep % 2:
                    to_shard = (shard + self.half) % self.shards
                    pairs.append((rep * self.shards + shard, (rep ^ 1) * self.shards + to_shard))
        return lax.ppermute(part, ("rep", "shard"), pairs)

    def home_join(self, part, other):
        return jnp.where(self.side == self.core, part, other)

    def half_gather(self, part):
        stack = part[None]
        for bits in self.low_bits():
            own = stack
            stack = ordered(own, self.shard_swap(own, bits), self.shard_bit(bits))
            stack = stack.reshape((-1,) + part.shape)
        return stack

    def cores_gather(self, stack):
        stack = ordered(stack, self.core_swap(stack), self.core)
        return stack.reshape((-1,) + stack.shape[2:])

    def exchange_bit(self, stack, bit, swap):
        sources, targets = stack.shape[:2]
        stack = stack.reshape((sources, 2, targets // 2) + stack.shape[2:])
        own, other = pick(stack, bit, 1), swap(pick(stack, 1 - bit, 1))
        return ordered(own, other, bit, 1).reshape((2 * sources,) + own.shape[1:])

    def half_exchange(self, stack):
        stack = stack[None]
        for bits in reversed(self.low_bits()):
            swap = functools.partial(self.shard_swap, bits=bits)
            stack = self.exchange_bit(stack, self.shard_bit(bits), swap)
        return stack.reshape((self.half,) + stack.shape[2:])

    def cores_exchange(self, stack):
        return self.exchange_bit(stack[None], self.core, self.core_swap)

    def members_exchange(self, stack):
        for bits in reversed(self.low_bits()):
            swap = functools.partial(self.shard_swap, bits=bits)
            stack = self.exchange_bit(stack, self.shard_bit(bits), swap)
        return stack.reshape((self.shards,) + stack.shape[2:])

    def reduce_bit(self, stack, bit, swap):
        stack = stack.reshape((2, stack.shape[0] // 2) + stack.shape[1:])
        other = swap(pick(stack, 1 - bit).astype(bf16))
        return pick(stack, bit).astype(f32) + other.astype(f32)

    def spread_open(self, part):
        if self.chips == 4:
            return (self.chip_swap(part, 1), self.chip_swap(part, 2))
        held, bits = [part], 1
        while bits < self.chips:
            held = held + [self.chip_swap(piece, bits) for piece in held]
            bits *= 2
        return tuple(held[1:])

    def spread_close(self, state):
        if self.chips == 4:
            by_x, by_y = state
            cut, axis = by_x.shape[-2] // 2, by_x.ndim - 2
            far = [
                self.chip_swap(by_x[..., :cut, :], 2),
                self.chip_swap(by_y[..., cut:, :], 1),
            ]
            return (by_x, by_y, jnp.concatenate(far, axis=axis))
        return state

    def far_open(self, states):
        if self.chips != 4:
            return ()
        cut = states[0][0].shape[0] // 2
        return (
            self.chip_swap(jnp.concatenate([by_x[:cut] for by_x, _ in states], axis=0), 2),
            self.chip_swap(jnp.concatenate([by_y[cut:] for _, by_y in states], axis=0), 1),
        )

    def far_parts(self, states, far):
        if self.chips != 4:
            return [[(k + 1, 0, part) for k, part in enumerate(state)] for state in states]
        cut = states[0][0].shape[0] // 2
        result = []
        for number, (by_x, by_y) in enumerate(states):
            rows = slice(number * cut, (number + 1) * cut)
            result.append([(1, 0, by_x), (2, 0, by_y), (3, 0, far[0][rows]), (3, cut, far[1][rows])])
        return result

    def chips_gather(self, part, axis, state=None):
        shape = part.shape[:axis] + (self.chips,) + part.shape[axis:]
        stack = place(jnp.zeros(shape, part.dtype), part, self.chip, axis)
        others = self.spread_close(self.spread_open(part) if state is None else state)
        for number, piece in enumerate(others):
            stack = place(stack, piece, self.chip ^ (number + 1), axis)
        return stack

    def reduce_open(self, stack, axis):
        return self.reduce_start(self.reduce_cut(stack, axis), axis)

    def reduce_cut(self, stack, axis):
        if self.chips != 4:
            return (stack,)
        shape = stack.shape[:axis] + (2, 2) + stack.shape[axis + 1 :]
        stack = stack.reshape(shape)
        bit_x, bit_y = self.chip & 1, self.chip >> 1
        cut = shape[0] // 2
        first, second = stack[:cut], stack[cut:]
        return (
            pick(first, bit_x, axis + 1),
            pick(second, bit_y, axis),
            pick(first, 1 - bit_x, axis + 1),
            pick(second, 1 - bit_y, axis),
        )

    def reduce_start(self, parts, axis):
        if self.chips == 4:
            first, second, send_first, send_second = parts
            return (first, second, self.chip_swap(send_first, 1), self.chip_swap(send_second, 2))
        (stack,) = parts
        count = self.chips
        stack = stack.astype(f32)
        while count > 1:
            count //= 2
            shape = stack.shape[:axis] + (2, count) + stack.shape[axis + 1 :]
            stack = stack.reshape(shape)
            bit = lax.div(self.chip, count) & 1
            got = self.chip_swap(pick(stack, 1 - bit, axis).astype(bf16), count)
            stack = pick(stack, bit, axis) + got.astype(f32)
        return (pick(stack, 0, axis).astype(bf16),)

    def reduce_add(self, state):
        if self.chips != 4:
            return state
        first, second, got_first, got_second = state
        first = (first.astype(f32) + got_first.astype(f32)).astype(bf16)
        second = (second.astype(f32) + got_second.astype(f32)).astype(bf16)
        return (first, second)

    def reduce_send(self, state, axis):
        if self.chips != 4:
            return state
        first, second = state
        bit_x, bit_y = self.chip & 1, self.chip >> 1
        got_first = self.chip_swap(pick(first, 1 - bit_y, axis), 2)
        got_second = self.chip_swap(pick(second, 1 - bit_x, axis), 1)
        return (pick(first, bit_y, axis), pick(second, bit_x, axis), got_first, got_second)

    def reduce_final(self, state):
        if self.chips != 4:
            return state[0]
        first, second, got_first, got_second = state
        first = first.astype(f32) + got_first.astype(f32)
        second = second.astype(f32) + got_second.astype(f32)
        return jnp.concatenate([first, second], axis=0).astype(bf16)

    def reduce_close(self, state, axis):
        return self.reduce_final(self.reduce_send(state, axis))

    def core_pair(self, part):
        other = self.core_swap(part)
        first = jnp.where(self.core == 0, part, other)
        second = jnp.where(self.core == 0, other, part)
        return first, second

    def sum_reps(self, vector):
        bits = 1
        while bits < self.reps:
            vector = vector + lax.ppermute(vector, "rep", [(r, r ^ bits) for r in range(self.reps)])
            bits *= 2
        return vector

    def sum_shards(self, vector):
        bits = 1
        while bits < self.shards:
            vector = vector + self.shard_swap(vector, bits)
            bits *= 2
        return vector


def stats_kernel(decay_rate, gradient_ref, old_ref, rows_ref, lane_rows_ref, sums_ref, total_ref, partial):
    step = pl.program_id(0)
    rows, columns = gradient_ref.shape

    @pl.when(step == 0)
    def _():
        partial[...] = jnp.zeros_like(partial)
        total_ref[...] = jnp.zeros_like(total_ref)

    gradient = gradient_ref[...].astype(f32)
    square = gradient * gradient
    row_mean = jnp.sum(square, axis=1, keepdims=True) / columns
    old = jnp.transpose(jnp.broadcast_to(old_ref[...], (128, rows)))[:, 0:1]
    rows_new = decay_rate * old + (1.0 - decay_rate) * (row_mean + eps_second)
    rows_ref[...] = rows_new
    lane_rows_ref[...] = jnp.transpose(jnp.broadcast_to(rows_new, (rows, 128)))[0:1, :]
    total_ref[...] += jnp.broadcast_to(jnp.sum(rows_new, axis=0, keepdims=True), (1, 128))
    partial[0:8, :] += eights(square, jnp.sum)
    partial[8:16, :] += eights(square * (1.0 / rows_new), jnp.sum)

    @pl.when(step == pl.num_programs(0) - 1)
    def _():
        sums_ref[0:1, :] = jnp.sum(partial[0:8, :], axis=0, keepdims=True)
        sums_ref[1:2, :] = jnp.sum(partial[8:16, :], axis=0, keepdims=True)


def factor_stats(gradient, rows_old, decay_rate):
    height, breadth = gradient.shape
    rows = min(256 if breadth <= 1024 else 128, height)
    return pl.pallas_call(
        functools.partial(stats_kernel, decay_rate),
        grid=(height // rows,),
        in_specs=[
            pl.BlockSpec((rows, breadth), lambda step: (step, 0)),
            pl.BlockSpec((1, rows), lambda step: (0, step)),
        ],
        out_specs=[
            pl.BlockSpec((rows, 1), lambda step: (step, 0)),
            pl.BlockSpec((1, rows), lambda step: (0, step)),
            pl.BlockSpec((2, breadth), lambda step: (0, 0)),
            pl.BlockSpec((1, 128), lambda step: (0, 0)),
        ],
        out_shape=[
            jax.ShapeDtypeStruct((height, 1), f32),
            jax.ShapeDtypeStruct((1, height), f32),
            jax.ShapeDtypeStruct((2, breadth), f32),
            jax.ShapeDtypeStruct((1, 128), f32),
        ],
        scratch_shapes=[pltpu.VMEM((16, breadth), f32)],
        compiler_params=pltpu.CompilerParams(
            dimension_semantics=("arbitrary",), vmem_limit_bytes=12 * 1024 * 1024
        ),
        name="factor_stats",
    )(gradient, rows_old)


def apply_kernel(
    decay_rate,
    height,
    gradient_ref,
    weight_ref,
    rows_ref,
    sums_ref,
    scalar_ref,
    old_ref,
    gradient_out,
    weight_out,
    copy_out,
    cols_out,
    rms_out,
    col_factor,
):
    columns = gradient_ref.shape[1]

    @pl.when(pl.program_id(0) == 0)
    def _():
        cols_new = decay_rate * old_ref[...] + (1.0 - decay_rate) * (
            sums_ref[0:1, :] / height + eps_second
        )
        row_mean = scalar_ref[0:1, 0:1] / height
        weight_mean = scalar_ref[1:2, 0:1] / (height * columns)
        scaled = jnp.sum(sums_ref[1:2, :] / cols_new, axis=1, keepdims=True)
        rms_update = jnp.sqrt(row_mean / (height * columns) * scaled)
        factor = rate_step * jnp.sqrt(weight_mean) * jnp.sqrt(row_mean)
        factor = factor / jnp.maximum(1.0, rms_update / clip_level)
        col_factor[...] = factor * lax.rsqrt(cols_new)
        cols_out[...] = cols_new
        rms_out[...] = jnp.broadcast_to(rms_update, (1, 128))

    gradient = gradient_ref[...].astype(f32)
    new_weight = weight_ref[...] - gradient * lax.rsqrt(rows_ref[...]) * col_factor[...]
    gradient_out[...] = gradient
    weight_out[...] = new_weight
    copy_out[...] = new_weight.astype(bf16)


def factor_apply(gradient, weight, rows_new, sums, scalars, cols_old, height, decay_rate):
    own_height, breadth = gradient.shape
    rows = min(256 if breadth <= 1024 else 64, own_height)

    def rows_spec():
        return pl.BlockSpec((rows, breadth), lambda step: (step, 0))

    def row_spec(count, wide):
        return pl.BlockSpec((count, wide), lambda step: (0, 0))

    return pl.pallas_call(
        functools.partial(apply_kernel, decay_rate, height),
        grid=(own_height // rows,),
        in_specs=[
            rows_spec(),
            rows_spec(),
            pl.BlockSpec((rows, 1), lambda step: (step, 0)),
            row_spec(2, breadth),
            row_spec(2, 128),
            row_spec(1, breadth),
        ],
        out_specs=[rows_spec(), rows_spec(), rows_spec(), row_spec(1, breadth), row_spec(1, 128)],
        out_shape=[
            jax.ShapeDtypeStruct((own_height, breadth), f32),
            jax.ShapeDtypeStruct((own_height, breadth), f32),
            jax.ShapeDtypeStruct((own_height, breadth), bf16),
            jax.ShapeDtypeStruct((1, breadth), f32),
            jax.ShapeDtypeStruct((1, 128), f32),
        ],
        scratch_shapes=[pltpu.VMEM((1, breadth), f32)],
        compiler_params=pltpu.CompilerParams(
            dimension_semantics=("arbitrary",), vmem_limit_bytes=14 * 1024 * 1024
        ),
        name="factor_apply",
    )(gradient, weight, rows_new, sums, scalars, cols_old)


def summed(moves, entries):
    total = moves.sum_shards(jnp.concatenate(entries, axis=1))
    result, offset = [], 0
    for entry in entries:
        result.append(total[:, offset : offset + entry.shape[1]])
        offset += entry.shape[1]
    return result


def on_device(
    tokens,
    cotangent,
    seq_lengths,
    qkv_weight,
    out_weight,
    up_weight,
    down_weight,
    vectors,
    row_state,
    down_rows,
    col_state,
    vector_state,
):
    moves = Moves()
    shards, half, chips, core = moves.shards, moves.half, moves.chips, moves.core
    row_count, width = tokens.shape
    hidden_width = up_weight.shape[1]
    group_rows = row_count * shards
    heads = HEADS // shards
    head_width = width // HEADS
    span = heads * head_width
    member = moves.member
    decay_rate = 1.0 - STEP ** (-0.8)
    head_number = (member * heads + jnp.arange(heads, dtype=jnp.int32)).astype(f32)
    slopes = jnp.exp2(-8.0 * (head_number + 1.0) / HEADS)

    gain_one = vectors[0:width]
    shift_one = vectors[width : 2 * width]
    bias_query = vectors[2 * width : 3 * width]
    bias_value = vectors[3 * width : 4 * width]
    bias_out = vectors[4 * width : 5 * width]
    gain_two = vectors[5 * width : 6 * width]
    shift_two = vectors[6 * width : 7 * width]
    bias_up = vectors[7 * width : 7 * width + hidden_width]
    bias_down = vectors[7 * width + hidden_width :]

    other_tokens = moves.home_send(tokens)
    other_lengths = moves.core_swap(seq_lengths)
    lengths = jnp.where(moves.side == core, seq_lengths, other_lengths)[0]
    plan = block_plan(lengths, group_rows, BLOCK)
    rows_z = width // shards
    rows_piece = rows_z // chips
    my_rows = cut_rows(qkv_weight, moves.chip * rows_piece, rows_piece)
    my_rows = my_rows.astype(bf16)
    my_blocks = []
    for number in range(half):
        kinds = []
        for kind in range(3):
            first = kind * width + number * span
            second = first + half * span
            kinds.append(
                jnp.where(
                    core == 0, my_rows[:, first : first + span], my_rows[:, second : second + span]
                )
            )
        my_blocks.append(jnp.concatenate(kinds, axis=1))
    qkv_part = moves.half_exchange(jnp.stack(my_blocks))
    half_cols = hidden_width // (2 * shards)
    up_wide = shards * half_cols
    out_wide = width // 2
    down_piece = half_cols // chips

    def core_half(values):
        parts = []
        for number in range(shards):
            start = 2 * number * half_cols
            first = values[..., start : start + half_cols]
            second = values[..., start + half_cols : start + 2 * half_cols]
            parts.append(jnp.where(core == 0, first, second))
        return jnp.concatenate(parts, axis=-1)

    up_own = core_half(up_weight).astype(bf16).reshape(chips, rows_piece, up_wide)
    out_own = jnp.where(core == 0, out_weight[:, :out_wide], out_weight[:, out_wide:]).astype(bf16)
    out_own = out_own.reshape(chips, rows_piece, out_wide)
    down_own = cut_rows(down_weight, core * half_cols, half_cols).astype(bf16)
    fold = down_piece // rows_piece
    down_own = down_own.reshape(chips, fold, rows_piece, width)
    my_down = pick(down_own, moves.chip)
    weight_piece = jnp.concatenate(
        [pick(up_own, moves.chip), pick(out_own, moves.chip)] + [my_down[k] for k in range(fold)],
        axis=1,
    )
    near_pieces, bits = [weight_piece], 1
    while bits < half:
        near_pieces = near_pieces + [moves.shard_swap(piece, bits) for piece in near_pieces]
        bits *= 2
    near_pieces = near_pieces[1:]
    weights = [qkv_weight, out_weight, up_weight, down_weight]
    weight_sums = [jnp.sum(weight * weight) for weight in weights]
    other_tokens, qkv_part, near_pieces, weight_piece, plan, weight_sums = together(
        other_tokens, qkv_part, near_pieces, weight_piece, plan, weight_sums
    )
    home_tokens = moves.home_join(tokens, other_tokens)
    far_piece = moves.shard_swap(weight_piece, half)
    near_open = [moves.spread_open(piece) for piece in near_pieces]
    qkv_far = moves.shard_swap(qkv_part, half)
    qkv_far, near_open = together(qkv_far, near_open)
    qkv_part = ordered(qkv_part, qkv_far, moves.side).reshape(shards, rows_piece, 3 * span)
    qkv_cols = moves.chips_gather(qkv_part, 1).reshape(width, 3 * span)
    inputs = home_tokens.astype(f32)
    normed_one, inv_std_one = norm_parts(inputs)
    act_one = (normed_one * gain_one + shift_one).astype(bf16)
    act_half = moves.half_gather(act_one)

    act_half, qkv_cols, far_piece, cotangent = together(
        act_half, qkv_cols, far_piece, cotangent
    )
    other_cot = moves.home_send(cotangent)
    act_all = moves.cores_gather(act_half).reshape(group_rows, width)
    far_open = moves.spread_open(far_piece)
    far_pieces, bits = [far_piece], 1
    while bits < half:
        far_pieces = far_pieces + [moves.shard_swap(piece, bits) for piece in far_pieces]
        bits *= 2
    far_pieces = far_pieces[1:]

    bias_q_part = cut_rows(bias_query, member * span, span)
    bias_v_part = cut_rows(bias_value, member * span, span)
    qkv_bias = jnp.concatenate([bias_q_part, jnp.zeros_like(bias_q_part), bias_v_part])
    qkv_rows = (dot(act_all, qkv_cols) + qkv_bias).astype(bf16)
    attended_cols, logs = attend_forward(qkv_rows, plan, slopes, heads, BLOCK)
    attended_cols, far_open, far_pieces, other_cot = together(
        attended_cols, far_open, far_pieces, other_cot
    )
    attended_parts = moves.cores_exchange(attended_cols.reshape(shards, row_count, span))
    attended_parts = moves.members_exchange(attended_parts)
    first_states = near_open + [far_open]
    first_far = moves.far_open(first_states)
    last_states = [moves.spread_open(piece) for piece in far_pieces]
    attended_parts, first_far, last_states, other_cot = together(
        attended_parts, first_far, last_states, other_cot
    )
    home_cot = moves.home_join(cotangent, other_cot)
    last_far = moves.far_open(last_states)
    attended = jnp.concatenate([attended_parts[k] for k in range(shards)], axis=1)

    up_all = place(jnp.zeros((shards, chips, rows_piece, up_wide), bf16), up_own, moves.shard)
    out_all = place(jnp.zeros((shards, chips, rows_piece, out_wide), bf16), out_own, moves.shard)
    down_all = place(jnp.zeros((shards, chips, fold, rows_piece, width), bf16), down_own, moves.shard)
    pieces = near_pieces + [far_piece] + far_pieces
    parts_of = moves.far_parts(first_states, first_far) + moves.far_parts(last_states, last_far)
    for number, (piece, parts) in enumerate(zip(pieces, parts_of)):
        plane = moves.shard ^ (number + 1)
        for far, row, rows in [(0, 0, piece)] + parts:
            chip = moves.chip ^ far
            up_all = lax.dynamic_update_slice(
                up_all, rows[None, None, :, :up_wide], (plane, chip, row, 0), allow_negative_indices=False
            )
            out_all = lax.dynamic_update_slice(
                out_all, rows[None, None, :, up_wide : up_wide + out_wide], (plane, chip, row, 0), allow_negative_indices=False
            )
            start = up_wide + out_wide
            folds = [rows[:, start + k * width : start + (k + 1) * width] for k in range(fold)]
            down_all = lax.dynamic_update_slice(
                down_all, jnp.stack(folds)[None, None], (plane, chip, 0, row, 0), allow_negative_indices=False
            )
    up_half = up_all.reshape(width, up_wide)
    down_half = down_all.reshape(up_wide, width)
    out_first, out_second = moves.core_pair(out_all.reshape(width, out_wide))
    out_low = jnp.concatenate([out_first, out_second], axis=1)
    residual = inputs + dot(attended, out_low) + bias_out
    normed_two, inv_std_two = norm_parts(residual)
    act_two = (normed_two * gain_two + shift_two).astype(bf16)

    act_two_other, attended_other, cot_other = together(
        moves.core_swap(act_two), moves.core_swap(attended), moves.core_swap(home_cot)
    )
    cot_pair = jnp.concatenate([home_cot, cot_other], axis=0)
    act_two_pair = jnp.concatenate([act_two, act_two_other], axis=0)
    attended_pair = jnp.concatenate([attended, attended_other], axis=0)
    bias_up_half = core_half(bias_up)
    up_pair = dot(act_two_pair, up_half) + bias_up_half
    hidden_pair = gelu_value(up_pair).astype(bf16)
    slope_pair = gelu_slope(up_pair).astype(bf16)
    down_terms = dot_rows(hidden_pair, cot_pair).astype(bf16)
    down_state = moves.reduce_cut(down_terms.reshape(shards, chips, down_piece, width), 1)
    slope_pair, down_state = together(slope_pair, down_state)
    down_state = moves.reduce_start(down_state, 1)
    grad_y = home_cot.astype(f32)
    grad_bias_down = jnp.sum(grad_y, axis=0)
    grad_up_pair, grad_bias_up = hidden_backward(down_half, home_cot, cot_other, slope_pair)
    grad_bias_up = grad_bias_up.reshape(-1)
    back_other = moves.core_swap(up_backward(up_half, grad_up_pair, 1, bf16))
    up_terms = up_gradient(act_two, act_two_other, grad_up_pair)
    down_pair = down_projection(hidden_pair, down_half)
    back_other, down_pair, up_terms, down_state = together(
        back_other, down_pair, up_terms, down_state
    )
    up_cut = moves.reduce_cut(up_terms.reshape(shards, chips, rows_piece, up_wide), 1)
    down_sums = moves.reduce_add(down_state)
    grad_act_two = up_backward(up_half, grad_up_pair, 0, f32) + back_other.astype(f32)
    grad_gain_two = jnp.sum(grad_act_two * normed_two, axis=0)
    grad_shift_two = jnp.sum(grad_act_two, axis=0)
    grad_residual = grad_y + norm_back(grad_act_two, normed_two, inv_std_two, gain_two)
    grad_attn = grad_residual.astype(bf16)
    grad_bias_out = jnp.sum(grad_attn, axis=0, dtype=f32)
    to_members = jnp.stack(
        [
            dot_right(grad_attn, out_low[k * span : (k + 1) * span]).astype(bf16)
            for k in range(shards)
        ]
    )
    attn_halves = [grad_attn[:, :out_wide], grad_attn[:, out_wide:]]
    attn_own = jnp.where(core == 0, attn_halves[0], attn_halves[1])
    attn_other = jnp.where(core == 0, attn_halves[1], attn_halves[0])
    down_other = moves.core_swap(down_pair[row_count:])
    grad_heads, attn_other, up_cut, down_sums, down_other = together(
        moves.cores_exchange(to_members), moves.core_swap(attn_other), up_cut, down_sums, down_other
    )
    attn_pair = jnp.concatenate([attn_own, attn_other], axis=0)
    grad_heads = moves.members_exchange(grad_heads).reshape(group_rows, span)
    up_state = moves.reduce_start(up_cut, 1)
    down_mid = moves.reduce_close(down_sums, 1)
    block_out = residual + down_pair[:row_count].astype(f32) + down_other.astype(f32) + bias_down
    block_out = block_out.astype(bf16)

    out_terms = dot_rows(attended_pair, attn_pair).astype(bf16)
    def shards_halve(piece, bits):
        piece = piece.reshape((piece.shape[0] // 2, 2) + piece.shape[1:])
        bit = moves.shard_bit(bits)
        return pick(piece, bit, 1), moves.shard_swap(pick(piece, 1 - bit, 1), bits)

    def halved(state):
        own, other = state
        return (own.astype(f32) + other.astype(f32)).astype(bf16)

    def shards_sum(piece):
        rows = piece.shape[1]
        return lax.psum_scatter(
            piece.reshape(shards * rows, piece.shape[2]), "shard", scatter_dimension=0, tiled=True
        )

    grad_heads, down_mid, out_terms, block_out = together(
        grad_heads, down_mid, out_terms, block_out
    )
    block_other = moves.home_send(block_out)
    down_owned = shards_sum(down_mid)
    out_state = moves.reduce_open(out_terms.reshape(shards, chips, rows_piece, out_wide), 1)
    attend_args = (plan, slopes)
    parts = 2 if heads % 4 == 0 else 1
    part_heads = heads // parts
    grad_qkv = attend_backward(
        qkv_rows, grad_heads, attended_cols, logs, *attend_args, part_heads, BLOCK, 0, None
    )
    grad_qkv, up_state, out_state = together(grad_qkv, up_state, out_state)
    up_sums, out_sums = moves.reduce_add(up_state), moves.reduce_add(out_state)
    grad_qkv, up_sums, out_sums = together(grad_qkv, up_sums, out_sums)
    up_out_state = [
        jnp.concatenate([up_part, out_part], axis=-1) for up_part, out_part in zip(up_sums, out_sums)
    ]
    if parts == 2:
        grad_qkv = attend_backward(
            qkv_rows, grad_heads, attended_cols, logs, *attend_args, part_heads, BLOCK, part_heads, grad_qkv
        )
    grad_qkv, up_out_state, block_other, down_owned = together(
        grad_qkv, moves.reduce_send(up_out_state, 1), block_other, down_owned
    )
    block_out = moves.home_join(block_out, block_other)
    up_out_piece = moves.reduce_final(up_out_state)
    up_out_state = shards_halve(up_out_piece, 1)

    grad_bias_q_part = jnp.sum(grad_qkv[:, :span], axis=0, dtype=f32)
    grad_bias_v_part = jnp.sum(grad_qkv[:, 2 * span :], axis=0, dtype=f32)

    grad_halves = grad_qkv.reshape(2, half * row_count, 3 * span)
    sent = dot_right(pick(grad_halves, 1 - core), qkv_cols).astype(bf16)
    sent = moves.core_swap(sent)
    qkv_terms = dot_rows(act_all, grad_qkv).astype(bf16)
    qkv_terms = qkv_terms.reshape(shards, chips, rows_piece, 3 * span)
    qkv_state = moves.reduce_open(qkv_terms, 1)
    back = dot_right(pick(grad_halves, core), qkv_cols) + sent.astype(f32)
    qkv_state, back = together(qkv_state, back)

    back = back.reshape(half, row_count, width)
    low_bits = list(reversed(moves.low_bits()))
    for bits in low_bits[:-1]:
        back = moves.reduce_bit(
            back, moves.shard_bit(bits), functools.partial(moves.shard_swap, bits=bits)
        )
    back = back.reshape((2, -1) + back.shape[1:])
    back_bit = moves.shard_bit(low_bits[-1])
    back_other = moves.shard_swap(pick(back, 1 - back_bit).astype(bf16), low_bits[-1])
    qkv_state = moves.reduce_send(moves.reduce_add(qkv_state), 1)
    qkv_state, up_out_state = together(qkv_state, up_out_state)

    up_out_piece, bits = halved(up_out_state), 2
    while bits < half:
        up_out_piece = halved(shards_halve(up_out_piece, bits))
        bits *= 2
    up_out_state = shards_halve(up_out_piece, half)
    qkv_piece = moves.reduce_final(qkv_state)
    qkv_piece = qkv_piece.reshape((2, half) + qkv_piece.shape[1:])
    qkv_own = pick(qkv_piece, moves.side)
    qkv_other = moves.shard_swap(pick(qkv_piece, 1 - moves.side), half)
    back_other, qkv_other, up_out_state, down_owned = together(
        back_other, qkv_other, up_out_state, down_owned
    )

    up_out_owned = halved(up_out_state)[0]
    up_out_state = moves.spread_open(up_out_owned)
    qkv_piece = moves.half_exchange(halved((qkv_own, qkv_other)))
    down_state = moves.spread_open(down_owned)
    grad_act_one = pick(back, back_bit) + back_other.astype(f32)
    grad_act_one = grad_act_one.reshape(row_count, width)
    grad_gain_one = jnp.sum(grad_act_one * normed_one, axis=0)
    grad_shift_one = jnp.sum(grad_act_one, axis=0)
    grad_inputs = grad_residual + norm_back(grad_act_one, normed_one, inv_std_one, gain_one)
    grad_inputs, grad_gain_one, grad_shift_one, qkv_piece, down_state, up_out_state = together(
        grad_inputs.astype(bf16), grad_gain_one, grad_shift_one, qkv_piece, down_state, up_out_state
    )
    tokens_other = moves.home_send(grad_inputs)
    qkv_owned = moves.chips_gather(qkv_piece, 1)

    up_out_first, up_out_second = moves.core_pair(
        moves.chips_gather(up_out_owned, 0, tuple(up_out_state)).reshape(rows_z, up_wide + out_wide)
    )
    out_grad = jnp.concatenate([up_out_first[:, up_wide:], up_out_second[:, up_wide:]], axis=1)
    up_columns = []
    for number in range(shards):
        part = slice(number * half_cols, (number + 1) * half_cols)
        up_columns += [up_out_first[:, part], up_out_second[:, part]]
    up_grad = jnp.concatenate(up_columns, axis=1)
    down_first, down_second = moves.core_pair(
        moves.chips_gather(down_owned, 0, tuple(down_state)).reshape(half_cols, width)
    )
    down_grad = jnp.concatenate([down_first, down_second], axis=0)
    qkv_owned = qkv_owned.reshape(half, rows_z, 3 * span)
    qkv_other, tokens_other = together(moves.core_swap(qkv_owned), tokens_other)
    tokens_grad = moves.home_join(grad_inputs, tokens_other)
    qkv_first = jnp.where(core == 0, qkv_owned, qkv_other)
    qkv_second = jnp.where(core == 0, qkv_other, qkv_owned)
    qkv_columns = []
    for kind in range(3):
        for source in (qkv_first, qkv_second):
            for number in range(half):
                qkv_columns.append(source[number][:, kind * span : (kind + 1) * span])
    qkv_grad = jnp.concatenate(qkv_columns, axis=1)

    gradients = [qkv_grad, out_grad, up_grad, down_grad]
    heights = [width, width, width, hidden_width]
    rows_old = [row_state[k : k + 1] for k in range(3)] + [down_rows.reshape(1, -1)]
    stats = [
        factor_stats(gradient, old, decay_rate) for gradient, old in zip(gradients, rows_old)
    ]

    def to_sum(number):
        weight_sum = jnp.broadcast_to(weight_sums[number], (1, 128))
        return [stats[number][2], jnp.concatenate([stats[number][3], weight_sum], axis=0)]

    def spread_heads(part):
        return [jnp.where(member == number, part, 0.0) for number in range(shards)]

    bias_up_parts = []
    for number in range(shards):
        part = grad_bias_up[number * half_cols : (number + 1) * half_cols]
        bias_up_parts += [jnp.where(core == 0, part, 0.0), jnp.where(core == 1, part, 0.0)]
    vector_part = moves.sum_reps(
        jnp.concatenate(
            [grad_gain_one, grad_shift_one]
            + spread_heads(grad_bias_q_part)
            + spread_heads(grad_bias_v_part)
            + [grad_bias_out, grad_gain_two, grad_shift_two]
            + bias_up_parts
            + [grad_bias_down]
        )
    )
    vector_rows = vector_part.reshape(2, -1)
    all_sums = summed(moves, to_sum(0) + to_sum(1) + to_sum(2) + to_sum(3) + [vector_rows])
    sums = [all_sums[0:2], all_sums[2:4], all_sums[4:6], all_sums[6:8]]
    vector_grad = all_sums[8].reshape(-1)
    updates = []
    offset = 0
    for number in range(4):
        end_col = offset + gradients[number].shape[1]
        updates.append(
            factor_apply(
                gradients[number],
                weights[number],
                stats[number][0],
                sums[number][0],
                sums[number][1],
                col_state[offset:end_col].reshape(1, -1),
                heights[number],
                decay_rate,
            )
        )
        offset = end_col
    grads_out, new_weights, copies, new_cols, rms_rows = zip(*updates)
    rms_values = [rms[0, 0] for rms in rms_rows]

    vector_state_new = decay_rate * vector_state + (1.0 - decay_rate) * (
        vector_grad * vector_grad + eps_second
    )
    vector_step = vector_grad * lax.rsqrt(vector_state_new)
    vector_rms = jnp.sqrt(jnp.mean(vector_step * vector_step))
    vector_new = vectors - rate_step * jnp.sqrt(
        jnp.mean(vectors * vectors)
    ) * vector_step / jnp.maximum(1.0, vector_rms / clip_level)
    update_rms = jnp.stack(rms_values + [vector_rms])
    return (
        block_out,
        tokens_grad,
        *grads_out,
        vector_grad,
        *new_weights,
        vector_new,
        *copies,
        jnp.concatenate([stats[0][1], stats[1][1], stats[2][1]], axis=0),
        stats[3][1].reshape(-1),
        jnp.concatenate(new_cols, axis=1).reshape(-1),
        vector_state_new,
        update_rms,
    )


def solution(mesh):
    in_specs = (
        P(("rep", "shard"), None),
        P(("rep", "shard"), None),
        P("rep", None),
        P("shard", None),
        P("shard", None),
        P("shard", None),
        P("shard", None),
        P(),
        P(None, "shard"),
        P("shard"),
        P(),
        P(),
    )
    out_specs = (
        P(("rep", "shard"), None),
        P(("rep", "shard"), None),
        P("shard", None),
        P("shard", None),
        P("shard", None),
        P("shard", None),
        P(),
        P("shard", None),
        P("shard", None),
        P("shard", None),
        P("shard", None),
        P(),
        P("shard", None),
        P("shard", None),
        P("shard", None),
        P("shard", None),
        P(None, "shard"),
        P("shard"),
        P(),
        P(),
        P(),
    )
    return jax.shard_map(
        on_device, mesh=mesh, in_specs=in_specs, out_specs=out_specs, check_vma=False
    )
```

```python
import functools

import jax
import jax.numpy as jnp
from jax import lax
from jax.experimental import pallas as pl
from jax.experimental.pallas import tpu as pltpu
from jax.sharding import PartitionSpec as P

HEADS = 16
STEP = 10
BLOCK = 256


eps_norm = 1e-05
eps_second = 1e-30
rate_step = 0.5
clip_level = 1.0
masked = -1e30
gelu_root = (2.0 / 3.141592653589793) ** 0.5
gelu_cubic = 0.044715

f32 = jnp.float32
bf16 = jnp.bfloat16


def norm_parts(values):
    average = jnp.mean(values, axis=-1, keepdims=True)
    centred = values - average
    inv_std = lax.rsqrt(jnp.mean(centred * centred, axis=-1, keepdims=True) + eps_norm)
    return (centred * inv_std, inv_std)


def norm_back(grad_out, normed, inv_std, gain_vec):
    grad_normed = grad_out * gain_vec
    inner_mean = jnp.mean(grad_normed * normed, axis=-1, keepdims=True)
    centred = grad_normed - jnp.mean(grad_normed, axis=-1, keepdims=True)
    return (centred - normed * inner_mean) * inv_std


def gelu_value(pre_act):
    curve = jnp.tanh(gelu_root * (pre_act + gelu_cubic * pre_act * pre_act * pre_act))
    return 0.5 * pre_act * (1.0 + curve)


def gelu_slope(pre_act):
    square = pre_act * pre_act
    curve = jnp.tanh(gelu_root * (pre_act + gelu_cubic * square * pre_act))
    inner = gelu_root * (1.0 + 3.0 * gelu_cubic * square)
    return 0.5 * (1.0 + curve) + 0.5 * pre_act * (1.0 - curve * curve) * inner


def dot(left_side, right_side):
    return jnp.dot(left_side, right_side, preferred_element_type=f32)


def dot_right(left_side, right_side):
    return lax.dot_general(
        left_side, right_side, (((1,), (1,)), ((), ())), preferred_element_type=f32
    )


def dot_rows(left_side, right_side):
    return lax.dot_general(
        left_side, right_side, (((0,), (0,)), ((), ())), preferred_element_type=f32
    )


def pick(stack, index, axis=0):
    return lax.dynamic_index_in_dim(stack, index, axis, keepdims=False, allow_negative_indices=False)


def cut_rows(values, start, count):
    return lax.dynamic_slice_in_dim(values, start, count, 0, allow_negative_indices=False)


def place(stack, part, index, axis=0):
    return lax.dynamic_update_index_in_dim(stack, part, index, axis, allow_negative_indices=False)


def head_rows(number, head_width):
    return slice(number * head_width, (number + 1) * head_width)


def lane_masks(block_rows, width, heads):
    lanes = lax.broadcasted_iota(jnp.int32, (block_rows, width), 1)
    head_width = width // heads
    return [
        (lanes >= number * head_width) & (lanes < (number + 1) * head_width)
        for number in range(heads)
    ]


def allowed_pairs(key_block, query_block, start_row, block):
    key_pos = lax.broadcasted_iota(jnp.int32, (block, block), 0) + key_block * block
    query_pos = lax.broadcasted_iota(jnp.int32, (block, block), 1) + query_block * block
    return (key_pos <= query_pos) & (key_pos >= start_row)


def key_offsets(key_block, query_block, block):
    rows = lax.broadcasted_iota(jnp.int32, (block, 1), 0)
    return (rows + (key_block - query_block) * block).astype(f32)


def turned(values):
    return jnp.transpose(values.astype(f32))


def head_stack(values, lanes):
    zero = jnp.zeros(values.shape, values.dtype)
    return jnp.concatenate([jnp.where(lane, values, zero) for lane in lanes], axis=0)


def eights(values, combine):
    rows, columns = values.shape
    return combine(values.reshape(rows // 8, 8, columns), axis=0)


def forward_kernel(
    heads,
    block,
    low_ref,
    mid_ref,
    slope_ref,
    start_ref,
    qkv_ref,
    out_ref,
    log_ref,
    values_turned,
    key_stack,
    score_ref,
):
    tokens = qkv_ref.shape[0]
    width = qkv_ref.shape[1] // 3
    head_width = width // heads
    blocks = tokens // block
    query_block = pl.program_id(0)

    @pl.when(query_block == 0)
    def _():
        lanes = lane_masks(block, width, heads)
        for number in range(blocks):
            rows = slice(number * block, (number + 1) * block)
            values_turned[number] = turned(qkv_ref[rows, 2 * width :]).astype(bf16)
            key_stack[number] = head_stack(qkv_ref[rows, width : 2 * width], lanes)

    first_row = pl.multiple_of(query_block * block, block)
    queries = qkv_ref[pl.ds(first_row, block), :width].astype(f32) * head_width ** (-0.5)
    queries = turned(queries).astype(bf16)
    start_row = start_ref[query_block]

    def score_step(key_block, bests, with_mask):
        scores = dot(key_stack[key_block], queries)
        offsets = key_offsets(key_block, query_block, block)
        allowed = allowed_pairs(key_block, query_block, start_row, block) if with_mask else None
        result = []
        for number in range(heads):
            rows = head_rows(number, block)
            part = scores[rows] + slope_ref[number] * offsets
            if with_mask:
                part = jnp.where(allowed, part, masked)
            score_ref[key_block, rows, :] = part
            result.append(jnp.maximum(bests[number], eights(part, jnp.max)))
        return tuple(result)

    low, mid = low_ref[query_block], mid_ref[query_block]
    bests = tuple(jnp.full((8, block), masked, f32) for _ in range(heads))
    bests = lax.fori_loop(low, mid, functools.partial(score_step, with_mask=True), bests)
    bests = lax.fori_loop(mid, query_block, functools.partial(score_step, with_mask=False), bests)
    bests = score_step(query_block, bests, True)
    bests = [jnp.max(best, axis=0, keepdims=True) for best in bests]

    def value_step(key_block, state):
        result = []
        for number in range(heads):
            total, gathered = state[2 * number : 2 * number + 2]
            weights = jnp.exp(score_ref[key_block, head_rows(number, block), :] - bests[number])
            value_rows = values_turned[key_block, head_rows(number, head_width), :]
            result += [
                total + eights(weights, jnp.sum),
                gathered + dot(value_rows, weights.astype(bf16)),
            ]
        return tuple(result)

    state = ()
    for number in range(heads):
        state += (jnp.zeros((8, block), f32), jnp.zeros((head_width, block), f32))
    state = lax.fori_loop(low, query_block + 1, value_step, state)
    columns = []
    for number in range(heads):
        total = jnp.sum(state[2 * number], axis=0, keepdims=True)
        columns.append(state[2 * number + 1] / total)
        log_ref[0, number : number + 1, :] = bests[number] + jnp.log(total)
    out_ref[...] = jnp.transpose(jnp.concatenate(columns, axis=0)).astype(bf16)


def backward_kernel(heads, block, first_head, merge, *refs):
    full_ref, high_ref, slope_ref, start_ref, log_ref, qkv_ref, grad_ref, out_ref = refs[:8]
    earlier_ref = refs[8] if merge else None
    result_ref = refs[9 if merge else 8]
    (
        queries_turned,
        grads_turned,
        keys_turned,
        query_stack,
        grad_stack,
        key_stack,
        value_stack,
        delta_rows,
        query_grads,
    ) = refs[10 if merge else 9 :]
    tokens, all_width = grad_ref.shape
    head_width = all_width // log_ref.shape[1]
    width = heads * head_width
    scale = head_width ** (-0.5)
    blocks = tokens // block
    key_block = pl.program_id(0)
    lanes = lane_masks(block, width, heads)

    def columns(kind):
        start = kind * all_width + first_head * head_width
        return slice(start, start + width)

    def target(kind):
        start = (kind * all_width + first_head * head_width) if merge else kind * width
        return slice(start, start + width)

    @pl.when(key_block == 0)
    def _():
        for number in range(blocks):
            rows = slice(number * block, (number + 1) * block)
            queries = qkv_ref[rows, columns(0)]
            queries_turned[number] = turned(queries.astype(f32) * scale).astype(bf16)
            query_stack[number] = head_stack(queries, lanes)
            keys_turned[number] = turned(qkv_ref[rows, columns(1)]).astype(bf16)
            grads = grad_ref[rows, columns(0)]
            grad_stack[number] = head_stack(grads, lanes)
            grads = grads.astype(f32)
            grads_turned[number] = turned(grads).astype(bf16)
            product = turned(grads * out_ref[rows, columns(0)].astype(f32))
            for head in range(heads):
                delta_rows[number, head : head + 1, :] = jnp.sum(
                    product[head_rows(head, head_width)], axis=0, keepdims=True
                )
            query_grads[number] = jnp.zeros((width, block), f32)

    key_row = pl.multiple_of(key_block * block, block)
    key_stack[...] = head_stack(qkv_ref[pl.ds(key_row, block), columns(1)], lanes)
    value_stack[...] = head_stack(qkv_ref[pl.ds(key_row, block), columns(2)], lanes)

    def step(query_block, state, with_mask):
        key_total, value_total = state
        scores = dot(key_stack[...], queries_turned[query_block])
        grad_weights = dot(value_stack[...], grads_turned[query_block])
        offsets = key_offsets(key_block, query_block, block)
        if with_mask:
            allowed = allowed_pairs(key_block, query_block, start_ref[query_block], block)
        weight_list, grad_list = [], []
        for number in range(heads):
            rows = head_rows(number, block)
            head = first_head + number
            part = scores[rows] + slope_ref[head] * offsets
            part = part - log_ref[query_block, head : head + 1, :]
            if with_mask:
                part = jnp.where(allowed, part, masked)
            probabilities = jnp.exp(part)
            delta = delta_rows[query_block, number : number + 1, :]
            grad_scores = (probabilities * (grad_weights[rows] - delta)).astype(bf16)
            weight_list.append(probabilities.astype(bf16))
            grad_list.append(grad_scores)
            rows = head_rows(number, head_width)
            query_grads[query_block, rows, :] += dot(keys_turned[key_block, rows, :], grad_scores)
        weight_row = jnp.concatenate(weight_list, axis=1)
        grad_row = jnp.concatenate(grad_list, axis=1)
        return (
            key_total + dot(grad_row, query_stack[query_block]),
            value_total + dot(weight_row, grad_stack[query_block]),
        )

    state = (jnp.zeros((block, width), f32), jnp.zeros((block, width), f32))
    state = step(key_block, state, True)
    full, high = full_ref[key_block], high_ref[key_block]
    state = lax.fori_loop(key_block + 1, full, functools.partial(step, with_mask=False), state)
    state = lax.fori_loop(full, high, functools.partial(step, with_mask=True), state)
    result_ref[pl.ds(key_row, block), target(1)] = (state[0] * scale).astype(bf16)
    result_ref[pl.ds(key_row, block), target(2)] = state[1].astype(bf16)
    if merge:
        other = first_head * head_width
        for kind in range(3):
            result_ref[pl.ds(key_row, block), kind * all_width : kind * all_width + other] = earlier_ref[
                pl.ds(key_row, block), kind * other : (kind + 1) * other
            ]

    @pl.when(key_block == blocks - 1)
    def _():
        for number in range(blocks):
            rows = slice(number * block, (number + 1) * block)
            result_ref[rows, target(0)] = jnp.transpose(query_grads[number] * scale).astype(bf16)


def block_plan(lengths, tokens, block):
    ends = jnp.cumsum(lengths)
    positions = jnp.arange(tokens, dtype=jnp.int32)
    passed = positions[:, None] >= ends[None, :]
    starts = jnp.max(jnp.where(passed, ends[None, :], 0), axis=1).astype(jnp.int32)
    finish = jnp.min(jnp.where(passed, tokens, ends[None, :]), axis=1).astype(jnp.int32)
    blocks = tokens // block
    number = jnp.arange(blocks, dtype=jnp.int32)
    first_start = starts[::block]
    last_start = starts[block - 1 :: block]
    low = first_start // block
    mid = jnp.clip((last_start + block - 1) // block, low, number)
    high = (finish[block - 1 :: block] - 1) // block + 1
    full = jnp.clip(finish[::block] // block, number + 1, high)
    return (starts.reshape(blocks, 1, block), low, mid, full, high)


def scalar_spec():
    return pl.BlockSpec(memory_space=pltpu.SMEM)


def whole_spec(shape):
    return pl.BlockSpec(shape, lambda step: (0,) * len(shape), pipeline_mode=pl.Buffered(1))


def attend_forward(qkv, plan, slopes, heads, block):
    tokens, triple = qkv.shape
    width = triple // 3
    blocks = tokens // block
    starts, low, mid, full, high = plan
    return pl.pallas_call(
        functools.partial(forward_kernel, heads, block),
        grid=(blocks,),
        in_specs=[
            scalar_spec(),
            scalar_spec(),
            scalar_spec(),
            whole_spec((blocks, 1, block)),
            whole_spec((tokens, triple)),
        ],
        out_specs=[
            pl.BlockSpec((block, width), lambda step: (step, 0)),
            pl.BlockSpec((1, heads, block), lambda step: (step, 0, 0)),
        ],
        out_shape=[
            jax.ShapeDtypeStruct((tokens, width), bf16),
            jax.ShapeDtypeStruct((blocks, heads, block), f32),
        ],
        scratch_shapes=[
            pltpu.VMEM((blocks, width, block), bf16),
            pltpu.VMEM((blocks, heads * block, width), bf16),
            pltpu.VMEM((blocks, heads * block, block), f32),
        ],
        compiler_params=pltpu.CompilerParams(
            dimension_semantics=("arbitrary",), vmem_limit_bytes=24 * 1024 * 1024
        ),
        cost_estimate=pl.CostEstimate(
            flops=3 * tokens * tokens * 256 * heads,
            bytes_accessed=10 * tokens * width,
            transcendentals=tokens * tokens * heads // 2,
        ),
        name="attend_forward",
    )(low, mid, slopes, starts, qkv)


def attend_backward(qkv, grads, outputs, logs, plan, slopes, heads, block, first_head, earlier):
    tokens, triple = qkv.shape
    all_width = triple // 3
    all_heads = logs.shape[1]
    width = all_width // all_heads * heads
    blocks = tokens // block
    starts, low, mid, full, high = plan
    merge = earlier is not None
    result_width = triple if merge else 3 * width
    operands = [full, high, slopes, starts, logs, qkv, grads, outputs]
    specs = [scalar_spec() for _ in range(3)] + [whole_spec(entry.shape) for entry in operands[3:]]
    if merge:
        operands.append(earlier)
        specs.append(whole_spec(earlier.shape))
    return pl.pallas_call(
        functools.partial(backward_kernel, heads, block, first_head, merge),
        grid=(blocks,),
        in_specs=specs,
        out_specs=pl.BlockSpec((tokens, result_width), lambda step: (0, 0)),
        out_shape=jax.ShapeDtypeStruct((tokens, result_width), bf16),
        scratch_shapes=[
            pltpu.VMEM((blocks, width, block), bf16),
            pltpu.VMEM((blocks, width, block), bf16),
            pltpu.VMEM((blocks, width, block), bf16),
            pltpu.VMEM((blocks, heads * block, width), bf16),
            pltpu.VMEM((blocks, heads * block, width), bf16),
            pltpu.VMEM((heads * block, width), bf16),
            pltpu.VMEM((heads * block, width), bf16),
            pltpu.VMEM((blocks, heads, block), f32),
            pltpu.VMEM((blocks, width, block), f32),
        ],
        compiler_params=pltpu.CompilerParams(
            dimension_semantics=("arbitrary",), vmem_limit_bytes=24 * 1024 * 1024
        ),
        cost_estimate=pl.CostEstimate(
            flops=8 * tokens * tokens * 256 * heads,
            bytes_accessed=20 * tokens * width,
            transcendentals=tokens * tokens * heads // 2,
        ),
        name="attend_backward",
    )(*operands)


def hidden_backward_kernel(own_ref, other_ref, weight_ref, slope_ref, result_ref, total_ref):
    rows = own_ref.shape[0]
    total = jnp.zeros(total_ref.shape, f32)
    for number, ref in enumerate((own_ref, other_ref)):
        part = slice(number * rows, (number + 1) * rows)
        grads = dot_right(ref[...], weight_ref[...]) * slope_ref[part, :].astype(f32)
        grads = grads.astype(bf16)
        result_ref[part, :] = grads
        total = total + jnp.sum(grads.astype(f32), axis=0, keepdims=True)
    total_ref[...] = total


def hidden_backward(weight, cot_own, cot_other, slopes):
    rows, width = cot_own.shape
    breadth = slopes.shape[1]
    tile = min(256, breadth)
    return pl.pallas_call(
        hidden_backward_kernel,
        grid=(breadth // tile,),
        in_specs=[
            whole_spec((rows, width)),
            whole_spec((rows, width)),
            pl.BlockSpec((tile, width), lambda step: (step, 0)),
            pl.BlockSpec((2 * rows, tile), lambda step: (0, step)),
        ],
        out_specs=[
            pl.BlockSpec((2 * rows, tile), lambda step: (0, step)),
            pl.BlockSpec((1, tile), lambda step: (0, step)),
        ],
        out_shape=[
            jax.ShapeDtypeStruct((2 * rows, breadth), bf16),
            jax.ShapeDtypeStruct((1, breadth), f32),
        ],
        compiler_params=pltpu.CompilerParams(
            dimension_semantics=("arbitrary",), vmem_limit_bytes=12 * 1024 * 1024
        ),
        cost_estimate=pl.CostEstimate(flops=1, bytes_accessed=1, transcendentals=0),
        name="hidden_backward",
    )(cot_own, cot_other, weight, slopes)


def up_backward_kernel(grads_ref, weight_ref, result_ref):
    result_ref[...] = dot_right(grads_ref[...], weight_ref[...]).astype(result_ref.dtype)


def up_backward(weight, grads, number, kind_of):
    rows, breadth = grads.shape[0] // 2, grads.shape[1]
    width = weight.shape[0]
    tile = width // 4
    return pl.pallas_call(
        up_backward_kernel,
        grid=(4,),
        in_specs=[
            pl.BlockSpec((rows, breadth), lambda step: (number, 0)),
            pl.BlockSpec((tile, breadth), lambda step: (step, 0)),
        ],
        out_specs=pl.BlockSpec((rows, tile), lambda step: (0, step)),
        out_shape=jax.ShapeDtypeStruct((rows, width), kind_of),
        compiler_params=pltpu.CompilerParams(
            dimension_semantics=("arbitrary",), vmem_limit_bytes=12 * 1024 * 1024
        ),
        cost_estimate=pl.CostEstimate(flops=1, bytes_accessed=1, transcendentals=0),
        name="up_backward",
    )(grads, weight)


def down_projection_kernel(hidden_ref, weight_ref, result_ref):
    result_ref[...] = dot(hidden_ref[...], weight_ref[...]).astype(result_ref.dtype)


def down_projection(hidden, weight):
    rows, breadth = hidden.shape
    width = weight.shape[1]
    tile = min(256, rows)
    return pl.pallas_call(
        down_projection_kernel,
        grid=(rows // tile,),
        in_specs=[
            pl.BlockSpec((tile, breadth), lambda step: (step, 0)),
            whole_spec((breadth, width)),
        ],
        out_specs=pl.BlockSpec((tile, width), lambda step: (step, 0)),
        out_shape=jax.ShapeDtypeStruct((rows, width), bf16),
        compiler_params=pltpu.CompilerParams(
            dimension_semantics=("arbitrary",), vmem_limit_bytes=14 * 1024 * 1024
        ),
        cost_estimate=pl.CostEstimate(flops=1, bytes_accessed=1, transcendentals=0),
        name="down_projection",
    )(hidden, weight)


def up_gradient_kernel(own_ref, other_ref, grads_ref, result_ref, act_turned):
    rows, width = own_ref.shape
    step = 256

    @pl.when(pl.program_id(0) == 0)
    def _():
        for number, ref in enumerate((own_ref, other_ref)):
            for row in range(0, rows, step):
                first = number * rows + row
                for column in range(0, width, step):
                    block = ref[row : row + step, column : column + step]
                    act_turned[column : column + step, first : first + step] = turned(block).astype(bf16)

    result_ref[...] = dot(act_turned[...], grads_ref[...]).astype(bf16)


def up_gradient(act_own, act_other, grads):
    rows, width = act_own.shape
    breadth = grads.shape[1]
    tile = min(512, breadth)
    return pl.pallas_call(
        up_gradient_kernel,
        grid=(breadth // tile,),
        in_specs=[
            whole_spec((rows, width)),
            whole_spec((rows, width)),
            pl.BlockSpec((2 * rows, tile), lambda step: (0, step)),
        ],
        out_specs=pl.BlockSpec((width, tile), lambda step: (0, step)),
        out_shape=jax.ShapeDtypeStruct((width, breadth), bf16),
        scratch_shapes=[pltpu.VMEM((width, 2 * rows), bf16)],
        compiler_params=pltpu.CompilerParams(
            dimension_semantics=("arbitrary",), vmem_limit_bytes=16 * 1024 * 1024
        ),
        cost_estimate=pl.CostEstimate(flops=1, bytes_accessed=1, transcendentals=0),
        name="up_gradient",
    )(act_own, act_other, grads)


def together(*values):
    return lax.optimization_barrier(tuple(values))


def ordered(own, other, bit, axis=0):
    first = jnp.where(bit == 0, own, other)
    second = jnp.where(bit == 0, other, own)
    return jnp.stack([first, second], axis=axis)


class Moves:
    def __init__(self):
        self.shards = lax.axis_size("shard")
        self.reps = lax.axis_size("rep")
        self.half = self.shards // 2
        self.chips = self.reps // 2
        self.shard = lax.axis_index("shard")
        self.rep = lax.axis_index("rep")
        self.core = self.rep & 1
        self.chip = self.rep >> 1
        self.side = lax.div(self.shard, self.half)
        self.member = lax.rem(self.shard, self.half) + self.core * self.half

    def core_swap(self, part):
        return lax.ppermute(part, "rep", [(r, r ^ 1) for r in range(self.reps)])

    def chip_swap(self, part, bits):
        return lax.ppermute(part, "rep", [(r, r ^ (2 * bits)) for r in range(self.reps)])

    def shard_swap(self, part, bits):
        return lax.ppermute(part, "shard", [(s, s ^ bits) for s in range(self.shards)])

    def shard_bit(self, bits):
        return lax.div(self.shard, bits) & 1

    def low_bits(self):
        bits, result = 1, []
        while bits < self.half:
            result.append(bits)
            bits *= 2
        return result

    def home_send(self, part):
        pairs = []
        for rep in range(self.reps):
            for shard in range(self.shards):
                if shard // self.half != rep % 2:
                    to_shard = (shard + self.half) % self.shards
                    pairs.append((rep * self.shards + shard, (rep ^ 1) * self.shards + to_shard))
        return lax.ppermute(part, ("rep", "shard"), pairs)

    def home_join(self, part, other):
        return jnp.where(self.side == self.core, part, other)

    def half_gather(self, part):
        stack = part[None]
        for bits in self.low_bits():
            own = stack
            stack = ordered(own, self.shard_swap(own, bits), self.shard_bit(bits))
            stack = stack.reshape((-1,) + part.shape)
        return stack

    def cores_gather(self, stack):
        stack = ordered(stack, self.core_swap(stack), self.core)
        return stack.reshape((-1,) + stack.shape[2:])

    def exchange_bit(self, stack, bit, swap):
        sources, targets = stack.shape[:2]
        stack = stack.reshape((sources, 2, targets // 2) + stack.shape[2:])
        own, other = pick(stack, bit, 1), swap(pick(stack, 1 - bit, 1))
        return ordered(own, other, bit, 1).reshape((2 * sources,) + own.shape[1:])

    def half_exchange(self, stack):
        stack = stack[None]
        for bits in reversed(self.low_bits()):
            swap = functools.partial(self.shard_swap, bits=bits)
            stack = self.exchange_bit(stack, self.shard_bit(bits), swap)
        return stack.reshape((self.half,) + stack.shape[2:])

    def cores_exchange(self, stack):
        return self.exchange_bit(stack[None], self.core, self.core_swap)

    def members_exchange(self, stack):
        for bits in reversed(self.low_bits()):
            swap = functools.partial(self.shard_swap, bits=bits)
            stack = self.exchange_bit(stack, self.shard_bit(bits), swap)
        return stack.reshape((self.shards,) + stack.shape[2:])

    def reduce_bit(self, stack, bit, swap):
        stack = stack.reshape((2, stack.shape[0] // 2) + stack.shape[1:])
        other = swap(pick(stack, 1 - bit).astype(bf16))
        return pick(stack, bit).astype(f32) + other.astype(f32)

    def spread_open(self, part):
        if self.chips == 4:
            return (self.chip_swap(part, 1), self.chip_swap(part, 2))
        held, bits = [part], 1
        while bits < self.chips:
            held = held + [self.chip_swap(piece, bits) for piece in held]
            bits *= 2
        return tuple(held[1:])

    def spread_close(self, state):
        if self.chips == 4:
            by_x, by_y = state
            cut, axis = by_x.shape[-2] // 2, by_x.ndim - 2
            far = [
                self.chip_swap(by_x[..., :cut, :], 2),
                self.chip_swap(by_y[..., cut:, :], 1),
            ]
            return (by_x, by_y, jnp.concatenate(far, axis=axis))
        return state

    def far_open(self, states):
        if self.chips != 4:
            return ()
        cut = states[0][0].shape[0] // 2
        return (
            self.chip_swap(jnp.concatenate([by_x[:cut] for by_x, _ in states], axis=0), 2),
            self.chip_swap(jnp.concatenate([by_y[cut:] for _, by_y in states], axis=0), 1),
        )

    def far_parts(self, states, far):
        if self.chips != 4:
            return [[(k + 1, 0, part) for k, part in enumerate(state)] for state in states]
        cut = states[0][0].shape[0] // 2
        result = []
        for number, (by_x, by_y) in enumerate(states):
            rows = slice(number * cut, (number + 1) * cut)
            result.append([(1, 0, by_x), (2, 0, by_y), (3, 0, far[0][rows]), (3, cut, far[1][rows])])
        return result

    def chips_gather(self, part, axis, state=None):
        shape = part.shape[:axis] + (self.chips,) + part.shape[axis:]
        stack = place(jnp.zeros(shape, part.dtype), part, self.chip, axis)
        others = self.spread_close(self.spread_open(part) if state is None else state)
        for number, piece in enumerate(others):
            stack = place(stack, piece, self.chip ^ (number + 1), axis)
        return stack

    def reduce_open(self, stack, axis):
        return self.reduce_start(self.reduce_cut(stack, axis), axis)

    def reduce_cut(self, stack, axis):
        if self.chips != 4:
            return (stack,)
        shape = stack.shape[:axis] + (2, 2) + stack.shape[axis + 1 :]
        stack = stack.reshape(shape)
        bit_x, bit_y = self.chip & 1, self.chip >> 1
        cut = shape[0] // 2
        first, second = stack[:cut], stack[cut:]
        return (
            pick(first, bit_x, axis + 1),
            pick(second, bit_y, axis),
            pick(first, 1 - bit_x, axis + 1),
            pick(second, 1 - bit_y, axis),
        )

    def reduce_start(self, parts, axis):
        if self.chips == 4:
            first, second, send_first, send_second = parts
            return (first, second, self.chip_swap(send_first, 1), self.chip_swap(send_second, 2))
        (stack,) = parts
        count = self.chips
        stack = stack.astype(f32)
        while count > 1:
            count //= 2
            shape = stack.shape[:axis] + (2, count) + stack.shape[axis + 1 :]
            stack = stack.reshape(shape)
            bit = lax.div(self.chip, count) & 1
            got = self.chip_swap(pick(stack, 1 - bit, axis).astype(bf16), count)
            stack = pick(stack, bit, axis) + got.astype(f32)
        return (pick(stack, 0, axis).astype(bf16),)

    def reduce_add(self, state):
        if self.chips != 4:
            return state
        first, second, got_first, got_second = state
        first = (first.astype(f32) + got_first.astype(f32)).astype(bf16)
        second = (second.astype(f32) + got_second.astype(f32)).astype(bf16)
        return (first, second)

    def reduce_send(self, state, axis):
        if self.chips != 4:
            return state
        first, second = state
        bit_x, bit_y = self.chip & 1, self.chip >> 1
        got_first = self.chip_swap(pick(first, 1 - bit_y, axis), 2)
        got_second = self.chip_swap(pick(second, 1 - bit_x, axis), 1)
        return (pick(first, bit_y, axis), pick(second, bit_x, axis), got_first, got_second)

    def reduce_final(self, state):
        if self.chips != 4:
            return state[0]
        first, second, got_first, got_second = state
        first = first.astype(f32) + got_first.astype(f32)
        second = second.astype(f32) + got_second.astype(f32)
        return jnp.concatenate([first, second], axis=0).astype(bf16)

    def reduce_close(self, state, axis):
        return self.reduce_final(self.reduce_send(state, axis))

    def core_pair(self, part):
        other = self.core_swap(part)
        first = jnp.where(self.core == 0, part, other)
        second = jnp.where(self.core == 0, other, part)
        return first, second

    def sum_reps(self, vector):
        bits = 1
        while bits < self.reps:
            vector = vector + lax.ppermute(vector, "rep", [(r, r ^ bits) for r in range(self.reps)])
            bits *= 2
        return vector

    def sum_shards(self, vector):
        bits = 1
        while bits < self.shards:
            vector = vector + self.shard_swap(vector, bits)
            bits *= 2
        return vector


def stats_kernel(decay_rate, gradient_ref, old_ref, rows_ref, lane_rows_ref, sums_ref, total_ref, partial):
    step = pl.program_id(0)
    rows, columns = gradient_ref.shape

    @pl.when(step == 0)
    def _():
        partial[...] = jnp.zeros_like(partial)
        total_ref[...] = jnp.zeros_like(total_ref)

    gradient = gradient_ref[...].astype(f32)
    square = gradient * gradient
    row_mean = jnp.sum(square, axis=1, keepdims=True) / columns
    old = jnp.transpose(jnp.broadcast_to(old_ref[...], (128, rows)))[:, 0:1]
    rows_new = decay_rate * old + (1.0 - decay_rate) * (row_mean + eps_second)
    rows_ref[...] = rows_new
    lane_rows_ref[...] = jnp.transpose(jnp.broadcast_to(rows_new, (rows, 128)))[0:1, :]
    total_ref[...] += jnp.broadcast_to(jnp.sum(rows_new, axis=0, keepdims=True), (1, 128))
    partial[0:8, :] += eights(square, jnp.sum)
    partial[8:16, :] += eights(square * (1.0 / rows_new), jnp.sum)

    @pl.when(step == pl.num_programs(0) - 1)
    def _():
        sums_ref[0:1, :] = jnp.sum(partial[0:8, :], axis=0, keepdims=True)
        sums_ref[1:2, :] = jnp.sum(partial[8:16, :], axis=0, keepdims=True)


def factor_stats(gradient, rows_old, decay_rate):
    height, breadth = gradient.shape
    rows = min(256 if breadth <= 1024 else 128, height)
    return pl.pallas_call(
        functools.partial(stats_kernel, decay_rate),
        grid=(height // rows,),
        in_specs=[
            pl.BlockSpec((rows, breadth), lambda step: (step, 0)),
            pl.BlockSpec((1, rows), lambda step: (0, step)),
        ],
        out_specs=[
            pl.BlockSpec((rows, 1), lambda step: (step, 0)),
            pl.BlockSpec((1, rows), lambda step: (0, step)),
            pl.BlockSpec((2, breadth), lambda step: (0, 0)),
            pl.BlockSpec((1, 128), lambda step: (0, 0)),
        ],
        out_shape=[
            jax.ShapeDtypeStruct((height, 1), f32),
            jax.ShapeDtypeStruct((1, height), f32),
            jax.ShapeDtypeStruct((2, breadth), f32),
            jax.ShapeDtypeStruct((1, 128), f32),
        ],
        scratch_shapes=[pltpu.VMEM((16, breadth), f32)],
        compiler_params=pltpu.CompilerParams(
            dimension_semantics=("arbitrary",), vmem_limit_bytes=12 * 1024 * 1024
        ),
        name="factor_stats",
    )(gradient, rows_old)


def apply_kernel(
    decay_rate,
    height,
    gradient_ref,
    weight_ref,
    rows_ref,
    sums_ref,
    scalar_ref,
    old_ref,
    gradient_out,
    weight_out,
    copy_out,
    cols_out,
    rms_out,
    col_factor,
):
    columns = gradient_ref.shape[1]

    @pl.when(pl.program_id(0) == 0)
    def _():
        cols_new = decay_rate * old_ref[...] + (1.0 - decay_rate) * (
            sums_ref[0:1, :] / height + eps_second
        )
        row_mean = scalar_ref[0:1, 0:1] / height
        weight_mean = scalar_ref[1:2, 0:1] / (height * columns)
        scaled = jnp.sum(sums_ref[1:2, :] / cols_new, axis=1, keepdims=True)
        rms_update = jnp.sqrt(row_mean / (height * columns) * scaled)
        factor = rate_step * jnp.sqrt(weight_mean) * jnp.sqrt(row_mean)
        factor = factor / jnp.maximum(1.0, rms_update / clip_level)
        col_factor[...] = factor * lax.rsqrt(cols_new)
        cols_out[...] = cols_new
        rms_out[...] = jnp.broadcast_to(rms_update, (1, 128))

    gradient = gradient_ref[...].astype(f32)
    new_weight = weight_ref[...] - gradient * lax.rsqrt(rows_ref[...]) * col_factor[...]
    gradient_out[...] = gradient
    weight_out[...] = new_weight
    copy_out[...] = new_weight.astype(bf16)


def factor_apply(gradient, weight, rows_new, sums, scalars, cols_old, height, decay_rate):
    own_height, breadth = gradient.shape
    rows = min(256 if breadth <= 1024 else 64, own_height)

    def rows_spec():
        return pl.BlockSpec((rows, breadth), lambda step: (step, 0))

    def row_spec(count, wide):
        return pl.BlockSpec((count, wide), lambda step: (0, 0))

    return pl.pallas_call(
        functools.partial(apply_kernel, decay_rate, height),
        grid=(own_height // rows,),
        in_specs=[
            rows_spec(),
            rows_spec(),
            pl.BlockSpec((rows, 1), lambda step: (step, 0)),
            row_spec(2, breadth),
            row_spec(2, 128),
            row_spec(1, breadth),
        ],
        out_specs=[rows_spec(), rows_spec(), rows_spec(), row_spec(1, breadth), row_spec(1, 128)],
        out_shape=[
            jax.ShapeDtypeStruct((own_height, breadth), f32),
            jax.ShapeDtypeStruct((own_height, breadth), f32),
            jax.ShapeDtypeStruct((own_height, breadth), bf16),
            jax.ShapeDtypeStruct((1, breadth), f32),
            jax.ShapeDtypeStruct((1, 128), f32),
        ],
        scratch_shapes=[pltpu.VMEM((1, breadth), f32)],
        compiler_params=pltpu.CompilerParams(
            dimension_semantics=("arbitrary",), vmem_limit_bytes=14 * 1024 * 1024
        ),
        name="factor_apply",
    )(gradient, weight, rows_new, sums, scalars, cols_old)


def summed(moves, entries):
    total = moves.sum_shards(jnp.concatenate(entries, axis=1))
    result, offset = [], 0
    for entry in entries:
        result.append(total[:, offset : offset + entry.shape[1]])
        offset += entry.shape[1]
    return result


def on_device(
    tokens,
    cotangent,
    seq_lengths,
    qkv_weight,
    out_weight,
    up_weight,
    down_weight,
    vectors,
    row_state,
    down_rows,
    col_state,
    vector_state,
):
    moves = Moves()
    shards, half, chips, core = moves.shards, moves.half, moves.chips, moves.core
    row_count, width = tokens.shape
    hidden_width = up_weight.shape[1]
    group_rows = row_count * shards
    heads = HEADS // shards
    head_width = width // HEADS
    span = heads * head_width
    member = moves.member
    decay_rate = 1.0 - STEP ** (-0.8)
    head_number = (member * heads + jnp.arange(heads, dtype=jnp.int32)).astype(f32)
    slopes = jnp.exp2(-8.0 * (head_number + 1.0) / HEADS)

    gain_one = vectors[0:width]
    shift_one = vectors[width : 2 * width]
    bias_query = vectors[2 * width : 3 * width]
    bias_value = vectors[3 * width : 4 * width]
    bias_out = vectors[4 * width : 5 * width]
    gain_two = vectors[5 * width : 6 * width]
    shift_two = vectors[6 * width : 7 * width]
    bias_up = vectors[7 * width : 7 * width + hidden_width]
    bias_down = vectors[7 * width + hidden_width :]

    other_tokens = moves.home_send(tokens)
    other_lengths = moves.core_swap(seq_lengths)
    lengths = jnp.where(moves.side == core, seq_lengths, other_lengths)[0]
    plan = block_plan(lengths, group_rows, BLOCK)
    rows_z = width // shards
    rows_piece = rows_z // chips
    my_rows = cut_rows(qkv_weight, moves.chip * rows_piece, rows_piece)
    my_rows = my_rows.astype(bf16)
    my_blocks = []
    for number in range(half):
        kinds = []
        for kind in range(3):
            first = kind * width + number * span
            second = first + half * span
            kinds.append(
                jnp.where(
                    core == 0, my_rows[:, first : first + span], my_rows[:, second : second + span]
                )
            )
        my_blocks.append(jnp.concatenate(kinds, axis=1))
    qkv_part = moves.half_exchange(jnp.stack(my_blocks))
    half_cols = hidden_width // (2 * shards)
    up_wide = shards * half_cols
    out_wide = width // 2
    down_piece = half_cols // chips

    def core_half(values):
        parts = []
        for number in range(shards):
            start = 2 * number * half_cols
            first = values[..., start : start + half_cols]
            second = values[..., start + half_cols : start + 2 * half_cols]
            parts.append(jnp.where(core == 0, first, second))
        return jnp.concatenate(parts, axis=-1)

    up_own = core_half(up_weight).astype(bf16).reshape(chips, rows_piece, up_wide)
    out_own = jnp.where(core == 0, out_weight[:, :out_wide], out_weight[:, out_wide:]).astype(bf16)
    out_own = out_own.reshape(chips, rows_piece, out_wide)
    down_own = cut_rows(down_weight, core * half_cols, half_cols).astype(bf16)
    fold = down_piece // rows_piece
    down_own = down_own.reshape(chips, fold, rows_piece, width)
    my_down = pick(down_own, moves.chip)
    weight_piece = jnp.concatenate(
        [pick(up_own, moves.chip), pick(out_own, moves.chip)] + [my_down[k] for k in range(fold)],
        axis=1,
    )
    near_pieces, bits = [weight_piece], 1
    while bits < half:
        near_pieces = near_pieces + [moves.shard_swap(piece, bits) for piece in near_pieces]
        bits *= 2
    near_pieces = near_pieces[1:]
    weights = [qkv_weight, out_weight, up_weight, down_weight]
    weight_sums = [jnp.sum(weight * weight) for weight in weights]
    other_tokens, qkv_part, near_pieces, weight_piece, plan, weight_sums = together(
        other_tokens, qkv_part, near_pieces, weight_piece, plan, weight_sums
    )
    home_tokens = moves.home_join(tokens, other_tokens)
    far_piece = moves.shard_swap(weight_piece, half)
    near_open = [moves.spread_open(piece) for piece in near_pieces]
    qkv_far = moves.shard_swap(qkv_part, half)
    qkv_far, near_open = together(qkv_far, near_open)
    qkv_part = ordered(qkv_part, qkv_far, moves.side).reshape(shards, rows_piece, 3 * span)
    qkv_cols = moves.chips_gather(qkv_part, 1).reshape(width, 3 * span)
    inputs = home_tokens.astype(f32)
    normed_one, inv_std_one = norm_parts(inputs)
    act_one = (normed_one * gain_one + shift_one).astype(bf16)
    act_half = moves.half_gather(act_one)

    act_half, qkv_cols, far_piece = together(act_half, qkv_cols, far_piece)
    near_far = moves.far_open(near_open)
    act_all = moves.cores_gather(act_half).reshape(group_rows, width)
    far_open = moves.spread_open(far_piece)
    far_pieces, bits = [far_piece], 1
    while bits < half:
        far_pieces = far_pieces + [moves.shard_swap(piece, bits) for piece in far_pieces]
        bits *= 2
    far_pieces = far_pieces[1:]

    bias_q_part = cut_rows(bias_query, member * span, span)
    bias_v_part = cut_rows(bias_value, member * span, span)
    qkv_bias = jnp.concatenate([bias_q_part, jnp.zeros_like(bias_q_part), bias_v_part])
    qkv_rows = (dot(act_all, qkv_cols) + qkv_bias).astype(bf16)
    attended_cols, logs = attend_forward(qkv_rows, plan, slopes, heads, BLOCK)
    attended_cols, far_open, far_pieces, near_far = together(
        attended_cols, far_open, far_pieces, near_far
    )
    attended_parts = moves.cores_exchange(attended_cols.reshape(shards, row_count, span))
    attended_parts = moves.members_exchange(attended_parts)
    second_far = moves.far_open([far_open])
    last_states = [moves.spread_open(piece) for piece in far_pieces]
    attended_parts, second_far, last_states, cotangent = together(
        attended_parts, second_far, last_states, cotangent
    )
    last_far = moves.far_open(last_states)
    other_cot = moves.home_send(cotangent)
    home_cot = moves.home_join(cotangent, other_cot)
    attended = jnp.concatenate([attended_parts[k] for k in range(shards)], axis=1)

    up_all = place(jnp.zeros((shards, chips, rows_piece, up_wide), bf16), up_own, moves.shard)
    out_all = place(jnp.zeros((shards, chips, rows_piece, out_wide), bf16), out_own, moves.shard)
    down_all = place(jnp.zeros((shards, chips, fold, rows_piece, width), bf16), down_own, moves.shard)
    pieces = near_pieces + [far_piece] + far_pieces
    parts_of = moves.far_parts(near_open, near_far) + moves.far_parts([far_open], second_far)
    parts_of += moves.far_parts(last_states, last_far)
    for number, (piece, parts) in enumerate(zip(pieces, parts_of)):
        plane = moves.shard ^ (number + 1)
        for far, row, rows in [(0, 0, piece)] + parts:
            chip = moves.chip ^ far
            up_all = lax.dynamic_update_slice(
                up_all, rows[None, None, :, :up_wide], (plane, chip, row, 0), allow_negative_indices=False
            )
            out_all = lax.dynamic_update_slice(
                out_all, rows[None, None, :, up_wide : up_wide + out_wide], (plane, chip, row, 0), allow_negative_indices=False
            )
            start = up_wide + out_wide
            folds = [rows[:, start + k * width : start + (k + 1) * width] for k in range(fold)]
            down_all = lax.dynamic_update_slice(
                down_all, jnp.stack(folds)[None, None], (plane, chip, 0, row, 0), allow_negative_indices=False
            )
    up_half = up_all.reshape(width, up_wide)
    down_half = down_all.reshape(up_wide, width)
    out_first, out_second = moves.core_pair(out_all.reshape(width, out_wide))
    out_low = jnp.concatenate([out_first, out_second], axis=1)
    residual = inputs + dot(attended, out_low) + bias_out
    normed_two, inv_std_two = norm_parts(residual)
    act_two = (normed_two * gain_two + shift_two).astype(bf16)

    act_two_other, attended_other = together(
        moves.core_swap(act_two), moves.core_swap(attended)
    )
    cot_other = moves.core_swap(home_cot)
    cot_pair = jnp.concatenate([home_cot, cot_other], axis=0)
    act_two_pair = jnp.concatenate([act_two, act_two_other], axis=0)
    attended_pair = jnp.concatenate([attended, attended_other], axis=0)
    bias_up_half = core_half(bias_up)
    up_pair = dot(act_two_pair, up_half) + bias_up_half
    hidden_pair = gelu_value(up_pair).astype(bf16)
    slope_pair = gelu_slope(up_pair).astype(bf16)
    down_terms = dot_rows(hidden_pair, cot_pair).astype(bf16)
    down_state = moves.reduce_cut(down_terms.reshape(shards, chips, down_piece, width), 1)
    slope_pair, down_state = together(slope_pair, down_state)
    down_state = moves.reduce_start(down_state, 1)
    grad_y = home_cot.astype(f32)
    grad_bias_down = jnp.sum(grad_y, axis=0)
    grad_up_pair, grad_bias_up = hidden_backward(down_half, home_cot, cot_other, slope_pair)
    grad_bias_up = grad_bias_up.reshape(-1)
    back_other = moves.core_swap(up_backward(up_half, grad_up_pair, 1, bf16))
    up_terms = up_gradient(act_two, act_two_other, grad_up_pair)
    down_pair = down_projection(hidden_pair, down_half)
    back_other, down_pair, up_terms, down_state = together(
        back_other, down_pair, up_terms, down_state
    )
    up_cut = moves.reduce_cut(up_terms.reshape(shards, chips, rows_piece, up_wide), 1)
    down_sums = moves.reduce_add(down_state)
    grad_act_two = up_backward(up_half, grad_up_pair, 0, f32) + back_other.astype(f32)
    grad_gain_two = jnp.sum(grad_act_two * normed_two, axis=0)
    grad_shift_two = jnp.sum(grad_act_two, axis=0)
    grad_residual = grad_y + norm_back(grad_act_two, normed_two, inv_std_two, gain_two)
    grad_attn = grad_residual.astype(bf16)
    grad_bias_out = jnp.sum(grad_attn, axis=0, dtype=f32)
    to_members = jnp.stack(
        [
            dot_right(grad_attn, out_low[k * span : (k + 1) * span]).astype(bf16)
            for k in range(shards)
        ]
    )
    attn_halves = [grad_attn[:, :out_wide], grad_attn[:, out_wide:]]
    attn_own = jnp.where(core == 0, attn_halves[0], attn_halves[1])
    attn_other = jnp.where(core == 0, attn_halves[1], attn_halves[0])
    down_other = moves.core_swap(down_pair[row_count:])
    grad_heads, attn_other, up_cut, down_sums, down_other = together(
        moves.cores_exchange(to_members), moves.core_swap(attn_other), up_cut, down_sums, down_other
    )
    attn_pair = jnp.concatenate([attn_own, attn_other], axis=0)
    grad_heads = moves.members_exchange(grad_heads).reshape(group_rows, span)
    up_state = moves.reduce_start(up_cut, 1)
    down_mid = moves.reduce_close(down_sums, 1)
    block_out = residual + down_pair[:row_count].astype(f32) + down_other.astype(f32) + bias_down
    block_out = block_out.astype(bf16)

    out_terms = dot_rows(attended_pair, attn_pair).astype(bf16)
    def shards_halve(piece, bits):
        piece = piece.reshape((piece.shape[0] // 2, 2) + piece.shape[1:])
        bit = moves.shard_bit(bits)
        return pick(piece, bit, 1), moves.shard_swap(pick(piece, 1 - bit, 1), bits)

    def halved(state):
        own, other = state
        return (own.astype(f32) + other.astype(f32)).astype(bf16)

    def shards_sum(piece):
        rows = piece.shape[1]
        return lax.psum_scatter(
            piece.reshape(shards * rows, piece.shape[2]), "shard", scatter_dimension=0, tiled=True
        )

    grad_heads, down_mid, out_terms, block_out = together(
        grad_heads, down_mid, out_terms, block_out
    )
    block_other = moves.home_send(block_out)
    down_owned = shards_sum(down_mid)
    out_state = moves.reduce_open(out_terms.reshape(shards, chips, rows_piece, out_wide), 1)
    attend_args = (plan, slopes)
    parts = 2 if heads % 4 == 0 else 1
    part_heads = heads // parts
    grad_qkv = attend_backward(
        qkv_rows, grad_heads, attended_cols, logs, *attend_args, part_heads, BLOCK, 0, None
    )
    grad_qkv, up_state, out_state = together(grad_qkv, up_state, out_state)
    up_sums, out_sums = moves.reduce_add(up_state), moves.reduce_add(out_state)
    grad_qkv, up_sums, out_sums = together(grad_qkv, up_sums, out_sums)
    up_out_state = [
        jnp.concatenate([up_part, out_part], axis=-1) for up_part, out_part in zip(up_sums, out_sums)
    ]
    if parts == 2:
        grad_qkv = attend_backward(
            qkv_rows, grad_heads, attended_cols, logs, *attend_args, part_heads, BLOCK, part_heads, grad_qkv
        )
    grad_qkv, up_out_state, block_other, down_owned = together(
        grad_qkv, moves.reduce_send(up_out_state, 1), block_other, down_owned
    )
    block_out = moves.home_join(block_out, block_other)
    up_out_piece = moves.reduce_final(up_out_state)
    up_out_state = shards_halve(up_out_piece, 1)

    grad_bias_q_part = jnp.sum(grad_qkv[:, :span], axis=0, dtype=f32)
    grad_bias_v_part = jnp.sum(grad_qkv[:, 2 * span :], axis=0, dtype=f32)

    grad_halves = grad_qkv.reshape(2, half * row_count, 3 * span)
    sent = dot_right(pick(grad_halves, 1 - core), qkv_cols).astype(bf16)
    sent = moves.core_swap(sent)
    qkv_terms = dot_rows(act_all, grad_qkv).astype(bf16)
    qkv_terms = qkv_terms.reshape(shards, chips, rows_piece, 3 * span)
    qkv_state = moves.reduce_open(qkv_terms, 1)
    back = dot_right(pick(grad_halves, core), qkv_cols) + sent.astype(f32)
    qkv_state, back = together(qkv_state, back)

    back = back.reshape(half, row_count, width)
    low_bits = list(reversed(moves.low_bits()))
    for bits in low_bits[:-1]:
        back = moves.reduce_bit(
            back, moves.shard_bit(bits), functools.partial(moves.shard_swap, bits=bits)
        )
    back = back.reshape((2, -1) + back.shape[1:])
    back_bit = moves.shard_bit(low_bits[-1])
    back_other = moves.shard_swap(pick(back, 1 - back_bit).astype(bf16), low_bits[-1])
    qkv_state = moves.reduce_send(moves.reduce_add(qkv_state), 1)
    qkv_state, up_out_state = together(qkv_state, up_out_state)

    up_out_piece, bits = halved(up_out_state), 2
    while bits < half:
        up_out_piece = halved(shards_halve(up_out_piece, bits))
        bits *= 2
    up_out_state = shards_halve(up_out_piece, half)
    qkv_piece = moves.reduce_final(qkv_state)
    qkv_piece = qkv_piece.reshape((2, half) + qkv_piece.shape[1:])
    qkv_own = pick(qkv_piece, moves.side)
    qkv_other = moves.shard_swap(pick(qkv_piece, 1 - moves.side), half)
    back_other, qkv_other, up_out_state, down_owned = together(
        back_other, qkv_other, up_out_state, down_owned
    )

    up_out_owned = halved(up_out_state)[0]
    up_out_state = moves.spread_open(up_out_owned)
    qkv_piece = moves.half_exchange(halved((qkv_own, qkv_other)))
    down_state = moves.spread_open(down_owned)
    grad_act_one = pick(back, back_bit) + back_other.astype(f32)
    grad_act_one = grad_act_one.reshape(row_count, width)
    grad_gain_one = jnp.sum(grad_act_one * normed_one, axis=0)
    grad_shift_one = jnp.sum(grad_act_one, axis=0)
    grad_inputs = grad_residual + norm_back(grad_act_one, normed_one, inv_std_one, gain_one)
    grad_inputs, grad_gain_one, grad_shift_one, qkv_piece, down_state, up_out_state = together(
        grad_inputs.astype(bf16), grad_gain_one, grad_shift_one, qkv_piece, down_state, up_out_state
    )
    tokens_other = moves.home_send(grad_inputs)
    qkv_owned = moves.chips_gather(qkv_piece, 1)

    up_out_first, up_out_second = moves.core_pair(
        moves.chips_gather(up_out_owned, 0, tuple(up_out_state)).reshape(rows_z, up_wide + out_wide)
    )
    out_grad = jnp.concatenate([up_out_first[:, up_wide:], up_out_second[:, up_wide:]], axis=1)
    up_columns = []
    for number in range(shards):
        part = slice(number * half_cols, (number + 1) * half_cols)
        up_columns += [up_out_first[:, part], up_out_second[:, part]]
    up_grad = jnp.concatenate(up_columns, axis=1)
    down_first, down_second = moves.core_pair(
        moves.chips_gather(down_owned, 0, tuple(down_state)).reshape(half_cols, width)
    )
    down_grad = jnp.concatenate([down_first, down_second], axis=0)
    qkv_owned = qkv_owned.reshape(half, rows_z, 3 * span)
    qkv_other, tokens_other = together(moves.core_swap(qkv_owned), tokens_other)
    tokens_grad = moves.home_join(grad_inputs, tokens_other)
    qkv_first = jnp.where(core == 0, qkv_owned, qkv_other)
    qkv_second = jnp.where(core == 0, qkv_other, qkv_owned)
    qkv_columns = []
    for kind in range(3):
        for source in (qkv_first, qkv_second):
            for number in range(half):
                qkv_columns.append(source[number][:, kind * span : (kind + 1) * span])
    qkv_grad = jnp.concatenate(qkv_columns, axis=1)

    gradients = [qkv_grad, out_grad, up_grad, down_grad]
    heights = [width, width, width, hidden_width]
    rows_old = [row_state[k : k + 1] for k in range(3)] + [down_rows.reshape(1, -1)]
    stats = [
        factor_stats(gradient, old, decay_rate) for gradient, old in zip(gradients, rows_old)
    ]

    def to_sum(number):
        weight_sum = jnp.broadcast_to(weight_sums[number], (1, 128))
        return [stats[number][2], jnp.concatenate([stats[number][3], weight_sum], axis=0)]

    def spread_heads(part):
        return [jnp.where(member == number, part, 0.0) for number in range(shards)]

    bias_up_parts = []
    for number in range(shards):
        part = grad_bias_up[number * half_cols : (number + 1) * half_cols]
        bias_up_parts += [jnp.where(core == 0, part, 0.0), jnp.where(core == 1, part, 0.0)]
    vector_part = moves.sum_reps(
        jnp.concatenate(
            [grad_gain_one, grad_shift_one]
            + spread_heads(grad_bias_q_part)
            + spread_heads(grad_bias_v_part)
            + [grad_bias_out, grad_gain_two, grad_shift_two]
            + bias_up_parts
            + [grad_bias_down]
        )
    )
    vector_rows = vector_part.reshape(2, -1)
    all_sums = summed(moves, to_sum(0) + to_sum(1) + to_sum(2) + to_sum(3) + [vector_rows])
    sums = [all_sums[0:2], all_sums[2:4], all_sums[4:6], all_sums[6:8]]
    vector_grad = all_sums[8].reshape(-1)
    updates = []
    offset = 0
    for number in range(4):
        end_col = offset + gradients[number].shape[1]
        updates.append(
            factor_apply(
                gradients[number],
                weights[number],
                stats[number][0],
                sums[number][0],
                sums[number][1],
                col_state[offset:end_col].reshape(1, -1),
                heights[number],
                decay_rate,
            )
        )
        offset = end_col
    grads_out, new_weights, copies, new_cols, rms_rows = zip(*updates)
    rms_values = [rms[0, 0] for rms in rms_rows]

    vector_state_new = decay_rate * vector_state + (1.0 - decay_rate) * (
        vector_grad * vector_grad + eps_second
    )
    vector_step = vector_grad * lax.rsqrt(vector_state_new)
    vector_rms = jnp.sqrt(jnp.mean(vector_step * vector_step))
    vector_new = vectors - rate_step * jnp.sqrt(
        jnp.mean(vectors * vectors)
    ) * vector_step / jnp.maximum(1.0, vector_rms / clip_level)
    update_rms = jnp.stack(rms_values + [vector_rms])
    return (
        block_out,
        tokens_grad,
        *grads_out,
        vector_grad,
        *new_weights,
        vector_new,
        *copies,
        jnp.concatenate([stats[0][1], stats[1][1], stats[2][1]], axis=0),
        stats[3][1].reshape(-1),
        jnp.concatenate(new_cols, axis=1).reshape(-1),
        vector_state_new,
        update_rms,
    )


def solution(mesh):
    in_specs = (
        P(("rep", "shard"), None),
        P(("rep", "shard"), None),
        P("rep", None),
        P("shard", None),
        P("shard", None),
        P("shard", None),
        P("shard", None),
        P(),
        P(None, "shard"),
        P("shard"),
        P(),
        P(),
    )
    out_specs = (
        P(("rep", "shard"), None),
        P(("rep", "shard"), None),
        P("shard", None),
        P("shard", None),
        P("shard", None),
        P("shard", None),
        P(),
        P("shard", None),
        P("shard", None),
        P("shard", None),
        P("shard", None),
        P(),
        P("shard", None),
        P("shard", None),
        P("shard", None),
        P("shard", None),
        P(None, "shard"),
        P("shard"),
        P(),
        P(),
        P(),
    )
    return jax.shard_map(
        on_device, mesh=mesh, in_specs=in_specs, out_specs=out_specs, check_vma=False
    )
```

```python
import functools

import jax
import jax.numpy as jnp
from jax import lax
from jax.experimental import pallas as pl
from jax.experimental.pallas import tpu as pltpu
from jax.sharding import PartitionSpec as P

HEADS = 16
STEP = 10
BLOCK = 256


eps_norm = 1e-05
eps_second = 1e-30
rate_step = 0.5
clip_level = 1.0
masked = -1e30
gelu_root = (2.0 / 3.141592653589793) ** 0.5
gelu_cubic = 0.044715

f32 = jnp.float32
bf16 = jnp.bfloat16


def norm_parts(values):
    average = jnp.mean(values, axis=-1, keepdims=True)
    centred = values - average
    inv_std = lax.rsqrt(jnp.mean(centred * centred, axis=-1, keepdims=True) + eps_norm)
    return (centred * inv_std, inv_std)


def norm_back(grad_out, normed, inv_std, gain_vec):
    grad_normed = grad_out * gain_vec
    inner_mean = jnp.mean(grad_normed * normed, axis=-1, keepdims=True)
    centred = grad_normed - jnp.mean(grad_normed, axis=-1, keepdims=True)
    return (centred - normed * inner_mean) * inv_std


def gelu_value(pre_act):
    curve = jnp.tanh(gelu_root * (pre_act + gelu_cubic * pre_act * pre_act * pre_act))
    return 0.5 * pre_act * (1.0 + curve)


def gelu_slope(pre_act):
    square = pre_act * pre_act
    curve = jnp.tanh(gelu_root * (pre_act + gelu_cubic * square * pre_act))
    inner = gelu_root * (1.0 + 3.0 * gelu_cubic * square)
    return 0.5 * (1.0 + curve) + 0.5 * pre_act * (1.0 - curve * curve) * inner


def dot(left_side, right_side):
    return jnp.dot(left_side, right_side, preferred_element_type=f32)


def dot_right(left_side, right_side):
    return lax.dot_general(
        left_side, right_side, (((1,), (1,)), ((), ())), preferred_element_type=f32
    )


def dot_rows(left_side, right_side):
    return lax.dot_general(
        left_side, right_side, (((0,), (0,)), ((), ())), preferred_element_type=f32
    )


def pick(stack, index, axis=0):
    return lax.dynamic_index_in_dim(stack, index, axis, keepdims=False, allow_negative_indices=False)


def cut_rows(values, start, count):
    return lax.dynamic_slice_in_dim(values, start, count, 0, allow_negative_indices=False)


def place(stack, part, index, axis=0):
    return lax.dynamic_update_index_in_dim(stack, part, index, axis, allow_negative_indices=False)


def head_rows(number, head_width):
    return slice(number * head_width, (number + 1) * head_width)


def lane_masks(block_rows, width, heads):
    lanes = lax.broadcasted_iota(jnp.int32, (block_rows, width), 1)
    head_width = width // heads
    return [
        (lanes >= number * head_width) & (lanes < (number + 1) * head_width)
        for number in range(heads)
    ]


def allowed_pairs(key_block, query_block, start_row, block):
    key_pos = lax.broadcasted_iota(jnp.int32, (block, block), 0) + key_block * block
    query_pos = lax.broadcasted_iota(jnp.int32, (block, block), 1) + query_block * block
    return (key_pos <= query_pos) & (key_pos >= start_row)


def key_offsets(key_block, query_block, block):
    rows = lax.broadcasted_iota(jnp.int32, (block, 1), 0)
    return (rows + (key_block - query_block) * block).astype(f32)


def turned(values):
    return jnp.transpose(values.astype(f32))


def head_stack(values, lanes):
    zero = jnp.zeros(values.shape, values.dtype)
    return jnp.concatenate([jnp.where(lane, values, zero) for lane in lanes], axis=0)


def eights(values, combine):
    rows, columns = values.shape
    return combine(values.reshape(rows // 8, 8, columns), axis=0)


def forward_kernel(
    heads,
    block,
    low_ref,
    mid_ref,
    slope_ref,
    start_ref,
    qkv_ref,
    out_ref,
    log_ref,
    values_turned,
    key_stack,
    score_ref,
):
    tokens = qkv_ref.shape[0]
    width = qkv_ref.shape[1] // 3
    head_width = width // heads
    blocks = tokens // block
    query_block = pl.program_id(0)

    @pl.when(query_block == 0)
    def _():
        lanes = lane_masks(block, width, heads)
        for number in range(blocks):
            rows = slice(number * block, (number + 1) * block)
            values_turned[number] = turned(qkv_ref[rows, 2 * width :]).astype(bf16)
            key_stack[number] = head_stack(qkv_ref[rows, width : 2 * width], lanes)

    first_row = pl.multiple_of(query_block * block, block)
    queries = qkv_ref[pl.ds(first_row, block), :width].astype(f32) * head_width ** (-0.5)
    queries = turned(queries).astype(bf16)
    start_row = start_ref[query_block]

    def score_step(key_block, bests, with_mask):
        scores = dot(key_stack[key_block], queries)
        offsets = key_offsets(key_block, query_block, block)
        allowed = allowed_pairs(key_block, query_block, start_row, block) if with_mask else None
        result = []
        for number in range(heads):
            rows = head_rows(number, block)
            part = scores[rows] + slope_ref[number] * offsets
            if with_mask:
                part = jnp.where(allowed, part, masked)
            score_ref[key_block, rows, :] = part
            result.append(jnp.maximum(bests[number], eights(part, jnp.max)))
        return tuple(result)

    low, mid = low_ref[query_block], mid_ref[query_block]
    bests = tuple(jnp.full((8, block), masked, f32) for _ in range(heads))
    bests = lax.fori_loop(low, mid, functools.partial(score_step, with_mask=True), bests)
    bests = lax.fori_loop(mid, query_block, functools.partial(score_step, with_mask=False), bests)
    bests = score_step(query_block, bests, True)
    bests = [jnp.max(best, axis=0, keepdims=True) for best in bests]

    def value_step(key_block, state):
        result = []
        for number in range(heads):
            total, gathered = state[2 * number : 2 * number + 2]
            weights = jnp.exp(score_ref[key_block, head_rows(number, block), :] - bests[number])
            value_rows = values_turned[key_block, head_rows(number, head_width), :]
            result += [
                total + eights(weights, jnp.sum),
                gathered + dot(value_rows, weights.astype(bf16)),
            ]
        return tuple(result)

    state = ()
    for number in range(heads):
        state += (jnp.zeros((8, block), f32), jnp.zeros((head_width, block), f32))
    state = lax.fori_loop(low, query_block + 1, value_step, state)
    columns = []
    for number in range(heads):
        total = jnp.sum(state[2 * number], axis=0, keepdims=True)
        columns.append(state[2 * number + 1] / total)
        log_ref[0, number : number + 1, :] = bests[number] + jnp.log(total)
    out_ref[...] = jnp.transpose(jnp.concatenate(columns, axis=0)).astype(bf16)


def backward_kernel(heads, block, first_head, merge, *refs):
    full_ref, high_ref, slope_ref, start_ref, log_ref, qkv_ref, grad_ref, out_ref = refs[:8]
    earlier_ref = refs[8] if merge else None
    result_ref = refs[9 if merge else 8]
    (
        queries_turned,
        grads_turned,
        keys_turned,
        query_stack,
        grad_stack,
        key_stack,
        value_stack,
        delta_rows,
        query_grads,
    ) = refs[10 if merge else 9 :]
    tokens, all_width = grad_ref.shape
    head_width = all_width // log_ref.shape[1]
    width = heads * head_width
    scale = head_width ** (-0.5)
    blocks = tokens // block
    key_block = pl.program_id(0)
    lanes = lane_masks(block, width, heads)

    def columns(kind):
        start = kind * all_width + first_head * head_width
        return slice(start, start + width)

    def target(kind):
        start = (kind * all_width + first_head * head_width) if merge else kind * width
        return slice(start, start + width)

    @pl.when(key_block == 0)
    def _():
        for number in range(blocks):
            rows = slice(number * block, (number + 1) * block)
            queries = qkv_ref[rows, columns(0)]
            queries_turned[number] = turned(queries.astype(f32) * scale).astype(bf16)
            query_stack[number] = head_stack(queries, lanes)
            keys_turned[number] = turned(qkv_ref[rows, columns(1)]).astype(bf16)
            grads = grad_ref[rows, columns(0)]
            grad_stack[number] = head_stack(grads, lanes)
            grads = grads.astype(f32)
            grads_turned[number] = turned(grads).astype(bf16)
            product = turned(grads * out_ref[rows, columns(0)].astype(f32))
            for head in range(heads):
                delta_rows[number, head : head + 1, :] = jnp.sum(
                    product[head_rows(head, head_width)], axis=0, keepdims=True
                )
            query_grads[number] = jnp.zeros((width, block), f32)

    key_row = pl.multiple_of(key_block * block, block)
    key_stack[...] = head_stack(qkv_ref[pl.ds(key_row, block), columns(1)], lanes)
    value_stack[...] = head_stack(qkv_ref[pl.ds(key_row, block), columns(2)], lanes)

    def step(query_block, state, with_mask):
        key_total, value_total = state
        scores = dot(key_stack[...], queries_turned[query_block])
        grad_weights = dot(value_stack[...], grads_turned[query_block])
        offsets = key_offsets(key_block, query_block, block)
        if with_mask:
            allowed = allowed_pairs(key_block, query_block, start_ref[query_block], block)
        weight_list, grad_list = [], []
        for number in range(heads):
            rows = head_rows(number, block)
            head = first_head + number
            part = scores[rows] + slope_ref[head] * offsets
            part = part - log_ref[query_block, head : head + 1, :]
            if with_mask:
                part = jnp.where(allowed, part, masked)
            probabilities = jnp.exp(part)
            delta = delta_rows[query_block, number : number + 1, :]
            grad_scores = (probabilities * (grad_weights[rows] - delta)).astype(bf16)
            weight_list.append(probabilities.astype(bf16))
            grad_list.append(grad_scores)
            rows = head_rows(number, head_width)
            query_grads[query_block, rows, :] += dot(keys_turned[key_block, rows, :], grad_scores)
        weight_row = jnp.concatenate(weight_list, axis=1)
        grad_row = jnp.concatenate(grad_list, axis=1)
        return (
            key_total + dot(grad_row, query_stack[query_block]),
            value_total + dot(weight_row, grad_stack[query_block]),
        )

    state = (jnp.zeros((block, width), f32), jnp.zeros((block, width), f32))
    state = step(key_block, state, True)
    full, high = full_ref[key_block], high_ref[key_block]
    state = lax.fori_loop(key_block + 1, full, functools.partial(step, with_mask=False), state)
    state = lax.fori_loop(full, high, functools.partial(step, with_mask=True), state)
    result_ref[pl.ds(key_row, block), target(1)] = (state[0] * scale).astype(bf16)
    result_ref[pl.ds(key_row, block), target(2)] = state[1].astype(bf16)
    if merge:
        other = first_head * head_width
        for kind in range(3):
            result_ref[pl.ds(key_row, block), kind * all_width : kind * all_width + other] = earlier_ref[
                pl.ds(key_row, block), kind * other : (kind + 1) * other
            ]

    @pl.when(key_block == blocks - 1)
    def _():
        for number in range(blocks):
            rows = slice(number * block, (number + 1) * block)
            result_ref[rows, target(0)] = jnp.transpose(query_grads[number] * scale).astype(bf16)


def block_plan(lengths, tokens, block):
    ends = jnp.cumsum(lengths)
    positions = jnp.arange(tokens, dtype=jnp.int32)
    passed = positions[:, None] >= ends[None, :]
    starts = jnp.max(jnp.where(passed, ends[None, :], 0), axis=1).astype(jnp.int32)
    finish = jnp.min(jnp.where(passed, tokens, ends[None, :]), axis=1).astype(jnp.int32)
    blocks = tokens // block
    number = jnp.arange(blocks, dtype=jnp.int32)
    first_start = starts[::block]
    last_start = starts[block - 1 :: block]
    low = first_start // block
    mid = jnp.clip((last_start + block - 1) // block, low, number)
    high = (finish[block - 1 :: block] - 1) // block + 1
    full = jnp.clip(finish[::block] // block, number + 1, high)
    return (starts.reshape(blocks, 1, block), low, mid, full, high)


def scalar_spec():
    return pl.BlockSpec(memory_space=pltpu.SMEM)


def whole_spec(shape):
    return pl.BlockSpec(shape, lambda step: (0,) * len(shape), pipeline_mode=pl.Buffered(1))


def attend_forward(qkv, plan, slopes, heads, block):
    tokens, triple = qkv.shape
    width = triple // 3
    blocks = tokens // block
    starts, low, mid, full, high = plan
    return pl.pallas_call(
        functools.partial(forward_kernel, heads, block),
        grid=(blocks,),
        in_specs=[
            scalar_spec(),
            scalar_spec(),
            scalar_spec(),
            whole_spec((blocks, 1, block)),
            whole_spec((tokens, triple)),
        ],
        out_specs=[
            pl.BlockSpec((block, width), lambda step: (step, 0)),
            pl.BlockSpec((1, heads, block), lambda step: (step, 0, 0)),
        ],
        out_shape=[
            jax.ShapeDtypeStruct((tokens, width), bf16),
            jax.ShapeDtypeStruct((blocks, heads, block), f32),
        ],
        scratch_shapes=[
            pltpu.VMEM((blocks, width, block), bf16),
            pltpu.VMEM((blocks, heads * block, width), bf16),
            pltpu.VMEM((blocks, heads * block, block), f32),
        ],
        compiler_params=pltpu.CompilerParams(
            dimension_semantics=("arbitrary",), vmem_limit_bytes=24 * 1024 * 1024
        ),
        cost_estimate=pl.CostEstimate(
            flops=3 * tokens * tokens * 256 * heads,
            bytes_accessed=10 * tokens * width,
            transcendentals=tokens * tokens * heads // 2,
        ),
        name="attend_forward",
    )(low, mid, slopes, starts, qkv)


def attend_backward(qkv, grads, outputs, logs, plan, slopes, heads, block, first_head, earlier):
    tokens, triple = qkv.shape
    all_width = triple // 3
    all_heads = logs.shape[1]
    width = all_width // all_heads * heads
    blocks = tokens // block
    starts, low, mid, full, high = plan
    merge = earlier is not None
    result_width = triple if merge else 3 * width
    operands = [full, high, slopes, starts, logs, qkv, grads, outputs]
    specs = [scalar_spec() for _ in range(3)] + [whole_spec(entry.shape) for entry in operands[3:]]
    if merge:
        operands.append(earlier)
        specs.append(whole_spec(earlier.shape))
    return pl.pallas_call(
        functools.partial(backward_kernel, heads, block, first_head, merge),
        grid=(blocks,),
        in_specs=specs,
        out_specs=pl.BlockSpec((tokens, result_width), lambda step: (0, 0)),
        out_shape=jax.ShapeDtypeStruct((tokens, result_width), bf16),
        scratch_shapes=[
            pltpu.VMEM((blocks, width, block), bf16),
            pltpu.VMEM((blocks, width, block), bf16),
            pltpu.VMEM((blocks, width, block), bf16),
            pltpu.VMEM((blocks, heads * block, width), bf16),
            pltpu.VMEM((blocks, heads * block, width), bf16),
            pltpu.VMEM((heads * block, width), bf16),
            pltpu.VMEM((heads * block, width), bf16),
            pltpu.VMEM((blocks, heads, block), f32),
            pltpu.VMEM((blocks, width, block), f32),
        ],
        compiler_params=pltpu.CompilerParams(
            dimension_semantics=("arbitrary",), vmem_limit_bytes=24 * 1024 * 1024
        ),
        cost_estimate=pl.CostEstimate(
            flops=8 * tokens * tokens * 256 * heads,
            bytes_accessed=20 * tokens * width,
            transcendentals=tokens * tokens * heads // 2,
        ),
        name="attend_backward",
    )(*operands)


def hidden_backward_kernel(own_ref, other_ref, weight_ref, slope_ref, result_ref, total_ref):
    rows = own_ref.shape[0]
    total = jnp.zeros(total_ref.shape, f32)
    for number, ref in enumerate((own_ref, other_ref)):
        part = slice(number * rows, (number + 1) * rows)
        grads = dot_right(ref[...], weight_ref[...]) * slope_ref[part, :].astype(f32)
        grads = grads.astype(bf16)
        result_ref[part, :] = grads
        total = total + jnp.sum(grads.astype(f32), axis=0, keepdims=True)
    total_ref[...] = total


def hidden_backward(weight, cot_own, cot_other, slopes):
    rows, width = cot_own.shape
    breadth = slopes.shape[1]
    tile = min(256, breadth)
    return pl.pallas_call(
        hidden_backward_kernel,
        grid=(breadth // tile,),
        in_specs=[
            whole_spec((rows, width)),
            whole_spec((rows, width)),
            pl.BlockSpec((tile, width), lambda step: (step, 0)),
            pl.BlockSpec((2 * rows, tile), lambda step: (0, step)),
        ],
        out_specs=[
            pl.BlockSpec((2 * rows, tile), lambda step: (0, step)),
            pl.BlockSpec((1, tile), lambda step: (0, step)),
        ],
        out_shape=[
            jax.ShapeDtypeStruct((2 * rows, breadth), bf16),
            jax.ShapeDtypeStruct((1, breadth), f32),
        ],
        compiler_params=pltpu.CompilerParams(
            dimension_semantics=("arbitrary",), vmem_limit_bytes=12 * 1024 * 1024
        ),
        cost_estimate=pl.CostEstimate(flops=1, bytes_accessed=1, transcendentals=0),
        name="hidden_backward",
    )(cot_own, cot_other, weight, slopes)


def up_backward_kernel(grads_ref, weight_ref, result_ref):
    result_ref[...] = dot_right(grads_ref[...], weight_ref[...]).astype(result_ref.dtype)


def up_backward(weight, grads, number, kind_of):
    rows, breadth = grads.shape[0] // 2, grads.shape[1]
    width = weight.shape[0]
    tile = width // 4
    return pl.pallas_call(
        up_backward_kernel,
        grid=(4,),
        in_specs=[
            pl.BlockSpec((rows, breadth), lambda step: (number, 0)),
            pl.BlockSpec((tile, breadth), lambda step: (step, 0)),
        ],
        out_specs=pl.BlockSpec((rows, tile), lambda step: (0, step)),
        out_shape=jax.ShapeDtypeStruct((rows, width), kind_of),
        compiler_params=pltpu.CompilerParams(
            dimension_semantics=("arbitrary",), vmem_limit_bytes=12 * 1024 * 1024
        ),
        cost_estimate=pl.CostEstimate(flops=1, bytes_accessed=1, transcendentals=0),
        name="up_backward",
    )(grads, weight)


def down_projection_kernel(hidden_ref, weight_ref, result_ref):
    result_ref[...] = dot(hidden_ref[...], weight_ref[...]).astype(result_ref.dtype)


def down_projection(hidden, weight):
    rows, breadth = hidden.shape
    width = weight.shape[1]
    tile = min(256, rows)
    return pl.pallas_call(
        down_projection_kernel,
        grid=(rows // tile,),
        in_specs=[
            pl.BlockSpec((tile, breadth), lambda step: (step, 0)),
            whole_spec((breadth, width)),
        ],
        out_specs=pl.BlockSpec((tile, width), lambda step: (step, 0)),
        out_shape=jax.ShapeDtypeStruct((rows, width), bf16),
        compiler_params=pltpu.CompilerParams(
            dimension_semantics=("arbitrary",), vmem_limit_bytes=14 * 1024 * 1024
        ),
        cost_estimate=pl.CostEstimate(flops=1, bytes_accessed=1, transcendentals=0),
        name="down_projection",
    )(hidden, weight)


def up_gradient_kernel(own_ref, other_ref, grads_ref, result_ref, act_turned):
    rows, width = own_ref.shape
    step = 256

    @pl.when(pl.program_id(0) == 0)
    def _():
        for number, ref in enumerate((own_ref, other_ref)):
            for row in range(0, rows, step):
                first = number * rows + row
                for column in range(0, width, step):
                    block = ref[row : row + step, column : column + step]
                    act_turned[column : column + step, first : first + step] = turned(block).astype(bf16)

    result_ref[...] = dot(act_turned[...], grads_ref[...]).astype(bf16)


def up_gradient(act_own, act_other, grads):
    rows, width = act_own.shape
    breadth = grads.shape[1]
    tile = min(512, breadth)
    return pl.pallas_call(
        up_gradient_kernel,
        grid=(breadth // tile,),
        in_specs=[
            whole_spec((rows, width)),
            whole_spec((rows, width)),
            pl.BlockSpec((2 * rows, tile), lambda step: (0, step)),
        ],
        out_specs=pl.BlockSpec((width, tile), lambda step: (0, step)),
        out_shape=jax.ShapeDtypeStruct((width, breadth), bf16),
        scratch_shapes=[pltpu.VMEM((width, 2 * rows), bf16)],
        compiler_params=pltpu.CompilerParams(
            dimension_semantics=("arbitrary",), vmem_limit_bytes=16 * 1024 * 1024
        ),
        cost_estimate=pl.CostEstimate(flops=1, bytes_accessed=1, transcendentals=0),
        name="up_gradient",
    )(act_own, act_other, grads)


def together(*values):
    return lax.optimization_barrier(tuple(values))


def ordered(own, other, bit, axis=0):
    first = jnp.where(bit == 0, own, other)
    second = jnp.where(bit == 0, other, own)
    return jnp.stack([first, second], axis=axis)


class Moves:
    def __init__(self):
        self.shards = lax.axis_size("shard")
        self.reps = lax.axis_size("rep")
        self.half = self.shards // 2
        self.chips = self.reps // 2
        self.shard = lax.axis_index("shard")
        self.rep = lax.axis_index("rep")
        self.core = self.rep & 1
        self.chip = self.rep >> 1
        self.side = lax.div(self.shard, self.half)
        self.member = lax.rem(self.shard, self.half) + self.core * self.half

    def core_swap(self, part):
        return lax.ppermute(part, "rep", [(r, r ^ 1) for r in range(self.reps)])

    def chip_swap(self, part, bits):
        return lax.ppermute(part, "rep", [(r, r ^ (2 * bits)) for r in range(self.reps)])

    def shard_swap(self, part, bits):
        return lax.ppermute(part, "shard", [(s, s ^ bits) for s in range(self.shards)])

    def shard_bit(self, bits):
        return lax.div(self.shard, bits) & 1

    def low_bits(self):
        bits, result = 1, []
        while bits < self.half:
            result.append(bits)
            bits *= 2
        return result

    def home_send(self, part):
        pairs = []
        for rep in range(self.reps):
            for shard in range(self.shards):
                if shard // self.half != rep % 2:
                    to_shard = (shard + self.half) % self.shards
                    pairs.append((rep * self.shards + shard, (rep ^ 1) * self.shards + to_shard))
        return lax.ppermute(part, ("rep", "shard"), pairs)

    def home_join(self, part, other):
        return jnp.where(self.side == self.core, part, other)

    def half_gather(self, part):
        stack = part[None]
        for bits in self.low_bits():
            own = stack
            stack = ordered(own, self.shard_swap(own, bits), self.shard_bit(bits))
            stack = stack.reshape((-1,) + part.shape)
        return stack

    def cores_gather(self, stack):
        stack = ordered(stack, self.core_swap(stack), self.core)
        return stack.reshape((-1,) + stack.shape[2:])

    def exchange_bit(self, stack, bit, swap):
        sources, targets = stack.shape[:2]
        stack = stack.reshape((sources, 2, targets // 2) + stack.shape[2:])
        own, other = pick(stack, bit, 1), swap(pick(stack, 1 - bit, 1))
        return ordered(own, other, bit, 1).reshape((2 * sources,) + own.shape[1:])

    def half_exchange(self, stack):
        stack = stack[None]
        for bits in reversed(self.low_bits()):
            swap = functools.partial(self.shard_swap, bits=bits)
            stack = self.exchange_bit(stack, self.shard_bit(bits), swap)
        return stack.reshape((self.half,) + stack.shape[2:])

    def cores_exchange(self, stack):
        return self.exchange_bit(stack[None], self.core, self.core_swap)

    def members_exchange(self, stack):
        for bits in reversed(self.low_bits()):
            swap = functools.partial(self.shard_swap, bits=bits)
            stack = self.exchange_bit(stack, self.shard_bit(bits), swap)
        return stack.reshape((self.shards,) + stack.shape[2:])

    def reduce_bit(self, stack, bit, swap):
        stack = stack.reshape((2, stack.shape[0] // 2) + stack.shape[1:])
        other = swap(pick(stack, 1 - bit).astype(bf16))
        return pick(stack, bit).astype(f32) + other.astype(f32)

    def spread_open(self, part):
        if self.chips == 4:
            return (self.chip_swap(part, 1), self.chip_swap(part, 2))
        held, bits = [part], 1
        while bits < self.chips:
            held = held + [self.chip_swap(piece, bits) for piece in held]
            bits *= 2
        return tuple(held[1:])

    def spread_close(self, state):
        if self.chips == 4:
            by_x, by_y = state
            cut, axis = by_x.shape[-2] // 2, by_x.ndim - 2
            far = [
                self.chip_swap(by_x[..., :cut, :], 2),
                self.chip_swap(by_y[..., cut:, :], 1),
            ]
            return (by_x, by_y, jnp.concatenate(far, axis=axis))
        return state

    def far_open(self, states):
        if self.chips != 4:
            return ()
        cut = states[0][0].shape[0] // 2
        return (
            self.chip_swap(jnp.concatenate([by_x[:cut] for by_x, _ in states], axis=0), 2),
            self.chip_swap(jnp.concatenate([by_y[cut:] for _, by_y in states], axis=0), 1),
        )

    def far_parts(self, states, far):
        if self.chips != 4:
            return [[(k + 1, 0, part) for k, part in enumerate(state)] for state in states]
        cut = states[0][0].shape[0] // 2
        result = []
        for number, (by_x, by_y) in enumerate(states):
            rows = slice(number * cut, (number + 1) * cut)
            result.append([(1, 0, by_x), (2, 0, by_y), (3, 0, far[0][rows]), (3, cut, far[1][rows])])
        return result

    def chips_gather(self, part, axis, state=None):
        shape = part.shape[:axis] + (self.chips,) + part.shape[axis:]
        stack = place(jnp.zeros(shape, part.dtype), part, self.chip, axis)
        others = self.spread_close(self.spread_open(part) if state is None else state)
        for number, piece in enumerate(others):
            stack = place(stack, piece, self.chip ^ (number + 1), axis)
        return stack

    def reduce_open(self, stack, axis):
        return self.reduce_start(self.reduce_cut(stack, axis), axis)

    def reduce_cut(self, stack, axis):
        if self.chips != 4:
            return (stack,)
        shape = stack.shape[:axis] + (2, 2) + stack.shape[axis + 1 :]
        stack = stack.reshape(shape)
        bit_x, bit_y = self.chip & 1, self.chip >> 1
        cut = shape[0] // 2
        first, second = stack[:cut], stack[cut:]
        return (
            pick(first, bit_x, axis + 1),
            pick(second, bit_y, axis),
            pick(first, 1 - bit_x, axis + 1),
            pick(second, 1 - bit_y, axis),
        )

    def reduce_start(self, parts, axis):
        if self.chips == 4:
            first, second, send_first, send_second = parts
            return (first, second, self.chip_swap(send_first, 1), self.chip_swap(send_second, 2))
        (stack,) = parts
        count = self.chips
        stack = stack.astype(f32)
        while count > 1:
            count //= 2
            shape = stack.shape[:axis] + (2, count) + stack.shape[axis + 1 :]
            stack = stack.reshape(shape)
            bit = lax.div(self.chip, count) & 1
            got = self.chip_swap(pick(stack, 1 - bit, axis).astype(bf16), count)
            stack = pick(stack, bit, axis) + got.astype(f32)
        return (pick(stack, 0, axis).astype(bf16),)

    def reduce_add(self, state):
        if self.chips != 4:
            return state
        first, second, got_first, got_second = state
        first = (first.astype(f32) + got_first.astype(f32)).astype(bf16)
        second = (second.astype(f32) + got_second.astype(f32)).astype(bf16)
        return (first, second)

    def reduce_send(self, state, axis):
        if self.chips != 4:
            return state
        first, second = state
        bit_x, bit_y = self.chip & 1, self.chip >> 1
        got_first = self.chip_swap(pick(first, 1 - bit_y, axis), 2)
        got_second = self.chip_swap(pick(second, 1 - bit_x, axis), 1)
        return (pick(first, bit_y, axis), pick(second, bit_x, axis), got_first, got_second)

    def reduce_final(self, state):
        if self.chips != 4:
            return state[0]
        first, second, got_first, got_second = state
        first = first.astype(f32) + got_first.astype(f32)
        second = second.astype(f32) + got_second.astype(f32)
        return jnp.concatenate([first, second], axis=0).astype(bf16)

    def reduce_close(self, state, axis):
        return self.reduce_final(self.reduce_send(state, axis))

    def core_pair(self, part):
        other = self.core_swap(part)
        first = jnp.where(self.core == 0, part, other)
        second = jnp.where(self.core == 0, other, part)
        return first, second

    def sum_reps(self, vector):
        bits = 1
        while bits < self.reps:
            vector = vector + lax.ppermute(vector, "rep", [(r, r ^ bits) for r in range(self.reps)])
            bits *= 2
        return vector

    def sum_shards(self, vector):
        bits = 1
        while bits < self.shards:
            vector = vector + self.shard_swap(vector, bits)
            bits *= 2
        return vector


def stats_kernel(decay_rate, gradient_ref, old_ref, rows_ref, lane_rows_ref, sums_ref, total_ref, partial):
    step = pl.program_id(0)
    rows, columns = gradient_ref.shape

    @pl.when(step == 0)
    def _():
        partial[...] = jnp.zeros_like(partial)
        total_ref[...] = jnp.zeros_like(total_ref)

    gradient = gradient_ref[...].astype(f32)
    square = gradient * gradient
    row_mean = jnp.sum(square, axis=1, keepdims=True) / columns
    old = jnp.transpose(jnp.broadcast_to(old_ref[...], (128, rows)))[:, 0:1]
    rows_new = decay_rate * old + (1.0 - decay_rate) * (row_mean + eps_second)
    rows_ref[...] = rows_new
    lane_rows_ref[...] = jnp.transpose(jnp.broadcast_to(rows_new, (rows, 128)))[0:1, :]
    total_ref[...] += jnp.broadcast_to(jnp.sum(rows_new, axis=0, keepdims=True), (1, 128))
    partial[0:8, :] += eights(square, jnp.sum)
    partial[8:16, :] += eights(square * (1.0 / rows_new), jnp.sum)

    @pl.when(step == pl.num_programs(0) - 1)
    def _():
        sums_ref[0:1, :] = jnp.sum(partial[0:8, :], axis=0, keepdims=True)
        sums_ref[1:2, :] = jnp.sum(partial[8:16, :], axis=0, keepdims=True)


def factor_stats(gradient, rows_old, decay_rate):
    height, breadth = gradient.shape
    rows = min(256 if breadth <= 1024 else 128, height)
    return pl.pallas_call(
        functools.partial(stats_kernel, decay_rate),
        grid=(height // rows,),
        in_specs=[
            pl.BlockSpec((rows, breadth), lambda step: (step, 0)),
            pl.BlockSpec((1, rows), lambda step: (0, step)),
        ],
        out_specs=[
            pl.BlockSpec((rows, 1), lambda step: (step, 0)),
            pl.BlockSpec((1, rows), lambda step: (0, step)),
            pl.BlockSpec((2, breadth), lambda step: (0, 0)),
            pl.BlockSpec((1, 128), lambda step: (0, 0)),
        ],
        out_shape=[
            jax.ShapeDtypeStruct((height, 1), f32),
            jax.ShapeDtypeStruct((1, height), f32),
            jax.ShapeDtypeStruct((2, breadth), f32),
            jax.ShapeDtypeStruct((1, 128), f32),
        ],
        scratch_shapes=[pltpu.VMEM((16, breadth), f32)],
        compiler_params=pltpu.CompilerParams(
            dimension_semantics=("arbitrary",), vmem_limit_bytes=12 * 1024 * 1024
        ),
        name="factor_stats",
    )(gradient, rows_old)


def apply_kernel(
    decay_rate,
    height,
    gradient_ref,
    weight_ref,
    rows_ref,
    sums_ref,
    scalar_ref,
    old_ref,
    gradient_out,
    weight_out,
    copy_out,
    cols_out,
    rms_out,
    col_factor,
):
    columns = gradient_ref.shape[1]

    @pl.when(pl.program_id(0) == 0)
    def _():
        cols_new = decay_rate * old_ref[...] + (1.0 - decay_rate) * (
            sums_ref[0:1, :] / height + eps_second
        )
        row_mean = scalar_ref[0:1, 0:1] / height
        weight_mean = scalar_ref[1:2, 0:1] / (height * columns)
        scaled = jnp.sum(sums_ref[1:2, :] / cols_new, axis=1, keepdims=True)
        rms_update = jnp.sqrt(row_mean / (height * columns) * scaled)
        factor = rate_step * jnp.sqrt(weight_mean) * jnp.sqrt(row_mean)
        factor = factor / jnp.maximum(1.0, rms_update / clip_level)
        col_factor[...] = factor * lax.rsqrt(cols_new)
        cols_out[...] = cols_new
        rms_out[...] = jnp.broadcast_to(rms_update, (1, 128))

    gradient = gradient_ref[...].astype(f32)
    new_weight = weight_ref[...] - gradient * lax.rsqrt(rows_ref[...]) * col_factor[...]
    gradient_out[...] = gradient
    weight_out[...] = new_weight
    copy_out[...] = new_weight.astype(bf16)


def factor_apply(gradient, weight, rows_new, sums, scalars, cols_old, height, decay_rate):
    own_height, breadth = gradient.shape
    rows = min(256 if breadth <= 1024 else 64, own_height)

    def rows_spec():
        return pl.BlockSpec((rows, breadth), lambda step: (step, 0))

    def row_spec(count, wide):
        return pl.BlockSpec((count, wide), lambda step: (0, 0))

    return pl.pallas_call(
        functools.partial(apply_kernel, decay_rate, height),
        grid=(own_height // rows,),
        in_specs=[
            rows_spec(),
            rows_spec(),
            pl.BlockSpec((rows, 1), lambda step: (step, 0)),
            row_spec(2, breadth),
            row_spec(2, 128),
            row_spec(1, breadth),
        ],
        out_specs=[rows_spec(), rows_spec(), rows_spec(), row_spec(1, breadth), row_spec(1, 128)],
        out_shape=[
            jax.ShapeDtypeStruct((own_height, breadth), f32),
            jax.ShapeDtypeStruct((own_height, breadth), f32),
            jax.ShapeDtypeStruct((own_height, breadth), bf16),
            jax.ShapeDtypeStruct((1, breadth), f32),
            jax.ShapeDtypeStruct((1, 128), f32),
        ],
        scratch_shapes=[pltpu.VMEM((1, breadth), f32)],
        compiler_params=pltpu.CompilerParams(
            dimension_semantics=("arbitrary",), vmem_limit_bytes=14 * 1024 * 1024
        ),
        name="factor_apply",
    )(gradient, weight, rows_new, sums, scalars, cols_old)


def summed(moves, entries):
    total = moves.sum_shards(jnp.concatenate(entries, axis=1))
    result, offset = [], 0
    for entry in entries:
        result.append(total[:, offset : offset + entry.shape[1]])
        offset += entry.shape[1]
    return result


def on_device(
    tokens,
    cotangent,
    seq_lengths,
    qkv_weight,
    out_weight,
    up_weight,
    down_weight,
    vectors,
    row_state,
    down_rows,
    col_state,
    vector_state,
):
    moves = Moves()
    shards, half, chips, core = moves.shards, moves.half, moves.chips, moves.core
    row_count, width = tokens.shape
    hidden_width = up_weight.shape[1]
    group_rows = row_count * shards
    heads = HEADS // shards
    head_width = width // HEADS
    span = heads * head_width
    member = moves.member
    decay_rate = 1.0 - STEP ** (-0.8)
    head_number = (member * heads + jnp.arange(heads, dtype=jnp.int32)).astype(f32)
    slopes = jnp.exp2(-8.0 * (head_number + 1.0) / HEADS)

    gain_one = vectors[0:width]
    shift_one = vectors[width : 2 * width]
    bias_query = vectors[2 * width : 3 * width]
    bias_value = vectors[3 * width : 4 * width]
    bias_out = vectors[4 * width : 5 * width]
    gain_two = vectors[5 * width : 6 * width]
    shift_two = vectors[6 * width : 7 * width]
    bias_up = vectors[7 * width : 7 * width + hidden_width]
    bias_down = vectors[7 * width + hidden_width :]

    other_tokens = moves.home_send(tokens)
    other_lengths = moves.core_swap(seq_lengths)
    lengths = jnp.where(moves.side == core, seq_lengths, other_lengths)[0]
    plan = block_plan(lengths, group_rows, BLOCK)
    rows_z = width // shards
    rows_piece = rows_z // chips
    my_rows = cut_rows(qkv_weight, moves.chip * rows_piece, rows_piece)
    my_rows = my_rows.astype(bf16)
    my_blocks = []
    for number in range(half):
        kinds = []
        for kind in range(3):
            first = kind * width + number * span
            second = first + half * span
            kinds.append(
                jnp.where(
                    core == 0, my_rows[:, first : first + span], my_rows[:, second : second + span]
                )
            )
        my_blocks.append(jnp.concatenate(kinds, axis=1))
    qkv_part = moves.half_exchange(jnp.stack(my_blocks))
    half_cols = hidden_width // (2 * shards)
    up_wide = shards * half_cols
    out_wide = width // 2
    down_piece = half_cols // chips

    def core_half(values):
        parts = []
        for number in range(shards):
            start = 2 * number * half_cols
            first = values[..., start : start + half_cols]
            second = values[..., start + half_cols : start + 2 * half_cols]
            parts.append(jnp.where(core == 0, first, second))
        return jnp.concatenate(parts, axis=-1)

    up_own = core_half(up_weight).astype(bf16).reshape(chips, rows_piece, up_wide)
    out_own = jnp.where(core == 0, out_weight[:, :out_wide], out_weight[:, out_wide:]).astype(bf16)
    out_own = out_own.reshape(chips, rows_piece, out_wide)
    down_own = cut_rows(down_weight, core * half_cols, half_cols).astype(bf16)
    fold = down_piece // rows_piece
    down_own = down_own.reshape(chips, fold, rows_piece, width)
    my_down = pick(down_own, moves.chip)
    weight_piece = jnp.concatenate(
        [pick(up_own, moves.chip), pick(out_own, moves.chip)] + [my_down[k] for k in range(fold)],
        axis=1,
    )
    near_pieces, bits = [weight_piece], 1
    while bits < half:
        near_pieces = near_pieces + [moves.shard_swap(piece, bits) for piece in near_pieces]
        bits *= 2
    near_pieces = near_pieces[1:]
    weights = [qkv_weight, out_weight, up_weight, down_weight]
    weight_sums = [jnp.sum(weight * weight) for weight in weights]
    other_tokens, qkv_part, near_pieces, weight_piece, plan, weight_sums = together(
        other_tokens, qkv_part, near_pieces, weight_piece, plan, weight_sums
    )
    home_tokens = moves.home_join(tokens, other_tokens)
    far_piece = moves.shard_swap(weight_piece, half)
    near_open = [moves.spread_open(piece) for piece in near_pieces]
    qkv_far = moves.shard_swap(qkv_part, half)
    qkv_far, near_open = together(qkv_far, near_open)
    qkv_part = ordered(qkv_part, qkv_far, moves.side).reshape(shards, rows_piece, 3 * span)
    qkv_cols = moves.chips_gather(qkv_part, 1).reshape(width, 3 * span)
    inputs = home_tokens.astype(f32)
    normed_one, inv_std_one = norm_parts(inputs)
    act_one = (normed_one * gain_one + shift_one).astype(bf16)
    act_half = moves.half_gather(act_one)

    act_half, qkv_cols, far_piece = together(act_half, qkv_cols, far_piece)
    near_far = moves.far_open(near_open)
    act_all = moves.cores_gather(act_half).reshape(group_rows, width)
    far_open = moves.spread_open(far_piece)
    far_pieces, bits = [far_piece], 1
    while bits < half:
        far_pieces = far_pieces + [moves.shard_swap(piece, bits) for piece in far_pieces]
        bits *= 2
    far_pieces = far_pieces[1:]

    bias_q_part = cut_rows(bias_query, member * span, span)
    bias_v_part = cut_rows(bias_value, member * span, span)
    qkv_bias = jnp.concatenate([bias_q_part, jnp.zeros_like(bias_q_part), bias_v_part])
    qkv_rows = (dot(act_all, qkv_cols) + qkv_bias).astype(bf16)
    attended_cols, logs = attend_forward(qkv_rows, plan, slopes, heads, BLOCK)
    attended_cols, far_open, far_pieces, near_far = together(
        attended_cols, far_open, far_pieces, near_far
    )
    attended_parts = moves.cores_exchange(attended_cols.reshape(shards, row_count, span))
    attended_parts = moves.members_exchange(attended_parts)
    second_far = moves.far_open([far_open])
    last_states = [moves.spread_open(piece) for piece in far_pieces]
    attended_parts, second_far, last_states, cotangent = together(
        attended_parts, second_far, last_states, cotangent
    )
    last_far = moves.far_open(last_states)
    other_cot = moves.home_send(cotangent)
    attended = jnp.concatenate([attended_parts[k] for k in range(shards)], axis=1)

    up_all = place(jnp.zeros((shards, chips, rows_piece, up_wide), bf16), up_own, moves.shard)
    out_all = place(jnp.zeros((shards, chips, rows_piece, out_wide), bf16), out_own, moves.shard)
    down_all = place(jnp.zeros((shards, chips, fold, rows_piece, width), bf16), down_own, moves.shard)
    pieces = near_pieces + [far_piece] + far_pieces
    parts_of = moves.far_parts(near_open, near_far) + moves.far_parts([far_open], second_far)
    parts_of += moves.far_parts(last_states, last_far)
    for number, (piece, parts) in enumerate(zip(pieces, parts_of)):
        plane = moves.shard ^ (number + 1)
        for far, row, rows in [(0, 0, piece)] + parts:
            chip = moves.chip ^ far
            up_all = lax.dynamic_update_slice(
                up_all, rows[None, None, :, :up_wide], (plane, chip, row, 0), allow_negative_indices=False
            )
            out_all = lax.dynamic_update_slice(
                out_all, rows[None, None, :, up_wide : up_wide + out_wide], (plane, chip, row, 0), allow_negative_indices=False
            )
            start = up_wide + out_wide
            folds = [rows[:, start + k * width : start + (k + 1) * width] for k in range(fold)]
            down_all = lax.dynamic_update_slice(
                down_all, jnp.stack(folds)[None, None], (plane, chip, 0, row, 0), allow_negative_indices=False
            )
    up_half = up_all.reshape(width, up_wide)
    down_half = down_all.reshape(up_wide, width)
    out_first, out_second = moves.core_pair(out_all.reshape(width, out_wide))
    out_low = jnp.concatenate([out_first, out_second], axis=1)
    residual = inputs + dot(attended, out_low) + bias_out
    normed_two, inv_std_two = norm_parts(residual)
    act_two = (normed_two * gain_two + shift_two).astype(bf16)

    act_two_other, attended_other = together(
        moves.core_swap(act_two), moves.core_swap(attended)
    )
    act_two_pair = jnp.concatenate([act_two, act_two_other], axis=0)
    attended_pair = jnp.concatenate([attended, attended_other], axis=0)
    bias_up_half = core_half(bias_up)
    up_pair = dot(act_two_pair, up_half) + bias_up_half
    hidden_pair = gelu_value(up_pair).astype(bf16)
    slope_pair = gelu_slope(up_pair).astype(bf16)
    hidden_pair, slope_pair, other_cot = together(hidden_pair, slope_pair, other_cot)
    home_cot = moves.home_join(cotangent, other_cot)
    cot_other = moves.core_swap(home_cot)
    cot_pair = jnp.concatenate([home_cot, cot_other], axis=0)
    down_terms = dot_rows(hidden_pair, cot_pair).astype(bf16)
    down_state = moves.reduce_cut(down_terms.reshape(shards, chips, down_piece, width), 1)
    slope_pair, down_state = together(slope_pair, down_state)
    down_state = moves.reduce_start(down_state, 1)
    grad_y = home_cot.astype(f32)
    grad_bias_down = jnp.sum(grad_y, axis=0)
    grad_up_pair, grad_bias_up = hidden_backward(down_half, home_cot, cot_other, slope_pair)
    grad_bias_up = grad_bias_up.reshape(-1)
    back_other = moves.core_swap(up_backward(up_half, grad_up_pair, 1, bf16))
    up_terms = up_gradient(act_two, act_two_other, grad_up_pair)
    down_pair = down_projection(hidden_pair, down_half)
    back_other, down_pair, up_terms, down_state = together(
        back_other, down_pair, up_terms, down_state
    )
    up_cut = moves.reduce_cut(up_terms.reshape(shards, chips, rows_piece, up_wide), 1)
    down_sums = moves.reduce_add(down_state)
    grad_act_two = up_backward(up_half, grad_up_pair, 0, f32) + back_other.astype(f32)
    grad_gain_two = jnp.sum(grad_act_two * normed_two, axis=0)
    grad_shift_two = jnp.sum(grad_act_two, axis=0)
    grad_residual = grad_y + norm_back(grad_act_two, normed_two, inv_std_two, gain_two)
    grad_attn = grad_residual.astype(bf16)
    grad_bias_out = jnp.sum(grad_attn, axis=0, dtype=f32)
    to_members = jnp.stack(
        [
            dot_right(grad_attn, out_low[k * span : (k + 1) * span]).astype(bf16)
            for k in range(shards)
        ]
    )
    attn_halves = [grad_attn[:, :out_wide], grad_attn[:, out_wide:]]
    attn_own = jnp.where(core == 0, attn_halves[0], attn_halves[1])
    attn_other = jnp.where(core == 0, attn_halves[1], attn_halves[0])
    down_other = moves.core_swap(down_pair[row_count:])
    grad_heads, attn_other, up_cut, down_sums, down_other = together(
        moves.cores_exchange(to_members), moves.core_swap(attn_other), up_cut, down_sums, down_other
    )
    attn_pair = jnp.concatenate([attn_own, attn_other], axis=0)
    grad_heads = moves.members_exchange(grad_heads).reshape(group_rows, span)
    up_state = moves.reduce_start(up_cut, 1)
    down_mid = moves.reduce_close(down_sums, 1)
    block_out = residual + down_pair[:row_count].astype(f32) + down_other.astype(f32) + bias_down
    block_out = block_out.astype(bf16)

    out_terms = dot_rows(attended_pair, attn_pair).astype(bf16)
    def shards_halve(piece, bits):
        piece = piece.reshape((piece.shape[0] // 2, 2) + piece.shape[1:])
        bit = moves.shard_bit(bits)
        return pick(piece, bit, 1), moves.shard_swap(pick(piece, 1 - bit, 1), bits)

    def halved(state):
        own, other = state
        return (own.astype(f32) + other.astype(f32)).astype(bf16)

    def shards_sum(piece):
        rows = piece.shape[1]
        return lax.psum_scatter(
            piece.reshape(shards * rows, piece.shape[2]), "shard", scatter_dimension=0, tiled=True
        )

    grad_heads, down_mid, out_terms, block_out = together(
        grad_heads, down_mid, out_terms, block_out
    )
    block_other = moves.home_send(block_out)
    down_owned = shards_sum(down_mid)
    out_state = moves.reduce_open(out_terms.reshape(shards, chips, rows_piece, out_wide), 1)
    attend_args = (plan, slopes)
    parts = 2 if heads % 4 == 0 else 1
    part_heads = heads // parts
    grad_qkv = attend_backward(
        qkv_rows, grad_heads, attended_cols, logs, *attend_args, part_heads, BLOCK, 0, None
    )
    grad_qkv, up_state, out_state = together(grad_qkv, up_state, out_state)
    up_sums, out_sums = moves.reduce_add(up_state), moves.reduce_add(out_state)
    grad_qkv, up_sums, out_sums = together(grad_qkv, up_sums, out_sums)
    up_out_state = [
        jnp.concatenate([up_part, out_part], axis=-1) for up_part, out_part in zip(up_sums, out_sums)
    ]
    if parts == 2:
        grad_qkv = attend_backward(
            qkv_rows, grad_heads, attended_cols, logs, *attend_args, part_heads, BLOCK, part_heads, grad_qkv
        )
    grad_qkv, up_out_state, block_other, down_owned = together(
        grad_qkv, moves.reduce_send(up_out_state, 1), block_other, down_owned
    )
    block_out = moves.home_join(block_out, block_other)
    up_out_piece = moves.reduce_final(up_out_state)
    up_out_state = shards_halve(up_out_piece, 1)

    grad_bias_q_part = jnp.sum(grad_qkv[:, :span], axis=0, dtype=f32)
    grad_bias_v_part = jnp.sum(grad_qkv[:, 2 * span :], axis=0, dtype=f32)

    grad_halves = grad_qkv.reshape(2, half * row_count, 3 * span)
    sent = dot_right(pick(grad_halves, 1 - core), qkv_cols).astype(bf16)
    sent = moves.core_swap(sent)
    qkv_terms = dot_rows(act_all, grad_qkv).astype(bf16)
    qkv_terms = qkv_terms.reshape(shards, chips, rows_piece, 3 * span)
    qkv_state = moves.reduce_open(qkv_terms, 1)
    back = dot_right(pick(grad_halves, core), qkv_cols) + sent.astype(f32)
    qkv_state, back = together(qkv_state, back)

    back = back.reshape(half, row_count, width)
    low_bits = list(reversed(moves.low_bits()))
    for bits in low_bits[:-1]:
        back = moves.reduce_bit(
            back, moves.shard_bit(bits), functools.partial(moves.shard_swap, bits=bits)
        )
    back = back.reshape((2, -1) + back.shape[1:])
    back_bit = moves.shard_bit(low_bits[-1])
    back_other = moves.shard_swap(pick(back, 1 - back_bit).astype(bf16), low_bits[-1])
    qkv_state = moves.reduce_send(moves.reduce_add(qkv_state), 1)
    qkv_state, up_out_state = together(qkv_state, up_out_state)

    up_out_piece, bits = halved(up_out_state), 2
    while bits < half:
        up_out_piece = halved(shards_halve(up_out_piece, bits))
        bits *= 2
    up_out_state = shards_halve(up_out_piece, half)
    qkv_piece = moves.reduce_final(qkv_state)
    qkv_piece = qkv_piece.reshape((2, half) + qkv_piece.shape[1:])
    qkv_own = pick(qkv_piece, moves.side)
    qkv_other = moves.shard_swap(pick(qkv_piece, 1 - moves.side), half)
    back_other, qkv_other, up_out_state, down_owned = together(
        back_other, qkv_other, up_out_state, down_owned
    )

    up_out_owned = halved(up_out_state)[0]
    up_out_state = moves.spread_open(up_out_owned)
    qkv_piece = moves.half_exchange(halved((qkv_own, qkv_other)))
    down_state = moves.spread_open(down_owned)
    grad_act_one = pick(back, back_bit) + back_other.astype(f32)
    grad_act_one = grad_act_one.reshape(row_count, width)
    grad_gain_one = jnp.sum(grad_act_one * normed_one, axis=0)
    grad_shift_one = jnp.sum(grad_act_one, axis=0)
    grad_inputs = grad_residual + norm_back(grad_act_one, normed_one, inv_std_one, gain_one)
    grad_inputs, grad_gain_one, grad_shift_one, qkv_piece, down_state, up_out_state = together(
        grad_inputs.astype(bf16), grad_gain_one, grad_shift_one, qkv_piece, down_state, up_out_state
    )
    tokens_other = moves.home_send(grad_inputs)
    qkv_owned = moves.chips_gather(qkv_piece, 1)

    up_out_first, up_out_second = moves.core_pair(
        moves.chips_gather(up_out_owned, 0, tuple(up_out_state)).reshape(rows_z, up_wide + out_wide)
    )
    out_grad = jnp.concatenate([up_out_first[:, up_wide:], up_out_second[:, up_wide:]], axis=1)
    up_columns = []
    for number in range(shards):
        part = slice(number * half_cols, (number + 1) * half_cols)
        up_columns += [up_out_first[:, part], up_out_second[:, part]]
    up_grad = jnp.concatenate(up_columns, axis=1)
    down_first, down_second = moves.core_pair(
        moves.chips_gather(down_owned, 0, tuple(down_state)).reshape(half_cols, width)
    )
    down_grad = jnp.concatenate([down_first, down_second], axis=0)
    qkv_owned = qkv_owned.reshape(half, rows_z, 3 * span)
    qkv_other, tokens_other = together(moves.core_swap(qkv_owned), tokens_other)
    tokens_grad = moves.home_join(grad_inputs, tokens_other)
    qkv_first = jnp.where(core == 0, qkv_owned, qkv_other)
    qkv_second = jnp.where(core == 0, qkv_other, qkv_owned)
    qkv_columns = []
    for kind in range(3):
        for source in (qkv_first, qkv_second):
            for number in range(half):
                qkv_columns.append(source[number][:, kind * span : (kind + 1) * span])
    qkv_grad = jnp.concatenate(qkv_columns, axis=1)

    gradients = [qkv_grad, out_grad, up_grad, down_grad]
    heights = [width, width, width, hidden_width]
    rows_old = [row_state[k : k + 1] for k in range(3)] + [down_rows.reshape(1, -1)]
    stats = [
        factor_stats(gradient, old, decay_rate) for gradient, old in zip(gradients, rows_old)
    ]

    def to_sum(number):
        weight_sum = jnp.broadcast_to(weight_sums[number], (1, 128))
        return [stats[number][2], jnp.concatenate([stats[number][3], weight_sum], axis=0)]

    def spread_heads(part):
        return [jnp.where(member == number, part, 0.0) for number in range(shards)]

    bias_up_parts = []
    for number in range(shards):
        part = grad_bias_up[number * half_cols : (number + 1) * half_cols]
        bias_up_parts += [jnp.where(core == 0, part, 0.0), jnp.where(core == 1, part, 0.0)]
    vector_part = moves.sum_reps(
        jnp.concatenate(
            [grad_gain_one, grad_shift_one]
            + spread_heads(grad_bias_q_part)
            + spread_heads(grad_bias_v_part)
            + [grad_bias_out, grad_gain_two, grad_shift_two]
            + bias_up_parts
            + [grad_bias_down]
        )
    )
    vector_rows = vector_part.reshape(2, -1)
    all_sums = summed(moves, to_sum(0) + to_sum(1) + to_sum(2) + to_sum(3) + [vector_rows])
    sums = [all_sums[0:2], all_sums[2:4], all_sums[4:6], all_sums[6:8]]
    vector_grad = all_sums[8].reshape(-1)
    updates = []
    offset = 0
    for number in range(4):
        end_col = offset + gradients[number].shape[1]
        updates.append(
            factor_apply(
                gradients[number],
                weights[number],
                stats[number][0],
                sums[number][0],
                sums[number][1],
                col_state[offset:end_col].reshape(1, -1),
                heights[number],
                decay_rate,
            )
        )
        offset = end_col
    grads_out, new_weights, copies, new_cols, rms_rows = zip(*updates)
    rms_values = [rms[0, 0] for rms in rms_rows]

    vector_state_new = decay_rate * vector_state + (1.0 - decay_rate) * (
        vector_grad * vector_grad + eps_second
    )
    vector_step = vector_grad * lax.rsqrt(vector_state_new)
    vector_rms = jnp.sqrt(jnp.mean(vector_step * vector_step))
    vector_new = vectors - rate_step * jnp.sqrt(
        jnp.mean(vectors * vectors)
    ) * vector_step / jnp.maximum(1.0, vector_rms / clip_level)
    update_rms = jnp.stack(rms_values + [vector_rms])
    return (
        block_out,
        tokens_grad,
        *grads_out,
        vector_grad,
        *new_weights,
        vector_new,
        *copies,
        jnp.concatenate([stats[0][1], stats[1][1], stats[2][1]], axis=0),
        stats[3][1].reshape(-1),
        jnp.concatenate(new_cols, axis=1).reshape(-1),
        vector_state_new,
        update_rms,
    )


def solution(mesh):
    in_specs = (
        P(("rep", "shard"), None),
        P(("rep", "shard"), None),
        P("rep", None),
        P("shard", None),
        P("shard", None),
        P("shard", None),
        P("shard", None),
        P(),
        P(None, "shard"),
        P("shard"),
        P(),
        P(),
    )
    out_specs = (
        P(("rep", "shard"), None),
        P(("rep", "shard"), None),
        P("shard", None),
        P("shard", None),
        P("shard", None),
        P("shard", None),
        P(),
        P("shard", None),
        P("shard", None),
        P("shard", None),
        P("shard", None),
        P(),
        P("shard", None),
        P("shard", None),
        P("shard", None),
        P("shard", None),
        P(None, "shard"),
        P("shard"),
        P(),
        P(),
        P(),
    )
    return jax.shard_map(
        on_device, mesh=mesh, in_specs=in_specs, out_specs=out_specs, check_vma=False
    )
```

```python
import functools

import jax
import jax.numpy as jnp
from jax import lax
from jax.experimental import pallas as pl
from jax.experimental.pallas import tpu as pltpu
from jax.sharding import PartitionSpec as P

HEADS = 16
STEP = 10
BLOCK = 256


eps_norm = 1e-05
eps_second = 1e-30
rate_step = 0.5
clip_level = 1.0
masked = -1e30
gelu_root = (2.0 / 3.141592653589793) ** 0.5
gelu_cubic = 0.044715

f32 = jnp.float32
bf16 = jnp.bfloat16


def norm_parts(values):
    average = jnp.mean(values, axis=-1, keepdims=True)
    centred = values - average
    inv_std = lax.rsqrt(jnp.mean(centred * centred, axis=-1, keepdims=True) + eps_norm)
    return (centred * inv_std, inv_std)


def norm_back(grad_out, normed, inv_std, gain_vec):
    grad_normed = grad_out * gain_vec
    inner_mean = jnp.mean(grad_normed * normed, axis=-1, keepdims=True)
    centred = grad_normed - jnp.mean(grad_normed, axis=-1, keepdims=True)
    return (centred - normed * inner_mean) * inv_std


def gelu_value(pre_act):
    curve = jnp.tanh(gelu_root * (pre_act + gelu_cubic * pre_act * pre_act * pre_act))
    return 0.5 * pre_act * (1.0 + curve)


def gelu_slope(pre_act):
    square = pre_act * pre_act
    curve = jnp.tanh(gelu_root * (pre_act + gelu_cubic * square * pre_act))
    inner = gelu_root * (1.0 + 3.0 * gelu_cubic * square)
    return 0.5 * (1.0 + curve) + 0.5 * pre_act * (1.0 - curve * curve) * inner


def dot(left_side, right_side):
    return jnp.dot(left_side, right_side, preferred_element_type=f32)


def dot_right(left_side, right_side):
    return lax.dot_general(
        left_side, right_side, (((1,), (1,)), ((), ())), preferred_element_type=f32
    )


def dot_rows(left_side, right_side):
    return lax.dot_general(
        left_side, right_side, (((0,), (0,)), ((), ())), preferred_element_type=f32
    )


def pick(stack, index, axis=0):
    return lax.dynamic_index_in_dim(stack, index, axis, keepdims=False, allow_negative_indices=False)


def cut_rows(values, start, count):
    return lax.dynamic_slice_in_dim(values, start, count, 0, allow_negative_indices=False)


def place(stack, part, index, axis=0):
    return lax.dynamic_update_index_in_dim(stack, part, index, axis, allow_negative_indices=False)


def head_rows(number, head_width):
    return slice(number * head_width, (number + 1) * head_width)


def lane_masks(block_rows, width, heads):
    lanes = lax.broadcasted_iota(jnp.int32, (block_rows, width), 1)
    head_width = width // heads
    return [
        (lanes >= number * head_width) & (lanes < (number + 1) * head_width)
        for number in range(heads)
    ]


def allowed_pairs(key_block, query_block, start_row, block):
    key_pos = lax.broadcasted_iota(jnp.int32, (block, block), 0) + key_block * block
    query_pos = lax.broadcasted_iota(jnp.int32, (block, block), 1) + query_block * block
    return (key_pos <= query_pos) & (key_pos >= start_row)


def key_offsets(key_block, query_block, block):
    rows = lax.broadcasted_iota(jnp.int32, (block, 1), 0)
    return (rows + (key_block - query_block) * block).astype(f32)


def turned(values):
    return jnp.transpose(values.astype(f32))


def head_stack(values, lanes):
    zero = jnp.zeros(values.shape, values.dtype)
    return jnp.concatenate([jnp.where(lane, values, zero) for lane in lanes], axis=0)


def eights(values, combine):
    rows, columns = values.shape
    return combine(values.reshape(rows // 8, 8, columns), axis=0)


def forward_kernel(
    heads,
    block,
    low_ref,
    mid_ref,
    slope_ref,
    start_ref,
    qkv_ref,
    out_ref,
    log_ref,
    values_turned,
    key_stack,
    score_ref,
):
    tokens = qkv_ref.shape[0]
    width = qkv_ref.shape[1] // 3
    head_width = width // heads
    blocks = tokens // block
    query_block = pl.program_id(0)

    @pl.when(query_block == 0)
    def _():
        lanes = lane_masks(block, width, heads)
        for number in range(blocks):
            rows = slice(number * block, (number + 1) * block)
            values_turned[number] = turned(qkv_ref[rows, 2 * width :]).astype(bf16)
            key_stack[number] = head_stack(qkv_ref[rows, width : 2 * width], lanes)

    first_row = pl.multiple_of(query_block * block, block)
    queries = qkv_ref[pl.ds(first_row, block), :width].astype(f32) * head_width ** (-0.5)
    queries = turned(queries).astype(bf16)
    start_row = start_ref[query_block]

    def score_step(key_block, bests, with_mask):
        scores = dot(key_stack[key_block], queries)
        offsets = key_offsets(key_block, query_block, block)
        allowed = allowed_pairs(key_block, query_block, start_row, block) if with_mask else None
        result = []
        for number in range(heads):
            rows = head_rows(number, block)
            part = scores[rows] + slope_ref[number] * offsets
            if with_mask:
                part = jnp.where(allowed, part, masked)
            score_ref[key_block, rows, :] = part
            result.append(jnp.maximum(bests[number], eights(part, jnp.max)))
        return tuple(result)

    low, mid = low_ref[query_block], mid_ref[query_block]
    bests = tuple(jnp.full((8, block), masked, f32) for _ in range(heads))
    bests = lax.fori_loop(low, mid, functools.partial(score_step, with_mask=True), bests)
    bests = lax.fori_loop(mid, query_block, functools.partial(score_step, with_mask=False), bests)
    bests = score_step(query_block, bests, True)
    bests = [jnp.max(best, axis=0, keepdims=True) for best in bests]

    def value_step(key_block, state):
        result = []
        for number in range(heads):
            total, gathered = state[2 * number : 2 * number + 2]
            weights = jnp.exp(score_ref[key_block, head_rows(number, block), :] - bests[number])
            value_rows = values_turned[key_block, head_rows(number, head_width), :]
            result += [
                total + eights(weights, jnp.sum),
                gathered + dot(value_rows, weights.astype(bf16)),
            ]
        return tuple(result)

    state = ()
    for number in range(heads):
        state += (jnp.zeros((8, block), f32), jnp.zeros((head_width, block), f32))
    state = lax.fori_loop(low, query_block + 1, value_step, state)
    columns = []
    for number in range(heads):
        total = jnp.sum(state[2 * number], axis=0, keepdims=True)
        columns.append(state[2 * number + 1] / total)
        log_ref[0, number : number + 1, :] = bests[number] + jnp.log(total)
    out_ref[...] = jnp.transpose(jnp.concatenate(columns, axis=0)).astype(bf16)


def backward_kernel(heads, block, first_head, merge, *refs):
    full_ref, high_ref, slope_ref, start_ref, log_ref, qkv_ref, grad_ref, out_ref = refs[:8]
    earlier_ref = refs[8] if merge else None
    result_ref = refs[9 if merge else 8]
    (
        queries_turned,
        grads_turned,
        keys_turned,
        query_stack,
        grad_stack,
        key_stack,
        value_stack,
        delta_rows,
        query_grads,
    ) = refs[10 if merge else 9 :]
    tokens, all_width = grad_ref.shape
    head_width = all_width // log_ref.shape[1]
    width = heads * head_width
    scale = head_width ** (-0.5)
    blocks = tokens // block
    key_block = pl.program_id(0)
    lanes = lane_masks(block, width, heads)

    def columns(kind):
        start = kind * all_width + first_head * head_width
        return slice(start, start + width)

    def target(kind):
        start = (kind * all_width + first_head * head_width) if merge else kind * width
        return slice(start, start + width)

    @pl.when(key_block == 0)
    def _():
        for number in range(blocks):
            rows = slice(number * block, (number + 1) * block)
            queries = qkv_ref[rows, columns(0)]
            queries_turned[number] = turned(queries.astype(f32) * scale).astype(bf16)
            query_stack[number] = head_stack(queries, lanes)
            keys_turned[number] = turned(qkv_ref[rows, columns(1)]).astype(bf16)
            grads = grad_ref[rows, columns(0)]
            grad_stack[number] = head_stack(grads, lanes)
            grads = grads.astype(f32)
            grads_turned[number] = turned(grads).astype(bf16)
            product = turned(grads * out_ref[rows, columns(0)].astype(f32))
            for head in range(heads):
                delta_rows[number, head : head + 1, :] = jnp.sum(
                    product[head_rows(head, head_width)], axis=0, keepdims=True
                )
            query_grads[number] = jnp.zeros((width, block), f32)

    key_row = pl.multiple_of(key_block * block, block)
    key_stack[...] = head_stack(qkv_ref[pl.ds(key_row, block), columns(1)], lanes)
    value_stack[...] = head_stack(qkv_ref[pl.ds(key_row, block), columns(2)], lanes)

    def step(query_block, state, with_mask):
        key_total, value_total = state
        scores = dot(key_stack[...], queries_turned[query_block])
        grad_weights = dot(value_stack[...], grads_turned[query_block])
        offsets = key_offsets(key_block, query_block, block)
        if with_mask:
            allowed = allowed_pairs(key_block, query_block, start_ref[query_block], block)
        weight_list, grad_list = [], []
        for number in range(heads):
            rows = head_rows(number, block)
            head = first_head + number
            part = scores[rows] + slope_ref[head] * offsets
            part = part - log_ref[query_block, head : head + 1, :]
            if with_mask:
                part = jnp.where(allowed, part, masked)
            probabilities = jnp.exp(part)
            delta = delta_rows[query_block, number : number + 1, :]
            grad_scores = (probabilities * (grad_weights[rows] - delta)).astype(bf16)
            weight_list.append(probabilities.astype(bf16))
            grad_list.append(grad_scores)
            rows = head_rows(number, head_width)
            query_grads[query_block, rows, :] += dot(keys_turned[key_block, rows, :], grad_scores)
        weight_row = jnp.concatenate(weight_list, axis=1)
        grad_row = jnp.concatenate(grad_list, axis=1)
        return (
            key_total + dot(grad_row, query_stack[query_block]),
            value_total + dot(weight_row, grad_stack[query_block]),
        )

    state = (jnp.zeros((block, width), f32), jnp.zeros((block, width), f32))
    state = step(key_block, state, True)
    full, high = full_ref[key_block], high_ref[key_block]
    state = lax.fori_loop(key_block + 1, full, functools.partial(step, with_mask=False), state)
    state = lax.fori_loop(full, high, functools.partial(step, with_mask=True), state)
    result_ref[pl.ds(key_row, block), target(1)] = (state[0] * scale).astype(bf16)
    result_ref[pl.ds(key_row, block), target(2)] = state[1].astype(bf16)
    if merge:
        other = first_head * head_width
        for kind in range(3):
            result_ref[pl.ds(key_row, block), kind * all_width : kind * all_width + other] = earlier_ref[
                pl.ds(key_row, block), kind * other : (kind + 1) * other
            ]

    @pl.when(key_block == blocks - 1)
    def _():
        for number in range(blocks):
            rows = slice(number * block, (number + 1) * block)
            result_ref[rows, target(0)] = jnp.transpose(query_grads[number] * scale).astype(bf16)


def block_plan(lengths, tokens, block):
    ends = jnp.cumsum(lengths)
    positions = jnp.arange(tokens, dtype=jnp.int32)
    passed = positions[:, None] >= ends[None, :]
    starts = jnp.max(jnp.where(passed, ends[None, :], 0), axis=1).astype(jnp.int32)
    finish = jnp.min(jnp.where(passed, tokens, ends[None, :]), axis=1).astype(jnp.int32)
    blocks = tokens // block
    number = jnp.arange(blocks, dtype=jnp.int32)
    first_start = starts[::block]
    last_start = starts[block - 1 :: block]
    low = first_start // block
    mid = jnp.clip((last_start + block - 1) // block, low, number)
    high = (finish[block - 1 :: block] - 1) // block + 1
    full = jnp.clip(finish[::block] // block, number + 1, high)
    return (starts.reshape(blocks, 1, block), low, mid, full, high)


def scalar_spec():
    return pl.BlockSpec(memory_space=pltpu.SMEM)


def whole_spec(shape):
    return pl.BlockSpec(shape, lambda step: (0,) * len(shape), pipeline_mode=pl.Buffered(1))


def attend_forward(qkv, plan, slopes, heads, block):
    tokens, triple = qkv.shape
    width = triple // 3
    blocks = tokens // block
    starts, low, mid, full, high = plan
    return pl.pallas_call(
        functools.partial(forward_kernel, heads, block),
        grid=(blocks,),
        in_specs=[
            scalar_spec(),
            scalar_spec(),
            scalar_spec(),
            whole_spec((blocks, 1, block)),
            whole_spec((tokens, triple)),
        ],
        out_specs=[
            pl.BlockSpec((block, width), lambda step: (step, 0)),
            pl.BlockSpec((1, heads, block), lambda step: (step, 0, 0)),
        ],
        out_shape=[
            jax.ShapeDtypeStruct((tokens, width), bf16),
            jax.ShapeDtypeStruct((blocks, heads, block), f32),
        ],
        scratch_shapes=[
            pltpu.VMEM((blocks, width, block), bf16),
            pltpu.VMEM((blocks, heads * block, width), bf16),
            pltpu.VMEM((blocks, heads * block, block), f32),
        ],
        compiler_params=pltpu.CompilerParams(
            dimension_semantics=("arbitrary",), vmem_limit_bytes=24 * 1024 * 1024
        ),
        cost_estimate=pl.CostEstimate(
            flops=3 * tokens * tokens * 256 * heads,
            bytes_accessed=10 * tokens * width,
            transcendentals=tokens * tokens * heads // 2,
        ),
        name="attend_forward",
    )(low, mid, slopes, starts, qkv)


def attend_backward(qkv, grads, outputs, logs, plan, slopes, heads, block, first_head, earlier):
    tokens, triple = qkv.shape
    all_width = triple // 3
    all_heads = logs.shape[1]
    width = all_width // all_heads * heads
    blocks = tokens // block
    starts, low, mid, full, high = plan
    merge = earlier is not None
    result_width = triple if merge else 3 * width
    operands = [full, high, slopes, starts, logs, qkv, grads, outputs]
    specs = [scalar_spec() for _ in range(3)] + [whole_spec(entry.shape) for entry in operands[3:]]
    if merge:
        operands.append(earlier)
        specs.append(whole_spec(earlier.shape))
    return pl.pallas_call(
        functools.partial(backward_kernel, heads, block, first_head, merge),
        grid=(blocks,),
        in_specs=specs,
        out_specs=pl.BlockSpec((tokens, result_width), lambda step: (0, 0)),
        out_shape=jax.ShapeDtypeStruct((tokens, result_width), bf16),
        scratch_shapes=[
            pltpu.VMEM((blocks, width, block), bf16),
            pltpu.VMEM((blocks, width, block), bf16),
            pltpu.VMEM((blocks, width, block), bf16),
            pltpu.VMEM((blocks, heads * block, width), bf16),
            pltpu.VMEM((blocks, heads * block, width), bf16),
            pltpu.VMEM((heads * block, width), bf16),
            pltpu.VMEM((heads * block, width), bf16),
            pltpu.VMEM((blocks, heads, block), f32),
            pltpu.VMEM((blocks, width, block), f32),
        ],
        compiler_params=pltpu.CompilerParams(
            dimension_semantics=("arbitrary",), vmem_limit_bytes=24 * 1024 * 1024
        ),
        cost_estimate=pl.CostEstimate(
            flops=8 * tokens * tokens * 256 * heads,
            bytes_accessed=20 * tokens * width,
            transcendentals=tokens * tokens * heads // 2,
        ),
        name="attend_backward",
    )(*operands)


def hidden_backward_kernel(own_ref, other_ref, weight_ref, slope_ref, result_ref, total_ref):
    rows = own_ref.shape[0]
    total = jnp.zeros(total_ref.shape, f32)
    for number, ref in enumerate((own_ref, other_ref)):
        part = slice(number * rows, (number + 1) * rows)
        grads = dot_right(ref[...], weight_ref[...]) * slope_ref[part, :].astype(f32)
        grads = grads.astype(bf16)
        result_ref[part, :] = grads
        total = total + jnp.sum(grads.astype(f32), axis=0, keepdims=True)
    total_ref[...] = total


def hidden_backward(weight, cot_own, cot_other, slopes):
    rows, width = cot_own.shape
    breadth = slopes.shape[1]
    tile = min(256, breadth)
    return pl.pallas_call(
        hidden_backward_kernel,
        grid=(breadth // tile,),
        in_specs=[
            whole_spec((rows, width)),
            whole_spec((rows, width)),
            pl.BlockSpec((tile, width), lambda step: (step, 0)),
            pl.BlockSpec((2 * rows, tile), lambda step: (0, step)),
        ],
        out_specs=[
            pl.BlockSpec((2 * rows, tile), lambda step: (0, step)),
            pl.BlockSpec((1, tile), lambda step: (0, step)),
        ],
        out_shape=[
            jax.ShapeDtypeStruct((2 * rows, breadth), bf16),
            jax.ShapeDtypeStruct((1, breadth), f32),
        ],
        compiler_params=pltpu.CompilerParams(
            dimension_semantics=("arbitrary",), vmem_limit_bytes=12 * 1024 * 1024
        ),
        cost_estimate=pl.CostEstimate(flops=1, bytes_accessed=1, transcendentals=0),
        name="hidden_backward",
    )(cot_own, cot_other, weight, slopes)


def up_backward_kernel(grads_ref, weight_ref, result_ref):
    result_ref[...] = dot_right(grads_ref[...], weight_ref[...]).astype(result_ref.dtype)


def up_backward(weight, grads, number, kind_of):
    rows, breadth = grads.shape[0] // 2, grads.shape[1]
    width = weight.shape[0]
    tile = width // 4
    return pl.pallas_call(
        up_backward_kernel,
        grid=(4,),
        in_specs=[
            pl.BlockSpec((rows, breadth), lambda step: (number, 0)),
            pl.BlockSpec((tile, breadth), lambda step: (step, 0)),
        ],
        out_specs=pl.BlockSpec((rows, tile), lambda step: (0, step)),
        out_shape=jax.ShapeDtypeStruct((rows, width), kind_of),
        compiler_params=pltpu.CompilerParams(
            dimension_semantics=("arbitrary",), vmem_limit_bytes=12 * 1024 * 1024
        ),
        cost_estimate=pl.CostEstimate(flops=1, bytes_accessed=1, transcendentals=0),
        name="up_backward",
    )(grads, weight)


def down_projection_kernel(hidden_ref, weight_ref, result_ref):
    result_ref[...] = dot(hidden_ref[...], weight_ref[...]).astype(result_ref.dtype)


def down_projection(hidden, weight):
    rows, breadth = hidden.shape
    width = weight.shape[1]
    tile = min(256, rows)
    return pl.pallas_call(
        down_projection_kernel,
        grid=(rows // tile,),
        in_specs=[
            pl.BlockSpec((tile, breadth), lambda step: (step, 0)),
            whole_spec((breadth, width)),
        ],
        out_specs=pl.BlockSpec((tile, width), lambda step: (step, 0)),
        out_shape=jax.ShapeDtypeStruct((rows, width), bf16),
        compiler_params=pltpu.CompilerParams(
            dimension_semantics=("arbitrary",), vmem_limit_bytes=14 * 1024 * 1024
        ),
        cost_estimate=pl.CostEstimate(flops=1, bytes_accessed=1, transcendentals=0),
        name="down_projection",
    )(hidden, weight)


def up_gradient_kernel(own_ref, other_ref, grads_ref, result_ref, act_turned):
    rows, width = own_ref.shape
    step = 256

    @pl.when(pl.program_id(0) == 0)
    def _():
        for number, ref in enumerate((own_ref, other_ref)):
            for row in range(0, rows, step):
                first = number * rows + row
                for column in range(0, width, step):
                    block = ref[row : row + step, column : column + step]
                    act_turned[column : column + step, first : first + step] = turned(block).astype(bf16)

    result_ref[...] = dot(act_turned[...], grads_ref[...]).astype(bf16)


def up_gradient(act_own, act_other, grads):
    rows, width = act_own.shape
    breadth = grads.shape[1]
    tile = min(512, breadth)
    return pl.pallas_call(
        up_gradient_kernel,
        grid=(breadth // tile,),
        in_specs=[
            whole_spec((rows, width)),
            whole_spec((rows, width)),
            pl.BlockSpec((2 * rows, tile), lambda step: (0, step)),
        ],
        out_specs=pl.BlockSpec((width, tile), lambda step: (0, step)),
        out_shape=jax.ShapeDtypeStruct((width, breadth), bf16),
        scratch_shapes=[pltpu.VMEM((width, 2 * rows), bf16)],
        compiler_params=pltpu.CompilerParams(
            dimension_semantics=("arbitrary",), vmem_limit_bytes=16 * 1024 * 1024
        ),
        cost_estimate=pl.CostEstimate(flops=1, bytes_accessed=1, transcendentals=0),
        name="up_gradient",
    )(act_own, act_other, grads)


def together(*values):
    return lax.optimization_barrier(tuple(values))


def ordered(own, other, bit, axis=0):
    first = jnp.where(bit == 0, own, other)
    second = jnp.where(bit == 0, other, own)
    return jnp.stack([first, second], axis=axis)


class Moves:
    def __init__(self):
        self.shards = lax.axis_size("shard")
        self.reps = lax.axis_size("rep")
        self.half = self.shards // 2
        self.chips = self.reps // 2
        self.shard = lax.axis_index("shard")
        self.rep = lax.axis_index("rep")
        self.core = self.rep & 1
        self.chip = self.rep >> 1
        self.side = lax.div(self.shard, self.half)
        self.member = lax.rem(self.shard, self.half) + self.core * self.half

    def core_swap(self, part):
        return lax.ppermute(part, "rep", [(r, r ^ 1) for r in range(self.reps)])

    def chip_swap(self, part, bits):
        return lax.ppermute(part, "rep", [(r, r ^ (2 * bits)) for r in range(self.reps)])

    def shard_swap(self, part, bits):
        return lax.ppermute(part, "shard", [(s, s ^ bits) for s in range(self.shards)])

    def shard_bit(self, bits):
        return lax.div(self.shard, bits) & 1

    def low_bits(self):
        bits, result = 1, []
        while bits < self.half:
            result.append(bits)
            bits *= 2
        return result

    def home_send(self, part):
        pairs = []
        for rep in range(self.reps):
            for shard in range(self.shards):
                if shard // self.half != rep % 2:
                    to_shard = (shard + self.half) % self.shards
                    pairs.append((rep * self.shards + shard, (rep ^ 1) * self.shards + to_shard))
        return lax.ppermute(part, ("rep", "shard"), pairs)

    def home_join(self, part, other):
        return jnp.where(self.side == self.core, part, other)

    def half_gather(self, part):
        stack = part[None]
        for bits in self.low_bits():
            own = stack
            stack = ordered(own, self.shard_swap(own, bits), self.shard_bit(bits))
            stack = stack.reshape((-1,) + part.shape)
        return stack

    def cores_gather(self, stack):
        stack = ordered(stack, self.core_swap(stack), self.core)
        return stack.reshape((-1,) + stack.shape[2:])

    def exchange_bit(self, stack, bit, swap):
        sources, targets = stack.shape[:2]
        stack = stack.reshape((sources, 2, targets // 2) + stack.shape[2:])
        own, other = pick(stack, bit, 1), swap(pick(stack, 1 - bit, 1))
        return ordered(own, other, bit, 1).reshape((2 * sources,) + own.shape[1:])

    def half_exchange(self, stack):
        stack = stack[None]
        for bits in reversed(self.low_bits()):
            swap = functools.partial(self.shard_swap, bits=bits)
            stack = self.exchange_bit(stack, self.shard_bit(bits), swap)
        return stack.reshape((self.half,) + stack.shape[2:])

    def cores_exchange(self, stack):
        return self.exchange_bit(stack[None], self.core, self.core_swap)

    def members_exchange(self, stack):
        for bits in reversed(self.low_bits()):
            swap = functools.partial(self.shard_swap, bits=bits)
            stack = self.exchange_bit(stack, self.shard_bit(bits), swap)
        return stack.reshape((self.shards,) + stack.shape[2:])

    def reduce_bit(self, stack, bit, swap):
        stack = stack.reshape((2, stack.shape[0] // 2) + stack.shape[1:])
        other = swap(pick(stack, 1 - bit).astype(bf16))
        return pick(stack, bit).astype(f32) + other.astype(f32)

    def spread_open(self, part):
        if self.chips == 4:
            return (self.chip_swap(part, 1), self.chip_swap(part, 2))
        held, bits = [part], 1
        while bits < self.chips:
            held = held + [self.chip_swap(piece, bits) for piece in held]
            bits *= 2
        return tuple(held[1:])

    def spread_close(self, state):
        if self.chips == 4:
            by_x, by_y = state
            cut, axis = by_x.shape[-2] // 2, by_x.ndim - 2
            far = [
                self.chip_swap(by_x[..., :cut, :], 2),
                self.chip_swap(by_y[..., cut:, :], 1),
            ]
            return (by_x, by_y, jnp.concatenate(far, axis=axis))
        return state

    def far_open(self, states):
        if self.chips != 4:
            return ()
        cut = states[0][0].shape[0] // 2
        return (
            self.chip_swap(jnp.concatenate([by_x[:cut] for by_x, _ in states], axis=0), 2),
            self.chip_swap(jnp.concatenate([by_y[cut:] for _, by_y in states], axis=0), 1),
        )

    def far_parts(self, states, far):
        if self.chips != 4:
            return [[(k + 1, 0, part) for k, part in enumerate(state)] for state in states]
        cut = states[0][0].shape[0] // 2
        result = []
        for number, (by_x, by_y) in enumerate(states):
            rows = slice(number * cut, (number + 1) * cut)
            result.append([(1, 0, by_x), (2, 0, by_y), (3, 0, far[0][rows]), (3, cut, far[1][rows])])
        return result

    def chips_gather(self, part, axis, state=None):
        shape = part.shape[:axis] + (self.chips,) + part.shape[axis:]
        stack = place(jnp.zeros(shape, part.dtype), part, self.chip, axis)
        others = self.spread_close(self.spread_open(part) if state is None else state)
        for number, piece in enumerate(others):
            stack = place(stack, piece, self.chip ^ (number + 1), axis)
        return stack

    def reduce_open(self, stack, axis):
        return self.reduce_start(self.reduce_cut(stack, axis), axis)

    def reduce_cut(self, stack, axis):
        if self.chips != 4:
            return (stack,)
        shape = stack.shape[:axis] + (2, 2) + stack.shape[axis + 1 :]
        stack = stack.reshape(shape)
        bit_x, bit_y = self.chip & 1, self.chip >> 1
        cut = shape[0] // 2
        first, second = stack[:cut], stack[cut:]
        return (
            pick(first, bit_x, axis + 1),
            pick(second, bit_y, axis),
            pick(first, 1 - bit_x, axis + 1),
            pick(second, 1 - bit_y, axis),
        )

    def reduce_start(self, parts, axis):
        if self.chips == 4:
            first, second, send_first, send_second = parts
            return (first, second, self.chip_swap(send_first, 1), self.chip_swap(send_second, 2))
        (stack,) = parts
        count = self.chips
        stack = stack.astype(f32)
        while count > 1:
            count //= 2
            shape = stack.shape[:axis] + (2, count) + stack.shape[axis + 1 :]
            stack = stack.reshape(shape)
            bit = lax.div(self.chip, count) & 1
            got = self.chip_swap(pick(stack, 1 - bit, axis).astype(bf16), count)
            stack = pick(stack, bit, axis) + got.astype(f32)
        return (pick(stack, 0, axis).astype(bf16),)

    def reduce_add(self, state):
        if self.chips != 4:
            return state
        first, second, got_first, got_second = state
        first = (first.astype(f32) + got_first.astype(f32)).astype(bf16)
        second = (second.astype(f32) + got_second.astype(f32)).astype(bf16)
        return (first, second)

    def reduce_send(self, state, axis):
        if self.chips != 4:
            return state
        first, second = state
        bit_x, bit_y = self.chip & 1, self.chip >> 1
        got_first = self.chip_swap(pick(first, 1 - bit_y, axis), 2)
        got_second = self.chip_swap(pick(second, 1 - bit_x, axis), 1)
        return (pick(first, bit_y, axis), pick(second, bit_x, axis), got_first, got_second)

    def reduce_final(self, state):
        if self.chips != 4:
            return state[0]
        first, second, got_first, got_second = state
        first = first.astype(f32) + got_first.astype(f32)
        second = second.astype(f32) + got_second.astype(f32)
        return jnp.concatenate([first, second], axis=0).astype(bf16)

    def reduce_close(self, state, axis):
        return self.reduce_final(self.reduce_send(state, axis))

    def core_pair(self, part):
        other = self.core_swap(part)
        first = jnp.where(self.core == 0, part, other)
        second = jnp.where(self.core == 0, other, part)
        return first, second

    def sum_reps(self, vector):
        bits = 1
        while bits < self.reps:
            vector = vector + lax.ppermute(vector, "rep", [(r, r ^ bits) for r in range(self.reps)])
            bits *= 2
        return vector

    def sum_shards(self, vector):
        bits = 1
        while bits < self.shards:
            vector = vector + self.shard_swap(vector, bits)
            bits *= 2
        return vector


def stats_kernel(decay_rate, gradient_ref, old_ref, rows_ref, lane_rows_ref, sums_ref, total_ref, partial):
    step = pl.program_id(0)
    rows, columns = gradient_ref.shape

    @pl.when(step == 0)
    def _():
        partial[...] = jnp.zeros_like(partial)
        total_ref[...] = jnp.zeros_like(total_ref)

    gradient = gradient_ref[...].astype(f32)
    square = gradient * gradient
    row_mean = jnp.sum(square, axis=1, keepdims=True) / columns
    old = jnp.transpose(jnp.broadcast_to(old_ref[...], (128, rows)))[:, 0:1]
    rows_new = decay_rate * old + (1.0 - decay_rate) * (row_mean + eps_second)
    rows_ref[...] = rows_new
    lane_rows_ref[...] = jnp.transpose(jnp.broadcast_to(rows_new, (rows, 128)))[0:1, :]
    total_ref[...] += jnp.broadcast_to(jnp.sum(rows_new, axis=0, keepdims=True), (1, 128))
    partial[0:8, :] += eights(square, jnp.sum)
    partial[8:16, :] += eights(square * (1.0 / rows_new), jnp.sum)

    @pl.when(step == pl.num_programs(0) - 1)
    def _():
        sums_ref[0:1, :] = jnp.sum(partial[0:8, :], axis=0, keepdims=True)
        sums_ref[1:2, :] = jnp.sum(partial[8:16, :], axis=0, keepdims=True)


def factor_stats(gradient, rows_old, decay_rate):
    height, breadth = gradient.shape
    rows = min(256 if breadth <= 1024 else 128, height)
    return pl.pallas_call(
        functools.partial(stats_kernel, decay_rate),
        grid=(height // rows,),
        in_specs=[
            pl.BlockSpec((rows, breadth), lambda step: (step, 0)),
            pl.BlockSpec((1, rows), lambda step: (0, step)),
        ],
        out_specs=[
            pl.BlockSpec((rows, 1), lambda step: (step, 0)),
            pl.BlockSpec((1, rows), lambda step: (0, step)),
            pl.BlockSpec((2, breadth), lambda step: (0, 0)),
            pl.BlockSpec((1, 128), lambda step: (0, 0)),
        ],
        out_shape=[
            jax.ShapeDtypeStruct((height, 1), f32),
            jax.ShapeDtypeStruct((1, height), f32),
            jax.ShapeDtypeStruct((2, breadth), f32),
            jax.ShapeDtypeStruct((1, 128), f32),
        ],
        scratch_shapes=[pltpu.VMEM((16, breadth), f32)],
        compiler_params=pltpu.CompilerParams(
            dimension_semantics=("arbitrary",), vmem_limit_bytes=12 * 1024 * 1024
        ),
        name="factor_stats",
    )(gradient, rows_old)


def apply_kernel(
    decay_rate,
    height,
    gradient_ref,
    weight_ref,
    rows_ref,
    sums_ref,
    scalar_ref,
    old_ref,
    gradient_out,
    weight_out,
    copy_out,
    cols_out,
    rms_out,
    col_factor,
):
    columns = gradient_ref.shape[1]

    @pl.when(pl.program_id(0) == 0)
    def _():
        cols_new = decay_rate * old_ref[...] + (1.0 - decay_rate) * (
            sums_ref[0:1, :] / height + eps_second
        )
        row_mean = scalar_ref[0:1, 0:1] / height
        weight_mean = scalar_ref[1:2, 0:1] / (height * columns)
        scaled = jnp.sum(sums_ref[1:2, :] / cols_new, axis=1, keepdims=True)
        rms_update = jnp.sqrt(row_mean / (height * columns) * scaled)
        factor = rate_step * jnp.sqrt(weight_mean) * jnp.sqrt(row_mean)
        factor = factor / jnp.maximum(1.0, rms_update / clip_level)
        col_factor[...] = factor * lax.rsqrt(cols_new)
        cols_out[...] = cols_new
        rms_out[...] = jnp.broadcast_to(rms_update, (1, 128))

    gradient = gradient_ref[...].astype(f32)
    new_weight = weight_ref[...] - gradient * lax.rsqrt(rows_ref[...]) * col_factor[...]
    gradient_out[...] = gradient
    weight_out[...] = new_weight
    copy_out[...] = new_weight.astype(bf16)


def factor_apply(gradient, weight, rows_new, sums, scalars, cols_old, height, decay_rate):
    own_height, breadth = gradient.shape
    rows = min(256 if breadth <= 1024 else 64, own_height)

    def rows_spec():
        return pl.BlockSpec((rows, breadth), lambda step: (step, 0))

    def row_spec(count, wide):
        return pl.BlockSpec((count, wide), lambda step: (0, 0))

    return pl.pallas_call(
        functools.partial(apply_kernel, decay_rate, height),
        grid=(own_height // rows,),
        in_specs=[
            rows_spec(),
            rows_spec(),
            pl.BlockSpec((rows, 1), lambda step: (step, 0)),
            row_spec(2, breadth),
            row_spec(2, 128),
            row_spec(1, breadth),
        ],
        out_specs=[rows_spec(), rows_spec(), rows_spec(), row_spec(1, breadth), row_spec(1, 128)],
        out_shape=[
            jax.ShapeDtypeStruct((own_height, breadth), f32),
            jax.ShapeDtypeStruct((own_height, breadth), f32),
            jax.ShapeDtypeStruct((own_height, breadth), bf16),
            jax.ShapeDtypeStruct((1, breadth), f32),
            jax.ShapeDtypeStruct((1, 128), f32),
        ],
        scratch_shapes=[pltpu.VMEM((1, breadth), f32)],
        compiler_params=pltpu.CompilerParams(
            dimension_semantics=("arbitrary",), vmem_limit_bytes=14 * 1024 * 1024
        ),
        name="factor_apply",
    )(gradient, weight, rows_new, sums, scalars, cols_old)


def summed(moves, entries):
    total = moves.sum_shards(jnp.concatenate(entries, axis=1))
    result, offset = [], 0
    for entry in entries:
        result.append(total[:, offset : offset + entry.shape[1]])
        offset += entry.shape[1]
    return result


def on_device(
    tokens,
    cotangent,
    seq_lengths,
    qkv_weight,
    out_weight,
    up_weight,
    down_weight,
    vectors,
    row_state,
    down_rows,
    col_state,
    vector_state,
):
    moves = Moves()
    shards, half, chips, core = moves.shards, moves.half, moves.chips, moves.core
    row_count, width = tokens.shape
    hidden_width = up_weight.shape[1]
    group_rows = row_count * shards
    heads = HEADS // shards
    head_width = width // HEADS
    span = heads * head_width
    member = moves.member
    decay_rate = 1.0 - STEP ** (-0.8)
    head_number = (member * heads + jnp.arange(heads, dtype=jnp.int32)).astype(f32)
    slopes = jnp.exp2(-8.0 * (head_number + 1.0) / HEADS)

    gain_one = vectors[0:width]
    shift_one = vectors[width : 2 * width]
    bias_query = vectors[2 * width : 3 * width]
    bias_value = vectors[3 * width : 4 * width]
    bias_out = vectors[4 * width : 5 * width]
    gain_two = vectors[5 * width : 6 * width]
    shift_two = vectors[6 * width : 7 * width]
    bias_up = vectors[7 * width : 7 * width + hidden_width]
    bias_down = vectors[7 * width + hidden_width :]

    other_tokens = moves.home_send(tokens)
    other_lengths = moves.core_swap(seq_lengths)
    lengths = jnp.where(moves.side == core, seq_lengths, other_lengths)[0]
    plan = block_plan(lengths, group_rows, BLOCK)
    rows_z = width // shards
    rows_piece = rows_z // chips
    my_rows = cut_rows(qkv_weight, moves.chip * rows_piece, rows_piece)
    my_rows = my_rows.astype(bf16)
    my_blocks = []
    for number in range(half):
        kinds = []
        for kind in range(3):
            first = kind * width + number * span
            second = first + half * span
            kinds.append(
                jnp.where(
                    core == 0, my_rows[:, first : first + span], my_rows[:, second : second + span]
                )
            )
        my_blocks.append(jnp.concatenate(kinds, axis=1))
    qkv_part = moves.half_exchange(jnp.stack(my_blocks))
    half_cols = hidden_width // (2 * shards)
    up_wide = shards * half_cols
    out_wide = width // 2
    down_piece = half_cols // chips

    def core_half(values):
        parts = []
        for number in range(shards):
            start = 2 * number * half_cols
            first = values[..., start : start + half_cols]
            second = values[..., start + half_cols : start + 2 * half_cols]
            parts.append(jnp.where(core == 0, first, second))
        return jnp.concatenate(parts, axis=-1)

    up_own = core_half(up_weight).astype(bf16).reshape(chips, rows_piece, up_wide)
    out_own = jnp.where(core == 0, out_weight[:, :out_wide], out_weight[:, out_wide:]).astype(bf16)
    out_own = out_own.reshape(chips, rows_piece, out_wide)
    down_own = cut_rows(down_weight, core * half_cols, half_cols).astype(bf16)
    fold = down_piece // rows_piece
    down_own = down_own.reshape(chips, fold, rows_piece, width)
    my_down = pick(down_own, moves.chip)
    weight_piece = jnp.concatenate(
        [pick(up_own, moves.chip), pick(out_own, moves.chip)] + [my_down[k] for k in range(fold)],
        axis=1,
    )
    near_pieces, bits = [weight_piece], 1
    while bits < half:
        near_pieces = near_pieces + [moves.shard_swap(piece, bits) for piece in near_pieces]
        bits *= 2
    near_pieces = near_pieces[1:]
    weights = [qkv_weight, out_weight, up_weight, down_weight]
    weight_sums = [jnp.sum(weight * weight) for weight in weights]
    other_tokens, qkv_part, near_pieces, weight_piece, plan, weight_sums = together(
        other_tokens, qkv_part, near_pieces, weight_piece, plan, weight_sums
    )
    home_tokens = moves.home_join(tokens, other_tokens)
    far_piece = moves.shard_swap(weight_piece, half)
    near_open = [moves.spread_open(piece) for piece in near_pieces]
    qkv_far = moves.shard_swap(qkv_part, half)
    qkv_far, near_open = together(qkv_far, near_open)
    qkv_part = ordered(qkv_part, qkv_far, moves.side).reshape(shards, rows_piece, 3 * span)
    qkv_cols = moves.chips_gather(qkv_part, 1).reshape(width, 3 * span)
    inputs = home_tokens.astype(f32)
    normed_one, inv_std_one = norm_parts(inputs)
    act_one = (normed_one * gain_one + shift_one).astype(bf16)
    act_half = moves.half_gather(act_one)

    act_half, qkv_cols, far_piece = together(act_half, qkv_cols, far_piece)
    near_far = moves.far_open(near_open)
    act_all = moves.cores_gather(act_half).reshape(group_rows, width)
    far_open = moves.spread_open(far_piece)
    far_pieces, bits = [far_piece], 1
    while bits < half:
        far_pieces = far_pieces + [moves.shard_swap(piece, bits) for piece in far_pieces]
        bits *= 2
    far_pieces = far_pieces[1:]

    bias_q_part = cut_rows(bias_query, member * span, span)
    bias_v_part = cut_rows(bias_value, member * span, span)
    qkv_bias = jnp.concatenate([bias_q_part, jnp.zeros_like(bias_q_part), bias_v_part])
    qkv_rows = (dot(act_all, qkv_cols) + qkv_bias).astype(bf16)
    attended_cols, logs = attend_forward(qkv_rows, plan, slopes, heads, BLOCK)
    attended_cols, far_open, far_pieces, near_far = together(
        attended_cols, far_open, far_pieces, near_far
    )
    attended_parts = moves.cores_exchange(attended_cols.reshape(shards, row_count, span))
    attended_parts = moves.members_exchange(attended_parts)
    second_far = moves.far_open([far_open])
    last_states = [moves.spread_open(piece) for piece in far_pieces]
    attended_parts, second_far, last_states, cotangent = together(
        attended_parts, second_far, last_states, cotangent
    )
    last_far = moves.far_open(last_states)
    other_cot = moves.home_send(cotangent)
    attended = jnp.concatenate([attended_parts[k] for k in range(shards)], axis=1)

    up_all = place(jnp.zeros((shards, chips, rows_piece, up_wide), bf16), up_own, moves.shard)
    out_all = place(jnp.zeros((shards, chips, rows_piece, out_wide), bf16), out_own, moves.shard)
    down_all = place(jnp.zeros((shards, chips, fold, rows_piece, width), bf16), down_own, moves.shard)
    pieces = near_pieces + [far_piece] + far_pieces
    parts_of = moves.far_parts(near_open, near_far) + moves.far_parts([far_open], second_far)
    parts_of += moves.far_parts(last_states, last_far)
    for number, (piece, parts) in enumerate(zip(pieces, parts_of)):
        plane = moves.shard ^ (number + 1)
        for far, row, rows in [(0, 0, piece)] + parts:
            chip = moves.chip ^ far
            up_all = lax.dynamic_update_slice(
                up_all, rows[None, None, :, :up_wide], (plane, chip, row, 0), allow_negative_indices=False
            )
            out_all = lax.dynamic_update_slice(
                out_all, rows[None, None, :, up_wide : up_wide + out_wide], (plane, chip, row, 0), allow_negative_indices=False
            )
            start = up_wide + out_wide
            folds = [rows[:, start + k * width : start + (k + 1) * width] for k in range(fold)]
            down_all = lax.dynamic_update_slice(
                down_all, jnp.stack(folds)[None, None], (plane, chip, 0, row, 0), allow_negative_indices=False
            )
    up_half = up_all.reshape(width, up_wide)
    down_half = down_all.reshape(up_wide, width)
    out_first, out_second = moves.core_pair(out_all.reshape(width, out_wide))
    out_low = jnp.concatenate([out_first, out_second], axis=1)
    residual = inputs + dot(attended, out_low) + bias_out
    normed_two, inv_std_two = norm_parts(residual)
    act_two = (normed_two * gain_two + shift_two).astype(bf16)

    act_two_other, attended_other = together(
        moves.core_swap(act_two), moves.core_swap(attended)
    )
    act_two_pair = jnp.concatenate([act_two, act_two_other], axis=0)
    attended_pair = jnp.concatenate([attended, attended_other], axis=0)
    bias_up_half = core_half(bias_up)
    up_pair = dot(act_two_pair, up_half) + bias_up_half
    hidden_pair = gelu_value(up_pair).astype(bf16)
    slope_pair = gelu_slope(up_pair).astype(bf16)
    hidden_pair, slope_pair, other_cot = together(hidden_pair, slope_pair, other_cot)
    home_cot = moves.home_join(cotangent, other_cot)
    cot_other = moves.core_swap(home_cot)
    cot_pair = jnp.concatenate([home_cot, cot_other], axis=0)
    down_terms = dot_rows(hidden_pair, cot_pair).astype(bf16)
    down_state = moves.reduce_cut(down_terms.reshape(shards, chips, down_piece, width), 1)
    slope_pair, down_state = together(slope_pair, down_state)
    down_state = moves.reduce_start(down_state, 1)
    grad_y = home_cot.astype(f32)
    grad_bias_down = jnp.sum(grad_y, axis=0)
    grad_up_pair, grad_bias_up = hidden_backward(down_half, home_cot, cot_other, slope_pair)
    grad_bias_up = grad_bias_up.reshape(-1)
    back_other = moves.core_swap(up_backward(up_half, grad_up_pair, 1, bf16))
    up_terms = up_gradient(act_two, act_two_other, grad_up_pair)
    down_pair = down_projection(hidden_pair, down_half)
    back_other, down_pair, up_terms, down_state = together(
        back_other, down_pair, up_terms, down_state
    )
    grad_act_two = up_backward(up_half, grad_up_pair, 0, f32) + back_other.astype(f32)
    grad_gain_two = jnp.sum(grad_act_two * normed_two, axis=0)
    grad_shift_two = jnp.sum(grad_act_two, axis=0)
    grad_residual = grad_y + norm_back(grad_act_two, normed_two, inv_std_two, gain_two)
    grad_attn = grad_residual.astype(bf16)
    grad_bias_out = jnp.sum(grad_attn, axis=0, dtype=f32)
    to_members = jnp.stack(
        [
            dot_right(grad_attn, out_low[k * span : (k + 1) * span]).astype(bf16)
            for k in range(shards)
        ]
    )
    attn_halves = [grad_attn[:, :out_wide], grad_attn[:, out_wide:]]
    attn_own = jnp.where(core == 0, attn_halves[0], attn_halves[1])
    attn_other = jnp.where(core == 0, attn_halves[1], attn_halves[0])
    down_other = moves.core_swap(down_pair[row_count:])
    grad_heads, attn_other, up_terms, down_state, down_other = together(
        moves.cores_exchange(to_members), moves.core_swap(attn_other), up_terms, down_state, down_other
    )
    up_cut = moves.reduce_cut(up_terms.reshape(shards, chips, rows_piece, up_wide), 1)
    down_sums = moves.reduce_add(down_state)
    attn_pair = jnp.concatenate([attn_own, attn_other], axis=0)
    grad_heads = moves.members_exchange(grad_heads).reshape(group_rows, span)
    up_state = moves.reduce_start(up_cut, 1)
    down_mid = moves.reduce_close(down_sums, 1)
    block_out = residual + down_pair[:row_count].astype(f32) + down_other.astype(f32) + bias_down
    block_out = block_out.astype(bf16)

    out_terms = dot_rows(attended_pair, attn_pair).astype(bf16)
    def shards_halve(piece, bits):
        piece = piece.reshape((piece.shape[0] // 2, 2) + piece.shape[1:])
        bit = moves.shard_bit(bits)
        return pick(piece, bit, 1), moves.shard_swap(pick(piece, 1 - bit, 1), bits)

    def halved(state):
        own, other = state
        return (own.astype(f32) + other.astype(f32)).astype(bf16)

    def shards_sum(piece):
        rows = piece.shape[1]
        return lax.psum_scatter(
            piece.reshape(shards * rows, piece.shape[2]), "shard", scatter_dimension=0, tiled=True
        )

    grad_heads, down_mid, out_terms, block_out = together(
        grad_heads, down_mid, out_terms, block_out
    )
    block_other = moves.home_send(block_out)
    down_owned = shards_sum(down_mid)
    out_state = moves.reduce_open(out_terms.reshape(shards, chips, rows_piece, out_wide), 1)
    attend_args = (plan, slopes)
    parts = 2 if heads % 4 == 0 else 1
    part_heads = heads // parts
    grad_qkv = attend_backward(
        qkv_rows, grad_heads, attended_cols, logs, *attend_args, part_heads, BLOCK, 0, None
    )
    grad_qkv, up_state, out_state = together(grad_qkv, up_state, out_state)
    up_sums, out_sums = moves.reduce_add(up_state), moves.reduce_add(out_state)
    grad_qkv, up_sums, out_sums = together(grad_qkv, up_sums, out_sums)
    up_out_state = [
        jnp.concatenate([up_part, out_part], axis=-1) for up_part, out_part in zip(up_sums, out_sums)
    ]
    if parts == 2:
        grad_qkv = attend_backward(
            qkv_rows, grad_heads, attended_cols, logs, *attend_args, part_heads, BLOCK, part_heads, grad_qkv
        )
    grad_qkv, up_out_state, block_other, down_owned = together(
        grad_qkv, moves.reduce_send(up_out_state, 1), block_other, down_owned
    )
    block_out = moves.home_join(block_out, block_other)
    up_out_piece = moves.reduce_final(up_out_state)
    up_out_state = shards_halve(up_out_piece, 1)

    grad_bias_q_part = jnp.sum(grad_qkv[:, :span], axis=0, dtype=f32)
    grad_bias_v_part = jnp.sum(grad_qkv[:, 2 * span :], axis=0, dtype=f32)

    grad_halves = grad_qkv.reshape(2, half * row_count, 3 * span)
    sent = dot_right(pick(grad_halves, 1 - core), qkv_cols).astype(bf16)
    sent = moves.core_swap(sent)
    qkv_terms = dot_rows(act_all, grad_qkv).astype(bf16)
    qkv_terms = qkv_terms.reshape(shards, chips, rows_piece, 3 * span)
    qkv_state = moves.reduce_open(qkv_terms, 1)
    back = dot_right(pick(grad_halves, core), qkv_cols) + sent.astype(f32)
    qkv_state, back = together(qkv_state, back)

    back = back.reshape(half, row_count, width)
    low_bits = list(reversed(moves.low_bits()))
    for bits in low_bits[:-1]:
        back = moves.reduce_bit(
            back, moves.shard_bit(bits), functools.partial(moves.shard_swap, bits=bits)
        )
    back = back.reshape((2, -1) + back.shape[1:])
    back_bit = moves.shard_bit(low_bits[-1])
    back_other = moves.shard_swap(pick(back, 1 - back_bit).astype(bf16), low_bits[-1])
    qkv_state = moves.reduce_send(moves.reduce_add(qkv_state), 1)
    qkv_state, up_out_state = together(qkv_state, up_out_state)

    up_out_piece, bits = halved(up_out_state), 2
    while bits < half:
        up_out_piece = halved(shards_halve(up_out_piece, bits))
        bits *= 2
    up_out_state = shards_halve(up_out_piece, half)
    qkv_piece = moves.reduce_final(qkv_state)
    qkv_piece = qkv_piece.reshape((2, half) + qkv_piece.shape[1:])
    qkv_own = pick(qkv_piece, moves.side)
    qkv_other = moves.shard_swap(pick(qkv_piece, 1 - moves.side), half)
    back_other, qkv_other, up_out_state, down_owned = together(
        back_other, qkv_other, up_out_state, down_owned
    )

    up_out_owned = halved(up_out_state)[0]
    up_out_state = moves.spread_open(up_out_owned)
    qkv_piece = moves.half_exchange(halved((qkv_own, qkv_other)))
    down_state = moves.spread_open(down_owned)
    grad_act_one = pick(back, back_bit) + back_other.astype(f32)
    grad_act_one = grad_act_one.reshape(row_count, width)
    grad_gain_one = jnp.sum(grad_act_one * normed_one, axis=0)
    grad_shift_one = jnp.sum(grad_act_one, axis=0)
    grad_inputs = grad_residual + norm_back(grad_act_one, normed_one, inv_std_one, gain_one)
    grad_inputs, grad_gain_one, grad_shift_one, qkv_piece, down_state, up_out_state = together(
        grad_inputs.astype(bf16), grad_gain_one, grad_shift_one, qkv_piece, down_state, up_out_state
    )
    tokens_other = moves.home_send(grad_inputs)
    qkv_owned = moves.chips_gather(qkv_piece, 1)

    up_out_first, up_out_second = moves.core_pair(
        moves.chips_gather(up_out_owned, 0, tuple(up_out_state)).reshape(rows_z, up_wide + out_wide)
    )
    out_grad = jnp.concatenate([up_out_first[:, up_wide:], up_out_second[:, up_wide:]], axis=1)
    up_columns = []
    for number in range(shards):
        part = slice(number * half_cols, (number + 1) * half_cols)
        up_columns += [up_out_first[:, part], up_out_second[:, part]]
    up_grad = jnp.concatenate(up_columns, axis=1)
    down_first, down_second = moves.core_pair(
        moves.chips_gather(down_owned, 0, tuple(down_state)).reshape(half_cols, width)
    )
    down_grad = jnp.concatenate([down_first, down_second], axis=0)
    qkv_owned = qkv_owned.reshape(half, rows_z, 3 * span)
    qkv_other, tokens_other = together(moves.core_swap(qkv_owned), tokens_other)
    tokens_grad = moves.home_join(grad_inputs, tokens_other)
    qkv_first = jnp.where(core == 0, qkv_owned, qkv_other)
    qkv_second = jnp.where(core == 0, qkv_other, qkv_owned)
    qkv_columns = []
    for kind in range(3):
        for source in (qkv_first, qkv_second):
            for number in range(half):
                qkv_columns.append(source[number][:, kind * span : (kind + 1) * span])
    qkv_grad = jnp.concatenate(qkv_columns, axis=1)

    gradients = [qkv_grad, out_grad, up_grad, down_grad]
    heights = [width, width, width, hidden_width]
    rows_old = [row_state[k : k + 1] for k in range(3)] + [down_rows.reshape(1, -1)]
    stats = [
        factor_stats(gradient, old, decay_rate) for gradient, old in zip(gradients, rows_old)
    ]

    def to_sum(number):
        weight_sum = jnp.broadcast_to(weight_sums[number], (1, 128))
        return [stats[number][2], jnp.concatenate([stats[number][3], weight_sum], axis=0)]

    def spread_heads(part):
        return [jnp.where(member == number, part, 0.0) for number in range(shards)]

    bias_up_parts = []
    for number in range(shards):
        part = grad_bias_up[number * half_cols : (number + 1) * half_cols]
        bias_up_parts += [jnp.where(core == 0, part, 0.0), jnp.where(core == 1, part, 0.0)]
    vector_part = moves.sum_reps(
        jnp.concatenate(
            [grad_gain_one, grad_shift_one]
            + spread_heads(grad_bias_q_part)
            + spread_heads(grad_bias_v_part)
            + [grad_bias_out, grad_gain_two, grad_shift_two]
            + bias_up_parts
            + [grad_bias_down]
        )
    )
    vector_rows = vector_part.reshape(2, -1)
    all_sums = summed(moves, to_sum(0) + to_sum(1) + to_sum(2) + to_sum(3) + [vector_rows])
    sums = [all_sums[0:2], all_sums[2:4], all_sums[4:6], all_sums[6:8]]
    vector_grad = all_sums[8].reshape(-1)
    updates = []
    offset = 0
    for number in range(4):
        end_col = offset + gradients[number].shape[1]
        updates.append(
            factor_apply(
                gradients[number],
                weights[number],
                stats[number][0],
                sums[number][0],
                sums[number][1],
                col_state[offset:end_col].reshape(1, -1),
                heights[number],
                decay_rate,
            )
        )
        offset = end_col
    grads_out, new_weights, copies, new_cols, rms_rows = zip(*updates)
    rms_values = [rms[0, 0] for rms in rms_rows]

    vector_state_new = decay_rate * vector_state + (1.0 - decay_rate) * (
        vector_grad * vector_grad + eps_second
    )
    vector_step = vector_grad * lax.rsqrt(vector_state_new)
    vector_rms = jnp.sqrt(jnp.mean(vector_step * vector_step))
    vector_new = vectors - rate_step * jnp.sqrt(
        jnp.mean(vectors * vectors)
    ) * vector_step / jnp.maximum(1.0, vector_rms / clip_level)
    update_rms = jnp.stack(rms_values + [vector_rms])
    return (
        block_out,
        tokens_grad,
        *grads_out,
        vector_grad,
        *new_weights,
        vector_new,
        *copies,
        jnp.concatenate([stats[0][1], stats[1][1], stats[2][1]], axis=0),
        stats[3][1].reshape(-1),
        jnp.concatenate(new_cols, axis=1).reshape(-1),
        vector_state_new,
        update_rms,
    )


def solution(mesh):
    in_specs = (
        P(("rep", "shard"), None),
        P(("rep", "shard"), None),
        P("rep", None),
        P("shard", None),
        P("shard", None),
        P("shard", None),
        P("shard", None),
        P(),
        P(None, "shard"),
        P("shard"),
        P(),
        P(),
    )
    out_specs = (
        P(("rep", "shard"), None),
        P(("rep", "shard"), None),
        P("shard", None),
        P("shard", None),
        P("shard", None),
        P("shard", None),
        P(),
        P("shard", None),
        P("shard", None),
        P("shard", None),
        P("shard", None),
        P(),
        P("shard", None),
        P("shard", None),
        P("shard", None),
        P("shard", None),
        P(None, "shard"),
        P("shard"),
        P(),
        P(),
        P(),
    )
    return jax.shard_map(
        on_device, mesh=mesh, in_specs=in_specs, out_specs=out_specs, check_vma=False
    )
```

```python
import functools

import jax
import jax.numpy as jnp
from jax import lax
from jax.experimental import pallas as pl
from jax.experimental.pallas import tpu as pltpu
from jax.sharding import PartitionSpec as P

HEADS = 16
STEP = 10
BLOCK = 256


eps_norm = 1e-05
eps_second = 1e-30
rate_step = 0.5
clip_level = 1.0
masked = -1e30
gelu_root = (2.0 / 3.141592653589793) ** 0.5
gelu_cubic = 0.044715

f32 = jnp.float32
bf16 = jnp.bfloat16


def norm_parts(values):
    average = jnp.mean(values, axis=-1, keepdims=True)
    centred = values - average
    inv_std = lax.rsqrt(jnp.mean(centred * centred, axis=-1, keepdims=True) + eps_norm)
    return (centred * inv_std, inv_std)


def norm_back(grad_out, normed, inv_std, gain_vec):
    grad_normed = grad_out * gain_vec
    inner_mean = jnp.mean(grad_normed * normed, axis=-1, keepdims=True)
    centred = grad_normed - jnp.mean(grad_normed, axis=-1, keepdims=True)
    return (centred - normed * inner_mean) * inv_std


def gelu_value(pre_act):
    curve = jnp.tanh(gelu_root * (pre_act + gelu_cubic * pre_act * pre_act * pre_act))
    return 0.5 * pre_act * (1.0 + curve)


def gelu_slope(pre_act):
    square = pre_act * pre_act
    curve = jnp.tanh(gelu_root * (pre_act + gelu_cubic * square * pre_act))
    inner = gelu_root * (1.0 + 3.0 * gelu_cubic * square)
    return 0.5 * (1.0 + curve) + 0.5 * pre_act * (1.0 - curve * curve) * inner


def dot(left_side, right_side):
    return jnp.dot(left_side, right_side, preferred_element_type=f32)


def dot_right(left_side, right_side):
    return lax.dot_general(
        left_side, right_side, (((1,), (1,)), ((), ())), preferred_element_type=f32
    )


def dot_rows(left_side, right_side):
    return lax.dot_general(
        left_side, right_side, (((0,), (0,)), ((), ())), preferred_element_type=f32
    )


def pick(stack, index, axis=0):
    return lax.dynamic_index_in_dim(stack, index, axis, keepdims=False, allow_negative_indices=False)


def cut_rows(values, start, count):
    return lax.dynamic_slice_in_dim(values, start, count, 0, allow_negative_indices=False)


def place(stack, part, index, axis=0):
    return lax.dynamic_update_index_in_dim(stack, part, index, axis, allow_negative_indices=False)


def head_rows(number, head_width):
    return slice(number * head_width, (number + 1) * head_width)


def lane_masks(block_rows, width, heads):
    lanes = lax.broadcasted_iota(jnp.int32, (block_rows, width), 1)
    head_width = width // heads
    return [
        (lanes >= number * head_width) & (lanes < (number + 1) * head_width)
        for number in range(heads)
    ]


def allowed_pairs(key_block, query_block, start_row, block):
    key_pos = lax.broadcasted_iota(jnp.int32, (block, block), 0) + key_block * block
    query_pos = lax.broadcasted_iota(jnp.int32, (block, block), 1) + query_block * block
    return (key_pos <= query_pos) & (key_pos >= start_row)


def key_offsets(key_block, query_block, block):
    rows = lax.broadcasted_iota(jnp.int32, (block, 1), 0)
    return (rows + (key_block - query_block) * block).astype(f32)


def turned(values):
    return jnp.transpose(values.astype(f32))


def head_stack(values, lanes):
    zero = jnp.zeros(values.shape, values.dtype)
    return jnp.concatenate([jnp.where(lane, values, zero) for lane in lanes], axis=0)


def eights(values, combine):
    rows, columns = values.shape
    return combine(values.reshape(rows // 8, 8, columns), axis=0)


def forward_kernel(
    heads,
    block,
    low_ref,
    mid_ref,
    slope_ref,
    start_ref,
    qkv_ref,
    out_ref,
    log_ref,
    values_turned,
    key_stack,
    score_ref,
):
    tokens = qkv_ref.shape[0]
    width = qkv_ref.shape[1] // 3
    head_width = width // heads
    blocks = tokens // block
    query_block = pl.program_id(0)

    @pl.when(query_block == 0)
    def _():
        lanes = lane_masks(block, width, heads)
        for number in range(blocks):
            rows = slice(number * block, (number + 1) * block)
            values_turned[number] = turned(qkv_ref[rows, 2 * width :]).astype(bf16)
            key_stack[number] = head_stack(qkv_ref[rows, width : 2 * width], lanes)

    first_row = pl.multiple_of(query_block * block, block)
    queries = qkv_ref[pl.ds(first_row, block), :width].astype(f32) * head_width ** (-0.5)
    queries = turned(queries).astype(bf16)
    start_row = start_ref[query_block]

    def score_step(key_block, bests, with_mask):
        scores = dot(key_stack[key_block], queries)
        offsets = key_offsets(key_block, query_block, block)
        allowed = allowed_pairs(key_block, query_block, start_row, block) if with_mask else None
        result = []
        for number in range(heads):
            rows = head_rows(number, block)
            part = scores[rows] + slope_ref[number] * offsets
            if with_mask:
                part = jnp.where(allowed, part, masked)
            score_ref[key_block, rows, :] = part
            result.append(jnp.maximum(bests[number], eights(part, jnp.max)))
        return tuple(result)

    low, mid = low_ref[query_block], mid_ref[query_block]
    bests = tuple(jnp.full((8, block), masked, f32) for _ in range(heads))
    bests = lax.fori_loop(low, mid, functools.partial(score_step, with_mask=True), bests)
    bests = lax.fori_loop(mid, query_block, functools.partial(score_step, with_mask=False), bests)
    bests = score_step(query_block, bests, True)
    bests = [jnp.max(best, axis=0, keepdims=True) for best in bests]

    def value_step(key_block, state):
        result = []
        for number in range(heads):
            total, gathered = state[2 * number : 2 * number + 2]
            weights = jnp.exp(score_ref[key_block, head_rows(number, block), :] - bests[number])
            value_rows = values_turned[key_block, head_rows(number, head_width), :]
            result += [
                total + eights(weights, jnp.sum),
                gathered + dot(value_rows, weights.astype(bf16)),
            ]
        return tuple(result)

    state = ()
    for number in range(heads):
        state += (jnp.zeros((8, block), f32), jnp.zeros((head_width, block), f32))
    state = lax.fori_loop(low, query_block + 1, value_step, state)
    columns = []
    for number in range(heads):
        total = jnp.sum(state[2 * number], axis=0, keepdims=True)
        columns.append(state[2 * number + 1] / total)
        log_ref[0, number : number + 1, :] = bests[number] + jnp.log(total)
    out_ref[...] = jnp.transpose(jnp.concatenate(columns, axis=0)).astype(bf16)


def backward_kernel(heads, block, first_head, merge, *refs):
    full_ref, high_ref, slope_ref, start_ref, log_ref, qkv_ref, grad_ref, out_ref = refs[:8]
    earlier_ref = refs[8] if merge else None
    result_ref = refs[9 if merge else 8]
    (
        queries_turned,
        grads_turned,
        keys_turned,
        query_stack,
        grad_stack,
        key_stack,
        value_stack,
        delta_rows,
        query_grads,
    ) = refs[10 if merge else 9 :]
    tokens, all_width = grad_ref.shape
    head_width = all_width // log_ref.shape[1]
    width = heads * head_width
    scale = head_width ** (-0.5)
    blocks = tokens // block
    key_block = pl.program_id(0)
    lanes = lane_masks(block, width, heads)

    def columns(kind):
        start = kind * all_width + first_head * head_width
        return slice(start, start + width)

    def target(kind):
        start = (kind * all_width + first_head * head_width) if merge else kind * width
        return slice(start, start + width)

    @pl.when(key_block == 0)
    def _():
        for number in range(blocks):
            rows = slice(number * block, (number + 1) * block)
            queries = qkv_ref[rows, columns(0)]
            queries_turned[number] = turned(queries.astype(f32) * scale).astype(bf16)
            query_stack[number] = head_stack(queries, lanes)
            keys_turned[number] = turned(qkv_ref[rows, columns(1)]).astype(bf16)
            grads = grad_ref[rows, columns(0)]
            grad_stack[number] = head_stack(grads, lanes)
            grads = grads.astype(f32)
            grads_turned[number] = turned(grads).astype(bf16)
            product = turned(grads * out_ref[rows, columns(0)].astype(f32))
            for head in range(heads):
                delta_rows[number, head : head + 1, :] = jnp.sum(
                    product[head_rows(head, head_width)], axis=0, keepdims=True
                )
            query_grads[number] = jnp.zeros((width, block), f32)

    key_row = pl.multiple_of(key_block * block, block)
    key_stack[...] = head_stack(qkv_ref[pl.ds(key_row, block), columns(1)], lanes)
    value_stack[...] = head_stack(qkv_ref[pl.ds(key_row, block), columns(2)], lanes)

    def step(query_block, state, with_mask):
        key_total, value_total = state
        scores = dot(key_stack[...], queries_turned[query_block])
        grad_weights = dot(value_stack[...], grads_turned[query_block])
        offsets = key_offsets(key_block, query_block, block)
        if with_mask:
            allowed = allowed_pairs(key_block, query_block, start_ref[query_block], block)
        weight_list, grad_list = [], []
        for number in range(heads):
            rows = head_rows(number, block)
            head = first_head + number
            part = scores[rows] + slope_ref[head] * offsets
            part = part - log_ref[query_block, head : head + 1, :]
            if with_mask:
                part = jnp.where(allowed, part, masked)
            probabilities = jnp.exp(part)
            delta = delta_rows[query_block, number : number + 1, :]
            grad_scores = (probabilities * (grad_weights[rows] - delta)).astype(bf16)
            weight_list.append(probabilities.astype(bf16))
            grad_list.append(grad_scores)
            rows = head_rows(number, head_width)
            query_grads[query_block, rows, :] += dot(keys_turned[key_block, rows, :], grad_scores)
        weight_row = jnp.concatenate(weight_list, axis=1)
        grad_row = jnp.concatenate(grad_list, axis=1)
        return (
            key_total + dot(grad_row, query_stack[query_block]),
            value_total + dot(weight_row, grad_stack[query_block]),
        )

    state = (jnp.zeros((block, width), f32), jnp.zeros((block, width), f32))
    state = step(key_block, state, True)
    full, high = full_ref[key_block], high_ref[key_block]
    state = lax.fori_loop(key_block + 1, full, functools.partial(step, with_mask=False), state)
    state = lax.fori_loop(full, high, functools.partial(step, with_mask=True), state)
    result_ref[pl.ds(key_row, block), target(1)] = (state[0] * scale).astype(bf16)
    result_ref[pl.ds(key_row, block), target(2)] = state[1].astype(bf16)
    if merge:
        other = first_head * head_width
        for kind in range(3):
            result_ref[pl.ds(key_row, block), kind * all_width : kind * all_width + other] = earlier_ref[
                pl.ds(key_row, block), kind * other : (kind + 1) * other
            ]

    @pl.when(key_block == blocks - 1)
    def _():
        for number in range(blocks):
            rows = slice(number * block, (number + 1) * block)
            result_ref[rows, target(0)] = jnp.transpose(query_grads[number] * scale).astype(bf16)


def block_plan(lengths, tokens, block):
    ends = jnp.cumsum(lengths)
    positions = jnp.arange(tokens, dtype=jnp.int32)
    passed = positions[:, None] >= ends[None, :]
    starts = jnp.max(jnp.where(passed, ends[None, :], 0), axis=1).astype(jnp.int32)
    finish = jnp.min(jnp.where(passed, tokens, ends[None, :]), axis=1).astype(jnp.int32)
    blocks = tokens // block
    number = jnp.arange(blocks, dtype=jnp.int32)
    first_start = starts[::block]
    last_start = starts[block - 1 :: block]
    low = first_start // block
    mid = jnp.clip((last_start + block - 1) // block, low, number)
    high = (finish[block - 1 :: block] - 1) // block + 1
    full = jnp.clip(finish[::block] // block, number + 1, high)
    return (starts.reshape(blocks, 1, block), low, mid, full, high)


def scalar_spec():
    return pl.BlockSpec(memory_space=pltpu.SMEM)


def whole_spec(shape):
    return pl.BlockSpec(shape, lambda step: (0,) * len(shape), pipeline_mode=pl.Buffered(1))


def attend_forward(qkv, plan, slopes, heads, block):
    tokens, triple = qkv.shape
    width = triple // 3
    blocks = tokens // block
    starts, low, mid, full, high = plan
    return pl.pallas_call(
        functools.partial(forward_kernel, heads, block),
        grid=(blocks,),
        in_specs=[
            scalar_spec(),
            scalar_spec(),
            scalar_spec(),
            whole_spec((blocks, 1, block)),
            whole_spec((tokens, triple)),
        ],
        out_specs=[
            pl.BlockSpec((block, width), lambda step: (step, 0)),
            pl.BlockSpec((1, heads, block), lambda step: (step, 0, 0)),
        ],
        out_shape=[
            jax.ShapeDtypeStruct((tokens, width), bf16),
            jax.ShapeDtypeStruct((blocks, heads, block), f32),
        ],
        scratch_shapes=[
            pltpu.VMEM((blocks, width, block), bf16),
            pltpu.VMEM((blocks, heads * block, width), bf16),
            pltpu.VMEM((blocks, heads * block, block), f32),
        ],
        compiler_params=pltpu.CompilerParams(
            dimension_semantics=("arbitrary",), vmem_limit_bytes=24 * 1024 * 1024
        ),
        cost_estimate=pl.CostEstimate(
            flops=3 * tokens * tokens * 256 * heads,
            bytes_accessed=10 * tokens * width,
            transcendentals=tokens * tokens * heads // 2,
        ),
        name="attend_forward",
    )(low, mid, slopes, starts, qkv)


def attend_backward(qkv, grads, outputs, logs, plan, slopes, heads, block, first_head, earlier):
    tokens, triple = qkv.shape
    all_width = triple // 3
    all_heads = logs.shape[1]
    width = all_width // all_heads * heads
    blocks = tokens // block
    starts, low, mid, full, high = plan
    merge = earlier is not None
    result_width = triple if merge else 3 * width
    operands = [full, high, slopes, starts, logs, qkv, grads, outputs]
    specs = [scalar_spec() for _ in range(3)] + [whole_spec(entry.shape) for entry in operands[3:]]
    if merge:
        operands.append(earlier)
        specs.append(whole_spec(earlier.shape))
    return pl.pallas_call(
        functools.partial(backward_kernel, heads, block, first_head, merge),
        grid=(blocks,),
        in_specs=specs,
        out_specs=pl.BlockSpec((tokens, result_width), lambda step: (0, 0)),
        out_shape=jax.ShapeDtypeStruct((tokens, result_width), bf16),
        scratch_shapes=[
            pltpu.VMEM((blocks, width, block), bf16),
            pltpu.VMEM((blocks, width, block), bf16),
            pltpu.VMEM((blocks, width, block), bf16),
            pltpu.VMEM((blocks, heads * block, width), bf16),
            pltpu.VMEM((blocks, heads * block, width), bf16),
            pltpu.VMEM((heads * block, width), bf16),
            pltpu.VMEM((heads * block, width), bf16),
            pltpu.VMEM((blocks, heads, block), f32),
            pltpu.VMEM((blocks, width, block), f32),
        ],
        compiler_params=pltpu.CompilerParams(
            dimension_semantics=("arbitrary",), vmem_limit_bytes=24 * 1024 * 1024
        ),
        cost_estimate=pl.CostEstimate(
            flops=8 * tokens * tokens * 256 * heads,
            bytes_accessed=20 * tokens * width,
            transcendentals=tokens * tokens * heads // 2,
        ),
        name="attend_backward",
    )(*operands)


def hidden_backward_kernel(own_ref, other_ref, weight_ref, slope_ref, result_ref, total_ref):
    rows = own_ref.shape[0]
    total = jnp.zeros(total_ref.shape, f32)
    for number, ref in enumerate((own_ref, other_ref)):
        part = slice(number * rows, (number + 1) * rows)
        grads = dot_right(ref[...], weight_ref[...]) * slope_ref[part, :].astype(f32)
        grads = grads.astype(bf16)
        result_ref[part, :] = grads
        total = total + jnp.sum(grads.astype(f32), axis=0, keepdims=True)
    total_ref[...] = total


def hidden_backward(weight, cot_own, cot_other, slopes):
    rows, width = cot_own.shape
    breadth = slopes.shape[1]
    tile = min(512, breadth)
    return pl.pallas_call(
        hidden_backward_kernel,
        grid=(breadth // tile,),
        in_specs=[
            whole_spec((rows, width)),
            whole_spec((rows, width)),
            pl.BlockSpec((tile, width), lambda step: (step, 0)),
            pl.BlockSpec((2 * rows, tile), lambda step: (0, step)),
        ],
        out_specs=[
            pl.BlockSpec((2 * rows, tile), lambda step: (0, step)),
            pl.BlockSpec((1, tile), lambda step: (0, step)),
        ],
        out_shape=[
            jax.ShapeDtypeStruct((2 * rows, breadth), bf16),
            jax.ShapeDtypeStruct((1, breadth), f32),
        ],
        compiler_params=pltpu.CompilerParams(
            dimension_semantics=("arbitrary",), vmem_limit_bytes=20 * 1024 * 1024
        ),
        cost_estimate=pl.CostEstimate(flops=1, bytes_accessed=1, transcendentals=0),
        name="hidden_backward",
    )(cot_own, cot_other, weight, slopes)


def up_backward_kernel(grads_ref, weight_ref, result_ref):
    result_ref[...] = dot_right(grads_ref[...], weight_ref[...]).astype(result_ref.dtype)


def up_backward(weight, grads, number, kind_of):
    rows, breadth = grads.shape[0] // 2, grads.shape[1]
    width = weight.shape[0]
    tile = width // 4
    return pl.pallas_call(
        up_backward_kernel,
        grid=(4,),
        in_specs=[
            pl.BlockSpec((rows, breadth), lambda step: (number, 0)),
            pl.BlockSpec((tile, breadth), lambda step: (step, 0)),
        ],
        out_specs=pl.BlockSpec((rows, tile), lambda step: (0, step)),
        out_shape=jax.ShapeDtypeStruct((rows, width), kind_of),
        compiler_params=pltpu.CompilerParams(
            dimension_semantics=("arbitrary",), vmem_limit_bytes=12 * 1024 * 1024
        ),
        cost_estimate=pl.CostEstimate(flops=1, bytes_accessed=1, transcendentals=0),
        name="up_backward",
    )(grads, weight)


def down_projection_kernel(hidden_ref, weight_ref, result_ref):
    result_ref[...] = dot(hidden_ref[...], weight_ref[...]).astype(result_ref.dtype)


def down_projection(hidden, weight):
    rows, breadth = hidden.shape
    width = weight.shape[1]
    tile = min(256, rows)
    return pl.pallas_call(
        down_projection_kernel,
        grid=(rows // tile,),
        in_specs=[
            pl.BlockSpec((tile, breadth), lambda step: (step, 0)),
            whole_spec((breadth, width)),
        ],
        out_specs=pl.BlockSpec((tile, width), lambda step: (step, 0)),
        out_shape=jax.ShapeDtypeStruct((rows, width), bf16),
        compiler_params=pltpu.CompilerParams(
            dimension_semantics=("arbitrary",), vmem_limit_bytes=14 * 1024 * 1024
        ),
        cost_estimate=pl.CostEstimate(flops=1, bytes_accessed=1, transcendentals=0),
        name="down_projection",
    )(hidden, weight)


def up_gradient_kernel(own_ref, other_ref, grads_ref, result_ref, act_turned):
    rows, width = own_ref.shape
    step = 256

    @pl.when(pl.program_id(0) == 0)
    def _():
        for number, ref in enumerate((own_ref, other_ref)):
            for row in range(0, rows, step):
                first = number * rows + row
                for column in range(0, width, step):
                    block = ref[row : row + step, column : column + step]
                    act_turned[column : column + step, first : first + step] = turned(block).astype(bf16)

    result_ref[...] = dot(act_turned[...], grads_ref[...]).astype(bf16)


def up_gradient(act_own, act_other, grads):
    rows, width = act_own.shape
    breadth = grads.shape[1]
    tile = min(512, breadth)
    return pl.pallas_call(
        up_gradient_kernel,
        grid=(breadth // tile,),
        in_specs=[
            whole_spec((rows, width)),
            whole_spec((rows, width)),
            pl.BlockSpec((2 * rows, tile), lambda step: (0, step)),
        ],
        out_specs=pl.BlockSpec((width, tile), lambda step: (0, step)),
        out_shape=jax.ShapeDtypeStruct((width, breadth), bf16),
        scratch_shapes=[pltpu.VMEM((width, 2 * rows), bf16)],
        compiler_params=pltpu.CompilerParams(
            dimension_semantics=("arbitrary",), vmem_limit_bytes=16 * 1024 * 1024
        ),
        cost_estimate=pl.CostEstimate(flops=1, bytes_accessed=1, transcendentals=0),
        name="up_gradient",
    )(act_own, act_other, grads)


def together(*values):
    return lax.optimization_barrier(tuple(values))


def ordered(own, other, bit, axis=0):
    first = jnp.where(bit == 0, own, other)
    second = jnp.where(bit == 0, other, own)
    return jnp.stack([first, second], axis=axis)


class Moves:
    def __init__(self):
        self.shards = lax.axis_size("shard")
        self.reps = lax.axis_size("rep")
        self.half = self.shards // 2
        self.chips = self.reps // 2
        self.shard = lax.axis_index("shard")
        self.rep = lax.axis_index("rep")
        self.core = self.rep & 1
        self.chip = self.rep >> 1
        self.side = lax.div(self.shard, self.half)
        self.member = lax.rem(self.shard, self.half) + self.core * self.half

    def core_swap(self, part):
        return lax.ppermute(part, "rep", [(r, r ^ 1) for r in range(self.reps)])

    def chip_swap(self, part, bits):
        return lax.ppermute(part, "rep", [(r, r ^ (2 * bits)) for r in range(self.reps)])

    def shard_swap(self, part, bits):
        return lax.ppermute(part, "shard", [(s, s ^ bits) for s in range(self.shards)])

    def shard_bit(self, bits):
        return lax.div(self.shard, bits) & 1

    def low_bits(self):
        bits, result = 1, []
        while bits < self.half:
            result.append(bits)
            bits *= 2
        return result

    def home_send(self, part):
        pairs = []
        for rep in range(self.reps):
            for shard in range(self.shards):
                if shard // self.half != rep % 2:
                    to_shard = (shard + self.half) % self.shards
                    pairs.append((rep * self.shards + shard, (rep ^ 1) * self.shards + to_shard))
        return lax.ppermute(part, ("rep", "shard"), pairs)

    def home_join(self, part, other):
        return jnp.where(self.side == self.core, part, other)

    def half_gather(self, part):
        stack = part[None]
        for bits in self.low_bits():
            own = stack
            stack = ordered(own, self.shard_swap(own, bits), self.shard_bit(bits))
            stack = stack.reshape((-1,) + part.shape)
        return stack

    def cores_gather(self, stack):
        stack = ordered(stack, self.core_swap(stack), self.core)
        return stack.reshape((-1,) + stack.shape[2:])

    def exchange_bit(self, stack, bit, swap):
        sources, targets = stack.shape[:2]
        stack = stack.reshape((sources, 2, targets // 2) + stack.shape[2:])
        own, other = pick(stack, bit, 1), swap(pick(stack, 1 - bit, 1))
        return ordered(own, other, bit, 1).reshape((2 * sources,) + own.shape[1:])

    def half_exchange(self, stack):
        stack = stack[None]
        for bits in reversed(self.low_bits()):
            swap = functools.partial(self.shard_swap, bits=bits)
            stack = self.exchange_bit(stack, self.shard_bit(bits), swap)
        return stack.reshape((self.half,) + stack.shape[2:])

    def cores_exchange(self, stack):
        return self.exchange_bit(stack[None], self.core, self.core_swap)

    def members_exchange(self, stack):
        for bits in reversed(self.low_bits()):
            swap = functools.partial(self.shard_swap, bits=bits)
            stack = self.exchange_bit(stack, self.shard_bit(bits), swap)
        return stack.reshape((self.shards,) + stack.shape[2:])

    def reduce_bit(self, stack, bit, swap):
        stack = stack.reshape((2, stack.shape[0] // 2) + stack.shape[1:])
        other = swap(pick(stack, 1 - bit).astype(bf16))
        return pick(stack, bit).astype(f32) + other.astype(f32)

    def spread_open(self, part):
        if self.chips == 4:
            return (self.chip_swap(part, 1), self.chip_swap(part, 2))
        held, bits = [part], 1
        while bits < self.chips:
            held = held + [self.chip_swap(piece, bits) for piece in held]
            bits *= 2
        return tuple(held[1:])

    def spread_close(self, state):
        if self.chips == 4:
            by_x, by_y = state
            cut, axis = by_x.shape[-2] // 2, by_x.ndim - 2
            far = [
                self.chip_swap(by_x[..., :cut, :], 2),
                self.chip_swap(by_y[..., cut:, :], 1),
            ]
            return (by_x, by_y, jnp.concatenate(far, axis=axis))
        return state

    def far_open(self, states):
        if self.chips != 4:
            return ()
        cut = states[0][0].shape[0] // 2
        return (
            self.chip_swap(jnp.concatenate([by_x[:cut] for by_x, _ in states], axis=0), 2),
            self.chip_swap(jnp.concatenate([by_y[cut:] for _, by_y in states], axis=0), 1),
        )

    def far_parts(self, states, far):
        if self.chips != 4:
            return [[(k + 1, 0, part) for k, part in enumerate(state)] for state in states]
        cut = states[0][0].shape[0] // 2
        result = []
        for number, (by_x, by_y) in enumerate(states):
            rows = slice(number * cut, (number + 1) * cut)
            result.append([(1, 0, by_x), (2, 0, by_y), (3, 0, far[0][rows]), (3, cut, far[1][rows])])
        return result

    def chips_gather(self, part, axis, state=None):
        shape = part.shape[:axis] + (self.chips,) + part.shape[axis:]
        stack = place(jnp.zeros(shape, part.dtype), part, self.chip, axis)
        others = self.spread_close(self.spread_open(part) if state is None else state)
        for number, piece in enumerate(others):
            stack = place(stack, piece, self.chip ^ (number + 1), axis)
        return stack

    def reduce_open(self, stack, axis):
        return self.reduce_start(self.reduce_cut(stack, axis), axis)

    def reduce_cut(self, stack, axis):
        if self.chips != 4:
            return (stack,)
        shape = stack.shape[:axis] + (2, 2) + stack.shape[axis + 1 :]
        stack = stack.reshape(shape)
        bit_x, bit_y = self.chip & 1, self.chip >> 1
        cut = shape[0] // 2
        first, second = stack[:cut], stack[cut:]
        return (
            pick(first, bit_x, axis + 1),
            pick(second, bit_y, axis),
            pick(first, 1 - bit_x, axis + 1),
            pick(second, 1 - bit_y, axis),
        )

    def reduce_start(self, parts, axis):
        if self.chips == 4:
            first, second, send_first, send_second = parts
            return (first, second, self.chip_swap(send_first, 1), self.chip_swap(send_second, 2))
        (stack,) = parts
        count = self.chips
        stack = stack.astype(f32)
        while count > 1:
            count //= 2
            shape = stack.shape[:axis] + (2, count) + stack.shape[axis + 1 :]
            stack = stack.reshape(shape)
            bit = lax.div(self.chip, count) & 1
            got = self.chip_swap(pick(stack, 1 - bit, axis).astype(bf16), count)
            stack = pick(stack, bit, axis) + got.astype(f32)
        return (pick(stack, 0, axis).astype(bf16),)

    def reduce_add(self, state):
        if self.chips != 4:
            return state
        first, second, got_first, got_second = state
        first = (first.astype(f32) + got_first.astype(f32)).astype(bf16)
        second = (second.astype(f32) + got_second.astype(f32)).astype(bf16)
        return (first, second)

    def reduce_send(self, state, axis):
        if self.chips != 4:
            return state
        first, second = state
        bit_x, bit_y = self.chip & 1, self.chip >> 1
        got_first = self.chip_swap(pick(first, 1 - bit_y, axis), 2)
        got_second = self.chip_swap(pick(second, 1 - bit_x, axis), 1)
        return (pick(first, bit_y, axis), pick(second, bit_x, axis), got_first, got_second)

    def reduce_final(self, state):
        if self.chips != 4:
            return state[0]
        first, second, got_first, got_second = state
        first = first.astype(f32) + got_first.astype(f32)
        second = second.astype(f32) + got_second.astype(f32)
        return jnp.concatenate([first, second], axis=0).astype(bf16)

    def reduce_close(self, state, axis):
        return self.reduce_final(self.reduce_send(state, axis))

    def core_pair(self, part):
        other = self.core_swap(part)
        first = jnp.where(self.core == 0, part, other)
        second = jnp.where(self.core == 0, other, part)
        return first, second

    def sum_reps(self, vector):
        bits = 1
        while bits < self.reps:
            vector = vector + lax.ppermute(vector, "rep", [(r, r ^ bits) for r in range(self.reps)])
            bits *= 2
        return vector

    def sum_shards(self, vector):
        bits = 1
        while bits < self.shards:
            vector = vector + self.shard_swap(vector, bits)
            bits *= 2
        return vector


def stats_kernel(decay_rate, gradient_ref, old_ref, rows_ref, lane_rows_ref, sums_ref, total_ref, partial):
    step = pl.program_id(0)
    rows, columns = gradient_ref.shape

    @pl.when(step == 0)
    def _():
        partial[...] = jnp.zeros_like(partial)
        total_ref[...] = jnp.zeros_like(total_ref)

    gradient = gradient_ref[...].astype(f32)
    square = gradient * gradient
    row_mean = jnp.sum(square, axis=1, keepdims=True) / columns
    old = jnp.transpose(jnp.broadcast_to(old_ref[...], (128, rows)))[:, 0:1]
    rows_new = decay_rate * old + (1.0 - decay_rate) * (row_mean + eps_second)
    rows_ref[...] = rows_new
    lane_rows_ref[...] = jnp.transpose(jnp.broadcast_to(rows_new, (rows, 128)))[0:1, :]
    total_ref[...] += jnp.broadcast_to(jnp.sum(rows_new, axis=0, keepdims=True), (1, 128))
    partial[0:8, :] += eights(square, jnp.sum)
    partial[8:16, :] += eights(square * (1.0 / rows_new), jnp.sum)

    @pl.when(step == pl.num_programs(0) - 1)
    def _():
        sums_ref[0:1, :] = jnp.sum(partial[0:8, :], axis=0, keepdims=True)
        sums_ref[1:2, :] = jnp.sum(partial[8:16, :], axis=0, keepdims=True)


def factor_stats(gradient, rows_old, decay_rate):
    height, breadth = gradient.shape
    rows = min(256 if breadth <= 1024 else 128, height)
    return pl.pallas_call(
        functools.partial(stats_kernel, decay_rate),
        grid=(height // rows,),
        in_specs=[
            pl.BlockSpec((rows, breadth), lambda step: (step, 0)),
            pl.BlockSpec((1, rows), lambda step: (0, step)),
        ],
        out_specs=[
            pl.BlockSpec((rows, 1), lambda step: (step, 0)),
            pl.BlockSpec((1, rows), lambda step: (0, step)),
            pl.BlockSpec((2, breadth), lambda step: (0, 0)),
            pl.BlockSpec((1, 128), lambda step: (0, 0)),
        ],
        out_shape=[
            jax.ShapeDtypeStruct((height, 1), f32),
            jax.ShapeDtypeStruct((1, height), f32),
            jax.ShapeDtypeStruct((2, breadth), f32),
            jax.ShapeDtypeStruct((1, 128), f32),
        ],
        scratch_shapes=[pltpu.VMEM((16, breadth), f32)],
        compiler_params=pltpu.CompilerParams(
            dimension_semantics=("arbitrary",), vmem_limit_bytes=12 * 1024 * 1024
        ),
        name="factor_stats",
    )(gradient, rows_old)


def apply_kernel(
    decay_rate,
    height,
    gradient_ref,
    weight_ref,
    rows_ref,
    sums_ref,
    scalar_ref,
    old_ref,
    gradient_out,
    weight_out,
    copy_out,
    cols_out,
    rms_out,
    col_factor,
):
    columns = gradient_ref.shape[1]

    @pl.when(pl.program_id(0) == 0)
    def _():
        cols_new = decay_rate * old_ref[...] + (1.0 - decay_rate) * (
            sums_ref[0:1, :] / height + eps_second
        )
        row_mean = scalar_ref[0:1, 0:1] / height
        weight_mean = scalar_ref[1:2, 0:1] / (height * columns)
        scaled = jnp.sum(sums_ref[1:2, :] / cols_new, axis=1, keepdims=True)
        rms_update = jnp.sqrt(row_mean / (height * columns) * scaled)
        factor = rate_step * jnp.sqrt(weight_mean) * jnp.sqrt(row_mean)
        factor = factor / jnp.maximum(1.0, rms_update / clip_level)
        col_factor[...] = factor * lax.rsqrt(cols_new)
        cols_out[...] = cols_new
        rms_out[...] = jnp.broadcast_to(rms_update, (1, 128))

    gradient = gradient_ref[...].astype(f32)
    new_weight = weight_ref[...] - gradient * lax.rsqrt(rows_ref[...]) * col_factor[...]
    gradient_out[...] = gradient
    weight_out[...] = new_weight
    copy_out[...] = new_weight.astype(bf16)


def factor_apply(gradient, weight, rows_new, sums, scalars, cols_old, height, decay_rate):
    own_height, breadth = gradient.shape
    rows = min(256 if breadth <= 1024 else 64, own_height)

    def rows_spec():
        return pl.BlockSpec((rows, breadth), lambda step: (step, 0))

    def row_spec(count, wide):
        return pl.BlockSpec((count, wide), lambda step: (0, 0))

    return pl.pallas_call(
        functools.partial(apply_kernel, decay_rate, height),
        grid=(own_height // rows,),
        in_specs=[
            rows_spec(),
            rows_spec(),
            pl.BlockSpec((rows, 1), lambda step: (step, 0)),
            row_spec(2, breadth),
            row_spec(2, 128),
            row_spec(1, breadth),
        ],
        out_specs=[rows_spec(), rows_spec(), rows_spec(), row_spec(1, breadth), row_spec(1, 128)],
        out_shape=[
            jax.ShapeDtypeStruct((own_height, breadth), f32),
            jax.ShapeDtypeStruct((own_height, breadth), f32),
            jax.ShapeDtypeStruct((own_height, breadth), bf16),
            jax.ShapeDtypeStruct((1, breadth), f32),
            jax.ShapeDtypeStruct((1, 128), f32),
        ],
        scratch_shapes=[pltpu.VMEM((1, breadth), f32)],
        compiler_params=pltpu.CompilerParams(
            dimension_semantics=("arbitrary",), vmem_limit_bytes=14 * 1024 * 1024
        ),
        name="factor_apply",
    )(gradient, weight, rows_new, sums, scalars, cols_old)


def summed(moves, entries):
    total = moves.sum_shards(jnp.concatenate(entries, axis=1))
    result, offset = [], 0
    for entry in entries:
        result.append(total[:, offset : offset + entry.shape[1]])
        offset += entry.shape[1]
    return result


def on_device(
    tokens,
    cotangent,
    seq_lengths,
    qkv_weight,
    out_weight,
    up_weight,
    down_weight,
    vectors,
    row_state,
    down_rows,
    col_state,
    vector_state,
):
    moves = Moves()
    shards, half, chips, core = moves.shards, moves.half, moves.chips, moves.core
    row_count, width = tokens.shape
    hidden_width = up_weight.shape[1]
    group_rows = row_count * shards
    heads = HEADS // shards
    head_width = width // HEADS
    span = heads * head_width
    member = moves.member
    decay_rate = 1.0 - STEP ** (-0.8)
    head_number = (member * heads + jnp.arange(heads, dtype=jnp.int32)).astype(f32)
    slopes = jnp.exp2(-8.0 * (head_number + 1.0) / HEADS)

    gain_one = vectors[0:width]
    shift_one = vectors[width : 2 * width]
    bias_query = vectors[2 * width : 3 * width]
    bias_value = vectors[3 * width : 4 * width]
    bias_out = vectors[4 * width : 5 * width]
    gain_two = vectors[5 * width : 6 * width]
    shift_two = vectors[6 * width : 7 * width]
    bias_up = vectors[7 * width : 7 * width + hidden_width]
    bias_down = vectors[7 * width + hidden_width :]

    other_tokens = moves.home_send(tokens)
    other_lengths = moves.core_swap(seq_lengths)
    lengths = jnp.where(moves.side == core, seq_lengths, other_lengths)[0]
    plan = block_plan(lengths, group_rows, BLOCK)
    rows_z = width // shards
    rows_piece = rows_z // chips
    my_rows = cut_rows(qkv_weight, moves.chip * rows_piece, rows_piece)
    my_rows = my_rows.astype(bf16)
    my_blocks = []
    for number in range(half):
        kinds = []
        for kind in range(3):
            first = kind * width + number * span
            second = first + half * span
            kinds.append(
                jnp.where(
                    core == 0, my_rows[:, first : first + span], my_rows[:, second : second + span]
                )
            )
        my_blocks.append(jnp.concatenate(kinds, axis=1))
    qkv_part = moves.half_exchange(jnp.stack(my_blocks))
    half_cols = hidden_width // (2 * shards)
    up_wide = shards * half_cols
    out_wide = width // 2
    down_piece = half_cols // chips

    def core_half(values):
        parts = []
        for number in range(shards):
            start = 2 * number * half_cols
            first = values[..., start : start + half_cols]
            second = values[..., start + half_cols : start + 2 * half_cols]
            parts.append(jnp.where(core == 0, first, second))
        return jnp.concatenate(parts, axis=-1)

    up_own = core_half(up_weight).astype(bf16).reshape(chips, rows_piece, up_wide)
    out_own = jnp.where(core == 0, out_weight[:, :out_wide], out_weight[:, out_wide:]).astype(bf16)
    out_own = out_own.reshape(chips, rows_piece, out_wide)
    down_own = cut_rows(down_weight, core * half_cols, half_cols).astype(bf16)
    fold = down_piece // rows_piece
    down_own = down_own.reshape(chips, fold, rows_piece, width)
    my_down = pick(down_own, moves.chip)
    weight_piece = jnp.concatenate(
        [pick(up_own, moves.chip), pick(out_own, moves.chip)] + [my_down[k] for k in range(fold)],
        axis=1,
    )
    near_pieces, bits = [weight_piece], 1
    while bits < half:
        near_pieces = near_pieces + [moves.shard_swap(piece, bits) for piece in near_pieces]
        bits *= 2
    near_pieces = near_pieces[1:]
    weights = [qkv_weight, out_weight, up_weight, down_weight]
    weight_sums = [jnp.sum(weight * weight) for weight in weights]
    other_tokens, qkv_part, near_pieces, weight_piece, plan, weight_sums = together(
        other_tokens, qkv_part, near_pieces, weight_piece, plan, weight_sums
    )
    home_tokens = moves.home_join(tokens, other_tokens)
    far_piece = moves.shard_swap(weight_piece, half)
    near_open = [moves.spread_open(piece) for piece in near_pieces]
    qkv_far = moves.shard_swap(qkv_part, half)
    qkv_far, near_open = together(qkv_far, near_open)
    qkv_part = ordered(qkv_part, qkv_far, moves.side).reshape(shards, rows_piece, 3 * span)
    qkv_cols = moves.chips_gather(qkv_part, 1).reshape(width, 3 * span)
    inputs = home_tokens.astype(f32)
    normed_one, inv_std_one = norm_parts(inputs)
    act_one = (normed_one * gain_one + shift_one).astype(bf16)
    act_half = moves.half_gather(act_one)

    act_half, qkv_cols, far_piece = together(act_half, qkv_cols, far_piece)
    near_far = moves.far_open(near_open)
    act_all = moves.cores_gather(act_half).reshape(group_rows, width)
    far_open = moves.spread_open(far_piece)
    far_pieces, bits = [far_piece], 1
    while bits < half:
        far_pieces = far_pieces + [moves.shard_swap(piece, bits) for piece in far_pieces]
        bits *= 2
    far_pieces = far_pieces[1:]

    bias_q_part = cut_rows(bias_query, member * span, span)
    bias_v_part = cut_rows(bias_value, member * span, span)
    qkv_bias = jnp.concatenate([bias_q_part, jnp.zeros_like(bias_q_part), bias_v_part])
    qkv_rows = (dot(act_all, qkv_cols) + qkv_bias).astype(bf16)
    attended_cols, logs = attend_forward(qkv_rows, plan, slopes, heads, BLOCK)
    attended_cols, far_open, far_pieces, near_far = together(
        attended_cols, far_open, far_pieces, near_far
    )
    attended_parts = moves.cores_exchange(attended_cols.reshape(shards, row_count, span))
    attended_parts = moves.members_exchange(attended_parts)
    second_far = moves.far_open([far_open])
    last_states = [moves.spread_open(piece) for piece in far_pieces]
    attended_parts, second_far, last_states, cotangent = together(
        attended_parts, second_far, last_states, cotangent
    )
    last_far = moves.far_open(last_states)
    other_cot = moves.home_send(cotangent)
    attended = jnp.concatenate([attended_parts[k] for k in range(shards)], axis=1)

    up_all = place(jnp.zeros((shards, chips, rows_piece, up_wide), bf16), up_own, moves.shard)
    out_all = place(jnp.zeros((shards, chips, rows_piece, out_wide), bf16), out_own, moves.shard)
    down_all = place(jnp.zeros((shards, chips, fold, rows_piece, width), bf16), down_own, moves.shard)
    pieces = near_pieces + [far_piece] + far_pieces
    parts_of = moves.far_parts(near_open, near_far) + moves.far_parts([far_open], second_far)
    parts_of += moves.far_parts(last_states, last_far)
    for number, (piece, parts) in enumerate(zip(pieces, parts_of)):
        plane = moves.shard ^ (number + 1)
        for far, row, rows in [(0, 0, piece)] + parts:
            chip = moves.chip ^ far
            up_all = lax.dynamic_update_slice(
                up_all, rows[None, None, :, :up_wide], (plane, chip, row, 0), allow_negative_indices=False
            )
            out_all = lax.dynamic_update_slice(
                out_all, rows[None, None, :, up_wide : up_wide + out_wide], (plane, chip, row, 0), allow_negative_indices=False
            )
            start = up_wide + out_wide
            folds = [rows[:, start + k * width : start + (k + 1) * width] for k in range(fold)]
            down_all = lax.dynamic_update_slice(
                down_all, jnp.stack(folds)[None, None], (plane, chip, 0, row, 0), allow_negative_indices=False
            )
    up_half = up_all.reshape(width, up_wide)
    down_half = down_all.reshape(up_wide, width)
    out_first, out_second = moves.core_pair(out_all.reshape(width, out_wide))
    out_low = jnp.concatenate([out_first, out_second], axis=1)
    residual = inputs + dot(attended, out_low) + bias_out
    normed_two, inv_std_two = norm_parts(residual)
    act_two = (normed_two * gain_two + shift_two).astype(bf16)

    act_two_other, attended_other = together(
        moves.core_swap(act_two), moves.core_swap(attended)
    )
    act_two_pair = jnp.concatenate([act_two, act_two_other], axis=0)
    attended_pair = jnp.concatenate([attended, attended_other], axis=0)
    bias_up_half = core_half(bias_up)
    up_pair = dot(act_two_pair, up_half) + bias_up_half
    hidden_pair = gelu_value(up_pair).astype(bf16)
    slope_pair = gelu_slope(up_pair).astype(bf16)
    hidden_pair, slope_pair, other_cot = together(hidden_pair, slope_pair, other_cot)
    home_cot = moves.home_join(cotangent, other_cot)
    cot_other = moves.core_swap(home_cot)
    cot_pair = jnp.concatenate([home_cot, cot_other], axis=0)
    down_terms = dot_rows(hidden_pair, cot_pair).astype(bf16)
    down_state = moves.reduce_cut(down_terms.reshape(shards, chips, down_piece, width), 1)
    slope_pair, down_state = together(slope_pair, down_state)
    down_state = moves.reduce_start(down_state, 1)
    grad_y = home_cot.astype(f32)
    grad_bias_down = jnp.sum(grad_y, axis=0)
    grad_up_pair, grad_bias_up = hidden_backward(down_half, home_cot, cot_other, slope_pair)
    grad_bias_up = grad_bias_up.reshape(-1)
    back_other = moves.core_swap(up_backward(up_half, grad_up_pair, 1, bf16))
    up_terms = up_gradient(act_two, act_two_other, grad_up_pair)
    down_pair = down_projection(hidden_pair, down_half)
    back_other, down_pair, up_terms, down_state = together(
        back_other, down_pair, up_terms, down_state
    )
    up_cut = moves.reduce_cut(up_terms.reshape(shards, chips, rows_piece, up_wide), 1)
    down_sums = moves.reduce_add(down_state)
    grad_act_two = up_backward(up_half, grad_up_pair, 0, f32) + back_other.astype(f32)
    grad_gain_two = jnp.sum(grad_act_two * normed_two, axis=0)
    grad_shift_two = jnp.sum(grad_act_two, axis=0)
    grad_residual = grad_y + norm_back(grad_act_two, normed_two, inv_std_two, gain_two)
    grad_attn = grad_residual.astype(bf16)
    grad_bias_out = jnp.sum(grad_attn, axis=0, dtype=f32)
    to_members = jnp.stack(
        [
            dot_right(grad_attn, out_low[k * span : (k + 1) * span]).astype(bf16)
            for k in range(shards)
        ]
    )
    attn_halves = [grad_attn[:, :out_wide], grad_attn[:, out_wide:]]
    attn_own = jnp.where(core == 0, attn_halves[0], attn_halves[1])
    attn_other = jnp.where(core == 0, attn_halves[1], attn_halves[0])
    down_other = moves.core_swap(down_pair[row_count:])
    grad_heads, attn_other, up_cut, down_sums, down_other = together(
        moves.cores_exchange(to_members), moves.core_swap(attn_other), up_cut, down_sums, down_other
    )
    attn_pair = jnp.concatenate([attn_own, attn_other], axis=0)
    grad_heads = moves.members_exchange(grad_heads).reshape(group_rows, span)
    up_state = moves.reduce_start(up_cut, 1)
    down_mid = moves.reduce_close(down_sums, 1)
    block_out = residual + down_pair[:row_count].astype(f32) + down_other.astype(f32) + bias_down
    block_out = block_out.astype(bf16)

    out_terms = dot_rows(attended_pair, attn_pair).astype(bf16)
    def shards_halve(piece, bits):
        piece = piece.reshape((piece.shape[0] // 2, 2) + piece.shape[1:])
        bit = moves.shard_bit(bits)
        return pick(piece, bit, 1), moves.shard_swap(pick(piece, 1 - bit, 1), bits)

    def halved(state):
        own, other = state
        return (own.astype(f32) + other.astype(f32)).astype(bf16)

    def shards_sum(piece):
        rows = piece.shape[1]
        return lax.psum_scatter(
            piece.reshape(shards * rows, piece.shape[2]), "shard", scatter_dimension=0, tiled=True
        )

    grad_heads, down_mid, out_terms, block_out = together(
        grad_heads, down_mid, out_terms, block_out
    )
    block_other = moves.home_send(block_out)
    down_owned = shards_sum(down_mid)
    out_state = moves.reduce_open(out_terms.reshape(shards, chips, rows_piece, out_wide), 1)
    attend_args = (plan, slopes)
    parts = 2 if heads % 4 == 0 else 1
    part_heads = heads // parts
    grad_qkv = attend_backward(
        qkv_rows, grad_heads, attended_cols, logs, *attend_args, part_heads, BLOCK, 0, None
    )
    grad_qkv, up_state, out_state = together(grad_qkv, up_state, out_state)
    up_sums, out_sums = moves.reduce_add(up_state), moves.reduce_add(out_state)
    grad_qkv, up_sums, out_sums = together(grad_qkv, up_sums, out_sums)
    up_out_state = [
        jnp.concatenate([up_part, out_part], axis=-1) for up_part, out_part in zip(up_sums, out_sums)
    ]
    if parts == 2:
        grad_qkv = attend_backward(
            qkv_rows, grad_heads, attended_cols, logs, *attend_args, part_heads, BLOCK, part_heads, grad_qkv
        )
    grad_qkv, up_out_state, block_other, down_owned = together(
        grad_qkv, moves.reduce_send(up_out_state, 1), block_other, down_owned
    )
    block_out = moves.home_join(block_out, block_other)
    up_out_piece = moves.reduce_final(up_out_state)
    up_out_state = shards_halve(up_out_piece, 1)

    grad_bias_q_part = jnp.sum(grad_qkv[:, :span], axis=0, dtype=f32)
    grad_bias_v_part = jnp.sum(grad_qkv[:, 2 * span :], axis=0, dtype=f32)

    grad_halves = grad_qkv.reshape(2, half * row_count, 3 * span)
    sent = dot_right(pick(grad_halves, 1 - core), qkv_cols).astype(bf16)
    sent = moves.core_swap(sent)
    qkv_terms = dot_rows(act_all, grad_qkv).astype(bf16)
    qkv_terms = qkv_terms.reshape(shards, chips, rows_piece, 3 * span)
    qkv_state = moves.reduce_open(qkv_terms, 1)
    back = dot_right(pick(grad_halves, core), qkv_cols) + sent.astype(f32)
    qkv_state, back = together(qkv_state, back)

    back = back.reshape(half, row_count, width)
    low_bits = list(reversed(moves.low_bits()))
    for bits in low_bits[:-1]:
        back = moves.reduce_bit(
            back, moves.shard_bit(bits), functools.partial(moves.shard_swap, bits=bits)
        )
    back = back.reshape((2, -1) + back.shape[1:])
    back_bit = moves.shard_bit(low_bits[-1])
    back_other = moves.shard_swap(pick(back, 1 - back_bit).astype(bf16), low_bits[-1])
    qkv_state = moves.reduce_send(moves.reduce_add(qkv_state), 1)
    qkv_state, up_out_state = together(qkv_state, up_out_state)

    up_out_piece, bits = halved(up_out_state), 2
    while bits < half:
        up_out_piece = halved(shards_halve(up_out_piece, bits))
        bits *= 2
    up_out_state = shards_halve(up_out_piece, half)
    qkv_piece = moves.reduce_final(qkv_state)
    qkv_piece = qkv_piece.reshape((2, half) + qkv_piece.shape[1:])
    qkv_own = pick(qkv_piece, moves.side)
    qkv_other = moves.shard_swap(pick(qkv_piece, 1 - moves.side), half)
    back_other, qkv_other, up_out_state, down_owned = together(
        back_other, qkv_other, up_out_state, down_owned
    )

    up_out_owned = halved(up_out_state)[0]
    up_out_state = moves.spread_open(up_out_owned)
    qkv_piece = moves.half_exchange(halved((qkv_own, qkv_other)))
    down_state = moves.spread_open(down_owned)
    grad_act_one = pick(back, back_bit) + back_other.astype(f32)
    grad_act_one = grad_act_one.reshape(row_count, width)
    grad_gain_one = jnp.sum(grad_act_one * normed_one, axis=0)
    grad_shift_one = jnp.sum(grad_act_one, axis=0)
    grad_inputs = grad_residual + norm_back(grad_act_one, normed_one, inv_std_one, gain_one)
    grad_inputs, grad_gain_one, grad_shift_one, qkv_piece, down_state, up_out_state = together(
        grad_inputs.astype(bf16), grad_gain_one, grad_shift_one, qkv_piece, down_state, up_out_state
    )
    tokens_other = moves.home_send(grad_inputs)
    qkv_owned = moves.chips_gather(qkv_piece, 1)

    up_out_first, up_out_second = moves.core_pair(
        moves.chips_gather(up_out_owned, 0, tuple(up_out_state)).reshape(rows_z, up_wide + out_wide)
    )
    out_grad = jnp.concatenate([up_out_first[:, up_wide:], up_out_second[:, up_wide:]], axis=1)
    up_columns = []
    for number in range(shards):
        part = slice(number * half_cols, (number + 1) * half_cols)
        up_columns += [up_out_first[:, part], up_out_second[:, part]]
    up_grad = jnp.concatenate(up_columns, axis=1)
    down_first, down_second = moves.core_pair(
        moves.chips_gather(down_owned, 0, tuple(down_state)).reshape(half_cols, width)
    )
    down_grad = jnp.concatenate([down_first, down_second], axis=0)
    qkv_owned = qkv_owned.reshape(half, rows_z, 3 * span)
    qkv_other, tokens_other = together(moves.core_swap(qkv_owned), tokens_other)
    tokens_grad = moves.home_join(grad_inputs, tokens_other)
    qkv_first = jnp.where(core == 0, qkv_owned, qkv_other)
    qkv_second = jnp.where(core == 0, qkv_other, qkv_owned)
    qkv_columns = []
    for kind in range(3):
        for source in (qkv_first, qkv_second):
            for number in range(half):
                qkv_columns.append(source[number][:, kind * span : (kind + 1) * span])
    qkv_grad = jnp.concatenate(qkv_columns, axis=1)

    gradients = [qkv_grad, out_grad, up_grad, down_grad]
    heights = [width, width, width, hidden_width]
    rows_old = [row_state[k : k + 1] for k in range(3)] + [down_rows.reshape(1, -1)]
    stats = [
        factor_stats(gradient, old, decay_rate) for gradient, old in zip(gradients, rows_old)
    ]

    def to_sum(number):
        weight_sum = jnp.broadcast_to(weight_sums[number], (1, 128))
        return [stats[number][2], jnp.concatenate([stats[number][3], weight_sum], axis=0)]

    def spread_heads(part):
        return [jnp.where(member == number, part, 0.0) for number in range(shards)]

    bias_up_parts = []
    for number in range(shards):
        part = grad_bias_up[number * half_cols : (number + 1) * half_cols]
        bias_up_parts += [jnp.where(core == 0, part, 0.0), jnp.where(core == 1, part, 0.0)]
    vector_part = moves.sum_reps(
        jnp.concatenate(
            [grad_gain_one, grad_shift_one]
            + spread_heads(grad_bias_q_part)
            + spread_heads(grad_bias_v_part)
            + [grad_bias_out, grad_gain_two, grad_shift_two]
            + bias_up_parts
            + [grad_bias_down]
        )
    )
    vector_rows = vector_part.reshape(2, -1)
    all_sums = summed(moves, to_sum(0) + to_sum(1) + to_sum(2) + to_sum(3) + [vector_rows])
    sums = [all_sums[0:2], all_sums[2:4], all_sums[4:6], all_sums[6:8]]
    vector_grad = all_sums[8].reshape(-1)
    updates = []
    offset = 0
    for number in range(4):
        end_col = offset + gradients[number].shape[1]
        updates.append(
            factor_apply(
                gradients[number],
                weights[number],
                stats[number][0],
                sums[number][0],
                sums[number][1],
                col_state[offset:end_col].reshape(1, -1),
                heights[number],
                decay_rate,
            )
        )
        offset = end_col
    grads_out, new_weights, copies, new_cols, rms_rows = zip(*updates)
    rms_values = [rms[0, 0] for rms in rms_rows]

    vector_state_new = decay_rate * vector_state + (1.0 - decay_rate) * (
        vector_grad * vector_grad + eps_second
    )
    vector_step = vector_grad * lax.rsqrt(vector_state_new)
    vector_rms = jnp.sqrt(jnp.mean(vector_step * vector_step))
    vector_new = vectors - rate_step * jnp.sqrt(
        jnp.mean(vectors * vectors)
    ) * vector_step / jnp.maximum(1.0, vector_rms / clip_level)
    update_rms = jnp.stack(rms_values + [vector_rms])
    return (
        block_out,
        tokens_grad,
        *grads_out,
        vector_grad,
        *new_weights,
        vector_new,
        *copies,
        jnp.concatenate([stats[0][1], stats[1][1], stats[2][1]], axis=0),
        stats[3][1].reshape(-1),
        jnp.concatenate(new_cols, axis=1).reshape(-1),
        vector_state_new,
        update_rms,
    )


def solution(mesh):
    in_specs = (
        P(("rep", "shard"), None),
        P(("rep", "shard"), None),
        P("rep", None),
        P("shard", None),
        P("shard", None),
        P("shard", None),
        P("shard", None),
        P(),
        P(None, "shard"),
        P("shard"),
        P(),
        P(),
    )
    out_specs = (
        P(("rep", "shard"), None),
        P(("rep", "shard"), None),
        P("shard", None),
        P("shard", None),
        P("shard", None),
        P("shard", None),
        P(),
        P("shard", None),
        P("shard", None),
        P("shard", None),
        P("shard", None),
        P(),
        P("shard", None),
        P("shard", None),
        P("shard", None),
        P("shard", None),
        P(None, "shard"),
        P("shard"),
        P(),
        P(),
        P(),
    )
    return jax.shard_map(
        on_device, mesh=mesh, in_specs=in_specs, out_specs=out_specs, check_vma=False
    )
```
